128 devices in a mesh: dp: 16 (over y, x_lo, core), tensor: 8 (over x_hi, z).
Axes of the slice: x: 4 (x_hi: 2, x_lo: 2; x = x_hi * 2 + x_lo), y: 4, z: 4, core: 2. Of those that a mesh axis runs over, the one named last changes fastest.
Arguments:
- tokens: bfloat16 [8192, 2560], P('dp'), may hold values from -6 to 6
- first_gain: float32 [2560], replicated, may hold values from 0.5 to 2
- query_down: bfloat16 [2560, 768], replicated, may hold values from -0.125 to 0.125
- query_gain: float32 [768], replicated, may hold values from 0.5 to 2
- query_up: bfloat16 [768, 3840], P(None, 'tensor'), may hold values from -0.3125 to 0.3125
- latent_down: bfloat16 [2560, 288], replicated, may hold values from -0.125 to 0.125
- latent_gain: float32 [256], replicated, may hold values from 0.5 to 2
- latent_up: bfloat16 [256, 5120], P(None, 'tensor'), may hold values from -0.375 to 0.375
- out_weight: bfloat16 [2560, 2560], P('tensor'), may hold values from -0.3125 to 0.3125
- second_gain: float32 [2560], replicated, may hold values from 0.5 to 2
- gate_weight: bfloat16 [2560, 6400], P(None, 'tensor'), may hold values from -0.125 to 0.125
- up_weight: bfloat16 [2560, 6400], P(None, 'tensor'), may hold values from -0.125 to 0.125
- down_weight: bfloat16 [6400, 2560], P('tensor'), may hold values from -0.15625 to 0.15625
- cotangent: bfloat16 [8192, 2560], P('dp'), may hold values from -6 to 6
Outputs:
- mixed: bfloat16 [8192, 2560], P('dp')
- tokens_grad: float32 [8192, 2560], P('dp')
- first_gain_grad: float32 [2560], P('dp')
- query_down_grad: float32 [2560, 768], P('dp')
- query_gain_grad: float32 [768], P('dp')
- query_up_grad: float32 [768, 3840], P('dp', 'tensor')
- latent_down_grad: float32 [2560, 288], P('dp')
- latent_gain_grad: float32 [256], P('dp')
- latent_up_grad: float32 [256, 5120], P('dp', 'tensor')
- out_weight_grad: float32 [2560, 2560], P('tensor', 'dp')
- second_gain_grad: float32 [2560], P('dp')
- gate_weight_grad: float32 [2560, 6400], P('dp', 'tensor')
- up_weight_grad: float32 [2560, 6400], P('dp', 'tensor')
- down_weight_grad: float32 [6400, 2560], P('tensor', 'dp')
The draws below stay inside these ranges and needn't reach their ends.
All inputs are finite; a program needn't handle non-finite values.
Results may differ from the reference program's by a relative error of at most 0.028.
Values may be sent and summed in bfloat16 or wider, within the bound.
No kernel may reach another device: no remote copies, remote signals or barrier semaphores. Data moves between devices by JAX's collectives and lax.ppermute only.
A program may use at most 192 MiB of HBM per device.

```python
import math
import jax
import jax.numpy as jnp
from jax import lax

D = 2560
H = 40
NOPE = 64
ROPE = 32
DV = 64
QR = 768
KVR = 256
FF = 6400
SEQ = 512
TOKENS = 8192
N_DP = 16


def strengthened(array, key, source, target, blocks, factor):
    def block_of(axis_at):
        return (jnp.arange(array.shape[axis_at]) // (array.shape[axis_at] // blocks)).reshape((-1,) + (1,) * (array.ndim - 1 - axis_at))

    one_side = jax.random.permutation(key, blocks)[block_of(target)]
    far = (block_of(target) + blocks // 2) % blocks
    return jnp.where((block_of(source) == one_side) | (block_of(source) == far), factor * array, array)


def levels(stream_key, dims, cuts, smallest, high):
    def one(position, parts):
        steps = jax.random.uniform(jax.random.fold_in(jax.random.fold_in(stream_key, 6), position), (parts,), jnp.float32, smallest / len(cuts), high / len(cuts))
        return jnp.repeat(jnp.exp(steps), dims[position] // parts).reshape((-1,) + (1,) * (len(dims) - position - 1))

    loudness = one(*cuts[0])
    for cut in cuts[1:]:
        loudness = loudness * one(*cut)
    return loudness


def normal_values(key, shape, scale, reach, cuts=(), dtype=jnp.bfloat16):
    loudness = levels(key, shape, cuts, -0.22, 0.18) if cuts else 1.0
    entries = jax.random.normal(key, shape, jnp.float32) * scale * loudness
    return jnp.minimum(jnp.maximum(entries, -reach), reach).astype(dtype)


def noise_with(own_key, extent, scale, most, split, heavy, held_as=jnp.bfloat16):
    values = scale * jax.random.normal(own_key, extent, jnp.float32)
    if split:
        values = values * levels(own_key, extent, split, -0.22, 0.18)
    return jnp.clip(strengthened(values, jax.random.fold_in(own_key, 3), *heavy), -most, most).astype(held_as)


def setup_inputs(seed: int = 0) -> dict:
    key_list = jax.random.split(jax.random.key(seed), 15)
    return {
        "tokens": normal_values(key_list[0], (TOKENS, D), 1.0, 6.0, ((0, 16),)),
        "first_gain": jnp.clip(jnp.exp(jax.random.uniform(key_list[1], (D,), jnp.float32, math.log(0.5), math.log(2.0))), 0.5, 2.0),
        "query_down": normal_values(key_list[2], (D, QR), D ** -0.5, 0.125),
        "query_gain": jnp.clip(jnp.exp(jax.random.uniform(key_list[3], (QR,), jnp.float32, math.log(0.5), math.log(2.0))), 0.5, 2.0),
        "query_up": normal_values(key_list[4], (QR, H * (NOPE + ROPE)), (QR // 2) ** -0.5, 0.3125, ((1, 8),)),
        "latent_down": normal_values(key_list[5], (D, KVR + ROPE), D ** -0.5, 0.125),
        "latent_gain": jnp.clip(jnp.exp(jax.random.uniform(key_list[6], (KVR,), jnp.float32, math.log(0.5), math.log(2.0))), 0.5, 2.0),
        "latent_up": normal_values(key_list[7], (KVR, H * (NOPE + DV)), KVR ** -0.5, 0.375, ((1, 8),)),
        "out_weight": normal_values(key_list[8], (H * DV, D), (H * DV // 8) ** -0.5, 0.3125, ((0, 8),)),
        "second_gain": jnp.clip(jnp.exp(jax.random.uniform(key_list[9], (D,), jnp.float32, math.log(0.5), math.log(2.0))), 0.5, 2.0),
        "gate_weight": normal_values(key_list[10], (D, FF), D ** -0.5, 0.125, ((1, 8),)),
        "up_weight": normal_values(key_list[11], (D, FF), D ** -0.5, 0.125, ((1, 8),)),
        "down_weight": normal_values(key_list[12], (FF, D), (FF // 4) ** -0.5, 0.15625, ((0, 8),)),
        "cotangent": noise_with(key_list[13], (TOKENS, D), 1.0, 6.0, ((0, 16),), (0, 1, 16, 2.0)),
    }


EPS = 1e-05
BASE = 10000.0
HIGH = lax.Precision.HIGHEST

@jax.custom_vjp
def low(v):
    return lax.optimization_barrier(v.astype(jnp.bfloat16)).astype(jnp.float32)

@jax.custom_vjp
def low_back(v):
    return v

def low_keep(v):
    return (low(v), None)

def low_pass(kept, grad):
    return (grad,)

def back_keep(v):
    return (v, None)

def back_low(kept, grad):
    return (low(grad),)
low.defvjp(low_keep, low_pass)
low_back.defvjp(back_keep, back_low)

def normalize(values, gain):
    return values * lax.rsqrt(lax.optimization_barrier(jnp.mean(values * values, axis=-1, keepdims=True)) + EPS) * gain

def matmul(left, right):
    return jnp.dot(left, right, precision=HIGH, preferred_element_type=jnp.float32)

def rope_tables(length, width):
    half = width // 2
    places = jnp.arange(length).astype(jnp.float32)
    rates = jnp.exp(jnp.arange(half).astype(jnp.float32) * (-2.0 * jnp.log(BASE) / width))
    angles = places[:, None] * rates[None, :]
    return (jnp.cos(angles), jnp.sin(angles))

def rotate(values, cosine, sine):
    half = values.shape[-1] // 2
    first = values[..., :half]
    second = values[..., half:]
    return jnp.concatenate([first * cosine - second * sine, second * cosine + first * sine], axis=-1)

def forward(tokens, first_gain, query_down, query_gain, query_up, latent_down, latent_gain, latent_up, out_weight, second_gain, gate_weight, up_weight, down_weight):
    scale = (NOPE + ROPE) ** (-0.5)
    cosine, sine = rope_tables(SEQ, ROPE)
    first_in = low(normalize(tokens, first_gain))
    query_latent = low_back(matmul(first_in, query_down))
    query_code = low(normalize(query_latent, query_gain))
    query_raw = low_back(matmul(query_code, query_up)).reshape(N_DP, SEQ, H, NOPE + ROPE)
    queries = low(jnp.concatenate([query_raw[..., :NOPE], rotate(query_raw[..., NOPE:], cosine[:, None, :], sine[:, None, :])], axis=-1))
    latent_raw = low_back(matmul(first_in, latent_down))
    latent_code = low(normalize(latent_raw[:, :KVR], latent_gain))
    rope_keys = low(rotate(latent_raw[:, KVR:].reshape(N_DP, SEQ, ROPE), cosine, sine))
    keyvals = low(low_back(matmul(latent_code, latent_up))).reshape(N_DP, SEQ, H, NOPE + DV)

    def attend(block):
        queries_one, keyvals_one, keys_one = block
        plain = jnp.einsum('qhd,khd->hqk', queries_one[..., :NOPE], keyvals_one[..., :NOPE], precision=HIGH)
        turned = jnp.einsum('qhd,kd->hqk', queries_one[..., NOPE:], keys_one, precision=HIGH)
        places = jnp.arange(SEQ)
        causal = (places[:, None] >= places[None, :])[None]
        scores = low_back(jnp.where(causal, (plain + turned) * scale, -1e+30))
        probs = low(jax.nn.softmax(scores, axis=-1))
        heads_out = low(low_back(jnp.einsum('hqk,khd->qhd', probs, keyvals_one[..., NOPE:], precision=HIGH)))
        return heads_out.reshape(SEQ, H * DV)
    heads_out = lax.map(jax.checkpoint(attend), (queries, keyvals, rope_keys)).reshape(TOKENS, H * DV)
    residual = tokens + low_back(matmul(heads_out, out_weight))
    second_in = low(normalize(residual, second_gain))
    gate = low_back(matmul(second_in, gate_weight))
    upward = low_back(matmul(second_in, up_weight))
    inner = low(jax.nn.silu(gate) * upward)
    return residual + low_back(matmul(inner, down_weight))

def reference(tokens, first_gain, query_down, query_gain, query_up, latent_down, latent_gain, latent_up, out_weight, second_gain, gate_weight, up_weight, down_weight, cotangent):
    inputs = (tokens, first_gain, query_down, query_gain, query_up, latent_down, latent_gain, latent_up, out_weight, second_gain, gate_weight, up_weight, down_weight)
    floats = tuple((item.astype(jnp.float32) for item in inputs))
    mixed, pull = jax.vjp(forward, *floats)
    grads = pull(cotangent.astype(jnp.float32))
    return (mixed.astype(jnp.bfloat16), grads[0], grads[1], grads[2], grads[3], grads[4], grads[5], grads[6], grads[7], grads[8], grads[9], grads[10], grads[11], grads[12])
```

```python
import jax
import jax.numpy as jnp
from jax import lax
from jax.sharding import Mesh, PartitionSpec as P

NOPE = 64
ROPE = 32
DV = 64
KVR = 256
QR = 768

EPS = 1e-05
BASE = 10000.0

DP = ("y", "xl", "core")
TP = ("xh", "z")
SWAP = [(0, 1), (1, 0)]
F32 = jnp.float32
BF16 = jnp.bfloat16


def inverse_root(values):
    return lax.rsqrt(jnp.mean(values * values, axis=-1, keepdims=True) + EPS)


def norm_back(upstream, normed, factor, gain):
    scaled = upstream * gain
    return factor * (scaled - normed * jnp.mean(scaled * normed, axis=-1, keepdims=True))


def rope_tables(length, width):
    half = width // 2
    places = jnp.arange(length).astype(F32)
    rates = jnp.exp(jnp.arange(half).astype(F32) * (-2.0 * jnp.log(BASE) / width))
    angles = places[:, None] * rates[None, :]
    return (jnp.cos(angles), jnp.sin(angles))


def rotate(values, cosine, sine):
    half = values.shape[-1] // 2
    first = values[..., :half]
    second = values[..., half:]
    return jnp.concatenate(
        [first * cosine - second * sine, second * cosine + first * sine], axis=-1
    )


def attention_scores(queries, keyvals, rope_keys, scale):
    length = queries.shape[0]
    plain = jnp.einsum(
        "qhd,khd->hqk", queries[..., :NOPE], keyvals[..., :NOPE], preferred_element_type=F32
    )
    turned = jnp.einsum("qhd,kd->hqk", queries[..., NOPE:], rope_keys, preferred_element_type=F32)
    row_ids = lax.broadcasted_iota(jnp.int32, (length, length), 0)
    column_ids = lax.broadcasted_iota(jnp.int32, (length, length), 1)
    return jnp.where((row_ids >= column_ids)[None], (plain + turned) * scale, -1e30)


def product(left, right):
    return jnp.dot(left, right, preferred_element_type=F32)


def scatter_tokens(partial):
    rows = partial.shape[0] // 8
    got = lax.all_to_all(partial, TP, 0, 0, tiled=True)
    return jnp.sum(got.reshape(8, rows, -1).astype(F32), axis=0)


def gather_tokens(own):
    many = jnp.broadcast_to(own[None], (8,) + own.shape).reshape(-1, own.shape[-1])
    return lax.all_to_all(many, TP, 0, 0, tiled=True)


def halves(values, width):
    n = values.shape[0]
    turned = values.T.reshape(4, 2, 2, width, n)
    y, xl, core = lax.axis_index("y"), lax.axis_index("xl"), lax.axis_index("core")

    def pick(which):
        return jnp.concatenate(
            [
                lax.dynamic_slice(
                    turned, (y ^ k, xl ^ j, which, 0, 0), (1, 1, 1, width, n)
                ).reshape(width, n)
                for k in range(4)
                for j in range(2)
            ],
            axis=0,
        )

    return pick(core), pick(1 - core)


def over_cores(values):
    return lax.ppermute(values, "core", SWAP)


def sum_over_chips(blocks):
    got = [
        lax.ppermute(blocks[k], "y", [(i, i ^ k) for i in range(4)]) for k in (2, 1, 3)
    ]
    total = blocks[0].astype(F32)
    for item in got:
        total = total + item.astype(F32)
    rows = total.shape[0] // 2
    other = lax.ppermute(total[rows:].astype(BF16), "xl", SWAP)
    return total[:rows] + other.astype(F32)


def on_device(
    tokens,
    first_gain,
    query_down,
    query_gain,
    query_up,
    latent_down,
    latent_gain,
    latent_up,
    out_weight,
    second_gain,
    gate_weight,
    up_weight,
    down_weight,
    cotangent,
):
    length = tokens.shape[0]
    rows = length // 8
    heads = query_up.shape[1] // (NOPE + ROPE)
    scale = (NOPE + ROPE) ** (-0.5)
    me = lax.axis_index(TP)
    cosine, sine = rope_tables(length, ROPE)

    def mine(values):
        return lax.dynamic_slice_in_dim(values, me * rows, rows, 0)

    hidden_in = tokens.astype(F32)
    factor_one = inverse_root(hidden_in)
    normed_one = hidden_in * factor_one
    first_in = (normed_one * first_gain).astype(BF16)
    query_latent = product(first_in, query_down)
    factor_query = inverse_root(query_latent)
    normed_query = query_latent * factor_query
    query_code = (normed_query * query_gain).astype(BF16)
    query_raw = product(query_code, query_up).reshape(length, heads, NOPE + ROPE)
    queries = jnp.concatenate(
        [
            query_raw[..., :NOPE],
            rotate(query_raw[..., NOPE:], cosine[:, None, :], sine[:, None, :]),
        ],
        axis=-1,
    ).astype(BF16)
    latent_raw = product(first_in, latent_down)
    latent_part = latent_raw[:, :KVR]
    factor_latent = inverse_root(latent_part)
    normed_latent = latent_part * factor_latent
    latent_code = (normed_latent * latent_gain).astype(BF16)
    rope_keys = rotate(latent_raw[:, KVR:], cosine, sine).astype(BF16)
    keyvals = product(latent_code, latent_up).astype(BF16).reshape(length, heads, NOPE + DV)
    values = keyvals[..., NOPE:]
    scores = attention_scores(queries, keyvals, rope_keys, scale)
    top = jnp.max(scores, axis=-1, keepdims=True)
    weights = jnp.exp(scores - top)
    total = jnp.sum(weights, axis=-1, keepdims=True)
    log_total = top + jnp.log(total)
    probs = (weights / total).astype(BF16)
    heads_out = (
        jnp.einsum("hqk,khd->qhd", probs, values, preferred_element_type=F32)
        .astype(BF16)
        .reshape(length, heads * DV)
    )
    attn_partial = product(heads_out, out_weight).astype(BF16)

    residual = mine(tokens).astype(F32) + scatter_tokens(attn_partial)
    factor_two = inverse_root(residual)
    normed_two = residual * factor_two
    second_in = gather_tokens((normed_two * second_gain).astype(BF16))

    gate_act = product(second_in, gate_weight)
    up_act = product(second_in, up_weight)
    sigma = jax.nn.sigmoid(gate_act)
    inner = (gate_act * sigma * up_act).astype(BF16)
    inner_back = product(cotangent, down_weight.T)
    gate_back = (inner_back * up_act * sigma * (1.0 + gate_act * (1.0 - sigma))).astype(BF16)
    up_back = (inner_back * gate_act * sigma).astype(BF16)
    back_partial = (
        product(gate_back, gate_weight.T) + product(up_back, up_weight.T)
    ).astype(BF16)
    second_back = scatter_tokens(back_partial)

    cot_keep, cot_give = halves(cotangent, 160)
    cot_both = jnp.concatenate([cot_keep, over_cores(cot_give)], axis=1)
    in_keep, in_give = halves(second_in, 160)
    in_both = jnp.concatenate([in_keep, over_cores(in_give)], axis=1)
    units = jnp.concatenate([gate_back, up_back, inner], axis=1)
    units_both = jnp.concatenate([units, over_cores(units)], axis=0)
    ff = gate_weight.shape[1]
    ffn_blocks = [
        jnp.concatenate(
            [
                product(in_both[320 * k : 320 * k + 320], units_both[:, : 2 * ff]).astype(BF16),
                product(cot_both[320 * k : 320 * k + 320], units_both[:, 2 * ff :]).astype(BF16),
            ],
            axis=1,
        )
        for k in range(4)
    ]
    ffn_grads = sum_over_chips(ffn_blocks)
    gate_weight_grad = ffn_grads[:, :ff]
    up_weight_grad = ffn_grads[:, ff : 2 * ff]
    down_weight_grad = ffn_grads[:, 2 * ff :].T

    second_gain_part = jnp.sum(second_back * normed_two, axis=0)
    residual_back = mine(cotangent).astype(F32) + norm_back(
        second_back, normed_two, factor_two, second_gain
    )
    attention_back = gather_tokens(residual_back.astype(BF16))

    ffn_partial = product(inner, down_weight).astype(BF16)
    mixed = gather_tokens((residual + scatter_tokens(ffn_partial)).astype(BF16))

    heads_back = (
        product(attention_back, out_weight.T).astype(BF16).reshape(length, heads, DV)
    )
    again = jnp.exp(attention_scores(queries, keyvals, rope_keys, scale) - log_total)
    value_back = jnp.einsum(
        "hqk,qhd->khd", again.astype(BF16), heads_back, preferred_element_type=F32
    )
    prob_back = jnp.einsum("qhd,khd->hqk", heads_back, values, preferred_element_type=F32)
    score_back = (again * (prob_back - jnp.sum(again * prob_back, axis=-1, keepdims=True))).astype(
        BF16
    )
    query_back = (
        jnp.einsum("hqk,khd->qhd", score_back, keyvals[..., :NOPE], preferred_element_type=F32)
        * scale
    )
    query_turn_back = (
        jnp.einsum("hqk,kd->qhd", score_back, rope_keys, preferred_element_type=F32) * scale
    )
    key_back = (
        jnp.einsum("hqk,qhd->khd", score_back, queries[..., :NOPE], preferred_element_type=F32)
        * scale
    )
    rope_key_back = (
        jnp.einsum("hqk,qhd->kd", score_back, queries[..., NOPE:], preferred_element_type=F32)
        * scale
    )
    query_raw_back = (
        jnp.concatenate(
            [query_back, rotate(query_turn_back, cosine[:, None, :], -sine[:, None, :])], axis=-1
        )
        .astype(BF16)
        .reshape(length, heads * (NOPE + ROPE))
    )
    keyval_back = (
        jnp.concatenate([key_back, value_back], axis=-1)
        .astype(BF16)
        .reshape(length, heads * (NOPE + DV))
    )
    latents_back = scatter_tokens(
        jnp.concatenate(
            [
                product(query_raw_back, query_up.T).astype(BF16),
                product(keyval_back, latent_up.T).astype(BF16),
                rope_key_back.astype(BF16),
            ],
            axis=1,
        )
    )

    out_keep, out_give = halves(attention_back, 160)
    out_both = jnp.concatenate([out_keep, over_cores(out_give)], axis=1)
    heads_both = jnp.concatenate([heads_out, over_cores(heads_out)], axis=0)
    code_keep, code_give = halves(query_code, 48)
    code_both = jnp.concatenate([code_keep, over_cores(code_give)], axis=1)
    raw_both = jnp.concatenate([query_raw_back, over_cores(query_raw_back)], axis=0)
    lat_keep, lat_give = halves(latent_code, 16)
    lat_both = jnp.concatenate([lat_keep, over_cores(lat_give)], axis=1)
    kv_both = jnp.concatenate([keyval_back, over_cores(keyval_back)], axis=0)
    out_grads = product(out_both, heads_both).astype(BF16)
    up_grads = product(code_both, raw_both).astype(BF16)
    lat_grads = product(lat_both, kv_both).astype(BF16)
    wide = kv_both.shape[1]

    def padded(values):
        return jnp.pad(values, ((0, 0), (0, wide - values.shape[1])))

    attn_blocks = [
        jnp.concatenate(
            [
                piece
                for j in range(2)
                for piece in (
                    padded(out_grads[(2 * k + j) * 160 : (2 * k + j + 1) * 160]),
                    padded(up_grads[(2 * k + j) * 48 : (2 * k + j + 1) * 48]),
                    lat_grads[(2 * k + j) * 16 : (2 * k + j + 1) * 16],
                )
            ],
            axis=0,
        )
        for k in range(4)
    ]
    attn_grads = sum_over_chips(attn_blocks)
    out_weight_grad = attn_grads[:160, : out_grads.shape[1]].T
    query_up_grad = attn_grads[160:208, : up_grads.shape[1]]
    latent_up_grad = attn_grads[208:224]

    code_back = latents_back[:, :QR]
    latent_code_back = latents_back[:, QR : QR + KVR]
    own_query = mine(normed_query)
    own_latent = mine(normed_latent)
    query_gain_part = jnp.sum(code_back * own_query, axis=0)
    latent_gain_part = jnp.sum(latent_code_back * own_latent, axis=0)
    raw_back = gather_tokens(
        jnp.concatenate(
            [
                norm_back(code_back, own_query, mine(factor_query), query_gain),
                norm_back(latent_code_back, own_latent, mine(factor_latent), latent_gain),
                rotate(latents_back[:, QR + KVR :], mine(cosine), -mine(sine)),
            ],
            axis=1,
        ).astype(BF16)
    )
    down_both = jnp.concatenate([query_down, latent_down], axis=1)
    first_back = product(raw_back, down_both.T)
    first_gain_part = jnp.sum(mine(first_back) * mine(normed_one), axis=0)
    tokens_grad = attention_back.astype(F32) + norm_back(
        first_back, normed_one, factor_one, first_gain
    )

    turned_in = first_in.T.reshape(16, 8, 20, length)
    own_in = lax.dynamic_slice_in_dim(turned_in, me, 1, 1).reshape(320, length)
    down_part = product(own_in, raw_back).astype(BF16).reshape(16, 20, QR + KVR + ROPE)
    gains = jnp.concatenate(
        [
            first_gain_part.reshape(16, -1),
            second_gain_part.reshape(16, -1),
            query_gain_part.reshape(16, -1),
            latent_gain_part.reshape(16, -1),
        ],
        axis=1,
    ).astype(BF16)
    wide_gains = jnp.pad(gains, ((0, 0), (0, down_part.shape[2] - gains.shape[1])))
    parts = jnp.concatenate(
        [down_part, wide_gains[:, None, :], jnp.zeros((16, 3, down_part.shape[2]), BF16)], axis=1
    )
    summed = jnp.sum(
        lax.all_to_all(parts, DP, 0, 0, tiled=True).astype(F32), axis=0
    ).astype(BF16)
    everyone = gather_tokens(summed).reshape(8, 24, -1).astype(F32)
    down_grads = everyone[:, :20].reshape(160, -1)
    query_down_grad = down_grads[:, :QR]
    latent_down_grad = down_grads[:, QR:]
    gain_grads = jnp.sum(everyone[:, 20], axis=0)

    return (
        mixed,
        tokens_grad,
        gain_grads[:160],
        query_down_grad,
        gain_grads[320:368],
        query_up_grad,
        latent_down_grad,
        gain_grads[368:384],
        latent_up_grad,
        out_weight_grad,
        gain_grads[160:320],
        gate_weight_grad,
        up_weight_grad,
        down_weight_grad,
    )


def solution(mesh):
    grid = Mesh(mesh.devices.reshape(4, 2, 2, 2, 4), ("y", "xl", "core", "xh", "z"))
    in_specs = (
        P(DP, None),
        P(),
        P(),
        P(),
        P(None, TP),
        P(),
        P(),
        P(None, TP),
        P(TP, None),
        P(),
        P(None, TP),
        P(None, TP),
        P(TP, None),
        P(DP, None),
    )
    out_specs = (
        P(DP, None),
        P(DP, None),
        P(DP),
        P(DP, None),
        P(DP),
        P(DP, TP),
        P(DP, None),
        P(DP),
        P(DP, TP),
        P(TP, DP),
        P(DP),
        P(DP, TP),
        P(DP, TP),
        P(TP, DP),
    )
    return jax.shard_map(
        on_device, mesh=grid, in_specs=in_specs, out_specs=out_specs, check_vma=False
    )
```

```python
import functools

import jax
import jax.numpy as jnp
import numpy as np
from jax import lax
from jax.experimental import pallas as pl
from jax.experimental.pallas import tpu as pltpu
from jax.sharding import Mesh, PartitionSpec as P

NOPE = 64
ROPE = 32
DV = 64
KVR = 256
QR = 768
LAT = QR + KVR
WIDE = LAT + 128

EPS = 1e-05
BASE = 10000.0
SCALE = (NOPE + ROPE) ** (-0.5)

DP = ("y", "xl", "core")
TP = ("xh", "z")
SWAP = [(0, 1), (1, 0)]
F32 = jnp.float32
BF16 = jnp.bfloat16
NT = (((1,), (1,)), ((), ()))
TN = (((0,), (0,)), ((), ()))
NN = (((1,), (0,)), ((), ()))
TILE = 256


def dot(left, right, dims=NN):
    return lax.dot_general(left, right, dims, preferred_element_type=F32)


def params(limit=56):
    return pltpu.CompilerParams(vmem_limit_bytes=limit * 2**20)


ANY = pl.BlockSpec(memory_space=pl.ANY)


def call(kernel, args, in_specs, out_specs, out_shape, name, grid=(1,), scratch=(), needs=(), me=None, limit=40):
    first = 0 if me is None else 1
    n_in, n_out = len(args), len(out_shape)

    def body(*refs):
        ins = refs[: first + n_in]
        rest = refs[first + n_in + len(needs) :]
        mark = rest[n_out]

        @pl.when(pl.program_id(0) == 0)
        def _():
            mark[...] = jnp.zeros_like(mark)

        kernel(*ins, *rest[:n_out], *rest[n_out + 1 :])

    *outs, mark = pl.pallas_call(
        body,
        grid_spec=pltpu.PrefetchScalarGridSpec(
            num_scalar_prefetch=first,
            grid=grid,
            in_specs=list(in_specs) + [ANY] * len(needs),
            out_specs=list(out_specs) + [full((8, 128))],
            scratch_shapes=list(scratch),
        ),
        out_shape=list(out_shape) + [jax.ShapeDtypeStruct((8, 128), F32)],
        compiler_params=params(limit),
        name=name,
    )(*(() if me is None else (me,)), *args, *needs)
    return outs, mark


def shaped(*shape, dtype=BF16):
    return jax.ShapeDtypeStruct(shape, dtype)


def full(shape):
    return pl.BlockSpec(shape, lambda *_: (0,) * len(shape))


def rope_tables(length):
    half = ROPE // 2
    rates = np.exp(np.arange(half, dtype=np.float32) * np.float32(-2.0 * np.log(BASE) / ROPE))
    angles = np.arange(length, dtype=np.float32)[:, None] * rates.astype(np.float32)[None, :]
    cosine, sine = np.cos(angles), np.sin(angles)
    keep = np.zeros((length, 128), np.float32)
    keep[:, :NOPE] = 1.0
    keep[:, 64:80] = cosine
    keep[:, 80:96] = cosine
    low = np.zeros((length, 128), np.float32)
    low[:, 64:80] = -sine
    high = np.zeros((length, 128), np.float32)
    high[:, 80:96] = sine
    return jnp.asarray(keep), jnp.asarray(low), jnp.asarray(high)


def turn(values, keep, low, high, back=False):
    moved = pltpu.roll(values, 112, 1) * low + pltpu.roll(values, 16, 1) * high
    return values * keep - moved if back else values * keep + moved


def root(values):
    return lax.rsqrt(jnp.mean(values * values, axis=-1, keepdims=True) + EPS)


def norm_back(upstream, normed, factor, gain):
    scaled = upstream * gain
    return factor * (scaled - normed * jnp.mean(scaled * normed, axis=-1, keepdims=True))


def spread_out_weight(weight_ref, spread_ref, heads):
    spread_ref[...] = jnp.zeros_like(spread_ref)
    for h in range(heads):
        spread_ref[128 * h + 64 : 128 * h + 128, :] = weight_ref[64 * h : 64 * h + 64, :]


def spread_query_up(weight_ref, spread_ref, heads):
    spread_ref[...] = jnp.zeros_like(spread_ref)
    for h in range(heads):
        spread_ref[128 * h : 128 * h + 96, :] = weight_ref[96 * h : 96 * h + 96, :]


def row(ref):
    return ref[...].reshape(1, -1)


def low_lanes(shape):
    return lax.broadcasted_iota(jnp.int32, shape, 1) < NOPE


def causal(keys, queries, first_query):
    key_ids = lax.broadcasted_iota(jnp.int32, (keys, queries), 0)
    query_ids = lax.broadcasted_iota(jnp.int32, (keys, queries), 1) + first_query
    return key_ids <= query_ids


def attend_kernel(
    heads,
    tokens,
    first_gain,
    query_down,
    latent_down,
    query_gain,
    latent_gain,
    query_up,
    latent_up,
    out_weight,
    keep,
    low,
    high,
    first_in,
    latents,
    query_code,
    latent_code,
    queries,
    keyvals,
    rope_keys,
    heads_out,
    log_total,
    partial,
    spread,
    spread_up,
    rope_down,
    kv_all,
    rope_all,
):
    step = pl.program_id(0)

    @pl.when(step == 0)
    def _():
        spread_out_weight(out_weight, spread, heads)
        spread_query_up(query_up, spread_up, heads)
        rope_down[...] = jnp.zeros_like(rope_down)
        rope_down[64:96, :] = latent_down[KVR:, :]

    def rows_of(index, carry):
        rows = pl.ds(pl.multiple_of(index * 32, 32), 32)
        values = tokens[rows, :].astype(F32)
        first_in[rows, :] = (values * root(values) * row(first_gain)).astype(BF16)
        return carry

    lax.fori_loop(0, TILE // 32, rows_of, 0)
    taken = first_in[...]
    query_latent = dot(taken, query_down[...])
    latents[:, :QR] = query_latent
    code = (query_latent * root(query_latent) * row(query_gain)).astype(BF16)
    query_code[...] = code
    latent = dot(taken, latent_down[:KVR, :], NT)
    latents[:, QR:] = latent
    lcode = (latent * root(latent) * row(latent_gain)).astype(BF16)
    latent_code[...] = lcode
    tables = keep[...], low[...], high[...]
    rope = turn(dot(taken, rope_down[...], NT), *tables).astype(BF16)
    rope_keys[...] = rope
    here = pl.ds(pl.multiple_of(step * TILE, TILE), TILE)
    rope_all[here, :] = rope
    kv = dot(lcode, latent_up[...]).astype(BF16)
    keyvals[...] = kv
    kv_all[here, :] = kv
    raw = dot(code, spread_up[...], NT)
    for h in range(heads):
        lanes = slice(128 * h, 128 * h + 128)
        queries[:, lanes] = turn(raw[:, lanes], *tables).astype(BF16)

    def tile(index):
        keys = TILE * (index + 1)
        for h in range(heads):
            lanes = slice(128 * h, 128 * h + 128)
            kv_h = kv_all[:keys, lanes]
            key = jnp.where(low_lanes((keys, 128)), kv_h, rope_all[:keys, :])
            scores = dot(key, queries[:, lanes], NT) * SCALE
            scores = jnp.where(causal(keys, TILE, TILE * index), scores, -1e30)
            top = jnp.max(scores, axis=0, keepdims=True)
            weights = jnp.exp(scores - top)
            total = jnp.sum(weights, axis=0, keepdims=True)
            log_total[h : h + 1, :] = top + jnp.log(total)
            probs = (weights * (1.0 / total)).astype(BF16)
            heads_out[:, lanes] = dot(probs, kv_h, TN).astype(BF16)

    for index in range(2):
        pl.when(step == index)(functools.partial(tile, index))
    partial[...] = dot(heads_out[...], spread[...]).astype(BF16)


def attend(tokens, first_gain, query_down, latent_down, query_gain, latent_gain, query_up, latent_up, out_weight, tables):
    latent_down, query_up = latent_down.T, query_up.T
    length, width = tokens.shape
    heads = out_weight.shape[0] // DV
    wide = 128 * heads

    def rows(columns):
        return pl.BlockSpec((TILE, columns), lambda i: (i, 0))

    return call(
        functools.partial(attend_kernel, heads),
        (tokens, first_gain, query_down, latent_down, query_gain, latent_gain, query_up, latent_up, out_weight, *tables),
        [
            rows(width),
            full((width,)),
            full(query_down.shape),
            full(latent_down.shape),
            full((QR,)),
            full((KVR,)),
            full(query_up.shape),
            full(latent_up.shape),
            full(out_weight.shape),
            rows(128),
            rows(128),
            rows(128),
        ],
        [
            rows(width),
            rows(LAT),
            rows(QR),
            rows(KVR),
            rows(wide),
            rows(wide),
            rows(128),
            rows(wide),
            pl.BlockSpec((8, TILE), lambda i: (0, i)),
            rows(width),
        ],
        [
            shaped(length, width),
            shaped(length, LAT, dtype=F32),
            shaped(length, QR),
            shaped(length, KVR),
            shaped(length, wide),
            shaped(length, wide),
            shaped(length, 128),
            shaped(length, wide),
            shaped(8, length, dtype=F32),
            shaped(length, width),
        ],
        "attend",
        grid=(length // TILE,),
        scratch=[
            pltpu.VMEM((wide, width), BF16),
            pltpu.VMEM((wide, QR), BF16),
            pltpu.VMEM((128, width), BF16),
            pltpu.VMEM((length, wide), BF16),
            pltpu.VMEM((length, 128), BF16),
        ],
    )


def attend_back_kernel(
    heads,
    attention_back,
    out_weight,
    queries,
    keyvals,
    rope_keys,
    log_total,
    query_up,
    latent_up,
    keep,
    low,
    high,
    query_back,
    keyval_back,
    partial,
    spread,
    spread_up,
    kv_grad,
    rope_grad,
    code_grad,
):
    step = pl.program_id(0)

    @pl.when(step == 0)
    def _():
        spread_out_weight(out_weight, spread, heads)
        spread_query_up(query_up, spread_up, heads)
        kv_grad[...] = jnp.zeros_like(kv_grad)
        rope_grad[...] = jnp.zeros_like(rope_grad)

    heads_back = dot(attention_back[...], spread[...], NT).astype(BF16)
    tables = keep[...], low[...], high[...]

    def tile(index):
        keys = TILE * (index + 1)
        low_part = low_lanes((keys, 128))
        for h in range(heads):
            lanes = slice(128 * h, 128 * h + 128)
            kv_h = keyvals[:keys, lanes]
            key = jnp.where(low_part, kv_h, rope_keys[:keys, :])
            query = queries[:, lanes]
            back = heads_back[:, lanes]
            scores = dot(key, query, NT) * SCALE
            probs = jnp.exp(scores - log_total[h : h + 1, :])
            probs = jnp.where(causal(keys, TILE, TILE * index), probs, 0.0)
            prob_back = dot(kv_h, back, NT)
            mean = jnp.sum(probs * prob_back, axis=0, keepdims=True)
            score_back = (probs * (prob_back - mean)).astype(BF16)
            of_values = dot(probs.astype(BF16), back)
            of_keys = dot(score_back, query) * SCALE
            kv_grad[:keys, lanes] += of_values + jnp.where(low_part, of_keys, 0.0)
            rope_grad[:keys, :] += jnp.where(low_part, 0.0, of_keys)
            of_query = dot(score_back, key, TN) * SCALE
            query_back[:, lanes] = turn(of_query, *tables, back=True).astype(BF16)

    for index in range(2):
        pl.when(step == index)(functools.partial(tile, index))
    here = pl.ds(pl.multiple_of(step * TILE, TILE), TILE)
    code_grad[here, :] = dot(query_back[...], spread_up[...]).astype(BF16)

    @pl.when(step == 1)
    def _():
        kv = kv_grad[...].astype(BF16)
        keyval_back[...] = kv
        partial[:, :QR] = code_grad[...]
        partial[:, QR:LAT] = dot(kv, latent_up[...], NT).astype(BF16)
        partial[:, LAT:] = rope_grad[...].astype(BF16)


def attend_back(attention_back, out_weight, queries, keyvals, rope_keys, log_total, query_up, latent_up, tables, needs):
    query_up = query_up.T
    length, width = attention_back.shape
    heads = out_weight.shape[0] // DV
    wide = 128 * heads

    def rows(columns):
        return pl.BlockSpec((TILE, columns), lambda i: (i, 0))

    return call(
        functools.partial(attend_back_kernel, heads),
        (attention_back, out_weight, queries, keyvals, rope_keys, log_total, query_up, latent_up, *tables),
        [
            rows(width),
            full(out_weight.shape),
            rows(wide),
            full((length, wide)),
            full((length, 128)),
            pl.BlockSpec((8, TILE), lambda i: (0, i)),
            full(query_up.shape),
            full(latent_up.shape),
            rows(128),
            rows(128),
            rows(128),
        ],
        [rows(wide), full((length, wide)), full((length, WIDE))],
        [shaped(length, wide), shaped(length, wide), shaped(length, WIDE)],
        "attend_back",
        grid=(length // TILE,),
        scratch=[
            pltpu.VMEM((wide, width), BF16),
            pltpu.VMEM((wide, QR), BF16),
            pltpu.VMEM((length, wide), F32),
            pltpu.VMEM((length, 128), F32),
            pltpu.VMEM((length, QR), BF16),
        ],
        needs=needs,
    )


def after(values, *others):
    def nothing(*refs):
        del refs

    return pl.pallas_call(
        nothing,
        in_specs=[ANY] * (1 + len(others)),
        out_specs=ANY,
        out_shape=jax.ShapeDtypeStruct(values.shape, values.dtype),
        input_output_aliases={0: 0},
        name="after",
    )(values, *others)


def add_up(got):
    total = got[0].astype(F32)
    for k in range(1, 8):
        total = total + got[k].astype(F32)
    return total


def residual_kernel(got, tokens, gain, residual, many):
    total = tokens[...].astype(F32) + add_up(got)
    residual[...] = total
    second_in = (total * root(total) * row(gain)).astype(BF16)
    for k in range(8):
        many[k] = second_in


def residual_of(got, own_tokens, gain, needs):
    rows, width = own_tokens.shape
    step = rows // 2
    many = pl.BlockSpec((8, step, width), lambda i: (0, i, 0))
    one = pl.BlockSpec((step, width), lambda i: (i, 0))
    return call(
        residual_kernel,
        (got.reshape(8, rows, width), own_tokens, gain),
        [many, one, full((width,))],
        [one, many],
        [shaped(rows, width, dtype=F32), shaped(8, rows, width)],
        "residual",
        grid=(2,),
        needs=needs,
        limit=24,
    )


def residual_back_kernel(got, residual, cotangent, gain, many, gain_part):
    second_back = add_up(got)
    values = residual[...]
    factor = root(values)
    normed = values * factor
    part = jnp.sum(second_back * normed, axis=0, keepdims=True)

    @pl.when(pl.program_id(0) == 0)
    def _():
        gain_part[...] = part

    @pl.when(pl.program_id(0) > 0)
    def _():
        gain_part[...] += part

    back = cotangent[...].astype(F32) + norm_back(second_back, normed, factor, row(gain))
    back = back.astype(BF16)
    for k in range(8):
        many[k] = back


def residual_back_of(got, residual, own_cotangent, gain, needs):
    rows, width = residual.shape
    step = rows // 2
    many = pl.BlockSpec((8, step, width), lambda i: (0, i, 0))
    one = pl.BlockSpec((step, width), lambda i: (i, 0))
    return call(
        residual_back_kernel,
        (got.reshape(8, rows, width), residual, own_cotangent, gain),
        [many, one, one, full((width,))],
        [many, full((1, width))],
        [shaped(8, rows, width), shaped(1, width, dtype=F32)],
        "residual_back",
        grid=(2,),
        needs=needs,
        limit=24,
    )


def ffn_kernel(
    second_in, gate_weight, up_weight, inner_back, gate_back, up_back, inner, partial
):
    taken = second_in[...]
    gate = dot(taken, gate_weight[...], NT)
    up = dot(taken, up_weight[...], NT)
    sigma = 1.0 / (1.0 + jnp.exp(-gate))
    act = gate * sigma
    inner[...] = (act * up).astype(BF16)
    back = inner_back[...]
    gate_back[...] = (back * up * sigma * (1.0 + gate * (1.0 - sigma))).astype(BF16)
    up_back[...] = (back * act).astype(BF16)
    partial[...] = (
        dot(gate_back[...], gate_weight[...]) + dot(up_back[...], up_weight[...])
    ).astype(BF16)


def ffn(second_in, gate_weight, up_weight, inner_back, needs):
    length, width = second_in.shape
    units = gate_weight.shape[0]

    def rows(columns):
        return pl.BlockSpec((TILE, columns), lambda i: (i, 0))

    return call(
        ffn_kernel,
        (second_in, gate_weight, up_weight, inner_back),
        [rows(width), full((units, width)), full((units, width)), rows(units)],
        [rows(units), rows(units), rows(units), rows(width)],
        [shaped(length, units)] * 3 + [shaped(length, width)],
        "ffn",
        grid=(length // TILE,),
        needs=needs,
    )


def ffn_down_kernel(me, inner, down_weight, residual, out):
    for i in range(2):
        rows = slice(i * TILE, i * TILE + TILE)
        out[rows, :] = dot(inner[rows, :], down_weight[...]).astype(BF16)
    count = residual.shape[0]
    own = pl.ds(pl.multiple_of(me[0] * count, count), count)
    out[own, :] = (out[own, :].astype(F32) + residual[...]).astype(BF16)


def ffn_down(me, inner, down_weight, residual, needs):
    length, width = inner.shape[0], down_weight.shape[1]
    return call(
        ffn_down_kernel,
        (inner, down_weight, residual),
        [full(inner.shape), full(down_weight.shape), full(residual.shape)],
        [full((length, width))],
        [shaped(length, width)],
        "ffn_down",
        needs=needs,
        me=me,
    )


def halves_kernel(blocks, width, starts, *refs):
    sources, outs, turned = refs[:blocks], refs[blocks : 3 * blocks], refs[3 * blocks]
    for n in range(blocks):
        source, keep, give = sources[n], outs[2 * n], outs[2 * n + 1]
        columns, each = source.shape[1], width[n]
        for c in range(0, columns, 256):
            turned[c : c + 256, :] = source[:, c : c + 256].T
        for which, out in enumerate((keep, give)):
            for k in range(8):
                first = pl.multiple_of(starts[8 * which + k] * each, 16)
                out[each * k : each * k + each, :] = turned[pl.ds(first, each), :]


def halves(starts, values, needs):
    length = values[0].shape[0]
    widths = [item.shape[1] // 16 for item in values]
    shapes = [(8 * w, length) for w in widths for _ in range(2)]
    return call(
        functools.partial(halves_kernel, len(values), widths),
        tuple(values),
        [full(item.shape) for item in values],
        [full(s) for s in shapes],
        [shaped(*s) for s in shapes],
        "halves",
        scratch=[pltpu.VMEM((max(item.shape[1] for item in values), length), BF16)],
        needs=needs,
        me=starts,
    )


ORDER = (2, 1, 3, 0)


def ffn_grads_kernel(in_keep, in_got, cot_keep, cot_got, *refs):
    ours, theirs, outs = refs[:3], refs[3:6], refs[6:]
    units = ours[0].shape[1]

    def block(out):
        for n, (keep, got) in enumerate(((in_keep, in_got), (in_keep, in_got), (cot_keep, cot_got))):
            total = dot(keep[...], ours[n][...]) + dot(got[...], theirs[n][...])
            out[:, units * n : units * n + units] = total.astype(BF16)

    for s in range(4):
        pl.when(pl.program_id(0) == s)(functools.partial(block, outs[s]))


def ffn_grads(in_keep, in_got, cot_keep, cot_got, ours, theirs, needs):
    length, units = ours[0].shape
    rows = in_keep.shape[0] // 4

    def index(i):
        return (jnp.where(i == 0, 2, jnp.where(i == 1, 1, jnp.where(i == 2, 3, 0))), 0)

    left = pl.BlockSpec((rows, length), index)
    out = (rows, 3 * units)
    outs, mark = call(
        ffn_grads_kernel,
        (in_keep, in_got, cot_keep, cot_got, *ours, *theirs),
        [left] * 4 + [full((length, units))] * 6,
        [full(out)] * 4,
        [shaped(*out)] * 4,
        "ffn_grads",
        grid=(4,),
        needs=needs,
        limit=48,
    )
    return dict(zip(ORDER, outs)), mark


def attn_grads_kernel(widths, *refs):
    keeps, gots, ours, theirs, outs = refs[:3], refs[3:6], refs[6:9], refs[9:12], refs[12:]
    rows = sum(widths)
    for s, k in enumerate(ORDER):
        first = 0
        for n, each in enumerate(widths):
            part = slice(2 * each * k, 2 * each * k + 2 * each)
            total = dot(keeps[n][part, :], ours[n][...]) + dot(gots[n][part, :], theirs[n][...])
            total = total.astype(BF16)
            outs[s][first : first + each, :] = total[:each]
            outs[s][rows + first : rows + first + each, :] = total[each:]
            first += each


def attn_grads(keeps, gots, ours, theirs, needs):
    widths = [item.shape[0] // 8 for item in keeps]
    out = (2 * sum(widths), ours[0].shape[1])
    args = (*keeps, *gots, *ours, *theirs)
    outs, mark = call(
        functools.partial(attn_grads_kernel, widths),
        args,
        [full(item.shape) for item in args],
        [full(out)] * 4,
        [shaped(*out)] * 4,
        "attn_grads",
        needs=needs,
    )
    return dict(zip(ORDER, outs)), mark


def add_chips_kernel(*refs):
    ins, keep, give = refs[:8], refs[8], refs[9]
    keep[...] = sum(item[...].astype(F32) for item in ins[:4])
    give[...] = sum(item[...].astype(F32) for item in ins[4:]).astype(BF16)


def add_chips(items, needs):
    rows, width = items[0].shape[0] // 2, items[0].shape[1]
    step = 32
    count = rows // step
    mine = pl.BlockSpec((step, width), lambda i: (i, 0))
    other = pl.BlockSpec((step, width), lambda i: (i + count, 0))
    outs, mark = call(
        add_chips_kernel,
        (*items, *items),
        [mine] * 4 + [other] * 4,
        [mine, mine],
        [shaped(rows, width, dtype=F32), shaped(rows, width)],
        "add_chips",
        grid=(count,),
        needs=needs,
        limit=24,
    )
    return outs, mark


def over_y(blocks):
    return [blocks[0]] + [
        lax.ppermute(blocks[k], "y", [(i, i ^ k) for i in range(4)]) for k in ORDER[:3]
    ]


def over_cores(values):
    return lax.ppermute(values, "core", SWAP)


def latents_back_kernel(
    got, latents, query_gain, latent_gain, keep, low, high, many, own, gain_part
):
    total = add_up(got)

    def back(lanes, gain):
        upstream, values = total[:, lanes], latents[:, lanes]
        factor = root(values)
        normed = values * factor
        gain_part[:, lanes] = jnp.sum(upstream * normed, axis=0, keepdims=True)
        return norm_back(upstream, normed, factor, row(gain)).astype(BF16)

    own[:, :QR] = back(slice(0, QR), query_gain)
    own[:, QR:LAT] = back(slice(QR, LAT), latent_gain)
    own[:, LAT:] = turn(total[:, LAT:], keep[...], low[...], high[...], back=True).astype(BF16)
    for k in range(8):
        many[k] = own[...]


def latents_back_of(got, own_latents, query_gain, latent_gain, own_tables, needs):
    rows = own_latents.shape[0]
    args = (got.reshape(8, rows, WIDE), own_latents, query_gain, latent_gain, *own_tables)
    return call(
        latents_back_kernel,
        args,
        [full(item.shape) for item in args],
        [full((8, rows, WIDE)), full((rows, WIDE)), full((1, LAT))],
        [shaped(8, rows, WIDE), shaped(rows, WIDE), shaped(1, LAT, dtype=F32)],
        "latents_back",
        needs=needs,
        limit=16,
    )


def first_back_of(raw_back, query_down, latent_down, rope_down):
    rope_down[...] = jnp.zeros_like(rope_down)
    rope_down[64:96, :] = latent_down[KVR:, :]
    return (
        dot(raw_back[:, :QR], query_down[...], NT)
        + dot(raw_back[:, QR:LAT], latent_down[:KVR, :])
        + dot(raw_back[:, LAT:], rope_down[...])
    )


def first_gain_kernel(raw_back, tokens, query_down, latent_down, gain_part, rope_down):
    first_back = first_back_of(raw_back, query_down, latent_down, rope_down)
    values = tokens[...].astype(F32)
    gain_part[...] = jnp.sum(first_back * (values * root(values)), axis=0, keepdims=True)


def first_gain_of(own_raw_back, own_tokens, query_down, latent_down, needs):
    width = own_tokens.shape[1]
    args = (own_raw_back, own_tokens, query_down, latent_down.T)
    return call(
        first_gain_kernel,
        args,
        [full(item.shape) for item in args],
        [full((1, width))],
        [shaped(1, width, dtype=F32)],
        "first_gain",
        scratch=[pltpu.VMEM((128, width), BF16)],
        needs=needs,
    )


def tokens_back_kernel(
    raw_back, tokens, attention_back, query_down, latent_down, gain, tokens_grad, rope_down
):
    first_back = first_back_of(raw_back, query_down, latent_down, rope_down)
    values = tokens[...].astype(F32)
    factor = root(values)
    tokens_grad[...] = attention_back[...].astype(F32) + norm_back(
        first_back, values * factor, factor, row(gain)
    )


def tokens_back_of(raw_back, tokens, attention_back, query_down, latent_down, gain, needs):
    length, width = tokens.shape

    def rows(columns):
        return pl.BlockSpec((TILE, columns), lambda i: (i, 0))

    return call(
        tokens_back_kernel,
        (raw_back, tokens, attention_back, query_down, latent_down.T, gain),
        [
            rows(WIDE),
            rows(width),
            rows(width),
            full(query_down.shape),
            full(latent_down.shape[::-1]),
            full((width,)),
        ],
        [rows(width)],
        [shaped(length, width, dtype=F32)],
        "tokens_back",
        grid=(length // TILE,),
        scratch=[pltpu.VMEM((128, width), BF16)],
        needs=needs,
        limit=48,
    )


def finish_ffn_kernel(keep, got, gate, up, down):
    units = gate.shape[1]
    for n, out in enumerate((gate, up, down)):
        lanes = slice(units * n, units * n + units)
        out[...] = keep[:, lanes] + got[:, lanes].astype(F32)


def finish_ffn(keep, got):
    rows, width = keep.shape
    out = (rows, width // 3)
    return call(
        finish_ffn_kernel,
        (keep, got),
        [full(keep.shape), full(got.shape)],
        [full(out)] * 3,
        [shaped(*out, dtype=F32)] * 3,
        "finish_ffn",
        limit=24,
    )[0]


def finish_attn_kernel(heads, keep, got, out_grad, query_grad, latent_grad):
    total = keep[...] + got[...].astype(F32)
    for h in range(heads):
        lanes = slice(128 * h, 128 * h + 128)
        out_grad[:, 64 * h : 64 * h + 64] = total[:160, 128 * h + 64 : 128 * h + 128]
        query_grad[:, 96 * h : 96 * h + 96] = total[160:208, 128 * h : 128 * h + 96]
    latent_grad[...] = total[208:224]


def finish_attn(keep, got):
    heads = keep.shape[1] // 128
    outs = [(160, 64 * heads), (48, 96 * heads), (16, 128 * heads)]
    return call(
        functools.partial(finish_attn_kernel, heads),
        (keep, got),
        [full(keep.shape), full(got.shape)],
        [full(s) for s in outs],
        [shaped(*s, dtype=F32) for s in outs],
        "finish_attn",
        limit=24,
    )[0]


def finish_down_kernel(everyone, query_grad, latent_grad, gains):
    for t in range(8):
        values = everyone[t].astype(F32)
        query_grad[20 * t : 20 * t + 20, :] = values[:20, :QR]
        latent_grad[20 * t : 20 * t + 20, :KVR] = values[:20, QR:LAT]
        latent_grad[20 * t : 20 * t + 20, KVR:] = values[:20, LAT + 64 : LAT + 96]
    gains[...] = sum(everyone[t, 16:24, :].astype(F32) for t in range(8))[4:5, :]


def finish_down(everyone):
    everyone = everyone.reshape(8, 24, WIDE)
    outs = [(160, QR), (160, KVR + ROPE), (1, WIDE)]
    return call(
        finish_down_kernel,
        (everyone,),
        [full(everyone.shape)],
        [full(s) for s in outs],
        [shaped(*s, dtype=F32) for s in outs],
        "finish_down",
        limit=24,
    )[0]


def exchange(blocks):
    return lax.all_to_all(blocks.reshape(-1, blocks.shape[-1]), TP, 0, 0, tiled=True)


def on_device(
    tokens,
    first_gain,
    query_down,
    query_gain,
    query_up,
    latent_down,
    latent_gain,
    latent_up,
    out_weight,
    second_gain,
    gate_weight,
    up_weight,
    down_weight,
    cotangent,
):
    length = tokens.shape[0]
    rows = length // 8
    me = lax.axis_index(TP).astype(jnp.int32).reshape(1)
    y, xl, core = lax.axis_index("y"), lax.axis_index("xl"), lax.axis_index("core")
    starts = jnp.stack(
        [
            ((y ^ k) * 2 + (xl ^ j)) * 2 + c
            for c in (core, 1 - core)
            for k in range(4)
            for j in range(2)
        ]
    ).astype(jnp.int32)
    tables = rope_tables(length)

    def own(values):
        return lax.dynamic_slice_in_dim(values, me[0] * rows, rows, 0)

    gate_turned, up_turned = gate_weight.T, up_weight.T

    (
        first_in,
        latents,
        query_code,
        latent_code,
        queries,
        keyvals,
        rope_keys,
        heads_out,
        log_total,
        attn_partial,
    ), started = attend(
        tokens,
        first_gain,
        query_down,
        latent_down,
        query_gain,
        latent_gain,
        query_up,
        latent_up,
        out_weight,
        tables,
    )
    attn_got = exchange(attn_partial)

    (cot_keep, cot_give), picked = halves(starts, [cotangent], [started])
    inner_back = dot(cotangent, down_weight, NT)
    cot_got = over_cores(cot_give)
    own_tokens, own_cotangent = own(tokens), own(cotangent)

    (residual, second_many), _ = residual_of(
        attn_got, own_tokens, second_gain, [picked, inner_back]
    )
    second_in = exchange(second_many)

    turned_in = first_in.T.reshape(16, 8, 20, length)
    own_in = lax.dynamic_slice_in_dim(turned_in, me[0], 1, 1).reshape(320, length)
    (code_keep, code_give, lat_keep, lat_give), picked = halves(
        starts, [query_code, latent_code], [residual]
    )
    code_got, lat_got = over_cores(code_give), over_cores(lat_give)
    heads_got = over_cores(heads_out)

    (gate_back, up_back, inner, back_partial), done = ffn(
        second_in, gate_turned, up_turned, inner_back, [picked, own_in]
    )
    back_got = exchange(back_partial)

    ours = (gate_back, up_back, inner)
    theirs = [over_cores(item) for item in ours]
    (in_keep, in_give), _ = halves(starts, [second_in], [done])
    in_got = over_cores(in_give)
    ffn_blocks, done = ffn_grads(in_keep, in_got, cot_keep, cot_got, ours, theirs, [])
    ffn_parts = over_y(ffn_blocks)

    (back_many, second_gain_part), _ = residual_back_of(
        back_got, residual, own_cotangent, second_gain, [done]
    )
    attention_back = exchange(back_many)
    (ffn_partial,), done = ffn_down(me, inner, down_weight, residual, [second_gain_part])

    (query_raw_back, keyval_back, latents_partial), back_done = attend_back(
        attention_back,
        out_weight,
        queries,
        keyvals,
        rope_keys,
        log_total,
        query_up,
        latent_up,
        tables,
        [done],
    )
    mixed = lax.psum(after(ffn_partial, attention_back), TP)
    latents_got = exchange(latents_partial)

    (out_keep, out_give), _ = halves(starts, [attention_back], [back_done])
    out_got = over_cores(out_give)
    raw_got, kv_got = over_cores(query_raw_back), over_cores(keyval_back)
    attn_blocks, done = attn_grads(
        (out_keep, code_keep, lat_keep),
        (out_got, code_got, lat_got),
        (heads_out, query_raw_back, keyval_back),
        (heads_got, raw_got, kv_got),
        [],
    )

    (raw_many, own_raw, latent_gain_parts), _ = latents_back_of(
        latents_got,
        own(latents),
        query_gain,
        latent_gain,
        [own(item) for item in tables],
        [done],
    )
    raw_back = exchange(raw_many)
    (first_gain_part,), done = first_gain_of(own_raw, own_tokens, query_down, latent_down, [])
    (ffn_keep, ffn_give), done = add_chips(ffn_parts, [done])
    ffn_got = lax.ppermute(ffn_give, "xl", SWAP)
    attn_parts = over_y(attn_blocks)

    down_part = dot(own_in, raw_back).astype(BF16).reshape(16, 20, WIDE)
    gains = jnp.concatenate(
        [
            first_gain_part.reshape(16, -1),
            second_gain_part.reshape(16, -1),
            latent_gain_parts[0, :QR].reshape(16, -1),
            latent_gain_parts[0, QR:].reshape(16, -1),
        ],
        axis=1,
    ).astype(BF16)
    wide_gains = jnp.pad(gains, ((0, 0), (0, WIDE - gains.shape[1])))
    parts = jnp.concatenate(
        [down_part, wide_gains[:, None, :], jnp.zeros((16, 3, WIDE), BF16)], axis=1
    )
    (tokens_grad,), done = tokens_back_of(
        raw_back, tokens, attention_back, query_down, latent_down, first_gain, [parts]
    )
    summed = jnp.sum(
        lax.all_to_all(parts, DP, 0, 0, tiled=True).astype(F32), axis=0
    ).astype(BF16)
    everyone = exchange(jnp.broadcast_to(summed[None], (8,) + summed.shape))

    (attn_keep, attn_give), _ = add_chips(attn_parts, [done])
    attn_got = lax.ppermute(attn_give, "xl", SWAP)
    gate_weight_grad, up_weight_grad, down_weight_grad = finish_ffn(ffn_keep, ffn_got)
    out_weight_grad, query_up_grad, latent_up_grad = finish_attn(attn_keep, attn_got)
    query_down_grad, latent_down_grad, gain_grads = finish_down(everyone)
    gain_grads = gain_grads[0]

    return (
        mixed,
        tokens_grad,
        gain_grads[:160],
        query_down_grad,
        gain_grads[320:368],
        query_up_grad,
        latent_down_grad,
        gain_grads[368:384],
        latent_up_grad,
        out_weight_grad.T,
        gain_grads[160:320],
        gate_weight_grad,
        up_weight_grad,
        down_weight_grad.T,
    )


def solution(mesh):
    grid = Mesh(mesh.devices.reshape(4, 2, 2, 2, 4), ("y", "xl", "core", "xh", "z"))
    in_specs = (
        P(DP, None),
        P(),
        P(),
        P(),
        P(None, TP),
        P(),
        P(),
        P(None, TP),
        P(TP, None),
        P(),
        P(None, TP),
        P(None, TP),
        P(TP, None),
        P(DP, None),
    )
    out_specs = (
        P(DP, None),
        P(DP, None),
        P(DP),
        P(DP, None),
        P(DP),
        P(DP, TP),
        P(DP, None),
        P(DP),
        P(DP, TP),
        P(TP, DP),
        P(DP),
        P(DP, TP),
        P(DP, TP),
        P(TP, DP),
    )
    return jax.shard_map(
        on_device, mesh=grid, in_specs=in_specs, out_specs=out_specs, check_vma=False
    )
```

```python
import functools

import jax
import jax.numpy as jnp
import numpy as np
from jax import lax
from jax.experimental import pallas as pl
from jax.experimental.pallas import tpu as pltpu
from jax.sharding import Mesh, PartitionSpec as P

NOPE = 64
ROPE = 32
DV = 64
KVR = 256
QR = 768
LAT = QR + KVR
WIDE = LAT + 128

EPS = 1e-05
BASE = 10000.0
SCALE = (NOPE + ROPE) ** (-0.5)

DP = ("y", "xl", "core")
TP = ("xh", "z")
SWAP = [(0, 1), (1, 0)]
F32 = jnp.float32
BF16 = jnp.bfloat16
NT = (((1,), (1,)), ((), ()))
TN = (((0,), (0,)), ((), ()))
NN = (((1,), (0,)), ((), ()))
TILE = 256


def dot(left, right, dims=NN):
    return lax.dot_general(left, right, dims, preferred_element_type=F32)


def params(limit=56):
    return pltpu.CompilerParams(vmem_limit_bytes=limit * 2**20)


ANY = pl.BlockSpec(memory_space=pl.ANY)


def call(kernel, args, in_specs, out_specs, out_shape, name, grid=(1,), scratch=(), needs=(), me=None, limit=60):
    first = 0 if me is None else 1
    n_in, n_out = len(args), len(out_shape)

    def body(*refs):
        ins = refs[: first + n_in]
        rest = refs[first + n_in + len(needs) :]
        mark = rest[n_out]

        @pl.when(pl.program_id(0) == 0)
        def _():
            mark[...] = jnp.zeros_like(mark)

        kernel(*ins, *rest[:n_out], *rest[n_out + 1 :])

    *outs, mark = pl.pallas_call(
        body,
        grid_spec=pltpu.PrefetchScalarGridSpec(
            num_scalar_prefetch=first,
            grid=grid,
            in_specs=list(in_specs) + [ANY] * len(needs),
            out_specs=list(out_specs) + [full((8, 128))],
            scratch_shapes=list(scratch),
        ),
        out_shape=list(out_shape) + [jax.ShapeDtypeStruct((8, 128), F32)],
        compiler_params=params(limit),
        name=name,
    )(*(() if me is None else (me,)), *args, *needs)
    return outs, mark


def shaped(*shape, dtype=BF16):
    return jax.ShapeDtypeStruct(shape, dtype)


def full(shape):
    return pl.BlockSpec(shape, lambda *_: (0,) * len(shape))


def rope_tables(length):
    half = ROPE // 2
    rates = np.exp(np.arange(half, dtype=np.float32) * np.float32(-2.0 * np.log(BASE) / ROPE))
    angles = np.arange(length, dtype=np.float32)[:, None] * rates.astype(np.float32)[None, :]
    cosine, sine = np.cos(angles), np.sin(angles)
    keep = np.zeros((length, 128), np.float32)
    keep[:, :NOPE] = 1.0
    keep[:, 64:80] = cosine
    keep[:, 80:96] = cosine
    low = np.zeros((length, 128), np.float32)
    low[:, 64:80] = -sine
    high = np.zeros((length, 128), np.float32)
    high[:, 80:96] = sine
    return jnp.asarray(keep), jnp.asarray(low), jnp.asarray(high)


def turn(values, keep, low, high, back=False):
    moved = pltpu.roll(values, 112, 1) * low + pltpu.roll(values, 16, 1) * high
    return values * keep - moved if back else values * keep + moved


def root(values):
    return lax.rsqrt(jnp.mean(values * values, axis=-1, keepdims=True) + EPS)


def norm_back(upstream, normed, factor, gain):
    scaled = upstream * gain
    return factor * (scaled - normed * jnp.mean(scaled * normed, axis=-1, keepdims=True))


def spread_out_weight(weight_ref, spread_ref, heads):
    spread_ref[...] = jnp.zeros_like(spread_ref)
    for h in range(heads):
        spread_ref[128 * h + 64 : 128 * h + 128, :] = weight_ref[64 * h : 64 * h + 64, :]


def spread_query_up(weight_ref, spread_ref, heads):
    spread_ref[...] = jnp.zeros_like(spread_ref)
    for h in range(heads):
        spread_ref[128 * h : 128 * h + 96, :] = weight_ref[96 * h : 96 * h + 96, :]


def row(ref):
    return ref[...].reshape(1, -1)


def low_lanes(shape):
    return lax.broadcasted_iota(jnp.int32, shape, 1) < NOPE


def causal(keys, queries, first_query):
    key_ids = lax.broadcasted_iota(jnp.int32, (keys, queries), 0)
    query_ids = lax.broadcasted_iota(jnp.int32, (keys, queries), 1) + first_query
    return key_ids <= query_ids


def attend_kernel(
    heads,
    tokens,
    first_gain,
    query_down,
    latent_down,
    query_gain,
    latent_gain,
    query_up,
    latent_up,
    out_weight,
    keep,
    low,
    high,
    first_in,
    latents,
    query_code,
    latent_code,
    queries,
    keyvals,
    rope_keys,
    heads_out,
    log_total,
    partial,
    spread,
    spread_up,
    rope_down,
    kv_all,
    rope_all,
):
    step = pl.program_id(0)

    @pl.when(step == 0)
    def _():
        spread_out_weight(out_weight, spread, heads)
        spread_query_up(query_up, spread_up, heads)
        rope_down[...] = jnp.zeros_like(rope_down)
        rope_down[64:96, :] = latent_down[KVR:, :]

    def rows_of(index, carry):
        rows = pl.ds(pl.multiple_of(index * 32, 32), 32)
        values = tokens[rows, :].astype(F32)
        first_in[rows, :] = (values * root(values) * row(first_gain)).astype(BF16)
        return carry

    lax.fori_loop(0, TILE // 32, rows_of, 0)
    taken = first_in[...]
    query_latent = dot(taken, query_down[...])
    latents[:, :QR] = query_latent
    code = (query_latent * root(query_latent) * row(query_gain)).astype(BF16)
    query_code[...] = code
    latent = dot(taken, latent_down[:KVR, :], NT)
    latents[:, QR:] = latent
    lcode = (latent * root(latent) * row(latent_gain)).astype(BF16)
    latent_code[...] = lcode
    tables = keep[...], low[...], high[...]
    rope = turn(dot(taken, rope_down[...], NT), *tables).astype(BF16)
    rope_keys[...] = rope
    here = pl.ds(pl.multiple_of(step * TILE, TILE), TILE)
    rope_all[here, :] = rope
    kv = dot(lcode, latent_up[...]).astype(BF16)
    keyvals[...] = kv
    kv_all[here, :] = kv
    raw = dot(code, spread_up[...], NT)
    for h in range(heads):
        lanes = slice(128 * h, 128 * h + 128)
        queries[:, lanes] = turn(raw[:, lanes], *tables).astype(BF16)

    def tile(index):
        keys = TILE * (index + 1)
        for h in range(heads):
            lanes = slice(128 * h, 128 * h + 128)
            kv_h = kv_all[:keys, lanes]
            key = jnp.where(low_lanes((keys, 128)), kv_h, rope_all[:keys, :])
            scores = dot(key, queries[:, lanes], NT) * SCALE
            scores = jnp.where(causal(keys, TILE, TILE * index), scores, -1e30)
            top = jnp.max(scores, axis=0, keepdims=True)
            weights = jnp.exp(scores - top)
            total = jnp.sum(weights, axis=0, keepdims=True)
            log_total[h : h + 1, :] = top + jnp.log(total)
            probs = (weights * (1.0 / total)).astype(BF16)
            heads_out[:, lanes] = dot(probs, kv_h, TN).astype(BF16)

    for index in range(2):
        pl.when(step == index)(functools.partial(tile, index))
    partial[...] = dot(heads_out[...], spread[...]).astype(BF16)


def attend(tokens, first_gain, query_down, latent_down, query_gain, latent_gain, query_up, latent_up, out_weight, tables):
    latent_down, query_up = latent_down.T, query_up.T
    length, width = tokens.shape
    heads = out_weight.shape[0] // DV
    wide = 128 * heads

    def rows(columns):
        return pl.BlockSpec((TILE, columns), lambda i: (i, 0))

    return call(
        functools.partial(attend_kernel, heads),
        (tokens, first_gain, query_down, latent_down, query_gain, latent_gain, query_up, latent_up, out_weight, *tables),
        [
            rows(width),
            full((width,)),
            full(query_down.shape),
            full(latent_down.shape),
            full((QR,)),
            full((KVR,)),
            full(query_up.shape),
            full(latent_up.shape),
            full(out_weight.shape),
            rows(128),
            rows(128),
            rows(128),
        ],
        [
            rows(width),
            rows(LAT),
            rows(QR),
            rows(KVR),
            rows(wide),
            rows(wide),
            rows(128),
            rows(wide),
            pl.BlockSpec((8, TILE), lambda i: (0, i)),
            rows(width),
        ],
        [
            shaped(length, width),
            shaped(length, LAT, dtype=F32),
            shaped(length, QR),
            shaped(length, KVR),
            shaped(length, wide),
            shaped(length, wide),
            shaped(length, 128),
            shaped(length, wide),
            shaped(8, length, dtype=F32),
            shaped(length, width),
        ],
        "attend",
        grid=(length // TILE,),
        scratch=[
            pltpu.VMEM((wide, width), BF16),
            pltpu.VMEM((wide, QR), BF16),
            pltpu.VMEM((128, width), BF16),
            pltpu.VMEM((length, wide), BF16),
            pltpu.VMEM((length, 128), BF16),
        ],
    )


def attend_back_kernel(
    heads,
    attention_back,
    out_weight,
    queries,
    keyvals,
    rope_keys,
    log_total,
    query_up,
    latent_up,
    keep,
    low,
    high,
    query_back,
    keyval_back,
    partial,
    spread,
    spread_up,
    kv_grad,
    rope_grad,
    code_grad,
):
    step = pl.program_id(0)

    @pl.when(step == 0)
    def _():
        spread_out_weight(out_weight, spread, heads)
        spread_query_up(query_up, spread_up, heads)
        kv_grad[...] = jnp.zeros_like(kv_grad)
        rope_grad[...] = jnp.zeros_like(rope_grad)

    heads_back = dot(attention_back[...], spread[...], NT).astype(BF16)
    tables = keep[...], low[...], high[...]

    def tile(index):
        keys = TILE * (index + 1)
        low_part = low_lanes((keys, 128))
        for h in range(heads):
            lanes = slice(128 * h, 128 * h + 128)
            kv_h = keyvals[:keys, lanes]
            key = jnp.where(low_part, kv_h, rope_keys[:keys, :])
            query = queries[:, lanes]
            back = heads_back[:, lanes]
            scores = dot(key, query, NT) * SCALE
            probs = jnp.exp(scores - log_total[h : h + 1, :])
            probs = jnp.where(causal(keys, TILE, TILE * index), probs, 0.0)
            prob_back = dot(kv_h, back, NT)
            mean = jnp.sum(probs * prob_back, axis=0, keepdims=True)
            score_back = (probs * (prob_back - mean)).astype(BF16)
            of_values = dot(probs.astype(BF16), back)
            of_keys = dot(score_back, query) * SCALE
            kv_grad[:keys, lanes] += of_values + jnp.where(low_part, of_keys, 0.0)
            rope_grad[:keys, :] += jnp.where(low_part, 0.0, of_keys)
            of_query = dot(score_back, key, TN) * SCALE
            query_back[:, lanes] = turn(of_query, *tables, back=True).astype(BF16)

    for index in range(2):
        pl.when(step == index)(functools.partial(tile, index))
    here = pl.ds(pl.multiple_of(step * TILE, TILE), TILE)
    code_grad[here, :] = dot(query_back[...], spread_up[...]).astype(BF16)

    @pl.when(step == 1)
    def _():
        kv = kv_grad[...].astype(BF16)
        keyval_back[...] = kv
        partial[:, :QR] = code_grad[...]
        partial[:, QR:LAT] = dot(kv, latent_up[...], NT).astype(BF16)
        partial[:, LAT:] = rope_grad[...].astype(BF16)


def attend_back(attention_back, out_weight, queries, keyvals, rope_keys, log_total, query_up, latent_up, tables, needs):
    query_up = query_up.T
    length, width = attention_back.shape
    heads = out_weight.shape[0] // DV
    wide = 128 * heads

    def rows(columns):
        return pl.BlockSpec((TILE, columns), lambda i: (i, 0))

    return call(
        functools.partial(attend_back_kernel, heads),
        (attention_back, out_weight, queries, keyvals, rope_keys, log_total, query_up, latent_up, *tables),
        [
            rows(width),
            full(out_weight.shape),
            rows(wide),
            full((length, wide)),
            full((length, 128)),
            pl.BlockSpec((8, TILE), lambda i: (0, i)),
            full(query_up.shape),
            full(latent_up.shape),
            rows(128),
            rows(128),
            rows(128),
        ],
        [rows(wide), full((length, wide)), full((length, WIDE))],
        [shaped(length, wide), shaped(length, wide), shaped(length, WIDE)],
        "attend_back",
        grid=(length // TILE,),
        scratch=[
            pltpu.VMEM((wide, width), BF16),
            pltpu.VMEM((wide, QR), BF16),
            pltpu.VMEM((length, wide), F32),
            pltpu.VMEM((length, 128), F32),
            pltpu.VMEM((length, QR), BF16),
        ],
        needs=needs,
    )


def add_up(got):
    total = got[0].astype(F32)
    for k in range(1, 8):
        total = total + got[k].astype(F32)
    return total


def residual_kernel(got, tokens, gain, residual, many):
    total = tokens[...].astype(F32) + add_up(got)
    residual[...] = total
    second_in = (total * root(total) * row(gain)).astype(BF16)
    for k in range(8):
        many[k] = second_in


def residual_of(got, own_tokens, gain, needs):
    rows, width = own_tokens.shape
    step = rows // 2
    many = pl.BlockSpec((8, step, width), lambda i: (0, i, 0))
    one = pl.BlockSpec((step, width), lambda i: (i, 0))
    return call(
        residual_kernel,
        (got.reshape(8, rows, width), own_tokens, gain),
        [many, one, full((width,))],
        [one, many],
        [shaped(rows, width, dtype=F32), shaped(8, rows, width)],
        "residual",
        grid=(2,),
        needs=needs,
    )


def residual_back_kernel(got, residual, cotangent, gain, many, gain_part):
    second_back = add_up(got)
    values = residual[...]
    factor = root(values)
    normed = values * factor
    part = jnp.sum(second_back * normed, axis=0, keepdims=True)

    @pl.when(pl.program_id(0) == 0)
    def _():
        gain_part[...] = part

    @pl.when(pl.program_id(0) > 0)
    def _():
        gain_part[...] += part

    back = cotangent[...].astype(F32) + norm_back(second_back, normed, factor, row(gain))
    back = back.astype(BF16)
    for k in range(8):
        many[k] = back


def residual_back_of(got, residual, own_cotangent, gain, needs):
    rows, width = residual.shape
    step = rows // 2
    many = pl.BlockSpec((8, step, width), lambda i: (0, i, 0))
    one = pl.BlockSpec((step, width), lambda i: (i, 0))
    return call(
        residual_back_kernel,
        (got.reshape(8, rows, width), residual, own_cotangent, gain),
        [many, one, one, full((width,))],
        [many, full((1, width))],
        [shaped(8, rows, width), shaped(1, width, dtype=F32)],
        "residual_back",
        grid=(2,),
        needs=needs,
    )


def ffn_kernel(
    second_in, gate_weight, up_weight, inner_back, gate_back, up_back, inner, partial
):
    taken = second_in[...]
    gate = dot(taken, gate_weight[...], NT)
    up = dot(taken, up_weight[...], NT)
    sigma = 1.0 / (1.0 + jnp.exp(-gate))
    act = gate * sigma
    units = gate.shape[1]
    back = inner_back[...]
    of_gate = (back * up * sigma * (1.0 + gate * (1.0 - sigma))).astype(BF16)
    of_up = (back * act).astype(BF16)
    for out, values in ((gate_back, of_gate), (up_back, of_up), (inner, (act * up).astype(BF16))):
        out[:, :units] = values
        out[:, units:] = jnp.zeros((values.shape[0], out.shape[1] - units), BF16)
    partial[...] = (dot(of_gate, gate_weight[...]) + dot(of_up, up_weight[...])).astype(BF16)


def ffn(second_in, gate_weight, up_weight, inner_back, needs):
    length, width = second_in.shape
    units = gate_weight.shape[0]
    wide = -(-units // 128) * 128

    def rows(columns):
        return pl.BlockSpec((TILE, columns), lambda i: (i, 0))

    return call(
        ffn_kernel,
        (second_in, gate_weight, up_weight, inner_back),
        [rows(width), full((units, width)), full((units, width)), rows(units)],
        [rows(wide), rows(wide), rows(wide), rows(width)],
        [shaped(length, wide)] * 3 + [shaped(length, width)],
        "ffn",
        grid=(length // TILE,),
        needs=needs,
    )


def ffn_down_kernel(me, inner, down_weight, residual, out):
    for i in range(2):
        rows = slice(i * TILE, i * TILE + TILE)
        out[rows, :] = dot(inner[rows, : down_weight.shape[0]], down_weight[...]).astype(BF16)
    count = residual.shape[0]
    own = pl.ds(pl.multiple_of(me[0] * count, count), count)
    out[own, :] = (out[own, :].astype(F32) + residual[...]).astype(BF16)


def ffn_down(me, inner, down_weight, residual, needs):
    length, width = inner.shape[0], down_weight.shape[1]
    return call(
        ffn_down_kernel,
        (inner, down_weight, residual),
        [full(inner.shape), full(down_weight.shape), full(residual.shape)],
        [full((length, width))],
        [shaped(length, width)],
        "ffn_down",
        needs=needs,
        me=me,
    )


def halves_kernel(blocks, width, starts, *refs):
    sources, outs, turned = refs[:blocks], refs[blocks : 3 * blocks], refs[3 * blocks]
    for n in range(blocks):
        source, keep, give = sources[n], outs[2 * n], outs[2 * n + 1]
        columns, each = source.shape[1], width[n]
        for c in range(0, columns, 256):
            turned[c : c + 256, :] = source[:, c : c + 256].T
        for which, out in enumerate((keep, give)):
            for k in range(8):
                first = pl.multiple_of(starts[8 * which + k] * each, 16)
                out[each * k : each * k + each, :] = turned[pl.ds(first, each), :]


def halves(starts, values, needs):
    length = values[0].shape[0]
    widths = [item.shape[1] // 16 for item in values]
    shapes = [(8 * w, length) for w in widths for _ in range(2)]
    return call(
        functools.partial(halves_kernel, len(values), widths),
        tuple(values),
        [full(item.shape) for item in values],
        [full(s) for s in shapes],
        [shaped(*s) for s in shapes],
        "halves",
        scratch=[pltpu.VMEM((max(item.shape[1] for item in values), length), BF16)],
        needs=needs,
        me=starts,
    )


ORDER = (2, 1, 3, 0)


def ffn_grads_kernel(in_keep, in_got, cot_keep, cot_got, *refs):
    ours, theirs, outs = refs[:3], refs[3:6], refs[6:]
    units = outs[0].shape[1] // 3

    def block(out):
        for n, (keep, got) in enumerate(((in_keep, in_got), (in_keep, in_got), (cot_keep, cot_got))):
            total = dot(keep[...], ours[n][...]) + dot(got[...], theirs[n][...])
            out[:, units * n : units * n + units] = total[:, :units].astype(BF16)

    for s in range(4):
        pl.when(pl.program_id(0) == s)(functools.partial(block, outs[s]))


def ffn_grads(in_keep, in_got, cot_keep, cot_got, ours, theirs, units, needs):
    length, wide = ours[0].shape
    rows = in_keep.shape[0] // 4

    def index(i):
        return (jnp.where(i == 0, 2, jnp.where(i == 1, 1, jnp.where(i == 2, 3, 0))), 0)

    left = pl.BlockSpec((rows, length), index)
    out = (rows, 3 * units)
    outs, mark = call(
        ffn_grads_kernel,
        (in_keep, in_got, cot_keep, cot_got, *ours, *theirs),
        [left] * 4 + [full((length, wide))] * 6,
        [full(out)] * 4,
        [shaped(*out)] * 4,
        "ffn_grads",
        grid=(4,),
        needs=needs,
    )
    return dict(zip(ORDER, outs)), mark


def attn_grads_kernel(widths, *refs):
    keeps, gots, ours, theirs, outs = refs[:3], refs[3:6], refs[6:9], refs[9:12], refs[12:]
    rows = sum(widths)
    for s, k in enumerate(ORDER):
        first = 0
        for n, each in enumerate(widths):
            part = slice(2 * each * k, 2 * each * k + 2 * each)
            total = dot(keeps[n][part, :], ours[n][...]) + dot(gots[n][part, :], theirs[n][...])
            total = total.astype(BF16)
            outs[s][first : first + each, :] = total[:each]
            outs[s][rows + first : rows + first + each, :] = total[each:]
            first += each


def attn_grads(keeps, gots, ours, theirs, needs):
    widths = [item.shape[0] // 8 for item in keeps]
    out = (2 * sum(widths), ours[0].shape[1])
    args = (*keeps, *gots, *ours, *theirs)
    outs, mark = call(
        functools.partial(attn_grads_kernel, widths),
        args,
        [full(item.shape) for item in args],
        [full(out)] * 4,
        [shaped(*out)] * 4,
        "attn_grads",
        needs=needs,
    )
    return dict(zip(ORDER, outs)), mark


def add_chips_kernel(*refs):
    ins, keep, give = refs[:8], refs[8], refs[9]
    keep[...] = sum(item[...].astype(F32) for item in ins[:4])
    give[...] = sum(item[...].astype(F32) for item in ins[4:]).astype(BF16)


def add_chips(items, needs):
    rows, width = items[0].shape[0] // 2, items[0].shape[1]
    step = 32
    count = rows // step
    mine = pl.BlockSpec((step, width), lambda i: (i, 0))
    other = pl.BlockSpec((step, width), lambda i: (i + count, 0))
    outs, mark = call(
        add_chips_kernel,
        (*items, *items),
        [mine] * 4 + [other] * 4,
        [mine, mine],
        [shaped(rows, width, dtype=F32), shaped(rows, width)],
        "add_chips",
        grid=(count,),
        needs=needs,
    )
    return outs, mark


def over_y(blocks):
    return [blocks[0]] + [
        lax.ppermute(blocks[k], "y", [(i, i ^ k) for i in range(4)]) for k in ORDER[:3]
    ]


def over_cores(values):
    return lax.ppermute(values, "core", SWAP)


def latents_back_kernel(
    got, latents, query_gain, latent_gain, keep, low, high, many, own, gain_part
):
    total = add_up(got)

    def back(lanes, gain):
        upstream, values = total[:, lanes], latents[:, lanes]
        factor = root(values)
        normed = values * factor
        gain_part[:, lanes] = jnp.sum(upstream * normed, axis=0, keepdims=True)
        return norm_back(upstream, normed, factor, row(gain)).astype(BF16)

    own[:, :QR] = back(slice(0, QR), query_gain)
    own[:, QR:LAT] = back(slice(QR, LAT), latent_gain)
    own[:, LAT:] = turn(total[:, LAT:], keep[...], low[...], high[...], back=True).astype(BF16)
    for k in range(8):
        many[k] = own[...]


def latents_back_of(got, own_latents, query_gain, latent_gain, own_tables, needs):
    rows = own_latents.shape[0]
    args = (got.reshape(8, rows, WIDE), own_latents, query_gain, latent_gain, *own_tables)
    return call(
        latents_back_kernel,
        args,
        [full(item.shape) for item in args],
        [full((8, rows, WIDE)), full((rows, WIDE)), full((1, LAT))],
        [shaped(8, rows, WIDE), shaped(rows, WIDE), shaped(1, LAT, dtype=F32)],
        "latents_back",
        needs=needs,
    )


def first_back_of(raw_back, query_down, latent_down, rope_down):
    rope_down[...] = jnp.zeros_like(rope_down)
    rope_down[64:96, :] = latent_down[KVR:, :]
    return (
        dot(raw_back[:, :QR], query_down[...], NT)
        + dot(raw_back[:, QR:LAT], latent_down[:KVR, :])
        + dot(raw_back[:, LAT:], rope_down[...])
    )


def first_gain_kernel(raw_back, tokens, query_down, latent_down, gain_part, rope_down):
    first_back = first_back_of(raw_back, query_down, latent_down, rope_down)
    values = tokens[...].astype(F32)
    gain_part[...] = jnp.sum(first_back * (values * root(values)), axis=0, keepdims=True)


def first_gain_of(own_raw_back, own_tokens, query_down, latent_down, needs):
    width = own_tokens.shape[1]
    args = (own_raw_back, own_tokens, query_down, latent_down.T)
    return call(
        first_gain_kernel,
        args,
        [full(item.shape) for item in args],
        [full((1, width))],
        [shaped(1, width, dtype=F32)],
        "first_gain",
        scratch=[pltpu.VMEM((128, width), BF16)],
        needs=needs,
    )


def tokens_back_kernel(
    raw_back, tokens, attention_back, query_down, latent_down, gain, tokens_grad, rope_down
):
    first_back = first_back_of(raw_back, query_down, latent_down, rope_down)
    values = tokens[...].astype(F32)
    factor = root(values)
    tokens_grad[...] = attention_back[...].astype(F32) + norm_back(
        first_back, values * factor, factor, row(gain)
    )


def tokens_back_of(raw_back, tokens, attention_back, query_down, latent_down, gain, needs):
    length, width = tokens.shape

    def rows(columns):
        return pl.BlockSpec((TILE, columns), lambda i: (i, 0))

    return call(
        tokens_back_kernel,
        (raw_back, tokens, attention_back, query_down, latent_down.T, gain),
        [
            rows(WIDE),
            rows(width),
            rows(width),
            full(query_down.shape),
            full(latent_down.shape[::-1]),
            full((width,)),
        ],
        [rows(width)],
        [shaped(length, width, dtype=F32)],
        "tokens_back",
        grid=(length // TILE,),
        scratch=[pltpu.VMEM((128, width), BF16)],
        needs=needs,
    )


def finish_ffn_kernel(keep, got, gate, up, down):
    units = gate.shape[1]
    for n, out in enumerate((gate, up, down)):
        lanes = slice(units * n, units * n + units)
        out[...] = keep[:, lanes] + got[:, lanes].astype(F32)


def finish_ffn(keep, got):
    rows, width = keep.shape
    out = (rows, width // 3)
    return call(
        finish_ffn_kernel,
        (keep, got),
        [full(keep.shape), full(got.shape)],
        [full(out)] * 3,
        [shaped(*out, dtype=F32)] * 3,
        "finish_ffn",
    )[0]


def finish_attn_kernel(heads, keep, got, out_grad, query_grad, latent_grad):
    total = keep[...] + got[...].astype(F32)
    for h in range(heads):
        lanes = slice(128 * h, 128 * h + 128)
        out_grad[:, 64 * h : 64 * h + 64] = total[:160, 128 * h + 64 : 128 * h + 128]
        query_grad[:, 96 * h : 96 * h + 96] = total[160:208, 128 * h : 128 * h + 96]
    latent_grad[...] = total[208:224]


def finish_attn(keep, got):
    heads = keep.shape[1] // 128
    outs = [(160, 64 * heads), (48, 96 * heads), (16, 128 * heads)]
    return call(
        functools.partial(finish_attn_kernel, heads),
        (keep, got),
        [full(keep.shape), full(got.shape)],
        [full(s) for s in outs],
        [shaped(*s, dtype=F32) for s in outs],
        "finish_attn",
    )[0]


def finish_down_kernel(everyone, query_grad, latent_grad, gains):
    for t in range(8):
        values = everyone[t].astype(F32)
        query_grad[20 * t : 20 * t + 20, :] = values[:20, :QR]
        latent_grad[20 * t : 20 * t + 20, :KVR] = values[:20, QR:LAT]
        latent_grad[20 * t : 20 * t + 20, KVR:] = values[:20, LAT + 64 : LAT + 96]
    gains[...] = sum(everyone[t, 16:24, :].astype(F32) for t in range(8))[4:5, :]


def finish_down(everyone):
    everyone = everyone.reshape(8, 24, WIDE)
    outs = [(160, QR), (160, KVR + ROPE), (1, WIDE)]
    return call(
        finish_down_kernel,
        (everyone,),
        [full(everyone.shape)],
        [full(s) for s in outs],
        [shaped(*s, dtype=F32) for s in outs],
        "finish_down",
    )[0]


def exchange(blocks):
    return lax.all_to_all(blocks.reshape(-1, blocks.shape[-1]), TP, 0, 0, tiled=True)


def on_device(
    tokens,
    first_gain,
    query_down,
    query_gain,
    query_up,
    latent_down,
    latent_gain,
    latent_up,
    out_weight,
    second_gain,
    gate_weight,
    up_weight,
    down_weight,
    cotangent,
):
    length = tokens.shape[0]
    rows = length // 8
    me = lax.axis_index(TP).astype(jnp.int32).reshape(1)
    y, xl, core = lax.axis_index("y"), lax.axis_index("xl"), lax.axis_index("core")
    starts = jnp.stack(
        [
            ((y ^ k) * 2 + (xl ^ j)) * 2 + c
            for c in (core, 1 - core)
            for k in range(4)
            for j in range(2)
        ]
    ).astype(jnp.int32)
    tables = rope_tables(length)

    def own(values):
        return lax.dynamic_slice_in_dim(values, me[0] * rows, rows, 0)

    gate_turned, up_turned = gate_weight.T, up_weight.T

    (
        first_in,
        latents,
        query_code,
        latent_code,
        queries,
        keyvals,
        rope_keys,
        heads_out,
        log_total,
        attn_partial,
    ), started = attend(
        tokens,
        first_gain,
        query_down,
        latent_down,
        query_gain,
        latent_gain,
        query_up,
        latent_up,
        out_weight,
        tables,
    )
    attn_got = exchange(attn_partial)

    (cot_keep, cot_give), picked = halves(starts, [cotangent], [started])
    inner_back = dot(cotangent, down_weight, NT)
    cot_got = over_cores(cot_give)
    own_tokens, own_cotangent = own(tokens), own(cotangent)

    (residual, second_many), _ = residual_of(
        attn_got, own_tokens, second_gain, [picked, inner_back]
    )
    second_in = exchange(second_many)

    turned_in = first_in.T.reshape(16, 8, 20, length)
    own_in = lax.dynamic_slice_in_dim(turned_in, me[0], 1, 1).reshape(320, length)
    (code_keep, code_give, lat_keep, lat_give), picked = halves(
        starts, [query_code, latent_code], [residual]
    )
    code_got, lat_got = over_cores(code_give), over_cores(lat_give)
    heads_got = over_cores(heads_out)

    (gate_back, up_back, inner, back_partial), done = ffn(
        second_in, gate_turned, up_turned, inner_back, [picked, own_in]
    )
    back_got = exchange(back_partial)

    ours = (gate_back, up_back, inner)
    theirs = [over_cores(item) for item in ours]
    (in_keep, in_give), _ = halves(starts, [second_in], [done])
    in_got = over_cores(in_give)
    ffn_blocks, done = ffn_grads(in_keep, in_got, cot_keep, cot_got, ours, theirs, gate_weight.shape[1], [])
    ffn_parts = over_y(ffn_blocks)

    (back_many, second_gain_part), _ = residual_back_of(
        back_got, residual, own_cotangent, second_gain, [done]
    )
    attention_back = exchange(back_many)
    (ffn_partial,), done = ffn_down(me, inner, down_weight, residual, [second_gain_part])

    (query_raw_back, keyval_back, latents_partial), back_done = attend_back(
        attention_back,
        out_weight,
        queries,
        keyvals,
        rope_keys,
        log_total,
        query_up,
        latent_up,
        tables,
        [done, ffn_parts[2], ffn_parts[3]],
    )
    mixed = lax.psum(ffn_partial, TP)
    latents_got = exchange(latents_partial)

    (out_keep, out_give), _ = halves(starts, [attention_back], [back_done])
    out_got = over_cores(out_give)
    raw_got, kv_got = over_cores(query_raw_back), over_cores(keyval_back)
    attn_blocks, done = attn_grads(
        (out_keep, code_keep, lat_keep),
        (out_got, code_got, lat_got),
        (heads_out, query_raw_back, keyval_back),
        (heads_got, raw_got, kv_got),
        [],
    )

    (raw_many, own_raw, latent_gain_parts), _ = latents_back_of(
        latents_got,
        own(latents),
        query_gain,
        latent_gain,
        [own(item) for item in tables],
        [done, ffn_parts[1]],
    )
    raw_back = exchange(raw_many)
    (first_gain_part,), done = first_gain_of(own_raw, own_tokens, query_down, latent_down, [])
    (ffn_keep, ffn_give), done = add_chips(ffn_parts, [done])
    ffn_got = lax.ppermute(ffn_give, "xl", SWAP)
    attn_parts = over_y(attn_blocks)

    down_part = dot(own_in, raw_back).astype(BF16).reshape(16, 20, WIDE)
    gains = jnp.concatenate(
        [
            first_gain_part.reshape(16, -1),
            second_gain_part.reshape(16, -1),
            latent_gain_parts[0, :QR].reshape(16, -1),
            latent_gain_parts[0, QR:].reshape(16, -1),
        ],
        axis=1,
    ).astype(BF16)
    wide_gains = jnp.pad(gains, ((0, 0), (0, WIDE - gains.shape[1])))
    parts = jnp.concatenate(
        [down_part, wide_gains[:, None, :], jnp.zeros((16, 3, WIDE), BF16)], axis=1
    )
    (tokens_grad,), done = tokens_back_of(
        raw_back, tokens, attention_back, query_down, latent_down, first_gain, [parts, ffn_got, *attn_parts[1:]]
    )
    summed = jnp.sum(
        lax.all_to_all(parts, DP, 0, 0, tiled=True).astype(F32), axis=0
    ).astype(BF16)
    everyone = exchange(jnp.broadcast_to(summed[None], (8,) + summed.shape))

    (attn_keep, attn_give), _ = add_chips(attn_parts, [done])
    attn_got = lax.ppermute(attn_give, "xl", SWAP)
    gate_weight_grad, up_weight_grad, down_weight_grad = finish_ffn(ffn_keep, ffn_got)
    out_weight_grad, query_up_grad, latent_up_grad = finish_attn(attn_keep, attn_got)
    query_down_grad, latent_down_grad, gain_grads = finish_down(everyone)
    gain_grads = gain_grads[0]

    return (
        mixed,
        tokens_grad,
        gain_grads[:160],
        query_down_grad,
        gain_grads[320:368],
        query_up_grad,
        latent_down_grad,
        gain_grads[368:384],
        latent_up_grad,
        out_weight_grad.T,
        gain_grads[160:320],
        gate_weight_grad,
        up_weight_grad,
        down_weight_grad.T,
    )


def solution(mesh):
    grid = Mesh(mesh.devices.reshape(4, 2, 2, 2, 4), ("y", "xl", "core", "xh", "z"))
    in_specs = (
        P(DP, None),
        P(),
        P(),
        P(),
        P(None, TP),
        P(),
        P(),
        P(None, TP),
        P(TP, None),
        P(),
        P(None, TP),
        P(None, TP),
        P(TP, None),
        P(DP, None),
    )
    out_specs = (
        P(DP, None),
        P(DP, None),
        P(DP),
        P(DP, None),
        P(DP),
        P(DP, TP),
        P(DP, None),
        P(DP),
        P(DP, TP),
        P(TP, DP),
        P(DP),
        P(DP, TP),
        P(DP, TP),
        P(TP, DP),
    )
    return jax.shard_map(
        on_device, mesh=grid, in_specs=in_specs, out_specs=out_specs, check_vma=False
    )
```

```python
import functools

import jax
import jax.numpy as jnp
import numpy as np
from jax import lax
from jax.experimental import pallas as pl
from jax.experimental.pallas import tpu as pltpu
from jax.sharding import Mesh, PartitionSpec as P

NOPE = 64
ROPE = 32
DV = 64
KVR = 256
QR = 768
LAT = QR + KVR
WIDE = LAT + 128

EPS = 1e-05
BASE = 10000.0
SCALE = (NOPE + ROPE) ** (-0.5)

DP = ("y", "xl", "core")
TP = ("xh", "z")
SWAP = [(0, 1), (1, 0)]
F32 = jnp.float32
BF16 = jnp.bfloat16
NT = (((1,), (1,)), ((), ()))
TN = (((0,), (0,)), ((), ()))
NN = (((1,), (0,)), ((), ()))
TILE = 256


def dot(left, right, dims=NN):
    return lax.dot_general(left, right, dims, preferred_element_type=F32)


def params(limit=56):
    return pltpu.CompilerParams(vmem_limit_bytes=limit * 2**20)


HBM = pl.BlockSpec(memory_space=pltpu.HBM)


def call(kernel, args, in_specs, out_specs, out_shape, name, grid=(1,), scratch=(), needs=(), me=None, limit=60):
    first = 0 if me is None else 1
    n_in, n_out = len(args), len(out_shape)

    def body(*refs):
        ins = refs[: first + n_in]
        rest = refs[first + n_in + len(needs) :]
        mark = rest[n_out]

        @pl.when(pl.program_id(0) == 0)
        def _():
            mark[...] = jnp.zeros_like(mark)

        kernel(*ins, *rest[:n_out], *rest[n_out + 1 :])

    *outs, mark = pl.pallas_call(
        body,
        grid_spec=pltpu.PrefetchScalarGridSpec(
            num_scalar_prefetch=first,
            grid=grid,
            in_specs=list(in_specs) + [HBM] * len(needs),
            out_specs=list(out_specs) + [full((8, 128))],
            scratch_shapes=list(scratch),
        ),
        out_shape=list(out_shape) + [jax.ShapeDtypeStruct((8, 128), F32)],
        compiler_params=params(limit),
        name=name,
    )(*(() if me is None else (me,)), *args, *needs)
    return outs, mark


def shaped(*shape, dtype=BF16):
    return jax.ShapeDtypeStruct(shape, dtype)


def full(shape):
    return pl.BlockSpec(shape, lambda *_: (0,) * len(shape))


def rope_tables(length):
    half = ROPE // 2
    rates = np.exp(np.arange(half, dtype=np.float32) * np.float32(-2.0 * np.log(BASE) / ROPE))
    angles = np.arange(length, dtype=np.float32)[:, None] * rates.astype(np.float32)[None, :]
    cosine, sine = np.cos(angles), np.sin(angles)
    keep = np.zeros((length, 128), np.float32)
    keep[:, :NOPE] = 1.0
    keep[:, 64:80] = cosine
    keep[:, 80:96] = cosine
    low = np.zeros((length, 128), np.float32)
    low[:, 64:80] = -sine
    high = np.zeros((length, 128), np.float32)
    high[:, 80:96] = sine
    return jnp.asarray(keep), jnp.asarray(low), jnp.asarray(high)


def turn(values, keep, low, high, back=False):
    moved = pltpu.roll(values, 112, 1) * low + pltpu.roll(values, 16, 1) * high
    return values * keep - moved if back else values * keep + moved


def root(values):
    return lax.rsqrt(jnp.mean(values * values, axis=-1, keepdims=True) + EPS)


def norm_back(upstream, normed, factor, gain):
    scaled = upstream * gain
    return factor * (scaled - normed * jnp.mean(scaled * normed, axis=-1, keepdims=True))


def spread_out_weight(weight_ref, spread_ref, heads):
    spread_ref[...] = jnp.zeros_like(spread_ref)
    for h in range(heads):
        spread_ref[128 * h + 64 : 128 * h + 128, :] = weight_ref[64 * h : 64 * h + 64, :]


def spread_query_up(weight_ref, spread_ref, heads):
    spread_ref[...] = jnp.zeros_like(spread_ref)
    for h in range(heads):
        spread_ref[128 * h : 128 * h + 96, :] = weight_ref[96 * h : 96 * h + 96, :]


def row(ref):
    return ref[...].reshape(1, -1)


def low_lanes(shape):
    return lax.broadcasted_iota(jnp.int32, shape, 1) < NOPE


def causal(keys, queries, first_query):
    key_ids = lax.broadcasted_iota(jnp.int32, (keys, queries), 0)
    query_ids = lax.broadcasted_iota(jnp.int32, (keys, queries), 1) + first_query
    return key_ids <= query_ids


def attend_kernel(
    heads,
    tokens,
    first_gain,
    query_down,
    latent_down,
    query_gain,
    latent_gain,
    query_up,
    latent_up,
    out_weight,
    keep,
    low,
    high,
    first_in,
    latents,
    query_code,
    latent_code,
    queries,
    keyvals,
    rope_keys,
    heads_out,
    log_total,
    partial,
    spread,
    spread_up,
    rope_down,
    kv_all,
    rope_all,
):
    step = pl.program_id(0)

    @pl.when(step == 0)
    def _():
        spread_out_weight(out_weight, spread, heads)
        spread_query_up(query_up, spread_up, heads)
        rope_down[...] = jnp.zeros_like(rope_down)
        rope_down[64:96, :] = latent_down[KVR:, :]

    def rows_of(index, carry):
        rows = pl.ds(pl.multiple_of(index * 32, 32), 32)
        values = tokens[rows, :].astype(F32)
        first_in[rows, :] = (values * root(values) * row(first_gain)).astype(BF16)
        return carry

    lax.fori_loop(0, TILE // 32, rows_of, 0)
    taken = first_in[...]
    query_latent = dot(taken, query_down[...])
    latents[:, :QR] = query_latent
    code = (query_latent * root(query_latent) * row(query_gain)).astype(BF16)
    query_code[...] = code
    latent = dot(taken, latent_down[:KVR, :], NT)
    latents[:, QR:] = latent
    lcode = (latent * root(latent) * row(latent_gain)).astype(BF16)
    latent_code[...] = lcode
    tables = keep[...], low[...], high[...]
    rope = turn(dot(taken, rope_down[...], NT), *tables).astype(BF16)
    rope_keys[...] = rope
    here = pl.ds(pl.multiple_of(step * TILE, TILE), TILE)
    rope_all[here, :] = rope
    kv = dot(lcode, latent_up[...]).astype(BF16)
    keyvals[...] = kv
    kv_all[here, :] = kv
    raw = dot(code, spread_up[...], NT)
    for h in range(heads):
        lanes = slice(128 * h, 128 * h + 128)
        queries[:, lanes] = turn(raw[:, lanes], *tables).astype(BF16)

    def tile(index):
        keys = TILE * (index + 1)
        for h in range(heads):
            lanes = slice(128 * h, 128 * h + 128)
            kv_h = kv_all[:keys, lanes]
            key = jnp.where(low_lanes((keys, 128)), kv_h, rope_all[:keys, :])
            scores = dot(key, queries[:, lanes], NT) * SCALE
            scores = jnp.where(causal(keys, TILE, TILE * index), scores, -1e30)
            top = jnp.max(scores, axis=0, keepdims=True)
            weights = jnp.exp(scores - top)
            total = jnp.sum(weights, axis=0, keepdims=True)
            log_total[h : h + 1, :] = top + jnp.log(total)
            probs = (weights * (1.0 / total)).astype(BF16)
            heads_out[:, lanes] = dot(probs, kv_h, TN).astype(BF16)

    for index in range(2):
        pl.when(step == index)(functools.partial(tile, index))
    partial[...] = dot(heads_out[...], spread[...]).astype(BF16)


def attend(tokens, first_gain, query_down, latent_down, query_gain, latent_gain, query_up, latent_up, out_weight, tables):
    latent_down, query_up = latent_down.T, query_up.T
    length, width = tokens.shape
    heads = out_weight.shape[0] // DV
    wide = 128 * heads

    def rows(columns):
        return pl.BlockSpec((TILE, columns), lambda i: (i, 0))

    return call(
        functools.partial(attend_kernel, heads),
        (tokens, first_gain, query_down, latent_down, query_gain, latent_gain, query_up, latent_up, out_weight, *tables),
        [
            rows(width),
            full((width,)),
            full(query_down.shape),
            full(latent_down.shape),
            full((QR,)),
            full((KVR,)),
            full(query_up.shape),
            full(latent_up.shape),
            full(out_weight.shape),
            rows(128),
            rows(128),
            rows(128),
        ],
        [
            rows(width),
            rows(LAT),
            rows(QR),
            rows(KVR),
            rows(wide),
            rows(wide),
            rows(128),
            rows(wide),
            pl.BlockSpec((8, TILE), lambda i: (0, i)),
            rows(width),
        ],
        [
            shaped(length, width),
            shaped(length, LAT, dtype=F32),
            shaped(length, QR),
            shaped(length, KVR),
            shaped(length, wide),
            shaped(length, wide),
            shaped(length, 128),
            shaped(length, wide),
            shaped(8, length, dtype=F32),
            shaped(length, width),
        ],
        "attend",
        grid=(length // TILE,),
        scratch=[
            pltpu.VMEM((wide, width), BF16),
            pltpu.VMEM((wide, QR), BF16),
            pltpu.VMEM((128, width), BF16),
            pltpu.VMEM((length, wide), BF16),
            pltpu.VMEM((length, 128), BF16),
        ],
    )


def attend_back_kernel(
    heads,
    attention_back,
    out_weight,
    queries,
    keyvals,
    rope_keys,
    log_total,
    query_up,
    latent_up,
    keep,
    low,
    high,
    query_back,
    keyval_back,
    partial,
    spread,
    spread_up,
    kv_grad,
    rope_grad,
    code_grad,
):
    step = pl.program_id(0)

    @pl.when(step == 0)
    def _():
        spread_out_weight(out_weight, spread, heads)
        spread_query_up(query_up, spread_up, heads)
        kv_grad[...] = jnp.zeros_like(kv_grad)
        rope_grad[...] = jnp.zeros_like(rope_grad)

    heads_back = dot(attention_back[...], spread[...], NT).astype(BF16)
    tables = keep[...], low[...], high[...]

    def tile(index):
        keys = TILE * (index + 1)
        low_part = low_lanes((keys, 128))
        for h in range(heads):
            lanes = slice(128 * h, 128 * h + 128)
            kv_h = keyvals[:keys, lanes]
            key = jnp.where(low_part, kv_h, rope_keys[:keys, :])
            query = queries[:, lanes]
            back = heads_back[:, lanes]
            scores = dot(key, query, NT) * SCALE
            probs = jnp.exp(scores - log_total[h : h + 1, :])
            probs = jnp.where(causal(keys, TILE, TILE * index), probs, 0.0)
            prob_back = dot(kv_h, back, NT)
            mean = jnp.sum(probs * prob_back, axis=0, keepdims=True)
            score_back = (probs * (prob_back - mean)).astype(BF16)
            of_values = dot(probs.astype(BF16), back)
            of_keys = dot(score_back, query) * SCALE
            kv_grad[:keys, lanes] += of_values + jnp.where(low_part, of_keys, 0.0)
            rope_grad[:keys, :] += jnp.where(low_part, 0.0, of_keys)
            of_query = dot(score_back, key, TN) * SCALE
            query_back[:, lanes] = turn(of_query, *tables, back=True).astype(BF16)

    for index in range(2):
        pl.when(step == index)(functools.partial(tile, index))
    here = pl.ds(pl.multiple_of(step * TILE, TILE), TILE)
    code_grad[here, :] = dot(query_back[...], spread_up[...]).astype(BF16)

    @pl.when(step == 1)
    def _():
        kv = kv_grad[...].astype(BF16)
        keyval_back[...] = kv
        partial[:, :QR] = code_grad[...]
        partial[:, QR:LAT] = dot(kv, latent_up[...], NT).astype(BF16)
        partial[:, LAT:] = rope_grad[...].astype(BF16)


def attend_back(attention_back, out_weight, queries, keyvals, rope_keys, log_total, query_up, latent_up, tables, needs):
    query_up = query_up.T
    length, width = attention_back.shape
    heads = out_weight.shape[0] // DV
    wide = 128 * heads

    def rows(columns):
        return pl.BlockSpec((TILE, columns), lambda i: (i, 0))

    return call(
        functools.partial(attend_back_kernel, heads),
        (attention_back, out_weight, queries, keyvals, rope_keys, log_total, query_up, latent_up, *tables),
        [
            rows(width),
            full(out_weight.shape),
            rows(wide),
            full((length, wide)),
            full((length, 128)),
            pl.BlockSpec((8, TILE), lambda i: (0, i)),
            full(query_up.shape),
            full(latent_up.shape),
            rows(128),
            rows(128),
            rows(128),
        ],
        [rows(wide), full((length, wide)), full((length, WIDE))],
        [shaped(length, wide), shaped(length, wide), shaped(length, WIDE)],
        "attend_back",
        grid=(length // TILE,),
        scratch=[
            pltpu.VMEM((wide, width), BF16),
            pltpu.VMEM((wide, QR), BF16),
            pltpu.VMEM((length, wide), F32),
            pltpu.VMEM((length, 128), F32),
            pltpu.VMEM((length, QR), BF16),
        ],
        needs=needs,
    )


def add_up(got):
    total = got[0].astype(F32)
    for k in range(1, 8):
        total = total + got[k].astype(F32)
    return total


def chunked(rows, body):
    def step(index, carry):
        body(pl.ds(pl.multiple_of(index * 16, 16), 16))
        return carry

    lax.fori_loop(0, rows // 16, step, 0)


def residual_kernel(me, got, tokens, gain, residual, many, own, sem):
    rows = own.shape[0]
    first = pl.multiple_of(me[0] * rows, rows)
    copy = pltpu.make_async_copy(tokens.at[pl.ds(first, rows), :], own, sem)
    copy.start()
    copy.wait()

    def part(here):
        total = own[here, :].astype(F32)
        for k in range(8):
            total = total + got[k, here, :].astype(F32)
        residual[here, :] = total
        second_in = (total * root(total) * row(gain)).astype(BF16)
        for k in range(8):
            many[k, here, :] = second_in

    chunked(rows, part)


def residual_of(me, got, tokens, gain, needs):
    width = tokens.shape[1]
    rows = tokens.shape[0] // 8
    return call(
        residual_kernel,
        (got.reshape(8, rows, width), tokens, gain),
        [full((8, rows, width)), HBM, full((width,))],
        [full((rows, width)), full((8, rows, width))],
        [shaped(rows, width, dtype=F32), shaped(8, rows, width)],
        "residual",
        scratch=[pltpu.VMEM((rows, width), BF16), pltpu.SemaphoreType.DMA],
        needs=needs,
        me=me,
        limit=24,
    )


def residual_back_kernel(me, got, residual, cotangent, gain, many, gain_part, own, kept, sems):
    rows = own.shape[0]
    first = pl.multiple_of(me[0] * rows, rows)
    copies = [
        pltpu.make_async_copy(cotangent.at[pl.ds(first, rows), :], own, sems.at[0]),
        pltpu.make_async_copy(residual, kept, sems.at[1]),
    ]
    for copy in copies:
        copy.start()
    gain_part[...] = jnp.zeros_like(gain_part)
    for copy in copies:
        copy.wait()

    def part(here):
        second_back = got[0, here, :].astype(F32)
        for k in range(1, 8):
            second_back = second_back + got[k, here, :].astype(F32)
        values = kept[here, :]
        factor = root(values)
        normed = values * factor
        gain_part[...] += jnp.sum(second_back * normed, axis=0, keepdims=True)
        back = own[here, :].astype(F32) + norm_back(second_back, normed, factor, row(gain))
        back = back.astype(BF16)
        for k in range(8):
            many[k, here, :] = back

    chunked(rows, part)


def residual_back_of(me, got, residual, cotangent, gain, needs):
    rows, width = residual.shape
    return call(
        residual_back_kernel,
        (got.reshape(8, rows, width), residual, cotangent, gain),
        [full((8, rows, width)), HBM, HBM, full((width,))],
        [full((8, rows, width)), full((1, width))],
        [shaped(8, rows, width), shaped(1, width, dtype=F32)],
        "residual_back",
        scratch=[
            pltpu.VMEM((rows, width), BF16),
            pltpu.VMEM((rows, width), F32),
            pltpu.SemaphoreType.DMA((2,)),
        ],
        needs=needs,
        me=me,
        limit=24,
    )


def ffn_kernel(
    second_in, gate_weight, up_weight, inner_back, gate_back, up_back, inner, partial
):
    taken = second_in[...]
    gate = dot(taken, gate_weight[...], NT)
    up = dot(taken, up_weight[...], NT)
    sigma = 1.0 / (1.0 + jnp.exp(-gate))
    act = gate * sigma
    units = gate.shape[1]
    back = inner_back[...]
    of_gate = (back * up * sigma * (1.0 + gate * (1.0 - sigma))).astype(BF16)
    of_up = (back * act).astype(BF16)
    for out, values in ((gate_back, of_gate), (up_back, of_up), (inner, (act * up).astype(BF16))):
        out[:, :units] = values
        out[:, units:] = jnp.zeros((values.shape[0], out.shape[1] - units), BF16)
    partial[...] = (dot(of_gate, gate_weight[...]) + dot(of_up, up_weight[...])).astype(BF16)


def ffn(second_in, gate_weight, up_weight, inner_back, needs):
    length, width = second_in.shape
    units = gate_weight.shape[0]
    wide = -(-units // 128) * 128

    def rows(columns):
        return pl.BlockSpec((TILE, columns), lambda i: (i, 0))

    return call(
        ffn_kernel,
        (second_in, gate_weight, up_weight, inner_back),
        [rows(width), full((units, width)), full((units, width)), rows(units)],
        [rows(wide), rows(wide), rows(wide), rows(width)],
        [shaped(length, wide)] * 3 + [shaped(length, width)],
        "ffn",
        grid=(length // TILE,),
        needs=needs,
    )


def ffn_down_kernel(me, inner, down_weight, residual, out):
    for i in range(2):
        rows = slice(i * TILE, i * TILE + TILE)
        out[rows, :] = dot(inner[rows, : down_weight.shape[0]], down_weight[...]).astype(BF16)
    count = residual.shape[0]
    own = pl.ds(pl.multiple_of(me[0] * count, count), count)
    out[own, :] = (out[own, :].astype(F32) + residual[...]).astype(BF16)


def ffn_down(me, inner, down_weight, residual, needs):
    length, width = inner.shape[0], down_weight.shape[1]
    return call(
        ffn_down_kernel,
        (inner, down_weight, residual),
        [full(inner.shape), full(down_weight.shape), full(residual.shape)],
        [full((length, width))],
        [shaped(length, width)],
        "ffn_down",
        needs=needs,
        me=me,
    )


def halves_kernel(blocks, width, starts, *refs):
    sources, outs, turned = refs[:blocks], refs[blocks : 3 * blocks], refs[3 * blocks]
    for n in range(blocks):
        source, keep, give = sources[n], outs[2 * n], outs[2 * n + 1]
        columns, each = source.shape[1], width[n]
        for c in range(0, columns, 256):
            turned[c : c + 256, :] = source[:, c : c + 256].T
        for which, out in enumerate((keep, give)):
            for k in range(8):
                first = pl.multiple_of(starts[8 * which + k] * each, 16)
                out[each * k : each * k + each, :] = turned[pl.ds(first, each), :]


def halves(starts, values, needs):
    length = values[0].shape[0]
    widths = [item.shape[1] // 16 for item in values]
    shapes = [(8 * w, length) for w in widths for _ in range(2)]
    return call(
        functools.partial(halves_kernel, len(values), widths),
        tuple(values),
        [full(item.shape) for item in values],
        [full(s) for s in shapes],
        [shaped(*s) for s in shapes],
        "halves",
        scratch=[pltpu.VMEM((max(item.shape[1] for item in values), length), BF16)],
        needs=needs,
        me=starts,
    )


ORDER = (2, 1, 3, 0)


def ffn_grads_kernel(in_keep, in_got, cot_keep, cot_got, *refs):
    ours, theirs, outs = refs[:3], refs[3:6], refs[6:]
    units = outs[0].shape[1] // 3

    def block(*parts):
        for n, (keep, got) in enumerate(((in_keep, in_got), (in_keep, in_got), (cot_keep, cot_got))):
            total = dot(keep[...], ours[n][...]) + dot(got[...], theirs[n][...])
            total = total[:, :units].astype(BF16)
            first = 0
            for out in parts:
                count = out.shape[0]
                out[:, units * n : units * n + units] = total[first : first + count]
                first += count

    for s, parts in enumerate((outs[:2], outs[2:3], outs[3:4], outs[4:])):
        pl.when(pl.program_id(0) == s)(functools.partial(block, *parts))


def ffn_grads(in_keep, in_got, cot_keep, cot_got, ours, theirs, units, needs):
    length, wide = ours[0].shape
    rows = in_keep.shape[0] // 4

    def index(i):
        return (jnp.where(i == 0, 2, jnp.where(i == 1, 1, jnp.where(i == 2, 3, 0))), 0)

    left = pl.BlockSpec((rows, length), index)
    out = (rows, 3 * units)
    outs = [(rows // 2, 3 * units)] * 2 + [out] * 3
    return call(
        ffn_grads_kernel,
        (in_keep, in_got, cot_keep, cot_got, *ours, *theirs),
        [left] * 4 + [full((length, wide))] * 6,
        [full(s) for s in outs],
        [shaped(*s) for s in outs],
        "ffn_grads",
        grid=(4,),
        needs=needs,
    )


def attn_grads_kernel(widths, *refs):
    keeps, gots, ours, theirs, outs = refs[:3], refs[3:6], refs[6:9], refs[9:12], refs[12:]
    rows = sum(widths)
    places = [((0, 0), (1, 0)), ((2, 0), (2, rows)), ((3, 0), (3, rows)), ((4, 0), (4, rows))]
    for (near, far), k in zip(places, ORDER):
        first = 0
        for n, each in enumerate(widths):
            part = slice(2 * each * k, 2 * each * k + 2 * each)
            total = dot(keeps[n][part, :], ours[n][...]) + dot(gots[n][part, :], theirs[n][...])
            total = total.astype(BF16)
            for (out, start), half in ((near, total[:each]), (far, total[each:])):
                outs[out][start + first : start + first + each, :] = half
            first += each


def attn_grads(keeps, gots, ours, theirs, needs):
    widths = [item.shape[0] // 8 for item in keeps]
    rows, wide = sum(widths), ours[0].shape[1]
    args = (*keeps, *gots, *ours, *theirs)
    outs = [(rows, wide)] * 2 + [(2 * rows, wide)] * 3
    return call(
        functools.partial(attn_grads_kernel, widths),
        args,
        [full(item.shape) for item in args],
        [full(s) for s in outs],
        [shaped(*s) for s in outs],
        "attn_grads",
        needs=needs,
    )


UP = [(i, (i + 1) % 4) for i in range(4)]
DOWN = [(i, (i + 3) % 4) for i in range(4)]


def relay_kernel(up, from_below, down, from_above, up_out, down_out):
    @pl.when(pl.program_id(0) == 0)
    def _():
        up_out[...] = (up[...].astype(F32) + from_below[...].astype(F32)).astype(BF16)
        down_out[...] = down[...]

    @pl.when(pl.program_id(0) == 1)
    def _():
        up_out[...] = up[...]
        down_out[...] = (down[...].astype(F32) + from_above[...].astype(F32)).astype(BF16)


def relay(up, from_below, down, from_above, needs):
    rows, width = from_below.shape
    half = pl.BlockSpec((rows, width), lambda i: (i, 0))
    return call(
        relay_kernel,
        (up, from_below, down, from_above),
        [half, full((rows, width)), half, full((rows, width))],
        [half, half],
        [shaped(2 * rows, width)] * 2,
        "relay",
        grid=(2,),
        needs=needs,
    )


def add_chips_kernel(*refs):
    ins, keep, give = refs[:6], refs[6], refs[7]
    keep[...] = sum(item[...].astype(F32) for item in ins[:3])
    give[...] = sum(item[...].astype(F32) for item in ins[3:]).astype(BF16)


def add_chips(items, needs):
    rows, width = items[0].shape[0] // 2, items[0].shape[1]
    step = rows // 2 if rows % 32 == 0 and (rows // 2) % 16 == 0 else rows
    count = rows // step
    mine = pl.BlockSpec((step, width), lambda i: (i, 0))
    other = pl.BlockSpec((step, width), lambda i: (i + count, 0))
    return call(
        add_chips_kernel,
        (*items, *items),
        [mine] * 3 + [other] * 3,
        [mine, mine],
        [shaped(rows, width, dtype=F32), shaped(rows, width)],
        "add_chips",
        grid=(count,),
        needs=needs,
    )


def over_cores(values):
    return lax.ppermute(values, "core", SWAP)


def latents_back_kernel(
    me, got, latents, query_gain, latent_gain, keep, low, high, many, own, gain_part, kept, turns, sems
):
    rows = own.shape[0]
    here = pl.ds(pl.multiple_of(me[0] * rows, rows), rows)
    copies = [pltpu.make_async_copy(latents.at[here, :], kept, sems.at[0])] + [
        pltpu.make_async_copy(table.at[here, :], turns.at[n], sems.at[n + 1])
        for n, table in enumerate((keep, low, high))
    ]
    for copy in copies:
        copy.start()
    total = add_up(got)
    for copy in copies:
        copy.wait()

    def back(lanes, gain):
        upstream, values = total[:, lanes], kept[:, lanes]
        factor = root(values)
        normed = values * factor
        gain_part[:, lanes] = jnp.sum(upstream * normed, axis=0, keepdims=True)
        return norm_back(upstream, normed, factor, row(gain)).astype(BF16)

    own[:, :QR] = back(slice(0, QR), query_gain)
    own[:, QR:LAT] = back(slice(QR, LAT), latent_gain)
    own[:, LAT:] = turn(total[:, LAT:], turns[0], turns[1], turns[2], back=True).astype(BF16)
    for k in range(8):
        many[k] = own[...]


def latents_back_of(me, got, latents, query_gain, latent_gain, tables, needs):
    rows = latents.shape[0] // 8
    return call(
        latents_back_kernel,
        (got.reshape(8, rows, WIDE), latents, query_gain, latent_gain, *tables),
        [full((8, rows, WIDE)), HBM, full((QR,)), full((KVR,)), HBM, HBM, HBM],
        [full((8, rows, WIDE)), full((rows, WIDE)), full((1, LAT))],
        [shaped(8, rows, WIDE), shaped(rows, WIDE), shaped(1, LAT, dtype=F32)],
        "latents_back",
        scratch=[
            pltpu.VMEM((rows, LAT), F32),
            pltpu.VMEM((3, rows, 128), F32),
            pltpu.SemaphoreType.DMA((4,)),
        ],
        needs=needs,
        me=me,
        limit=24,
    )


def first_back_of(raw_back, query_down, latent_down, rope_down):
    rope_down[...] = jnp.zeros_like(rope_down)
    rope_down[64:96, :] = latent_down[KVR:, :]
    return (
        dot(raw_back[:, :QR], query_down[...], NT)
        + dot(raw_back[:, QR:LAT], latent_down[:KVR, :])
        + dot(raw_back[:, LAT:], rope_down[...])
    )


def first_gain_kernel(
    me, raw_back, tokens, query_down, latent_down, gain_part, rope_down, own, sem
):
    rows = own.shape[0]
    here = pl.ds(pl.multiple_of(me[0] * rows, rows), rows)
    copy = pltpu.make_async_copy(tokens.at[here, :], own, sem)
    copy.start()
    first_back = first_back_of(raw_back, query_down, latent_down, rope_down)
    copy.wait()
    values = own[...].astype(F32)
    gain_part[...] = jnp.sum(first_back * (values * root(values)), axis=0, keepdims=True)


def first_gain_of(me, own_raw_back, tokens, query_down, latent_down, needs):
    width = tokens.shape[1]
    return call(
        first_gain_kernel,
        (own_raw_back, tokens, query_down, latent_down.T),
        [full(own_raw_back.shape), HBM, full(query_down.shape), full(latent_down.shape[::-1])],
        [full((1, width))],
        [shaped(1, width, dtype=F32)],
        "first_gain",
        scratch=[
            pltpu.VMEM((128, width), BF16),
            pltpu.VMEM((own_raw_back.shape[0], width), BF16),
            pltpu.SemaphoreType.DMA,
        ],
        needs=needs,
        me=me,
    )


def tokens_back_kernel(
    raw_back, tokens, attention_back, query_down, latent_down, gain, tokens_grad, rope_down
):
    first_back = first_back_of(raw_back, query_down, latent_down, rope_down)
    values = tokens[...].astype(F32)
    factor = root(values)
    tokens_grad[...] = attention_back[...].astype(F32) + norm_back(
        first_back, values * factor, factor, row(gain)
    )


def tokens_back_of(raw_back, tokens, attention_back, query_down, latent_down, gain, needs):
    length, width = tokens.shape

    def rows(columns):
        return pl.BlockSpec((TILE, columns), lambda i: (i, 0))

    return call(
        tokens_back_kernel,
        (raw_back, tokens, attention_back, query_down, latent_down.T, gain),
        [
            rows(WIDE),
            rows(width),
            rows(width),
            full(query_down.shape),
            full(latent_down.shape[::-1]),
            full((width,)),
        ],
        [rows(width)],
        [shaped(length, width, dtype=F32)],
        "tokens_back",
        grid=(length // TILE,),
        scratch=[pltpu.VMEM((128, width), BF16)],
        needs=needs,
    )


def finish_ffn_kernel(keep, got, gate, up, down):
    units = gate.shape[1]
    for n, out in enumerate((gate, up, down)):
        lanes = slice(units * n, units * n + units)
        out[...] = keep[:, lanes] + got[:, lanes].astype(F32)


def finish_ffn(keep, got, needs):
    rows, width = keep.shape
    out = (rows, width // 3)
    return call(
        finish_ffn_kernel,
        (keep, got),
        [full(keep.shape), full(got.shape)],
        [full(out)] * 3,
        [shaped(*out, dtype=F32)] * 3,
        "finish_ffn",
        needs=needs,
    )[0]


def finish_attn_kernel(heads, keep, got, out_grad, query_grad, latent_grad):
    total = keep[...] + got[...].astype(F32)
    for h in range(heads):
        lanes = slice(128 * h, 128 * h + 128)
        out_grad[:, 64 * h : 64 * h + 64] = total[:160, 128 * h + 64 : 128 * h + 128]
        query_grad[:, 96 * h : 96 * h + 96] = total[160:208, 128 * h : 128 * h + 96]
    latent_grad[...] = total[208:224]


def finish_attn(keep, got):
    heads = keep.shape[1] // 128
    outs = [(160, 64 * heads), (48, 96 * heads), (16, 128 * heads)]
    return call(
        functools.partial(finish_attn_kernel, heads),
        (keep, got),
        [full(keep.shape), full(got.shape)],
        [full(s) for s in outs],
        [shaped(*s, dtype=F32) for s in outs],
        "finish_attn",
    )[0]


GAINS = ((0, 160), (160, 160), (320, 48), (368, 16))


def down_parts_kernel(own_in, raw_back, gains, out):
    total = dot(own_in[...], raw_back[...]).astype(BF16)
    for d in range(16):
        out[d, :20, :] = total[20 * d : 20 * d + 20]
        out[d, 20:, :] = jnp.zeros((4, WIDE), BF16)
        out[d, 20:21, :] = gains[d : d + 1, :]


def down_parts(own_in, raw_back, gains, needs):
    args = (own_in, raw_back, gains)
    return call(
        down_parts_kernel,
        args,
        [full(item.shape) for item in args],
        [full((16, 24, WIDE))],
        [shaped(16, 24, WIDE)],
        "down_parts",
        needs=needs,
        limit=24,
    )


def sum_copies_kernel(got, many):
    total = got[0].astype(F32)
    for d in range(1, 16):
        total = total + got[d].astype(F32)
    for k in range(8):
        many[k] = total.astype(BF16)


def sum_copies(got):
    return call(
        sum_copies_kernel,
        (got,),
        [full(got.shape)],
        [full((8, 24, WIDE))],
        [shaped(8, 24, WIDE)],
        "sum_copies",
        limit=24,
    )


def finish_down_kernel(everyone, query_grad, latent_grad, *gains):
    for t in range(8):
        values = everyone[t].astype(F32)
        query_grad[20 * t : 20 * t + 20, :] = values[:20, :QR]
        latent_grad[20 * t : 20 * t + 20, :KVR] = values[:20, QR:LAT]
        latent_grad[20 * t : 20 * t + 20, KVR:] = values[:20, LAT + 64 : LAT + 96]
    total = sum(everyone[t, 16:24, :].astype(F32) for t in range(8))[4:5, :]
    for out, (first, count) in zip(gains, GAINS):
        out[...] = total[:, first : first + count]


def finish_down(everyone):
    everyone = everyone.reshape(8, 24, WIDE)
    outs = [(160, QR), (160, KVR + ROPE)] + [(1, count) for _, count in GAINS]
    return call(
        finish_down_kernel,
        (everyone,),
        [full(everyone.shape)],
        [full(s) for s in outs],
        [shaped(*s, dtype=F32) for s in outs],
        "finish_down",
        limit=24,
    )[0]


def exchange(blocks):
    return lax.all_to_all(blocks.reshape(-1, blocks.shape[-1]), TP, 0, 0, tiled=True)


def on_device(
    tokens,
    first_gain,
    query_down,
    query_gain,
    query_up,
    latent_down,
    latent_gain,
    latent_up,
    out_weight,
    second_gain,
    gate_weight,
    up_weight,
    down_weight,
    cotangent,
):
    length = tokens.shape[0]
    me = lax.axis_index(TP).astype(jnp.int32).reshape(1)
    y, xl, core = lax.axis_index("y"), lax.axis_index("xl"), lax.axis_index("core")
    starts = jnp.stack(
        [
            ((y + k) % 4 * 2 + (xl ^ j)) * 2 + c
            for c in (core, 1 - core)
            for k in range(4)
            for j in range(2)
        ]
    ).astype(jnp.int32)
    tables = rope_tables(length)

    gate_turned, up_turned = gate_weight.T, up_weight.T

    (
        first_in,
        latents,
        query_code,
        latent_code,
        queries,
        keyvals,
        rope_keys,
        heads_out,
        log_total,
        attn_partial,
    ), started = attend(
        tokens,
        first_gain,
        query_down,
        latent_down,
        query_gain,
        latent_gain,
        query_up,
        latent_up,
        out_weight,
        tables,
    )
    attn_got = exchange(attn_partial)

    (cot_keep, cot_give), picked = halves(starts, [cotangent], [started])
    inner_back = dot(cotangent, down_weight, NT)
    cot_got = over_cores(cot_give)

    (residual, second_many), _ = residual_of(
        me, attn_got, tokens, second_gain, [picked]
    )
    second_in = exchange(second_many)

    turned_in = first_in.T.reshape(16, 8, 20, length)
    own_in = lax.dynamic_slice_in_dim(turned_in, me[0], 1, 1).reshape(320, length)
    (code_keep, code_give, lat_keep, lat_give), picked = halves(
        starts, [query_code, latent_code], [residual]
    )
    code_got, lat_got = over_cores(code_give), over_cores(lat_give)
    heads_got = over_cores(heads_out)

    (gate_back, up_back, inner, back_partial), done = ffn(
        second_in, gate_turned, up_turned, inner_back, [picked, own_in]
    )
    back_got = exchange(back_partial)

    ours = (gate_back, up_back, inner)
    theirs = [over_cores(item) for item in ours]
    (in_keep, in_give), _ = halves(starts, [second_in], [done])
    in_got = over_cores(in_give)
    (far_up, far_down, ffn_up, ffn_down_way, ffn_own), done = ffn_grads(in_keep, in_got, cot_keep, cot_got, ours, theirs, gate_weight.shape[1], [])
    below, above = lax.ppermute(far_up, "y", UP), lax.ppermute(far_down, "y", DOWN)

    (back_many, second_gain_part), done = residual_back_of(
        me, back_got, residual, cotangent, second_gain, [done]
    )
    attention_back = exchange(back_many)
    (ffn_partial,), done = ffn_down(me, inner, down_weight, residual, [done])
    (ffn_up, ffn_down_way), done = relay(ffn_up, below, ffn_down_way, above, [done])
    below, above = lax.ppermute(ffn_up, "y", UP), lax.ppermute(ffn_down_way, "y", DOWN)

    (query_raw_back, keyval_back, latents_partial), back_done = attend_back(
        attention_back,
        out_weight,
        queries,
        keyvals,
        rope_keys,
        log_total,
        query_up,
        latent_up,
        tables,
        [done],
    )
    mixed = lax.psum(ffn_partial, TP)
    latents_got = exchange(latents_partial)

    (ffn_keep, ffn_give), done = add_chips([ffn_own, below, above], [back_done])
    ffn_got = lax.ppermute(ffn_give, "xl", SWAP)
    raw_got, kv_got = over_cores(query_raw_back), over_cores(keyval_back)

    (raw_many, own_raw, latent_gain_parts), done = latents_back_of(
        me, latents_got, latents, query_gain, latent_gain, tables, [done]
    )
    raw_back = exchange(raw_many)

    (first_gain_part,), _ = first_gain_of(me, own_raw, tokens, query_down, latent_down, [done])
    (out_keep, out_give), _ = halves(starts, [attention_back], [done])
    out_got = over_cores(out_give)
    (far_up, far_down, attn_up, attn_down, attn_own), done = attn_grads(
        (out_keep, code_keep, lat_keep),
        (out_got, code_got, lat_got),
        (heads_out, query_raw_back, keyval_back),
        (heads_got, raw_got, kv_got),
        [],
    )
    below, above = lax.ppermute(far_up, "y", UP), lax.ppermute(far_down, "y", DOWN)

    gains = jnp.concatenate(
        [
            first_gain_part.reshape(16, -1),
            second_gain_part.reshape(16, -1),
            latent_gain_parts[0, :QR].reshape(16, -1),
            latent_gain_parts[0, QR:].reshape(16, -1),
        ],
        axis=1,
    ).astype(BF16)
    gains = jnp.pad(gains, ((0, 0), (0, WIDE - gains.shape[1])))
    (parts,), parts_done = down_parts(own_in, raw_back, gains, [done])
    parts_got = lax.all_to_all(parts, DP, 0, 0, tiled=True)

    (attn_up, attn_down), done = relay(attn_up, below, attn_down, above, [parts_done])
    below, above = lax.ppermute(attn_up, "y", UP), lax.ppermute(attn_down, "y", DOWN)
    (tokens_grad,), done = tokens_back_of(
        raw_back, tokens, attention_back, query_down, latent_down, first_gain, [done]
    )
    (many,), summed = sum_copies(parts_got)
    everyone = exchange(many)

    (attn_keep, attn_give), done = add_chips([attn_own, below, above], [done, summed])
    attn_got = lax.ppermute(attn_give, "xl", SWAP)
    gate_weight_grad, up_weight_grad, down_weight_grad = finish_ffn(ffn_keep, ffn_got, [done])
    out_weight_grad, query_up_grad, latent_up_grad = finish_attn(attn_keep, attn_got)
    (
        query_down_grad,
        latent_down_grad,
        first_gain_grad,
        second_gain_grad,
        query_gain_grad,
        latent_gain_grad,
    ) = finish_down(everyone)

    return (
        mixed,
        tokens_grad,
        first_gain_grad[0],
        query_down_grad,
        query_gain_grad[0],
        query_up_grad,
        latent_down_grad,
        latent_gain_grad[0],
        latent_up_grad,
        out_weight_grad.T,
        second_gain_grad[0],
        gate_weight_grad,
        up_weight_grad,
        down_weight_grad.T,
    )


def solution(mesh):
    grid = Mesh(mesh.devices.reshape(4, 2, 2, 2, 4), ("y", "xl", "core", "xh", "z"))
    in_specs = (
        P(DP, None),
        P(),
        P(),
        P(),
        P(None, TP),
        P(),
        P(),
        P(None, TP),
        P(TP, None),
        P(),
        P(None, TP),
        P(None, TP),
        P(TP, None),
        P(DP, None),
    )
    out_specs = (
        P(DP, None),
        P(DP, None),
        P(DP),
        P(DP, None),
        P(DP),
        P(DP, TP),
        P(DP, None),
        P(DP),
        P(DP, TP),
        P(TP, DP),
        P(DP),
        P(DP, TP),
        P(DP, TP),
        P(TP, DP),
    )
    return jax.shard_map(
        on_device, mesh=grid, in_specs=in_specs, out_specs=out_specs, check_vma=False
    )
```

```python
import functools

import jax
import jax.numpy as jnp
import numpy as np
from jax import lax
from jax.experimental import pallas as pl
from jax.experimental.pallas import tpu as pltpu
from jax.sharding import Mesh, PartitionSpec as P

NOPE = 64
ROPE = 32
DV = 64
KVR = 256
QR = 768
LAT = QR + KVR
WIDE = LAT + 128

EPS = 1e-05
BASE = 10000.0
SCALE = (NOPE + ROPE) ** (-0.5)

DP = ("y", "xl", "core")
TP = ("xh", "z")
SWAP = [(0, 1), (1, 0)]
F32 = jnp.float32
BF16 = jnp.bfloat16
NT = (((1,), (1,)), ((), ()))
TN = (((0,), (0,)), ((), ()))
NN = (((1,), (0,)), ((), ()))
TILE = 256


def dot(left, right, dims=NN):
    return lax.dot_general(left, right, dims, preferred_element_type=F32)


def params(limit=56):
    return pltpu.CompilerParams(vmem_limit_bytes=limit * 2**20)


HBM = pl.BlockSpec(memory_space=pltpu.HBM)


def call(kernel, args, in_specs, out_specs, out_shape, name, grid=(1,), scratch=(), needs=(), me=None, limit=60):
    first = 0 if me is None else 1
    n_in, n_out = len(args), len(out_shape)

    def body(*refs):
        ins = refs[: first + n_in]
        rest = refs[first + n_in + len(needs) :]
        mark = rest[n_out]

        @pl.when(pl.program_id(0) == 0)
        def _():
            mark[...] = jnp.zeros_like(mark)

        kernel(*ins, *rest[:n_out], *rest[n_out + 1 :])

    *outs, mark = pl.pallas_call(
        body,
        grid_spec=pltpu.PrefetchScalarGridSpec(
            num_scalar_prefetch=first,
            grid=grid,
            in_specs=list(in_specs) + [HBM] * len(needs),
            out_specs=list(out_specs) + [full((8, 128))],
            scratch_shapes=list(scratch),
        ),
        out_shape=list(out_shape) + [jax.ShapeDtypeStruct((8, 128), F32)],
        compiler_params=params(limit),
        cost_estimate=pl.CostEstimate(flops=1, bytes_accessed=1, transcendentals=0),
        name=name,
    )(*(() if me is None else (me,)), *args, *needs)
    return outs, mark


def shaped(*shape, dtype=BF16):
    return jax.ShapeDtypeStruct(shape, dtype)


def full(shape):
    return pl.BlockSpec(shape, lambda *_: (0,) * len(shape))


def rope_tables(length):
    half = ROPE // 2
    rates = np.exp(np.arange(half, dtype=np.float32) * np.float32(-2.0 * np.log(BASE) / ROPE))
    angles = np.arange(length, dtype=np.float32)[:, None] * rates.astype(np.float32)[None, :]
    cosine, sine = np.cos(angles), np.sin(angles)
    keep = np.zeros((length, 128), np.float32)
    keep[:, :NOPE] = 1.0
    keep[:, 64:80] = cosine
    keep[:, 80:96] = cosine
    low = np.zeros((length, 128), np.float32)
    low[:, 64:80] = -sine
    high = np.zeros((length, 128), np.float32)
    high[:, 80:96] = sine
    return jnp.asarray(keep), jnp.asarray(low), jnp.asarray(high)


def turn(values, keep, low, high, back=False):
    moved = pltpu.roll(values, 112, 1) * low + pltpu.roll(values, 16, 1) * high
    return values * keep - moved if back else values * keep + moved


def root(values):
    return lax.rsqrt(jnp.mean(values * values, axis=-1, keepdims=True) + EPS)


def norm_back(upstream, normed, factor, gain):
    scaled = upstream * gain
    return factor * (scaled - normed * jnp.mean(scaled * normed, axis=-1, keepdims=True))


def spread_out_weight(weight_ref, spread_ref, heads):
    spread_ref[...] = jnp.zeros_like(spread_ref)
    for h in range(heads):
        spread_ref[128 * h + 64 : 128 * h + 128, :] = weight_ref[64 * h : 64 * h + 64, :]


def spread_query_up(weight_ref, spread_ref, heads):
    spread_ref[...] = jnp.zeros_like(spread_ref)
    for h in range(heads):
        spread_ref[128 * h : 128 * h + 96, :] = weight_ref[96 * h : 96 * h + 96, :]


def row(ref):
    return ref[...].reshape(1, -1)


def low_lanes(shape):
    return lax.broadcasted_iota(jnp.int32, shape, 1) < NOPE


def causal(keys, queries, first_query):
    key_ids = lax.broadcasted_iota(jnp.int32, (keys, queries), 0)
    query_ids = lax.broadcasted_iota(jnp.int32, (keys, queries), 1) + first_query
    return key_ids <= query_ids


def attend_kernel(
    heads,
    me,
    tokens,
    first_gain,
    query_down,
    latent_down,
    query_gain,
    latent_gain,
    query_up,
    latent_up,
    out_weight,
    keep,
    low,
    high,
    first_in,
    latents,
    query_code,
    latent_code,
    queries,
    keyvals,
    rope_keys,
    heads_out,
    log_total,
    partial,
    raw_latents,
    spread,
    spread_up,
    rope_down,
    kv_all,
    rope_all,
):
    step = pl.program_id(0)

    @pl.when(step == 0)
    def _():
        spread_out_weight(out_weight, spread, heads)
        spread_query_up(query_up, spread_up, heads)
        rope_down[...] = jnp.zeros_like(rope_down)
        rope_down[64:96, :] = latent_down[KVR:, :]

    def rows_of(index, carry):
        rows = pl.ds(pl.multiple_of(index * 32, 32), 32)
        values = tokens[rows, :].astype(F32)
        first_in[rows, :] = (values * root(values) * row(first_gain)).astype(BF16)
        return carry

    lax.fori_loop(0, TILE // 32, rows_of, 0)
    taken = first_in[...]
    query_latent = dot(taken, query_down[...])
    raw_latents[:, :QR] = query_latent
    code = (query_latent * root(query_latent) * row(query_gain)).astype(BF16)
    query_code[...] = code
    latent = dot(taken, latent_down[:KVR, :], NT)
    raw_latents[:, QR:] = latent
    count = latents.shape[0]
    own = me[0] * count

    @pl.when(own // TILE == step)
    def _():
        latents[...] = raw_latents[pl.ds(pl.multiple_of(own % TILE, count), count), :]

    lcode = (latent * root(latent) * row(latent_gain)).astype(BF16)
    latent_code[...] = lcode
    tables = keep[...], low[...], high[...]
    rope = turn(dot(taken, rope_down[...], NT), *tables).astype(BF16)
    rope_keys[...] = rope
    here = pl.ds(pl.multiple_of(step * TILE, TILE), TILE)
    rope_all[here, :] = rope
    kv = dot(lcode, latent_up[...]).astype(BF16)
    keyvals[...] = kv
    kv_all[here, :] = kv
    raw = dot(code, spread_up[...], NT)
    for h in range(heads):
        lanes = slice(128 * h, 128 * h + 128)
        queries[:, lanes] = turn(raw[:, lanes], *tables).astype(BF16)

    def tile(index):
        keys = TILE * (index + 1)
        for h in range(heads):
            lanes = slice(128 * h, 128 * h + 128)
            kv_h = kv_all[:keys, lanes]
            key = jnp.where(low_lanes((keys, 128)), kv_h, rope_all[:keys, :])
            scores = dot(key, queries[:, lanes], NT) * SCALE
            scores = jnp.where(causal(keys, TILE, TILE * index), scores, -1e30)
            top = jnp.max(scores, axis=0, keepdims=True)
            weights = jnp.exp(scores - top)
            total = jnp.sum(weights, axis=0, keepdims=True)
            log_total[h : h + 1, :] = top + jnp.log(total)
            probs = (weights * (1.0 / total)).astype(BF16)
            heads_out[:, lanes] = dot(probs, kv_h, TN).astype(BF16)

    for index in range(2):
        pl.when(step == index)(functools.partial(tile, index))
    partial[...] = dot(heads_out[...], spread[...]).astype(BF16)


def attend(me, tokens, first_gain, query_down, latent_down, query_gain, latent_gain, query_up, latent_up, out_weight, tables):
    latent_down, query_up = latent_down.T, query_up.T
    length, width = tokens.shape
    heads = out_weight.shape[0] // DV
    wide = 128 * heads

    def rows(columns):
        return pl.BlockSpec((TILE, columns), lambda i, *_: (i, 0))

    return call(
        functools.partial(attend_kernel, heads),
        (tokens, first_gain, query_down, latent_down, query_gain, latent_gain, query_up, latent_up, out_weight, *tables),
        [
            rows(width),
            full((width,)),
            full(query_down.shape),
            full(latent_down.shape),
            full((QR,)),
            full((KVR,)),
            full(query_up.shape),
            full(latent_up.shape),
            full(out_weight.shape),
            rows(128),
            rows(128),
            rows(128),
        ],
        [
            rows(width),
            full((length // 8, LAT)),
            rows(QR),
            rows(KVR),
            rows(wide),
            rows(wide),
            rows(128),
            rows(wide),
            pl.BlockSpec((8, TILE), lambda i, *_: (0, i)),
            rows(width),
        ],
        [
            shaped(length, width),
            shaped(length // 8, LAT, dtype=F32),
            shaped(length, QR),
            shaped(length, KVR),
            shaped(length, wide),
            shaped(length, wide),
            shaped(length, 128),
            shaped(length, wide),
            shaped(8, length, dtype=F32),
            shaped(length, width),
        ],
        "attend",
        grid=(length // TILE,),
        me=me,
        scratch=[
            pltpu.VMEM((TILE, LAT), F32),
            pltpu.VMEM((wide, width), BF16),
            pltpu.VMEM((wide, QR), BF16),
            pltpu.VMEM((128, width), BF16),
            pltpu.VMEM((length, wide), BF16),
            pltpu.VMEM((length, 128), BF16),
        ],
    )


def attend_back_kernel(
    heads,
    attention_back,
    out_weight,
    queries,
    keyvals,
    rope_keys,
    log_total,
    query_up,
    latent_up,
    keep,
    low,
    high,
    query_back,
    keyval_back,
    partial,
    spread,
    spread_up,
    kv_grad,
    rope_grad,
    code_grad,
):
    step = pl.program_id(0)

    @pl.when(step == 0)
    def _():
        spread_out_weight(out_weight, spread, heads)
        spread_query_up(query_up, spread_up, heads)
        kv_grad[...] = jnp.zeros_like(kv_grad)
        rope_grad[...] = jnp.zeros_like(rope_grad)

    heads_back = dot(attention_back[...], spread[...], NT).astype(BF16)
    tables = keep[...], low[...], high[...]

    def tile(index):
        keys = TILE * (index + 1)
        low_part = low_lanes((keys, 128))
        for h in range(heads):
            lanes = slice(128 * h, 128 * h + 128)
            kv_h = keyvals[:keys, lanes]
            key = jnp.where(low_part, kv_h, rope_keys[:keys, :])
            query = queries[:, lanes]
            back = heads_back[:, lanes]
            scores = dot(key, query, NT) * SCALE
            probs = jnp.exp(scores - log_total[h : h + 1, :])
            probs = jnp.where(causal(keys, TILE, TILE * index), probs, 0.0)
            prob_back = dot(kv_h, back, NT)
            mean = jnp.sum(probs * prob_back, axis=0, keepdims=True)
            score_back = (probs * (prob_back - mean)).astype(BF16)
            of_values = dot(probs.astype(BF16), back)
            of_keys = dot(score_back, query) * SCALE
            kv_grad[:keys, lanes] += of_values + jnp.where(low_part, of_keys, 0.0)
            rope_grad[:keys, :] += jnp.where(low_part, 0.0, of_keys)
            of_query = dot(score_back, key, TN) * SCALE
            query_back[:, lanes] = turn(of_query, *tables, back=True).astype(BF16)

    for index in range(2):
        pl.when(step == index)(functools.partial(tile, index))
    here = pl.ds(pl.multiple_of(step * TILE, TILE), TILE)
    code_grad[here, :] = dot(query_back[...], spread_up[...]).astype(BF16)

    @pl.when(step == 1)
    def _():
        kv = kv_grad[...].astype(BF16)
        keyval_back[...] = kv
        partial[:, :QR] = code_grad[...]
        partial[:, QR:LAT] = dot(kv, latent_up[...], NT).astype(BF16)
        partial[:, LAT:] = rope_grad[...].astype(BF16)


def attend_back(attention_back, out_weight, queries, keyvals, rope_keys, log_total, query_up, latent_up, tables, needs):
    query_up = query_up.T
    length, width = attention_back.shape
    heads = out_weight.shape[0] // DV
    wide = 128 * heads

    def rows(columns):
        return pl.BlockSpec((TILE, columns), lambda i, *_: (i, 0))

    return call(
        functools.partial(attend_back_kernel, heads),
        (attention_back, out_weight, queries, keyvals, rope_keys, log_total, query_up, latent_up, *tables),
        [
            rows(width),
            full(out_weight.shape),
            rows(wide),
            full((length, wide)),
            full((length, 128)),
            pl.BlockSpec((8, TILE), lambda i, *_: (0, i)),
            full(query_up.shape),
            full(latent_up.shape),
            rows(128),
            rows(128),
            rows(128),
        ],
        [rows(wide), full((length, wide)), full((length, WIDE))],
        [shaped(length, wide), shaped(length, wide), shaped(length, WIDE)],
        "attend_back",
        grid=(length // TILE,),
        scratch=[
            pltpu.VMEM((wide, width), BF16),
            pltpu.VMEM((wide, QR), BF16),
            pltpu.VMEM((length, wide), F32),
            pltpu.VMEM((length, 128), F32),
            pltpu.VMEM((length, QR), BF16),
        ],
        needs=needs,
    )


def add_up(got):
    total = got[0].astype(F32)
    for k in range(1, 8):
        total = total + got[k].astype(F32)
    return total


def chunked(rows, body):
    def step(index, carry):
        body(pl.ds(pl.multiple_of(index * 16, 16), 16))
        return carry

    lax.fori_loop(0, rows // 16, step, 0)


def residual_kernel(me, got, tokens, gain, residual, many, own, sem):
    rows = own.shape[0]
    first = pl.multiple_of(me[0] * rows, rows)
    copy = pltpu.make_async_copy(tokens.at[pl.ds(first, rows), :], own, sem)
    copy.start()
    copy.wait()

    def part(here):
        total = own[here, :].astype(F32)
        for k in range(8):
            total = total + got[k, here, :].astype(F32)
        residual[here, :] = total
        second_in = (total * root(total) * row(gain)).astype(BF16)
        for k in range(8):
            many[k, here, :] = second_in

    chunked(rows, part)


def residual_of(me, got, tokens, gain, needs):
    width = tokens.shape[1]
    rows = tokens.shape[0] // 8
    return call(
        residual_kernel,
        (got.reshape(8, rows, width), tokens, gain),
        [full((8, rows, width)), HBM, full((width,))],
        [full((rows, width)), full((8, rows, width))],
        [shaped(rows, width, dtype=F32), shaped(8, rows, width)],
        "residual",
        scratch=[pltpu.VMEM((rows, width), BF16), pltpu.SemaphoreType.DMA],
        needs=needs,
        me=me,
        limit=58,
    )


def residual_back_kernel(me, got, residual, cotangent, gain, many, gain_part, own, kept, sems):
    rows = own.shape[0]
    first = pl.multiple_of(me[0] * rows, rows)
    copies = [
        pltpu.make_async_copy(cotangent.at[pl.ds(first, rows), :], own, sems.at[0]),
        pltpu.make_async_copy(residual, kept, sems.at[1]),
    ]
    for copy in copies:
        copy.start()
    gain_part[...] = jnp.zeros_like(gain_part)
    for copy in copies:
        copy.wait()

    def part(here):
        second_back = got[0, here, :].astype(F32)
        for k in range(1, 8):
            second_back = second_back + got[k, here, :].astype(F32)
        values = kept[here, :]
        factor = root(values)
        normed = values * factor
        gain_part[...] += jnp.sum(second_back * normed, axis=0, keepdims=True)
        back = own[here, :].astype(F32) + norm_back(second_back, normed, factor, row(gain))
        back = back.astype(BF16)
        for k in range(8):
            many[k, here, :] = back

    chunked(rows, part)


def residual_back_of(me, got, residual, cotangent, gain, needs):
    rows, width = residual.shape
    return call(
        residual_back_kernel,
        (got.reshape(8, rows, width), residual, cotangent, gain),
        [full((8, rows, width)), HBM, HBM, full((width,))],
        [full((8, rows, width)), full((1, width))],
        [shaped(8, rows, width), shaped(1, width, dtype=F32)],
        "residual_back",
        scratch=[
            pltpu.VMEM((rows, width), BF16),
            pltpu.VMEM((rows, width), F32),
            pltpu.SemaphoreType.DMA((2,)),
        ],
        needs=needs,
        me=me,
        limit=58,
    )


def ffn_kernel(
    second_in, gate_weight, up_weight, inner_back, gate_back, up_back, inner, partial
):
    taken = second_in[...]
    gate = dot(taken, gate_weight[...], NT)
    up = dot(taken, up_weight[...], NT)
    sigma = 1.0 / (1.0 + jnp.exp(-gate))
    act = gate * sigma
    units = gate.shape[1]
    back = inner_back[...]
    of_gate = (back * up * sigma * (1.0 + gate * (1.0 - sigma))).astype(BF16)
    of_up = (back * act).astype(BF16)
    for out, values in ((gate_back, of_gate), (up_back, of_up), (inner, (act * up).astype(BF16))):
        out[:, :units] = values
        out[:, units:] = jnp.zeros((values.shape[0], out.shape[1] - units), BF16)
    partial[...] = (dot(of_gate, gate_weight[...]) + dot(of_up, up_weight[...])).astype(BF16)


def ffn(second_in, gate_weight, up_weight, inner_back, needs):
    length, width = second_in.shape
    units = gate_weight.shape[0]
    wide = -(-units // 128) * 128

    def rows(columns):
        return pl.BlockSpec((TILE, columns), lambda i, *_: (i, 0))

    return call(
        ffn_kernel,
        (second_in, gate_weight, up_weight, inner_back),
        [rows(width), full((units, width)), full((units, width)), rows(units)],
        [rows(wide), rows(wide), rows(wide), rows(width)],
        [shaped(length, wide)] * 3 + [shaped(length, width)],
        "ffn",
        grid=(length // TILE,),
        needs=needs,
    )


def ffn_down_kernel(me, inner, down_weight, residual, out):
    for i in range(2):
        rows = slice(i * TILE, i * TILE + TILE)
        out[rows, :] = dot(inner[rows, : down_weight.shape[0]], down_weight[...]).astype(BF16)
    count = residual.shape[0]
    own = pl.ds(pl.multiple_of(me[0] * count, count), count)
    out[own, :] = (out[own, :].astype(F32) + residual[...]).astype(BF16)


def ffn_down(me, inner, down_weight, residual, needs):
    length, width = inner.shape[0], down_weight.shape[1]
    return call(
        ffn_down_kernel,
        (inner, down_weight, residual),
        [full(inner.shape), full(down_weight.shape), full(residual.shape)],
        [full((length, width))],
        [shaped(length, width)],
        "ffn_down",
        needs=needs,
        me=me,
    )


def halves_kernel(blocks, width, starts, *refs):
    sources, outs, turned = refs[:blocks], refs[blocks : 3 * blocks], refs[3 * blocks]
    for n in range(blocks):
        source, keep, give = sources[n], outs[2 * n], outs[2 * n + 1]
        columns, each = source.shape[1], width[n]
        for c in range(0, columns, 256):
            turned[c : c + 256, :] = source[:, c : c + 256].T
        for which, out in enumerate((keep, give)):
            for k in range(8):
                first = pl.multiple_of(starts[8 * which + k] * each, 16)
                out[each * k : each * k + each, :] = turned[pl.ds(first, each), :]


def halves(starts, values, needs):
    length = values[0].shape[0]
    widths = [item.shape[1] // 16 for item in values]
    shapes = [(8 * w, length) for w in widths for _ in range(2)]
    return call(
        functools.partial(halves_kernel, len(values), widths),
        tuple(values),
        [full(item.shape) for item in values],
        [full(s) for s in shapes],
        [shaped(*s) for s in shapes],
        "halves",
        scratch=[pltpu.VMEM((max(item.shape[1] for item in values), length), BF16)],
        needs=needs,
        me=starts,
    )


ORDER = (2, 1, 3, 0)


def ffn_grads_kernel(in_keep, in_got, cot_keep, cot_got, *refs):
    ours, theirs, outs = refs[:3], refs[3:6], refs[6:]
    units = outs[0].shape[1] // 3

    def block(*parts):
        for n, (keep, got) in enumerate(((in_keep, in_got), (in_keep, in_got), (cot_keep, cot_got))):
            total = dot(keep[...], ours[n][...]) + dot(got[...], theirs[n][...])
            total = total[:, :units].astype(BF16)
            first = 0
            for out in parts:
                count = out.shape[0]
                out[:, units * n : units * n + units] = total[first : first + count]
                first += count

    for s, parts in enumerate((outs[:2], outs[2:3], outs[3:4], outs[4:])):
        pl.when(pl.program_id(0) == s)(functools.partial(block, *parts))


def ffn_grads(in_keep, in_got, cot_keep, cot_got, ours, theirs, units, needs):
    length, wide = ours[0].shape
    rows = in_keep.shape[0] // 4

    def index(i):
        return (jnp.where(i == 0, 2, jnp.where(i == 1, 1, jnp.where(i == 2, 3, 0))), 0)

    left = pl.BlockSpec((rows, length), index)
    out = (rows, 3 * units)
    outs = [(rows // 2, 3 * units)] * 2 + [out] * 3
    return call(
        ffn_grads_kernel,
        (in_keep, in_got, cot_keep, cot_got, *ours, *theirs),
        [left] * 4 + [full((length, wide))] * 6,
        [full(s) for s in outs],
        [shaped(*s) for s in outs],
        "ffn_grads",
        grid=(4,),
        needs=needs,
    )


def attn_grads_kernel(widths, *refs):
    keeps, gots, ours, theirs, outs = refs[:3], refs[3:6], refs[6:9], refs[9:12], refs[12:]
    rows = sum(widths)
    for out, k in zip(outs, ORDER):
        first = 0
        for n, each in enumerate(widths):
            part = slice(2 * each * k, 2 * each * k + 2 * each)
            total = dot(keeps[n][part, :], ours[n][...]) + dot(gots[n][part, :], theirs[n][...])
            total = total.astype(BF16)
            out[first : first + each, :] = total[:each]
            out[rows + first : rows + first + each, :] = total[each:]
            first += each


def attn_grads(keeps, gots, ours, theirs, needs):
    widths = [item.shape[0] // 8 for item in keeps]
    rows, wide = sum(widths), ours[0].shape[1]
    args = (*keeps, *gots, *ours, *theirs)
    outs = [(2 * rows, wide)] * 4
    return call(
        functools.partial(attn_grads_kernel, widths),
        args,
        [full(item.shape) for item in args],
        [full(s) for s in outs],
        [shaped(*s) for s in outs],
        "attn_grads",
        needs=needs,
    )


UP = [(i, (i + 1) % 4) for i in range(4)]
DOWN = [(i, (i + 3) % 4) for i in range(4)]
ACROSS = [(i, (i + 2) % 4) for i in range(4)]


def relay_kernel(up, from_below, down, from_above, up_out, down_out):
    @pl.when(pl.program_id(0) == 0)
    def _():
        up_out[...] = (up[...].astype(F32) + from_below[...].astype(F32)).astype(BF16)
        down_out[...] = down[...]

    @pl.when(pl.program_id(0) == 1)
    def _():
        up_out[...] = up[...]
        down_out[...] = (down[...].astype(F32) + from_above[...].astype(F32)).astype(BF16)


def relay(up, from_below, down, from_above, needs):
    rows, width = from_below.shape
    half = pl.BlockSpec((rows, width), lambda i, *_: (i, 0))
    return call(
        relay_kernel,
        (up, from_below, down, from_above),
        [half, full((rows, width)), half, full((rows, width))],
        [half, half],
        [shaped(2 * rows, width)] * 2,
        "relay",
        grid=(2,),
        needs=needs,
    )


def add_chips_kernel(*refs):
    ins, keep, give = refs[:-2], refs[-2], refs[-1]
    count = len(ins) // 2
    keep[...] = sum(item[...].astype(F32) for item in ins[:count])
    give[...] = sum(item[...].astype(F32) for item in ins[count:]).astype(BF16)


def add_chips(items, needs):
    rows, width = items[0].shape[0] // 2, items[0].shape[1]
    step = rows // 2 if rows % 32 == 0 and (rows // 2) % 16 == 0 else rows
    count = rows // step
    mine = pl.BlockSpec((step, width), lambda i, *_: (i, 0))
    other = pl.BlockSpec((step, width), lambda i, *_: (i + count, 0))
    return call(
        add_chips_kernel,
        (*items, *items),
        [mine] * len(items) + [other] * len(items),
        [mine, mine],
        [shaped(rows, width, dtype=F32), shaped(rows, width)],
        "add_chips",
        grid=(count,),
        needs=needs,
    )


def over_cores(values):
    return lax.ppermute(values, "core", SWAP)


def latents_back_kernel(
    me, got, latents, query_gain, latent_gain, keep, low, high, many, own, gain_part, turns, sems
):
    rows = own.shape[0]
    here = pl.ds(pl.multiple_of(me[0] * rows, rows), rows)
    copies = [
        pltpu.make_async_copy(table.at[here, :], turns.at[n], sems.at[n])
        for n, table in enumerate((keep, low, high))
    ]
    for copy in copies:
        copy.start()
    total = add_up(got)
    for copy in copies:
        copy.wait()

    def back(lanes, gain):
        upstream, values = total[:, lanes], latents[:, lanes]
        factor = root(values)
        normed = values * factor
        gain_part[:, lanes] = jnp.sum(upstream * normed, axis=0, keepdims=True)
        return norm_back(upstream, normed, factor, row(gain)).astype(BF16)

    own[:, :QR] = back(slice(0, QR), query_gain)
    own[:, QR:LAT] = back(slice(QR, LAT), latent_gain)
    own[:, LAT:] = turn(total[:, LAT:], turns[0], turns[1], turns[2], back=True).astype(BF16)
    for k in range(8):
        many[k] = own[...]


def latents_back_of(me, got, latents, query_gain, latent_gain, tables, needs):
    rows = latents.shape[0]
    return call(
        latents_back_kernel,
        (got.reshape(8, rows, WIDE), latents, query_gain, latent_gain, *tables),
        [full((8, rows, WIDE)), full(latents.shape), full((QR,)), full((KVR,)), HBM, HBM, HBM],
        [full((8, rows, WIDE)), full((rows, WIDE)), full((1, LAT))],
        [shaped(8, rows, WIDE), shaped(rows, WIDE), shaped(1, LAT, dtype=F32)],
        "latents_back",
        scratch=[
            pltpu.VMEM((3, rows, 128), F32),
            pltpu.SemaphoreType.DMA((3,)),
        ],
        needs=needs,
        me=me,
        limit=58,
    )


def first_back_of(raw_back, query_down, latent_down, rope_down):
    rope_down[...] = jnp.zeros_like(rope_down)
    rope_down[64:96, :] = latent_down[KVR:, :]
    return (
        dot(raw_back[:, :QR], query_down[...], NT)
        + dot(raw_back[:, QR:LAT], latent_down[:KVR, :])
        + dot(raw_back[:, LAT:], rope_down[...])
    )


def first_gain_kernel(
    me, raw_back, tokens, query_down, latent_down, gain_part, rope_down, own, sem
):
    rows = own.shape[0]
    here = pl.ds(pl.multiple_of(me[0] * rows, rows), rows)
    copy = pltpu.make_async_copy(tokens.at[here, :], own, sem)
    copy.start()
    first_back = first_back_of(raw_back, query_down, latent_down, rope_down)
    copy.wait()
    values = own[...].astype(F32)
    gain_part[...] = jnp.sum(first_back * (values * root(values)), axis=0, keepdims=True)


def first_gain_of(me, own_raw_back, tokens, query_down, latent_down, needs):
    width = tokens.shape[1]
    return call(
        first_gain_kernel,
        (own_raw_back, tokens, query_down, latent_down.T),
        [full(own_raw_back.shape), HBM, full(query_down.shape), full(latent_down.shape[::-1])],
        [full((1, width))],
        [shaped(1, width, dtype=F32)],
        "first_gain",
        scratch=[
            pltpu.VMEM((128, width), BF16),
            pltpu.VMEM((own_raw_back.shape[0], width), BF16),
            pltpu.SemaphoreType.DMA,
        ],
        needs=needs,
        me=me,
    )


def tokens_back_kernel(
    raw_back, tokens, attention_back, query_down, latent_down, gain, tokens_grad, rope_down
):
    first_back = first_back_of(raw_back, query_down, latent_down, rope_down)
    values = tokens[...].astype(F32)
    factor = root(values)
    tokens_grad[...] = attention_back[...].astype(F32) + norm_back(
        first_back, values * factor, factor, row(gain)
    )


def tokens_back_of(raw_back, tokens, attention_back, query_down, latent_down, gain, needs):
    length, width = tokens.shape

    def rows(columns):
        return pl.BlockSpec((TILE, columns), lambda i, *_: (i, 0))

    return call(
        tokens_back_kernel,
        (raw_back, tokens, attention_back, query_down, latent_down.T, gain),
        [
            rows(WIDE),
            rows(width),
            rows(width),
            full(query_down.shape),
            full(latent_down.shape[::-1]),
            full((width,)),
        ],
        [rows(width)],
        [shaped(length, width, dtype=F32)],
        "tokens_back",
        grid=(length // TILE,),
        scratch=[pltpu.VMEM((128, width), BF16)],
        needs=needs,
    )


def finish_ffn_kernel(keep, got, gate, up, down):
    units = gate.shape[1]
    for n, out in enumerate((gate, up, down)):
        lanes = slice(units * n, units * n + units)
        out[...] = keep[:, lanes] + got[:, lanes].astype(F32)


def finish_ffn(keep, got, needs):
    rows, width = keep.shape
    out = (rows, width // 3)
    return call(
        finish_ffn_kernel,
        (keep, got),
        [full(keep.shape), full(got.shape)],
        [full(out)] * 3,
        [shaped(*out, dtype=F32)] * 3,
        "finish_ffn",
        needs=needs,
    )


def finish_attn_kernel(heads, keep, got, out_grad, query_grad, latent_grad):
    total = keep[...] + got[...].astype(F32)
    for h in range(heads):
        lanes = slice(128 * h, 128 * h + 128)
        out_grad[:, 64 * h : 64 * h + 64] = total[:160, 128 * h + 64 : 128 * h + 128]
        query_grad[:, 96 * h : 96 * h + 96] = total[160:208, 128 * h : 128 * h + 96]
    latent_grad[...] = total[208:224]


def finish_attn(keep, got, needs):
    heads = keep.shape[1] // 128
    outs = [(160, 64 * heads), (48, 96 * heads), (16, 128 * heads)]
    return call(
        functools.partial(finish_attn_kernel, heads),
        (keep, got),
        [full(keep.shape), full(got.shape)],
        [full(s) for s in outs],
        [shaped(*s, dtype=F32) for s in outs],
        "finish_attn",
        needs=needs,
    )


GAINS = ((0, 160), (160, 160), (320, 48), (368, 16))


def down_parts_kernel(own_in, raw_back, gains, out):
    total = dot(own_in[...], raw_back[...]).astype(BF16)
    for d in range(16):
        out[d, :20, :] = total[20 * d : 20 * d + 20]
        out[d, 20:, :] = jnp.zeros((4, WIDE), BF16)
        out[d, 20:21, :] = gains[d : d + 1, :]


def down_parts(own_in, raw_back, gains, needs):
    args = (own_in, raw_back, gains)
    return call(
        down_parts_kernel,
        args,
        [full(item.shape) for item in args],
        [full((16, 24, WIDE))],
        [shaped(16, 24, WIDE)],
        "down_parts",
        needs=needs,
        limit=58,
    )


def sum_copies_kernel(got, many):
    total = got[0].astype(F32)
    for d in range(1, 16):
        total = total + got[d].astype(F32)
    for k in range(8):
        many[k] = total.astype(BF16)


def sum_copies(got, needs):
    return call(
        sum_copies_kernel,
        (got,),
        [full(got.shape)],
        [full((8, 24, WIDE))],
        [shaped(8, 24, WIDE)],
        "sum_copies",
        needs=needs,
        limit=58,
    )


def finish_down_kernel(everyone, query_grad, latent_grad, *gains):
    for t in range(8):
        values = everyone[t].astype(F32)
        query_grad[20 * t : 20 * t + 20, :] = values[:20, :QR]
        latent_grad[20 * t : 20 * t + 20, :KVR] = values[:20, QR:LAT]
        latent_grad[20 * t : 20 * t + 20, KVR:] = values[:20, LAT + 64 : LAT + 96]
    total = sum(everyone[t, 16:24, :].astype(F32) for t in range(8))[4:5, :]
    for out, (first, count) in zip(gains, GAINS):
        out[...] = total[:, first : first + count]


def finish_down(everyone):
    everyone = everyone.reshape(8, 24, WIDE)
    outs = [(160, QR), (160, KVR + ROPE)] + [(1, count) for _, count in GAINS]
    return call(
        finish_down_kernel,
        (everyone,),
        [full(everyone.shape)],
        [full(s) for s in outs],
        [shaped(*s, dtype=F32) for s in outs],
        "finish_down",
        limit=58,
    )[0]


def exchange(blocks):
    return lax.all_to_all(blocks.reshape(-1, blocks.shape[-1]), TP, 0, 0, tiled=True)


def on_device(
    tokens,
    first_gain,
    query_down,
    query_gain,
    query_up,
    latent_down,
    latent_gain,
    latent_up,
    out_weight,
    second_gain,
    gate_weight,
    up_weight,
    down_weight,
    cotangent,
):
    length = tokens.shape[0]
    me = lax.axis_index(TP).astype(jnp.int32).reshape(1)
    y, xl, core = lax.axis_index("y"), lax.axis_index("xl"), lax.axis_index("core")
    starts = jnp.stack(
        [
            ((y + k) % 4 * 2 + (xl ^ j)) * 2 + c
            for c in (core, 1 - core)
            for k in range(4)
            for j in range(2)
        ]
    ).astype(jnp.int32)
    tables = rope_tables(length)

    gate_turned, up_turned = gate_weight.T, up_weight.T

    (
        first_in,
        latents,
        query_code,
        latent_code,
        queries,
        keyvals,
        rope_keys,
        heads_out,
        log_total,
        attn_partial,
    ), started = attend(
        me,
        tokens,
        first_gain,
        query_down,
        latent_down,
        query_gain,
        latent_gain,
        query_up,
        latent_up,
        out_weight,
        tables,
    )
    attn_got = exchange(attn_partial)

    (cot_keep, cot_give), picked = halves(starts, [cotangent], [started])
    inner_back = dot(cotangent, down_weight, NT)
    cot_got = over_cores(cot_give)

    (residual, second_many), _ = residual_of(
        me, attn_got, tokens, second_gain, [picked]
    )
    second_in = exchange(second_many)

    turned_in = first_in.T.reshape(16, 8, 20, length)
    own_in = lax.dynamic_slice_in_dim(turned_in, me[0], 1, 1).reshape(320, length)
    (code_keep, code_give, lat_keep, lat_give), picked = halves(
        starts, [query_code, latent_code], [residual]
    )
    code_got, lat_got = over_cores(code_give), over_cores(lat_give)
    heads_got = over_cores(heads_out)

    (gate_back, up_back, inner, back_partial), done = ffn(
        second_in, gate_turned, up_turned, inner_back, [picked, own_in]
    )
    back_got = exchange(back_partial)

    ours = (gate_back, up_back, inner)
    theirs = [over_cores(item) for item in ours]
    (in_keep, in_give), _ = halves(starts, [second_in], [done])
    in_got = over_cores(in_give)
    (far_up, far_down, ffn_up, ffn_down_way, ffn_own), done = ffn_grads(in_keep, in_got, cot_keep, cot_got, ours, theirs, gate_weight.shape[1], [])
    below, above = lax.ppermute(far_up, "y", UP), lax.ppermute(far_down, "y", DOWN)

    (back_many, second_gain_part), done = residual_back_of(
        me, back_got, residual, cotangent, second_gain, [done]
    )
    attention_back = exchange(back_many)
    (ffn_partial,), done = ffn_down(me, inner, down_weight, residual, [done])
    (ffn_up, ffn_down_way), done = relay(ffn_up, below, ffn_down_way, above, [done])
    below, above = lax.ppermute(ffn_up, "y", UP), lax.ppermute(ffn_down_way, "y", DOWN)

    (query_raw_back, keyval_back, latents_partial), back_done = attend_back(
        attention_back,
        out_weight,
        queries,
        keyvals,
        rope_keys,
        log_total,
        query_up,
        latent_up,
        tables,
        [done],
    )
    mixed = lax.psum(ffn_partial, TP)
    latents_got = exchange(latents_partial)

    (out_keep, out_give), picked = halves(starts, [attention_back], [back_done])
    (ffn_keep, ffn_give), done = add_chips([ffn_own, below, above], [back_done])
    ffn_got = lax.ppermute(ffn_give, "xl", SWAP)

    (raw_many, own_raw, latent_gain_parts), done = latents_back_of(
        me, latents_got, latents, query_gain, latent_gain, tables, [done, picked]
    )
    raw_back = exchange(raw_many)

    out_got = over_cores(out_give)
    raw_got, kv_got = over_cores(query_raw_back), over_cores(keyval_back)
    (attn_across, attn_up, attn_down, attn_own), done = attn_grads(
        (out_keep, code_keep, lat_keep),
        (out_got, code_got, lat_got),
        (heads_out, query_raw_back, keyval_back),
        (heads_got, raw_got, kv_got),
        [done],
    )
    attn_got = [
        lax.ppermute(attn_across, "y", ACROSS),
        lax.ppermute(attn_up, "y", UP),
        lax.ppermute(attn_down, "y", DOWN),
    ]
    (first_gain_part,), gain_done = first_gain_of(
        me, own_raw, tokens, query_down, latent_down, [done]
    )

    gains = jnp.concatenate(
        [
            first_gain_part.reshape(16, -1),
            second_gain_part.reshape(16, -1),
            latent_gain_parts[0, :QR].reshape(16, -1),
            latent_gain_parts[0, QR:].reshape(16, -1),
        ],
        axis=1,
    ).astype(BF16)
    gains = jnp.pad(gains, ((0, 0), (0, WIDE - gains.shape[1])))
    (gate_weight_grad, up_weight_grad, down_weight_grad), ended = finish_ffn(
        ffn_keep, ffn_got, [gain_done]
    )
    (parts,), done = down_parts(own_in, raw_back, gains, [ended])
    parts_got = lax.all_to_all(parts, DP, 0, 0, tiled=True)

    (attn_keep, attn_give), done = add_chips([attn_own, *attn_got], [done])
    attn_other = lax.ppermute(attn_give, "xl", SWAP)
    (tokens_grad,), done = tokens_back_of(
        raw_back, tokens, attention_back, query_down, latent_down, first_gain, [done]
    )
    (many,), summed = sum_copies(parts_got, [done])
    everyone = exchange(many)
    (out_weight_grad, query_up_grad, latent_up_grad), done = finish_attn(
        attn_keep, attn_other, [summed, mixed]
    )
    (
        query_down_grad,
        latent_down_grad,
        first_gain_grad,
        second_gain_grad,
        query_gain_grad,
        latent_gain_grad,
    ) = finish_down(everyone)

    return (
        mixed,
        tokens_grad,
        first_gain_grad[0],
        query_down_grad,
        query_gain_grad[0],
        query_up_grad,
        latent_down_grad,
        latent_gain_grad[0],
        latent_up_grad,
        out_weight_grad.T,
        second_gain_grad[0],
        gate_weight_grad,
        up_weight_grad,
        down_weight_grad.T,
    )


def solution(mesh):
    grid = Mesh(mesh.devices.reshape(4, 2, 2, 2, 4), ("y", "xl", "core", "xh", "z"))
    in_specs = (
        P(DP, None),
        P(),
        P(),
        P(),
        P(None, TP),
        P(),
        P(),
        P(None, TP),
        P(TP, None),
        P(),
        P(None, TP),
        P(None, TP),
        P(TP, None),
        P(DP, None),
    )
    out_specs = (
        P(DP, None),
        P(DP, None),
        P(DP),
        P(DP, None),
        P(DP),
        P(DP, TP),
        P(DP, None),
        P(DP),
        P(DP, TP),
        P(TP, DP),
        P(DP),
        P(DP, TP),
        P(DP, TP),
        P(TP, DP),
    )
    return jax.shard_map(
        on_device, mesh=grid, in_specs=in_specs, out_specs=out_specs, check_vma=False
    )
```

```python
import functools

import jax
import jax.numpy as jnp
import numpy as np
from jax import lax
from jax.experimental import pallas as pl
from jax.experimental.pallas import tpu as pltpu
from jax.sharding import Mesh, PartitionSpec as P

NOPE = 64
ROPE = 32
DV = 64
KVR = 256
QR = 768
LAT = QR + KVR
WIDE = LAT + 128

EPS = 1e-05
BASE = 10000.0
SCALE = (NOPE + ROPE) ** (-0.5)

DP = ("y", "xl", "core")
TP = ("xh", "z")
SWAP = [(0, 1), (1, 0)]
F32 = jnp.float32
BF16 = jnp.bfloat16
NT = (((1,), (1,)), ((), ()))
TN = (((0,), (0,)), ((), ()))
NN = (((1,), (0,)), ((), ()))
TILE = 256


def dot(left, right, dims=NN):
    return lax.dot_general(left, right, dims, preferred_element_type=F32)


def params(limit=56):
    return pltpu.CompilerParams(vmem_limit_bytes=limit * 2**20)


HBM = pl.BlockSpec(memory_space=pltpu.HBM)


def call(kernel, args, in_specs, out_specs, out_shape, name, grid=(1,), scratch=(), needs=(), me=None, limit=60):
    first = 0 if me is None else 1
    n_in, n_out = len(args), len(out_shape)

    def body(*refs):
        ins = refs[: first + n_in]
        rest = refs[first + n_in + len(needs) :]
        mark = rest[n_out]

        @pl.when(pl.program_id(0) == 0)
        def _():
            mark[...] = jnp.zeros_like(mark)

        kernel(*ins, *rest[:n_out], *rest[n_out + 1 :])

    *outs, mark = pl.pallas_call(
        body,
        grid_spec=pltpu.PrefetchScalarGridSpec(
            num_scalar_prefetch=first,
            grid=grid,
            in_specs=list(in_specs) + [HBM] * len(needs),
            out_specs=list(out_specs) + [full((8, 128))],
            scratch_shapes=list(scratch),
        ),
        out_shape=list(out_shape) + [jax.ShapeDtypeStruct((8, 128), F32)],
        compiler_params=params(limit),
        cost_estimate=pl.CostEstimate(flops=1, bytes_accessed=1, transcendentals=0),
        name=name,
    )(*(() if me is None else (me,)), *args, *needs)
    return outs, mark


def shaped(*shape, dtype=BF16):
    return jax.ShapeDtypeStruct(shape, dtype)


def full(shape):
    return pl.BlockSpec(shape, lambda *_: (0,) * len(shape))


def rope_tables(length):
    half = ROPE // 2
    rates = np.exp(np.arange(half, dtype=np.float32) * np.float32(-2.0 * np.log(BASE) / ROPE))
    angles = np.arange(length, dtype=np.float32)[:, None] * rates.astype(np.float32)[None, :]
    cosine, sine = np.cos(angles), np.sin(angles)
    keep = np.zeros((length, 128), np.float32)
    keep[:, :NOPE] = 1.0
    keep[:, 64:80] = cosine
    keep[:, 80:96] = cosine
    low = np.zeros((length, 128), np.float32)
    low[:, 64:80] = -sine
    high = np.zeros((length, 128), np.float32)
    high[:, 80:96] = sine
    return jnp.asarray(keep), jnp.asarray(low), jnp.asarray(high)


def turn(values, keep, low, high, back=False):
    moved = pltpu.roll(values, 112, 1) * low + pltpu.roll(values, 16, 1) * high
    return values * keep - moved if back else values * keep + moved


def root(values):
    return lax.rsqrt(jnp.mean(values * values, axis=-1, keepdims=True) + EPS)


def norm_back(upstream, normed, factor, gain):
    scaled = upstream * gain
    return factor * (scaled - normed * jnp.mean(scaled * normed, axis=-1, keepdims=True))


def spread_out_weight(weight_ref, spread_ref, heads):
    spread_ref[...] = jnp.zeros_like(spread_ref)
    for h in range(heads):
        spread_ref[128 * h + 64 : 128 * h + 128, :] = weight_ref[64 * h : 64 * h + 64, :]


def spread_query_up(weight_ref, spread_ref, heads):
    spread_ref[...] = jnp.zeros_like(spread_ref)
    for h in range(heads):
        spread_ref[128 * h : 128 * h + 96, :] = weight_ref[96 * h : 96 * h + 96, :]


def row(ref):
    return ref[...].reshape(1, -1)


def low_lanes(shape):
    return lax.broadcasted_iota(jnp.int32, shape, 1) < NOPE


def causal(keys, queries, first_query):
    key_ids = lax.broadcasted_iota(jnp.int32, (keys, queries), 0)
    query_ids = lax.broadcasted_iota(jnp.int32, (keys, queries), 1) + first_query
    return key_ids <= query_ids


def attend_kernel(
    heads,
    me,
    tokens,
    first_gain,
    query_down,
    latent_down,
    query_gain,
    latent_gain,
    query_up,
    latent_up,
    out_weight,
    keep,
    low,
    high,
    first_in,
    latents,
    query_code,
    latent_code,
    queries,
    keyvals,
    rope_keys,
    heads_out,
    log_total,
    partial,
    raw_latents,
    spread,
    spread_up,
    rope_down,
    kv_all,
    rope_all,
):
    step = pl.program_id(0)

    @pl.when(step == 0)
    def _():
        spread_out_weight(out_weight, spread, heads)
        spread_query_up(query_up, spread_up, heads)
        rope_down[...] = jnp.zeros_like(rope_down)
        rope_down[64:96, :] = latent_down[KVR:, :]

    def rows_of(index, carry):
        rows = pl.ds(pl.multiple_of(index * 32, 32), 32)
        values = tokens[rows, :].astype(F32)
        first_in[rows, :] = (values * root(values) * row(first_gain)).astype(BF16)
        return carry

    lax.fori_loop(0, TILE // 32, rows_of, 0)
    taken = first_in[...]
    query_latent = dot(taken, query_down[...])
    raw_latents[:, :QR] = query_latent
    code = (query_latent * root(query_latent) * row(query_gain)).astype(BF16)
    query_code[...] = code
    latent = dot(taken, latent_down[:KVR, :], NT)
    raw_latents[:, QR:] = latent
    count = latents.shape[0]
    own = me[0] * count

    @pl.when(own // TILE == step)
    def _():
        latents[...] = raw_latents[pl.ds(pl.multiple_of(own % TILE, count), count), :]

    lcode = (latent * root(latent) * row(latent_gain)).astype(BF16)
    latent_code[...] = lcode
    tables = keep[...], low[...], high[...]
    rope = turn(dot(taken, rope_down[...], NT), *tables).astype(BF16)
    rope_keys[...] = rope
    here = pl.ds(pl.multiple_of(step * TILE, TILE), TILE)
    rope_all[here, :] = rope
    kv = dot(lcode, latent_up[...]).astype(BF16)
    keyvals[...] = kv
    kv_all[here, :] = kv
    raw = dot(code, spread_up[...], NT)
    for h in range(heads):
        lanes = slice(128 * h, 128 * h + 128)
        queries[:, lanes] = turn(raw[:, lanes], *tables).astype(BF16)

    def tile(index):
        keys = TILE * (index + 1)
        for h in range(heads):
            lanes = slice(128 * h, 128 * h + 128)
            kv_h = kv_all[:keys, lanes]
            key = jnp.where(low_lanes((keys, 128)), kv_h, rope_all[:keys, :])
            scores = dot(key, queries[:, lanes], NT) * SCALE
            scores = jnp.where(causal(keys, TILE, TILE * index), scores, -1e30)
            top = jnp.max(scores, axis=0, keepdims=True)
            weights = jnp.exp(scores - top)
            total = jnp.sum(weights, axis=0, keepdims=True)
            log_total[h : h + 1, :] = top + jnp.log(total)
            probs = (weights * (1.0 / total)).astype(BF16)
            heads_out[:, lanes] = dot(probs, kv_h, TN).astype(BF16)

    for index in range(2):
        pl.when(step == index)(functools.partial(tile, index))
    partial[...] = dot(heads_out[...], spread[...]).astype(BF16)


def attend(me, tokens, first_gain, query_down, latent_down, query_gain, latent_gain, query_up, latent_up, out_weight, tables):
    latent_down, query_up = latent_down.T, query_up.T
    length, width = tokens.shape
    heads = out_weight.shape[0] // DV
    wide = 128 * heads

    def rows(columns):
        return pl.BlockSpec((TILE, columns), lambda i, *_: (i, 0))

    return call(
        functools.partial(attend_kernel, heads),
        (tokens, first_gain, query_down, latent_down, query_gain, latent_gain, query_up, latent_up, out_weight, *tables),
        [
            rows(width),
            full((width,)),
            full(query_down.shape),
            full(latent_down.shape),
            full((QR,)),
            full((KVR,)),
            full(query_up.shape),
            full(latent_up.shape),
            full(out_weight.shape),
            rows(128),
            rows(128),
            rows(128),
        ],
        [
            rows(width),
            full((length // 8, LAT)),
            rows(QR),
            rows(KVR),
            rows(wide),
            rows(wide),
            rows(128),
            rows(wide),
            pl.BlockSpec((8, TILE), lambda i, *_: (0, i)),
            rows(width),
        ],
        [
            shaped(length, width),
            shaped(length // 8, LAT, dtype=F32),
            shaped(length, QR),
            shaped(length, KVR),
            shaped(length, wide),
            shaped(length, wide),
            shaped(length, 128),
            shaped(length, wide),
            shaped(8, length, dtype=F32),
            shaped(length, width),
        ],
        "attend",
        grid=(length // TILE,),
        me=me,
        scratch=[
            pltpu.VMEM((TILE, LAT), F32),
            pltpu.VMEM((wide, width), BF16),
            pltpu.VMEM((wide, QR), BF16),
            pltpu.VMEM((128, width), BF16),
            pltpu.VMEM((length, wide), BF16),
            pltpu.VMEM((length, 128), BF16),
        ],
    )


def attend_back_kernel(
    heads,
    attention_back,
    out_weight,
    queries,
    keyvals,
    rope_keys,
    log_total,
    query_up,
    latent_up,
    keep,
    low,
    high,
    query_back,
    keyval_back,
    partial,
    spread,
    spread_up,
    kv_grad,
    rope_grad,
    code_grad,
):
    step = pl.program_id(0)

    @pl.when(step == 0)
    def _():
        spread_out_weight(out_weight, spread, heads)
        spread_query_up(query_up, spread_up, heads)
        kv_grad[...] = jnp.zeros_like(kv_grad)
        rope_grad[...] = jnp.zeros_like(rope_grad)

    heads_back = dot(attention_back[...], spread[...], NT).astype(BF16)
    tables = keep[...], low[...], high[...]

    def tile(index):
        keys = TILE * (index + 1)
        low_part = low_lanes((keys, 128))
        for h in range(heads):
            lanes = slice(128 * h, 128 * h + 128)
            kv_h = keyvals[:keys, lanes]
            key = jnp.where(low_part, kv_h, rope_keys[:keys, :])
            query = queries[:, lanes]
            back = heads_back[:, lanes]
            scores = dot(key, query, NT) * SCALE
            probs = jnp.exp(scores - log_total[h : h + 1, :])
            probs = jnp.where(causal(keys, TILE, TILE * index), probs, 0.0)
            prob_back = dot(kv_h, back, NT)
            mean = jnp.sum(probs * prob_back, axis=0, keepdims=True)
            score_back = (probs * (prob_back - mean)).astype(BF16)
            of_values = dot(probs.astype(BF16), back)
            of_keys = dot(score_back, query) * SCALE
            kv_grad[:keys, lanes] += of_values + jnp.where(low_part, of_keys, 0.0)
            rope_grad[:keys, :] += jnp.where(low_part, 0.0, of_keys)
            of_query = dot(score_back, key, TN) * SCALE
            query_back[:, lanes] = turn(of_query, *tables, back=True).astype(BF16)

    for index in range(2):
        pl.when(step == index)(functools.partial(tile, index))
    here = pl.ds(pl.multiple_of(step * TILE, TILE), TILE)
    code_grad[here, :] = dot(query_back[...], spread_up[...]).astype(BF16)

    @pl.when(step == 1)
    def _():
        kv = kv_grad[...].astype(BF16)
        keyval_back[...] = kv
        partial[:, :QR] = code_grad[...]
        partial[:, QR:LAT] = dot(kv, latent_up[...], NT).astype(BF16)
        partial[:, LAT:] = rope_grad[...].astype(BF16)


def attend_back(attention_back, out_weight, queries, keyvals, rope_keys, log_total, query_up, latent_up, tables, needs):
    query_up = query_up.T
    length, width = attention_back.shape
    heads = out_weight.shape[0] // DV
    wide = 128 * heads

    def rows(columns):
        return pl.BlockSpec((TILE, columns), lambda i, *_: (i, 0))

    return call(
        functools.partial(attend_back_kernel, heads),
        (attention_back, out_weight, queries, keyvals, rope_keys, log_total, query_up, latent_up, *tables),
        [
            rows(width),
            full(out_weight.shape),
            rows(wide),
            full((length, wide)),
            full((length, 128)),
            pl.BlockSpec((8, TILE), lambda i, *_: (0, i)),
            full(query_up.shape),
            full(latent_up.shape),
            rows(128),
            rows(128),
            rows(128),
        ],
        [rows(wide), full((length, wide)), full((length, WIDE))],
        [shaped(length, wide), shaped(length, wide), shaped(length, WIDE)],
        "attend_back",
        grid=(length // TILE,),
        scratch=[
            pltpu.VMEM((wide, width), BF16),
            pltpu.VMEM((wide, QR), BF16),
            pltpu.VMEM((length, wide), F32),
            pltpu.VMEM((length, 128), F32),
            pltpu.VMEM((length, QR), BF16),
        ],
        needs=needs,
    )


def add_up(got):
    total = got[0].astype(F32)
    for k in range(1, 8):
        total = total + got[k].astype(F32)
    return total


STEPS = 4


def residual_kernel(me, got, tokens, gain, residual, many):
    del me
    total = tokens[...].astype(F32) + add_up(got)
    residual[...] = total
    second_in = (total * root(total) * row(gain)).astype(BF16)
    for k in range(8):
        many[k] = second_in


def own_specs(rows, width):
    step = rows // STEPS
    return (
        pl.BlockSpec((8, step, width), lambda i, me: (0, i, 0)),
        pl.BlockSpec((step, width), lambda i, me: (i, 0)),
        pl.BlockSpec((step, width), lambda i, me: (me[0] * STEPS + i, 0)),
    )


def residual_of(me, got, tokens, gain, needs):
    width = tokens.shape[1]
    rows = tokens.shape[0] // 8
    eight, one, own = own_specs(rows, width)
    return call(
        residual_kernel,
        (got.reshape(8, rows, width), tokens, gain),
        [eight, own, full((width,))],
        [one, eight],
        [shaped(rows, width, dtype=F32), shaped(8, rows, width)],
        "residual",
        grid=(STEPS,),
        needs=needs,
        me=me,
        limit=58,
    )


def residual_back_kernel(me, got, residual, cotangent, gain, many, gain_part):
    del me
    second_back = add_up(got)
    values = residual[...]
    factor = root(values)
    normed = values * factor
    part = jnp.sum(second_back * normed, axis=0, keepdims=True)

    @pl.when(pl.program_id(0) == 0)
    def _():
        gain_part[...] = part

    @pl.when(pl.program_id(0) > 0)
    def _():
        gain_part[...] += part

    back = cotangent[...].astype(F32) + norm_back(second_back, normed, factor, row(gain))
    back = back.astype(BF16)
    for k in range(8):
        many[k] = back


def residual_back_of(me, got, residual, cotangent, gain, needs):
    rows, width = residual.shape
    eight, one, own = own_specs(rows, width)
    return call(
        residual_back_kernel,
        (got.reshape(8, rows, width), residual, cotangent, gain),
        [eight, one, own, full((width,))],
        [eight, full((1, width))],
        [shaped(8, rows, width), shaped(1, width, dtype=F32)],
        "residual_back",
        grid=(STEPS,),
        needs=needs,
        me=me,
        limit=58,
    )


def ffn_kernel(
    second_in, gate_weight, up_weight, inner_back, gate_back, up_back, inner, partial
):
    taken = second_in[...]
    gate = dot(taken, gate_weight[...], NT)
    up = dot(taken, up_weight[...], NT)
    sigma = 1.0 / (1.0 + jnp.exp(-gate))
    act = gate * sigma
    units = gate.shape[1]
    back = inner_back[...]
    of_gate = (back * up * sigma * (1.0 + gate * (1.0 - sigma))).astype(BF16)
    of_up = (back * act).astype(BF16)
    for out, values in ((gate_back, of_gate), (up_back, of_up), (inner, (act * up).astype(BF16))):
        out[:, :units] = values
        out[:, units:] = jnp.zeros((values.shape[0], out.shape[1] - units), BF16)
    partial[...] = (dot(of_gate, gate_weight[...]) + dot(of_up, up_weight[...])).astype(BF16)


def ffn(second_in, gate_weight, up_weight, inner_back, needs):
    length, width = second_in.shape
    units = gate_weight.shape[0]
    wide = -(-units // 128) * 128

    def rows(columns):
        return pl.BlockSpec((TILE, columns), lambda i, *_: (i, 0))

    return call(
        ffn_kernel,
        (second_in, gate_weight, up_weight, inner_back),
        [rows(width), full((units, width)), full((units, width)), rows(units)],
        [rows(wide), rows(wide), rows(wide), rows(width)],
        [shaped(length, wide)] * 3 + [shaped(length, width)],
        "ffn",
        grid=(length // TILE,),
        needs=needs,
    )


def ffn_down_kernel(me, inner, down_weight, residual, out):
    for i in range(2):
        rows = slice(i * TILE, i * TILE + TILE)
        out[rows, :] = dot(inner[rows, : down_weight.shape[0]], down_weight[...]).astype(BF16)
    count = residual.shape[0]
    own = pl.ds(pl.multiple_of(me[0] * count, count), count)
    out[own, :] = (out[own, :].astype(F32) + residual[...]).astype(BF16)


def ffn_down(me, inner, down_weight, residual, needs):
    length, width = inner.shape[0], down_weight.shape[1]
    return call(
        ffn_down_kernel,
        (inner, down_weight, residual),
        [full(inner.shape), full(down_weight.shape), full(residual.shape)],
        [full((length, width))],
        [shaped(length, width)],
        "ffn_down",
        needs=needs,
        me=me,
    )


def halves_kernel(blocks, width, starts, *refs):
    sources, outs, turned = refs[:blocks], refs[blocks : 3 * blocks], refs[3 * blocks]
    for n in range(blocks):
        source, keep, give = sources[n], outs[2 * n], outs[2 * n + 1]
        columns, each = source.shape[1], width[n]
        for c in range(0, columns, 256):
            turned[c : c + 256, :] = source[:, c : c + 256].T
        for which, out in enumerate((keep, give)):
            for k in range(8):
                first = pl.multiple_of(starts[8 * which + k] * each, 16)
                out[each * k : each * k + each, :] = turned[pl.ds(first, each), :]


def halves(starts, values, needs):
    length = values[0].shape[0]
    widths = [item.shape[1] // 16 for item in values]
    shapes = [(8 * w, length) for w in widths for _ in range(2)]
    return call(
        functools.partial(halves_kernel, len(values), widths),
        tuple(values),
        [full(item.shape) for item in values],
        [full(s) for s in shapes],
        [shaped(*s) for s in shapes],
        "halves",
        scratch=[pltpu.VMEM((max(item.shape[1] for item in values), length), BF16)],
        needs=needs,
        me=starts,
    )


ORDER = (2, 1, 3, 0)


def ffn_grads_kernel(in_keep, in_got, cot_keep, cot_got, *refs):
    ours, theirs, outs = refs[:3], refs[3:6], refs[6:]
    units = outs[0].shape[1] // 3

    def block(*parts):
        for n, (keep, got) in enumerate(((in_keep, in_got), (in_keep, in_got), (cot_keep, cot_got))):
            total = dot(keep[...], ours[n][...]) + dot(got[...], theirs[n][...])
            total = total[:, :units].astype(BF16)
            first = 0
            for out in parts:
                count = out.shape[0]
                out[:, units * n : units * n + units] = total[first : first + count]
                first += count

    for s, parts in enumerate((outs[:2], outs[2:3], outs[3:4], outs[4:])):
        pl.when(pl.program_id(0) == s)(functools.partial(block, *parts))


def ffn_grads(in_keep, in_got, cot_keep, cot_got, ours, theirs, units, needs):
    length, wide = ours[0].shape
    rows = in_keep.shape[0] // 4

    def index(i):
        return (jnp.where(i == 0, 2, jnp.where(i == 1, 1, jnp.where(i == 2, 3, 0))), 0)

    left = pl.BlockSpec((rows, length), index)
    out = (rows, 3 * units)
    outs = [(rows // 2, 3 * units)] * 2 + [out] * 3
    return call(
        ffn_grads_kernel,
        (in_keep, in_got, cot_keep, cot_got, *ours, *theirs),
        [left] * 4 + [full((length, wide))] * 6,
        [full(s) for s in outs],
        [shaped(*s) for s in outs],
        "ffn_grads",
        grid=(4,),
        needs=needs,
    )


def attn_grads_kernel(widths, *refs):
    keeps, gots, ours, theirs, outs = refs[:3], refs[3:6], refs[6:9], refs[9:12], refs[12:]
    rows = sum(widths)
    for out, k in zip(outs, ORDER):
        first = 0
        for n, each in enumerate(widths):
            part = slice(2 * each * k, 2 * each * k + 2 * each)
            total = dot(keeps[n][part, :], ours[n][...]) + dot(gots[n][part, :], theirs[n][...])
            total = total.astype(BF16)
            out[first : first + each, :] = total[:each]
            out[rows + first : rows + first + each, :] = total[each:]
            first += each


def attn_grads(keeps, gots, ours, theirs, needs):
    widths = [item.shape[0] // 8 for item in keeps]
    rows, wide = sum(widths), ours[0].shape[1]
    args = (*keeps, *gots, *ours, *theirs)
    outs = [(2 * rows, wide)] * 4
    return call(
        functools.partial(attn_grads_kernel, widths),
        args,
        [full(item.shape) for item in args],
        [full(s) for s in outs],
        [shaped(*s) for s in outs],
        "attn_grads",
        needs=needs,
    )


UP = [(i, (i + 1) % 4) for i in range(4)]
DOWN = [(i, (i + 3) % 4) for i in range(4)]
ACROSS = [(i, (i + 2) % 4) for i in range(4)]


def relay_kernel(up, from_below, down, from_above, up_out, down_out):
    @pl.when(pl.program_id(0) == 0)
    def _():
        up_out[...] = (up[...].astype(F32) + from_below[...].astype(F32)).astype(BF16)
        down_out[...] = down[...]

    @pl.when(pl.program_id(0) == 1)
    def _():
        up_out[...] = up[...]
        down_out[...] = (down[...].astype(F32) + from_above[...].astype(F32)).astype(BF16)


def relay(up, from_below, down, from_above, needs):
    rows, width = from_below.shape
    half = pl.BlockSpec((rows, width), lambda i, *_: (i, 0))
    return call(
        relay_kernel,
        (up, from_below, down, from_above),
        [half, full((rows, width)), half, full((rows, width))],
        [half, half],
        [shaped(2 * rows, width)] * 2,
        "relay",
        grid=(2,),
        needs=needs,
    )


def add_chips_kernel(*refs):
    ins, keep, give = refs[:-2], refs[-2], refs[-1]
    count = len(ins) // 2
    keep[...] = sum(item[...].astype(F32) for item in ins[:count])
    give[...] = sum(item[...].astype(F32) for item in ins[count:]).astype(BF16)


def add_chips(items, needs):
    rows, width = items[0].shape[0] // 2, items[0].shape[1]
    step = rows // 2 if rows % 32 == 0 and (rows // 2) % 16 == 0 else rows
    count = rows // step
    mine = pl.BlockSpec((step, width), lambda i, *_: (i, 0))
    other = pl.BlockSpec((step, width), lambda i, *_: (i + count, 0))
    return call(
        add_chips_kernel,
        (*items, *items),
        [mine] * len(items) + [other] * len(items),
        [mine, mine],
        [shaped(rows, width, dtype=F32), shaped(rows, width)],
        "add_chips",
        grid=(count,),
        needs=needs,
    )


def over_cores(values):
    return lax.ppermute(values, "core", SWAP)


def latents_back_kernel(
    me, got, latents, query_gain, latent_gain, keep, low, high, many, own, gain_part, turns, sems
):
    rows = own.shape[0]
    here = pl.ds(pl.multiple_of(me[0] * rows, rows), rows)
    copies = [
        pltpu.make_async_copy(table.at[here, :], turns.at[n], sems.at[n])
        for n, table in enumerate((keep, low, high))
    ]
    for copy in copies:
        copy.start()
    total = add_up(got)
    for copy in copies:
        copy.wait()

    def back(lanes, gain):
        upstream, values = total[:, lanes], latents[:, lanes]
        factor = root(values)
        normed = values * factor
        gain_part[:, lanes] = jnp.sum(upstream * normed, axis=0, keepdims=True)
        return norm_back(upstream, normed, factor, row(gain)).astype(BF16)

    own[:, :QR] = back(slice(0, QR), query_gain)
    own[:, QR:LAT] = back(slice(QR, LAT), latent_gain)
    own[:, LAT:] = turn(total[:, LAT:], turns[0], turns[1], turns[2], back=True).astype(BF16)
    for k in range(8):
        many[k] = own[...]


def latents_back_of(me, got, latents, query_gain, latent_gain, tables, needs):
    rows = latents.shape[0]
    return call(
        latents_back_kernel,
        (got.reshape(8, rows, WIDE), latents, query_gain, latent_gain, *tables),
        [full((8, rows, WIDE)), full(latents.shape), full((QR,)), full((KVR,)), HBM, HBM, HBM],
        [full((8, rows, WIDE)), full((rows, WIDE)), full((1, LAT))],
        [shaped(8, rows, WIDE), shaped(rows, WIDE), shaped(1, LAT, dtype=F32)],
        "latents_back",
        scratch=[
            pltpu.VMEM((3, rows, 128), F32),
            pltpu.SemaphoreType.DMA((3,)),
        ],
        needs=needs,
        me=me,
        limit=24,
    )


def first_back_of(raw_back, query_down, latent_down, rope_down):
    rope_down[...] = jnp.zeros_like(rope_down)
    rope_down[64:96, :] = latent_down[KVR:, :]
    return (
        dot(raw_back[:, :QR], query_down[...], NT)
        + dot(raw_back[:, QR:LAT], latent_down[:KVR, :])
        + dot(raw_back[:, LAT:], rope_down[...])
    )


def first_gain_kernel(
    me, raw_back, tokens, query_down, latent_down, gain_part, rope_down, own, sem
):
    rows = own.shape[0]
    here = pl.ds(pl.multiple_of(me[0] * rows, rows), rows)
    copy = pltpu.make_async_copy(tokens.at[here, :], own, sem)
    copy.start()
    first_back = first_back_of(raw_back, query_down, latent_down, rope_down)
    copy.wait()
    values = own[...].astype(F32)
    gain_part[...] = jnp.sum(first_back * (values * root(values)), axis=0, keepdims=True)


def first_gain_of(me, own_raw_back, tokens, query_down, latent_down, needs):
    width = tokens.shape[1]
    return call(
        first_gain_kernel,
        (own_raw_back, tokens, query_down, latent_down.T),
        [full(own_raw_back.shape), HBM, full(query_down.shape), full(latent_down.shape[::-1])],
        [full((1, width))],
        [shaped(1, width, dtype=F32)],
        "first_gain",
        scratch=[
            pltpu.VMEM((128, width), BF16),
            pltpu.VMEM((own_raw_back.shape[0], width), BF16),
            pltpu.SemaphoreType.DMA,
        ],
        needs=needs,
        me=me,
    )


def tokens_back_kernel(
    raw_back, tokens, attention_back, query_down, latent_down, gain, tokens_grad, rope_down
):
    first_back = first_back_of(raw_back, query_down, latent_down, rope_down)
    values = tokens[...].astype(F32)
    factor = root(values)
    tokens_grad[...] = attention_back[...].astype(F32) + norm_back(
        first_back, values * factor, factor, row(gain)
    )


def tokens_back_of(raw_back, tokens, attention_back, query_down, latent_down, gain, needs):
    length, width = tokens.shape

    def rows(columns):
        return pl.BlockSpec((TILE, columns), lambda i, *_: (i, 0))

    return call(
        tokens_back_kernel,
        (raw_back, tokens, attention_back, query_down, latent_down.T, gain),
        [
            rows(WIDE),
            rows(width),
            rows(width),
            full(query_down.shape),
            full(latent_down.shape[::-1]),
            full((width,)),
        ],
        [rows(width)],
        [shaped(length, width, dtype=F32)],
        "tokens_back",
        grid=(length // TILE,),
        scratch=[pltpu.VMEM((128, width), BF16)],
        needs=needs,
    )


def finish_ffn_kernel(keep, got, gate, up, down):
    units = gate.shape[1]
    for n, out in enumerate((gate, up, down)):
        lanes = slice(units * n, units * n + units)
        out[...] = keep[:, lanes] + got[:, lanes].astype(F32)


def finish_ffn(keep, got, needs):
    rows, width = keep.shape
    out = (rows, width // 3)
    return call(
        finish_ffn_kernel,
        (keep, got),
        [full(keep.shape), full(got.shape)],
        [full(out)] * 3,
        [shaped(*out, dtype=F32)] * 3,
        "finish_ffn",
        needs=needs,
    )


def finish_attn_kernel(heads, keep, got, out_grad, query_grad, latent_grad):
    total = keep[...] + got[...].astype(F32)
    for h in range(heads):
        lanes = slice(128 * h, 128 * h + 128)
        out_grad[:, 64 * h : 64 * h + 64] = total[:160, 128 * h + 64 : 128 * h + 128]
        query_grad[:, 96 * h : 96 * h + 96] = total[160:208, 128 * h : 128 * h + 96]
    latent_grad[...] = total[208:224]


def finish_attn(keep, got, needs):
    heads = keep.shape[1] // 128
    outs = [(160, 64 * heads), (48, 96 * heads), (16, 128 * heads)]
    return call(
        functools.partial(finish_attn_kernel, heads),
        (keep, got),
        [full(keep.shape), full(got.shape)],
        [full(s) for s in outs],
        [shaped(*s, dtype=F32) for s in outs],
        "finish_attn",
        needs=needs,
    )


GAINS = ((0, 160), (160, 160), (320, 48), (368, 16))


def down_parts_kernel(own_in, raw_back, gains, out):
    total = dot(own_in[...], raw_back[...]).astype(BF16)
    for d in range(16):
        out[d, :20, :] = total[20 * d : 20 * d + 20]
        out[d, 20:, :] = jnp.zeros((4, WIDE), BF16)
        out[d, 20:21, :] = gains[d : d + 1, :]


def down_parts(own_in, raw_back, gains, needs):
    args = (own_in, raw_back, gains)
    return call(
        down_parts_kernel,
        args,
        [full(item.shape) for item in args],
        [full((16, 24, WIDE))],
        [shaped(16, 24, WIDE)],
        "down_parts",
        needs=needs,
        limit=24,
    )


def sum_copies_kernel(got, many):
    total = got[0].astype(F32)
    for d in range(1, 16):
        total = total + got[d].astype(F32)
    for k in range(8):
        many[k] = total.astype(BF16)


def sum_copies(got, needs):
    return call(
        sum_copies_kernel,
        (got,),
        [full(got.shape)],
        [full((8, 24, WIDE))],
        [shaped(8, 24, WIDE)],
        "sum_copies",
        needs=needs,
        limit=24,
    )


def finish_down_kernel(everyone, query_grad, latent_grad, *gains):
    for t in range(8):
        values = everyone[t].astype(F32)
        query_grad[20 * t : 20 * t + 20, :] = values[:20, :QR]
        latent_grad[20 * t : 20 * t + 20, :KVR] = values[:20, QR:LAT]
        latent_grad[20 * t : 20 * t + 20, KVR:] = values[:20, LAT + 64 : LAT + 96]
    total = sum(everyone[t, 16:24, :].astype(F32) for t in range(8))[4:5, :]
    for out, (first, count) in zip(gains, GAINS):
        out[...] = total[:, first : first + count]


def finish_down(everyone):
    everyone = everyone.reshape(8, 24, WIDE)
    outs = [(160, QR), (160, KVR + ROPE)] + [(1, count) for _, count in GAINS]
    return call(
        finish_down_kernel,
        (everyone,),
        [full(everyone.shape)],
        [full(s) for s in outs],
        [shaped(*s, dtype=F32) for s in outs],
        "finish_down",
        limit=24,
    )[0]


def exchange(blocks):
    return lax.all_to_all(blocks.reshape(-1, blocks.shape[-1]), TP, 0, 0, tiled=True)


def on_device(
    tokens,
    first_gain,
    query_down,
    query_gain,
    query_up,
    latent_down,
    latent_gain,
    latent_up,
    out_weight,
    second_gain,
    gate_weight,
    up_weight,
    down_weight,
    cotangent,
):
    length = tokens.shape[0]
    me = lax.axis_index(TP).astype(jnp.int32).reshape(1)
    y, xl, core = lax.axis_index("y"), lax.axis_index("xl"), lax.axis_index("core")
    starts = jnp.stack(
        [
            ((y + k) % 4 * 2 + (xl ^ j)) * 2 + c
            for c in (core, 1 - core)
            for k in range(4)
            for j in range(2)
        ]
    ).astype(jnp.int32)
    tables = rope_tables(length)

    gate_turned, up_turned = gate_weight.T, up_weight.T

    (
        first_in,
        latents,
        query_code,
        latent_code,
        queries,
        keyvals,
        rope_keys,
        heads_out,
        log_total,
        attn_partial,
    ), started = attend(
        me,
        tokens,
        first_gain,
        query_down,
        latent_down,
        query_gain,
        latent_gain,
        query_up,
        latent_up,
        out_weight,
        tables,
    )
    attn_got = exchange(attn_partial)

    (cot_keep, cot_give), picked = halves(starts, [cotangent], [started])
    inner_back = dot(cotangent, down_weight, NT)
    cot_got = over_cores(cot_give)

    (residual, second_many), _ = residual_of(
        me, attn_got, tokens, second_gain, [picked]
    )
    second_in = exchange(second_many)

    turned_in = first_in.T.reshape(16, 8, 20, length)
    own_in = lax.dynamic_slice_in_dim(turned_in, me[0], 1, 1).reshape(320, length)
    (code_keep, code_give, lat_keep, lat_give), picked = halves(
        starts, [query_code, latent_code], [residual]
    )
    code_got, lat_got = over_cores(code_give), over_cores(lat_give)
    heads_got = over_cores(heads_out)

    (gate_back, up_back, inner, back_partial), done = ffn(
        second_in, gate_turned, up_turned, inner_back, [picked, own_in]
    )
    back_got = exchange(back_partial)

    ours = (gate_back, up_back, inner)
    theirs = [over_cores(item) for item in ours]
    (in_keep, in_give), done = halves(starts, [second_in], [done])
    (ffn_partial,), done = ffn_down(me, inner, down_weight, residual, [done])
    mixed = lax.psum(ffn_partial, TP)
    in_got = over_cores(in_give)
    (far_up, far_down, ffn_up, ffn_down_way, ffn_own), done = ffn_grads(in_keep, in_got, cot_keep, cot_got, ours, theirs, gate_weight.shape[1], [done])
    below, above = lax.ppermute(far_up, "y", UP), lax.ppermute(far_down, "y", DOWN)

    (back_many, second_gain_part), done = residual_back_of(
        me, back_got, residual, cotangent, second_gain, [done]
    )
    attention_back = exchange(back_many)
    (ffn_up, ffn_down_way), done = relay(ffn_up, below, ffn_down_way, above, [done])
    below, above = lax.ppermute(ffn_up, "y", UP), lax.ppermute(ffn_down_way, "y", DOWN)

    (query_raw_back, keyval_back, latents_partial), back_done = attend_back(
        attention_back,
        out_weight,
        queries,
        keyvals,
        rope_keys,
        log_total,
        query_up,
        latent_up,
        tables,
        [done],
    )
    latents_got = exchange(latents_partial)

    (out_keep, out_give), picked = halves(starts, [attention_back], [back_done])
    (ffn_keep, ffn_give), done = add_chips([ffn_own, below, above], [back_done])
    ffn_got = lax.ppermute(ffn_give, "xl", SWAP)

    (raw_many, own_raw, latent_gain_parts), done = latents_back_of(
        me, latents_got, latents, query_gain, latent_gain, tables, [done, picked]
    )
    raw_back = exchange(raw_many)

    out_got = over_cores(out_give)
    raw_got, kv_got = over_cores(query_raw_back), over_cores(keyval_back)
    (attn_across, attn_up, attn_down, attn_own), done = attn_grads(
        (out_keep, code_keep, lat_keep),
        (out_got, code_got, lat_got),
        (heads_out, query_raw_back, keyval_back),
        (heads_got, raw_got, kv_got),
        [done],
    )
    attn_got = [
        lax.ppermute(attn_across, "y", ACROSS),
        lax.ppermute(attn_up, "y", UP),
        lax.ppermute(attn_down, "y", DOWN),
    ]
    (first_gain_part,), gain_done = first_gain_of(
        me, own_raw, tokens, query_down, latent_down, [done]
    )

    gains = jnp.concatenate(
        [
            first_gain_part.reshape(16, -1),
            second_gain_part.reshape(16, -1),
            latent_gain_parts[0, :QR].reshape(16, -1),
            latent_gain_parts[0, QR:].reshape(16, -1),
        ],
        axis=1,
    ).astype(BF16)
    gains = jnp.pad(gains, ((0, 0), (0, WIDE - gains.shape[1])))
    (gate_weight_grad, up_weight_grad, down_weight_grad), ended = finish_ffn(
        ffn_keep, ffn_got, [gain_done, mixed]
    )
    (parts,), done = down_parts(own_in, raw_back, gains, [ended, attn_got[1], attn_got[2]])
    parts_got = lax.all_to_all(parts, DP, 0, 0, tiled=True)

    (attn_keep, attn_give), done = add_chips([attn_own, *attn_got], [done])
    attn_other = lax.ppermute(attn_give, "xl", SWAP)
    (tokens_grad,), done = tokens_back_of(
        raw_back, tokens, attention_back, query_down, latent_down, first_gain, [done]
    )
    (many,), summed = sum_copies(parts_got, [done])
    everyone = exchange(many)
    (out_weight_grad, query_up_grad, latent_up_grad), done = finish_attn(
        attn_keep, attn_other, [summed]
    )
    (
        query_down_grad,
        latent_down_grad,
        first_gain_grad,
        second_gain_grad,
        query_gain_grad,
        latent_gain_grad,
    ) = finish_down(everyone)

    return (
        mixed,
        tokens_grad,
        first_gain_grad[0],
        query_down_grad,
        query_gain_grad[0],
        query_up_grad,
        latent_down_grad,
        latent_gain_grad[0],
        latent_up_grad,
        out_weight_grad.T,
        second_gain_grad[0],
        gate_weight_grad,
        up_weight_grad,
        down_weight_grad.T,
    )


def solution(mesh):
    grid = Mesh(mesh.devices.reshape(4, 2, 2, 2, 4), ("y", "xl", "core", "xh", "z"))
    in_specs = (
        P(DP, None),
        P(),
        P(),
        P(),
        P(None, TP),
        P(),
        P(),
        P(None, TP),
        P(TP, None),
        P(),
        P(None, TP),
        P(None, TP),
        P(TP, None),
        P(DP, None),
    )
    out_specs = (
        P(DP, None),
        P(DP, None),
        P(DP),
        P(DP, None),
        P(DP),
        P(DP, TP),
        P(DP, None),
        P(DP),
        P(DP, TP),
        P(TP, DP),
        P(DP),
        P(DP, TP),
        P(DP, TP),
        P(TP, DP),
    )
    return jax.shard_map(
        on_device, mesh=grid, in_specs=in_specs, out_specs=out_specs, check_vma=False
    )
```

```python
import functools

import jax
import jax.numpy as jnp
import numpy as np
from jax import lax
from jax.experimental import pallas as pl
from jax.experimental.pallas import tpu as pltpu
from jax.sharding import Mesh, PartitionSpec as P

NOPE = 64
ROPE = 32
DV = 64
KVR = 256
QR = 768
LAT = QR + KVR
WIDE = LAT + 128

EPS = 1e-05
BASE = 10000.0
SCALE = (NOPE + ROPE) ** (-0.5)

DP = ("y", "xl", "core")
TP = ("xh", "z")
SWAP = [(0, 1), (1, 0)]
F32 = jnp.float32
BF16 = jnp.bfloat16
NT = (((1,), (1,)), ((), ()))
TN = (((0,), (0,)), ((), ()))
NN = (((1,), (0,)), ((), ()))
TILE = 256


def dot(left, right, dims=NN):
    return lax.dot_general(left, right, dims, preferred_element_type=F32)


def params(limit=56):
    return pltpu.CompilerParams(vmem_limit_bytes=limit * 2**20)


HBM = pl.BlockSpec(memory_space=pltpu.HBM)


def call(kernel, args, in_specs, out_specs, out_shape, name, grid=(1,), scratch=(), needs=(), me=None, limit=60):
    first = 0 if me is None else 1
    n_in, n_out = len(args), len(out_shape)

    def body(*refs):
        ins = refs[: first + n_in]
        rest = refs[first + n_in + len(needs) :]
        mark = rest[n_out]

        @pl.when(pl.program_id(0) == 0)
        def _():
            mark[...] = jnp.zeros_like(mark)

        kernel(*ins, *rest[:n_out], *rest[n_out + 1 :])

    *outs, mark = pl.pallas_call(
        body,
        grid_spec=pltpu.PrefetchScalarGridSpec(
            num_scalar_prefetch=first,
            grid=grid,
            in_specs=list(in_specs) + [HBM] * len(needs),
            out_specs=list(out_specs) + [full((8, 128))],
            scratch_shapes=list(scratch),
        ),
        out_shape=list(out_shape) + [jax.ShapeDtypeStruct((8, 128), F32)],
        compiler_params=params(limit),
        cost_estimate=pl.CostEstimate(flops=1, bytes_accessed=1, transcendentals=0),
        name=name,
    )(*(() if me is None else (me,)), *args, *needs)
    return outs, mark


def shaped(*shape, dtype=BF16):
    return jax.ShapeDtypeStruct(shape, dtype)


def full(shape):
    return pl.BlockSpec(shape, lambda *_: (0,) * len(shape))


def rope_tables(length):
    half = ROPE // 2
    rates = np.exp(np.arange(half, dtype=np.float32) * np.float32(-2.0 * np.log(BASE) / ROPE))
    angles = np.arange(length, dtype=np.float32)[:, None] * rates.astype(np.float32)[None, :]
    cosine, sine = np.cos(angles), np.sin(angles)
    keep = np.zeros((length, 128), np.float32)
    keep[:, :NOPE] = 1.0
    keep[:, 64:80] = cosine
    keep[:, 80:96] = cosine
    low = np.zeros((length, 128), np.float32)
    low[:, 64:80] = -sine
    high = np.zeros((length, 128), np.float32)
    high[:, 80:96] = sine
    return jnp.asarray(keep), jnp.asarray(low), jnp.asarray(high)


def turn(values, keep, low, high, back=False):
    moved = pltpu.roll(values, 112, 1) * low + pltpu.roll(values, 16, 1) * high
    return values * keep - moved if back else values * keep + moved


def root(values):
    return lax.rsqrt(jnp.mean(values * values, axis=-1, keepdims=True) + EPS)


def norm_back(upstream, normed, factor, gain):
    scaled = upstream * gain
    return factor * (scaled - normed * jnp.mean(scaled * normed, axis=-1, keepdims=True))


def spread_out_weight(weight_ref, spread_ref, heads):
    spread_ref[...] = jnp.zeros_like(spread_ref)
    for h in range(heads):
        spread_ref[128 * h + 64 : 128 * h + 128, :] = weight_ref[64 * h : 64 * h + 64, :]


def spread_query_up(weight_ref, spread_ref, heads):
    spread_ref[...] = jnp.zeros_like(spread_ref)
    for h in range(heads):
        spread_ref[128 * h : 128 * h + 96, :] = weight_ref[96 * h : 96 * h + 96, :]


def row(ref):
    return ref[...].reshape(1, -1)


def low_lanes(shape):
    return lax.broadcasted_iota(jnp.int32, shape, 1) < NOPE


def causal(keys, queries, first_query):
    key_ids = lax.broadcasted_iota(jnp.int32, (keys, queries), 0)
    query_ids = lax.broadcasted_iota(jnp.int32, (keys, queries), 1) + first_query
    return key_ids <= query_ids


def attend_kernel(
    heads,
    me,
    tokens,
    first_gain,
    query_down,
    latent_down,
    query_gain,
    latent_gain,
    query_up,
    latent_up,
    out_weight,
    keep,
    low,
    high,
    first_in,
    latents,
    query_code,
    latent_code,
    queries,
    keyvals,
    rope_keys,
    heads_out,
    log_total,
    partial,
    raw_latents,
    spread,
    spread_up,
    rope_down,
    kv_all,
    rope_all,
):
    step = pl.program_id(0)

    @pl.when(step == 0)
    def _():
        spread_out_weight(out_weight, spread, heads)
        spread_query_up(query_up, spread_up, heads)
        rope_down[...] = jnp.zeros_like(rope_down)
        rope_down[64:96, :] = latent_down[KVR:, :]

    def rows_of(index, carry):
        rows = pl.ds(pl.multiple_of(index * 32, 32), 32)
        values = tokens[rows, :].astype(F32)
        first_in[rows, :] = (values * root(values) * row(first_gain)).astype(BF16)
        return carry

    lax.fori_loop(0, TILE // 32, rows_of, 0)
    taken = first_in[...]
    query_latent = dot(taken, query_down[...])
    raw_latents[:, :QR] = query_latent
    code = (query_latent * root(query_latent) * row(query_gain)).astype(BF16)
    query_code[...] = code
    latent = dot(taken, latent_down[:KVR, :], NT)
    raw_latents[:, QR:] = latent
    count = latents.shape[0]
    own = me[0] * count

    @pl.when(own // TILE == step)
    def _():
        latents[...] = raw_latents[pl.ds(pl.multiple_of(own % TILE, count), count), :]

    lcode = (latent * root(latent) * row(latent_gain)).astype(BF16)
    latent_code[...] = lcode
    tables = keep[...], low[...], high[...]
    rope = turn(dot(taken, rope_down[...], NT), *tables).astype(BF16)
    rope_keys[...] = rope
    here = pl.ds(pl.multiple_of(step * TILE, TILE), TILE)
    rope_all[here, :] = rope
    kv = dot(lcode, latent_up[...]).astype(BF16)
    keyvals[...] = kv
    kv_all[here, :] = kv
    raw = dot(code, spread_up[...], NT)
    for h in range(heads):
        lanes = slice(128 * h, 128 * h + 128)
        queries[:, lanes] = turn(raw[:, lanes], *tables).astype(BF16)

    def tile(index):
        keys = TILE * (index + 1)
        for h in range(heads):
            lanes = slice(128 * h, 128 * h + 128)
            kv_h = kv_all[:keys, lanes]
            key = jnp.where(low_lanes((keys, 128)), kv_h, rope_all[:keys, :])
            scores = dot(key, queries[:, lanes], NT) * SCALE
            scores = jnp.where(causal(keys, TILE, TILE * index), scores, -1e30)
            top = jnp.max(scores, axis=0, keepdims=True)
            weights = jnp.exp(scores - top)
            total = jnp.sum(weights, axis=0, keepdims=True)
            log_total[h : h + 1, :] = top + jnp.log(total)
            probs = (weights * (1.0 / total)).astype(BF16)
            heads_out[:, lanes] = dot(probs, kv_h, TN).astype(BF16)

    for index in range(2):
        pl.when(step == index)(functools.partial(tile, index))
    partial[...] = dot(heads_out[...], spread[...]).astype(BF16)


def attend(me, tokens, first_gain, query_down, latent_down, query_gain, latent_gain, query_up, latent_up, out_weight, tables):
    latent_down, query_up = latent_down.T, query_up.T
    length, width = tokens.shape
    heads = out_weight.shape[0] // DV
    wide = 128 * heads

    def rows(columns):
        return pl.BlockSpec((TILE, columns), lambda i, *_: (i, 0))

    return call(
        functools.partial(attend_kernel, heads),
        (tokens, first_gain, query_down, latent_down, query_gain, latent_gain, query_up, latent_up, out_weight, *tables),
        [
            rows(width),
            full((width,)),
            full(query_down.shape),
            full(latent_down.shape),
            full((QR,)),
            full((KVR,)),
            full(query_up.shape),
            full(latent_up.shape),
            full(out_weight.shape),
            rows(128),
            rows(128),
            rows(128),
        ],
        [
            rows(width),
            full((length // 8, LAT)),
            rows(QR),
            rows(KVR),
            rows(wide),
            rows(wide),
            rows(128),
            rows(wide),
            pl.BlockSpec((8, TILE), lambda i, *_: (0, i)),
            rows(width),
        ],
        [
            shaped(length, width),
            shaped(length // 8, LAT, dtype=F32),
            shaped(length, QR),
            shaped(length, KVR),
            shaped(length, wide),
            shaped(length, wide),
            shaped(length, 128),
            shaped(length, wide),
            shaped(8, length, dtype=F32),
            shaped(length, width),
        ],
        "attend",
        grid=(length // TILE,),
        me=me,
        scratch=[
            pltpu.VMEM((TILE, LAT), F32),
            pltpu.VMEM((wide, width), BF16),
            pltpu.VMEM((wide, QR), BF16),
            pltpu.VMEM((128, width), BF16),
            pltpu.VMEM((length, wide), BF16),
            pltpu.VMEM((length, 128), BF16),
        ],
    )


def attend_back_kernel(
    heads,
    attention_back,
    out_weight,
    queries,
    keyvals,
    rope_keys,
    log_total,
    query_up,
    latent_up,
    keep,
    low,
    high,
    query_back,
    keyval_back,
    partial,
    spread,
    spread_up,
    kv_grad,
    rope_grad,
    code_grad,
):
    step = pl.program_id(0)

    @pl.when(step == 0)
    def _():
        spread_out_weight(out_weight, spread, heads)
        spread_query_up(query_up, spread_up, heads)
        kv_grad[...] = jnp.zeros_like(kv_grad)
        rope_grad[...] = jnp.zeros_like(rope_grad)

    heads_back = dot(attention_back[...], spread[...], NT).astype(BF16)
    tables = keep[...], low[...], high[...]

    def tile(index):
        keys = TILE * (index + 1)
        low_part = low_lanes((keys, 128))
        for h in range(heads):
            lanes = slice(128 * h, 128 * h + 128)
            kv_h = keyvals[:keys, lanes]
            key = jnp.where(low_part, kv_h, rope_keys[:keys, :])
            query = queries[:, lanes]
            back = heads_back[:, lanes]
            scores = dot(key, query, NT) * SCALE
            probs = jnp.exp(scores - log_total[h : h + 1, :])
            probs = jnp.where(causal(keys, TILE, TILE * index), probs, 0.0)
            prob_back = dot(kv_h, back, NT)
            mean = jnp.sum(probs * prob_back, axis=0, keepdims=True)
            score_back = (probs * (prob_back - mean)).astype(BF16)
            of_values = dot(probs.astype(BF16), back)
            of_keys = dot(score_back, query) * SCALE
            kv_grad[:keys, lanes] += of_values + jnp.where(low_part, of_keys, 0.0)
            rope_grad[:keys, :] += jnp.where(low_part, 0.0, of_keys)
            of_query = dot(score_back, key, TN) * SCALE
            query_back[:, lanes] = turn(of_query, *tables, back=True).astype(BF16)

    for index in range(2):
        pl.when(step == index)(functools.partial(tile, index))
    here = pl.ds(pl.multiple_of(step * TILE, TILE), TILE)
    code_grad[here, :] = dot(query_back[...], spread_up[...]).astype(BF16)

    @pl.when(step == 1)
    def _():
        kv = kv_grad[...].astype(BF16)
        keyval_back[...] = kv
        partial[:, :QR] = code_grad[...]
        partial[:, QR:LAT] = dot(kv, latent_up[...], NT).astype(BF16)
        partial[:, LAT:] = rope_grad[...].astype(BF16)


def attend_back(attention_back, out_weight, queries, keyvals, rope_keys, log_total, query_up, latent_up, tables, needs):
    query_up = query_up.T
    length, width = attention_back.shape
    heads = out_weight.shape[0] // DV
    wide = 128 * heads

    def rows(columns):
        return pl.BlockSpec((TILE, columns), lambda i, *_: (i, 0))

    return call(
        functools.partial(attend_back_kernel, heads),
        (attention_back, out_weight, queries, keyvals, rope_keys, log_total, query_up, latent_up, *tables),
        [
            rows(width),
            full(out_weight.shape),
            rows(wide),
            full((length, wide)),
            full((length, 128)),
            pl.BlockSpec((8, TILE), lambda i, *_: (0, i)),
            full(query_up.shape),
            full(latent_up.shape),
            rows(128),
            rows(128),
            rows(128),
        ],
        [rows(wide), full((length, wide)), full((length, WIDE))],
        [shaped(length, wide), shaped(length, wide), shaped(length, WIDE)],
        "attend_back",
        grid=(length // TILE,),
        scratch=[
            pltpu.VMEM((wide, width), BF16),
            pltpu.VMEM((wide, QR), BF16),
            pltpu.VMEM((length, wide), F32),
            pltpu.VMEM((length, 128), F32),
            pltpu.VMEM((length, QR), BF16),
        ],
        needs=needs,
    )


def after(values, *others):
    def nothing(*refs):
        del refs

    return pl.pallas_call(
        nothing,
        in_specs=[HBM] * (1 + len(others)),
        out_specs=HBM,
        out_shape=jax.ShapeDtypeStruct(values.shape, values.dtype),
        input_output_aliases={0: 0},
        compiler_params=params(60),
        cost_estimate=pl.CostEstimate(flops=1, bytes_accessed=1, transcendentals=0),
        name="after",
    )(values, *others)


def add_up(got):
    total = got[0].astype(F32)
    for k in range(1, 8):
        total = total + got[k].astype(F32)
    return total


STEPS = 2


def residual_kernel(me, got, tokens, gain, residual, many):
    del me
    total = tokens[...].astype(F32) + add_up(got)
    residual[...] = total
    second_in = (total * root(total) * row(gain)).astype(BF16)
    for k in range(8):
        many[k] = second_in


def own_specs(rows, width):
    step = rows // STEPS
    return (
        pl.BlockSpec((8, step, width), lambda i, me: (0, i, 0)),
        pl.BlockSpec((step, width), lambda i, me: (i, 0)),
        pl.BlockSpec((step, width), lambda i, me: (me[0] * STEPS + i, 0)),
    )


def residual_of(me, got, tokens, gain, needs):
    width = tokens.shape[1]
    rows = tokens.shape[0] // 8
    eight, one, own = own_specs(rows, width)
    return call(
        residual_kernel,
        (got.reshape(8, rows, width), tokens, gain),
        [eight, own, full((width,))],
        [one, eight],
        [shaped(rows, width, dtype=F32), shaped(8, rows, width)],
        "residual",
        grid=(STEPS,),
        needs=needs,
        me=me,
        limit=58,
    )


def residual_back_kernel(me, got, residual, cotangent, gain, many, gain_part):
    del me
    second_back = add_up(got)
    values = residual[...]
    factor = root(values)
    normed = values * factor
    part = jnp.sum(second_back * normed, axis=0, keepdims=True)

    @pl.when(pl.program_id(0) == 0)
    def _():
        gain_part[...] = part

    @pl.when(pl.program_id(0) > 0)
    def _():
        gain_part[...] += part

    back = cotangent[...].astype(F32) + norm_back(second_back, normed, factor, row(gain))
    back = back.astype(BF16)
    for k in range(8):
        many[k] = back


def residual_back_of(me, got, residual, cotangent, gain, needs):
    rows, width = residual.shape
    eight, one, own = own_specs(rows, width)
    return call(
        residual_back_kernel,
        (got.reshape(8, rows, width), residual, cotangent, gain),
        [eight, one, own, full((width,))],
        [eight, full((1, width))],
        [shaped(8, rows, width), shaped(1, width, dtype=F32)],
        "residual_back",
        grid=(STEPS,),
        needs=needs,
        me=me,
        limit=58,
    )


def ffn_kernel(
    second_in, gate_weight, up_weight, inner_back, gate_back, up_back, inner, partial
):
    taken = second_in[...]
    gate = dot(taken, gate_weight[...], NT)
    up = dot(taken, up_weight[...], NT)
    sigma = 1.0 / (1.0 + jnp.exp(-gate))
    act = gate * sigma
    units = gate.shape[1]
    back = inner_back[...]
    of_gate = (back * up * sigma * (1.0 + gate * (1.0 - sigma))).astype(BF16)
    of_up = (back * act).astype(BF16)
    for out, values in ((gate_back, of_gate), (up_back, of_up), (inner, (act * up).astype(BF16))):
        out[:, :units] = values
        out[:, units:] = jnp.zeros((values.shape[0], out.shape[1] - units), BF16)
    partial[...] = (dot(of_gate, gate_weight[...]) + dot(of_up, up_weight[...])).astype(BF16)


def ffn(second_in, gate_weight, up_weight, inner_back, needs):
    length, width = second_in.shape
    units = gate_weight.shape[0]
    wide = -(-units // 128) * 128

    def rows(columns):
        return pl.BlockSpec((TILE, columns), lambda i, *_: (i, 0))

    return call(
        ffn_kernel,
        (second_in, gate_weight, up_weight, inner_back),
        [rows(width), full((units, width)), full((units, width)), rows(units)],
        [rows(wide), rows(wide), rows(wide), rows(width)],
        [shaped(length, wide)] * 3 + [shaped(length, width)],
        "ffn",
        grid=(length // TILE,),
        needs=needs,
    )


def ffn_down_kernel(inner, down_weight, out):
    out[...] = dot(inner[:, : down_weight.shape[0]], down_weight[...]).astype(BF16)


def ffn_down(inner, down_weight, needs):
    length, width = inner.shape[0], down_weight.shape[1]
    return call(
        ffn_down_kernel,
        (inner, down_weight),
        [pl.BlockSpec((TILE, inner.shape[1]), lambda i: (i, 0)), full(down_weight.shape)],
        [pl.BlockSpec((TILE, width), lambda i: (i, 0))],
        [shaped(length, width)],
        "ffn_down",
        grid=(length // TILE,),
        needs=needs,
    )


def mixed_kernel(got, residual, out):
    out[...] = (residual[...] + add_up(got)).astype(BF16)


def mixed_of(got, residual, needs):
    rows, width = residual.shape
    step = rows // STEPS
    one = pl.BlockSpec((step, width), lambda i: (i, 0))
    return call(
        mixed_kernel,
        (got.reshape(8, rows, width), residual),
        [pl.BlockSpec((8, step, width), lambda i: (0, i, 0)), one],
        [one],
        [shaped(rows, width)],
        "mixed",
        grid=(STEPS,),
        needs=needs,
        limit=58,
    )


def halves_kernel(blocks, width, starts, *refs):
    sources, outs, turned = refs[:blocks], refs[blocks : 3 * blocks], refs[3 * blocks]
    for n in range(blocks):
        source, keep, give = sources[n], outs[2 * n], outs[2 * n + 1]
        columns, each = source.shape[1], width[n]
        for c in range(0, columns, 256):
            turned[c : c + 256, :] = source[:, c : c + 256].T
        for which, out in enumerate((keep, give)):
            for k in range(8):
                first = pl.multiple_of(starts[8 * which + k] * each, 16)
                out[each * k : each * k + each, :] = turned[pl.ds(first, each), :]


def halves(starts, values, needs):
    length = values[0].shape[0]
    widths = [item.shape[1] // 16 for item in values]
    shapes = [(8 * w, length) for w in widths for _ in range(2)]
    return call(
        functools.partial(halves_kernel, len(values), widths),
        tuple(values),
        [full(item.shape) for item in values],
        [full(s) for s in shapes],
        [shaped(*s) for s in shapes],
        "halves",
        scratch=[pltpu.VMEM((max(item.shape[1] for item in values), length), BF16)],
        needs=needs,
        me=starts,
    )


ORDER = (2, 1, 3, 0)


def ffn_grads_kernel(in_keep, in_got, cot_keep, cot_got, *refs):
    ours, theirs, outs = refs[:3], refs[3:6], refs[6:]
    units = outs[0].shape[1] // 3

    def block(*parts):
        for n, (keep, got) in enumerate(((in_keep, in_got), (in_keep, in_got), (cot_keep, cot_got))):
            total = dot(keep[...], ours[n][...]) + dot(got[...], theirs[n][...])
            total = total[:, :units].astype(BF16)
            first = 0
            for out in parts:
                count = out.shape[0]
                out[:, units * n : units * n + units] = total[first : first + count]
                first += count

    for s, parts in enumerate((outs[:2], outs[2:3], outs[3:4], outs[4:])):
        pl.when(pl.program_id(0) == s)(functools.partial(block, *parts))


def ffn_grads(in_keep, in_got, cot_keep, cot_got, ours, theirs, units, needs):
    length, wide = ours[0].shape
    rows = in_keep.shape[0] // 4

    def index(i):
        return (jnp.where(i == 0, 2, jnp.where(i == 1, 1, jnp.where(i == 2, 3, 0))), 0)

    left = pl.BlockSpec((rows, length), index)
    out = (rows, 3 * units)
    outs = [(rows // 2, 3 * units)] * 2 + [out] * 3
    return call(
        ffn_grads_kernel,
        (in_keep, in_got, cot_keep, cot_got, *ours, *theirs),
        [left] * 4 + [full((length, wide))] * 6,
        [full(s) for s in outs],
        [shaped(*s) for s in outs],
        "ffn_grads",
        grid=(4,),
        needs=needs,
    )


def attn_grads_kernel(widths, *refs):
    keeps, gots, ours, theirs, outs = refs[:3], refs[3:6], refs[6:9], refs[9:12], refs[12:]
    rows = sum(widths)
    for out, k in zip(outs, ORDER):
        first = 0
        for n, each in enumerate(widths):
            part = slice(2 * each * k, 2 * each * k + 2 * each)
            total = dot(keeps[n][part, :], ours[n][...]) + dot(gots[n][part, :], theirs[n][...])
            total = total.astype(BF16)
            out[first : first + each, :] = total[:each]
            out[rows + first : rows + first + each, :] = total[each:]
            first += each


def attn_grads(keeps, gots, ours, theirs, needs):
    widths = [item.shape[0] // 8 for item in keeps]
    rows, wide = sum(widths), ours[0].shape[1]
    args = (*keeps, *gots, *ours, *theirs)
    outs = [(2 * rows, wide)] * 4
    return call(
        functools.partial(attn_grads_kernel, widths),
        args,
        [full(item.shape) for item in args],
        [full(s) for s in outs],
        [shaped(*s) for s in outs],
        "attn_grads",
        needs=needs,
    )


UP = [(i, (i + 1) % 4) for i in range(4)]
DOWN = [(i, (i + 3) % 4) for i in range(4)]
ACROSS = [(i, (i + 2) % 4) for i in range(4)]


def relay_kernel(up, from_below, down, from_above, up_out, down_out):
    @pl.when(pl.program_id(0) == 0)
    def _():
        up_out[...] = (up[...].astype(F32) + from_below[...].astype(F32)).astype(BF16)
        down_out[...] = down[...]

    @pl.when(pl.program_id(0) == 1)
    def _():
        up_out[...] = up[...]
        down_out[...] = (down[...].astype(F32) + from_above[...].astype(F32)).astype(BF16)


def relay(up, from_below, down, from_above, needs):
    rows, width = from_below.shape
    half = pl.BlockSpec((rows, width), lambda i, *_: (i, 0))
    return call(
        relay_kernel,
        (up, from_below, down, from_above),
        [half, full((rows, width)), half, full((rows, width))],
        [half, half],
        [shaped(2 * rows, width)] * 2,
        "relay",
        grid=(2,),
        needs=needs,
    )


def add_chips_kernel(*refs):
    ins, keep, give = refs[:-2], refs[-2], refs[-1]
    count = len(ins) // 2
    keep[...] = sum(item[...].astype(F32) for item in ins[:count])
    give[...] = sum(item[...].astype(F32) for item in ins[count:]).astype(BF16)


def add_chips(items, needs):
    rows, width = items[0].shape[0] // 2, items[0].shape[1]
    step = rows // 2 if rows % 32 == 0 and (rows // 2) % 16 == 0 else rows
    count = rows // step
    mine = pl.BlockSpec((step, width), lambda i, *_: (i, 0))
    other = pl.BlockSpec((step, width), lambda i, *_: (i + count, 0))
    return call(
        add_chips_kernel,
        (*items, *items),
        [mine] * len(items) + [other] * len(items),
        [mine, mine],
        [shaped(rows, width, dtype=F32), shaped(rows, width)],
        "add_chips",
        grid=(count,),
        needs=needs,
    )


def over_cores(values):
    return lax.ppermute(values, "core", SWAP)


def latents_back_kernel(
    me, got, latents, query_gain, latent_gain, keep, low, high, many, own, gain_part, turns, sems
):
    rows = own.shape[0]
    here = pl.ds(pl.multiple_of(me[0] * rows, rows), rows)
    copies = [
        pltpu.make_async_copy(table.at[here, :], turns.at[n], sems.at[n])
        for n, table in enumerate((keep, low, high))
    ]
    for copy in copies:
        copy.start()
    total = add_up(got)
    for copy in copies:
        copy.wait()

    def back(lanes, gain):
        upstream, values = total[:, lanes], latents[:, lanes]
        factor = root(values)
        normed = values * factor
        gain_part[:, lanes] = jnp.sum(upstream * normed, axis=0, keepdims=True)
        return norm_back(upstream, normed, factor, row(gain)).astype(BF16)

    own[:, :QR] = back(slice(0, QR), query_gain)
    own[:, QR:LAT] = back(slice(QR, LAT), latent_gain)
    own[:, LAT:] = turn(total[:, LAT:], turns[0], turns[1], turns[2], back=True).astype(BF16)
    for k in range(8):
        many[k] = own[...]


def latents_back_of(me, got, latents, query_gain, latent_gain, tables, needs):
    rows = latents.shape[0]
    return call(
        latents_back_kernel,
        (got.reshape(8, rows, WIDE), latents, query_gain, latent_gain, *tables),
        [full((8, rows, WIDE)), full(latents.shape), full((QR,)), full((KVR,)), HBM, HBM, HBM],
        [full((8, rows, WIDE)), full((rows, WIDE)), full((1, LAT))],
        [shaped(8, rows, WIDE), shaped(rows, WIDE), shaped(1, LAT, dtype=F32)],
        "latents_back",
        scratch=[
            pltpu.VMEM((3, rows, 128), F32),
            pltpu.SemaphoreType.DMA((3,)),
        ],
        needs=needs,
        me=me,
        limit=24,
    )


def first_back_of(raw_back, query_down, latent_down, rope_down):
    rope_down[...] = jnp.zeros_like(rope_down)
    rope_down[64:96, :] = latent_down[KVR:, :]
    return (
        dot(raw_back[:, :QR], query_down[...], NT)
        + dot(raw_back[:, QR:LAT], latent_down[:KVR, :])
        + dot(raw_back[:, LAT:], rope_down[...])
    )


def first_gain_kernel(
    me, raw_back, tokens, query_down, latent_down, gain_part, rope_down, own, sem
):
    rows = own.shape[0]
    here = pl.ds(pl.multiple_of(me[0] * rows, rows), rows)
    copy = pltpu.make_async_copy(tokens.at[here, :], own, sem)
    copy.start()
    first_back = first_back_of(raw_back, query_down, latent_down, rope_down)
    copy.wait()
    values = own[...].astype(F32)
    gain_part[...] = jnp.sum(first_back * (values * root(values)), axis=0, keepdims=True)


def first_gain_of(me, own_raw_back, tokens, query_down, latent_down, needs):
    width = tokens.shape[1]
    return call(
        first_gain_kernel,
        (own_raw_back, tokens, query_down, latent_down.T),
        [full(own_raw_back.shape), HBM, full(query_down.shape), full(latent_down.shape[::-1])],
        [full((1, width))],
        [shaped(1, width, dtype=F32)],
        "first_gain",
        scratch=[
            pltpu.VMEM((128, width), BF16),
            pltpu.VMEM((own_raw_back.shape[0], width), BF16),
            pltpu.SemaphoreType.DMA,
        ],
        needs=needs,
        me=me,
    )


def tokens_back_kernel(
    raw_back, tokens, attention_back, query_down, latent_down, gain, tokens_grad, rope_down
):
    first_back = first_back_of(raw_back, query_down, latent_down, rope_down)
    values = tokens[...].astype(F32)
    factor = root(values)
    tokens_grad[...] = attention_back[...].astype(F32) + norm_back(
        first_back, values * factor, factor, row(gain)
    )


def tokens_back_of(raw_back, tokens, attention_back, query_down, latent_down, gain, needs):
    length, width = tokens.shape

    def rows(columns):
        return pl.BlockSpec((TILE, columns), lambda i, *_: (i, 0))

    return call(
        tokens_back_kernel,
        (raw_back, tokens, attention_back, query_down, latent_down.T, gain),
        [
            rows(WIDE),
            rows(width),
            rows(width),
            full(query_down.shape),
            full(latent_down.shape[::-1]),
            full((width,)),
        ],
        [rows(width)],
        [shaped(length, width, dtype=F32)],
        "tokens_back",
        grid=(length // TILE,),
        scratch=[pltpu.VMEM((128, width), BF16)],
        needs=needs,
    )


def finish_ffn_kernel(keep, got, gate, up, down):
    units = gate.shape[1]
    for n, out in enumerate((gate, up, down)):
        lanes = slice(units * n, units * n + units)
        out[...] = keep[:, lanes] + got[:, lanes].astype(F32)


def finish_ffn(keep, got, needs):
    rows, width = keep.shape
    out = (rows, width // 3)
    return call(
        finish_ffn_kernel,
        (keep, got),
        [full(keep.shape), full(got.shape)],
        [full(out)] * 3,
        [shaped(*out, dtype=F32)] * 3,
        "finish_ffn",
        needs=needs,
    )


def finish_attn_kernel(heads, keep, got, out_grad, query_grad, latent_grad):
    total = keep[...] + got[...].astype(F32)
    for h in range(heads):
        lanes = slice(128 * h, 128 * h + 128)
        out_grad[:, 64 * h : 64 * h + 64] = total[:160, 128 * h + 64 : 128 * h + 128]
        query_grad[:, 96 * h : 96 * h + 96] = total[160:208, 128 * h : 128 * h + 96]
    latent_grad[...] = total[208:224]


def finish_attn(keep, got, needs):
    heads = keep.shape[1] // 128
    outs = [(160, 64 * heads), (48, 96 * heads), (16, 128 * heads)]
    return call(
        functools.partial(finish_attn_kernel, heads),
        (keep, got),
        [full(keep.shape), full(got.shape)],
        [full(s) for s in outs],
        [shaped(*s, dtype=F32) for s in outs],
        "finish_attn",
        needs=needs,
    )


GAINS = ((0, 160), (160, 160), (320, 48), (368, 16))


def down_parts_kernel(own_in, raw_back, gains, out):
    total = dot(own_in[...], raw_back[...]).astype(BF16)
    for d in range(16):
        out[d, :20, :] = total[20 * d : 20 * d + 20]
        out[d, 20:, :] = jnp.zeros((4, WIDE), BF16)
        out[d, 20:21, :] = gains[d : d + 1, :]


def down_parts(own_in, raw_back, gains, needs):
    args = (own_in, raw_back, gains)
    return call(
        down_parts_kernel,
        args,
        [full(item.shape) for item in args],
        [full((16, 24, WIDE))],
        [shaped(16, 24, WIDE)],
        "down_parts",
        needs=needs,
        limit=24,
    )


def sum_copies_kernel(got, many):
    total = got[0].astype(F32)
    for d in range(1, 16):
        total = total + got[d].astype(F32)
    for k in range(8):
        many[k] = total.astype(BF16)


def sum_copies(got, needs):
    return call(
        sum_copies_kernel,
        (got,),
        [full(got.shape)],
        [full((8, 24, WIDE))],
        [shaped(8, 24, WIDE)],
        "sum_copies",
        needs=needs,
        limit=24,
    )


def finish_down_kernel(everyone, query_grad, latent_grad, *gains):
    for t in range(8):
        values = everyone[t].astype(F32)
        query_grad[20 * t : 20 * t + 20, :] = values[:20, :QR]
        latent_grad[20 * t : 20 * t + 20, :KVR] = values[:20, QR:LAT]
        latent_grad[20 * t : 20 * t + 20, KVR:] = values[:20, LAT + 64 : LAT + 96]
    total = sum(everyone[t, 16:24, :].astype(F32) for t in range(8))[4:5, :]
    for out, (first, count) in zip(gains, GAINS):
        out[...] = total[:, first : first + count]


def finish_down(everyone):
    everyone = everyone.reshape(8, 24, WIDE)
    outs = [(160, QR), (160, KVR + ROPE)] + [(1, count) for _, count in GAINS]
    return call(
        finish_down_kernel,
        (everyone,),
        [full(everyone.shape)],
        [full(s) for s in outs],
        [shaped(*s, dtype=F32) for s in outs],
        "finish_down",
        limit=24,
    )[0]


def exchange(blocks):
    return lax.all_to_all(blocks.reshape(-1, blocks.shape[-1]), TP, 0, 0, tiled=True)


def on_device(
    tokens,
    first_gain,
    query_down,
    query_gain,
    query_up,
    latent_down,
    latent_gain,
    latent_up,
    out_weight,
    second_gain,
    gate_weight,
    up_weight,
    down_weight,
    cotangent,
):
    length = tokens.shape[0]
    me = lax.axis_index(TP).astype(jnp.int32).reshape(1)
    y, xl, core = lax.axis_index("y"), lax.axis_index("xl"), lax.axis_index("core")
    starts = jnp.stack(
        [
            ((y + k) % 4 * 2 + (xl ^ j)) * 2 + c
            for c in (core, 1 - core)
            for k in range(4)
            for j in range(2)
        ]
    ).astype(jnp.int32)
    tables = rope_tables(length)

    gate_turned, up_turned = gate_weight.T, up_weight.T

    (
        first_in,
        latents,
        query_code,
        latent_code,
        queries,
        keyvals,
        rope_keys,
        heads_out,
        log_total,
        attn_partial,
    ), started = attend(
        me,
        tokens,
        first_gain,
        query_down,
        latent_down,
        query_gain,
        latent_gain,
        query_up,
        latent_up,
        out_weight,
        tables,
    )
    attn_got = exchange(attn_partial)

    (cot_keep, cot_give), picked = halves(starts, [cotangent], [started])
    inner_back = dot(cotangent, down_weight, NT)
    cot_got = over_cores(cot_give)

    (residual, second_many), _ = residual_of(
        me, attn_got, tokens, second_gain, [picked, cot_got]
    )
    second_in = exchange(second_many)

    turned_in = first_in.T.reshape(16, 8, 20, length)
    own_in = lax.dynamic_slice_in_dim(turned_in, me[0], 1, 1).reshape(320, length)
    (code_keep, code_give, lat_keep, lat_give), picked = halves(
        starts, [query_code, latent_code], [residual]
    )
    code_got, lat_got = over_cores(code_give), over_cores(lat_give)
    heads_got = over_cores(heads_out)

    (gate_back, up_back, inner, back_partial), done = ffn(
        second_in, gate_turned, up_turned, inner_back, [picked, own_in, code_got, lat_got, heads_got]
    )
    back_got = exchange(back_partial)

    ours = (gate_back, up_back, inner)
    theirs = [over_cores(item) for item in ours]
    (in_keep, in_give), _ = halves(starts, [second_in], [done])
    in_got = over_cores(in_give)
    (far_up, far_down, ffn_up, ffn_down_way, ffn_own), done = ffn_grads(in_keep, in_got, cot_keep, cot_got, ours, theirs, gate_weight.shape[1], [])
    below, above = lax.ppermute(far_up, "y", UP), lax.ppermute(far_down, "y", DOWN)

    (back_many, second_gain_part), done = residual_back_of(
        me, back_got, residual, cotangent, second_gain, [done]
    )
    attention_back = exchange(back_many)
    (ffn_up, ffn_down_way), done = relay(ffn_up, below, ffn_down_way, above, [done])
    below, above = lax.ppermute(ffn_up, "y", UP), lax.ppermute(ffn_down_way, "y", DOWN)
    (ffn_partial,), done = ffn_down(inner, down_weight, [done])
    mixed_got = exchange(after(ffn_partial, attention_back, done))

    (query_raw_back, keyval_back, latents_partial), back_done = attend_back(
        attention_back,
        out_weight,
        queries,
        keyvals,
        rope_keys,
        log_total,
        query_up,
        latent_up,
        tables,
        [done],
    )
    (ffn_keep, ffn_give), done = add_chips([ffn_own, below, above], [back_done])
    ffn_got = lax.ppermute(ffn_give, "xl", SWAP)
    (out_keep, out_give), done = halves(starts, [attention_back], [done])
    out_got = over_cores(out_give)
    raw_got, kv_got = over_cores(query_raw_back), over_cores(keyval_back)
    (attn_across, attn_up, attn_down, attn_own), done = attn_grads(
        (out_keep, code_keep, lat_keep),
        (out_got, code_got, lat_got),
        (heads_out, query_raw_back, keyval_back),
        (heads_got, raw_got, kv_got),
        [done],
    )
    attn_got = [
        lax.ppermute(attn_across, "y", ACROSS),
        lax.ppermute(attn_up, "y", UP),
        lax.ppermute(attn_down, "y", DOWN),
    ]
    latents_got = exchange(after(latents_partial, mixed_got, done))

    (mixed_own,), done = mixed_of(mixed_got, residual, [done])
    mixed = lax.all_gather(mixed_own, TP, axis=0, tiled=True)

    (raw_many, own_raw, latent_gain_parts), done = latents_back_of(
        me, latents_got, latents, query_gain, latent_gain, tables, [done]
    )
    raw_back = exchange(raw_many)

    (first_gain_part,), gain_done = first_gain_of(
        me, own_raw, tokens, query_down, latent_down, [done]
    )

    gains = jnp.concatenate(
        [
            first_gain_part.reshape(16, -1),
            second_gain_part.reshape(16, -1),
            latent_gain_parts[0, :QR].reshape(16, -1),
            latent_gain_parts[0, QR:].reshape(16, -1),
        ],
        axis=1,
    ).astype(BF16)
    gains = jnp.pad(gains, ((0, 0), (0, WIDE - gains.shape[1])))
    (attn_keep, attn_give), done = add_chips([attn_own, *attn_got], [gain_done])
    attn_other = lax.ppermute(attn_give, "xl", SWAP)
    (parts,), done = down_parts(own_in, raw_back, gains, [done])
    parts_got = lax.all_to_all(parts, DP, 0, 0, tiled=True)

    (tokens_grad,), done = tokens_back_of(
        raw_back, tokens, attention_back, query_down, latent_down, first_gain, [done]
    )
    (out_weight_grad, query_up_grad, latent_up_grad), done = finish_attn(
        attn_keep, attn_other, [done]
    )
    (many,), summed = sum_copies(parts_got, [done])
    everyone = exchange(many)
    (gate_weight_grad, up_weight_grad, down_weight_grad), done = finish_ffn(
        ffn_keep, ffn_got, [summed]
    )
    (
        query_down_grad,
        latent_down_grad,
        first_gain_grad,
        second_gain_grad,
        query_gain_grad,
        latent_gain_grad,
    ) = finish_down(everyone)

    return (
        mixed,
        tokens_grad,
        first_gain_grad[0],
        query_down_grad,
        query_gain_grad[0],
        query_up_grad,
        latent_down_grad,
        latent_gain_grad[0],
        latent_up_grad,
        out_weight_grad.T,
        second_gain_grad[0],
        gate_weight_grad,
        up_weight_grad,
        down_weight_grad.T,
    )


def solution(mesh):
    grid = Mesh(mesh.devices.reshape(4, 2, 2, 2, 4), ("y", "xl", "core", "xh", "z"))
    in_specs = (
        P(DP, None),
        P(),
        P(),
        P(),
        P(None, TP),
        P(),
        P(),
        P(None, TP),
        P(TP, None),
        P(),
        P(None, TP),
        P(None, TP),
        P(TP, None),
        P(DP, None),
    )
    out_specs = (
        P(DP, None),
        P(DP, None),
        P(DP),
        P(DP, None),
        P(DP),
        P(DP, TP),
        P(DP, None),
        P(DP),
        P(DP, TP),
        P(TP, DP),
        P(DP),
        P(DP, TP),
        P(DP, TP),
        P(TP, DP),
    )
    return jax.shard_map(
        on_device, mesh=grid, in_specs=in_specs, out_specs=out_specs, check_vma=False
    )
```

```python
import functools

import jax
import jax.numpy as jnp
import numpy as np
from jax import lax
from jax.experimental import pallas as pl
from jax.experimental.pallas import tpu as pltpu
from jax.sharding import Mesh, PartitionSpec as P

NOPE = 64
ROPE = 32
DV = 64
KVR = 256
QR = 768
LAT = QR + KVR
WIDE = LAT + 128

EPS = 1e-05
BASE = 10000.0
SCALE = (NOPE + ROPE) ** (-0.5)

DP = ("y", "xl", "core")
TP = ("xh", "z")
SWAP = [(0, 1), (1, 0)]
F32 = jnp.float32
BF16 = jnp.bfloat16
NT = (((1,), (1,)), ((), ()))
TN = (((0,), (0,)), ((), ()))
NN = (((1,), (0,)), ((), ()))
TILE = 256


def dot(left, right, dims=NN):
    return lax.dot_general(left, right, dims, preferred_element_type=F32)


def params(limit=56):
    return pltpu.CompilerParams(vmem_limit_bytes=limit * 2**20)


HBM = pl.BlockSpec(memory_space=pltpu.HBM)


def call(kernel, args, in_specs, out_specs, out_shape, name, grid=(1,), scratch=(), needs=(), me=None, limit=60):
    first = 0 if me is None else 1
    n_in, n_out = len(args), len(out_shape)

    def body(*refs):
        ins = refs[: first + n_in]
        rest = refs[first + n_in + len(needs) :]
        mark = rest[n_out]

        @pl.when(pl.program_id(0) == 0)
        def _():
            mark[...] = jnp.zeros_like(mark)

        kernel(*ins, *rest[:n_out], *rest[n_out + 1 :])

    *outs, mark = pl.pallas_call(
        body,
        grid_spec=pltpu.PrefetchScalarGridSpec(
            num_scalar_prefetch=first,
            grid=grid,
            in_specs=list(in_specs) + [HBM] * len(needs),
            out_specs=list(out_specs) + [full((8, 128))],
            scratch_shapes=list(scratch),
        ),
        out_shape=list(out_shape) + [jax.ShapeDtypeStruct((8, 128), F32)],
        compiler_params=params(limit),
        cost_estimate=pl.CostEstimate(flops=1, bytes_accessed=1, transcendentals=0),
        name=name,
    )(*(() if me is None else (me,)), *args, *needs)
    return outs, mark


def shaped(*shape, dtype=BF16):
    return jax.ShapeDtypeStruct(shape, dtype)


def full(shape):
    return pl.BlockSpec(shape, lambda *_: (0,) * len(shape))


def rope_tables(length):
    half = ROPE // 2
    rates = np.exp(np.arange(half, dtype=np.float32) * np.float32(-2.0 * np.log(BASE) / ROPE))
    angles = np.arange(length, dtype=np.float32)[:, None] * rates.astype(np.float32)[None, :]
    cosine, sine = np.cos(angles), np.sin(angles)
    keep = np.zeros((length, 128), np.float32)
    keep[:, :NOPE] = 1.0
    keep[:, 64:80] = cosine
    keep[:, 80:96] = cosine
    low = np.zeros((length, 128), np.float32)
    low[:, 64:80] = -sine
    high = np.zeros((length, 128), np.float32)
    high[:, 80:96] = sine
    return jnp.asarray(keep), jnp.asarray(low), jnp.asarray(high)


def turn(values, keep, low, high, back=False):
    moved = pltpu.roll(values, 112, 1) * low + pltpu.roll(values, 16, 1) * high
    return values * keep - moved if back else values * keep + moved


def root(values):
    return lax.rsqrt(jnp.mean(values * values, axis=-1, keepdims=True) + EPS)


def norm_back(upstream, normed, factor, gain):
    scaled = upstream * gain
    return factor * (scaled - normed * jnp.mean(scaled * normed, axis=-1, keepdims=True))


def spread_out_weight(weight_ref, spread_ref, heads):
    spread_ref[...] = jnp.zeros_like(spread_ref)
    for h in range(heads):
        spread_ref[128 * h + 64 : 128 * h + 128, :] = weight_ref[64 * h : 64 * h + 64, :]


def spread_query_up(weight_ref, spread_ref, heads):
    spread_ref[...] = jnp.zeros_like(spread_ref)
    for h in range(heads):
        spread_ref[128 * h : 128 * h + 96, :] = weight_ref[96 * h : 96 * h + 96, :]


def row(ref):
    return ref[...].reshape(1, -1)


def low_lanes(shape):
    return lax.broadcasted_iota(jnp.int32, shape, 1) < NOPE


def causal(keys, queries, first_query):
    key_ids = lax.broadcasted_iota(jnp.int32, (keys, queries), 0)
    query_ids = lax.broadcasted_iota(jnp.int32, (keys, queries), 1) + first_query
    return key_ids <= query_ids


def attend_kernel(
    heads,
    me,
    tokens,
    first_gain,
    query_down,
    latent_down,
    query_gain,
    latent_gain,
    query_up,
    latent_up,
    out_weight,
    keep,
    low,
    high,
    first_in,
    latents,
    query_code,
    latent_code,
    queries,
    keyvals,
    rope_keys,
    heads_out,
    log_total,
    partial,
    raw_latents,
    spread,
    spread_up,
    rope_down,
    kv_all,
    rope_all,
):
    step = pl.program_id(0)

    @pl.when(step == 0)
    def _():
        spread_out_weight(out_weight, spread, heads)
        spread_query_up(query_up, spread_up, heads)
        rope_down[...] = jnp.zeros_like(rope_down)
        rope_down[64:96, :] = latent_down[KVR:, :]

    def rows_of(index, carry):
        rows = pl.ds(pl.multiple_of(index * 32, 32), 32)
        values = tokens[rows, :].astype(F32)
        first_in[rows, :] = (values * root(values) * row(first_gain)).astype(BF16)
        return carry

    lax.fori_loop(0, TILE // 32, rows_of, 0)
    taken = first_in[...]
    query_latent = dot(taken, query_down[...])
    raw_latents[:, :QR] = query_latent
    code = (query_latent * root(query_latent) * row(query_gain)).astype(BF16)
    query_code[...] = code
    latent = dot(taken, latent_down[:KVR, :], NT)
    raw_latents[:, QR:] = latent
    count = latents.shape[0]
    own = me[0] * count

    @pl.when(own // TILE == step)
    def _():
        latents[...] = raw_latents[pl.ds(pl.multiple_of(own % TILE, count), count), :]

    lcode = (latent * root(latent) * row(latent_gain)).astype(BF16)
    latent_code[...] = lcode
    tables = keep[...], low[...], high[...]
    rope = turn(dot(taken, rope_down[...], NT), *tables).astype(BF16)
    rope_keys[...] = rope
    here = pl.ds(pl.multiple_of(step * TILE, TILE), TILE)
    rope_all[here, :] = rope
    kv = dot(lcode, latent_up[...]).astype(BF16)
    keyvals[...] = kv
    kv_all[here, :] = kv
    raw = dot(code, spread_up[...], NT)
    for h in range(heads):
        lanes = slice(128 * h, 128 * h + 128)
        queries[:, lanes] = turn(raw[:, lanes], *tables).astype(BF16)

    def tile(index):
        keys = TILE * (index + 1)
        for h in range(heads):
            lanes = slice(128 * h, 128 * h + 128)
            kv_h = kv_all[:keys, lanes]
            key = jnp.where(low_lanes((keys, 128)), kv_h, rope_all[:keys, :])
            scores = dot(key, queries[:, lanes], NT) * SCALE
            scores = jnp.where(causal(keys, TILE, TILE * index), scores, -1e30)
            top = jnp.max(scores, axis=0, keepdims=True)
            weights = jnp.exp(scores - top)
            total = jnp.sum(weights, axis=0, keepdims=True)
            log_total[h : h + 1, :] = top + jnp.log(total)
            probs = (weights * (1.0 / total)).astype(BF16)
            heads_out[:, lanes] = dot(probs, kv_h, TN).astype(BF16)

    for index in range(2):
        pl.when(step == index)(functools.partial(tile, index))
    partial[...] = dot(heads_out[...], spread[...]).astype(BF16)


def attend(me, tokens, first_gain, query_down, latent_down, query_gain, latent_gain, query_up, latent_up, out_weight, tables):
    latent_down, query_up = latent_down.T, query_up.T
    length, width = tokens.shape
    heads = out_weight.shape[0] // DV
    wide = 128 * heads

    def rows(columns):
        return pl.BlockSpec((TILE, columns), lambda i, *_: (i, 0))

    return call(
        functools.partial(attend_kernel, heads),
        (tokens, first_gain, query_down, latent_down, query_gain, latent_gain, query_up, latent_up, out_weight, *tables),
        [
            rows(width),
            full((width,)),
            full(query_down.shape),
            full(latent_down.shape),
            full((QR,)),
            full((KVR,)),
            full(query_up.shape),
            full(latent_up.shape),
            full(out_weight.shape),
            rows(128),
            rows(128),
            rows(128),
        ],
        [
            rows(width),
            full((length // 8, LAT)),
            rows(QR),
            rows(KVR),
            rows(wide),
            rows(wide),
            rows(128),
            rows(wide),
            pl.BlockSpec((8, TILE), lambda i, *_: (0, i)),
            rows(width),
        ],
        [
            shaped(length, width),
            shaped(length // 8, LAT, dtype=F32),
            shaped(length, QR),
            shaped(length, KVR),
            shaped(length, wide),
            shaped(length, wide),
            shaped(length, 128),
            shaped(length, wide),
            shaped(8, length, dtype=F32),
            shaped(length, width),
        ],
        "attend",
        grid=(length // TILE,),
        me=me,
        scratch=[
            pltpu.VMEM((TILE, LAT), F32),
            pltpu.VMEM((wide, width), BF16),
            pltpu.VMEM((wide, QR), BF16),
            pltpu.VMEM((128, width), BF16),
            pltpu.VMEM((length, wide), BF16),
            pltpu.VMEM((length, 128), BF16),
        ],
    )


def attend_back_kernel(
    heads,
    attention_back,
    out_weight,
    queries,
    keyvals,
    rope_keys,
    log_total,
    query_up,
    latent_up,
    keep,
    low,
    high,
    query_back,
    keyval_back,
    partial,
    spread,
    spread_up,
    kv_grad,
    rope_grad,
    code_grad,
):
    step = pl.program_id(0)

    @pl.when(step == 0)
    def _():
        spread_out_weight(out_weight, spread, heads)
        spread_query_up(query_up, spread_up, heads)
        kv_grad[...] = jnp.zeros_like(kv_grad)
        rope_grad[...] = jnp.zeros_like(rope_grad)

    heads_back = dot(attention_back[...], spread[...], NT).astype(BF16)
    tables = keep[...], low[...], high[...]

    def tile(index):
        keys = TILE * (index + 1)
        low_part = low_lanes((keys, 128))
        for h in range(heads):
            lanes = slice(128 * h, 128 * h + 128)
            kv_h = keyvals[:keys, lanes]
            key = jnp.where(low_part, kv_h, rope_keys[:keys, :])
            query = queries[:, lanes]
            back = heads_back[:, lanes]
            scores = dot(key, query, NT) * SCALE
            probs = jnp.exp(scores - log_total[h : h + 1, :])
            probs = jnp.where(causal(keys, TILE, TILE * index), probs, 0.0)
            prob_back = dot(kv_h, back, NT)
            mean = jnp.sum(probs * prob_back, axis=0, keepdims=True)
            score_back = (probs * (prob_back - mean)).astype(BF16)
            of_values = dot(probs.astype(BF16), back)
            of_keys = dot(score_back, query) * SCALE
            kv_grad[:keys, lanes] += of_values + jnp.where(low_part, of_keys, 0.0)
            rope_grad[:keys, :] += jnp.where(low_part, 0.0, of_keys)
            of_query = dot(score_back, key, TN) * SCALE
            query_back[:, lanes] = turn(of_query, *tables, back=True).astype(BF16)

    for index in range(2):
        pl.when(step == index)(functools.partial(tile, index))
    here = pl.ds(pl.multiple_of(step * TILE, TILE), TILE)
    code_grad[here, :] = dot(query_back[...], spread_up[...]).astype(BF16)

    @pl.when(step == 1)
    def _():
        kv = kv_grad[...].astype(BF16)
        keyval_back[...] = kv
        partial[:, :QR] = code_grad[...]
        partial[:, QR:LAT] = dot(kv, latent_up[...], NT).astype(BF16)
        partial[:, LAT:] = rope_grad[...].astype(BF16)


def attend_back(attention_back, out_weight, queries, keyvals, rope_keys, log_total, query_up, latent_up, tables, needs):
    query_up = query_up.T
    length, width = attention_back.shape
    heads = out_weight.shape[0] // DV
    wide = 128 * heads

    def rows(columns):
        return pl.BlockSpec((TILE, columns), lambda i, *_: (i, 0))

    return call(
        functools.partial(attend_back_kernel, heads),
        (attention_back, out_weight, queries, keyvals, rope_keys, log_total, query_up, latent_up, *tables),
        [
            rows(width),
            full(out_weight.shape),
            rows(wide),
            full((length, wide)),
            full((length, 128)),
            pl.BlockSpec((8, TILE), lambda i, *_: (0, i)),
            full(query_up.shape),
            full(latent_up.shape),
            rows(128),
            rows(128),
            rows(128),
        ],
        [rows(wide), full((length, wide)), full((length, WIDE))],
        [shaped(length, wide), shaped(length, wide), shaped(length, WIDE)],
        "attend_back",
        grid=(length // TILE,),
        scratch=[
            pltpu.VMEM((wide, width), BF16),
            pltpu.VMEM((wide, QR), BF16),
            pltpu.VMEM((length, wide), F32),
            pltpu.VMEM((length, 128), F32),
            pltpu.VMEM((length, QR), BF16),
        ],
        needs=needs,
    )


def add_up(got):
    total = got[0].astype(F32)
    for k in range(1, 8):
        total = total + got[k].astype(F32)
    return total


STEPS = 2


def residual_kernel(me, got, tokens, gain, residual, many):
    del me
    total = tokens[...].astype(F32) + add_up(got)
    residual[...] = total
    second_in = (total * root(total) * row(gain)).astype(BF16)
    for k in range(8):
        many[k] = second_in


def own_specs(rows, width):
    step = rows // STEPS
    return (
        pl.BlockSpec((8, step, width), lambda i, me: (0, i, 0)),
        pl.BlockSpec((step, width), lambda i, me: (i, 0)),
        pl.BlockSpec((step, width), lambda i, me: (me[0] * STEPS + i, 0)),
    )


def residual_of(me, got, tokens, gain, needs):
    width = tokens.shape[1]
    rows = tokens.shape[0] // 8
    eight, one, own = own_specs(rows, width)
    return call(
        residual_kernel,
        (got.reshape(8, rows, width), tokens, gain),
        [eight, own, full((width,))],
        [one, eight],
        [shaped(rows, width, dtype=F32), shaped(8, rows, width)],
        "residual",
        grid=(STEPS,),
        needs=needs,
        me=me,
        limit=58,
    )


def residual_back_kernel(me, got, residual, cotangent, gain, many, gain_part):
    del me
    second_back = add_up(got)
    values = residual[...]
    factor = root(values)
    normed = values * factor
    part = jnp.sum(second_back * normed, axis=0, keepdims=True)

    @pl.when(pl.program_id(0) == 0)
    def _():
        gain_part[...] = part

    @pl.when(pl.program_id(0) > 0)
    def _():
        gain_part[...] += part

    back = cotangent[...].astype(F32) + norm_back(second_back, normed, factor, row(gain))
    back = back.astype(BF16)
    for k in range(8):
        many[k] = back


def residual_back_of(me, got, residual, cotangent, gain, needs):
    rows, width = residual.shape
    eight, one, own = own_specs(rows, width)
    return call(
        residual_back_kernel,
        (got.reshape(8, rows, width), residual, cotangent, gain),
        [eight, one, own, full((width,))],
        [eight, full((1, width))],
        [shaped(8, rows, width), shaped(1, width, dtype=F32)],
        "residual_back",
        grid=(STEPS,),
        needs=needs,
        me=me,
        limit=58,
    )


def ffn_kernel(
    second_in, gate_weight, up_weight, inner_back, gate_back, up_back, inner, partial
):
    taken = second_in[...]
    gate = dot(taken, gate_weight[...], NT)
    up = dot(taken, up_weight[...], NT)
    sigma = 1.0 / (1.0 + jnp.exp(-gate))
    act = gate * sigma
    units = gate.shape[1]
    back = inner_back[...]
    of_gate = (back * up * sigma * (1.0 + gate * (1.0 - sigma))).astype(BF16)
    of_up = (back * act).astype(BF16)
    for out, values in ((gate_back, of_gate), (up_back, of_up), (inner, (act * up).astype(BF16))):
        out[:, :units] = values
        out[:, units:] = jnp.zeros((values.shape[0], out.shape[1] - units), BF16)
    partial[...] = (dot(of_gate, gate_weight[...]) + dot(of_up, up_weight[...])).astype(BF16)


def ffn(second_in, gate_weight, up_weight, inner_back, needs):
    length, width = second_in.shape
    units = gate_weight.shape[0]
    wide = -(-units // 128) * 128

    def rows(columns):
        return pl.BlockSpec((TILE, columns), lambda i, *_: (i, 0))

    return call(
        ffn_kernel,
        (second_in, gate_weight, up_weight, inner_back),
        [rows(width), full((units, width)), full((units, width)), rows(units)],
        [rows(wide), rows(wide), rows(wide), rows(width)],
        [shaped(length, wide)] * 3 + [shaped(length, width)],
        "ffn",
        grid=(length // TILE,),
        needs=needs,
    )


def ffn_down_kernel(me, inner, down_weight, residual, out):
    for i in range(2):
        rows = slice(i * TILE, i * TILE + TILE)
        out[rows, :] = dot(inner[rows, : down_weight.shape[0]], down_weight[...]).astype(BF16)
    count = residual.shape[0]
    own = pl.ds(pl.multiple_of(me[0] * count, count), count)
    out[own, :] = (out[own, :].astype(F32) + residual[...]).astype(BF16)


def ffn_down(me, inner, down_weight, residual, needs):
    length, width = inner.shape[0], down_weight.shape[1]
    return call(
        ffn_down_kernel,
        (inner, down_weight, residual),
        [full(inner.shape), full(down_weight.shape), full(residual.shape)],
        [full((length, width))],
        [shaped(length, width)],
        "ffn_down",
        needs=needs,
        me=me,
    )


def halves_kernel(blocks, width, starts, *refs):
    sources, outs, turned = refs[:blocks], refs[blocks : 3 * blocks], refs[3 * blocks]
    for n in range(blocks):
        source, keep, give = sources[n], outs[2 * n], outs[2 * n + 1]
        columns, each = source.shape[1], width[n]
        for c in range(0, columns, 256):
            turned[c : c + 256, :] = source[:, c : c + 256].T
        for which, out in enumerate((keep, give)):
            for k in range(8):
                first = pl.multiple_of(starts[8 * which + k] * each, 16)
                out[each * k : each * k + each, :] = turned[pl.ds(first, each), :]


def halves(starts, values, needs):
    length = values[0].shape[0]
    widths = [item.shape[1] // 16 for item in values]
    shapes = [(8 * w, length) for w in widths for _ in range(2)]
    return call(
        functools.partial(halves_kernel, len(values), widths),
        tuple(values),
        [full(item.shape) for item in values],
        [full(s) for s in shapes],
        [shaped(*s) for s in shapes],
        "halves",
        scratch=[pltpu.VMEM((max(item.shape[1] for item in values), length), BF16)],
        needs=needs,
        me=starts,
    )


ORDER = (2, 1, 3, 0)


def ffn_grads_kernel(in_keep, in_got, cot_keep, cot_got, *refs):
    ours, theirs, outs = refs[:3], refs[3:6], refs[6:]
    units = outs[0].shape[1] // 3

    def block(*parts):
        for n, (keep, got) in enumerate(((in_keep, in_got), (in_keep, in_got), (cot_keep, cot_got))):
            total = dot(keep[...], ours[n][...]) + dot(got[...], theirs[n][...])
            total = total[:, :units].astype(BF16)
            first = 0
            for out in parts:
                count = out.shape[0]
                out[:, units * n : units * n + units] = total[first : first + count]
                first += count

    for s, parts in enumerate((outs[:2], outs[2:3], outs[3:4], outs[4:])):
        pl.when(pl.program_id(0) == s)(functools.partial(block, *parts))


def ffn_grads(in_keep, in_got, cot_keep, cot_got, ours, theirs, units, needs):
    length, wide = ours[0].shape
    rows = in_keep.shape[0] // 4

    def index(i):
        return (jnp.where(i == 0, 2, jnp.where(i == 1, 1, jnp.where(i == 2, 3, 0))), 0)

    left = pl.BlockSpec((rows, length), index)
    out = (rows, 3 * units)
    outs = [(rows // 2, 3 * units)] * 2 + [out] * 3
    return call(
        ffn_grads_kernel,
        (in_keep, in_got, cot_keep, cot_got, *ours, *theirs),
        [left] * 4 + [full((length, wide))] * 6,
        [full(s) for s in outs],
        [shaped(*s) for s in outs],
        "ffn_grads",
        grid=(4,),
        needs=needs,
    )


def attn_grads_kernel(widths, *refs):
    keeps, gots, ours, theirs, outs = refs[:3], refs[3:6], refs[6:9], refs[9:12], refs[12:]
    rows = sum(widths)
    for out, k in zip(outs, ORDER):
        first = 0
        for n, each in enumerate(widths):
            part = slice(2 * each * k, 2 * each * k + 2 * each)
            total = dot(keeps[n][part, :], ours[n][...]) + dot(gots[n][part, :], theirs[n][...])
            total = total.astype(BF16)
            out[first : first + each, :] = total[:each]
            out[rows + first : rows + first + each, :] = total[each:]
            first += each


def attn_grads(keeps, gots, ours, theirs, needs):
    widths = [item.shape[0] // 8 for item in keeps]
    rows, wide = sum(widths), ours[0].shape[1]
    args = (*keeps, *gots, *ours, *theirs)
    outs = [(2 * rows, wide)] * 4
    return call(
        functools.partial(attn_grads_kernel, widths),
        args,
        [full(item.shape) for item in args],
        [full(s) for s in outs],
        [shaped(*s) for s in outs],
        "attn_grads",
        needs=needs,
    )


UP = [(i, (i + 1) % 4) for i in range(4)]
DOWN = [(i, (i + 3) % 4) for i in range(4)]
ACROSS = [(i, (i + 2) % 4) for i in range(4)]


def relay_kernel(up, from_below, down, from_above, up_out, down_out):
    @pl.when(pl.program_id(0) == 0)
    def _():
        up_out[...] = (up[...].astype(F32) + from_below[...].astype(F32)).astype(BF16)
        down_out[...] = down[...]

    @pl.when(pl.program_id(0) == 1)
    def _():
        up_out[...] = up[...]
        down_out[...] = (down[...].astype(F32) + from_above[...].astype(F32)).astype(BF16)


def relay(up, from_below, down, from_above, needs):
    rows, width = from_below.shape
    half = pl.BlockSpec((rows, width), lambda i, *_: (i, 0))
    return call(
        relay_kernel,
        (up, from_below, down, from_above),
        [half, full((rows, width)), half, full((rows, width))],
        [half, half],
        [shaped(2 * rows, width)] * 2,
        "relay",
        grid=(2,),
        needs=needs,
    )


def add_chips_kernel(*refs):
    ins, keep, give = refs[:-2], refs[-2], refs[-1]
    count = len(ins) // 2
    keep[...] = sum(item[...].astype(F32) for item in ins[:count])
    give[...] = sum(item[...].astype(F32) for item in ins[count:]).astype(BF16)


def add_chips(items, needs):
    rows, width = items[0].shape[0] // 2, items[0].shape[1]
    step = rows // 2 if rows % 32 == 0 and (rows // 2) % 16 == 0 else rows
    count = rows // step
    mine = pl.BlockSpec((step, width), lambda i, *_: (i, 0))
    other = pl.BlockSpec((step, width), lambda i, *_: (i + count, 0))
    return call(
        add_chips_kernel,
        (*items, *items),
        [mine] * len(items) + [other] * len(items),
        [mine, mine],
        [shaped(rows, width, dtype=F32), shaped(rows, width)],
        "add_chips",
        grid=(count,),
        needs=needs,
    )


def over_cores(values):
    return lax.ppermute(values, "core", SWAP)


def latents_back_kernel(
    me, got, latents, query_gain, latent_gain, keep, low, high, many, own, gain_part, turns, sems
):
    rows = own.shape[0]
    here = pl.ds(pl.multiple_of(me[0] * rows, rows), rows)
    copies = [
        pltpu.make_async_copy(table.at[here, :], turns.at[n], sems.at[n])
        for n, table in enumerate((keep, low, high))
    ]
    for copy in copies:
        copy.start()
    total = add_up(got)
    for copy in copies:
        copy.wait()

    def back(lanes, gain):
        upstream, values = total[:, lanes], latents[:, lanes]
        factor = root(values)
        normed = values * factor
        gain_part[:, lanes] = jnp.sum(upstream * normed, axis=0, keepdims=True)
        return norm_back(upstream, normed, factor, row(gain)).astype(BF16)

    own[:, :QR] = back(slice(0, QR), query_gain)
    own[:, QR:LAT] = back(slice(QR, LAT), latent_gain)
    own[:, LAT:] = turn(total[:, LAT:], turns[0], turns[1], turns[2], back=True).astype(BF16)
    for k in range(8):
        many[k] = own[...]


def latents_back_of(me, got, latents, query_gain, latent_gain, tables, needs):
    rows = latents.shape[0]
    return call(
        latents_back_kernel,
        (got.reshape(8, rows, WIDE), latents, query_gain, latent_gain, *tables),
        [full((8, rows, WIDE)), full(latents.shape), full((QR,)), full((KVR,)), HBM, HBM, HBM],
        [full((8, rows, WIDE)), full((rows, WIDE)), full((1, LAT))],
        [shaped(8, rows, WIDE), shaped(rows, WIDE), shaped(1, LAT, dtype=F32)],
        "latents_back",
        scratch=[
            pltpu.VMEM((3, rows, 128), F32),
            pltpu.SemaphoreType.DMA((3,)),
        ],
        needs=needs,
        me=me,
        limit=24,
    )


def first_back_of(raw_back, query_down, latent_down, rope_down):
    rope_down[...] = jnp.zeros_like(rope_down)
    rope_down[64:96, :] = latent_down[KVR:, :]
    return (
        dot(raw_back[:, :QR], query_down[...], NT)
        + dot(raw_back[:, QR:LAT], latent_down[:KVR, :])
        + dot(raw_back[:, LAT:], rope_down[...])
    )


def first_gain_kernel(
    me, raw_back, tokens, query_down, latent_down, gain_part, rope_down, own, sem
):
    rows = own.shape[0]
    here = pl.ds(pl.multiple_of(me[0] * rows, rows), rows)
    copy = pltpu.make_async_copy(tokens.at[here, :], own, sem)
    copy.start()
    first_back = first_back_of(raw_back, query_down, latent_down, rope_down)
    copy.wait()
    values = own[...].astype(F32)
    gain_part[...] = jnp.sum(first_back * (values * root(values)), axis=0, keepdims=True)


def first_gain_of(me, own_raw_back, tokens, query_down, latent_down, needs):
    width = tokens.shape[1]
    return call(
        first_gain_kernel,
        (own_raw_back, tokens, query_down, latent_down.T),
        [full(own_raw_back.shape), HBM, full(query_down.shape), full(latent_down.shape[::-1])],
        [full((1, width))],
        [shaped(1, width, dtype=F32)],
        "first_gain",
        scratch=[
            pltpu.VMEM((128, width), BF16),
            pltpu.VMEM((own_raw_back.shape[0], width), BF16),
            pltpu.SemaphoreType.DMA,
        ],
        needs=needs,
        me=me,
    )


def tokens_back_kernel(
    raw_back, tokens, attention_back, query_down, latent_down, gain, tokens_grad, rope_down
):
    first_back = first_back_of(raw_back, query_down, latent_down, rope_down)
    values = tokens[...].astype(F32)
    factor = root(values)
    tokens_grad[...] = attention_back[...].astype(F32) + norm_back(
        first_back, values * factor, factor, row(gain)
    )


def tokens_back_of(raw_back, tokens, attention_back, query_down, latent_down, gain, needs):
    length, width = tokens.shape

    def rows(columns):
        return pl.BlockSpec((TILE, columns), lambda i, *_: (i, 0))

    return call(
        tokens_back_kernel,
        (raw_back, tokens, attention_back, query_down, latent_down.T, gain),
        [
            rows(WIDE),
            rows(width),
            rows(width),
            full(query_down.shape),
            full(latent_down.shape[::-1]),
            full((width,)),
        ],
        [rows(width)],
        [shaped(length, width, dtype=F32)],
        "tokens_back",
        grid=(length // TILE,),
        scratch=[pltpu.VMEM((128, width), BF16)],
        needs=needs,
    )


def finish_ffn_kernel(keep, got, gate, up, down):
    units = gate.shape[1]
    for n, out in enumerate((gate, up, down)):
        lanes = slice(units * n, units * n + units)
        out[...] = keep[:, lanes] + got[:, lanes].astype(F32)


def finish_ffn(keep, got, needs):
    rows, width = keep.shape
    out = (rows, width // 3)
    return call(
        finish_ffn_kernel,
        (keep, got),
        [full(keep.shape), full(got.shape)],
        [full(out)] * 3,
        [shaped(*out, dtype=F32)] * 3,
        "finish_ffn",
        needs=needs,
    )


def finish_attn_kernel(heads, keep, got, out_grad, query_grad, latent_grad):
    total = keep[...] + got[...].astype(F32)
    for h in range(heads):
        lanes = slice(128 * h, 128 * h + 128)
        out_grad[:, 64 * h : 64 * h + 64] = total[:160, 128 * h + 64 : 128 * h + 128]
        query_grad[:, 96 * h : 96 * h + 96] = total[160:208, 128 * h : 128 * h + 96]
    latent_grad[...] = total[208:224]


def finish_attn(keep, got, needs):
    heads = keep.shape[1] // 128
    outs = [(160, 64 * heads), (48, 96 * heads), (16, 128 * heads)]
    return call(
        functools.partial(finish_attn_kernel, heads),
        (keep, got),
        [full(keep.shape), full(got.shape)],
        [full(s) for s in outs],
        [shaped(*s, dtype=F32) for s in outs],
        "finish_attn",
        needs=needs,
    )


GAINS = ((0, 160), (160, 160), (320, 48), (368, 16))


def down_parts_kernel(own_in, raw_back, gains, out):
    total = dot(own_in[...], raw_back[...]).astype(BF16)
    for d in range(16):
        out[d, :20, :] = total[20 * d : 20 * d + 20]
        out[d, 20:, :] = jnp.zeros((4, WIDE), BF16)
        out[d, 20:21, :] = gains[d : d + 1, :]


def down_parts(own_in, raw_back, gains, needs):
    args = (own_in, raw_back, gains)
    return call(
        down_parts_kernel,
        args,
        [full(item.shape) for item in args],
        [full((16, 24, WIDE))],
        [shaped(16, 24, WIDE)],
        "down_parts",
        needs=needs,
        limit=24,
    )


def sum_copies_kernel(got, many):
    total = got[0].astype(F32)
    for d in range(1, 16):
        total = total + got[d].astype(F32)
    for k in range(8):
        many[k] = total.astype(BF16)


def sum_copies(got, needs):
    return call(
        sum_copies_kernel,
        (got,),
        [full(got.shape)],
        [full((8, 24, WIDE))],
        [shaped(8, 24, WIDE)],
        "sum_copies",
        needs=needs,
        limit=24,
    )


def finish_down_kernel(everyone, query_grad, latent_grad, *gains):
    for t in range(8):
        values = everyone[t].astype(F32)
        query_grad[20 * t : 20 * t + 20, :] = values[:20, :QR]
        latent_grad[20 * t : 20 * t + 20, :KVR] = values[:20, QR:LAT]
        latent_grad[20 * t : 20 * t + 20, KVR:] = values[:20, LAT + 64 : LAT + 96]
    total = sum(everyone[t, 16:24, :].astype(F32) for t in range(8))[4:5, :]
    for out, (first, count) in zip(gains, GAINS):
        out[...] = total[:, first : first + count]


def finish_down(everyone):
    everyone = everyone.reshape(8, 24, WIDE)
    outs = [(160, QR), (160, KVR + ROPE)] + [(1, count) for _, count in GAINS]
    return call(
        finish_down_kernel,
        (everyone,),
        [full(everyone.shape)],
        [full(s) for s in outs],
        [shaped(*s, dtype=F32) for s in outs],
        "finish_down",
        limit=24,
    )[0]


def exchange(blocks):
    return lax.all_to_all(blocks.reshape(-1, blocks.shape[-1]), TP, 0, 0, tiled=True)


def on_device(
    tokens,
    first_gain,
    query_down,
    query_gain,
    query_up,
    latent_down,
    latent_gain,
    latent_up,
    out_weight,
    second_gain,
    gate_weight,
    up_weight,
    down_weight,
    cotangent,
):
    length = tokens.shape[0]
    me = lax.axis_index(TP).astype(jnp.int32).reshape(1)
    y, xl, core = lax.axis_index("y"), lax.axis_index("xl"), lax.axis_index("core")
    starts = jnp.stack(
        [
            ((y + k) % 4 * 2 + (xl ^ j)) * 2 + c
            for c in (core, 1 - core)
            for k in range(4)
            for j in range(2)
        ]
    ).astype(jnp.int32)
    tables = rope_tables(length)

    gate_turned, up_turned = gate_weight.T, up_weight.T

    (
        first_in,
        latents,
        query_code,
        latent_code,
        queries,
        keyvals,
        rope_keys,
        heads_out,
        log_total,
        attn_partial,
    ), started = attend(
        me,
        tokens,
        first_gain,
        query_down,
        latent_down,
        query_gain,
        latent_gain,
        query_up,
        latent_up,
        out_weight,
        tables,
    )
    attn_got = exchange(attn_partial)

    (cot_keep, cot_give), picked = halves(starts, [cotangent], [started])
    inner_back = dot(cotangent, down_weight, NT)
    cot_got = over_cores(cot_give)

    (residual, second_many), _ = residual_of(
        me, attn_got, tokens, second_gain, [picked, cot_got]
    )
    second_in = exchange(second_many)

    turned_in = first_in.T.reshape(16, 8, 20, length)
    own_in = lax.dynamic_slice_in_dim(turned_in, me[0], 1, 1).reshape(320, length)
    (code_keep, code_give, lat_keep, lat_give), picked = halves(
        starts, [query_code, latent_code], [residual]
    )
    code_got, lat_got = over_cores(code_give), over_cores(lat_give)
    heads_got = over_cores(heads_out)

    (gate_back, up_back, inner, back_partial), done = ffn(
        second_in, gate_turned, up_turned, inner_back, [picked, own_in, code_got, lat_got, heads_got]
    )
    back_got = exchange(back_partial)

    ours = (gate_back, up_back, inner)
    theirs = [over_cores(item) for item in ours]
    (in_keep, in_give), _ = halves(starts, [second_in], [done])
    in_got = over_cores(in_give)
    (far_up, far_down, ffn_up, ffn_down_way, ffn_own), done = ffn_grads(in_keep, in_got, cot_keep, cot_got, ours, theirs, gate_weight.shape[1], [])
    below, above = lax.ppermute(far_up, "y", UP), lax.ppermute(far_down, "y", DOWN)

    (back_many, second_gain_part), done = residual_back_of(
        me, back_got, residual, cotangent, second_gain, [done]
    )
    attention_back = exchange(back_many)
    (ffn_partial,), done = ffn_down(me, inner, down_weight, residual, [done])
    mixed = lax.psum(ffn_partial, TP)
    (ffn_up, ffn_down_way), done = relay(ffn_up, below, ffn_down_way, above, [done])
    below, above = lax.ppermute(ffn_up, "y", UP), lax.ppermute(ffn_down_way, "y", DOWN)

    (query_raw_back, keyval_back, latents_partial), back_done = attend_back(
        attention_back,
        out_weight,
        queries,
        keyvals,
        rope_keys,
        log_total,
        query_up,
        latent_up,
        tables,
        [done],
    )
    latents_got = exchange(latents_partial)

    (out_keep, out_give), picked = halves(starts, [attention_back], [back_done])
    (ffn_keep, ffn_give), done = add_chips([ffn_own, below, above], [back_done])
    ffn_got = lax.ppermute(ffn_give, "xl", SWAP)

    (raw_many, own_raw, latent_gain_parts), done = latents_back_of(
        me, latents_got, latents, query_gain, latent_gain, tables, [done, picked]
    )
    raw_back = exchange(raw_many)

    out_got = over_cores(out_give)
    raw_got, kv_got = over_cores(query_raw_back), over_cores(keyval_back)
    (attn_across, attn_up, attn_down, attn_own), done = attn_grads(
        (out_keep, code_keep, lat_keep),
        (out_got, code_got, lat_got),
        (heads_out, query_raw_back, keyval_back),
        (heads_got, raw_got, kv_got),
        [done],
    )
    attn_got = [
        lax.ppermute(attn_across, "y", ACROSS),
        lax.ppermute(attn_up, "y", UP),
        lax.ppermute(attn_down, "y", DOWN),
    ]
    (first_gain_part,), gain_done = first_gain_of(
        me, own_raw, tokens, query_down, latent_down, [done]
    )

    gains = jnp.concatenate(
        [
            first_gain_part.reshape(16, -1),
            second_gain_part.reshape(16, -1),
            latent_gain_parts[0, :QR].reshape(16, -1),
            latent_gain_parts[0, QR:].reshape(16, -1),
        ],
        axis=1,
    ).astype(BF16)
    gains = jnp.pad(gains, ((0, 0), (0, WIDE - gains.shape[1])))
    (parts,), done = down_parts(own_in, raw_back, gains, [attn_got[1], attn_got[2]])
    parts_got = lax.all_to_all(parts, DP, 0, 0, tiled=True)

    (tokens_grad,), done = tokens_back_of(
        raw_back, tokens, attention_back, query_down, latent_down, first_gain, [done]
    )
    (many,), summed = sum_copies(parts_got, [done])
    everyone = exchange(many)

    (attn_keep, attn_give), done = add_chips([attn_own, *attn_got], [summed])
    attn_other = lax.ppermute(attn_give, "xl", SWAP)
    (gate_weight_grad, up_weight_grad, down_weight_grad), done = finish_ffn(
        ffn_keep, ffn_got, [done]
    )
    (out_weight_grad, query_up_grad, latent_up_grad), done = finish_attn(
        attn_keep, attn_other, [done]
    )
    (
        query_down_grad,
        latent_down_grad,
        first_gain_grad,
        second_gain_grad,
        query_gain_grad,
        latent_gain_grad,
    ) = finish_down(everyone)

    return (
        mixed,
        tokens_grad,
        first_gain_grad[0],
        query_down_grad,
        query_gain_grad[0],
        query_up_grad,
        latent_down_grad,
        latent_gain_grad[0],
        latent_up_grad,
        out_weight_grad.T,
        second_gain_grad[0],
        gate_weight_grad,
        up_weight_grad,
        down_weight_grad.T,
    )


def solution(mesh):
    grid = Mesh(mesh.devices.reshape(4, 2, 2, 2, 4), ("y", "xl", "core", "xh", "z"))
    in_specs = (
        P(DP, None),
        P(),
        P(),
        P(),
        P(None, TP),
        P(),
        P(),
        P(None, TP),
        P(TP, None),
        P(),
        P(None, TP),
        P(None, TP),
        P(TP, None),
        P(DP, None),
    )
    out_specs = (
        P(DP, None),
        P(DP, None),
        P(DP),
        P(DP, None),
        P(DP),
        P(DP, TP),
        P(DP, None),
        P(DP),
        P(DP, TP),
        P(TP, DP),
        P(DP),
        P(DP, TP),
        P(DP, TP),
        P(TP, DP),
    )
    return jax.shard_map(
        on_device, mesh=grid, in_specs=in_specs, out_specs=out_specs, check_vma=False
    )
```

```python
import functools

import jax
import jax.numpy as jnp
import numpy as np
from jax import lax
from jax.experimental import pallas as pl
from jax.experimental.pallas import tpu as pltpu
from jax.sharding import Mesh, PartitionSpec as P

NOPE = 64
ROPE = 32
DV = 64
KVR = 256
QR = 768
LAT = QR + KVR
WIDE = LAT + 128

EPS = 1e-05
BASE = 10000.0
SCALE = (NOPE + ROPE) ** (-0.5)

DP = ("y", "xl", "core")
TP = ("xh", "z")
SWAP = [(0, 1), (1, 0)]
F32 = jnp.float32
BF16 = jnp.bfloat16
NT = (((1,), (1,)), ((), ()))
TN = (((0,), (0,)), ((), ()))
NN = (((1,), (0,)), ((), ()))
TILE = 256


def dot(left, right, dims=NN):
    return lax.dot_general(left, right, dims, preferred_element_type=F32)


def params(limit=56):
    return pltpu.CompilerParams(vmem_limit_bytes=limit * 2**20)


HBM = pl.BlockSpec(memory_space=pltpu.HBM)


def call(kernel, args, in_specs, out_specs, out_shape, name, grid=(1,), scratch=(), needs=(), me=None, limit=60):
    first = 0 if me is None else 1
    n_in, n_out = len(args), len(out_shape)

    def body(*refs):
        ins = refs[: first + n_in]
        rest = refs[first + n_in + len(needs) :]
        mark = rest[n_out]

        @pl.when(pl.program_id(0) == 0)
        def _():
            mark[...] = jnp.zeros_like(mark)

        kernel(*ins, *rest[:n_out], *rest[n_out + 1 :])

    *outs, mark = pl.pallas_call(
        body,
        grid_spec=pltpu.PrefetchScalarGridSpec(
            num_scalar_prefetch=first,
            grid=grid,
            in_specs=list(in_specs) + [HBM] * len(needs),
            out_specs=list(out_specs) + [full((8, 128))],
            scratch_shapes=list(scratch),
        ),
        out_shape=list(out_shape) + [jax.ShapeDtypeStruct((8, 128), F32)],
        compiler_params=params(limit),
        cost_estimate=pl.CostEstimate(flops=1, bytes_accessed=1, transcendentals=0),
        name=name,
    )(*(() if me is None else (me,)), *args, *needs)
    return outs, mark


def shaped(*shape, dtype=BF16):
    return jax.ShapeDtypeStruct(shape, dtype)


def full(shape):
    return pl.BlockSpec(shape, lambda *_: (0,) * len(shape))


def rope_tables(length):
    half = ROPE // 2
    rates = np.exp(np.arange(half, dtype=np.float32) * np.float32(-2.0 * np.log(BASE) / ROPE))
    angles = np.arange(length, dtype=np.float32)[:, None] * rates.astype(np.float32)[None, :]
    cosine, sine = np.cos(angles), np.sin(angles)
    keep = np.zeros((length, 128), np.float32)
    keep[:, :NOPE] = 1.0
    keep[:, 64:80] = cosine
    keep[:, 80:96] = cosine
    low = np.zeros((length, 128), np.float32)
    low[:, 64:80] = -sine
    high = np.zeros((length, 128), np.float32)
    high[:, 80:96] = sine
    return jnp.asarray(keep), jnp.asarray(low), jnp.asarray(high)


def turn(values, keep, low, high, back=False):
    moved = pltpu.roll(values, 112, 1) * low + pltpu.roll(values, 16, 1) * high
    return values * keep - moved if back else values * keep + moved


def root(values):
    return lax.rsqrt(jnp.mean(values * values, axis=-1, keepdims=True) + EPS)


def norm_back(upstream, normed, factor, gain):
    scaled = upstream * gain
    return factor * (scaled - normed * jnp.mean(scaled * normed, axis=-1, keepdims=True))


def spread_out_weight(weight_ref, spread_ref, heads):
    spread_ref[...] = jnp.zeros_like(spread_ref)
    for h in range(heads):
        spread_ref[128 * h + 64 : 128 * h + 128, :] = weight_ref[64 * h : 64 * h + 64, :]


def spread_query_up(weight_ref, spread_ref, heads):
    spread_ref[...] = jnp.zeros_like(spread_ref)
    for h in range(heads):
        spread_ref[128 * h : 128 * h + 96, :] = weight_ref[96 * h : 96 * h + 96, :]


def row(ref):
    return ref[...].reshape(1, -1)


def low_lanes(shape):
    return lax.broadcasted_iota(jnp.int32, shape, 1) < NOPE


def causal(keys, queries, first_query):
    key_ids = lax.broadcasted_iota(jnp.int32, (keys, queries), 0)
    query_ids = lax.broadcasted_iota(jnp.int32, (keys, queries), 1) + first_query
    return key_ids <= query_ids


def attend_kernel(
    heads,
    me,
    tokens,
    first_gain,
    query_down,
    latent_down,
    query_gain,
    latent_gain,
    query_up,
    latent_up,
    out_weight,
    keep,
    low,
    high,
    first_in,
    latents,
    query_code,
    latent_code,
    queries,
    keyvals,
    rope_keys,
    heads_out,
    log_total,
    partial,
    raw_latents,
    spread,
    spread_up,
    rope_down,
    kv_all,
    rope_all,
):
    step = pl.program_id(0)

    @pl.when(step == 0)
    def _():
        spread_out_weight(out_weight, spread, heads)
        spread_query_up(query_up, spread_up, heads)
        rope_down[...] = jnp.zeros_like(rope_down)
        rope_down[64:96, :] = latent_down[KVR:, :]

    def rows_of(index, carry):
        rows = pl.ds(pl.multiple_of(index * 32, 32), 32)
        values = tokens[rows, :].astype(F32)
        first_in[rows, :] = (values * root(values) * row(first_gain)).astype(BF16)
        return carry

    lax.fori_loop(0, TILE // 32, rows_of, 0)
    taken = first_in[...]
    query_latent = dot(taken, query_down[...])
    raw_latents[:, :QR] = query_latent
    code = (query_latent * root(query_latent) * row(query_gain)).astype(BF16)
    query_code[...] = code
    latent = dot(taken, latent_down[:KVR, :], NT)
    raw_latents[:, QR:] = latent
    count = latents.shape[0]
    own = me[0] * count

    @pl.when(own // TILE == step)
    def _():
        latents[...] = raw_latents[pl.ds(pl.multiple_of(own % TILE, count), count), :]

    lcode = (latent * root(latent) * row(latent_gain)).astype(BF16)
    latent_code[...] = lcode
    tables = keep[...], low[...], high[...]
    rope = turn(dot(taken, rope_down[...], NT), *tables).astype(BF16)
    rope_keys[...] = rope
    here = pl.ds(pl.multiple_of(step * TILE, TILE), TILE)
    rope_all[here, :] = rope
    kv = dot(lcode, latent_up[...]).astype(BF16)
    keyvals[...] = kv
    kv_all[here, :] = kv
    raw = dot(code, spread_up[...], NT)
    for h in range(heads):
        lanes = slice(128 * h, 128 * h + 128)
        queries[:, lanes] = turn(raw[:, lanes], *tables).astype(BF16)

    def tile(index):
        keys = TILE * (index + 1)
        for h in range(heads):
            lanes = slice(128 * h, 128 * h + 128)
            kv_h = kv_all[:keys, lanes]
            key = jnp.where(low_lanes((keys, 128)), kv_h, rope_all[:keys, :])
            scores = dot(key, queries[:, lanes], NT) * SCALE
            scores = jnp.where(causal(keys, TILE, TILE * index), scores, -1e30)
            top = jnp.max(scores, axis=0, keepdims=True)
            weights = jnp.exp(scores - top)
            total = jnp.sum(weights, axis=0, keepdims=True)
            log_total[h : h + 1, :] = top + jnp.log(total)
            probs = (weights * (1.0 / total)).astype(BF16)
            heads_out[:, lanes] = dot(probs, kv_h, TN).astype(BF16)

    for index in range(2):
        pl.when(step == index)(functools.partial(tile, index))
    partial[...] = dot(heads_out[...], spread[...]).astype(BF16)


def attend(me, tokens, first_gain, query_down, latent_down, query_gain, latent_gain, query_up, latent_up, out_weight, tables):
    latent_down, query_up = latent_down.T, query_up.T
    length, width = tokens.shape
    heads = out_weight.shape[0] // DV
    wide = 128 * heads

    def rows(columns):
        return pl.BlockSpec((TILE, columns), lambda i, *_: (i, 0))

    return call(
        functools.partial(attend_kernel, heads),
        (tokens, first_gain, query_down, latent_down, query_gain, latent_gain, query_up, latent_up, out_weight, *tables),
        [
            rows(width),
            full((width,)),
            full(query_down.shape),
            full(latent_down.shape),
            full((QR,)),
            full((KVR,)),
            full(query_up.shape),
            full(latent_up.shape),
            full(out_weight.shape),
            rows(128),
            rows(128),
            rows(128),
        ],
        [
            rows(width),
            full((length // 8, LAT)),
            rows(QR),
            rows(KVR),
            rows(wide),
            rows(wide),
            rows(128),
            rows(wide),
            pl.BlockSpec((8, TILE), lambda i, *_: (0, i)),
            rows(width),
        ],
        [
            shaped(length, width),
            shaped(length // 8, LAT, dtype=F32),
            shaped(length, QR),
            shaped(length, KVR),
            shaped(length, wide),
            shaped(length, wide),
            shaped(length, 128),
            shaped(length, wide),
            shaped(8, length, dtype=F32),
            shaped(length, width),
        ],
        "attend",
        grid=(length // TILE,),
        me=me,
        scratch=[
            pltpu.VMEM((TILE, LAT), F32),
            pltpu.VMEM((wide, width), BF16),
            pltpu.VMEM((wide, QR), BF16),
            pltpu.VMEM((128, width), BF16),
            pltpu.VMEM((length, wide), BF16),
            pltpu.VMEM((length, 128), BF16),
        ],
    )


def attend_back_kernel(
    heads,
    attention_back,
    out_weight,
    queries,
    keyvals,
    rope_keys,
    log_total,
    query_up,
    latent_up,
    keep,
    low,
    high,
    query_back,
    keyval_back,
    partial,
    spread,
    spread_up,
    kv_grad,
    rope_grad,
    code_grad,
):
    step = pl.program_id(0)

    @pl.when(step == 0)
    def _():
        spread_out_weight(out_weight, spread, heads)
        spread_query_up(query_up, spread_up, heads)
        kv_grad[...] = jnp.zeros_like(kv_grad)
        rope_grad[...] = jnp.zeros_like(rope_grad)

    heads_back = dot(attention_back[...], spread[...], NT).astype(BF16)
    tables = keep[...], low[...], high[...]

    def tile(index):
        keys = TILE * (index + 1)
        low_part = low_lanes((keys, 128))
        for h in range(heads):
            lanes = slice(128 * h, 128 * h + 128)
            kv_h = keyvals[:keys, lanes]
            key = jnp.where(low_part, kv_h, rope_keys[:keys, :])
            query = queries[:, lanes]
            back = heads_back[:, lanes]
            scores = dot(key, query, NT) * SCALE
            probs = jnp.exp(scores - log_total[h : h + 1, :])
            probs = jnp.where(causal(keys, TILE, TILE * index), probs, 0.0)
            prob_back = dot(kv_h, back, NT)
            mean = jnp.sum(probs * prob_back, axis=0, keepdims=True)
            score_back = (probs * (prob_back - mean)).astype(BF16)
            of_values = dot(probs.astype(BF16), back)
            of_keys = dot(score_back, query) * SCALE
            kv_grad[:keys, lanes] += of_values + jnp.where(low_part, of_keys, 0.0)
            rope_grad[:keys, :] += jnp.where(low_part, 0.0, of_keys)
            of_query = dot(score_back, key, TN) * SCALE
            query_back[:, lanes] = turn(of_query, *tables, back=True).astype(BF16)

    for index in range(2):
        pl.when(step == index)(functools.partial(tile, index))
    here = pl.ds(pl.multiple_of(step * TILE, TILE), TILE)
    code_grad[here, :] = dot(query_back[...], spread_up[...]).astype(BF16)

    @pl.when(step == 1)
    def _():
        kv = kv_grad[...].astype(BF16)
        keyval_back[...] = kv
        partial[:, :QR] = code_grad[...]
        partial[:, QR:LAT] = dot(kv, latent_up[...], NT).astype(BF16)
        partial[:, LAT:] = rope_grad[...].astype(BF16)


def attend_back(attention_back, out_weight, queries, keyvals, rope_keys, log_total, query_up, latent_up, tables, needs):
    query_up = query_up.T
    length, width = attention_back.shape
    heads = out_weight.shape[0] // DV
    wide = 128 * heads

    def rows(columns):
        return pl.BlockSpec((TILE, columns), lambda i, *_: (i, 0))

    return call(
        functools.partial(attend_back_kernel, heads),
        (attention_back, out_weight, queries, keyvals, rope_keys, log_total, query_up, latent_up, *tables),
        [
            rows(width),
            full(out_weight.shape),
            rows(wide),
            full((length, wide)),
            full((length, 128)),
            pl.BlockSpec((8, TILE), lambda i, *_: (0, i)),
            full(query_up.shape),
            full(latent_up.shape),
            rows(128),
            rows(128),
            rows(128),
        ],
        [rows(wide), full((length, wide)), full((length, WIDE))],
        [shaped(length, wide), shaped(length, wide), shaped(length, WIDE)],
        "attend_back",
        grid=(length // TILE,),
        scratch=[
            pltpu.VMEM((wide, width), BF16),
            pltpu.VMEM((wide, QR), BF16),
            pltpu.VMEM((length, wide), F32),
            pltpu.VMEM((length, 128), F32),
            pltpu.VMEM((length, QR), BF16),
        ],
        needs=needs,
    )


def add_up(got):
    total = got[0].astype(F32)
    for k in range(1, 8):
        total = total + got[k].astype(F32)
    return total


STEPS = 2


def residual_kernel(me, got, tokens, gain, residual, many):
    del me
    total = tokens[...].astype(F32) + add_up(got)
    residual[...] = total
    second_in = (total * root(total) * row(gain)).astype(BF16)
    for k in range(8):
        many[k] = second_in


def own_specs(rows, width):
    step = rows // STEPS
    return (
        pl.BlockSpec((8, step, width), lambda i, me: (0, i, 0)),
        pl.BlockSpec((step, width), lambda i, me: (i, 0)),
        pl.BlockSpec((step, width), lambda i, me: (me[0] * STEPS + i, 0)),
    )


def residual_of(me, got, tokens, gain, needs):
    width = tokens.shape[1]
    rows = tokens.shape[0] // 8
    eight, one, own = own_specs(rows, width)
    return call(
        residual_kernel,
        (got.reshape(8, rows, width), tokens, gain),
        [eight, own, full((width,))],
        [one, eight],
        [shaped(rows, width, dtype=F32), shaped(8, rows, width)],
        "residual",
        grid=(STEPS,),
        needs=needs,
        me=me,
        limit=58,
    )


def residual_back_kernel(me, got, residual, cotangent, gain, many, gain_part):
    del me
    second_back = add_up(got)
    values = residual[...]
    factor = root(values)
    normed = values * factor
    part = jnp.sum(second_back * normed, axis=0, keepdims=True)

    @pl.when(pl.program_id(0) == 0)
    def _():
        gain_part[...] = part

    @pl.when(pl.program_id(0) > 0)
    def _():
        gain_part[...] += part

    back = cotangent[...].astype(F32) + norm_back(second_back, normed, factor, row(gain))
    back = back.astype(BF16)
    for k in range(8):
        many[k] = back


def residual_back_of(me, got, residual, cotangent, gain, needs):
    rows, width = residual.shape
    eight, one, own = own_specs(rows, width)
    return call(
        residual_back_kernel,
        (got.reshape(8, rows, width), residual, cotangent, gain),
        [eight, one, own, full((width,))],
        [eight, full((1, width))],
        [shaped(8, rows, width), shaped(1, width, dtype=F32)],
        "residual_back",
        grid=(STEPS,),
        needs=needs,
        me=me,
        limit=58,
    )


def ffn_kernel(
    second_in, gate_weight, up_weight, inner_back, gate_back, up_back, inner, partial
):
    taken = second_in[...]
    gate = dot(taken, gate_weight[...], NT)
    up = dot(taken, up_weight[...], NT)
    sigma = 1.0 / (1.0 + jnp.exp(-gate))
    act = gate * sigma
    units = gate.shape[1]
    back = inner_back[...]
    of_gate = (back * up * sigma * (1.0 + gate * (1.0 - sigma))).astype(BF16)
    of_up = (back * act).astype(BF16)
    for out, values in ((gate_back, of_gate), (up_back, of_up), (inner, (act * up).astype(BF16))):
        out[:, :units] = values
        out[:, units:] = jnp.zeros((values.shape[0], out.shape[1] - units), BF16)
    partial[...] = (dot(of_gate, gate_weight[...]) + dot(of_up, up_weight[...])).astype(BF16)


def ffn(second_in, gate_weight, up_weight, inner_back, needs):
    length, width = second_in.shape
    units = gate_weight.shape[0]
    wide = -(-units // 128) * 128

    def rows(columns):
        return pl.BlockSpec((TILE, columns), lambda i, *_: (i, 0))

    return call(
        ffn_kernel,
        (second_in, gate_weight, up_weight, inner_back),
        [rows(width), full((units, width)), full((units, width)), rows(units)],
        [rows(wide), rows(wide), rows(wide), rows(width)],
        [shaped(length, wide)] * 3 + [shaped(length, width)],
        "ffn",
        grid=(length // TILE,),
        needs=needs,
    )


def ffn_down_kernel(places, inner, down_weight, residual, *refs):
    outs, total = refs[:4], refs[4]
    for i in range(2):
        rows = slice(i * TILE, i * TILE + TILE)
        total[rows, :] = dot(inner[rows, : down_weight.shape[0]], down_weight[...]).astype(BF16)
    count = residual.shape[0]
    own = pl.ds(pl.multiple_of(places[4] * count, count), count)
    total[own, :] = (total[own, :].astype(F32) + residual[...]).astype(BF16)
    for k, out in enumerate(outs):
        rows = out.shape[0]
        out[...] = total[pl.ds(pl.multiple_of(places[k] * rows, rows), rows), :]


def ffn_down(places, inner, down_weight, residual, needs):
    length, width = inner.shape[0], down_weight.shape[1]
    block = (length // 4, width)
    return call(
        ffn_down_kernel,
        (inner, down_weight, residual),
        [full(inner.shape), full(down_weight.shape), full(residual.shape)],
        [full(block)] * 4,
        [shaped(*block)] * 4,
        "ffn_down",
        scratch=[pltpu.VMEM((length, width), BF16)],
        needs=needs,
        me=places,
    )


def halves_kernel(blocks, width, starts, *refs):
    sources, outs, turned = refs[:blocks], refs[blocks : 3 * blocks], refs[3 * blocks]
    for n in range(blocks):
        source, keep, give = sources[n], outs[2 * n], outs[2 * n + 1]
        columns, each = source.shape[1], width[n]
        for c in range(0, columns, 256):
            turned[c : c + 256, :] = source[:, c : c + 256].T
        for which, out in enumerate((keep, give)):
            for k in range(8):
                first = pl.multiple_of(starts[8 * which + k] * each, 16)
                out[each * k : each * k + each, :] = turned[pl.ds(first, each), :]


def halves(starts, values, needs):
    length = values[0].shape[0]
    widths = [item.shape[1] // 16 for item in values]
    shapes = [(8 * w, length) for w in widths for _ in range(2)]
    return call(
        functools.partial(halves_kernel, len(values), widths),
        tuple(values),
        [full(item.shape) for item in values],
        [full(s) for s in shapes],
        [shaped(*s) for s in shapes],
        "halves",
        scratch=[pltpu.VMEM((max(item.shape[1] for item in values), length), BF16)],
        needs=needs,
        me=starts,
    )


ORDER = (2, 1, 3, 0)


def ffn_grads_kernel(in_keep, in_got, cot_keep, cot_got, *refs):
    ours, theirs, outs = refs[:3], refs[3:6], refs[6:]
    units = outs[0].shape[1] // 3

    def block(*parts):
        for n, (keep, got) in enumerate(((in_keep, in_got), (in_keep, in_got), (cot_keep, cot_got))):
            total = dot(keep[...], ours[n][...]) + dot(got[...], theirs[n][...])
            total = total[:, :units].astype(BF16)
            first = 0
            for out in parts:
                count = out.shape[0]
                out[:, units * n : units * n + units] = total[first : first + count]
                first += count

    for s, parts in enumerate((outs[:2], outs[2:3], outs[3:4], outs[4:])):
        pl.when(pl.program_id(0) == s)(functools.partial(block, *parts))


def ffn_grads(in_keep, in_got, cot_keep, cot_got, ours, theirs, units, needs):
    length, wide = ours[0].shape
    rows = in_keep.shape[0] // 4

    def index(i):
        return (jnp.where(i == 0, 2, jnp.where(i == 1, 1, jnp.where(i == 2, 3, 0))), 0)

    left = pl.BlockSpec((rows, length), index)
    out = (rows, 3 * units)
    outs = [(rows // 2, 3 * units)] * 2 + [out] * 3
    return call(
        ffn_grads_kernel,
        (in_keep, in_got, cot_keep, cot_got, *ours, *theirs),
        [left] * 4 + [full((length, wide))] * 6,
        [full(s) for s in outs],
        [shaped(*s) for s in outs],
        "ffn_grads",
        grid=(4,),
        needs=needs,
    )


def attn_grads_kernel(widths, *refs):
    keeps, gots, ours, theirs, outs = refs[:3], refs[3:6], refs[6:9], refs[9:12], refs[12:]
    rows = sum(widths)
    for out, k in zip(outs, ORDER):
        first = 0
        for n, each in enumerate(widths):
            part = slice(2 * each * k, 2 * each * k + 2 * each)
            total = dot(keeps[n][part, :], ours[n][...]) + dot(gots[n][part, :], theirs[n][...])
            total = total.astype(BF16)
            out[first : first + each, :] = total[:each]
            out[rows + first : rows + first + each, :] = total[each:]
            first += each


def attn_grads(keeps, gots, ours, theirs, needs):
    widths = [item.shape[0] // 8 for item in keeps]
    rows, wide = sum(widths), ours[0].shape[1]
    args = (*keeps, *gots, *ours, *theirs)
    outs = [(2 * rows, wide)] * 4
    return call(
        functools.partial(attn_grads_kernel, widths),
        args,
        [full(item.shape) for item in args],
        [full(s) for s in outs],
        [shaped(*s) for s in outs],
        "attn_grads",
        needs=needs,
    )


UP = [(i, (i + 1) % 4) for i in range(4)]
DOWN = [(i, (i + 3) % 4) for i in range(4)]
ACROSS = [(i, (i + 2) % 4) for i in range(4)]


def relay_kernel(up, from_below, down, from_above, up_out, down_out):
    @pl.when(pl.program_id(0) == 0)
    def _():
        up_out[...] = (up[...].astype(F32) + from_below[...].astype(F32)).astype(BF16)
        down_out[...] = down[...]

    @pl.when(pl.program_id(0) == 1)
    def _():
        up_out[...] = up[...]
        down_out[...] = (down[...].astype(F32) + from_above[...].astype(F32)).astype(BF16)


def relay(up, from_below, down, from_above, needs):
    rows, width = from_below.shape
    half = pl.BlockSpec((rows, width), lambda i, *_: (i, 0))
    return call(
        relay_kernel,
        (up, from_below, down, from_above),
        [half, full((rows, width)), half, full((rows, width))],
        [half, half],
        [shaped(2 * rows, width)] * 2,
        "relay",
        grid=(2,),
        needs=needs,
    )


def add_chips_kernel(*refs):
    ins, keep, give = refs[:-2], refs[-2], refs[-1]
    count = len(ins) // 2
    keep[...] = sum(item[...].astype(F32) for item in ins[:count])
    give[...] = sum(item[...].astype(F32) for item in ins[count:]).astype(BF16)


def add_chips(items, needs):
    rows, width = items[0].shape[0] // 2, items[0].shape[1]
    step = rows // 2 if rows % 32 == 0 and (rows // 2) % 16 == 0 else rows
    count = rows // step
    mine = pl.BlockSpec((step, width), lambda i, *_: (i, 0))
    other = pl.BlockSpec((step, width), lambda i, *_: (i + count, 0))
    return call(
        add_chips_kernel,
        (*items, *items),
        [mine] * len(items) + [other] * len(items),
        [mine, mine],
        [shaped(rows, width, dtype=F32), shaped(rows, width)],
        "add_chips",
        grid=(count,),
        needs=needs,
    )


def add_all_kernel(*refs):
    refs[-1][...] = sum(item[...].astype(F32) for item in refs[:-1]).astype(BF16)


def add_all(items, needs):
    rows, width = items[0].shape
    half = pl.BlockSpec((rows // 2, width), lambda i, *_: (i, 0))
    return call(
        add_all_kernel,
        tuple(items),
        [half] * len(items),
        [half],
        [shaped(rows, width)],
        "add_all",
        grid=(2,),
        needs=needs,
        limit=58,
    )


def over_z(blocks):
    return [lax.ppermute(blocks[k], "z", [(i, i ^ k) for i in range(4)]) for k in (1, 2, 3)]


def assemble_kernel(places, *refs):
    del places
    for k in range(4):

        @pl.when(pl.program_id(0) == k)
        def _(k=k):
            refs[4][...] = refs[k][...]


def assemble(places, blocks):
    rows, width = blocks[0].shape
    return call(
        assemble_kernel,
        tuple(blocks),
        [full((rows, width))] * 4,
        [pl.BlockSpec((rows, width), lambda i, places: (places[i], 0))],
        [shaped(4 * rows, width)],
        "assemble",
        grid=(4,),
        me=places,
    )[0][0]


def over_cores(values):
    return lax.ppermute(values, "core", SWAP)


def latents_back_kernel(
    me, got, latents, query_gain, latent_gain, keep, low, high, many, own, gain_part, turns, sems
):
    rows = own.shape[0]
    here = pl.ds(pl.multiple_of(me[0] * rows, rows), rows)
    copies = [
        pltpu.make_async_copy(table.at[here, :], turns.at[n], sems.at[n])
        for n, table in enumerate((keep, low, high))
    ]
    for copy in copies:
        copy.start()
    total = add_up(got)
    for copy in copies:
        copy.wait()

    def back(lanes, gain):
        upstream, values = total[:, lanes], latents[:, lanes]
        factor = root(values)
        normed = values * factor
        gain_part[:, lanes] = jnp.sum(upstream * normed, axis=0, keepdims=True)
        return norm_back(upstream, normed, factor, row(gain)).astype(BF16)

    own[:, :QR] = back(slice(0, QR), query_gain)
    own[:, QR:LAT] = back(slice(QR, LAT), latent_gain)
    own[:, LAT:] = turn(total[:, LAT:], turns[0], turns[1], turns[2], back=True).astype(BF16)
    for k in range(8):
        many[k] = own[...]


def latents_back_of(me, got, latents, query_gain, latent_gain, tables, needs):
    rows = latents.shape[0]
    return call(
        latents_back_kernel,
        (got.reshape(8, rows, WIDE), latents, query_gain, latent_gain, *tables),
        [full((8, rows, WIDE)), full(latents.shape), full((QR,)), full((KVR,)), HBM, HBM, HBM],
        [full((8, rows, WIDE)), full((rows, WIDE)), full((1, LAT))],
        [shaped(8, rows, WIDE), shaped(rows, WIDE), shaped(1, LAT, dtype=F32)],
        "latents_back",
        scratch=[
            pltpu.VMEM((3, rows, 128), F32),
            pltpu.SemaphoreType.DMA((3,)),
        ],
        needs=needs,
        me=me,
        limit=24,
    )


def first_back_of(raw_back, query_down, latent_down, rope_down):
    rope_down[...] = jnp.zeros_like(rope_down)
    rope_down[64:96, :] = latent_down[KVR:, :]
    return (
        dot(raw_back[:, :QR], query_down[...], NT)
        + dot(raw_back[:, QR:LAT], latent_down[:KVR, :])
        + dot(raw_back[:, LAT:], rope_down[...])
    )


def first_gain_kernel(
    me, raw_back, tokens, query_down, latent_down, gain_part, rope_down, own, sem
):
    rows = own.shape[0]
    here = pl.ds(pl.multiple_of(me[0] * rows, rows), rows)
    copy = pltpu.make_async_copy(tokens.at[here, :], own, sem)
    copy.start()
    first_back = first_back_of(raw_back, query_down, latent_down, rope_down)
    copy.wait()
    values = own[...].astype(F32)
    gain_part[...] = jnp.sum(first_back * (values * root(values)), axis=0, keepdims=True)


def first_gain_of(me, own_raw_back, tokens, query_down, latent_down, needs):
    width = tokens.shape[1]
    return call(
        first_gain_kernel,
        (own_raw_back, tokens, query_down, latent_down.T),
        [full(own_raw_back.shape), HBM, full(query_down.shape), full(latent_down.shape[::-1])],
        [full((1, width))],
        [shaped(1, width, dtype=F32)],
        "first_gain",
        scratch=[
            pltpu.VMEM((128, width), BF16),
            pltpu.VMEM((own_raw_back.shape[0], width), BF16),
            pltpu.SemaphoreType.DMA,
        ],
        needs=needs,
        me=me,
    )


def tokens_back_kernel(
    raw_back, tokens, attention_back, query_down, latent_down, gain, tokens_grad, rope_down
):
    first_back = first_back_of(raw_back, query_down, latent_down, rope_down)
    values = tokens[...].astype(F32)
    factor = root(values)
    tokens_grad[...] = attention_back[...].astype(F32) + norm_back(
        first_back, values * factor, factor, row(gain)
    )


def tokens_back_of(raw_back, tokens, attention_back, query_down, latent_down, gain, needs):
    length, width = tokens.shape

    def rows(columns):
        return pl.BlockSpec((TILE, columns), lambda i, *_: (i, 0))

    return call(
        tokens_back_kernel,
        (raw_back, tokens, attention_back, query_down, latent_down.T, gain),
        [
            rows(WIDE),
            rows(width),
            rows(width),
            full(query_down.shape),
            full(latent_down.shape[::-1]),
            full((width,)),
        ],
        [rows(width)],
        [shaped(length, width, dtype=F32)],
        "tokens_back",
        grid=(length // TILE,),
        scratch=[pltpu.VMEM((128, width), BF16)],
        needs=needs,
    )


def finish_ffn_kernel(keep, got, gate, up, down):
    units = gate.shape[1]
    for n, out in enumerate((gate, up, down)):
        lanes = slice(units * n, units * n + units)
        out[...] = keep[:, lanes] + got[:, lanes].astype(F32)


def finish_ffn(keep, got, needs):
    rows, width = keep.shape
    out = (rows, width // 3)
    return call(
        finish_ffn_kernel,
        (keep, got),
        [full(keep.shape), full(got.shape)],
        [full(out)] * 3,
        [shaped(*out, dtype=F32)] * 3,
        "finish_ffn",
        needs=needs,
    )


def finish_attn_kernel(heads, keep, got, out_grad, query_grad, latent_grad):
    total = keep[...] + got[...].astype(F32)
    for h in range(heads):
        lanes = slice(128 * h, 128 * h + 128)
        out_grad[:, 64 * h : 64 * h + 64] = total[:160, 128 * h + 64 : 128 * h + 128]
        query_grad[:, 96 * h : 96 * h + 96] = total[160:208, 128 * h : 128 * h + 96]
    latent_grad[...] = total[208:224]


def finish_attn(keep, got, needs):
    heads = keep.shape[1] // 128
    outs = [(160, 64 * heads), (48, 96 * heads), (16, 128 * heads)]
    return call(
        functools.partial(finish_attn_kernel, heads),
        (keep, got),
        [full(keep.shape), full(got.shape)],
        [full(s) for s in outs],
        [shaped(*s, dtype=F32) for s in outs],
        "finish_attn",
        needs=needs,
    )


GAINS = ((0, 160), (160, 160), (320, 48), (368, 16))


def down_parts_kernel(own_in, raw_back, gains, out):
    total = dot(own_in[...], raw_back[...]).astype(BF16)
    for d in range(16):
        out[d, :20, :] = total[20 * d : 20 * d + 20]
        out[d, 20:, :] = jnp.zeros((4, WIDE), BF16)
        out[d, 20:21, :] = gains[d : d + 1, :]


def down_parts(own_in, raw_back, gains, needs):
    args = (own_in, raw_back, gains)
    return call(
        down_parts_kernel,
        args,
        [full(item.shape) for item in args],
        [full((16, 24, WIDE))],
        [shaped(16, 24, WIDE)],
        "down_parts",
        needs=needs,
        limit=24,
    )


def sum_copies_kernel(got, many):
    total = got[0].astype(F32)
    for d in range(1, 16):
        total = total + got[d].astype(F32)
    for k in range(8):
        many[k] = total.astype(BF16)


def sum_copies(got, needs):
    return call(
        sum_copies_kernel,
        (got,),
        [full(got.shape)],
        [full((8, 24, WIDE))],
        [shaped(8, 24, WIDE)],
        "sum_copies",
        needs=needs,
        limit=24,
    )


def finish_down_kernel(everyone, query_grad, latent_grad, *gains):
    for t in range(8):
        values = everyone[t].astype(F32)
        query_grad[20 * t : 20 * t + 20, :] = values[:20, :QR]
        latent_grad[20 * t : 20 * t + 20, :KVR] = values[:20, QR:LAT]
        latent_grad[20 * t : 20 * t + 20, KVR:] = values[:20, LAT + 64 : LAT + 96]
    total = sum(everyone[t, 16:24, :].astype(F32) for t in range(8))[4:5, :]
    for out, (first, count) in zip(gains, GAINS):
        out[...] = total[:, first : first + count]


def finish_down(everyone):
    everyone = everyone.reshape(8, 24, WIDE)
    outs = [(160, QR), (160, KVR + ROPE)] + [(1, count) for _, count in GAINS]
    return call(
        finish_down_kernel,
        (everyone,),
        [full(everyone.shape)],
        [full(s) for s in outs],
        [shaped(*s, dtype=F32) for s in outs],
        "finish_down",
        limit=24,
    )[0]


def exchange(blocks):
    return lax.all_to_all(blocks.reshape(-1, blocks.shape[-1]), TP, 0, 0, tiled=True)


def on_device(
    tokens,
    first_gain,
    query_down,
    query_gain,
    query_up,
    latent_down,
    latent_gain,
    latent_up,
    out_weight,
    second_gain,
    gate_weight,
    up_weight,
    down_weight,
    cotangent,
):
    length = tokens.shape[0]
    me = lax.axis_index(TP).astype(jnp.int32).reshape(1)
    y, xl, core = lax.axis_index("y"), lax.axis_index("xl"), lax.axis_index("core")
    starts = jnp.stack(
        [
            ((y + k) % 4 * 2 + (xl ^ j)) * 2 + c
            for c in (core, 1 - core)
            for k in range(4)
            for j in range(2)
        ]
    ).astype(jnp.int32)
    places = jnp.stack([lax.axis_index("z") ^ k for k in range(4)] + [me[0]]).astype(jnp.int32)
    tables = rope_tables(length)

    gate_turned, up_turned = gate_weight.T, up_weight.T

    (
        first_in,
        latents,
        query_code,
        latent_code,
        queries,
        keyvals,
        rope_keys,
        heads_out,
        log_total,
        attn_partial,
    ), started = attend(
        me,
        tokens,
        first_gain,
        query_down,
        latent_down,
        query_gain,
        latent_gain,
        query_up,
        latent_up,
        out_weight,
        tables,
    )
    attn_got = exchange(attn_partial)

    (cot_keep, cot_give), picked = halves(starts, [cotangent], [started])
    inner_back = dot(cotangent, down_weight, NT)
    cot_got = over_cores(cot_give)

    (residual, second_many), _ = residual_of(
        me, attn_got, tokens, second_gain, [picked, cot_got]
    )
    second_in = exchange(second_many)

    turned_in = first_in.T.reshape(16, 8, 20, length)
    own_in = lax.dynamic_slice_in_dim(turned_in, me[0], 1, 1).reshape(320, length)
    (code_keep, code_give, lat_keep, lat_give), picked = halves(
        starts, [query_code, latent_code], [residual]
    )
    code_got, lat_got = over_cores(code_give), over_cores(lat_give)
    heads_got = over_cores(heads_out)

    (gate_back, up_back, inner, back_partial), done = ffn(
        second_in, gate_turned, up_turned, inner_back, [picked, own_in, code_got, lat_got, heads_got]
    )
    back_got = exchange(back_partial)

    ours = (gate_back, up_back, inner)
    theirs = [over_cores(item) for item in ours]
    (in_keep, in_give), _ = halves(starts, [second_in], [done])
    in_got = over_cores(in_give)
    (far_up, far_down, ffn_up, ffn_down_way, ffn_own), done = ffn_grads(in_keep, in_got, cot_keep, cot_got, ours, theirs, gate_weight.shape[1], [])
    below, above = lax.ppermute(far_up, "y", UP), lax.ppermute(far_down, "y", DOWN)

    (back_many, second_gain_part), done = residual_back_of(
        me, back_got, residual, cotangent, second_gain, [done]
    )
    attention_back = exchange(back_many)
    mixed_blocks, done = ffn_down(places, inner, down_weight, residual, [done])
    mixed_got = over_z(mixed_blocks)
    (ffn_up, ffn_down_way), done = relay(ffn_up, below, ffn_down_way, above, [done])
    below, above = lax.ppermute(ffn_up, "y", UP), lax.ppermute(ffn_down_way, "y", DOWN)

    (query_raw_back, keyval_back, latents_partial), back_done = attend_back(
        attention_back,
        out_weight,
        queries,
        keyvals,
        rope_keys,
        log_total,
        query_up,
        latent_up,
        tables,
        [done],
    )
    latents_got = exchange(latents_partial)

    (out_keep, out_give), picked = halves(starts, [attention_back], [back_done])
    (ffn_keep, ffn_give), done = add_chips([ffn_own, below, above], [back_done])
    ffn_got = lax.ppermute(ffn_give, "xl", SWAP)

    (raw_many, own_raw, latent_gain_parts), done = latents_back_of(
        me, latents_got, latents, query_gain, latent_gain, tables, [done, picked]
    )
    raw_back = exchange(raw_many)

    out_got = over_cores(out_give)
    raw_got, kv_got = over_cores(query_raw_back), over_cores(keyval_back)
    (attn_across, attn_up, attn_down, attn_own), done = attn_grads(
        (out_keep, code_keep, lat_keep),
        (out_got, code_got, lat_got),
        (heads_out, query_raw_back, keyval_back),
        (heads_got, raw_got, kv_got),
        [done],
    )
    attn_got = [
        lax.ppermute(attn_across, "y", ACROSS),
        lax.ppermute(attn_up, "y", UP),
        lax.ppermute(attn_down, "y", DOWN),
    ]
    (mixed_part,), done = add_all([mixed_blocks[0], *mixed_got], [done])
    mixed_other = lax.ppermute(mixed_part, "xh", SWAP)
    (first_gain_part,), gain_done = first_gain_of(
        me, own_raw, tokens, query_down, latent_down, [done]
    )

    (mixed_part,), _ = add_all([mixed_part, mixed_other], [gain_done])

    gains = jnp.concatenate(
        [
            first_gain_part.reshape(16, -1),
            second_gain_part.reshape(16, -1),
            latent_gain_parts[0, :QR].reshape(16, -1),
            latent_gain_parts[0, QR:].reshape(16, -1),
        ],
        axis=1,
    ).astype(BF16)
    gains = jnp.pad(gains, ((0, 0), (0, WIDE - gains.shape[1])))
    (parts,), done = down_parts(own_in, raw_back, gains, [attn_got[1], attn_got[2]])
    parts_got = lax.all_to_all(parts, DP, 0, 0, tiled=True)

    (tokens_grad,), done = tokens_back_of(
        raw_back, tokens, attention_back, query_down, latent_down, first_gain, [done]
    )
    (many,), summed = sum_copies(parts_got, [done])
    everyone = exchange(many)

    (attn_keep, attn_give), done = add_chips([attn_own, *attn_got], [summed])
    attn_other = lax.ppermute(attn_give, "xl", SWAP)
    (gate_weight_grad, up_weight_grad, down_weight_grad), done = finish_ffn(
        ffn_keep, ffn_got, [done]
    )
    (out_weight_grad, query_up_grad, latent_up_grad), done = finish_attn(
        attn_keep, attn_other, [done]
    )
    (
        query_down_grad,
        latent_down_grad,
        first_gain_grad,
        second_gain_grad,
        query_gain_grad,
        latent_gain_grad,
    ) = finish_down(everyone)

    mixed = assemble(places, [mixed_part, *over_z([mixed_part] * 4)])

    return (
        mixed,
        tokens_grad,
        first_gain_grad[0],
        query_down_grad,
        query_gain_grad[0],
        query_up_grad,
        latent_down_grad,
        latent_gain_grad[0],
        latent_up_grad,
        out_weight_grad.T,
        second_gain_grad[0],
        gate_weight_grad,
        up_weight_grad,
        down_weight_grad.T,
    )


def solution(mesh):
    grid = Mesh(mesh.devices.reshape(4, 2, 2, 2, 4), ("y", "xl", "core", "xh", "z"))
    in_specs = (
        P(DP, None),
        P(),
        P(),
        P(),
        P(None, TP),
        P(),
        P(),
        P(None, TP),
        P(TP, None),
        P(),
        P(None, TP),
        P(None, TP),
        P(TP, None),
        P(DP, None),
    )
    out_specs = (
        P(DP, None),
        P(DP, None),
        P(DP),
        P(DP, None),
        P(DP),
        P(DP, TP),
        P(DP, None),
        P(DP),
        P(DP, TP),
        P(TP, DP),
        P(DP),
        P(DP, TP),
        P(DP, TP),
        P(TP, DP),
    )
    return jax.shard_map(
        on_device, mesh=grid, in_specs=in_specs, out_specs=out_specs, check_vma=False
    )
```

```python
import functools

import jax
import jax.numpy as jnp
import numpy as np
from jax import lax
from jax.experimental import pallas as pl
from jax.experimental.pallas import tpu as pltpu
from jax.sharding import Mesh, PartitionSpec as P

NOPE = 64
ROPE = 32
DV = 64
KVR = 256
QR = 768
LAT = QR + KVR
WIDE = LAT + 128

EPS = 1e-05
BASE = 10000.0
SCALE = (NOPE + ROPE) ** (-0.5)

DP = ("y", "xl", "core")
TP = ("xh", "z")
SWAP = [(0, 1), (1, 0)]
F32 = jnp.float32
BF16 = jnp.bfloat16
NT = (((1,), (1,)), ((), ()))
TN = (((0,), (0,)), ((), ()))
NN = (((1,), (0,)), ((), ()))
TILE = 256


def dot(left, right, dims=NN):
    return lax.dot_general(left, right, dims, preferred_element_type=F32)


def params(limit=56):
    return pltpu.CompilerParams(vmem_limit_bytes=limit * 2**20)


HBM = pl.BlockSpec(memory_space=pltpu.HBM)


def call(kernel, args, in_specs, out_specs, out_shape, name, grid=(1,), scratch=(), needs=(), me=None, limit=60):
    first = 0 if me is None else 1
    n_in, n_out = len(args), len(out_shape)

    def body(*refs):
        ins = refs[: first + n_in]
        rest = refs[first + n_in + len(needs) :]
        mark = rest[n_out]

        @pl.when(pl.program_id(0) == 0)
        def _():
            mark[...] = jnp.zeros_like(mark)

        kernel(*ins, *rest[:n_out], *rest[n_out + 1 :])

    *outs, mark = pl.pallas_call(
        body,
        grid_spec=pltpu.PrefetchScalarGridSpec(
            num_scalar_prefetch=first,
            grid=grid,
            in_specs=list(in_specs) + [HBM] * len(needs),
            out_specs=list(out_specs) + [full((8, 128))],
            scratch_shapes=list(scratch),
        ),
        out_shape=list(out_shape) + [jax.ShapeDtypeStruct((8, 128), F32)],
        compiler_params=params(limit),
        cost_estimate=pl.CostEstimate(flops=1, bytes_accessed=1, transcendentals=0),
        name=name,
    )(*(() if me is None else (me,)), *args, *needs)
    return outs, mark


def shaped(*shape, dtype=BF16):
    return jax.ShapeDtypeStruct(shape, dtype)


def full(shape):
    return pl.BlockSpec(shape, lambda *_: (0,) * len(shape))


def rope_tables(length):
    half = ROPE // 2
    rates = np.exp(np.arange(half, dtype=np.float32) * np.float32(-2.0 * np.log(BASE) / ROPE))
    angles = np.arange(length, dtype=np.float32)[:, None] * rates.astype(np.float32)[None, :]
    cosine, sine = np.cos(angles), np.sin(angles)
    keep = np.zeros((length, 128), np.float32)
    keep[:, :NOPE] = 1.0
    keep[:, 64:80] = cosine
    keep[:, 80:96] = cosine
    low = np.zeros((length, 128), np.float32)
    low[:, 64:80] = -sine
    high = np.zeros((length, 128), np.float32)
    high[:, 80:96] = sine
    return jnp.asarray(keep), jnp.asarray(low), jnp.asarray(high)


def turn(values, keep, low, high, back=False):
    moved = pltpu.roll(values, 112, 1) * low + pltpu.roll(values, 16, 1) * high
    return values * keep - moved if back else values * keep + moved


def root(values):
    return lax.rsqrt(jnp.mean(values * values, axis=-1, keepdims=True) + EPS)


def norm_back(upstream, normed, factor, gain):
    scaled = upstream * gain
    return factor * (scaled - normed * jnp.mean(scaled * normed, axis=-1, keepdims=True))


def spread_out_weight(weight_ref, spread_ref, heads):
    spread_ref[...] = jnp.zeros_like(spread_ref)
    for h in range(heads):
        spread_ref[128 * h + 64 : 128 * h + 128, :] = weight_ref[64 * h : 64 * h + 64, :]


def spread_query_up(weight_ref, spread_ref, heads):
    spread_ref[...] = jnp.zeros_like(spread_ref)
    for h in range(heads):
        spread_ref[128 * h : 128 * h + 96, :] = weight_ref[96 * h : 96 * h + 96, :]


def row(ref):
    return ref[...].reshape(1, -1)


def low_lanes(shape):
    return lax.broadcasted_iota(jnp.int32, shape, 1) < NOPE


def causal(keys, queries, first_query):
    key_ids = lax.broadcasted_iota(jnp.int32, (keys, queries), 0)
    query_ids = lax.broadcasted_iota(jnp.int32, (keys, queries), 1) + first_query
    return key_ids <= query_ids


def attend_kernel(
    heads,
    me,
    tokens,
    first_gain,
    query_down,
    latent_down,
    query_gain,
    latent_gain,
    query_up,
    latent_up,
    out_weight,
    keep,
    low,
    high,
    first_in,
    latents,
    query_code,
    latent_code,
    queries,
    keyvals,
    rope_keys,
    heads_out,
    log_total,
    partial,
    raw_latents,
    spread,
    spread_up,
    rope_down,
    kv_all,
    rope_all,
):
    step = pl.program_id(0)

    @pl.when(step == 0)
    def _():
        spread_out_weight(out_weight, spread, heads)
        spread_query_up(query_up, spread_up, heads)
        rope_down[...] = jnp.zeros_like(rope_down)
        rope_down[64:96, :] = latent_down[KVR:, :]

    def rows_of(index, carry):
        rows = pl.ds(pl.multiple_of(index * 32, 32), 32)
        values = tokens[rows, :].astype(F32)
        first_in[rows, :] = (values * root(values) * row(first_gain)).astype(BF16)
        return carry

    lax.fori_loop(0, TILE // 32, rows_of, 0)
    taken = first_in[...]
    query_latent = dot(taken, query_down[...])
    raw_latents[:, :QR] = query_latent
    code = (query_latent * root(query_latent) * row(query_gain)).astype(BF16)
    query_code[...] = code
    latent = dot(taken, latent_down[:KVR, :], NT)
    raw_latents[:, QR:] = latent
    count = latents.shape[0]
    own = me[0] * count

    @pl.when(own // TILE == step)
    def _():
        latents[...] = raw_latents[pl.ds(pl.multiple_of(own % TILE, count), count), :]

    lcode = (latent * root(latent) * row(latent_gain)).astype(BF16)
    latent_code[...] = lcode
    tables = keep[...], low[...], high[...]
    rope = turn(dot(taken, rope_down[...], NT), *tables).astype(BF16)
    rope_keys[...] = rope
    here = pl.ds(pl.multiple_of(step * TILE, TILE), TILE)
    rope_all[here, :] = rope
    kv = dot(lcode, latent_up[...]).astype(BF16)
    keyvals[...] = kv
    kv_all[here, :] = kv
    raw = dot(code, spread_up[...], NT)
    for h in range(heads):
        lanes = slice(128 * h, 128 * h + 128)
        queries[:, lanes] = turn(raw[:, lanes], *tables).astype(BF16)

    def tile(index):
        keys = TILE * (index + 1)
        for h in range(heads):
            lanes = slice(128 * h, 128 * h + 128)
            kv_h = kv_all[:keys, lanes]
            key = jnp.where(low_lanes((keys, 128)), kv_h, rope_all[:keys, :])
            scores = dot(key, queries[:, lanes], NT) * SCALE
            scores = jnp.where(causal(keys, TILE, TILE * index), scores, -1e30)
            top = jnp.max(scores, axis=0, keepdims=True)
            weights = jnp.exp(scores - top)
            total = jnp.sum(weights, axis=0, keepdims=True)
            log_total[h : h + 1, :] = top + jnp.log(total)
            probs = (weights * (1.0 / total)).astype(BF16)
            heads_out[:, lanes] = dot(probs, kv_h, TN).astype(BF16)

    for index in range(2):
        pl.when(step == index)(functools.partial(tile, index))
    partial[...] = dot(heads_out[...], spread[...]).astype(BF16)


def attend(me, tokens, first_gain, query_down, latent_down, query_gain, latent_gain, query_up, latent_up, out_weight, tables):
    latent_down, query_up = latent_down.T, query_up.T
    length, width = tokens.shape
    heads = out_weight.shape[0] // DV
    wide = 128 * heads

    def rows(columns):
        return pl.BlockSpec((TILE, columns), lambda i, *_: (i, 0))

    return call(
        functools.partial(attend_kernel, heads),
        (tokens, first_gain, query_down, latent_down, query_gain, latent_gain, query_up, latent_up, out_weight, *tables),
        [
            rows(width),
            full((width,)),
            full(query_down.shape),
            full(latent_down.shape),
            full((QR,)),
            full((KVR,)),
            full(query_up.shape),
            full(latent_up.shape),
            full(out_weight.shape),
            rows(128),
            rows(128),
            rows(128),
        ],
        [
            rows(width),
            full((length // 8, LAT)),
            rows(QR),
            rows(KVR),
            rows(wide),
            rows(wide),
            rows(128),
            rows(wide),
            pl.BlockSpec((8, TILE), lambda i, *_: (0, i)),
            rows(width),
        ],
        [
            shaped(length, width),
            shaped(length // 8, LAT, dtype=F32),
            shaped(length, QR),
            shaped(length, KVR),
            shaped(length, wide),
            shaped(length, wide),
            shaped(length, 128),
            shaped(length, wide),
            shaped(8, length, dtype=F32),
            shaped(length, width),
        ],
        "attend",
        grid=(length // TILE,),
        me=me,
        scratch=[
            pltpu.VMEM((TILE, LAT), F32),
            pltpu.VMEM((wide, width), BF16),
            pltpu.VMEM((wide, QR), BF16),
            pltpu.VMEM((128, width), BF16),
            pltpu.VMEM((length, wide), BF16),
            pltpu.VMEM((length, 128), BF16),
        ],
    )


def attend_back_kernel(
    heads,
    attention_back,
    out_weight,
    queries,
    keyvals,
    rope_keys,
    log_total,
    query_up,
    latent_up,
    keep,
    low,
    high,
    both_back,
    partial,
    spread,
    spread_up,
    kv_grad,
    rope_grad,
    code_grad,
):
    step = pl.program_id(0)

    @pl.when(step == 0)
    def _():
        spread_out_weight(out_weight, spread, heads)
        spread_query_up(query_up, spread_up, heads)
        kv_grad[...] = jnp.zeros_like(kv_grad)
        rope_grad[...] = jnp.zeros_like(rope_grad)

    heads_back = dot(attention_back[...], spread[...], NT).astype(BF16)
    tables = keep[...], low[...], high[...]

    def tile(index):
        keys = TILE * (index + 1)
        low_part = low_lanes((keys, 128))
        for h in range(heads):
            lanes = slice(128 * h, 128 * h + 128)
            kv_h = keyvals[:keys, lanes]
            key = jnp.where(low_part, kv_h, rope_keys[:keys, :])
            query = queries[:, lanes]
            back = heads_back[:, lanes]
            scores = dot(key, query, NT) * SCALE
            probs = jnp.exp(scores - log_total[h : h + 1, :])
            probs = jnp.where(causal(keys, TILE, TILE * index), probs, 0.0)
            prob_back = dot(kv_h, back, NT)
            mean = jnp.sum(probs * prob_back, axis=0, keepdims=True)
            score_back = (probs * (prob_back - mean)).astype(BF16)
            of_values = dot(probs.astype(BF16), back)
            of_keys = dot(score_back, query) * SCALE
            kv_grad[:keys, lanes] += of_values + jnp.where(low_part, of_keys, 0.0)
            rope_grad[:keys, :] += jnp.where(low_part, 0.0, of_keys)
            of_query = dot(score_back, key, TN) * SCALE
            both_back[here, lanes] = turn(of_query, *tables, back=True).astype(BF16)

    wide = 128 * heads
    here = pl.ds(pl.multiple_of(step * TILE, TILE), TILE)
    for index in range(2):
        pl.when(step == index)(functools.partial(tile, index))
    code_grad[here, :] = dot(both_back[here, :wide], spread_up[...]).astype(BF16)

    @pl.when(step == 1)
    def _():
        kv = kv_grad[...].astype(BF16)
        both_back[:, wide:] = kv
        partial[:, :QR] = code_grad[...]
        partial[:, QR:LAT] = dot(kv, latent_up[...], NT).astype(BF16)
        partial[:, LAT:] = rope_grad[...].astype(BF16)


def attend_back(attention_back, out_weight, queries, keyvals, rope_keys, log_total, query_up, latent_up, tables, needs):
    query_up = query_up.T
    length, width = attention_back.shape
    heads = out_weight.shape[0] // DV
    wide = 128 * heads

    def rows(columns):
        return pl.BlockSpec((TILE, columns), lambda i, *_: (i, 0))

    return call(
        functools.partial(attend_back_kernel, heads),
        (attention_back, out_weight, queries, keyvals, rope_keys, log_total, query_up, latent_up, *tables),
        [
            rows(width),
            full(out_weight.shape),
            rows(wide),
            full((length, wide)),
            full((length, 128)),
            pl.BlockSpec((8, TILE), lambda i, *_: (0, i)),
            full(query_up.shape),
            full(latent_up.shape),
            rows(128),
            rows(128),
            rows(128),
        ],
        [full((length, 2 * wide)), full((length, WIDE))],
        [shaped(length, 2 * wide), shaped(length, WIDE)],
        "attend_back",
        grid=(length // TILE,),
        scratch=[
            pltpu.VMEM((wide, width), BF16),
            pltpu.VMEM((wide, QR), BF16),
            pltpu.VMEM((length, wide), F32),
            pltpu.VMEM((length, 128), F32),
            pltpu.VMEM((length, QR), BF16),
        ],
        needs=needs,
    )


def add_up(got):
    total = got[0].astype(F32)
    for k in range(1, 8):
        total = total + got[k].astype(F32)
    return total


STEPS = 2


def residual_kernel(me, got, tokens, gain, residual, many):
    del me
    total = tokens[...].astype(F32) + add_up(got)
    residual[...] = total
    second_in = (total * root(total) * row(gain)).astype(BF16)
    for k in range(8):
        many[k] = second_in


def own_specs(rows, width):
    step = rows // STEPS
    return (
        pl.BlockSpec((8, step, width), lambda i, me: (0, i, 0)),
        pl.BlockSpec((step, width), lambda i, me: (i, 0)),
        pl.BlockSpec((step, width), lambda i, me: (me[0] * STEPS + i, 0)),
    )


def residual_of(me, got, tokens, gain, needs):
    width = tokens.shape[1]
    rows = tokens.shape[0] // 8
    eight, one, own = own_specs(rows, width)
    return call(
        residual_kernel,
        (got.reshape(8, rows, width), tokens, gain),
        [eight, own, full((width,))],
        [one, eight],
        [shaped(rows, width, dtype=F32), shaped(8, rows, width)],
        "residual",
        grid=(STEPS,),
        needs=needs,
        me=me,
        limit=58,
    )


def residual_back_kernel(me, got, residual, cotangent, gain, many, gain_part):
    del me
    second_back = add_up(got)
    values = residual[...]
    factor = root(values)
    normed = values * factor
    part = jnp.sum(second_back * normed, axis=0, keepdims=True)

    @pl.when(pl.program_id(0) == 0)
    def _():
        gain_part[...] = part

    @pl.when(pl.program_id(0) > 0)
    def _():
        gain_part[...] += part

    back = cotangent[...].astype(F32) + norm_back(second_back, normed, factor, row(gain))
    back = back.astype(BF16)
    for k in range(8):
        many[k] = back


def residual_back_of(me, got, residual, cotangent, gain, needs):
    rows, width = residual.shape
    eight, one, own = own_specs(rows, width)
    return call(
        residual_back_kernel,
        (got.reshape(8, rows, width), residual, cotangent, gain),
        [eight, one, own, full((width,))],
        [eight, full((1, width))],
        [shaped(8, rows, width), shaped(1, width, dtype=F32)],
        "residual_back",
        grid=(STEPS,),
        needs=needs,
        me=me,
        limit=58,
    )


def ffn_kernel(
    second_in, gate_weight, up_weight, inner_back, gate_back, up_back, inner, partial
):
    taken = second_in[...]
    gate = dot(taken, gate_weight[...], NT)
    up = dot(taken, up_weight[...], NT)
    sigma = 1.0 / (1.0 + jnp.exp(-gate))
    act = gate * sigma
    units = gate.shape[1]
    back = inner_back[...]
    of_gate = (back * up * sigma * (1.0 + gate * (1.0 - sigma))).astype(BF16)
    of_up = (back * act).astype(BF16)
    for out, values in ((gate_back, of_gate), (up_back, of_up), (inner, (act * up).astype(BF16))):
        out[:, :units] = values
        out[:, units:] = jnp.zeros((values.shape[0], out.shape[1] - units), BF16)
    partial[...] = (dot(of_gate, gate_weight[...]) + dot(of_up, up_weight[...])).astype(BF16)


def ffn(second_in, gate_weight, up_weight, inner_back, needs):
    length, width = second_in.shape
    units = gate_weight.shape[0]
    wide = -(-units // 128) * 128

    def rows(columns):
        return pl.BlockSpec((TILE, columns), lambda i, *_: (i, 0))

    return call(
        ffn_kernel,
        (second_in, gate_weight, up_weight, inner_back),
        [rows(width), full((units, width)), full((units, width)), rows(units)],
        [rows(wide), rows(wide), rows(wide), rows(width)],
        [shaped(length, wide)] * 3 + [shaped(length, width)],
        "ffn",
        grid=(length // TILE,),
        needs=needs,
    )


def ffn_down_kernel(places, inner, down_weight, residual, *refs):
    outs, total = refs[:4], refs[4]
    for i in range(2):
        rows = slice(i * TILE, i * TILE + TILE)
        total[rows, :] = dot(inner[rows, : down_weight.shape[0]], down_weight[...]).astype(BF16)
    count = residual.shape[0]
    own = pl.ds(pl.multiple_of(places[4] * count, count), count)
    total[own, :] = (total[own, :].astype(F32) + residual[...]).astype(BF16)
    for k, out in enumerate(outs):
        rows = out.shape[0]
        out[...] = total[pl.ds(pl.multiple_of(places[k] * rows, rows), rows), :]


def ffn_down(places, inner, down_weight, residual, needs):
    length, width = inner.shape[0], down_weight.shape[1]
    block = (length // 4, width)
    return call(
        ffn_down_kernel,
        (inner, down_weight, residual),
        [full(inner.shape), full(down_weight.shape), full(residual.shape)],
        [full(block)] * 4,
        [shaped(*block)] * 4,
        "ffn_down",
        scratch=[pltpu.VMEM((length, width), BF16)],
        needs=needs,
        me=places,
    )


def halves_kernel(blocks, width, starts, *refs):
    sources, outs, turned = refs[:blocks], refs[blocks : 3 * blocks], refs[3 * blocks]
    for n in range(blocks):
        source, keep, give = sources[n], outs[2 * n], outs[2 * n + 1]
        columns, each = source.shape[1], width[n]
        for c in range(0, columns, 256):
            turned[c : c + 256, :] = source[:, c : c + 256].T
        for which, out in enumerate((keep, give)):
            for k in range(8):
                first = pl.multiple_of(starts[8 * which + k] * each, 16)
                out[each * k : each * k + each, :] = turned[pl.ds(first, each), :]


def halves(starts, values, needs):
    length = values[0].shape[0]
    widths = [item.shape[1] // 16 for item in values]
    shapes = [(8 * w, length) for w in widths for _ in range(2)]
    return call(
        functools.partial(halves_kernel, len(values), widths),
        tuple(values),
        [full(item.shape) for item in values],
        [full(s) for s in shapes],
        [shaped(*s) for s in shapes],
        "halves",
        scratch=[pltpu.VMEM((max(item.shape[1] for item in values), length), BF16)],
        needs=needs,
        me=starts,
    )


ORDER = (2, 1, 3, 0)


def ffn_grads_kernel(in_keep, in_got, cot_keep, cot_got, *refs):
    ours, theirs, outs = refs[:3], refs[3:6], refs[6:]
    units = outs[0].shape[1] // 3

    def block(*parts):
        for n, (keep, got) in enumerate(((in_keep, in_got), (in_keep, in_got), (cot_keep, cot_got))):
            total = dot(keep[...], ours[n][...]) + dot(got[...], theirs[n][...])
            total = total[:, :units].astype(BF16)
            first = 0
            for out in parts:
                count = out.shape[0]
                out[:, units * n : units * n + units] = total[first : first + count]
                first += count

    for s, parts in enumerate((outs[:2], outs[2:3], outs[3:4], outs[4:])):
        pl.when(pl.program_id(0) == s)(functools.partial(block, *parts))


def ffn_grads(in_keep, in_got, cot_keep, cot_got, ours, theirs, units, needs):
    length, wide = ours[0].shape
    rows = in_keep.shape[0] // 4

    def index(i):
        return (jnp.where(i == 0, 2, jnp.where(i == 1, 1, jnp.where(i == 2, 3, 0))), 0)

    left = pl.BlockSpec((rows, length), index)
    out = (rows, 3 * units)
    outs = [(rows // 2, 3 * units)] * 2 + [out] * 3
    return call(
        ffn_grads_kernel,
        (in_keep, in_got, cot_keep, cot_got, *ours, *theirs),
        [left] * 4 + [full((length, wide))] * 6,
        [full(s) for s in outs],
        [shaped(*s) for s in outs],
        "ffn_grads",
        grid=(4,),
        needs=needs,
    )


def attn_grads_kernel(widths, *refs):
    keeps, gots, outs = refs[:3], refs[3:6], refs[10:]
    wide = outs[0].shape[1]
    ours, theirs = (
        (heads, both.at[:, :wide], both.at[:, wide:]) for heads, both in (refs[6:8], refs[8:10])
    )
    rows = sum(widths)
    for out, k in zip(outs, ORDER):
        first = 0
        for n, each in enumerate(widths):
            part = slice(2 * each * k, 2 * each * k + 2 * each)
            total = dot(keeps[n][part, :], ours[n][...]) + dot(gots[n][part, :], theirs[n][...])
            total = total.astype(BF16)
            out[first : first + each, :] = total[:each]
            out[rows + first : rows + first + each, :] = total[each:]
            first += each


def attn_grads(keeps, gots, ours, theirs, needs):
    widths = [item.shape[0] // 8 for item in keeps]
    rows, wide = sum(widths), ours[0].shape[1]
    args = (*keeps, *gots, *ours, *theirs)
    outs = [(2 * rows, wide)] * 4
    return call(
        functools.partial(attn_grads_kernel, widths),
        args,
        [full(item.shape) for item in args],
        [full(s) for s in outs],
        [shaped(*s) for s in outs],
        "attn_grads",
        needs=needs,
    )


UP = [(i, (i + 1) % 4) for i in range(4)]
DOWN = [(i, (i + 3) % 4) for i in range(4)]
ACROSS = [(i, (i + 2) % 4) for i in range(4)]


def relay_kernel(up, from_below, down, from_above, up_out, down_out):
    @pl.when(pl.program_id(0) == 0)
    def _():
        up_out[...] = (up[...].astype(F32) + from_below[...].astype(F32)).astype(BF16)
        down_out[...] = down[...]

    @pl.when(pl.program_id(0) == 1)
    def _():
        up_out[...] = up[...]
        down_out[...] = (down[...].astype(F32) + from_above[...].astype(F32)).astype(BF16)


def relay(up, from_below, down, from_above, needs):
    rows, width = from_below.shape
    half = pl.BlockSpec((rows, width), lambda i, *_: (i, 0))
    return call(
        relay_kernel,
        (up, from_below, down, from_above),
        [half, full((rows, width)), half, full((rows, width))],
        [half, half],
        [shaped(2 * rows, width)] * 2,
        "relay",
        grid=(2,),
        needs=needs,
    )


def add_chips_kernel(*refs):
    ins, keep, give = refs[:-2], refs[-2], refs[-1]
    count = len(ins) // 2
    keep[...] = sum(item[...].astype(F32) for item in ins[:count])
    give[...] = sum(item[...].astype(F32) for item in ins[count:]).astype(BF16)


def add_chips(items, needs):
    rows, width = items[0].shape[0] // 2, items[0].shape[1]
    step = rows // 2 if rows % 32 == 0 and (rows // 2) % 16 == 0 else rows
    count = rows // step
    mine = pl.BlockSpec((step, width), lambda i, *_: (i, 0))
    other = pl.BlockSpec((step, width), lambda i, *_: (i + count, 0))
    return call(
        add_chips_kernel,
        (*items, *items),
        [mine] * len(items) + [other] * len(items),
        [mine, mine],
        [shaped(rows, width, dtype=F32), shaped(rows, width)],
        "add_chips",
        grid=(count,),
        needs=needs,
    )


def add_all_kernel(*refs):
    refs[-1][...] = sum(item[...].astype(F32) for item in refs[:-1]).astype(BF16)


def add_all(items, needs):
    rows, width = items[0].shape
    half = pl.BlockSpec((rows // 2, width), lambda i, *_: (i, 0))
    return call(
        add_all_kernel,
        tuple(items),
        [half] * len(items),
        [half],
        [shaped(rows, width)],
        "add_all",
        grid=(2,),
        needs=needs,
        limit=58,
    )


def over_z(blocks):
    return [lax.ppermute(blocks[k], "z", [(i, i ^ k) for i in range(4)]) for k in (1, 2, 3)]


def assemble_kernel(places, *refs):
    del places
    for k in range(4):

        @pl.when(pl.program_id(0) == k)
        def _(k=k):
            refs[4][...] = refs[k][...]


def assemble(places, blocks):
    rows, width = blocks[0].shape
    return call(
        assemble_kernel,
        tuple(blocks),
        [full((rows, width))] * 4,
        [pl.BlockSpec((rows, width), lambda i, places: (places[i], 0))],
        [shaped(4 * rows, width)],
        "assemble",
        grid=(4,),
        me=places,
    )[0][0]


def over_cores(values):
    return lax.ppermute(values, "core", SWAP)


def latents_back_kernel(
    me, got, latents, query_gain, latent_gain, keep, low, high, many, own, gain_part, turns, sems
):
    rows = own.shape[0]
    here = pl.ds(pl.multiple_of(me[0] * rows, rows), rows)
    copies = [
        pltpu.make_async_copy(table.at[here, :], turns.at[n], sems.at[n])
        for n, table in enumerate((keep, low, high))
    ]
    for copy in copies:
        copy.start()
    total = add_up(got)
    for copy in copies:
        copy.wait()

    def back(lanes, gain):
        upstream, values = total[:, lanes], latents[:, lanes]
        factor = root(values)
        normed = values * factor
        gain_part[:, lanes] = jnp.sum(upstream * normed, axis=0, keepdims=True)
        return norm_back(upstream, normed, factor, row(gain)).astype(BF16)

    own[:, :QR] = back(slice(0, QR), query_gain)
    own[:, QR:LAT] = back(slice(QR, LAT), latent_gain)
    own[:, LAT:] = turn(total[:, LAT:], turns[0], turns[1], turns[2], back=True).astype(BF16)
    for k in range(8):
        many[k] = own[...]


def latents_back_of(me, got, latents, query_gain, latent_gain, tables, needs):
    rows = latents.shape[0]
    return call(
        latents_back_kernel,
        (got.reshape(8, rows, WIDE), latents, query_gain, latent_gain, *tables),
        [full((8, rows, WIDE)), full(latents.shape), full((QR,)), full((KVR,)), HBM, HBM, HBM],
        [full((8, rows, WIDE)), full((rows, WIDE)), full((1, LAT))],
        [shaped(8, rows, WIDE), shaped(rows, WIDE), shaped(1, LAT, dtype=F32)],
        "latents_back",
        scratch=[
            pltpu.VMEM((3, rows, 128), F32),
            pltpu.SemaphoreType.DMA((3,)),
        ],
        needs=needs,
        me=me,
        limit=24,
    )


def first_back_of(raw_back, query_down, latent_down, rope_down):
    rope_down[...] = jnp.zeros_like(rope_down)
    rope_down[64:96, :] = latent_down[KVR:, :]
    return (
        dot(raw_back[:, :QR], query_down[...], NT)
        + dot(raw_back[:, QR:LAT], latent_down[:KVR, :])
        + dot(raw_back[:, LAT:], rope_down[...])
    )


def first_gain_kernel(
    me, raw_back, tokens, query_down, latent_down, gain_part, rope_down, own, sem
):
    rows = own.shape[0]
    here = pl.ds(pl.multiple_of(me[0] * rows, rows), rows)
    copy = pltpu.make_async_copy(tokens.at[here, :], own, sem)
    copy.start()
    first_back = first_back_of(raw_back, query_down, latent_down, rope_down)
    copy.wait()
    values = own[...].astype(F32)
    gain_part[...] = jnp.sum(first_back * (values * root(values)), axis=0, keepdims=True)


def first_gain_of(me, own_raw_back, tokens, query_down, latent_down, needs):
    width = tokens.shape[1]
    return call(
        first_gain_kernel,
        (own_raw_back, tokens, query_down, latent_down.T),
        [full(own_raw_back.shape), HBM, full(query_down.shape), full(latent_down.shape[::-1])],
        [full((1, width))],
        [shaped(1, width, dtype=F32)],
        "first_gain",
        scratch=[
            pltpu.VMEM((128, width), BF16),
            pltpu.VMEM((own_raw_back.shape[0], width), BF16),
            pltpu.SemaphoreType.DMA,
        ],
        needs=needs,
        me=me,
    )


def tokens_back_kernel(
    raw_back, tokens, attention_back, query_down, latent_down, gain, tokens_grad, rope_down
):
    first_back = first_back_of(raw_back, query_down, latent_down, rope_down)
    values = tokens[...].astype(F32)
    factor = root(values)
    tokens_grad[...] = attention_back[...].astype(F32) + norm_back(
        first_back, values * factor, factor, row(gain)
    )


def tokens_back_of(raw_back, tokens, attention_back, query_down, latent_down, gain, needs):
    length, width = tokens.shape

    def rows(columns):
        return pl.BlockSpec((TILE, columns), lambda i, *_: (i, 0))

    return call(
        tokens_back_kernel,
        (raw_back, tokens, attention_back, query_down, latent_down.T, gain),
        [
            rows(WIDE),
            rows(width),
            rows(width),
            full(query_down.shape),
            full(latent_down.shape[::-1]),
            full((width,)),
        ],
        [rows(width)],
        [shaped(length, width, dtype=F32)],
        "tokens_back",
        grid=(length // TILE,),
        scratch=[pltpu.VMEM((128, width), BF16)],
        needs=needs,
    )


def finish_ffn_kernel(keep, got, gate, up, down):
    units = gate.shape[1]
    for n, out in enumerate((gate, up, down)):
        lanes = slice(units * n, units * n + units)
        out[...] = keep[:, lanes] + got[:, lanes].astype(F32)


def finish_ffn(keep, got, needs):
    rows, width = keep.shape
    out = (rows, width // 3)
    return call(
        finish_ffn_kernel,
        (keep, got),
        [full(keep.shape), full(got.shape)],
        [full(out)] * 3,
        [shaped(*out, dtype=F32)] * 3,
        "finish_ffn",
        needs=needs,
    )


def finish_attn_kernel(heads, keep, got, out_grad, query_grad, latent_grad):
    total = keep[...] + got[...].astype(F32)
    for h in range(heads):
        lanes = slice(128 * h, 128 * h + 128)
        out_grad[:, 64 * h : 64 * h + 64] = total[:160, 128 * h + 64 : 128 * h + 128]
        query_grad[:, 96 * h : 96 * h + 96] = total[160:208, 128 * h : 128 * h + 96]
    latent_grad[...] = total[208:224]


def finish_attn(keep, got, needs):
    heads = keep.shape[1] // 128
    outs = [(160, 64 * heads), (48, 96 * heads), (16, 128 * heads)]
    return call(
        functools.partial(finish_attn_kernel, heads),
        (keep, got),
        [full(keep.shape), full(got.shape)],
        [full(s) for s in outs],
        [shaped(*s, dtype=F32) for s in outs],
        "finish_attn",
        needs=needs,
    )


GAINS = ((0, 160), (160, 160), (320, 48), (368, 16))


def down_parts_kernel(own_in, raw_back, gains, out):
    total = dot(own_in[...], raw_back[...]).astype(BF16)
    for d in range(16):
        out[d, :20, :] = total[20 * d : 20 * d + 20]
        out[d, 20:, :] = jnp.zeros((4, WIDE), BF16)
        out[d, 20:21, :] = gains[d : d + 1, :]


def down_parts(own_in, raw_back, gains, needs):
    args = (own_in, raw_back, gains)
    return call(
        down_parts_kernel,
        args,
        [full(item.shape) for item in args],
        [full((16, 24, WIDE))],
        [shaped(16, 24, WIDE)],
        "down_parts",
        needs=needs,
        limit=24,
    )


def sum_copies_kernel(got, many):
    total = got[0].astype(F32)
    for d in range(1, 16):
        total = total + got[d].astype(F32)
    for k in range(8):
        many[k] = total.astype(BF16)


def sum_copies(got, needs):
    return call(
        sum_copies_kernel,
        (got,),
        [full(got.shape)],
        [full((8, 24, WIDE))],
        [shaped(8, 24, WIDE)],
        "sum_copies",
        needs=needs,
        limit=24,
    )


def finish_down_kernel(everyone, query_grad, latent_grad, *gains):
    for t in range(8):
        values = everyone[t].astype(F32)
        query_grad[20 * t : 20 * t + 20, :] = values[:20, :QR]
        latent_grad[20 * t : 20 * t + 20, :KVR] = values[:20, QR:LAT]
        latent_grad[20 * t : 20 * t + 20, KVR:] = values[:20, LAT + 64 : LAT + 96]
    total = sum(everyone[t, 16:24, :].astype(F32) for t in range(8))[4:5, :]
    for out, (first, count) in zip(gains, GAINS):
        out[...] = total[:, first : first + count]


def finish_down(everyone):
    everyone = everyone.reshape(8, 24, WIDE)
    outs = [(160, QR), (160, KVR + ROPE)] + [(1, count) for _, count in GAINS]
    return call(
        finish_down_kernel,
        (everyone,),
        [full(everyone.shape)],
        [full(s) for s in outs],
        [shaped(*s, dtype=F32) for s in outs],
        "finish_down",
        limit=24,
    )[0]


def exchange(blocks):
    return lax.all_to_all(blocks.reshape(-1, blocks.shape[-1]), TP, 0, 0, tiled=True)


def on_device(
    tokens,
    first_gain,
    query_down,
    query_gain,
    query_up,
    latent_down,
    latent_gain,
    latent_up,
    out_weight,
    second_gain,
    gate_weight,
    up_weight,
    down_weight,
    cotangent,
):
    length = tokens.shape[0]
    me = lax.axis_index(TP).astype(jnp.int32).reshape(1)
    y, xl, core = lax.axis_index("y"), lax.axis_index("xl"), lax.axis_index("core")
    starts = jnp.stack(
        [
            ((y + k) % 4 * 2 + (xl ^ j)) * 2 + c
            for c in (core, 1 - core)
            for k in range(4)
            for j in range(2)
        ]
    ).astype(jnp.int32)
    places = jnp.stack([lax.axis_index("z") ^ k for k in range(4)] + [me[0]]).astype(jnp.int32)
    tables = rope_tables(length)

    gate_turned, up_turned = gate_weight.T, up_weight.T

    (
        first_in,
        latents,
        query_code,
        latent_code,
        queries,
        keyvals,
        rope_keys,
        heads_out,
        log_total,
        attn_partial,
    ), started = attend(
        me,
        tokens,
        first_gain,
        query_down,
        latent_down,
        query_gain,
        latent_gain,
        query_up,
        latent_up,
        out_weight,
        tables,
    )
    attn_got = exchange(attn_partial)

    (cot_keep, cot_give), picked = halves(starts, [cotangent], [started])
    inner_back = dot(cotangent, down_weight, NT)
    cot_got = over_cores(cot_give)

    (residual, second_many), _ = residual_of(
        me, attn_got, tokens, second_gain, [picked, cot_got]
    )
    second_in = exchange(second_many)

    turned_in = first_in.T.reshape(16, 8, 20, length)
    own_in = lax.dynamic_slice_in_dim(turned_in, me[0], 1, 1).reshape(320, length)
    (code_keep, code_give, lat_keep, lat_give), picked = halves(
        starts, [query_code, latent_code], [residual]
    )
    code_got, lat_got = over_cores(code_give), over_cores(lat_give)
    heads_got = over_cores(heads_out)

    (gate_back, up_back, inner, back_partial), done = ffn(
        second_in, gate_turned, up_turned, inner_back, [picked, own_in, code_got, lat_got, heads_got]
    )
    back_got = exchange(back_partial)

    ours = (gate_back, up_back, inner)
    theirs = [over_cores(item) for item in ours]
    (in_keep, in_give), _ = halves(starts, [second_in], [done])
    in_got = over_cores(in_give)
    (far_up, far_down, ffn_up, ffn_down_way, ffn_own), done = ffn_grads(in_keep, in_got, cot_keep, cot_got, ours, theirs, gate_weight.shape[1], [])
    below, above = lax.ppermute(far_up, "y", UP), lax.ppermute(far_down, "y", DOWN)

    (back_many, second_gain_part), done = residual_back_of(
        me, back_got, residual, cotangent, second_gain, [done]
    )
    attention_back = exchange(back_many)
    mixed_blocks, done = ffn_down(places, inner, down_weight, residual, [done])
    mixed_got = over_z(mixed_blocks)
    (ffn_up, ffn_down_way), done = relay(ffn_up, below, ffn_down_way, above, [done])
    below, above = lax.ppermute(ffn_up, "y", UP), lax.ppermute(ffn_down_way, "y", DOWN)

    (both_back, latents_partial), back_done = attend_back(
        attention_back,
        out_weight,
        queries,
        keyvals,
        rope_keys,
        log_total,
        query_up,
        latent_up,
        tables,
        [done],
    )
    latents_got = exchange(latents_partial)

    (out_keep, out_give), picked = halves(starts, [attention_back], [back_done])
    (ffn_keep, ffn_give), done = add_chips([ffn_own, below, above], [back_done])
    ffn_got = lax.ppermute(ffn_give, "xl", SWAP)

    (raw_many, own_raw, latent_gain_parts), done = latents_back_of(
        me, latents_got, latents, query_gain, latent_gain, tables, [done, picked]
    )
    raw_back = exchange(raw_many)

    (mixed_part,), done = add_all([mixed_blocks[0], *mixed_got], [done])
    mixed_other = lax.ppermute(mixed_part, "xh", SWAP)

    out_got, both_got = over_cores(out_give), over_cores(both_back)
    (attn_across, attn_up, attn_down, attn_own), done = attn_grads(
        (out_keep, code_keep, lat_keep),
        (out_got, code_got, lat_got),
        (heads_out, both_back),
        (heads_got, both_got),
        [done],
    )
    attn_got = [
        lax.ppermute(attn_across, "y", ACROSS),
        lax.ppermute(attn_up, "y", UP),
        lax.ppermute(attn_down, "y", DOWN),
    ]
    (mixed_part,), done = add_all([mixed_part, mixed_other], [done])
    (first_gain_part,), gain_done = first_gain_of(
        me, own_raw, tokens, query_down, latent_down, [done]
    )


    gains = jnp.concatenate(
        [
            first_gain_part.reshape(16, -1),
            second_gain_part.reshape(16, -1),
            latent_gain_parts[0, :QR].reshape(16, -1),
            latent_gain_parts[0, QR:].reshape(16, -1),
        ],
        axis=1,
    ).astype(BF16)
    gains = jnp.pad(gains, ((0, 0), (0, WIDE - gains.shape[1])))
    (parts,), done = down_parts(own_in, raw_back, gains, [attn_got[1], attn_got[2]])
    parts_got = lax.all_to_all(parts, DP, 0, 0, tiled=True)

    (tokens_grad,), done = tokens_back_of(
        raw_back, tokens, attention_back, query_down, latent_down, first_gain, [done]
    )
    (many,), summed = sum_copies(parts_got, [done])
    everyone = exchange(many)

    (attn_keep, attn_give), done = add_chips([attn_own, *attn_got], [summed])
    attn_other = lax.ppermute(attn_give, "xl", SWAP)
    (gate_weight_grad, up_weight_grad, down_weight_grad), done = finish_ffn(
        ffn_keep, ffn_got, [done]
    )
    (out_weight_grad, query_up_grad, latent_up_grad), done = finish_attn(
        attn_keep, attn_other, [done]
    )
    (
        query_down_grad,
        latent_down_grad,
        first_gain_grad,
        second_gain_grad,
        query_gain_grad,
        latent_gain_grad,
    ) = finish_down(everyone)

    mixed = assemble(places, [mixed_part, *over_z([mixed_part] * 4)])

    return (
        mixed,
        tokens_grad,
        first_gain_grad[0],
        query_down_grad,
        query_gain_grad[0],
        query_up_grad,
        latent_down_grad,
        latent_gain_grad[0],
        latent_up_grad,
        out_weight_grad.T,
        second_gain_grad[0],
        gate_weight_grad,
        up_weight_grad,
        down_weight_grad.T,
    )


def solution(mesh):
    grid = Mesh(mesh.devices.reshape(4, 2, 2, 2, 4), ("y", "xl", "core", "xh", "z"))
    in_specs = (
        P(DP, None),
        P(),
        P(),
        P(),
        P(None, TP),
        P(),
        P(),
        P(None, TP),
        P(TP, None),
        P(),
        P(None, TP),
        P(None, TP),
        P(TP, None),
        P(DP, None),
    )
    out_specs = (
        P(DP, None),
        P(DP, None),
        P(DP),
        P(DP, None),
        P(DP),
        P(DP, TP),
        P(DP, None),
        P(DP),
        P(DP, TP),
        P(TP, DP),
        P(DP),
        P(DP, TP),
        P(DP, TP),
        P(TP, DP),
    )
    return jax.shard_map(
        on_device, mesh=grid, in_specs=in_specs, out_specs=out_specs, check_vma=False
    )
```

```python
import functools

import jax
import jax.numpy as jnp
import numpy as np
from jax import lax
from jax.experimental import pallas as pl
from jax.experimental.pallas import tpu as pltpu
from jax.sharding import Mesh, PartitionSpec as P

NOPE = 64
ROPE = 32
DV = 64
KVR = 256
QR = 768
LAT = QR + KVR
WIDE = LAT + 128

EPS = 1e-05
BASE = 10000.0
SCALE = (NOPE + ROPE) ** (-0.5)

DP = ("y", "xl", "core")
TP = ("xh", "z")
SWAP = [(0, 1), (1, 0)]
F32 = jnp.float32
BF16 = jnp.bfloat16
NT = (((1,), (1,)), ((), ()))
TN = (((0,), (0,)), ((), ()))
NN = (((1,), (0,)), ((), ()))
TILE = 256


def dot(left, right, dims=NN):
    return lax.dot_general(left, right, dims, preferred_element_type=F32)


def params(limit=56):
    return pltpu.CompilerParams(vmem_limit_bytes=limit * 2**20)


HBM = pl.BlockSpec(memory_space=pltpu.HBM)


def call(kernel, args, in_specs, out_specs, out_shape, name, grid=(1,), scratch=(), needs=(), me=None, limit=60):
    first = 0 if me is None else 1
    n_in, n_out = len(args), len(out_shape)

    def body(*refs):
        ins = refs[: first + n_in]
        rest = refs[first + n_in + len(needs) :]
        mark = rest[n_out]

        @pl.when(pl.program_id(0) == 0)
        def _():
            mark[...] = jnp.zeros_like(mark)

        kernel(*ins, *rest[:n_out], *rest[n_out + 1 :])

    *outs, mark = pl.pallas_call(
        body,
        grid_spec=pltpu.PrefetchScalarGridSpec(
            num_scalar_prefetch=first,
            grid=grid,
            in_specs=list(in_specs) + [HBM] * len(needs),
            out_specs=list(out_specs) + [full((8, 128))],
            scratch_shapes=list(scratch),
        ),
        out_shape=list(out_shape) + [jax.ShapeDtypeStruct((8, 128), F32)],
        compiler_params=params(limit),
        cost_estimate=pl.CostEstimate(flops=1, bytes_accessed=1, transcendentals=0),
        name=name,
    )(*(() if me is None else (me,)), *args, *needs)
    return outs, mark


def shaped(*shape, dtype=BF16):
    return jax.ShapeDtypeStruct(shape, dtype)


def full(shape):
    return pl.BlockSpec(shape, lambda *_: (0,) * len(shape))


def rope_tables(length):
    half = ROPE // 2
    rates = np.exp(np.arange(half, dtype=np.float32) * np.float32(-2.0 * np.log(BASE) / ROPE))
    angles = np.arange(length, dtype=np.float32)[:, None] * rates.astype(np.float32)[None, :]
    cosine, sine = np.cos(angles), np.sin(angles)
    keep = np.zeros((length, 128), np.float32)
    keep[:, :NOPE] = 1.0
    keep[:, 64:80] = cosine
    keep[:, 80:96] = cosine
    low = np.zeros((length, 128), np.float32)
    low[:, 64:80] = -sine
    high = np.zeros((length, 128), np.float32)
    high[:, 80:96] = sine
    return jnp.asarray(keep), jnp.asarray(low), jnp.asarray(high)


def turn(values, keep, low, high, back=False):
    moved = pltpu.roll(values, 112, 1) * low + pltpu.roll(values, 16, 1) * high
    return values * keep - moved if back else values * keep + moved


def root(values):
    return lax.rsqrt(jnp.mean(values * values, axis=-1, keepdims=True) + EPS)


def norm_back(upstream, normed, factor, gain):
    scaled = upstream * gain
    return factor * (scaled - normed * jnp.mean(scaled * normed, axis=-1, keepdims=True))


def spread_out_weight(weight_ref, spread_ref, heads):
    spread_ref[...] = jnp.zeros_like(spread_ref)
    for h in range(heads):
        spread_ref[128 * h + 64 : 128 * h + 128, :] = weight_ref[64 * h : 64 * h + 64, :]


def spread_query_up(weight_ref, spread_ref, heads):
    spread_ref[...] = jnp.zeros_like(spread_ref)
    for h in range(heads):
        spread_ref[128 * h : 128 * h + 96, :] = weight_ref[96 * h : 96 * h + 96, :]


def row(ref):
    return ref[...].reshape(1, -1)


def low_lanes(shape):
    return lax.broadcasted_iota(jnp.int32, shape, 1) < NOPE


def causal(keys, queries, first_query):
    key_ids = lax.broadcasted_iota(jnp.int32, (keys, queries), 0)
    query_ids = lax.broadcasted_iota(jnp.int32, (keys, queries), 1) + first_query
    return key_ids <= query_ids


def attend_kernel(
    heads,
    me,
    tokens,
    first_gain,
    query_down,
    latent_down,
    query_gain,
    latent_gain,
    query_up,
    latent_up,
    out_weight,
    keep,
    low,
    high,
    first_in,
    latents,
    query_code,
    latent_code,
    queries,
    keyvals,
    rope_keys,
    heads_out,
    log_total,
    partial,
    raw_latents,
    spread,
    spread_up,
    rope_down,
    kv_all,
    rope_all,
):
    step = pl.program_id(0)

    @pl.when(step == 0)
    def _():
        spread_out_weight(out_weight, spread, heads)
        spread_query_up(query_up, spread_up, heads)
        rope_down[...] = jnp.zeros_like(rope_down)
        rope_down[64:96, :] = latent_down[KVR:, :]

    def rows_of(index, carry):
        rows = pl.ds(pl.multiple_of(index * 32, 32), 32)
        values = tokens[rows, :].astype(F32)
        first_in[rows, :] = (values * root(values) * row(first_gain)).astype(BF16)
        return carry

    lax.fori_loop(0, TILE // 32, rows_of, 0)
    taken = first_in[...]
    query_latent = dot(taken, query_down[...])
    raw_latents[:, :QR] = query_latent
    code = (query_latent * root(query_latent) * row(query_gain)).astype(BF16)
    query_code[...] = code
    latent = dot(taken, latent_down[:KVR, :], NT)
    raw_latents[:, QR:] = latent
    count = latents.shape[0]
    own = me[0] * count

    @pl.when(own // TILE == step)
    def _():
        latents[...] = raw_latents[pl.ds(pl.multiple_of(own % TILE, count), count), :]

    lcode = (latent * root(latent) * row(latent_gain)).astype(BF16)
    latent_code[...] = lcode
    tables = keep[...], low[...], high[...]
    rope = turn(dot(taken, rope_down[...], NT), *tables).astype(BF16)
    rope_keys[...] = rope
    here = pl.ds(pl.multiple_of(step * TILE, TILE), TILE)
    rope_all[here, :] = rope
    kv = dot(lcode, latent_up[...]).astype(BF16)
    keyvals[...] = kv
    kv_all[here, :] = kv
    raw = dot(code, spread_up[...], NT)
    for h in range(heads):
        lanes = slice(128 * h, 128 * h + 128)
        queries[:, lanes] = turn(raw[:, lanes], *tables).astype(BF16)

    def tile(index):
        keys = TILE * (index + 1)
        for h in range(heads):
            lanes = slice(128 * h, 128 * h + 128)
            kv_h = kv_all[:keys, lanes]
            key = jnp.where(low_lanes((keys, 128)), kv_h, rope_all[:keys, :])
            scores = dot(key, queries[:, lanes], NT) * SCALE
            scores = jnp.where(causal(keys, TILE, TILE * index), scores, -1e30)
            top = jnp.max(scores, axis=0, keepdims=True)
            weights = jnp.exp(scores - top)
            total = jnp.sum(weights, axis=0, keepdims=True)
            log_total[h : h + 1, :] = top + jnp.log(total)
            probs = (weights * (1.0 / total)).astype(BF16)
            heads_out[:, lanes] = dot(probs, kv_h, TN).astype(BF16)

    for index in range(2):
        pl.when(step == index)(functools.partial(tile, index))
    partial[...] = dot(heads_out[...], spread[...]).astype(BF16)


def attend(me, tokens, first_gain, query_down, latent_down, query_gain, latent_gain, query_up, latent_up, out_weight, tables):
    latent_down, query_up = latent_down.T, query_up.T
    length, width = tokens.shape
    heads = out_weight.shape[0] // DV
    wide = 128 * heads

    def rows(columns):
        return pl.BlockSpec((TILE, columns), lambda i, *_: (i, 0))

    return call(
        functools.partial(attend_kernel, heads),
        (tokens, first_gain, query_down, latent_down, query_gain, latent_gain, query_up, latent_up, out_weight, *tables),
        [
            rows(width),
            full((width,)),
            full(query_down.shape),
            full(latent_down.shape),
            full((QR,)),
            full((KVR,)),
            full(query_up.shape),
            full(latent_up.shape),
            full(out_weight.shape),
            rows(128),
            rows(128),
            rows(128),
        ],
        [
            rows(width),
            full((length // 8, LAT)),
            rows(QR),
            rows(KVR),
            rows(wide),
            rows(wide),
            rows(128),
            rows(wide),
            pl.BlockSpec((8, TILE), lambda i, *_: (0, i)),
            rows(width),
        ],
        [
            shaped(length, width),
            shaped(length // 8, LAT, dtype=F32),
            shaped(length, QR),
            shaped(length, KVR),
            shaped(length, wide),
            shaped(length, wide),
            shaped(length, 128),
            shaped(length, wide),
            shaped(8, length, dtype=F32),
            shaped(length, width),
        ],
        "attend",
        grid=(length // TILE,),
        me=me,
        scratch=[
            pltpu.VMEM((TILE, LAT), F32),
            pltpu.VMEM((wide, width), BF16),
            pltpu.VMEM((wide, QR), BF16),
            pltpu.VMEM((128, width), BF16),
            pltpu.VMEM((length, wide), BF16),
            pltpu.VMEM((length, 128), BF16),
        ],
    )


def attend_back_kernel(
    heads,
    attention_back,
    out_weight,
    queries,
    keyvals,
    rope_keys,
    log_total,
    query_up,
    latent_up,
    keep,
    low,
    high,
    both_back,
    partial,
    spread,
    spread_up,
    kv_grad,
    rope_grad,
    code_grad,
):
    step = pl.program_id(0)

    @pl.when(step == 0)
    def _():
        spread_out_weight(out_weight, spread, heads)
        spread_query_up(query_up, spread_up, heads)
        kv_grad[...] = jnp.zeros_like(kv_grad)
        rope_grad[...] = jnp.zeros_like(rope_grad)

    heads_back = dot(attention_back[...], spread[...], NT).astype(BF16)
    tables = keep[...], low[...], high[...]

    def tile(index):
        keys = TILE * (index + 1)
        low_part = low_lanes((keys, 128))
        for h in range(heads):
            lanes = slice(128 * h, 128 * h + 128)
            kv_h = keyvals[:keys, lanes]
            key = jnp.where(low_part, kv_h, rope_keys[:keys, :])
            query = queries[:, lanes]
            back = heads_back[:, lanes]
            scores = dot(key, query, NT) * SCALE
            probs = jnp.exp(scores - log_total[h : h + 1, :])
            probs = jnp.where(causal(keys, TILE, TILE * index), probs, 0.0)
            prob_back = dot(kv_h, back, NT)
            mean = jnp.sum(probs * prob_back, axis=0, keepdims=True)
            score_back = (probs * (prob_back - mean)).astype(BF16)
            of_values = dot(probs.astype(BF16), back)
            of_keys = dot(score_back, query) * SCALE
            kv_grad[:keys, lanes] += of_values + jnp.where(low_part, of_keys, 0.0)
            rope_grad[:keys, :] += jnp.where(low_part, 0.0, of_keys)
            of_query = dot(score_back, key, TN) * SCALE
            both_back[here, lanes] = turn(of_query, *tables, back=True).astype(BF16)

    wide = 128 * heads
    here = pl.ds(pl.multiple_of(step * TILE, TILE), TILE)
    for index in range(2):
        pl.when(step == index)(functools.partial(tile, index))
    code_grad[here, :] = dot(both_back[here, :wide], spread_up[...]).astype(BF16)

    @pl.when(step == 1)
    def _():
        kv = kv_grad[...].astype(BF16)
        both_back[:, wide:] = kv
        partial[:, :QR] = code_grad[...]
        partial[:, QR:LAT] = dot(kv, latent_up[...], NT).astype(BF16)
        partial[:, LAT:] = rope_grad[...].astype(BF16)


def attend_back(attention_back, out_weight, queries, keyvals, rope_keys, log_total, query_up, latent_up, tables, needs):
    query_up = query_up.T
    length, width = attention_back.shape
    heads = out_weight.shape[0] // DV
    wide = 128 * heads

    def rows(columns):
        return pl.BlockSpec((TILE, columns), lambda i, *_: (i, 0))

    return call(
        functools.partial(attend_back_kernel, heads),
        (attention_back, out_weight, queries, keyvals, rope_keys, log_total, query_up, latent_up, *tables),
        [
            rows(width),
            full(out_weight.shape),
            rows(wide),
            full((length, wide)),
            full((length, 128)),
            pl.BlockSpec((8, TILE), lambda i, *_: (0, i)),
            full(query_up.shape),
            full(latent_up.shape),
            rows(128),
            rows(128),
            rows(128),
        ],
        [full((length, 2 * wide)), full((length, WIDE))],
        [shaped(length, 2 * wide), shaped(length, WIDE)],
        "attend_back",
        grid=(length // TILE,),
        scratch=[
            pltpu.VMEM((wide, width), BF16),
            pltpu.VMEM((wide, QR), BF16),
            pltpu.VMEM((length, wide), F32),
            pltpu.VMEM((length, 128), F32),
            pltpu.VMEM((length, QR), BF16),
        ],
        needs=needs,
    )


def add_up(got):
    total = got[0].astype(F32)
    for k in range(1, 8):
        total = total + got[k].astype(F32)
    return total


STEPS = 2


def residual_kernel(me, got, tokens, gain, residual, many):
    del me
    total = tokens[...].astype(F32) + add_up(got)
    residual[...] = total
    second_in = (total * root(total) * row(gain)).astype(BF16)
    for k in range(8):
        many[k] = second_in


def own_specs(rows, width):
    step = rows // STEPS
    return (
        pl.BlockSpec((8, step, width), lambda i, me: (0, i, 0)),
        pl.BlockSpec((step, width), lambda i, me: (i, 0)),
        pl.BlockSpec((step, width), lambda i, me: (me[0] * STEPS + i, 0)),
    )


def residual_of(me, got, tokens, gain, needs):
    width = tokens.shape[1]
    rows = tokens.shape[0] // 8
    eight, one, own = own_specs(rows, width)
    return call(
        residual_kernel,
        (got.reshape(8, rows, width), tokens, gain),
        [eight, own, full((width,))],
        [one, eight],
        [shaped(rows, width, dtype=F32), shaped(8, rows, width)],
        "residual",
        grid=(STEPS,),
        needs=needs,
        me=me,
        limit=58,
    )


def residual_back_kernel(me, got, residual, cotangent, gain, many, gain_part):
    del me
    second_back = add_up(got)
    values = residual[...]
    factor = root(values)
    normed = values * factor
    part = jnp.sum(second_back * normed, axis=0, keepdims=True)

    @pl.when(pl.program_id(0) == 0)
    def _():
        gain_part[...] = part

    @pl.when(pl.program_id(0) > 0)
    def _():
        gain_part[...] += part

    back = cotangent[...].astype(F32) + norm_back(second_back, normed, factor, row(gain))
    back = back.astype(BF16)
    for k in range(8):
        many[k] = back


def residual_back_of(me, got, residual, cotangent, gain, needs):
    rows, width = residual.shape
    eight, one, own = own_specs(rows, width)
    return call(
        residual_back_kernel,
        (got.reshape(8, rows, width), residual, cotangent, gain),
        [eight, one, own, full((width,))],
        [eight, full((1, width))],
        [shaped(8, rows, width), shaped(1, width, dtype=F32)],
        "residual_back",
        grid=(STEPS,),
        needs=needs,
        me=me,
        limit=58,
    )


def ffn_kernel(
    second_in, gate_weight, up_weight, inner_back, gate_back, up_back, inner, partial
):
    taken = second_in[...]
    gate = dot(taken, gate_weight[...], NT)
    up = dot(taken, up_weight[...], NT)
    sigma = 1.0 / (1.0 + jnp.exp(-gate))
    act = gate * sigma
    units = gate.shape[1]
    back = inner_back[...]
    of_gate = (back * up * sigma * (1.0 + gate * (1.0 - sigma))).astype(BF16)
    of_up = (back * act).astype(BF16)
    for out, values in ((gate_back, of_gate), (up_back, of_up), (inner, (act * up).astype(BF16))):
        out[:, :units] = values
        out[:, units:] = jnp.zeros((values.shape[0], out.shape[1] - units), BF16)
    partial[...] = (dot(of_gate, gate_weight[...]) + dot(of_up, up_weight[...])).astype(BF16)


def ffn(second_in, gate_weight, up_weight, inner_back, needs):
    length, width = second_in.shape
    units = gate_weight.shape[0]
    wide = -(-units // 128) * 128

    def rows(columns):
        return pl.BlockSpec((TILE, columns), lambda i, *_: (i, 0))

    return call(
        ffn_kernel,
        (second_in, gate_weight, up_weight, inner_back),
        [rows(width), full((units, width)), full((units, width)), rows(units)],
        [rows(wide), rows(wide), rows(wide), rows(width)],
        [shaped(length, wide)] * 3 + [shaped(length, width)],
        "ffn",
        grid=(length // TILE,),
        needs=needs,
    )


def ffn_down_kernel(places, inner, down_weight, residual, *refs):
    outs, total = refs[:4], refs[4]
    for i in range(2):
        rows = slice(i * TILE, i * TILE + TILE)
        total[rows, :] = dot(inner[rows, : down_weight.shape[0]], down_weight[...]).astype(BF16)
    count = residual.shape[0]
    own = pl.ds(pl.multiple_of(places[4] * count, count), count)
    total[own, :] = (total[own, :].astype(F32) + residual[...]).astype(BF16)
    for k, out in enumerate(outs):
        rows = out.shape[0]
        out[...] = total[pl.ds(pl.multiple_of(places[k] * rows, rows), rows), :]


def ffn_down(places, inner, down_weight, residual, needs):
    length, width = inner.shape[0], down_weight.shape[1]
    block = (length // 4, width)
    return call(
        ffn_down_kernel,
        (inner, down_weight, residual),
        [full(inner.shape), full(down_weight.shape), full(residual.shape)],
        [full(block)] * 4,
        [shaped(*block)] * 4,
        "ffn_down",
        scratch=[pltpu.VMEM((length, width), BF16)],
        needs=needs,
        me=places,
    )


def halves_kernel(blocks, width, starts, *refs):
    sources, outs, turned = refs[:blocks], refs[blocks : 3 * blocks], refs[3 * blocks]
    for n in range(blocks):
        source, keep, give = sources[n], outs[2 * n], outs[2 * n + 1]
        columns, each = source.shape[1], width[n]
        for c in range(0, columns, 256):
            turned[c : c + 256, :] = source[:, c : c + 256].T
        for which, out in enumerate((keep, give)):
            for k in range(8):
                first = pl.multiple_of(starts[8 * which + k] * each, 16)
                out[each * k : each * k + each, :] = turned[pl.ds(first, each), :]


def halves(starts, values, needs):
    length = values[0].shape[0]
    widths = [item.shape[1] // 16 for item in values]
    shapes = [(8 * w, length) for w in widths for _ in range(2)]
    return call(
        functools.partial(halves_kernel, len(values), widths),
        tuple(values),
        [full(item.shape) for item in values],
        [full(s) for s in shapes],
        [shaped(*s) for s in shapes],
        "halves",
        scratch=[pltpu.VMEM((max(item.shape[1] for item in values), length), BF16)],
        needs=needs,
        me=starts,
    )


ORDER = (2, 1, 3, 0)


def ffn_grads_kernel(in_keep, in_got, cot_keep, cot_got, *refs):
    ours, theirs, outs = refs[:3], refs[3:6], refs[6:]
    units = outs[0].shape[1] // 3

    def block(*parts):
        for n, (keep, got) in enumerate(((in_keep, in_got), (in_keep, in_got), (cot_keep, cot_got))):
            total = dot(keep[...], ours[n][...]) + dot(got[...], theirs[n][...])
            total = total[:, :units].astype(BF16)
            first = 0
            for out in parts:
                count = out.shape[0]
                out[:, units * n : units * n + units] = total[first : first + count]
                first += count

    for s, parts in enumerate((outs[:2], outs[2:3], outs[3:4], outs[4:])):
        pl.when(pl.program_id(0) == s)(functools.partial(block, *parts))


def ffn_grads(in_keep, in_got, cot_keep, cot_got, ours, theirs, units, needs):
    length, wide = ours[0].shape
    rows = in_keep.shape[0] // 4

    def index(i):
        return (jnp.where(i == 0, 2, jnp.where(i == 1, 1, jnp.where(i == 2, 3, 0))), 0)

    left = pl.BlockSpec((rows, length), index)
    out = (rows, 3 * units)
    outs = [(rows // 2, 3 * units)] * 2 + [out] * 3
    return call(
        ffn_grads_kernel,
        (in_keep, in_got, cot_keep, cot_got, *ours, *theirs),
        [left] * 4 + [full((length, wide))] * 6,
        [full(s) for s in outs],
        [shaped(*s) for s in outs],
        "ffn_grads",
        grid=(4,),
        needs=needs,
    )


def attn_grads_kernel(widths, *refs):
    keeps, gots, outs = refs[:3], refs[3:6], refs[10:]
    wide = outs[0].shape[1]
    ours, theirs = (
        (heads, both.at[:, :wide], both.at[:, wide:]) for heads, both in (refs[6:8], refs[8:10])
    )
    rows = sum(widths)
    for out, k in zip(outs, ORDER):
        first = 0
        for n, each in enumerate(widths):
            part = slice(2 * each * k, 2 * each * k + 2 * each)
            total = dot(keeps[n][part, :], ours[n][...]) + dot(gots[n][part, :], theirs[n][...])
            total = total.astype(BF16)
            out[first : first + each, :] = total[:each]
            out[rows + first : rows + first + each, :] = total[each:]
            first += each


def attn_grads(keeps, gots, ours, theirs, needs):
    widths = [item.shape[0] // 8 for item in keeps]
    rows, wide = sum(widths), ours[0].shape[1]
    args = (*keeps, *gots, *ours, *theirs)
    outs = [(2 * rows, wide)] * 4
    return call(
        functools.partial(attn_grads_kernel, widths),
        args,
        [full(item.shape) for item in args],
        [full(s) for s in outs],
        [shaped(*s) for s in outs],
        "attn_grads",
        needs=needs,
    )


UP = [(i, (i + 1) % 4) for i in range(4)]
DOWN = [(i, (i + 3) % 4) for i in range(4)]
ACROSS = [(i, (i + 2) % 4) for i in range(4)]


def relay_kernel(up, from_below, down, from_above, up_out, down_out):
    @pl.when(pl.program_id(0) == 0)
    def _():
        up_out[...] = (up[...].astype(F32) + from_below[...].astype(F32)).astype(BF16)
        down_out[...] = down[...]

    @pl.when(pl.program_id(0) == 1)
    def _():
        up_out[...] = up[...]
        down_out[...] = (down[...].astype(F32) + from_above[...].astype(F32)).astype(BF16)


def relay(up, from_below, down, from_above, needs):
    rows, width = from_below.shape
    half = pl.BlockSpec((rows, width), lambda i, *_: (i, 0))
    return call(
        relay_kernel,
        (up, from_below, down, from_above),
        [half, full((rows, width)), half, full((rows, width))],
        [half, half],
        [shaped(2 * rows, width)] * 2,
        "relay",
        grid=(2,),
        needs=needs,
    )


def add_chips_kernel(*refs):
    ins, keep, give = refs[:-2], refs[-2], refs[-1]
    count = len(ins) // 2
    keep[...] = sum(item[...].astype(F32) for item in ins[:count])
    give[...] = sum(item[...].astype(F32) for item in ins[count:]).astype(BF16)


def add_chips(items, needs):
    rows, width = items[0].shape[0] // 2, items[0].shape[1]
    step = rows // 2 if rows % 32 == 0 and (rows // 2) % 16 == 0 else rows
    count = rows // step
    mine = pl.BlockSpec((step, width), lambda i, *_: (i, 0))
    other = pl.BlockSpec((step, width), lambda i, *_: (i + count, 0))
    return call(
        add_chips_kernel,
        (*items, *items),
        [mine] * len(items) + [other] * len(items),
        [mine, mine],
        [shaped(rows, width, dtype=F32), shaped(rows, width)],
        "add_chips",
        grid=(count,),
        needs=needs,
    )


def add_all_kernel(*refs):
    refs[-1][...] = sum(item[...].astype(F32) for item in refs[:-1]).astype(BF16)


def add_all(items, needs):
    rows, width = items[0].shape
    half = pl.BlockSpec((rows // 2, width), lambda i, *_: (i, 0))
    return call(
        add_all_kernel,
        tuple(items),
        [half] * len(items),
        [half],
        [shaped(rows, width)],
        "add_all",
        grid=(2,),
        needs=needs,
        limit=58,
    )


def over_z(blocks):
    return [lax.ppermute(blocks[k], "z", [(i, i ^ k) for i in range(4)]) for k in (1, 2, 3)]


def assemble_kernel(places, *refs):
    del places
    for k in range(4):

        @pl.when(pl.program_id(0) == k)
        def _(k=k):
            refs[4][...] = refs[k][...]


def assemble(places, blocks):
    rows, width = blocks[0].shape
    return call(
        assemble_kernel,
        tuple(blocks),
        [full((rows, width))] * 4,
        [pl.BlockSpec((rows, width), lambda i, places: (places[i], 0))],
        [shaped(4 * rows, width)],
        "assemble",
        grid=(4,),
        me=places,
    )[0][0]


def over_cores(values):
    return lax.ppermute(values, "core", SWAP)


def latents_back_kernel(
    me, got, latents, query_gain, latent_gain, keep, low, high, many, own, gain_part, turns, sems
):
    rows = own.shape[0]
    here = pl.ds(pl.multiple_of(me[0] * rows, rows), rows)
    copies = [
        pltpu.make_async_copy(table.at[here, :], turns.at[n], sems.at[n])
        for n, table in enumerate((keep, low, high))
    ]
    for copy in copies:
        copy.start()
    total = add_up(got)
    for copy in copies:
        copy.wait()

    def back(lanes, gain):
        upstream, values = total[:, lanes], latents[:, lanes]
        factor = root(values)
        normed = values * factor
        gain_part[:, lanes] = jnp.sum(upstream * normed, axis=0, keepdims=True)
        return norm_back(upstream, normed, factor, row(gain)).astype(BF16)

    own[:, :QR] = back(slice(0, QR), query_gain)
    own[:, QR:LAT] = back(slice(QR, LAT), latent_gain)
    own[:, LAT:] = turn(total[:, LAT:], turns[0], turns[1], turns[2], back=True).astype(BF16)
    for k in range(8):
        many[k] = own[...]


def latents_back_of(me, got, latents, query_gain, latent_gain, tables, needs):
    rows = latents.shape[0]
    return call(
        latents_back_kernel,
        (got.reshape(8, rows, WIDE), latents, query_gain, latent_gain, *tables),
        [full((8, rows, WIDE)), full(latents.shape), full((QR,)), full((KVR,)), HBM, HBM, HBM],
        [full((8, rows, WIDE)), full((rows, WIDE)), full((1, LAT))],
        [shaped(8, rows, WIDE), shaped(rows, WIDE), shaped(1, LAT, dtype=F32)],
        "latents_back",
        scratch=[
            pltpu.VMEM((3, rows, 128), F32),
            pltpu.SemaphoreType.DMA((3,)),
        ],
        needs=needs,
        me=me,
        limit=24,
    )


def first_back_of(raw_back, query_down, latent_down, rope_down):
    rope_down[...] = jnp.zeros_like(rope_down)
    rope_down[64:96, :] = latent_down[KVR:, :]
    return (
        dot(raw_back[:, :QR], query_down[...], NT)
        + dot(raw_back[:, QR:LAT], latent_down[:KVR, :])
        + dot(raw_back[:, LAT:], rope_down[...])
    )


def first_gain_kernel(
    me, raw_back, tokens, query_down, latent_down, gain_part, rope_down, own, sem
):
    rows = own.shape[0]
    here = pl.ds(pl.multiple_of(me[0] * rows, rows), rows)
    copy = pltpu.make_async_copy(tokens.at[here, :], own, sem)
    copy.start()
    first_back = first_back_of(raw_back, query_down, latent_down, rope_down)
    copy.wait()
    values = own[...].astype(F32)
    gain_part[...] = jnp.sum(first_back * (values * root(values)), axis=0, keepdims=True)


def first_gain_of(me, own_raw_back, tokens, query_down, latent_down, needs):
    width = tokens.shape[1]
    return call(
        first_gain_kernel,
        (own_raw_back, tokens, query_down, latent_down.T),
        [full(own_raw_back.shape), HBM, full(query_down.shape), full(latent_down.shape[::-1])],
        [full((1, width))],
        [shaped(1, width, dtype=F32)],
        "first_gain",
        scratch=[
            pltpu.VMEM((128, width), BF16),
            pltpu.VMEM((own_raw_back.shape[0], width), BF16),
            pltpu.SemaphoreType.DMA,
        ],
        needs=needs,
        me=me,
    )


def tokens_back_kernel(
    raw_back, tokens, attention_back, query_down, latent_down, gain, tokens_grad, rope_down
):
    first_back = first_back_of(raw_back, query_down, latent_down, rope_down)
    values = tokens[...].astype(F32)
    factor = root(values)
    tokens_grad[...] = attention_back[...].astype(F32) + norm_back(
        first_back, values * factor, factor, row(gain)
    )


def tokens_back_of(raw_back, tokens, attention_back, query_down, latent_down, gain, needs):
    length, width = tokens.shape

    def rows(columns):
        return pl.BlockSpec((TILE, columns), lambda i, *_: (i, 0))

    return call(
        tokens_back_kernel,
        (raw_back, tokens, attention_back, query_down, latent_down.T, gain),
        [
            rows(WIDE),
            rows(width),
            rows(width),
            full(query_down.shape),
            full(latent_down.shape[::-1]),
            full((width,)),
        ],
        [rows(width)],
        [shaped(length, width, dtype=F32)],
        "tokens_back",
        grid=(length // TILE,),
        scratch=[pltpu.VMEM((128, width), BF16)],
        needs=needs,
    )


def finish_ffn_kernel(keep, got, gate, up, down):
    units = gate.shape[1]
    for n, out in enumerate((gate, up, down)):
        lanes = slice(units * n, units * n + units)
        out[...] = keep[:, lanes] + got[:, lanes].astype(F32)


def finish_ffn(keep, got, needs):
    rows, width = keep.shape
    out = (rows, width // 3)
    return call(
        finish_ffn_kernel,
        (keep, got),
        [full(keep.shape), full(got.shape)],
        [full(out)] * 3,
        [shaped(*out, dtype=F32)] * 3,
        "finish_ffn",
        needs=needs,
    )


def finish_attn_kernel(heads, keep, got, out_grad, query_grad, latent_grad):
    total = keep[...] + got[...].astype(F32)
    for h in range(heads):
        lanes = slice(128 * h, 128 * h + 128)
        out_grad[:, 64 * h : 64 * h + 64] = total[:160, 128 * h + 64 : 128 * h + 128]
        query_grad[:, 96 * h : 96 * h + 96] = total[160:208, 128 * h : 128 * h + 96]
    latent_grad[...] = total[208:224]


def finish_attn(keep, got, needs):
    heads = keep.shape[1] // 128
    outs = [(160, 64 * heads), (48, 96 * heads), (16, 128 * heads)]
    return call(
        functools.partial(finish_attn_kernel, heads),
        (keep, got),
        [full(keep.shape), full(got.shape)],
        [full(s) for s in outs],
        [shaped(*s, dtype=F32) for s in outs],
        "finish_attn",
        needs=needs,
    )


GAINS = ((0, 160), (160, 160), (320, 48), (368, 16))


def down_parts_kernel(own_in, raw_back, gains, out):
    total = dot(own_in[...], raw_back[...]).astype(BF16)
    for d in range(16):
        out[d, :20, :] = total[20 * d : 20 * d + 20]
        out[d, 20:, :] = jnp.zeros((4, WIDE), BF16)
        out[d, 20:21, :] = gains[d : d + 1, :]


def down_parts(own_in, raw_back, gains, needs):
    args = (own_in, raw_back, gains)
    return call(
        down_parts_kernel,
        args,
        [full(item.shape) for item in args],
        [full((16, 24, WIDE))],
        [shaped(16, 24, WIDE)],
        "down_parts",
        needs=needs,
        limit=24,
    )


def sum_copies_kernel(got, many):
    total = got[0].astype(F32)
    for d in range(1, 16):
        total = total + got[d].astype(F32)
    for k in range(8):
        many[k] = total.astype(BF16)


def sum_copies(got, needs):
    return call(
        sum_copies_kernel,
        (got,),
        [full(got.shape)],
        [full((8, 24, WIDE))],
        [shaped(8, 24, WIDE)],
        "sum_copies",
        needs=needs,
        limit=24,
    )


def finish_down_kernel(everyone, query_grad, latent_grad, *gains):
    for t in range(8):
        values = everyone[t].astype(F32)
        query_grad[20 * t : 20 * t + 20, :] = values[:20, :QR]
        latent_grad[20 * t : 20 * t + 20, :KVR] = values[:20, QR:LAT]
        latent_grad[20 * t : 20 * t + 20, KVR:] = values[:20, LAT + 64 : LAT + 96]
    total = sum(everyone[t, 16:24, :].astype(F32) for t in range(8))[4:5, :]
    for out, (first, count) in zip(gains, GAINS):
        out[...] = total[:, first : first + count]


def finish_down(everyone):
    everyone = everyone.reshape(8, 24, WIDE)
    outs = [(160, QR), (160, KVR + ROPE)] + [(1, count) for _, count in GAINS]
    return call(
        finish_down_kernel,
        (everyone,),
        [full(everyone.shape)],
        [full(s) for s in outs],
        [shaped(*s, dtype=F32) for s in outs],
        "finish_down",
        limit=24,
    )[0]


def exchange(blocks):
    return lax.all_to_all(blocks.reshape(-1, blocks.shape[-1]), TP, 0, 0, tiled=True)


def on_device(
    tokens,
    first_gain,
    query_down,
    query_gain,
    query_up,
    latent_down,
    latent_gain,
    latent_up,
    out_weight,
    second_gain,
    gate_weight,
    up_weight,
    down_weight,
    cotangent,
):
    length = tokens.shape[0]
    me = lax.axis_index(TP).astype(jnp.int32).reshape(1)
    y, xl, core = lax.axis_index("y"), lax.axis_index("xl"), lax.axis_index("core")
    starts = jnp.stack(
        [
            ((y + k) % 4 * 2 + (xl ^ j)) * 2 + c
            for c in (core, 1 - core)
            for k in range(4)
            for j in range(2)
        ]
    ).astype(jnp.int32)
    places = jnp.stack([lax.axis_index("z") ^ k for k in range(4)] + [me[0]]).astype(jnp.int32)
    tables = rope_tables(length)

    gate_turned, up_turned = gate_weight.T, up_weight.T

    (
        first_in,
        latents,
        query_code,
        latent_code,
        queries,
        keyvals,
        rope_keys,
        heads_out,
        log_total,
        attn_partial,
    ), started = attend(
        me,
        tokens,
        first_gain,
        query_down,
        latent_down,
        query_gain,
        latent_gain,
        query_up,
        latent_up,
        out_weight,
        tables,
    )
    attn_got = exchange(attn_partial)

    (cot_keep, cot_give), picked = halves(starts, [cotangent], [started])
    inner_back = dot(cotangent, down_weight, NT)
    cot_got = over_cores(cot_give)

    (residual, second_many), _ = residual_of(
        me, attn_got, tokens, second_gain, [picked, cot_got]
    )
    second_in = exchange(second_many)

    turned_in = first_in.T.reshape(16, 8, 20, length)
    own_in = lax.dynamic_slice_in_dim(turned_in, me[0], 1, 1).reshape(320, length)
    (code_keep, code_give, lat_keep, lat_give), picked = halves(
        starts, [query_code, latent_code], [residual]
    )
    code_got, lat_got = over_cores(code_give), over_cores(lat_give)
    heads_got = over_cores(heads_out)

    (gate_back, up_back, inner, back_partial), done = ffn(
        second_in, gate_turned, up_turned, inner_back, [picked, own_in, code_got, lat_got, heads_got]
    )
    back_got = exchange(back_partial)

    ours = (gate_back, up_back, inner)
    theirs = [over_cores(item) for item in ours]
    (in_keep, in_give), _ = halves(starts, [second_in], [done])
    in_got = over_cores(in_give)
    (far_up, far_down, ffn_up, ffn_down_way, ffn_own), done = ffn_grads(in_keep, in_got, cot_keep, cot_got, ours, theirs, gate_weight.shape[1], [])
    below, above = lax.ppermute(far_up, "y", UP), lax.ppermute(far_down, "y", DOWN)

    (back_many, second_gain_part), done = residual_back_of(
        me, back_got, residual, cotangent, second_gain, [done]
    )
    attention_back = exchange(back_many)
    mixed_blocks, done = ffn_down(places, inner, down_weight, residual, [done])
    mixed_got = over_z(mixed_blocks)
    (ffn_up, ffn_down_way), done = relay(ffn_up, below, ffn_down_way, above, [done])
    below, above = lax.ppermute(ffn_up, "y", UP), lax.ppermute(ffn_down_way, "y", DOWN)

    (both_back, latents_partial), back_done = attend_back(
        attention_back,
        out_weight,
        queries,
        keyvals,
        rope_keys,
        log_total,
        query_up,
        latent_up,
        tables,
        [done],
    )
    latents_got = exchange(latents_partial)

    (out_keep, out_give), picked = halves(
        starts, [attention_back], [back_done, below, above, *mixed_got]
    )
    (ffn_keep, ffn_give), done = add_chips([ffn_own, below, above], [back_done])
    ffn_got = lax.ppermute(ffn_give, "xl", SWAP)

    (raw_many, own_raw, latent_gain_parts), done = latents_back_of(
        me, latents_got, latents, query_gain, latent_gain, tables, [done, picked]
    )
    raw_back = exchange(raw_many)

    (mixed_part,), done = add_all([mixed_blocks[0], *mixed_got], [done])
    mixed_other = lax.ppermute(mixed_part, "xh", SWAP)

    out_got, both_got = over_cores(out_give), over_cores(both_back)
    (attn_across, attn_up, attn_down, attn_own), done = attn_grads(
        (out_keep, code_keep, lat_keep),
        (out_got, code_got, lat_got),
        (heads_out, both_back),
        (heads_got, both_got),
        [done],
    )
    attn_got = [
        lax.ppermute(attn_across, "y", ACROSS),
        lax.ppermute(attn_up, "y", UP),
        lax.ppermute(attn_down, "y", DOWN),
    ]
    (mixed_part,), done = add_all([mixed_part, mixed_other], [done])
    mixed_got = over_z([mixed_part] * 4)
    (first_gain_part,), gain_done = first_gain_of(
        me, own_raw, tokens, query_down, latent_down, [done]
    )


    gains = jnp.concatenate(
        [
            first_gain_part.reshape(16, -1),
            second_gain_part.reshape(16, -1),
            latent_gain_parts[0, :QR].reshape(16, -1),
            latent_gain_parts[0, QR:].reshape(16, -1),
        ],
        axis=1,
    ).astype(BF16)
    gains = jnp.pad(gains, ((0, 0), (0, WIDE - gains.shape[1])))
    (parts,), done = down_parts(own_in, raw_back, gains, [attn_got[1], attn_got[2]])
    parts_got = lax.all_to_all(parts, DP, 0, 0, tiled=True)

    (tokens_grad,), done = tokens_back_of(
        raw_back, tokens, attention_back, query_down, latent_down, first_gain, [done]
    )
    (many,), summed = sum_copies(parts_got, [done])
    everyone = exchange(many)

    (attn_keep, attn_give), done = add_chips([attn_own, *attn_got], [summed])
    attn_other = lax.ppermute(attn_give, "xl", SWAP)
    (gate_weight_grad, up_weight_grad, down_weight_grad), done = finish_ffn(
        ffn_keep, ffn_got, [done]
    )
    (out_weight_grad, query_up_grad, latent_up_grad), done = finish_attn(
        attn_keep, attn_other, [done]
    )
    (
        query_down_grad,
        latent_down_grad,
        first_gain_grad,
        second_gain_grad,
        query_gain_grad,
        latent_gain_grad,
    ) = finish_down(everyone)

    mixed = assemble(places, [mixed_part, *mixed_got])

    return (
        mixed,
        tokens_grad,
        first_gain_grad[0],
        query_down_grad,
        query_gain_grad[0],
        query_up_grad,
        latent_down_grad,
        latent_gain_grad[0],
        latent_up_grad,
        out_weight_grad.T,
        second_gain_grad[0],
        gate_weight_grad,
        up_weight_grad,
        down_weight_grad.T,
    )


def solution(mesh):
    grid = Mesh(mesh.devices.reshape(4, 2, 2, 2, 4), ("y", "xl", "core", "xh", "z"))
    in_specs = (
        P(DP, None),
        P(),
        P(),
        P(),
        P(None, TP),
        P(),
        P(),
        P(None, TP),
        P(TP, None),
        P(),
        P(None, TP),
        P(None, TP),
        P(TP, None),
        P(DP, None),
    )
    out_specs = (
        P(DP, None),
        P(DP, None),
        P(DP),
        P(DP, None),
        P(DP),
        P(DP, TP),
        P(DP, None),
        P(DP),
        P(DP, TP),
        P(TP, DP),
        P(DP),
        P(DP, TP),
        P(DP, TP),
        P(TP, DP),
    )
    return jax.shard_map(
        on_device, mesh=grid, in_specs=in_specs, out_specs=out_specs, check_vma=False
    )
```

```python
import functools

import jax
import jax.numpy as jnp
import numpy as np
from jax import lax
from jax.experimental import pallas as pl
from jax.experimental.pallas import tpu as pltpu
from jax.sharding import Mesh, PartitionSpec as P

NOPE = 64
ROPE = 32
DV = 64
KVR = 256
QR = 768
LAT = QR + KVR
WIDE = LAT + 128

EPS = 1e-05
BASE = 10000.0
SCALE = (NOPE + ROPE) ** (-0.5)

DP = ("y", "xl", "core")
TP = ("xh", "z")
SWAP = [(0, 1), (1, 0)]
F32 = jnp.float32
BF16 = jnp.bfloat16
NT = (((1,), (1,)), ((), ()))
TN = (((0,), (0,)), ((), ()))
NN = (((1,), (0,)), ((), ()))
TILE = 256


def dot(left, right, dims=NN):
    return lax.dot_general(left, right, dims, preferred_element_type=F32)


def params(limit=56):
    return pltpu.CompilerParams(vmem_limit_bytes=limit * 2**20)


HBM = pl.BlockSpec(memory_space=pltpu.HBM)


def call(kernel, args, in_specs, out_specs, out_shape, name, grid=(1,), scratch=(), needs=(), me=None, limit=60):
    first = 0 if me is None else 1
    n_in, n_out = len(args), len(out_shape)

    def body(*refs):
        ins = refs[: first + n_in]
        rest = refs[first + n_in + len(needs) :]
        mark = rest[n_out]

        @pl.when(pl.program_id(0) == 0)
        def _():
            mark[...] = jnp.zeros_like(mark)

        kernel(*ins, *rest[:n_out], *rest[n_out + 1 :])

    *outs, mark = pl.pallas_call(
        body,
        grid_spec=pltpu.PrefetchScalarGridSpec(
            num_scalar_prefetch=first,
            grid=grid,
            in_specs=list(in_specs) + [HBM] * len(needs),
            out_specs=list(out_specs) + [full((8, 128))],
            scratch_shapes=list(scratch),
        ),
        out_shape=list(out_shape) + [jax.ShapeDtypeStruct((8, 128), F32)],
        compiler_params=params(limit),
        cost_estimate=pl.CostEstimate(flops=1, bytes_accessed=1, transcendentals=0),
        name=name,
    )(*(() if me is None else (me,)), *args, *needs)
    return outs, mark


def shaped(*shape, dtype=BF16):
    return jax.ShapeDtypeStruct(shape, dtype)


def full(shape):
    return pl.BlockSpec(shape, lambda *_: (0,) * len(shape))


def rope_tables(length):
    half = ROPE // 2
    rates = np.exp(np.arange(half, dtype=np.float32) * np.float32(-2.0 * np.log(BASE) / ROPE))
    angles = np.arange(length, dtype=np.float32)[:, None] * rates.astype(np.float32)[None, :]
    cosine, sine = np.cos(angles), np.sin(angles)
    keep = np.zeros((length, 128), np.float32)
    keep[:, :NOPE] = 1.0
    keep[:, 64:80] = cosine
    keep[:, 80:96] = cosine
    low = np.zeros((length, 128), np.float32)
    low[:, 64:80] = -sine
    high = np.zeros((length, 128), np.float32)
    high[:, 80:96] = sine
    return jnp.asarray(keep), jnp.asarray(low), jnp.asarray(high)


def turn(values, keep, low, high, back=False):
    moved = pltpu.roll(values, 112, 1) * low + pltpu.roll(values, 16, 1) * high
    return values * keep - moved if back else values * keep + moved


def root(values):
    return lax.rsqrt(jnp.mean(values * values, axis=-1, keepdims=True) + EPS)


def norm_back(upstream, normed, factor, gain):
    scaled = upstream * gain
    return factor * (scaled - normed * jnp.mean(scaled * normed, axis=-1, keepdims=True))


def spread_out_weight(weight_ref, spread_ref, heads):
    spread_ref[...] = jnp.zeros_like(spread_ref)
    for h in range(heads):
        spread_ref[128 * h + 64 : 128 * h + 128, :] = weight_ref[64 * h : 64 * h + 64, :]


def spread_query_up(weight_ref, spread_ref, heads):
    spread_ref[...] = jnp.zeros_like(spread_ref)
    for h in range(heads):
        spread_ref[128 * h : 128 * h + 96, :] = weight_ref[96 * h : 96 * h + 96, :]


def row(ref):
    return ref[...].reshape(1, -1)


def low_lanes(shape):
    return lax.broadcasted_iota(jnp.int32, shape, 1) < NOPE


def causal(keys, queries, first_query):
    key_ids = lax.broadcasted_iota(jnp.int32, (keys, queries), 0)
    query_ids = lax.broadcasted_iota(jnp.int32, (keys, queries), 1) + first_query
    return key_ids <= query_ids


def attend_kernel(
    heads,
    me,
    tokens,
    first_gain,
    query_down,
    latent_down,
    query_gain,
    latent_gain,
    query_up,
    latent_up,
    out_weight,
    keep,
    low,
    high,
    first_in,
    latents,
    query_code,
    latent_code,
    queries,
    keyvals,
    rope_keys,
    heads_out,
    log_total,
    partial,
    raw_latents,
    spread,
    spread_up,
    rope_down,
    kv_all,
    rope_all,
):
    step = pl.program_id(0)

    @pl.when(step == 0)
    def _():
        spread_out_weight(out_weight, spread, heads)
        spread_query_up(query_up, spread_up, heads)
        rope_down[...] = jnp.zeros_like(rope_down)
        rope_down[64:96, :] = latent_down[KVR:, :]

    def rows_of(index, carry):
        rows = pl.ds(pl.multiple_of(index * 32, 32), 32)
        values = tokens[rows, :].astype(F32)
        first_in[rows, :] = (values * root(values) * row(first_gain)).astype(BF16)
        return carry

    lax.fori_loop(0, TILE // 32, rows_of, 0)
    taken = first_in[...]
    query_latent = dot(taken, query_down[...])
    raw_latents[:, :QR] = query_latent
    code = (query_latent * root(query_latent) * row(query_gain)).astype(BF16)
    query_code[...] = code
    latent = dot(taken, latent_down[:KVR, :], NT)
    raw_latents[:, QR:] = latent
    count = latents.shape[0]
    own = me[0] * count

    @pl.when(own // TILE == step)
    def _():
        latents[...] = raw_latents[pl.ds(pl.multiple_of(own % TILE, count), count), :]

    lcode = (latent * root(latent) * row(latent_gain)).astype(BF16)
    latent_code[...] = lcode
    tables = keep[...], low[...], high[...]
    rope = turn(dot(taken, rope_down[...], NT), *tables).astype(BF16)
    rope_keys[...] = rope
    here = pl.ds(pl.multiple_of(step * TILE, TILE), TILE)
    rope_all[here, :] = rope
    kv = dot(lcode, latent_up[...]).astype(BF16)
    keyvals[...] = kv
    kv_all[here, :] = kv
    raw = dot(code, spread_up[...], NT)
    for h in range(heads):
        lanes = slice(128 * h, 128 * h + 128)
        queries[:, lanes] = turn(raw[:, lanes], *tables).astype(BF16)

    def tile(index):
        keys = TILE * (index + 1)
        for h in range(heads):
            lanes = slice(128 * h, 128 * h + 128)
            kv_h = kv_all[:keys, lanes]
            key = jnp.where(low_lanes((keys, 128)), kv_h, rope_all[:keys, :])
            scores = dot(key, queries[:, lanes], NT) * SCALE
            scores = jnp.where(causal(keys, TILE, TILE * index), scores, -1e30)
            top = jnp.max(scores, axis=0, keepdims=True)
            weights = jnp.exp(scores - top)
            total = jnp.sum(weights, axis=0, keepdims=True)
            log_total[h : h + 1, :] = top + jnp.log(total)
            probs = (weights * (1.0 / total)).astype(BF16)
            heads_out[:, lanes] = dot(probs, kv_h, TN).astype(BF16)

    for index in range(2):
        pl.when(step == index)(functools.partial(tile, index))
    partial[...] = dot(heads_out[...], spread[...]).astype(BF16)


def attend(me, tokens, first_gain, query_down, latent_down, query_gain, latent_gain, query_up, latent_up, out_weight, tables):
    latent_down, query_up = latent_down.T, query_up.T
    length, width = tokens.shape
    heads = out_weight.shape[0] // DV
    wide = 128 * heads

    def rows(columns):
        return pl.BlockSpec((TILE, columns), lambda i, *_: (i, 0))

    return call(
        functools.partial(attend_kernel, heads),
        (tokens, first_gain, query_down, latent_down, query_gain, latent_gain, query_up, latent_up, out_weight, *tables),
        [
            rows(width),
            full((width,)),
            full(query_down.shape),
            full(latent_down.shape),
            full((QR,)),
            full((KVR,)),
            full(query_up.shape),
            full(latent_up.shape),
            full(out_weight.shape),
            rows(128),
            rows(128),
            rows(128),
        ],
        [
            rows(width),
            full((length // 8, LAT)),
            rows(QR),
            rows(KVR),
            rows(wide),
            rows(wide),
            rows(128),
            rows(wide),
            pl.BlockSpec((8, TILE), lambda i, *_: (0, i)),
            rows(width),
        ],
        [
            shaped(length, width),
            shaped(length // 8, LAT, dtype=F32),
            shaped(length, QR),
            shaped(length, KVR),
            shaped(length, wide),
            shaped(length, wide),
            shaped(length, 128),
            shaped(length, wide),
            shaped(8, length, dtype=F32),
            shaped(length, width),
        ],
        "attend",
        grid=(length // TILE,),
        me=me,
        scratch=[
            pltpu.VMEM((TILE, LAT), F32),
            pltpu.VMEM((wide, width), BF16),
            pltpu.VMEM((wide, QR), BF16),
            pltpu.VMEM((128, width), BF16),
            pltpu.VMEM((length, wide), BF16),
            pltpu.VMEM((length, 128), BF16),
        ],
    )


def attend_back_kernel(
    heads,
    attention_back,
    out_weight,
    queries,
    keyvals,
    rope_keys,
    log_total,
    query_up,
    latent_up,
    keep,
    low,
    high,
    both_back,
    partial,
    spread,
    spread_up,
    kv_grad,
    rope_grad,
    code_grad,
):
    step = pl.program_id(0)

    @pl.when(step == 0)
    def _():
        spread_out_weight(out_weight, spread, heads)
        spread_query_up(query_up, spread_up, heads)
        kv_grad[...] = jnp.zeros_like(kv_grad)
        rope_grad[...] = jnp.zeros_like(rope_grad)

    heads_back = dot(attention_back[...], spread[...], NT).astype(BF16)
    tables = keep[...], low[...], high[...]

    def tile(index):
        keys = TILE * (index + 1)
        low_part = low_lanes((keys, 128))
        for h in range(heads):
            lanes = slice(128 * h, 128 * h + 128)
            kv_h = keyvals[:keys, lanes]
            key = jnp.where(low_part, kv_h, rope_keys[:keys, :])
            query = queries[:, lanes]
            back = heads_back[:, lanes]
            scores = dot(key, query, NT) * SCALE
            probs = jnp.exp(scores - log_total[h : h + 1, :])
            probs = jnp.where(causal(keys, TILE, TILE * index), probs, 0.0)
            prob_back = dot(kv_h, back, NT)
            mean = jnp.sum(probs * prob_back, axis=0, keepdims=True)
            score_back = (probs * (prob_back - mean)).astype(BF16)
            of_values = dot(probs.astype(BF16), back)
            of_keys = dot(score_back, query) * SCALE
            kv_grad[:keys, lanes] += of_values + jnp.where(low_part, of_keys, 0.0)
            rope_grad[:keys, :] += jnp.where(low_part, 0.0, of_keys)
            of_query = dot(score_back, key, TN) * SCALE
            both_back[here, lanes] = turn(of_query, *tables, back=True).astype(BF16)

    wide = 128 * heads
    here = pl.ds(pl.multiple_of(step * TILE, TILE), TILE)
    for index in range(2):
        pl.when(step == index)(functools.partial(tile, index))
    code_grad[here, :] = dot(both_back[here, :wide], spread_up[...]).astype(BF16)

    @pl.when(step == 1)
    def _():
        kv = kv_grad[...].astype(BF16)
        both_back[:, wide:] = kv
        partial[:, :QR] = code_grad[...]
        partial[:, QR:LAT] = dot(kv, latent_up[...], NT).astype(BF16)
        partial[:, LAT:] = rope_grad[...].astype(BF16)


def attend_back(attention_back, out_weight, queries, keyvals, rope_keys, log_total, query_up, latent_up, tables, needs):
    query_up = query_up.T
    length, width = attention_back.shape
    heads = out_weight.shape[0] // DV
    wide = 128 * heads

    def rows(columns):
        return pl.BlockSpec((TILE, columns), lambda i, *_: (i, 0))

    return call(
        functools.partial(attend_back_kernel, heads),
        (attention_back, out_weight, queries, keyvals, rope_keys, log_total, query_up, latent_up, *tables),
        [
            rows(width),
            full(out_weight.shape),
            rows(wide),
            full((length, wide)),
            full((length, 128)),
            pl.BlockSpec((8, TILE), lambda i, *_: (0, i)),
            full(query_up.shape),
            full(latent_up.shape),
            rows(128),
            rows(128),
            rows(128),
        ],
        [full((length, 2 * wide)), full((length, WIDE))],
        [shaped(length, 2 * wide), shaped(length, WIDE)],
        "attend_back",
        grid=(length // TILE,),
        scratch=[
            pltpu.VMEM((wide, width), BF16),
            pltpu.VMEM((wide, QR), BF16),
            pltpu.VMEM((length, wide), F32),
            pltpu.VMEM((length, 128), F32),
            pltpu.VMEM((length, QR), BF16),
        ],
        needs=needs,
    )


def add_up(got):
    total = got[0].astype(F32)
    for k in range(1, 8):
        total = total + got[k].astype(F32)
    return total


STEPS = 2


def residual_kernel(me, got, tokens, gain, residual, many):
    del me
    total = tokens[...].astype(F32) + add_up(got)
    residual[...] = total
    second_in = (total * root(total) * row(gain)).astype(BF16)
    for k in range(8):
        many[k] = second_in


def own_specs(rows, width):
    step = rows // STEPS
    return (
        pl.BlockSpec((8, step, width), lambda i, me: (0, i, 0)),
        pl.BlockSpec((step, width), lambda i, me: (i, 0)),
        pl.BlockSpec((step, width), lambda i, me: (me[0] * STEPS + i, 0)),
    )


def residual_of(me, got, tokens, gain, needs):
    width = tokens.shape[1]
    rows = tokens.shape[0] // 8
    eight, one, own = own_specs(rows, width)
    return call(
        residual_kernel,
        (got.reshape(8, rows, width), tokens, gain),
        [eight, own, full((width,))],
        [one, eight],
        [shaped(rows, width, dtype=F32), shaped(8, rows, width)],
        "residual",
        grid=(STEPS,),
        needs=needs,
        me=me,
        limit=58,
    )


def residual_back_kernel(me, got, residual, cotangent, gain, many, gain_part):
    del me
    second_back = add_up(got)
    values = residual[...]
    factor = root(values)
    normed = values * factor
    part = jnp.sum(second_back * normed, axis=0, keepdims=True)

    @pl.when(pl.program_id(0) == 0)
    def _():
        gain_part[...] = part

    @pl.when(pl.program_id(0) > 0)
    def _():
        gain_part[...] += part

    back = cotangent[...].astype(F32) + norm_back(second_back, normed, factor, row(gain))
    back = back.astype(BF16)
    for k in range(8):
        many[k] = back


def residual_back_of(me, got, residual, cotangent, gain, needs):
    rows, width = residual.shape
    eight, one, own = own_specs(rows, width)
    return call(
        residual_back_kernel,
        (got.reshape(8, rows, width), residual, cotangent, gain),
        [eight, one, own, full((width,))],
        [eight, full((1, width))],
        [shaped(8, rows, width), shaped(1, width, dtype=F32)],
        "residual_back",
        grid=(STEPS,),
        needs=needs,
        me=me,
        limit=58,
    )


def ffn_kernel(
    second_in, gate_weight, up_weight, inner_back, gate_back, up_back, inner, partial
):
    taken = second_in[...]
    gate = dot(taken, gate_weight[...], NT)
    up = dot(taken, up_weight[...], NT)
    sigma = 1.0 / (1.0 + jnp.exp(-gate))
    act = gate * sigma
    units = gate.shape[1]
    back = inner_back[...]
    of_gate = (back * up * sigma * (1.0 + gate * (1.0 - sigma))).astype(BF16)
    of_up = (back * act).astype(BF16)
    for out, values in ((gate_back, of_gate), (up_back, of_up), (inner, (act * up).astype(BF16))):
        out[:, :units] = values
        out[:, units:] = jnp.zeros((values.shape[0], out.shape[1] - units), BF16)
    partial[...] = (dot(of_gate, gate_weight[...]) + dot(of_up, up_weight[...])).astype(BF16)


def ffn(second_in, gate_weight, up_weight, inner_back, needs):
    length, width = second_in.shape
    units = gate_weight.shape[0]
    wide = -(-units // 128) * 128

    def rows(columns):
        return pl.BlockSpec((TILE, columns), lambda i, *_: (i, 0))

    return call(
        ffn_kernel,
        (second_in, gate_weight, up_weight, inner_back),
        [rows(width), full((units, width)), full((units, width)), rows(units)],
        [rows(wide), rows(wide), rows(wide), rows(width)],
        [shaped(length, wide)] * 3 + [shaped(length, width)],
        "ffn",
        grid=(length // TILE,),
        needs=needs,
    )


def ffn_down_kernel(places, inner, down_weight, residual, far_up, far_down, up, down, own, total):
    for i in range(2):
        rows = slice(i * TILE, i * TILE + TILE)
        total[rows, :] = dot(inner[rows, : down_weight.shape[0]], down_weight[...]).astype(BF16)
    count = residual.shape[0]
    mine = pl.ds(pl.multiple_of(places[4] * count, count), count)
    total[mine, :] = (total[mine, :].astype(F32) + residual[...]).astype(BF16)

    def block(k, half=None):
        rows = own.shape[0]
        first = pl.multiple_of(places[k] * rows, rows)
        if half is None:
            return total[pl.ds(first, rows), :]
        return total[pl.ds(first + half * (rows // 2), rows // 2), :]

    far_up[...] = block(2, 0)
    far_down[...] = block(2, 1)
    up[...] = block(1)
    down[...] = block(3)
    own[...] = block(0)


def ffn_down(places, inner, down_weight, residual, needs):
    length, width = inner.shape[0], down_weight.shape[1]
    rows = length // 4
    outs = [(rows // 2, width)] * 2 + [(rows, width)] * 3
    return call(
        ffn_down_kernel,
        (inner, down_weight, residual),
        [full(inner.shape), full(down_weight.shape), full(residual.shape)],
        [full(s) for s in outs],
        [shaped(*s) for s in outs],
        "ffn_down",
        scratch=[pltpu.VMEM((length, width), BF16)],
        needs=needs,
        me=places,
    )


def halves_kernel(blocks, width, starts, *refs):
    sources, outs, turned = refs[:blocks], refs[blocks : 3 * blocks], refs[3 * blocks]
    for n in range(blocks):
        source, keep, give = sources[n], outs[2 * n], outs[2 * n + 1]
        columns, each = source.shape[1], width[n]
        for c in range(0, columns, 256):
            turned[c : c + 256, :] = source[:, c : c + 256].T
        for which, out in enumerate((keep, give)):
            for k in range(8):
                first = pl.multiple_of(starts[8 * which + k] * each, 16)
                out[each * k : each * k + each, :] = turned[pl.ds(first, each), :]


def halves(starts, values, needs):
    length = values[0].shape[0]
    widths = [item.shape[1] // 16 for item in values]
    shapes = [(8 * w, length) for w in widths for _ in range(2)]
    return call(
        functools.partial(halves_kernel, len(values), widths),
        tuple(values),
        [full(item.shape) for item in values],
        [full(s) for s in shapes],
        [shaped(*s) for s in shapes],
        "halves",
        scratch=[pltpu.VMEM((max(item.shape[1] for item in values), length), BF16)],
        needs=needs,
        me=starts,
    )


ORDER = (2, 1, 3, 0)


def ffn_grads_kernel(in_keep, in_got, cot_keep, cot_got, *refs):
    ours, theirs, outs = refs[:3], refs[3:6], refs[6:]
    units = outs[0].shape[1] // 3

    def block(*parts):
        for n, (keep, got) in enumerate(((in_keep, in_got), (in_keep, in_got), (cot_keep, cot_got))):
            total = dot(keep[...], ours[n][...]) + dot(got[...], theirs[n][...])
            total = total[:, :units].astype(BF16)
            first = 0
            for out in parts:
                count = out.shape[0]
                out[:, units * n : units * n + units] = total[first : first + count]
                first += count

    for s, parts in enumerate((outs[:2], outs[2:3], outs[3:4], outs[4:])):
        pl.when(pl.program_id(0) == s)(functools.partial(block, *parts))


def ffn_grads(in_keep, in_got, cot_keep, cot_got, ours, theirs, units, needs):
    length, wide = ours[0].shape
    rows = in_keep.shape[0] // 4

    def index(i):
        return (jnp.where(i == 0, 2, jnp.where(i == 1, 1, jnp.where(i == 2, 3, 0))), 0)

    left = pl.BlockSpec((rows, length), index)
    out = (rows, 3 * units)
    outs = [(rows // 2, 3 * units)] * 2 + [out] * 3
    return call(
        ffn_grads_kernel,
        (in_keep, in_got, cot_keep, cot_got, *ours, *theirs),
        [left] * 4 + [full((length, wide))] * 6,
        [full(s) for s in outs],
        [shaped(*s) for s in outs],
        "ffn_grads",
        grid=(4,),
        needs=needs,
    )


def attn_grads_kernel(widths, *refs):
    keeps, gots, outs = refs[:3], refs[3:6], refs[10:]
    wide = outs[0].shape[1]
    ours, theirs = (
        (heads, both.at[:, :wide], both.at[:, wide:]) for heads, both in (refs[6:8], refs[8:10])
    )
    rows = sum(widths)
    for out, k in zip(outs, ORDER):
        first = 0
        for n, each in enumerate(widths):
            part = slice(2 * each * k, 2 * each * k + 2 * each)
            total = dot(keeps[n][part, :], ours[n][...]) + dot(gots[n][part, :], theirs[n][...])
            total = total.astype(BF16)
            out[first : first + each, :] = total[:each]
            out[rows + first : rows + first + each, :] = total[each:]
            first += each


def attn_grads(keeps, gots, ours, theirs, needs):
    widths = [item.shape[0] // 8 for item in keeps]
    rows, wide = sum(widths), ours[0].shape[1]
    args = (*keeps, *gots, *ours, *theirs)
    outs = [(2 * rows, wide)] * 4
    return call(
        functools.partial(attn_grads_kernel, widths),
        args,
        [full(item.shape) for item in args],
        [full(s) for s in outs],
        [shaped(*s) for s in outs],
        "attn_grads",
        needs=needs,
    )


UP = [(i, (i + 1) % 4) for i in range(4)]
DOWN = [(i, (i + 3) % 4) for i in range(4)]
ACROSS = [(i, (i + 2) % 4) for i in range(4)]


def relay_kernel(*refs):
    count = len(refs) // 6
    for n in range(count):
        up, from_below, down, from_above = refs[4 * n : 4 * n + 4]
        up_out, down_out = refs[4 * count + 2 * n : 4 * count + 2 * n + 2]

        @pl.when(pl.program_id(0) == 0)
        def _():
            up_out[...] = (up[...].astype(F32) + from_below[...].astype(F32)).astype(BF16)
            down_out[...] = down[...]

        @pl.when(pl.program_id(0) == 1)
        def _():
            up_out[...] = up[...]
            down_out[...] = (down[...].astype(F32) + from_above[...].astype(F32)).astype(BF16)


def relay(rings, needs):
    in_specs, outs, shapes = [], [], []
    for _, from_below, _, _ in rings:
        rows, width = from_below.shape
        half = pl.BlockSpec((rows, width), lambda i: (i, 0))
        in_specs += [half, full((rows, width)), half, full((rows, width))]
        outs += [half, half]
        shapes += [shaped(2 * rows, width)] * 2
    return call(
        relay_kernel,
        tuple(item for ring in rings for item in ring),
        in_specs,
        outs,
        shapes,
        "relay",
        grid=(2,),
        needs=needs,
    )


def add_chips_kernel(*refs):
    ins, keep, give = refs[:-2], refs[-2], refs[-1]
    count = len(ins) // 2
    keep[...] = sum(item[...].astype(F32) for item in ins[:count])
    give[...] = sum(item[...].astype(F32) for item in ins[count:]).astype(BF16)


def add_chips(items, needs):
    rows, width = items[0].shape[0] // 2, items[0].shape[1]
    step = rows // 2 if rows % 32 == 0 and (rows // 2) % 16 == 0 else rows
    count = rows // step
    mine = pl.BlockSpec((step, width), lambda i, *_: (i, 0))
    other = pl.BlockSpec((step, width), lambda i, *_: (i + count, 0))
    return call(
        add_chips_kernel,
        (*items, *items),
        [mine] * len(items) + [other] * len(items),
        [mine, mine],
        [shaped(rows, width, dtype=F32), shaped(rows, width)],
        "add_chips",
        grid=(count,),
        needs=needs,
    )


def add_all_kernel(*refs):
    refs[-1][...] = sum(item[...].astype(F32) for item in refs[:-1]).astype(BF16)


def add_all(items, needs):
    rows, width = items[0].shape
    half = pl.BlockSpec((rows // 2, width), lambda i, *_: (i, 0))
    return call(
        add_all_kernel,
        tuple(items),
        [half] * len(items),
        [half],
        [shaped(rows, width)],
        "add_all",
        grid=(2,),
        needs=needs,
        limit=58,
    )


def assemble_kernel(places, *refs):
    del places
    for k in range(4):

        @pl.when(pl.program_id(0) == k)
        def _(k=k):
            refs[4][...] = refs[k][...]


def assemble(places, blocks):
    rows, width = blocks[0].shape
    return call(
        assemble_kernel,
        tuple(blocks),
        [full((rows, width))] * 4,
        [pl.BlockSpec((rows, width), lambda i, places: (places[i], 0))],
        [shaped(4 * rows, width)],
        "assemble",
        grid=(4,),
        me=places,
    )[0][0]


def over_cores(values):
    return lax.ppermute(values, "core", SWAP)


def latents_back_kernel(
    me, got, latents, query_gain, latent_gain, keep, low, high, many, own, gain_part, turns, sems
):
    rows = own.shape[0]
    here = pl.ds(pl.multiple_of(me[0] * rows, rows), rows)
    copies = [
        pltpu.make_async_copy(table.at[here, :], turns.at[n], sems.at[n])
        for n, table in enumerate((keep, low, high))
    ]
    for copy in copies:
        copy.start()
    total = add_up(got)
    for copy in copies:
        copy.wait()

    def back(lanes, gain):
        upstream, values = total[:, lanes], latents[:, lanes]
        factor = root(values)
        normed = values * factor
        gain_part[:, lanes] = jnp.sum(upstream * normed, axis=0, keepdims=True)
        return norm_back(upstream, normed, factor, row(gain)).astype(BF16)

    own[:, :QR] = back(slice(0, QR), query_gain)
    own[:, QR:LAT] = back(slice(QR, LAT), latent_gain)
    own[:, LAT:] = turn(total[:, LAT:], turns[0], turns[1], turns[2], back=True).astype(BF16)
    for k in range(8):
        many[k] = own[...]


def latents_back_of(me, got, latents, query_gain, latent_gain, tables, needs):
    rows = latents.shape[0]
    return call(
        latents_back_kernel,
        (got.reshape(8, rows, WIDE), latents, query_gain, latent_gain, *tables),
        [full((8, rows, WIDE)), full(latents.shape), full((QR,)), full((KVR,)), HBM, HBM, HBM],
        [full((8, rows, WIDE)), full((rows, WIDE)), full((1, LAT))],
        [shaped(8, rows, WIDE), shaped(rows, WIDE), shaped(1, LAT, dtype=F32)],
        "latents_back",
        scratch=[
            pltpu.VMEM((3, rows, 128), F32),
            pltpu.SemaphoreType.DMA((3,)),
        ],
        needs=needs,
        me=me,
        limit=24,
    )


def first_back_of(raw_back, query_down, latent_down, rope_down):
    rope_down[...] = jnp.zeros_like(rope_down)
    rope_down[64:96, :] = latent_down[KVR:, :]
    return (
        dot(raw_back[:, :QR], query_down[...], NT)
        + dot(raw_back[:, QR:LAT], latent_down[:KVR, :])
        + dot(raw_back[:, LAT:], rope_down[...])
    )


def first_gain_kernel(
    me, raw_back, tokens, query_down, latent_down, gain_part, rope_down, own, sem
):
    rows = own.shape[0]
    here = pl.ds(pl.multiple_of(me[0] * rows, rows), rows)
    copy = pltpu.make_async_copy(tokens.at[here, :], own, sem)
    copy.start()
    first_back = first_back_of(raw_back, query_down, latent_down, rope_down)
    copy.wait()
    values = own[...].astype(F32)
    gain_part[...] = jnp.sum(first_back * (values * root(values)), axis=0, keepdims=True)


def first_gain_of(me, own_raw_back, tokens, query_down, latent_down, needs):
    width = tokens.shape[1]
    return call(
        first_gain_kernel,
        (own_raw_back, tokens, query_down, latent_down.T),
        [full(own_raw_back.shape), HBM, full(query_down.shape), full(latent_down.shape[::-1])],
        [full((1, width))],
        [shaped(1, width, dtype=F32)],
        "first_gain",
        scratch=[
            pltpu.VMEM((128, width), BF16),
            pltpu.VMEM((own_raw_back.shape[0], width), BF16),
            pltpu.SemaphoreType.DMA,
        ],
        needs=needs,
        me=me,
    )


def tokens_back_kernel(
    raw_back, tokens, attention_back, query_down, latent_down, gain, tokens_grad, rope_down
):
    first_back = first_back_of(raw_back, query_down, latent_down, rope_down)
    values = tokens[...].astype(F32)
    factor = root(values)
    tokens_grad[...] = attention_back[...].astype(F32) + norm_back(
        first_back, values * factor, factor, row(gain)
    )


def tokens_back_of(raw_back, tokens, attention_back, query_down, latent_down, gain, needs):
    length, width = tokens.shape

    def rows(columns):
        return pl.BlockSpec((TILE, columns), lambda i, *_: (i, 0))

    return call(
        tokens_back_kernel,
        (raw_back, tokens, attention_back, query_down, latent_down.T, gain),
        [
            rows(WIDE),
            rows(width),
            rows(width),
            full(query_down.shape),
            full(latent_down.shape[::-1]),
            full((width,)),
        ],
        [rows(width)],
        [shaped(length, width, dtype=F32)],
        "tokens_back",
        grid=(length // TILE,),
        scratch=[pltpu.VMEM((128, width), BF16)],
        needs=needs,
    )


def finish_ffn_kernel(keep, got, gate, up, down):
    units = gate.shape[1]
    for n, out in enumerate((gate, up, down)):
        lanes = slice(units * n, units * n + units)
        out[...] = keep[:, lanes] + got[:, lanes].astype(F32)


def finish_ffn(keep, got, needs):
    rows, width = keep.shape
    out = (rows, width // 3)
    return call(
        finish_ffn_kernel,
        (keep, got),
        [full(keep.shape), full(got.shape)],
        [full(out)] * 3,
        [shaped(*out, dtype=F32)] * 3,
        "finish_ffn",
        needs=needs,
    )


def finish_attn_kernel(heads, keep, got, out_grad, query_grad, latent_grad):
    total = keep[...] + got[...].astype(F32)
    for h in range(heads):
        lanes = slice(128 * h, 128 * h + 128)
        out_grad[:, 64 * h : 64 * h + 64] = total[:160, 128 * h + 64 : 128 * h + 128]
        query_grad[:, 96 * h : 96 * h + 96] = total[160:208, 128 * h : 128 * h + 96]
    latent_grad[...] = total[208:224]


def finish_attn(keep, got, needs):
    heads = keep.shape[1] // 128
    outs = [(160, 64 * heads), (48, 96 * heads), (16, 128 * heads)]
    return call(
        functools.partial(finish_attn_kernel, heads),
        (keep, got),
        [full(keep.shape), full(got.shape)],
        [full(s) for s in outs],
        [shaped(*s, dtype=F32) for s in outs],
        "finish_attn",
        needs=needs,
    )


GAINS = ((0, 160), (160, 160), (320, 48), (368, 16))


def down_parts_kernel(own_in, raw_back, gains, out):
    total = dot(own_in[...], raw_back[...]).astype(BF16)
    for d in range(16):
        out[d, :20, :] = total[20 * d : 20 * d + 20]
        out[d, 20:, :] = jnp.zeros((4, WIDE), BF16)
        out[d, 20:21, :] = gains[d : d + 1, :]


def down_parts(own_in, raw_back, gains, needs):
    args = (own_in, raw_back, gains)
    return call(
        down_parts_kernel,
        args,
        [full(item.shape) for item in args],
        [full((16, 24, WIDE))],
        [shaped(16, 24, WIDE)],
        "down_parts",
        needs=needs,
        limit=24,
    )


def sum_copies_kernel(got, many):
    total = got[0].astype(F32)
    for d in range(1, 16):
        total = total + got[d].astype(F32)
    for k in range(8):
        many[k] = total.astype(BF16)


def sum_copies(got, needs):
    return call(
        sum_copies_kernel,
        (got,),
        [full(got.shape)],
        [full((8, 24, WIDE))],
        [shaped(8, 24, WIDE)],
        "sum_copies",
        needs=needs,
        limit=24,
    )


def finish_down_kernel(everyone, query_grad, latent_grad, *gains):
    for t in range(8):
        values = everyone[t].astype(F32)
        query_grad[20 * t : 20 * t + 20, :] = values[:20, :QR]
        latent_grad[20 * t : 20 * t + 20, :KVR] = values[:20, QR:LAT]
        latent_grad[20 * t : 20 * t + 20, KVR:] = values[:20, LAT + 64 : LAT + 96]
    total = sum(everyone[t, 16:24, :].astype(F32) for t in range(8))[4:5, :]
    for out, (first, count) in zip(gains, GAINS):
        out[...] = total[:, first : first + count]


def finish_down(everyone):
    everyone = everyone.reshape(8, 24, WIDE)
    outs = [(160, QR), (160, KVR + ROPE)] + [(1, count) for _, count in GAINS]
    return call(
        finish_down_kernel,
        (everyone,),
        [full(everyone.shape)],
        [full(s) for s in outs],
        [shaped(*s, dtype=F32) for s in outs],
        "finish_down",
        limit=24,
    )[0]


def exchange(blocks):
    return lax.all_to_all(blocks.reshape(-1, blocks.shape[-1]), TP, 0, 0, tiled=True)


def on_device(
    tokens,
    first_gain,
    query_down,
    query_gain,
    query_up,
    latent_down,
    latent_gain,
    latent_up,
    out_weight,
    second_gain,
    gate_weight,
    up_weight,
    down_weight,
    cotangent,
):
    length = tokens.shape[0]
    me = lax.axis_index(TP).astype(jnp.int32).reshape(1)
    y, xl, core = lax.axis_index("y"), lax.axis_index("xl"), lax.axis_index("core")
    starts = jnp.stack(
        [
            ((y + k) % 4 * 2 + (xl ^ j)) * 2 + c
            for c in (core, 1 - core)
            for k in range(4)
            for j in range(2)
        ]
    ).astype(jnp.int32)
    places = jnp.stack([(lax.axis_index("z") + k) % 4 for k in range(4)] + [me[0]]).astype(jnp.int32)
    tables = rope_tables(length)

    gate_turned, up_turned = gate_weight.T, up_weight.T

    (
        first_in,
        latents,
        query_code,
        latent_code,
        queries,
        keyvals,
        rope_keys,
        heads_out,
        log_total,
        attn_partial,
    ), started = attend(
        me,
        tokens,
        first_gain,
        query_down,
        latent_down,
        query_gain,
        latent_gain,
        query_up,
        latent_up,
        out_weight,
        tables,
    )
    attn_got = exchange(attn_partial)

    (cot_keep, cot_give), picked = halves(starts, [cotangent], [started])
    inner_back = dot(cotangent, down_weight, NT)
    cot_got = over_cores(cot_give)

    (residual, second_many), _ = residual_of(
        me, attn_got, tokens, second_gain, [picked, cot_got]
    )
    second_in = exchange(second_many)

    turned_in = first_in.T.reshape(16, 8, 20, length)
    own_in = lax.dynamic_slice_in_dim(turned_in, me[0], 1, 1).reshape(320, length)
    (code_keep, code_give, lat_keep, lat_give), picked = halves(
        starts, [query_code, latent_code], [residual]
    )
    code_got, lat_got = over_cores(code_give), over_cores(lat_give)
    heads_got = over_cores(heads_out)

    (gate_back, up_back, inner, back_partial), done = ffn(
        second_in, gate_turned, up_turned, inner_back, [picked, own_in, code_got, lat_got, heads_got]
    )
    back_got = exchange(back_partial)

    ours = (gate_back, up_back, inner)
    theirs = [over_cores(item) for item in ours]
    (in_keep, in_give), _ = halves(starts, [second_in], [done])
    in_got = over_cores(in_give)
    (far_up, far_down, ffn_up, ffn_down_way, ffn_own), done = ffn_grads(in_keep, in_got, cot_keep, cot_got, ours, theirs, gate_weight.shape[1], [])
    below, above = lax.ppermute(far_up, "y", UP), lax.ppermute(far_down, "y", DOWN)

    (back_many, second_gain_part), done = residual_back_of(
        me, back_got, residual, cotangent, second_gain, [done]
    )
    attention_back = exchange(back_many)
    (far_up, far_down, mixed_up, mixed_down, mixed_own), done = ffn_down(
        places, inner, down_weight, residual, [done]
    )
    lower, upper = lax.ppermute(far_up, "z", UP), lax.ppermute(far_down, "z", DOWN)
    (ffn_up, ffn_down_way, mixed_up, mixed_down), done = relay(
        [(ffn_up, below, ffn_down_way, above), (mixed_up, lower, mixed_down, upper)], [done]
    )
    below, above = lax.ppermute(ffn_up, "y", UP), lax.ppermute(ffn_down_way, "y", DOWN)
    lower, upper = lax.ppermute(mixed_up, "z", UP), lax.ppermute(mixed_down, "z", DOWN)

    (both_back, latents_partial), back_done = attend_back(
        attention_back,
        out_weight,
        queries,
        keyvals,
        rope_keys,
        log_total,
        query_up,
        latent_up,
        tables,
        [done],
    )
    latents_got = exchange(latents_partial)

    (mixed_part,), done = add_all([mixed_own, lower, upper], [back_done])
    mixed_other = lax.ppermute(mixed_part, "xh", SWAP)
    (out_keep, out_give), done = halves(starts, [attention_back], [done])
    (ffn_keep, ffn_give), done = add_chips([ffn_own, below, above], [done])
    ffn_got = lax.ppermute(ffn_give, "xl", SWAP)

    (raw_many, own_raw, latent_gain_parts), done = latents_back_of(
        me, latents_got, latents, query_gain, latent_gain, tables, [done]
    )
    raw_back = exchange(raw_many)

    out_got, both_got = over_cores(out_give), over_cores(both_back)
    (attn_across, attn_up, attn_down, attn_own), done = attn_grads(
        (out_keep, code_keep, lat_keep),
        (out_got, code_got, lat_got),
        (heads_out, both_back),
        (heads_got, both_got),
        [done],
    )
    attn_got = [
        lax.ppermute(attn_across, "y", ACROSS),
        lax.ppermute(attn_up, "y", UP),
        lax.ppermute(attn_down, "y", DOWN),
    ]
    (first_gain_part,), gain_done = first_gain_of(
        me, own_raw, tokens, query_down, latent_down, [done]
    )


    gains = jnp.concatenate(
        [
            first_gain_part.reshape(16, -1),
            second_gain_part.reshape(16, -1),
            latent_gain_parts[0, :QR].reshape(16, -1),
            latent_gain_parts[0, QR:].reshape(16, -1),
        ],
        axis=1,
    ).astype(BF16)
    gains = jnp.pad(gains, ((0, 0), (0, WIDE - gains.shape[1])))
    (parts,), done = down_parts(own_in, raw_back, gains, [attn_got[1], attn_got[2]])
    parts_got = lax.all_to_all(parts, DP, 0, 0, tiled=True)

    (mixed_part,), done = add_all([mixed_part, mixed_other], [done])
    mixed_got = [
        lax.ppermute(mixed_part, "z", way) for way in (DOWN, ACROSS, UP)
    ]
    (tokens_grad,), done = tokens_back_of(
        raw_back, tokens, attention_back, query_down, latent_down, first_gain, [done]
    )
    (many,), summed = sum_copies(parts_got, [done])
    everyone = exchange(many)

    (attn_keep, attn_give), done = add_chips([attn_own, *attn_got], [summed])
    attn_other = lax.ppermute(attn_give, "xl", SWAP)
    (gate_weight_grad, up_weight_grad, down_weight_grad), done = finish_ffn(
        ffn_keep, ffn_got, [done]
    )
    (out_weight_grad, query_up_grad, latent_up_grad), done = finish_attn(
        attn_keep, attn_other, [done]
    )
    (
        query_down_grad,
        latent_down_grad,
        first_gain_grad,
        second_gain_grad,
        query_gain_grad,
        latent_gain_grad,
    ) = finish_down(everyone)

    mixed = assemble(places, [mixed_part, *mixed_got])

    return (
        mixed,
        tokens_grad,
        first_gain_grad[0],
        query_down_grad,
        query_gain_grad[0],
        query_up_grad,
        latent_down_grad,
        latent_gain_grad[0],
        latent_up_grad,
        out_weight_grad.T,
        second_gain_grad[0],
        gate_weight_grad,
        up_weight_grad,
        down_weight_grad.T,
    )


def solution(mesh):
    grid = Mesh(mesh.devices.reshape(4, 2, 2, 2, 4), ("y", "xl", "core", "xh", "z"))
    in_specs = (
        P(DP, None),
        P(),
        P(),
        P(),
        P(None, TP),
        P(),
        P(),
        P(None, TP),
        P(TP, None),
        P(),
        P(None, TP),
        P(None, TP),
        P(TP, None),
        P(DP, None),
    )
    out_specs = (
        P(DP, None),
        P(DP, None),
        P(DP),
        P(DP, None),
        P(DP),
        P(DP, TP),
        P(DP, None),
        P(DP),
        P(DP, TP),
        P(TP, DP),
        P(DP),
        P(DP, TP),
        P(DP, TP),
        P(TP, DP),
    )
    return jax.shard_map(
        on_device, mesh=grid, in_specs=in_specs, out_specs=out_specs, check_vma=False
    )
```

```python
import functools

import jax
import jax.numpy as jnp
import numpy as np
from jax import lax
from jax.experimental import pallas as pl
from jax.experimental.pallas import tpu as pltpu
from jax.sharding import Mesh, PartitionSpec as P

NOPE = 64
ROPE = 32
DV = 64
KVR = 256
QR = 768
LAT = QR + KVR
WIDE = LAT + 128

EPS = 1e-05
BASE = 10000.0
SCALE = (NOPE + ROPE) ** (-0.5)

DP = ("y", "xl", "core")
TP = ("xh", "z")
SWAP = [(0, 1), (1, 0)]
F32 = jnp.float32
BF16 = jnp.bfloat16
NT = (((1,), (1,)), ((), ()))
TN = (((0,), (0,)), ((), ()))
NN = (((1,), (0,)), ((), ()))
TILE = 256


def dot(left, right, dims=NN):
    return lax.dot_general(left, right, dims, preferred_element_type=F32)


def params(limit=56):
    return pltpu.CompilerParams(vmem_limit_bytes=limit * 2**20)


HBM = pl.BlockSpec(memory_space=pltpu.HBM)


def call(kernel, args, in_specs, out_specs, out_shape, name, grid=(1,), scratch=(), needs=(), me=None, limit=60):
    first = 0 if me is None else 1
    n_in, n_out = len(args), len(out_shape)

    def body(*refs):
        ins = refs[: first + n_in]
        rest = refs[first + n_in + len(needs) :]
        mark = rest[n_out]

        @pl.when(pl.program_id(0) == 0)
        def _():
            mark[...] = jnp.zeros_like(mark)

        kernel(*ins, *rest[:n_out], *rest[n_out + 1 :])

    *outs, mark = pl.pallas_call(
        body,
        grid_spec=pltpu.PrefetchScalarGridSpec(
            num_scalar_prefetch=first,
            grid=grid,
            in_specs=list(in_specs) + [HBM] * len(needs),
            out_specs=list(out_specs) + [full((8, 128))],
            scratch_shapes=list(scratch),
        ),
        out_shape=list(out_shape) + [jax.ShapeDtypeStruct((8, 128), F32)],
        compiler_params=params(limit),
        cost_estimate=pl.CostEstimate(flops=1, bytes_accessed=1, transcendentals=0),
        name=name,
    )(*(() if me is None else (me,)), *args, *needs)
    return outs, mark


def shaped(*shape, dtype=BF16):
    return jax.ShapeDtypeStruct(shape, dtype)


def full(shape):
    return pl.BlockSpec(shape, lambda *_: (0,) * len(shape))


def rope_tables(length):
    half = ROPE // 2
    rates = np.exp(np.arange(half, dtype=np.float32) * np.float32(-2.0 * np.log(BASE) / ROPE))
    angles = np.arange(length, dtype=np.float32)[:, None] * rates.astype(np.float32)[None, :]
    cosine, sine = np.cos(angles), np.sin(angles)
    keep = np.zeros((length, 128), np.float32)
    keep[:, :NOPE] = 1.0
    keep[:, 64:80] = cosine
    keep[:, 80:96] = cosine
    low = np.zeros((length, 128), np.float32)
    low[:, 64:80] = -sine
    high = np.zeros((length, 128), np.float32)
    high[:, 80:96] = sine
    return jnp.asarray(keep), jnp.asarray(low), jnp.asarray(high)


def turn(values, keep, low, high, back=False):
    moved = pltpu.roll(values, 112, 1) * low + pltpu.roll(values, 16, 1) * high
    return values * keep - moved if back else values * keep + moved


def root(values):
    return lax.rsqrt(jnp.mean(values * values, axis=-1, keepdims=True) + EPS)


def norm_back(upstream, normed, factor, gain):
    scaled = upstream * gain
    return factor * (scaled - normed * jnp.mean(scaled * normed, axis=-1, keepdims=True))


def spread_out_weight(weight_ref, spread_ref, heads):
    spread_ref[...] = jnp.zeros_like(spread_ref)
    for h in range(heads):
        spread_ref[128 * h + 64 : 128 * h + 128, :] = weight_ref[64 * h : 64 * h + 64, :]


def spread_query_up(weight_ref, spread_ref, heads):
    spread_ref[...] = jnp.zeros_like(spread_ref)
    for h in range(heads):
        spread_ref[128 * h : 128 * h + 96, :] = weight_ref[96 * h : 96 * h + 96, :]


def row(ref):
    return ref[...].reshape(1, -1)


def low_lanes(shape):
    return lax.broadcasted_iota(jnp.int32, shape, 1) < NOPE


def causal(keys, queries, first_query):
    key_ids = lax.broadcasted_iota(jnp.int32, (keys, queries), 0)
    query_ids = lax.broadcasted_iota(jnp.int32, (keys, queries), 1) + first_query
    return key_ids <= query_ids


def attend_kernel(
    heads,
    me,
    tokens,
    first_gain,
    query_down,
    latent_down,
    query_gain,
    latent_gain,
    query_up,
    latent_up,
    out_weight,
    keep,
    low,
    high,
    first_in,
    latents,
    query_code,
    latent_code,
    queries,
    keyvals,
    rope_keys,
    heads_out,
    log_total,
    partial,
    raw_latents,
    spread,
    spread_up,
    rope_down,
    kv_all,
    rope_all,
):
    step = pl.program_id(0)

    @pl.when(step == 0)
    def _():
        spread_out_weight(out_weight, spread, heads)
        spread_query_up(query_up, spread_up, heads)
        rope_down[...] = jnp.zeros_like(rope_down)
        rope_down[64:96, :] = latent_down[KVR:, :]

    def rows_of(index, carry):
        rows = pl.ds(pl.multiple_of(index * 32, 32), 32)
        values = tokens[rows, :].astype(F32)
        first_in[rows, :] = (values * root(values) * row(first_gain)).astype(BF16)
        return carry

    lax.fori_loop(0, TILE // 32, rows_of, 0)
    taken = first_in[...]
    query_latent = dot(taken, query_down[...])
    raw_latents[:, :QR] = query_latent
    code = (query_latent * root(query_latent) * row(query_gain)).astype(BF16)
    query_code[...] = code
    latent = dot(taken, latent_down[:KVR, :], NT)
    raw_latents[:, QR:] = latent
    count = latents.shape[0]
    own = me[0] * count

    @pl.when(own // TILE == step)
    def _():
        latents[...] = raw_latents[pl.ds(pl.multiple_of(own % TILE, count), count), :]

    lcode = (latent * root(latent) * row(latent_gain)).astype(BF16)
    latent_code[...] = lcode
    tables = keep[...], low[...], high[...]
    rope = turn(dot(taken, rope_down[...], NT), *tables).astype(BF16)
    rope_keys[...] = rope
    here = pl.ds(pl.multiple_of(step * TILE, TILE), TILE)
    rope_all[here, :] = rope
    kv = dot(lcode, latent_up[...]).astype(BF16)
    keyvals[...] = kv
    kv_all[here, :] = kv
    raw = dot(code, spread_up[...], NT)
    for h in range(heads):
        lanes = slice(128 * h, 128 * h + 128)
        queries[:, lanes] = turn(raw[:, lanes], *tables).astype(BF16)

    def tile(index):
        keys = TILE * (index + 1)
        for h in range(heads):
            lanes = slice(128 * h, 128 * h + 128)
            kv_h = kv_all[:keys, lanes]
            key = jnp.where(low_lanes((keys, 128)), kv_h, rope_all[:keys, :])
            scores = dot(key, queries[:, lanes], NT) * SCALE
            scores = jnp.where(causal(keys, TILE, TILE * index), scores, -1e30)
            top = jnp.max(scores, axis=0, keepdims=True)
            weights = jnp.exp(scores - top)
            total = jnp.sum(weights, axis=0, keepdims=True)
            log_total[h : h + 1, :] = top + jnp.log(total)
            probs = (weights * (1.0 / total)).astype(BF16)
            heads_out[:, lanes] = dot(probs, kv_h, TN).astype(BF16)

    for index in range(2):
        pl.when(step == index)(functools.partial(tile, index))
    partial[...] = dot(heads_out[...], spread[...]).astype(BF16)


def attend(me, tokens, first_gain, query_down, latent_down, query_gain, latent_gain, query_up, latent_up, out_weight, tables):
    latent_down, query_up = latent_down.T, query_up.T
    length, width = tokens.shape
    heads = out_weight.shape[0] // DV
    wide = 128 * heads

    def rows(columns):
        return pl.BlockSpec((TILE, columns), lambda i, *_: (i, 0))

    return call(
        functools.partial(attend_kernel, heads),
        (tokens, first_gain, query_down, latent_down, query_gain, latent_gain, query_up, latent_up, out_weight, *tables),
        [
            rows(width),
            full((width,)),
            full(query_down.shape),
            full(latent_down.shape),
            full((QR,)),
            full((KVR,)),
            full(query_up.shape),
            full(latent_up.shape),
            full(out_weight.shape),
            rows(128),
            rows(128),
            rows(128),
        ],
        [
            rows(width),
            full((length // 8, LAT)),
            rows(QR),
            rows(KVR),
            rows(wide),
            rows(wide),
            rows(128),
            rows(wide),
            pl.BlockSpec((8, TILE), lambda i, *_: (0, i)),
            rows(width),
        ],
        [
            shaped(length, width),
            shaped(length // 8, LAT, dtype=F32),
            shaped(length, QR),
            shaped(length, KVR),
            shaped(length, wide),
            shaped(length, wide),
            shaped(length, 128),
            shaped(length, wide),
            shaped(8, length, dtype=F32),
            shaped(length, width),
        ],
        "attend",
        grid=(length // TILE,),
        me=me,
        scratch=[
            pltpu.VMEM((TILE, LAT), F32),
            pltpu.VMEM((wide, width), BF16),
            pltpu.VMEM((wide, QR), BF16),
            pltpu.VMEM((128, width), BF16),
            pltpu.VMEM((length, wide), BF16),
            pltpu.VMEM((length, 128), BF16),
        ],
    )


def attend_back_kernel(
    heads,
    attention_back,
    out_weight,
    queries,
    keyvals,
    rope_keys,
    log_total,
    query_up,
    latent_up,
    keep,
    low,
    high,
    both_back,
    partial,
    spread,
    spread_up,
    kv_grad,
    rope_grad,
    code_grad,
):
    step = pl.program_id(0)

    @pl.when(step == 0)
    def _():
        spread_out_weight(out_weight, spread, heads)
        spread_query_up(query_up, spread_up, heads)
        kv_grad[...] = jnp.zeros_like(kv_grad)
        rope_grad[...] = jnp.zeros_like(rope_grad)

    heads_back = dot(attention_back[...], spread[...], NT).astype(BF16)
    tables = keep[...], low[...], high[...]

    def tile(index):
        keys = TILE * (index + 1)
        low_part = low_lanes((keys, 128))
        for h in range(heads):
            lanes = slice(128 * h, 128 * h + 128)
            kv_h = keyvals[:keys, lanes]
            key = jnp.where(low_part, kv_h, rope_keys[:keys, :])
            query = queries[:, lanes]
            back = heads_back[:, lanes]
            scores = dot(key, query, NT) * SCALE
            probs = jnp.exp(scores - log_total[h : h + 1, :])
            probs = jnp.where(causal(keys, TILE, TILE * index), probs, 0.0)
            prob_back = dot(kv_h, back, NT)
            mean = jnp.sum(probs * prob_back, axis=0, keepdims=True)
            score_back = (probs * (prob_back - mean)).astype(BF16)
            of_values = dot(probs.astype(BF16), back)
            of_keys = dot(score_back, query) * SCALE
            kv_grad[:keys, lanes] += of_values + jnp.where(low_part, of_keys, 0.0)
            rope_grad[:keys, :] += jnp.where(low_part, 0.0, of_keys)
            of_query = dot(score_back, key, TN) * SCALE
            both_back[here, lanes] = turn(of_query, *tables, back=True).astype(BF16)

    wide = 128 * heads
    here = pl.ds(pl.multiple_of(step * TILE, TILE), TILE)
    for index in range(2):
        pl.when(step == index)(functools.partial(tile, index))
    code_grad[here, :] = dot(both_back[here, :wide], spread_up[...]).astype(BF16)

    @pl.when(step == 1)
    def _():
        kv = kv_grad[...].astype(BF16)
        both_back[:, wide:] = kv
        partial[:, :QR] = code_grad[...]
        partial[:, QR:LAT] = dot(kv, latent_up[...], NT).astype(BF16)
        partial[:, LAT:] = rope_grad[...].astype(BF16)


def attend_back(attention_back, out_weight, queries, keyvals, rope_keys, log_total, query_up, latent_up, tables, needs):
    query_up = query_up.T
    length, width = attention_back.shape
    heads = out_weight.shape[0] // DV
    wide = 128 * heads

    def rows(columns):
        return pl.BlockSpec((TILE, columns), lambda i, *_: (i, 0))

    return call(
        functools.partial(attend_back_kernel, heads),
        (attention_back, out_weight, queries, keyvals, rope_keys, log_total, query_up, latent_up, *tables),
        [
            rows(width),
            full(out_weight.shape),
            rows(wide),
            full((length, wide)),
            full((length, 128)),
            pl.BlockSpec((8, TILE), lambda i, *_: (0, i)),
            full(query_up.shape),
            full(latent_up.shape),
            rows(128),
            rows(128),
            rows(128),
        ],
        [full((length, 2 * wide)), full((length, WIDE))],
        [shaped(length, 2 * wide), shaped(length, WIDE)],
        "attend_back",
        grid=(length // TILE,),
        scratch=[
            pltpu.VMEM((wide, width), BF16),
            pltpu.VMEM((wide, QR), BF16),
            pltpu.VMEM((length, wide), F32),
            pltpu.VMEM((length, 128), F32),
            pltpu.VMEM((length, QR), BF16),
        ],
        needs=needs,
    )


def add_up(got):
    total = got[0].astype(F32)
    for k in range(1, 8):
        total = total + got[k].astype(F32)
    return total


STEPS = 2


def residual_kernel(me, got, tokens, gain, residual, many):
    del me
    total = tokens[...].astype(F32) + add_up(got)
    residual[...] = total
    second_in = (total * root(total) * row(gain)).astype(BF16)
    for k in range(8):
        many[k] = second_in


def own_specs(rows, width):
    step = rows // STEPS
    return (
        pl.BlockSpec((8, step, width), lambda i, me: (0, i, 0)),
        pl.BlockSpec((step, width), lambda i, me: (i, 0)),
        pl.BlockSpec((step, width), lambda i, me: (me[0] * STEPS + i, 0)),
    )


def residual_of(me, got, tokens, gain, needs):
    width = tokens.shape[1]
    rows = tokens.shape[0] // 8
    eight, one, own = own_specs(rows, width)
    return call(
        residual_kernel,
        (got.reshape(8, rows, width), tokens, gain),
        [eight, own, full((width,))],
        [one, eight],
        [shaped(rows, width, dtype=F32), shaped(8, rows, width)],
        "residual",
        grid=(STEPS,),
        needs=needs,
        me=me,
        limit=58,
    )


def residual_back_kernel(me, got, residual, cotangent, gain, many, gain_part):
    del me
    second_back = add_up(got)
    values = residual[...]
    factor = root(values)
    normed = values * factor
    part = jnp.sum(second_back * normed, axis=0, keepdims=True)

    @pl.when(pl.program_id(0) == 0)
    def _():
        gain_part[...] = part

    @pl.when(pl.program_id(0) > 0)
    def _():
        gain_part[...] += part

    back = cotangent[...].astype(F32) + norm_back(second_back, normed, factor, row(gain))
    back = back.astype(BF16)
    for k in range(8):
        many[k] = back


def residual_back_of(me, got, residual, cotangent, gain, needs):
    rows, width = residual.shape
    eight, one, own = own_specs(rows, width)
    return call(
        residual_back_kernel,
        (got.reshape(8, rows, width), residual, cotangent, gain),
        [eight, one, own, full((width,))],
        [eight, full((1, width))],
        [shaped(8, rows, width), shaped(1, width, dtype=F32)],
        "residual_back",
        grid=(STEPS,),
        needs=needs,
        me=me,
        limit=58,
    )


def ffn_kernel(
    second_in, gate_weight, up_weight, inner_back, gate_back, up_back, inner, partial
):
    taken = second_in[...]
    gate = dot(taken, gate_weight[...], NT)
    up = dot(taken, up_weight[...], NT)
    sigma = 1.0 / (1.0 + jnp.exp(-gate))
    act = gate * sigma
    units = gate.shape[1]
    back = inner_back[...]
    of_gate = (back * up * sigma * (1.0 + gate * (1.0 - sigma))).astype(BF16)
    of_up = (back * act).astype(BF16)
    for out, values in ((gate_back, of_gate), (up_back, of_up), (inner, (act * up).astype(BF16))):
        out[:, :units] = values
        out[:, units:] = jnp.zeros((values.shape[0], out.shape[1] - units), BF16)
    partial[...] = (dot(of_gate, gate_weight[...]) + dot(of_up, up_weight[...])).astype(BF16)


def ffn(second_in, gate_weight, up_weight, inner_back, needs):
    length, width = second_in.shape
    units = gate_weight.shape[0]
    wide = -(-units // 128) * 128

    def rows(columns):
        return pl.BlockSpec((TILE, columns), lambda i, *_: (i, 0))

    return call(
        ffn_kernel,
        (second_in, gate_weight, up_weight, inner_back),
        [rows(width), full((units, width)), full((units, width)), rows(units)],
        [rows(wide), rows(wide), rows(wide), rows(width)],
        [shaped(length, wide)] * 3 + [shaped(length, width)],
        "ffn",
        grid=(length // TILE,),
        needs=needs,
    )


def ffn_down_kernel(places, inner, down_weight, residual, *refs):
    outs, total = refs[:4], refs[4]
    for i in range(2):
        rows = slice(i * TILE, i * TILE + TILE)
        total[rows, :] = dot(inner[rows, : down_weight.shape[0]], down_weight[...]).astype(BF16)
    count = residual.shape[0]
    own = pl.ds(pl.multiple_of(places[4] * count, count), count)
    total[own, :] = (total[own, :].astype(F32) + residual[...]).astype(BF16)
    for k, out in enumerate(outs):
        rows = out.shape[0]
        out[...] = total[pl.ds(pl.multiple_of(places[k] * rows, rows), rows), :]


def ffn_down(places, inner, down_weight, residual, needs):
    length, width = inner.shape[0], down_weight.shape[1]
    block = (length // 4, width)
    return call(
        ffn_down_kernel,
        (inner, down_weight, residual),
        [full(inner.shape), full(down_weight.shape), full(residual.shape)],
        [full(block)] * 4,
        [shaped(*block)] * 4,
        "ffn_down",
        scratch=[pltpu.VMEM((length, width), BF16)],
        needs=needs,
        me=places,
    )


def halves_kernel(blocks, width, starts, *refs):
    sources, outs, turned = refs[:blocks], refs[blocks : 3 * blocks], refs[3 * blocks]
    for n in range(blocks):
        source, keep, give = sources[n], outs[2 * n], outs[2 * n + 1]
        columns, each = source.shape[1], width[n]
        for c in range(0, columns, 256):
            turned[c : c + 256, :] = source[:, c : c + 256].T
        for which, out in enumerate((keep, give)):
            for k in range(8):
                first = pl.multiple_of(starts[8 * which + k] * each, 16)
                out[each * k : each * k + each, :] = turned[pl.ds(first, each), :]


def halves(starts, values, needs):
    length = values[0].shape[0]
    widths = [item.shape[1] // 16 for item in values]
    shapes = [(8 * w, length) for w in widths for _ in range(2)]
    return call(
        functools.partial(halves_kernel, len(values), widths),
        tuple(values),
        [full(item.shape) for item in values],
        [full(s) for s in shapes],
        [shaped(*s) for s in shapes],
        "halves",
        scratch=[pltpu.VMEM((max(item.shape[1] for item in values), length), BF16)],
        needs=needs,
        me=starts,
    )


ORDER = (2, 1, 3, 0)


def ffn_grads_kernel(in_keep, in_got, cot_keep, cot_got, *refs):
    ours, theirs, outs = refs[:3], refs[3:6], refs[6:]
    units = outs[0].shape[1] // 3

    def block(*parts):
        for n, (keep, got) in enumerate(((in_keep, in_got), (in_keep, in_got), (cot_keep, cot_got))):
            total = dot(keep[...], ours[n][...]) + dot(got[...], theirs[n][...])
            total = total[:, :units].astype(BF16)
            first = 0
            for out in parts:
                count = out.shape[0]
                out[:, units * n : units * n + units] = total[first : first + count]
                first += count

    for s, parts in enumerate((outs[:2], outs[2:3], outs[3:4], outs[4:])):
        pl.when(pl.program_id(0) == s)(functools.partial(block, *parts))


def ffn_grads(in_keep, in_got, cot_keep, cot_got, ours, theirs, units, needs):
    length, wide = ours[0].shape
    rows = in_keep.shape[0] // 4

    def index(i):
        return (jnp.where(i == 0, 2, jnp.where(i == 1, 1, jnp.where(i == 2, 3, 0))), 0)

    left = pl.BlockSpec((rows, length), index)
    out = (rows, 3 * units)
    outs = [(rows // 2, 3 * units)] * 2 + [out] * 3
    return call(
        ffn_grads_kernel,
        (in_keep, in_got, cot_keep, cot_got, *ours, *theirs),
        [left] * 4 + [full((length, wide))] * 6,
        [full(s) for s in outs],
        [shaped(*s) for s in outs],
        "ffn_grads",
        grid=(4,),
        needs=needs,
    )


def attn_grads_kernel(widths, *refs):
    keeps, gots, outs = refs[:3], refs[3:6], refs[10:]
    wide = outs[0].shape[1]
    ours, theirs = (
        (heads, both.at[:, :wide], both.at[:, wide:]) for heads, both in (refs[6:8], refs[8:10])
    )
    rows = sum(widths)
    for out, k in zip(outs, ORDER):
        first = 0
        for n, each in enumerate(widths):
            part = slice(2 * each * k, 2 * each * k + 2 * each)
            total = dot(keeps[n][part, :], ours[n][...]) + dot(gots[n][part, :], theirs[n][...])
            total = total.astype(BF16)
            out[first : first + each, :] = total[:each]
            out[rows + first : rows + first + each, :] = total[each:]
            first += each


def attn_grads(keeps, gots, ours, theirs, needs):
    widths = [item.shape[0] // 8 for item in keeps]
    rows, wide = sum(widths), ours[0].shape[1]
    args = (*keeps, *gots, *ours, *theirs)
    outs = [(2 * rows, wide)] * 4
    return call(
        functools.partial(attn_grads_kernel, widths),
        args,
        [full(item.shape) for item in args],
        [full(s) for s in outs],
        [shaped(*s) for s in outs],
        "attn_grads",
        needs=needs,
    )


UP = [(i, (i + 1) % 4) for i in range(4)]
DOWN = [(i, (i + 3) % 4) for i in range(4)]
ACROSS = [(i, (i + 2) % 4) for i in range(4)]


def relay_kernel(up, from_below, down, from_above, up_out, down_out):
    @pl.when(pl.program_id(0) == 0)
    def _():
        up_out[...] = (up[...].astype(F32) + from_below[...].astype(F32)).astype(BF16)
        down_out[...] = down[...]

    @pl.when(pl.program_id(0) == 1)
    def _():
        up_out[...] = up[...]
        down_out[...] = (down[...].astype(F32) + from_above[...].astype(F32)).astype(BF16)


def relay(up, from_below, down, from_above, needs):
    rows, width = from_below.shape
    half = pl.BlockSpec((rows, width), lambda i, *_: (i, 0))
    return call(
        relay_kernel,
        (up, from_below, down, from_above),
        [half, full((rows, width)), half, full((rows, width))],
        [half, half],
        [shaped(2 * rows, width)] * 2,
        "relay",
        grid=(2,),
        needs=needs,
    )


def add_chips_kernel(*refs):
    ins, keep, give = refs[:-2], refs[-2], refs[-1]
    count = len(ins) // 2
    keep[...] = sum(item[...].astype(F32) for item in ins[:count])
    give[...] = sum(item[...].astype(F32) for item in ins[count:]).astype(BF16)


def add_chips(items, needs):
    rows, width = items[0].shape[0] // 2, items[0].shape[1]
    step = rows // 2 if rows % 32 == 0 and (rows // 2) % 16 == 0 else rows
    count = rows // step
    mine = pl.BlockSpec((step, width), lambda i, *_: (i, 0))
    other = pl.BlockSpec((step, width), lambda i, *_: (i + count, 0))
    return call(
        add_chips_kernel,
        (*items, *items),
        [mine] * len(items) + [other] * len(items),
        [mine, mine],
        [shaped(rows, width, dtype=F32), shaped(rows, width)],
        "add_chips",
        grid=(count,),
        needs=needs,
    )


def add_all_kernel(*refs):
    refs[-1][...] = sum(item[...].astype(F32) for item in refs[:-1]).astype(BF16)


def add_all(items, needs):
    rows, width = items[0].shape
    half = pl.BlockSpec((rows // 2, width), lambda i, *_: (i, 0))
    return call(
        add_all_kernel,
        tuple(items),
        [half] * len(items),
        [half],
        [shaped(rows, width)],
        "add_all",
        grid=(2,),
        needs=needs,
        limit=58,
    )


def over_z(blocks):
    return [lax.ppermute(blocks[k], "z", [(i, i ^ k) for i in range(4)]) for k in (1, 2, 3)]


def assemble_kernel(places, own, above, far_low, far_high, below, out):
    del places
    rows = far_low.shape[0]
    for k, blocks in enumerate(((own,), (above,), (far_low, far_high), (below,))):

        @pl.when(pl.program_id(0) == k)
        def _(blocks=blocks):
            if len(blocks) == 1:
                out[...] = blocks[0][...]
            else:
                out[:rows, :] = blocks[0][...]
                out[rows:, :] = blocks[1][...]


def assemble(places, blocks, needs):
    rows, width = blocks[0].shape
    return call(
        assemble_kernel,
        tuple(blocks),
        [full(item.shape) for item in blocks],
        [pl.BlockSpec((rows, width), lambda i, places: (places[i], 0))],
        [shaped(4 * rows, width)],
        "assemble",
        grid=(4,),
        needs=needs,
        me=places,
    )[0][0]


def over_cores(values):
    return lax.ppermute(values, "core", SWAP)


def latents_back_kernel(
    me, got, latents, query_gain, latent_gain, keep, low, high, many, own, gain_part, turns, sems
):
    rows = own.shape[0]
    here = pl.ds(pl.multiple_of(me[0] * rows, rows), rows)
    copies = [
        pltpu.make_async_copy(table.at[here, :], turns.at[n], sems.at[n])
        for n, table in enumerate((keep, low, high))
    ]
    for copy in copies:
        copy.start()
    total = add_up(got)
    for copy in copies:
        copy.wait()

    def back(lanes, gain):
        upstream, values = total[:, lanes], latents[:, lanes]
        factor = root(values)
        normed = values * factor
        gain_part[:, lanes] = jnp.sum(upstream * normed, axis=0, keepdims=True)
        return norm_back(upstream, normed, factor, row(gain)).astype(BF16)

    own[:, :QR] = back(slice(0, QR), query_gain)
    own[:, QR:LAT] = back(slice(QR, LAT), latent_gain)
    own[:, LAT:] = turn(total[:, LAT:], turns[0], turns[1], turns[2], back=True).astype(BF16)
    for k in range(8):
        many[k] = own[...]


def latents_back_of(me, got, latents, query_gain, latent_gain, tables, needs):
    rows = latents.shape[0]
    return call(
        latents_back_kernel,
        (got.reshape(8, rows, WIDE), latents, query_gain, latent_gain, *tables),
        [full((8, rows, WIDE)), full(latents.shape), full((QR,)), full((KVR,)), HBM, HBM, HBM],
        [full((8, rows, WIDE)), full((rows, WIDE)), full((1, LAT))],
        [shaped(8, rows, WIDE), shaped(rows, WIDE), shaped(1, LAT, dtype=F32)],
        "latents_back",
        scratch=[
            pltpu.VMEM((3, rows, 128), F32),
            pltpu.SemaphoreType.DMA((3,)),
        ],
        needs=needs,
        me=me,
        limit=24,
    )


def first_back_of(raw_back, query_down, latent_down, rope_down):
    rope_down[...] = jnp.zeros_like(rope_down)
    rope_down[64:96, :] = latent_down[KVR:, :]
    return (
        dot(raw_back[:, :QR], query_down[...], NT)
        + dot(raw_back[:, QR:LAT], latent_down[:KVR, :])
        + dot(raw_back[:, LAT:], rope_down[...])
    )


def first_gain_kernel(
    me, raw_back, tokens, query_down, latent_down, gain_part, rope_down, own, sem
):
    rows = own.shape[0]
    here = pl.ds(pl.multiple_of(me[0] * rows, rows), rows)
    copy = pltpu.make_async_copy(tokens.at[here, :], own, sem)
    copy.start()
    first_back = first_back_of(raw_back, query_down, latent_down, rope_down)
    copy.wait()
    values = own[...].astype(F32)
    gain_part[...] = jnp.sum(first_back * (values * root(values)), axis=0, keepdims=True)


def first_gain_of(me, own_raw_back, tokens, query_down, latent_down, needs):
    width = tokens.shape[1]
    return call(
        first_gain_kernel,
        (own_raw_back, tokens, query_down, latent_down.T),
        [full(own_raw_back.shape), HBM, full(query_down.shape), full(latent_down.shape[::-1])],
        [full((1, width))],
        [shaped(1, width, dtype=F32)],
        "first_gain",
        scratch=[
            pltpu.VMEM((128, width), BF16),
            pltpu.VMEM((own_raw_back.shape[0], width), BF16),
            pltpu.SemaphoreType.DMA,
        ],
        needs=needs,
        me=me,
    )


def tokens_back_kernel(
    raw_back, tokens, attention_back, query_down, latent_down, gain, tokens_grad, rope_down
):
    first_back = first_back_of(raw_back, query_down, latent_down, rope_down)
    values = tokens[...].astype(F32)
    factor = root(values)
    tokens_grad[...] = attention_back[...].astype(F32) + norm_back(
        first_back, values * factor, factor, row(gain)
    )


def tokens_back_of(raw_back, tokens, attention_back, query_down, latent_down, gain, needs):
    length, width = tokens.shape

    def rows(columns):
        return pl.BlockSpec((TILE, columns), lambda i, *_: (i, 0))

    return call(
        tokens_back_kernel,
        (raw_back, tokens, attention_back, query_down, latent_down.T, gain),
        [
            rows(WIDE),
            rows(width),
            rows(width),
            full(query_down.shape),
            full(latent_down.shape[::-1]),
            full((width,)),
        ],
        [rows(width)],
        [shaped(length, width, dtype=F32)],
        "tokens_back",
        grid=(length // TILE,),
        scratch=[pltpu.VMEM((128, width), BF16)],
        needs=needs,
    )


def finish_ffn_kernel(keep, got, gate, up, down):
    units = gate.shape[1]
    for n, out in enumerate((gate, up, down)):
        lanes = slice(units * n, units * n + units)
        out[...] = keep[:, lanes] + got[:, lanes].astype(F32)


def finish_ffn(keep, got, needs):
    rows, width = keep.shape
    out = (rows, width // 3)
    return call(
        finish_ffn_kernel,
        (keep, got),
        [full(keep.shape), full(got.shape)],
        [full(out)] * 3,
        [shaped(*out, dtype=F32)] * 3,
        "finish_ffn",
        needs=needs,
    )


def finish_attn_kernel(heads, keep, got, out_grad, query_grad, latent_grad):
    total = keep[...] + got[...].astype(F32)
    for h in range(heads):
        lanes = slice(128 * h, 128 * h + 128)
        out_grad[:, 64 * h : 64 * h + 64] = total[:160, 128 * h + 64 : 128 * h + 128]
        query_grad[:, 96 * h : 96 * h + 96] = total[160:208, 128 * h : 128 * h + 96]
    latent_grad[...] = total[208:224]


def finish_attn(keep, got, needs):
    heads = keep.shape[1] // 128
    outs = [(160, 64 * heads), (48, 96 * heads), (16, 128 * heads)]
    return call(
        functools.partial(finish_attn_kernel, heads),
        (keep, got),
        [full(keep.shape), full(got.shape)],
        [full(s) for s in outs],
        [shaped(*s, dtype=F32) for s in outs],
        "finish_attn",
        needs=needs,
    )


GAINS = ((0, 160), (160, 160), (320, 48), (368, 16))


def down_parts_kernel(own_in, raw_back, gains, out):
    total = dot(own_in[...], raw_back[...]).astype(BF16)
    for d in range(16):
        out[d, :20, :] = total[20 * d : 20 * d + 20]
        out[d, 20:, :] = jnp.zeros((4, WIDE), BF16)
        out[d, 20:21, :] = gains[d : d + 1, :]


def down_parts(own_in, raw_back, gains, needs):
    args = (own_in, raw_back, gains)
    return call(
        down_parts_kernel,
        args,
        [full(item.shape) for item in args],
        [full((16, 24, WIDE))],
        [shaped(16, 24, WIDE)],
        "down_parts",
        needs=needs,
        limit=24,
    )


def sum_copies_kernel(got, many):
    total = got[0].astype(F32)
    for d in range(1, 16):
        total = total + got[d].astype(F32)
    for k in range(8):
        many[k] = total.astype(BF16)


def sum_copies(got, needs):
    return call(
        sum_copies_kernel,
        (got,),
        [full(got.shape)],
        [full((8, 24, WIDE))],
        [shaped(8, 24, WIDE)],
        "sum_copies",
        needs=needs,
        limit=24,
    )


def finish_down_kernel(everyone, query_grad, latent_grad, *gains):
    for t in range(8):
        values = everyone[t].astype(F32)
        query_grad[20 * t : 20 * t + 20, :] = values[:20, :QR]
        latent_grad[20 * t : 20 * t + 20, :KVR] = values[:20, QR:LAT]
        latent_grad[20 * t : 20 * t + 20, KVR:] = values[:20, LAT + 64 : LAT + 96]
    total = sum(everyone[t, 16:24, :].astype(F32) for t in range(8))[4:5, :]
    for out, (first, count) in zip(gains, GAINS):
        out[...] = total[:, first : first + count]


def finish_down(everyone):
    everyone = everyone.reshape(8, 24, WIDE)
    outs = [(160, QR), (160, KVR + ROPE)] + [(1, count) for _, count in GAINS]
    return call(
        finish_down_kernel,
        (everyone,),
        [full(everyone.shape)],
        [full(s) for s in outs],
        [shaped(*s, dtype=F32) for s in outs],
        "finish_down",
        limit=24,
    )[0]


def exchange(blocks):
    return lax.all_to_all(blocks.reshape(-1, blocks.shape[-1]), TP, 0, 0, tiled=True)


def on_device(
    tokens,
    first_gain,
    query_down,
    query_gain,
    query_up,
    latent_down,
    latent_gain,
    latent_up,
    out_weight,
    second_gain,
    gate_weight,
    up_weight,
    down_weight,
    cotangent,
):
    length = tokens.shape[0]
    me = lax.axis_index(TP).astype(jnp.int32).reshape(1)
    y, xl, core = lax.axis_index("y"), lax.axis_index("xl"), lax.axis_index("core")
    starts = jnp.stack(
        [
            ((y + k) % 4 * 2 + (xl ^ j)) * 2 + c
            for c in (core, 1 - core)
            for k in range(4)
            for j in range(2)
        ]
    ).astype(jnp.int32)
    places = jnp.stack([lax.axis_index("z") ^ k for k in range(4)] + [me[0]]).astype(jnp.int32)
    z_order = jnp.stack([(lax.axis_index("z") + k) % 4 for k in range(4)]).astype(jnp.int32)
    tables = rope_tables(length)

    gate_turned, up_turned = gate_weight.T, up_weight.T

    (
        first_in,
        latents,
        query_code,
        latent_code,
        queries,
        keyvals,
        rope_keys,
        heads_out,
        log_total,
        attn_partial,
    ), started = attend(
        me,
        tokens,
        first_gain,
        query_down,
        latent_down,
        query_gain,
        latent_gain,
        query_up,
        latent_up,
        out_weight,
        tables,
    )
    attn_got = exchange(attn_partial)

    (cot_keep, cot_give), picked = halves(starts, [cotangent], [started])
    inner_back = dot(cotangent, down_weight, NT)
    cot_got = over_cores(cot_give)

    (residual, second_many), _ = residual_of(
        me, attn_got, tokens, second_gain, [picked, cot_got]
    )
    second_in = exchange(second_many)

    turned_in = first_in.T.reshape(16, 8, 20, length)
    own_in = lax.dynamic_slice_in_dim(turned_in, me[0], 1, 1).reshape(320, length)
    (code_keep, code_give, lat_keep, lat_give), picked = halves(
        starts, [query_code, latent_code], [residual]
    )
    code_got, lat_got = over_cores(code_give), over_cores(lat_give)
    heads_got = over_cores(heads_out)

    (gate_back, up_back, inner, back_partial), done = ffn(
        second_in, gate_turned, up_turned, inner_back, [picked, own_in, code_got, lat_got, heads_got]
    )
    back_got = exchange(back_partial)

    ours = (gate_back, up_back, inner)
    theirs = [over_cores(item) for item in ours]
    (in_keep, in_give), _ = halves(starts, [second_in], [done])
    in_got = over_cores(in_give)
    (far_up, far_down, ffn_up, ffn_down_way, ffn_own), done = ffn_grads(in_keep, in_got, cot_keep, cot_got, ours, theirs, gate_weight.shape[1], [])
    below, above = lax.ppermute(far_up, "y", UP), lax.ppermute(far_down, "y", DOWN)

    (back_many, second_gain_part), done = residual_back_of(
        me, back_got, residual, cotangent, second_gain, [done]
    )
    attention_back = exchange(back_many)
    mixed_blocks, done = ffn_down(places, inner, down_weight, residual, [done])
    mixed_got = over_z(mixed_blocks)
    (ffn_up, ffn_down_way), done = relay(ffn_up, below, ffn_down_way, above, [done])
    below, above = lax.ppermute(ffn_up, "y", UP), lax.ppermute(ffn_down_way, "y", DOWN)

    (both_back, latents_partial), back_done = attend_back(
        attention_back,
        out_weight,
        queries,
        keyvals,
        rope_keys,
        log_total,
        query_up,
        latent_up,
        tables,
        [done],
    )
    latents_got = exchange(latents_partial)

    (out_keep, out_give), picked = halves(starts, [attention_back], [back_done])
    (mixed_part,), done = add_all([mixed_blocks[0], *mixed_got], [back_done, below, above, picked])
    mixed_other = lax.ppermute(mixed_part, "xh", SWAP)

    (raw_many, own_raw, latent_gain_parts), done = latents_back_of(
        me, latents_got, latents, query_gain, latent_gain, tables, [done]
    )
    raw_back = exchange(raw_many)

    out_got, both_got = over_cores(out_give), over_cores(both_back)
    (attn_across, attn_up, attn_down, attn_own), done = attn_grads(
        (out_keep, code_keep, lat_keep),
        (out_got, code_got, lat_got),
        (heads_out, both_back),
        (heads_got, both_got),
        [done],
    )
    (ffn_keep, ffn_give), added = add_chips([ffn_own, below, above], [done])
    ffn_got = lax.ppermute(ffn_give, "xl", SWAP)
    attn_got = [
        lax.ppermute(attn_across, "y", ACROSS),
        lax.ppermute(attn_up, "y", UP),
        lax.ppermute(attn_down, "y", DOWN),
    ]
    (first_gain_part,), gain_done = first_gain_of(
        me, own_raw, tokens, query_down, latent_down, [done]
    )
    (mixed_part,), _ = add_all([mixed_part, mixed_other], [added])
    from_above = lax.ppermute(mixed_part, "z", DOWN)
    from_below = lax.ppermute(mixed_part, "z", UP)
    count = mixed_part.shape[0] // 2
    far_low = lax.ppermute(from_below[:count], "z", UP)
    far_high = lax.ppermute(from_above[count:], "z", DOWN)


    gains = jnp.concatenate(
        [
            first_gain_part.reshape(16, -1),
            second_gain_part.reshape(16, -1),
            latent_gain_parts[0, :QR].reshape(16, -1),
            latent_gain_parts[0, QR:].reshape(16, -1),
        ],
        axis=1,
    ).astype(BF16)
    gains = jnp.pad(gains, ((0, 0), (0, WIDE - gains.shape[1])))
    (parts,), done = down_parts(own_in, raw_back, gains, [])
    parts_got = lax.all_to_all(parts, DP, 0, 0, tiled=True)

    (tokens_grad,), done = tokens_back_of(
        raw_back, tokens, attention_back, query_down, latent_down, first_gain, [done]
    )
    (many,), summed = sum_copies(parts_got, [done])
    everyone = exchange(many)

    (attn_keep, attn_give), done = add_chips([attn_own, *attn_got], [summed])
    attn_other = lax.ppermute(attn_give, "xl", SWAP)
    (gate_weight_grad, up_weight_grad, down_weight_grad), done = finish_ffn(
        ffn_keep, ffn_got, [done]
    )
    (out_weight_grad, query_up_grad, latent_up_grad), done = finish_attn(
        attn_keep, attn_other, [done]
    )
    (
        query_down_grad,
        latent_down_grad,
        first_gain_grad,
        second_gain_grad,
        query_gain_grad,
        latent_gain_grad,
    ) = finish_down(everyone)

    mixed = assemble(
        z_order, [mixed_part, from_above, far_low, far_high, from_below], [done]
    )

    return (
        mixed,
        tokens_grad,
        first_gain_grad[0],
        query_down_grad,
        query_gain_grad[0],
        query_up_grad,
        latent_down_grad,
        latent_gain_grad[0],
        latent_up_grad,
        out_weight_grad.T,
        second_gain_grad[0],
        gate_weight_grad,
        up_weight_grad,
        down_weight_grad.T,
    )


def solution(mesh):
    grid = Mesh(mesh.devices.reshape(4, 2, 2, 2, 4), ("y", "xl", "core", "xh", "z"))
    in_specs = (
        P(DP, None),
        P(),
        P(),
        P(),
        P(None, TP),
        P(),
        P(),
        P(None, TP),
        P(TP, None),
        P(),
        P(None, TP),
        P(None, TP),
        P(TP, None),
        P(DP, None),
    )
    out_specs = (
        P(DP, None),
        P(DP, None),
        P(DP),
        P(DP, None),
        P(DP),
        P(DP, TP),
        P(DP, None),
        P(DP),
        P(DP, TP),
        P(TP, DP),
        P(DP),
        P(DP, TP),
        P(DP, TP),
        P(TP, DP),
    )
    return jax.shard_map(
        on_device, mesh=grid, in_specs=in_specs, out_specs=out_specs, check_vma=False
    )
```

```python
import functools

import jax
import jax.numpy as jnp
import numpy as np
from jax import lax
from jax.experimental import pallas as pl
from jax.experimental.pallas import tpu as pltpu
from jax.sharding import Mesh, PartitionSpec as P

NOPE = 64
ROPE = 32
DV = 64
KVR = 256
QR = 768
LAT = QR + KVR
WIDE = LAT + 128

EPS = 1e-05
BASE = 10000.0
SCALE = (NOPE + ROPE) ** (-0.5)

DP = ("y", "xl", "core")
TP = ("xh", "z")
SWAP = [(0, 1), (1, 0)]
F32 = jnp.float32
BF16 = jnp.bfloat16
NT = (((1,), (1,)), ((), ()))
TN = (((0,), (0,)), ((), ()))
NN = (((1,), (0,)), ((), ()))
TILE = 256


def dot(left, right, dims=NN):
    return lax.dot_general(left, right, dims, preferred_element_type=F32)


def params(limit=56):
    return pltpu.CompilerParams(vmem_limit_bytes=limit * 2**20)


HBM = pl.BlockSpec(memory_space=pltpu.HBM)


def call(kernel, args, in_specs, out_specs, out_shape, name, grid=(1,), scratch=(), needs=(), me=None, limit=60):
    first = 0 if me is None else 1
    n_in, n_out = len(args), len(out_shape)

    def body(*refs):
        ins = refs[: first + n_in]
        rest = refs[first + n_in + len(needs) :]
        mark = rest[n_out]

        @pl.when(pl.program_id(0) == 0)
        def _():
            mark[...] = jnp.zeros_like(mark)

        kernel(*ins, *rest[:n_out], *rest[n_out + 1 :])

    *outs, mark = pl.pallas_call(
        body,
        grid_spec=pltpu.PrefetchScalarGridSpec(
            num_scalar_prefetch=first,
            grid=grid,
            in_specs=list(in_specs) + [HBM] * len(needs),
            out_specs=list(out_specs) + [full((8, 128))],
            scratch_shapes=list(scratch),
        ),
        out_shape=list(out_shape) + [jax.ShapeDtypeStruct((8, 128), F32)],
        compiler_params=params(limit),
        cost_estimate=pl.CostEstimate(flops=1, bytes_accessed=1, transcendentals=0),
        name=name,
    )(*(() if me is None else (me,)), *args, *needs)
    return outs, mark


def shaped(*shape, dtype=BF16):
    return jax.ShapeDtypeStruct(shape, dtype)


def full(shape):
    return pl.BlockSpec(shape, lambda *_: (0,) * len(shape))


def rope_tables(length):
    half = ROPE // 2
    rates = np.exp(np.arange(half, dtype=np.float32) * np.float32(-2.0 * np.log(BASE) / ROPE))
    angles = np.arange(length, dtype=np.float32)[:, None] * rates.astype(np.float32)[None, :]
    cosine, sine = np.cos(angles), np.sin(angles)
    keep = np.zeros((length, 128), np.float32)
    keep[:, :NOPE] = 1.0
    keep[:, 64:80] = cosine
    keep[:, 80:96] = cosine
    low = np.zeros((length, 128), np.float32)
    low[:, 64:80] = -sine
    high = np.zeros((length, 128), np.float32)
    high[:, 80:96] = sine
    return jnp.asarray(keep), jnp.asarray(low), jnp.asarray(high)


def turn(values, keep, low, high, back=False):
    moved = pltpu.roll(values, 112, 1) * low + pltpu.roll(values, 16, 1) * high
    return values * keep - moved if back else values * keep + moved


def root(values):
    return lax.rsqrt(jnp.mean(values * values, axis=-1, keepdims=True) + EPS)


def norm_back(upstream, normed, factor, gain):
    scaled = upstream * gain
    return factor * (scaled - normed * jnp.mean(scaled * normed, axis=-1, keepdims=True))


def spread_out_weight(weight_ref, spread_ref, heads):
    spread_ref[...] = jnp.zeros_like(spread_ref)
    for h in range(heads):
        spread_ref[128 * h + 64 : 128 * h + 128, :] = weight_ref[64 * h : 64 * h + 64, :]


def spread_query_up(weight_ref, spread_ref, heads):
    spread_ref[...] = jnp.zeros_like(spread_ref)
    for h in range(heads):
        spread_ref[128 * h : 128 * h + 96, :] = weight_ref[96 * h : 96 * h + 96, :]


def row(ref):
    return ref[...].reshape(1, -1)


def low_lanes(shape):
    return lax.broadcasted_iota(jnp.int32, shape, 1) < NOPE


def causal(keys, queries, first_query):
    key_ids = lax.broadcasted_iota(jnp.int32, (keys, queries), 0)
    query_ids = lax.broadcasted_iota(jnp.int32, (keys, queries), 1) + first_query
    return key_ids <= query_ids


def attend_kernel(
    heads,
    me,
    tokens,
    first_gain,
    query_down,
    latent_down,
    query_gain,
    latent_gain,
    query_up,
    latent_up,
    out_weight,
    keep,
    low,
    high,
    first_in,
    latents,
    query_code,
    latent_code,
    queries,
    keyvals,
    rope_keys,
    heads_out,
    log_total,
    partial,
    raw_latents,
    spread,
    spread_up,
    rope_down,
    kv_all,
    rope_all,
):
    step = pl.program_id(0)

    @pl.when(step == 0)
    def _():
        spread_out_weight(out_weight, spread, heads)
        spread_query_up(query_up, spread_up, heads)
        rope_down[...] = jnp.zeros_like(rope_down)
        rope_down[64:96, :] = latent_down[KVR:, :]

    def rows_of(index, carry):
        rows = pl.ds(pl.multiple_of(index * 32, 32), 32)
        values = tokens[rows, :].astype(F32)
        first_in[rows, :] = (values * root(values) * row(first_gain)).astype(BF16)
        return carry

    lax.fori_loop(0, TILE // 32, rows_of, 0)
    taken = first_in[...]
    query_latent = dot(taken, query_down[...])
    raw_latents[:, :QR] = query_latent
    code = (query_latent * root(query_latent) * row(query_gain)).astype(BF16)
    query_code[...] = code
    latent = dot(taken, latent_down[:KVR, :], NT)
    raw_latents[:, QR:] = latent
    count = latents.shape[0]
    own = me[0] * count

    @pl.when(own // TILE == step)
    def _():
        latents[...] = raw_latents[pl.ds(pl.multiple_of(own % TILE, count), count), :]

    lcode = (latent * root(latent) * row(latent_gain)).astype(BF16)
    latent_code[...] = lcode
    tables = keep[...], low[...], high[...]
    rope = turn(dot(taken, rope_down[...], NT), *tables).astype(BF16)
    rope_keys[...] = rope
    here = pl.ds(pl.multiple_of(step * TILE, TILE), TILE)
    rope_all[here, :] = rope
    kv = dot(lcode, latent_up[...]).astype(BF16)
    keyvals[...] = kv
    kv_all[here, :] = kv
    raw = dot(code, spread_up[...], NT)
    for h in range(heads):
        lanes = slice(128 * h, 128 * h + 128)
        queries[:, lanes] = turn(raw[:, lanes], *tables).astype(BF16)

    def tile(index):
        keys = TILE * (index + 1)
        for h in range(heads):
            lanes = slice(128 * h, 128 * h + 128)
            kv_h = kv_all[:keys, lanes]
            key = jnp.where(low_lanes((keys, 128)), kv_h, rope_all[:keys, :])
            scores = dot(key, queries[:, lanes], NT) * SCALE
            scores = jnp.where(causal(keys, TILE, TILE * index), scores, -1e30)
            top = jnp.max(scores, axis=0, keepdims=True)
            weights = jnp.exp(scores - top)
            total = jnp.sum(weights, axis=0, keepdims=True)
            log_total[h : h + 1, :] = top + jnp.log(total)
            probs = (weights * (1.0 / total)).astype(BF16)
            heads_out[:, lanes] = dot(probs, kv_h, TN).astype(BF16)

    for index in range(2):
        pl.when(step == index)(functools.partial(tile, index))
    partial[...] = dot(heads_out[...], spread[...]).astype(BF16)


def attend(me, tokens, first_gain, query_down, latent_down, query_gain, latent_gain, query_up, latent_up, out_weight, tables):
    latent_down, query_up = latent_down.T, query_up.T
    length, width = tokens.shape
    heads = out_weight.shape[0] // DV
    wide = 128 * heads

    def rows(columns):
        return pl.BlockSpec((TILE, columns), lambda i, *_: (i, 0))

    return call(
        functools.partial(attend_kernel, heads),
        (tokens, first_gain, query_down, latent_down, query_gain, latent_gain, query_up, latent_up, out_weight, *tables),
        [
            rows(width),
            full((width,)),
            full(query_down.shape),
            full(latent_down.shape),
            full((QR,)),
            full((KVR,)),
            full(query_up.shape),
            full(latent_up.shape),
            full(out_weight.shape),
            rows(128),
            rows(128),
            rows(128),
        ],
        [
            rows(width),
            full((length // 8, LAT)),
            rows(QR),
            rows(KVR),
            rows(wide),
            rows(wide),
            rows(128),
            rows(wide),
            pl.BlockSpec((8, TILE), lambda i, *_: (0, i)),
            rows(width),
        ],
        [
            shaped(length, width),
            shaped(length // 8, LAT, dtype=F32),
            shaped(length, QR),
            shaped(length, KVR),
            shaped(length, wide),
            shaped(length, wide),
            shaped(length, 128),
            shaped(length, wide),
            shaped(8, length, dtype=F32),
            shaped(length, width),
        ],
        "attend",
        grid=(length // TILE,),
        me=me,
        scratch=[
            pltpu.VMEM((TILE, LAT), F32),
            pltpu.VMEM((wide, width), BF16),
            pltpu.VMEM((wide, QR), BF16),
            pltpu.VMEM((128, width), BF16),
            pltpu.VMEM((length, wide), BF16),
            pltpu.VMEM((length, 128), BF16),
        ],
    )


def attend_back_kernel(
    heads,
    attention_back,
    out_weight,
    queries,
    keyvals,
    rope_keys,
    log_total,
    query_up,
    latent_up,
    keep,
    low,
    high,
    both_back,
    partial,
    spread,
    spread_up,
    kv_grad,
    rope_grad,
    code_grad,
):
    step = pl.program_id(0)

    @pl.when(step == 0)
    def _():
        spread_out_weight(out_weight, spread, heads)
        spread_query_up(query_up, spread_up, heads)
        kv_grad[...] = jnp.zeros_like(kv_grad)
        rope_grad[...] = jnp.zeros_like(rope_grad)

    heads_back = dot(attention_back[...], spread[...], NT).astype(BF16)
    tables = keep[...], low[...], high[...]

    def tile(index):
        keys = TILE * (index + 1)
        low_part = low_lanes((keys, 128))
        for h in range(heads):
            lanes = slice(128 * h, 128 * h + 128)
            kv_h = keyvals[:keys, lanes]
            key = jnp.where(low_part, kv_h, rope_keys[:keys, :])
            query = queries[:, lanes]
            back = heads_back[:, lanes]
            scores = dot(key, query, NT) * SCALE
            probs = jnp.exp(scores - log_total[h : h + 1, :])
            probs = jnp.where(causal(keys, TILE, TILE * index), probs, 0.0)
            prob_back = dot(kv_h, back, NT)
            mean = jnp.sum(probs * prob_back, axis=0, keepdims=True)
            score_back = (probs * (prob_back - mean)).astype(BF16)
            of_values = dot(probs.astype(BF16), back)
            of_keys = dot(score_back, query) * SCALE
            kv_grad[:keys, lanes] += of_values + jnp.where(low_part, of_keys, 0.0)
            rope_grad[:keys, :] += jnp.where(low_part, 0.0, of_keys)
            of_query = dot(score_back, key, TN) * SCALE
            both_back[here, lanes] = turn(of_query, *tables, back=True).astype(BF16)

    wide = 128 * heads
    here = pl.ds(pl.multiple_of(step * TILE, TILE), TILE)
    for index in range(2):
        pl.when(step == index)(functools.partial(tile, index))
    code_grad[here, :] = dot(both_back[here, :wide], spread_up[...]).astype(BF16)

    @pl.when(step == 1)
    def _():
        kv = kv_grad[...].astype(BF16)
        both_back[:, wide:] = kv
        partial[:, :QR] = code_grad[...]
        partial[:, QR:LAT] = dot(kv, latent_up[...], NT).astype(BF16)
        partial[:, LAT:] = rope_grad[...].astype(BF16)


def attend_back(attention_back, out_weight, queries, keyvals, rope_keys, log_total, query_up, latent_up, tables, needs):
    query_up = query_up.T
    length, width = attention_back.shape
    heads = out_weight.shape[0] // DV
    wide = 128 * heads

    def rows(columns):
        return pl.BlockSpec((TILE, columns), lambda i, *_: (i, 0))

    return call(
        functools.partial(attend_back_kernel, heads),
        (attention_back, out_weight, queries, keyvals, rope_keys, log_total, query_up, latent_up, *tables),
        [
            rows(width),
            full(out_weight.shape),
            rows(wide),
            full((length, wide)),
            full((length, 128)),
            pl.BlockSpec((8, TILE), lambda i, *_: (0, i)),
            full(query_up.shape),
            full(latent_up.shape),
            rows(128),
            rows(128),
            rows(128),
        ],
        [full((length, 2 * wide)), full((length, WIDE))],
        [shaped(length, 2 * wide), shaped(length, WIDE)],
        "attend_back",
        grid=(length // TILE,),
        scratch=[
            pltpu.VMEM((wide, width), BF16),
            pltpu.VMEM((wide, QR), BF16),
            pltpu.VMEM((length, wide), F32),
            pltpu.VMEM((length, 128), F32),
            pltpu.VMEM((length, QR), BF16),
        ],
        needs=needs,
    )


def add_up(got):
    total = got[0].astype(F32)
    for k in range(1, 8):
        total = total + got[k].astype(F32)
    return total


STEPS = 2


def residual_kernel(me, got, tokens, gain, residual, many):
    del me
    total = tokens[...].astype(F32) + add_up(got)
    residual[...] = total
    second_in = (total * root(total) * row(gain)).astype(BF16)
    for k in range(8):
        many[k] = second_in


def own_specs(rows, width):
    step = rows // STEPS
    return (
        pl.BlockSpec((8, step, width), lambda i, me: (0, i, 0)),
        pl.BlockSpec((step, width), lambda i, me: (i, 0)),
        pl.BlockSpec((step, width), lambda i, me: (me[0] * STEPS + i, 0)),
    )


def residual_of(me, got, tokens, gain, needs):
    width = tokens.shape[1]
    rows = tokens.shape[0] // 8
    eight, one, own = own_specs(rows, width)
    return call(
        residual_kernel,
        (got.reshape(8, rows, width), tokens, gain),
        [eight, own, full((width,))],
        [one, eight],
        [shaped(rows, width, dtype=F32), shaped(8, rows, width)],
        "residual",
        grid=(STEPS,),
        needs=needs,
        me=me,
        limit=58,
    )


def residual_back_kernel(me, got, residual, cotangent, gain, many, gain_part):
    del me
    second_back = add_up(got)
    values = residual[...]
    factor = root(values)
    normed = values * factor
    part = jnp.sum(second_back * normed, axis=0, keepdims=True)

    @pl.when(pl.program_id(0) == 0)
    def _():
        gain_part[...] = part

    @pl.when(pl.program_id(0) > 0)
    def _():
        gain_part[...] += part

    back = cotangent[...].astype(F32) + norm_back(second_back, normed, factor, row(gain))
    back = back.astype(BF16)
    for k in range(8):
        many[k] = back


def residual_back_of(me, got, residual, cotangent, gain, needs):
    rows, width = residual.shape
    eight, one, own = own_specs(rows, width)
    return call(
        residual_back_kernel,
        (got.reshape(8, rows, width), residual, cotangent, gain),
        [eight, one, own, full((width,))],
        [eight, full((1, width))],
        [shaped(8, rows, width), shaped(1, width, dtype=F32)],
        "residual_back",
        grid=(STEPS,),
        needs=needs,
        me=me,
        limit=58,
    )


def ffn_kernel(
    second_in, gate_weight, up_weight, inner_back, gate_back, up_back, inner, partial
):
    taken = second_in[...]
    gate = dot(taken, gate_weight[...], NT)
    up = dot(taken, up_weight[...], NT)
    sigma = 1.0 / (1.0 + jnp.exp(-gate))
    act = gate * sigma
    units = gate.shape[1]
    back = inner_back[...]
    of_gate = (back * up * sigma * (1.0 + gate * (1.0 - sigma))).astype(BF16)
    of_up = (back * act).astype(BF16)
    for out, values in ((gate_back, of_gate), (up_back, of_up), (inner, (act * up).astype(BF16))):
        out[:, :units] = values
        out[:, units:] = jnp.zeros((values.shape[0], out.shape[1] - units), BF16)
    partial[...] = (dot(of_gate, gate_weight[...]) + dot(of_up, up_weight[...])).astype(BF16)


def ffn(second_in, gate_weight, up_weight, inner_back, needs):
    length, width = second_in.shape
    units = gate_weight.shape[0]
    wide = -(-units // 128) * 128

    def rows(columns):
        return pl.BlockSpec((TILE, columns), lambda i, *_: (i, 0))

    return call(
        ffn_kernel,
        (second_in, gate_weight, up_weight, inner_back),
        [rows(width), full((units, width)), full((units, width)), rows(units)],
        [rows(wide), rows(wide), rows(wide), rows(width)],
        [shaped(length, wide)] * 3 + [shaped(length, width)],
        "ffn",
        grid=(length // TILE,),
        needs=needs,
    )


def ffn_down_kernel(places, inner, down_weight, residual, *refs):
    outs, total = refs[:4], refs[4]
    for i in range(2):
        rows = slice(i * TILE, i * TILE + TILE)
        total[rows, :] = dot(inner[rows, : down_weight.shape[0]], down_weight[...]).astype(BF16)
    count = residual.shape[0]
    own = pl.ds(pl.multiple_of(places[4] * count, count), count)
    total[own, :] = (total[own, :].astype(F32) + residual[...]).astype(BF16)
    for k, out in enumerate(outs):
        rows = out.shape[0]
        out[...] = total[pl.ds(pl.multiple_of(places[k] * rows, rows), rows), :]


def ffn_down(places, inner, down_weight, residual, needs):
    length, width = inner.shape[0], down_weight.shape[1]
    block = (length // 4, width)
    return call(
        ffn_down_kernel,
        (inner, down_weight, residual),
        [full(inner.shape), full(down_weight.shape), full(residual.shape)],
        [full(block)] * 4,
        [shaped(*block)] * 4,
        "ffn_down",
        scratch=[pltpu.VMEM((length, width), BF16)],
        needs=needs,
        me=places,
    )


def halves_kernel(blocks, width, starts, *refs):
    sources, outs, turned = refs[:blocks], refs[blocks : 3 * blocks], refs[3 * blocks]
    for n in range(blocks):
        source, keep, give = sources[n], outs[2 * n], outs[2 * n + 1]
        columns, each = source.shape[1], width[n]
        for c in range(0, columns, 256):
            turned[c : c + 256, :] = source[:, c : c + 256].T
        for which, out in enumerate((keep, give)):
            for k in range(8):
                first = pl.multiple_of(starts[8 * which + k] * each, 16)
                out[each * k : each * k + each, :] = turned[pl.ds(first, each), :]


def halves(starts, values, needs):
    length = values[0].shape[0]
    widths = [item.shape[1] // 16 for item in values]
    shapes = [(8 * w, length) for w in widths for _ in range(2)]
    return call(
        functools.partial(halves_kernel, len(values), widths),
        tuple(values),
        [full(item.shape) for item in values],
        [full(s) for s in shapes],
        [shaped(*s) for s in shapes],
        "halves",
        scratch=[pltpu.VMEM((max(item.shape[1] for item in values), length), BF16)],
        needs=needs,
        me=starts,
    )


ORDER = (2, 1, 3, 0)


def ffn_grads_kernel(in_keep, in_got, cot_keep, cot_got, *refs):
    ours, theirs, outs = refs[:3], refs[3:6], refs[6:]
    units = outs[0].shape[1] // 3

    def block(*parts):
        for n, (keep, got) in enumerate(((in_keep, in_got), (in_keep, in_got), (cot_keep, cot_got))):
            total = dot(keep[...], ours[n][...]) + dot(got[...], theirs[n][...])
            total = total[:, :units].astype(BF16)
            first = 0
            for out in parts:
                count = out.shape[0]
                out[:, units * n : units * n + units] = total[first : first + count]
                first += count

    for s, parts in enumerate((outs[:2], outs[2:3], outs[3:4], outs[4:])):
        pl.when(pl.program_id(0) == s)(functools.partial(block, *parts))


def ffn_grads(in_keep, in_got, cot_keep, cot_got, ours, theirs, units, needs):
    length, wide = ours[0].shape
    rows = in_keep.shape[0] // 4

    def index(i):
        return (jnp.where(i == 0, 2, jnp.where(i == 1, 1, jnp.where(i == 2, 3, 0))), 0)

    left = pl.BlockSpec((rows, length), index)
    out = (rows, 3 * units)
    outs = [(rows // 2, 3 * units)] * 2 + [out] * 3
    return call(
        ffn_grads_kernel,
        (in_keep, in_got, cot_keep, cot_got, *ours, *theirs),
        [left] * 4 + [full((length, wide))] * 6,
        [full(s) for s in outs],
        [shaped(*s) for s in outs],
        "ffn_grads",
        grid=(4,),
        needs=needs,
    )


def attn_grads_kernel(widths, *refs):
    keeps, gots, outs = refs[:3], refs[3:6], refs[10:]
    wide = outs[0].shape[1]
    ours, theirs = (
        (heads, both.at[:, :wide], both.at[:, wide:]) for heads, both in (refs[6:8], refs[8:10])
    )
    rows = sum(widths)
    for out, k in zip(outs, ORDER):
        first = 0
        for n, each in enumerate(widths):
            part = slice(2 * each * k, 2 * each * k + 2 * each)
            total = dot(keeps[n][part, :], ours[n][...]) + dot(gots[n][part, :], theirs[n][...])
            total = total.astype(BF16)
            out[first : first + each, :] = total[:each]
            out[rows + first : rows + first + each, :] = total[each:]
            first += each


def attn_grads(keeps, gots, ours, theirs, needs):
    widths = [item.shape[0] // 8 for item in keeps]
    rows, wide = sum(widths), ours[0].shape[1]
    args = (*keeps, *gots, *ours, *theirs)
    outs = [(2 * rows, wide)] * 4
    return call(
        functools.partial(attn_grads_kernel, widths),
        args,
        [full(item.shape) for item in args],
        [full(s) for s in outs],
        [shaped(*s) for s in outs],
        "attn_grads",
        needs=needs,
    )


UP = [(i, (i + 1) % 4) for i in range(4)]
DOWN = [(i, (i + 3) % 4) for i in range(4)]
ACROSS = [(i, (i + 2) % 4) for i in range(4)]


def relay_kernel(up, from_below, down, from_above, up_out, down_out):
    @pl.when(pl.program_id(0) == 0)
    def _():
        up_out[...] = (up[...].astype(F32) + from_below[...].astype(F32)).astype(BF16)
        down_out[...] = down[...]

    @pl.when(pl.program_id(0) == 1)
    def _():
        up_out[...] = up[...]
        down_out[...] = (down[...].astype(F32) + from_above[...].astype(F32)).astype(BF16)


def relay(up, from_below, down, from_above, needs):
    rows, width = from_below.shape
    half = pl.BlockSpec((rows, width), lambda i, *_: (i, 0))
    return call(
        relay_kernel,
        (up, from_below, down, from_above),
        [half, full((rows, width)), half, full((rows, width))],
        [half, half],
        [shaped(2 * rows, width)] * 2,
        "relay",
        grid=(2,),
        needs=needs,
    )


def add_chips_kernel(*refs):
    ins, keep, give = refs[:-2], refs[-2], refs[-1]
    count = len(ins) // 2
    keep[...] = sum(item[...].astype(F32) for item in ins[:count])
    give[...] = sum(item[...].astype(F32) for item in ins[count:]).astype(BF16)


def add_chips(items, needs):
    rows, width = items[0].shape[0] // 2, items[0].shape[1]
    step = rows // 2 if rows % 32 == 0 and (rows // 2) % 16 == 0 else rows
    count = rows // step
    mine = pl.BlockSpec((step, width), lambda i, *_: (i, 0))
    other = pl.BlockSpec((step, width), lambda i, *_: (i + count, 0))
    return call(
        add_chips_kernel,
        (*items, *items),
        [mine] * len(items) + [other] * len(items),
        [mine, mine],
        [shaped(rows, width, dtype=F32), shaped(rows, width)],
        "add_chips",
        grid=(count,),
        needs=needs,
    )


def add_all_kernel(*refs):
    refs[-1][...] = sum(item[...].astype(F32) for item in refs[:-1]).astype(BF16)


def add_all(items, needs):
    rows, width = items[0].shape
    half = pl.BlockSpec((rows // 2, width), lambda i, *_: (i, 0))
    return call(
        add_all_kernel,
        tuple(items),
        [half] * len(items),
        [half],
        [shaped(rows, width)],
        "add_all",
        grid=(2,),
        needs=needs,
        limit=58,
    )


def over_z(blocks):
    return [lax.ppermute(blocks[k], "z", [(i, i ^ k) for i in range(4)]) for k in (1, 2, 3)]


def assemble_kernel(places, *refs):
    del places
    for k in range(4):

        @pl.when(pl.program_id(0) == k)
        def _(k=k):
            refs[4][...] = refs[k][...]


def assemble(places, blocks, needs):
    rows, width = blocks[0].shape
    return call(
        assemble_kernel,
        tuple(blocks),
        [full(item.shape) for item in blocks],
        [pl.BlockSpec((rows, width), lambda i, places: (places[i], 0))],
        [shaped(4 * rows, width)],
        "assemble",
        grid=(4,),
        needs=needs,
        me=places,
    )[0][0]


def over_cores(values):
    return lax.ppermute(values, "core", SWAP)


def latents_back_kernel(
    me, got, latents, query_gain, latent_gain, keep, low, high, many, own, gain_part, turns, sems
):
    rows = own.shape[0]
    here = pl.ds(pl.multiple_of(me[0] * rows, rows), rows)
    copies = [
        pltpu.make_async_copy(table.at[here, :], turns.at[n], sems.at[n])
        for n, table in enumerate((keep, low, high))
    ]
    for copy in copies:
        copy.start()
    total = add_up(got)
    for copy in copies:
        copy.wait()

    def back(lanes, gain):
        upstream, values = total[:, lanes], latents[:, lanes]
        factor = root(values)
        normed = values * factor
        gain_part[:, lanes] = jnp.sum(upstream * normed, axis=0, keepdims=True)
        return norm_back(upstream, normed, factor, row(gain)).astype(BF16)

    own[:, :QR] = back(slice(0, QR), query_gain)
    own[:, QR:LAT] = back(slice(QR, LAT), latent_gain)
    own[:, LAT:] = turn(total[:, LAT:], turns[0], turns[1], turns[2], back=True).astype(BF16)
    for k in range(8):
        many[k] = own[...]


def latents_back_of(me, got, latents, query_gain, latent_gain, tables, needs):
    rows = latents.shape[0]
    return call(
        latents_back_kernel,
        (got.reshape(8, rows, WIDE), latents, query_gain, latent_gain, *tables),
        [full((8, rows, WIDE)), full(latents.shape), full((QR,)), full((KVR,)), HBM, HBM, HBM],
        [full((8, rows, WIDE)), full((rows, WIDE)), full((1, LAT))],
        [shaped(8, rows, WIDE), shaped(rows, WIDE), shaped(1, LAT, dtype=F32)],
        "latents_back",
        scratch=[
            pltpu.VMEM((3, rows, 128), F32),
            pltpu.SemaphoreType.DMA((3,)),
        ],
        needs=needs,
        me=me,
        limit=24,
    )


def first_back_of(raw_back, query_down, latent_down, rope_down):
    rope_down[...] = jnp.zeros_like(rope_down)
    rope_down[64:96, :] = latent_down[KVR:, :]
    return (
        dot(raw_back[:, :QR], query_down[...], NT)
        + dot(raw_back[:, QR:LAT], latent_down[:KVR, :])
        + dot(raw_back[:, LAT:], rope_down[...])
    )


def first_gain_kernel(
    me, raw_back, tokens, query_down, latent_down, gain_part, rope_down, own, sem
):
    rows = own.shape[0]
    here = pl.ds(pl.multiple_of(me[0] * rows, rows), rows)
    copy = pltpu.make_async_copy(tokens.at[here, :], own, sem)
    copy.start()
    first_back = first_back_of(raw_back, query_down, latent_down, rope_down)
    copy.wait()
    values = own[...].astype(F32)
    gain_part[...] = jnp.sum(first_back * (values * root(values)), axis=0, keepdims=True)


def first_gain_of(me, own_raw_back, tokens, query_down, latent_down, needs):
    width = tokens.shape[1]
    return call(
        first_gain_kernel,
        (own_raw_back, tokens, query_down, latent_down.T),
        [full(own_raw_back.shape), HBM, full(query_down.shape), full(latent_down.shape[::-1])],
        [full((1, width))],
        [shaped(1, width, dtype=F32)],
        "first_gain",
        scratch=[
            pltpu.VMEM((128, width), BF16),
            pltpu.VMEM((own_raw_back.shape[0], width), BF16),
            pltpu.SemaphoreType.DMA,
        ],
        needs=needs,
        me=me,
    )


def tokens_back_kernel(
    raw_back, tokens, attention_back, query_down, latent_down, gain, tokens_grad, rope_down
):
    first_back = first_back_of(raw_back, query_down, latent_down, rope_down)
    values = tokens[...].astype(F32)
    factor = root(values)
    tokens_grad[...] = attention_back[...].astype(F32) + norm_back(
        first_back, values * factor, factor, row(gain)
    )


def tokens_back_of(raw_back, tokens, attention_back, query_down, latent_down, gain, needs):
    length, width = tokens.shape

    def rows(columns):
        return pl.BlockSpec((TILE, columns), lambda i, *_: (i, 0))

    return call(
        tokens_back_kernel,
        (raw_back, tokens, attention_back, query_down, latent_down.T, gain),
        [
            rows(WIDE),
            rows(width),
            rows(width),
            full(query_down.shape),
            full(latent_down.shape[::-1]),
            full((width,)),
        ],
        [rows(width)],
        [shaped(length, width, dtype=F32)],
        "tokens_back",
        grid=(length // TILE,),
        scratch=[pltpu.VMEM((128, width), BF16)],
        needs=needs,
    )


def finish_ffn_kernel(keep, got, gate, up, down):
    units = gate.shape[1]
    for n, out in enumerate((gate, up, down)):
        lanes = slice(units * n, units * n + units)
        out[...] = keep[:, lanes] + got[:, lanes].astype(F32)


def finish_ffn(keep, got, needs):
    rows, width = keep.shape
    out = (rows, width // 3)
    return call(
        finish_ffn_kernel,
        (keep, got),
        [full(keep.shape), full(got.shape)],
        [full(out)] * 3,
        [shaped(*out, dtype=F32)] * 3,
        "finish_ffn",
        needs=needs,
    )


def finish_attn_kernel(heads, keep, got, out_grad, query_grad, latent_grad):
    total = keep[...] + got[...].astype(F32)
    for h in range(heads):
        lanes = slice(128 * h, 128 * h + 128)
        out_grad[:, 64 * h : 64 * h + 64] = total[:160, 128 * h + 64 : 128 * h + 128]
        query_grad[:, 96 * h : 96 * h + 96] = total[160:208, 128 * h : 128 * h + 96]
    latent_grad[...] = total[208:224]


def finish_attn(keep, got, needs):
    heads = keep.shape[1] // 128
    outs = [(160, 64 * heads), (48, 96 * heads), (16, 128 * heads)]
    return call(
        functools.partial(finish_attn_kernel, heads),
        (keep, got),
        [full(keep.shape), full(got.shape)],
        [full(s) for s in outs],
        [shaped(*s, dtype=F32) for s in outs],
        "finish_attn",
        needs=needs,
    )


GAINS = ((0, 160), (160, 160), (320, 48), (368, 16))


def down_parts_kernel(own_in, raw_back, gains, out):
    total = dot(own_in[...], raw_back[...]).astype(BF16)
    for d in range(16):
        out[d, :20, :] = total[20 * d : 20 * d + 20]
        out[d, 20:, :] = jnp.zeros((4, WIDE), BF16)
        out[d, 20:21, :] = gains[d : d + 1, :]


def down_parts(own_in, raw_back, gains, needs):
    args = (own_in, raw_back, gains)
    return call(
        down_parts_kernel,
        args,
        [full(item.shape) for item in args],
        [full((16, 24, WIDE))],
        [shaped(16, 24, WIDE)],
        "down_parts",
        needs=needs,
        limit=24,
    )


def sum_copies_kernel(got, many):
    total = got[0].astype(F32)
    for d in range(1, 16):
        total = total + got[d].astype(F32)
    for k in range(8):
        many[k] = total.astype(BF16)


def sum_copies(got, needs):
    return call(
        sum_copies_kernel,
        (got,),
        [full(got.shape)],
        [full((8, 24, WIDE))],
        [shaped(8, 24, WIDE)],
        "sum_copies",
        needs=needs,
        limit=24,
    )


def finish_down_kernel(everyone, query_grad, latent_grad, *gains):
    for t in range(8):
        values = everyone[t].astype(F32)
        query_grad[20 * t : 20 * t + 20, :] = values[:20, :QR]
        latent_grad[20 * t : 20 * t + 20, :KVR] = values[:20, QR:LAT]
        latent_grad[20 * t : 20 * t + 20, KVR:] = values[:20, LAT + 64 : LAT + 96]
    total = sum(everyone[t, 16:24, :].astype(F32) for t in range(8))[4:5, :]
    for out, (first, count) in zip(gains, GAINS):
        out[...] = total[:, first : first + count]


def finish_down(everyone):
    everyone = everyone.reshape(8, 24, WIDE)
    outs = [(160, QR), (160, KVR + ROPE)] + [(1, count) for _, count in GAINS]
    return call(
        finish_down_kernel,
        (everyone,),
        [full(everyone.shape)],
        [full(s) for s in outs],
        [shaped(*s, dtype=F32) for s in outs],
        "finish_down",
        limit=24,
    )[0]


def exchange(blocks):
    return lax.all_to_all(blocks.reshape(-1, blocks.shape[-1]), TP, 0, 0, tiled=True)


def on_device(
    tokens,
    first_gain,
    query_down,
    query_gain,
    query_up,
    latent_down,
    latent_gain,
    latent_up,
    out_weight,
    second_gain,
    gate_weight,
    up_weight,
    down_weight,
    cotangent,
):
    length = tokens.shape[0]
    me = lax.axis_index(TP).astype(jnp.int32).reshape(1)
    y, xl, core = lax.axis_index("y"), lax.axis_index("xl"), lax.axis_index("core")
    starts = jnp.stack(
        [
            ((y + k) % 4 * 2 + (xl ^ j)) * 2 + c
            for c in (core, 1 - core)
            for k in range(4)
            for j in range(2)
        ]
    ).astype(jnp.int32)
    places = jnp.stack([lax.axis_index("z") ^ k for k in range(4)] + [me[0]]).astype(jnp.int32)
    z_order = jnp.stack([(lax.axis_index("z") + k) % 4 for k in range(4)]).astype(jnp.int32)
    tables = rope_tables(length)

    gate_turned, up_turned = gate_weight.T, up_weight.T

    (
        first_in,
        latents,
        query_code,
        latent_code,
        queries,
        keyvals,
        rope_keys,
        heads_out,
        log_total,
        attn_partial,
    ), started = attend(
        me,
        tokens,
        first_gain,
        query_down,
        latent_down,
        query_gain,
        latent_gain,
        query_up,
        latent_up,
        out_weight,
        tables,
    )
    attn_got = exchange(attn_partial)

    (cot_keep, cot_give), picked = halves(starts, [cotangent], [started])
    inner_back = dot(cotangent, down_weight, NT)
    cot_got = over_cores(cot_give)

    (residual, second_many), _ = residual_of(
        me, attn_got, tokens, second_gain, [picked, cot_got]
    )
    second_in = exchange(second_many)

    turned_in = first_in.T.reshape(16, 8, 20, length)
    own_in = lax.dynamic_slice_in_dim(turned_in, me[0], 1, 1).reshape(320, length)
    (code_keep, code_give, lat_keep, lat_give), picked = halves(
        starts, [query_code, latent_code], [residual]
    )
    code_got, lat_got = over_cores(code_give), over_cores(lat_give)
    heads_got = over_cores(heads_out)

    (gate_back, up_back, inner, back_partial), done = ffn(
        second_in, gate_turned, up_turned, inner_back, [picked, own_in, code_got, lat_got, heads_got]
    )
    back_got = exchange(back_partial)

    ours = (gate_back, up_back, inner)
    theirs = [over_cores(item) for item in ours]
    (in_keep, in_give), _ = halves(starts, [second_in], [done])
    in_got = over_cores(in_give)
    (far_up, far_down, ffn_up, ffn_down_way, ffn_own), done = ffn_grads(in_keep, in_got, cot_keep, cot_got, ours, theirs, gate_weight.shape[1], [])
    below, above = lax.ppermute(far_up, "y", UP), lax.ppermute(far_down, "y", DOWN)

    (back_many, second_gain_part), done = residual_back_of(
        me, back_got, residual, cotangent, second_gain, [done]
    )
    attention_back = exchange(back_many)
    mixed_blocks, done = ffn_down(places, inner, down_weight, residual, [done])
    mixed_got = over_z(mixed_blocks)
    (ffn_up, ffn_down_way), done = relay(ffn_up, below, ffn_down_way, above, [done])
    below, above = lax.ppermute(ffn_up, "y", UP), lax.ppermute(ffn_down_way, "y", DOWN)

    (both_back, latents_partial), back_done = attend_back(
        attention_back,
        out_weight,
        queries,
        keyvals,
        rope_keys,
        log_total,
        query_up,
        latent_up,
        tables,
        [done],
    )
    latents_got = exchange(latents_partial)

    (out_keep, out_give), picked = halves(starts, [attention_back], [back_done])
    (out_keep, out_give), done = halves(
        starts, [attention_back], [back_done, below, above, *mixed_got]
    )

    (raw_many, own_raw, latent_gain_parts), done = latents_back_of(
        me, latents_got, latents, query_gain, latent_gain, tables, [done]
    )
    raw_back = exchange(raw_many)

    out_got, both_got = over_cores(out_give), over_cores(both_back)
    (attn_across, attn_up, attn_down, attn_own), done = attn_grads(
        (out_keep, code_keep, lat_keep),
        (out_got, code_got, lat_got),
        (heads_out, both_back),
        (heads_got, both_got),
        [done],
    )
    (mixed_part,), done = add_all([mixed_blocks[0], *mixed_got], [done])
    mixed_other = lax.ppermute(mixed_part, "xh", SWAP)
    (first_gain_part,), done = first_gain_of(
        me, own_raw, tokens, query_down, latent_down, [done]
    )
    attn_got = [
        lax.ppermute(attn_across, "y", ACROSS),
        lax.ppermute(attn_up, "y", UP),
        lax.ppermute(attn_down, "y", DOWN),
    ]
    gains = jnp.concatenate(
        [
            first_gain_part.reshape(16, -1),
            second_gain_part.reshape(16, -1),
            latent_gain_parts[0, :QR].reshape(16, -1),
            latent_gain_parts[0, QR:].reshape(16, -1),
        ],
        axis=1,
    ).astype(BF16)
    gains = jnp.pad(gains, ((0, 0), (0, WIDE - gains.shape[1])))
    (parts,), done = down_parts(own_in, raw_back, gains, [done])
    parts_got = lax.all_to_all(parts, DP, 0, 0, tiled=True)

    (ffn_keep, ffn_give), done = add_chips([ffn_own, below, above], [done])
    ffn_got = lax.ppermute(ffn_give, "xl", SWAP)
    (mixed_part,), done = add_all([mixed_part, mixed_other], [done])
    from_above, across, from_below = (
        lax.ppermute(mixed_part, "z", way) for way in (DOWN, ACROSS, UP)
    )
    (tokens_grad,), done = tokens_back_of(
        raw_back, tokens, attention_back, query_down, latent_down, first_gain, [done]
    )
    (many,), summed = sum_copies(parts_got, [done])
    everyone = exchange(many)

    (attn_keep, attn_give), done = add_chips([attn_own, *attn_got], [summed])
    attn_other = lax.ppermute(attn_give, "xl", SWAP)
    (gate_weight_grad, up_weight_grad, down_weight_grad), done = finish_ffn(
        ffn_keep, ffn_got, [done]
    )
    (out_weight_grad, query_up_grad, latent_up_grad), done = finish_attn(
        attn_keep, attn_other, [done]
    )
    (
        query_down_grad,
        latent_down_grad,
        first_gain_grad,
        second_gain_grad,
        query_gain_grad,
        latent_gain_grad,
    ) = finish_down(everyone)

    mixed = assemble(
        z_order, [mixed_part, from_above, across, from_below], [done]
    )

    return (
        mixed,
        tokens_grad,
        first_gain_grad[0],
        query_down_grad,
        query_gain_grad[0],
        query_up_grad,
        latent_down_grad,
        latent_gain_grad[0],
        latent_up_grad,
        out_weight_grad.T,
        second_gain_grad[0],
        gate_weight_grad,
        up_weight_grad,
        down_weight_grad.T,
    )


def solution(mesh):
    grid = Mesh(mesh.devices.reshape(4, 2, 2, 2, 4), ("y", "xl", "core", "xh", "z"))
    in_specs = (
        P(DP, None),
        P(),
        P(),
        P(),
        P(None, TP),
        P(),
        P(),
        P(None, TP),
        P(TP, None),
        P(),
        P(None, TP),
        P(None, TP),
        P(TP, None),
        P(DP, None),
    )
    out_specs = (
        P(DP, None),
        P(DP, None),
        P(DP),
        P(DP, None),
        P(DP),
        P(DP, TP),
        P(DP, None),
        P(DP),
        P(DP, TP),
        P(TP, DP),
        P(DP),
        P(DP, TP),
        P(DP, TP),
        P(TP, DP),
    )
    return jax.shard_map(
        on_device, mesh=grid, in_specs=in_specs, out_specs=out_specs, check_vma=False
    )
```

```python
import functools

import jax
import jax.numpy as jnp
import numpy as np
from jax import lax
from jax.experimental import pallas as pl
from jax.experimental.pallas import tpu as pltpu
from jax.sharding import Mesh, PartitionSpec as P

NOPE = 64
ROPE = 32
DV = 64
KVR = 256
QR = 768
LAT = QR + KVR
WIDE = LAT + 128

EPS = 1e-05
BASE = 10000.0
SCALE = (NOPE + ROPE) ** (-0.5)

DP = ("y", "xl", "core")
TP = ("xh", "z")
SWAP = [(0, 1), (1, 0)]
F32 = jnp.float32
BF16 = jnp.bfloat16
NT = (((1,), (1,)), ((), ()))
TN = (((0,), (0,)), ((), ()))
NN = (((1,), (0,)), ((), ()))
TILE = 256


def dot(left, right, dims=NN):
    return lax.dot_general(left, right, dims, preferred_element_type=F32)


def params(limit=56):
    return pltpu.CompilerParams(vmem_limit_bytes=limit * 2**20)


HBM = pl.BlockSpec(memory_space=pltpu.HBM)


def call(kernel, args, in_specs, out_specs, out_shape, name, grid=(1,), scratch=(), needs=(), me=None, limit=60):
    first = 0 if me is None else 1
    n_in, n_out = len(args), len(out_shape)

    def body(*refs):
        ins = refs[: first + n_in]
        rest = refs[first + n_in + len(needs) :]
        mark = rest[n_out]

        @pl.when(pl.program_id(0) == 0)
        def _():
            mark[...] = jnp.zeros_like(mark)

        kernel(*ins, *rest[:n_out], *rest[n_out + 1 :])

    *outs, mark = pl.pallas_call(
        body,
        grid_spec=pltpu.PrefetchScalarGridSpec(
            num_scalar_prefetch=first,
            grid=grid,
            in_specs=list(in_specs) + [HBM] * len(needs),
            out_specs=list(out_specs) + [full((8, 128))],
            scratch_shapes=list(scratch),
        ),
        out_shape=list(out_shape) + [jax.ShapeDtypeStruct((8, 128), F32)],
        compiler_params=params(limit),
        cost_estimate=pl.CostEstimate(flops=1, bytes_accessed=1, transcendentals=0),
        name=name,
    )(*(() if me is None else (me,)), *args, *needs)
    return outs, mark


def shaped(*shape, dtype=BF16):
    return jax.ShapeDtypeStruct(shape, dtype)


def full(shape):
    return pl.BlockSpec(shape, lambda *_: (0,) * len(shape))


def rope_tables(length):
    half = ROPE // 2
    rates = np.exp(np.arange(half, dtype=np.float32) * np.float32(-2.0 * np.log(BASE) / ROPE))
    angles = np.arange(length, dtype=np.float32)[:, None] * rates.astype(np.float32)[None, :]
    cosine, sine = np.cos(angles), np.sin(angles)
    keep = np.zeros((length, 128), np.float32)
    keep[:, :NOPE] = 1.0
    keep[:, 64:80] = cosine
    keep[:, 80:96] = cosine
    low = np.zeros((length, 128), np.float32)
    low[:, 64:80] = -sine
    high = np.zeros((length, 128), np.float32)
    high[:, 80:96] = sine
    return jnp.asarray(keep), jnp.asarray(low), jnp.asarray(high)


def turn(values, keep, low, high, back=False):
    moved = pltpu.roll(values, 112, 1) * low + pltpu.roll(values, 16, 1) * high
    return values * keep - moved if back else values * keep + moved


def root(values):
    return lax.rsqrt(jnp.mean(values * values, axis=-1, keepdims=True) + EPS)


def norm_back(upstream, normed, factor, gain):
    scaled = upstream * gain
    return factor * (scaled - normed * jnp.mean(scaled * normed, axis=-1, keepdims=True))


def spread_out_weight(weight_ref, spread_ref, heads):
    spread_ref[...] = jnp.zeros_like(spread_ref)
    for h in range(heads):
        spread_ref[128 * h + 64 : 128 * h + 128, :] = weight_ref[64 * h : 64 * h + 64, :]


def spread_query_up(weight_ref, spread_ref, heads):
    spread_ref[...] = jnp.zeros_like(spread_ref)
    for h in range(heads):
        spread_ref[128 * h : 128 * h + 96, :] = weight_ref[96 * h : 96 * h + 96, :]


def row(ref):
    return ref[...].reshape(1, -1)


def low_lanes(shape):
    return lax.broadcasted_iota(jnp.int32, shape, 1) < NOPE


def causal(keys, queries, first_query):
    key_ids = lax.broadcasted_iota(jnp.int32, (keys, queries), 0)
    query_ids = lax.broadcasted_iota(jnp.int32, (keys, queries), 1) + first_query
    return key_ids <= query_ids


def attend_kernel(
    heads,
    me,
    tokens,
    first_gain,
    query_down,
    latent_down,
    query_gain,
    latent_gain,
    query_up,
    latent_up,
    out_weight,
    keep,
    low,
    high,
    first_in,
    latents,
    query_code,
    latent_code,
    queries,
    keyvals,
    rope_keys,
    heads_out,
    log_total,
    partial,
    raw_latents,
    spread,
    spread_up,
    rope_down,
    kv_all,
    rope_all,
):
    step = pl.program_id(0)

    @pl.when(step == 0)
    def _():
        spread_out_weight(out_weight, spread, heads)
        spread_query_up(query_up, spread_up, heads)
        rope_down[...] = jnp.zeros_like(rope_down)
        rope_down[64:96, :] = latent_down[KVR:, :]

    def rows_of(index, carry):
        rows = pl.ds(pl.multiple_of(index * 32, 32), 32)
        values = tokens[rows, :].astype(F32)
        first_in[rows, :] = (values * root(values) * row(first_gain)).astype(BF16)
        return carry

    lax.fori_loop(0, TILE // 32, rows_of, 0)
    taken = first_in[...]
    query_latent = dot(taken, query_down[...])
    raw_latents[:, :QR] = query_latent
    code = (query_latent * root(query_latent) * row(query_gain)).astype(BF16)
    query_code[...] = code
    latent = dot(taken, latent_down[:KVR, :], NT)
    raw_latents[:, QR:] = latent
    count = latents.shape[0]
    own = me[0] * count

    @pl.when(own // TILE == step)
    def _():
        latents[...] = raw_latents[pl.ds(pl.multiple_of(own % TILE, count), count), :]

    lcode = (latent * root(latent) * row(latent_gain)).astype(BF16)
    latent_code[...] = lcode
    tables = keep[...], low[...], high[...]
    rope = turn(dot(taken, rope_down[...], NT), *tables).astype(BF16)
    rope_keys[...] = rope
    here = pl.ds(pl.multiple_of(step * TILE, TILE), TILE)
    rope_all[here, :] = rope
    kv = dot(lcode, latent_up[...]).astype(BF16)
    keyvals[...] = kv
    kv_all[here, :] = kv
    raw = dot(code, spread_up[...], NT)
    for h in range(heads):
        lanes = slice(128 * h, 128 * h + 128)
        queries[:, lanes] = turn(raw[:, lanes], *tables).astype(BF16)

    def tile(index):
        keys = TILE * (index + 1)
        for h in range(heads):
            lanes = slice(128 * h, 128 * h + 128)
            kv_h = kv_all[:keys, lanes]
            key = jnp.where(low_lanes((keys, 128)), kv_h, rope_all[:keys, :])
            scores = dot(key, queries[:, lanes], NT) * SCALE
            scores = jnp.where(causal(keys, TILE, TILE * index), scores, -1e30)
            top = jnp.max(scores, axis=0, keepdims=True)
            weights = jnp.exp(scores - top)
            total = jnp.sum(weights, axis=0, keepdims=True)
            log_total[h : h + 1, :] = top + jnp.log(total)
            probs = (weights * (1.0 / total)).astype(BF16)
            heads_out[:, lanes] = dot(probs, kv_h, TN).astype(BF16)

    for index in range(2):
        pl.when(step == index)(functools.partial(tile, index))
    partial[...] = dot(heads_out[...], spread[...]).astype(BF16)


def attend(me, tokens, first_gain, query_down, latent_down, query_gain, latent_gain, query_up, latent_up, out_weight, tables):
    latent_down, query_up = latent_down.T, query_up.T
    length, width = tokens.shape
    heads = out_weight.shape[0] // DV
    wide = 128 * heads

    def rows(columns):
        return pl.BlockSpec((TILE, columns), lambda i, *_: (i, 0))

    return call(
        functools.partial(attend_kernel, heads),
        (tokens, first_gain, query_down, latent_down, query_gain, latent_gain, query_up, latent_up, out_weight, *tables),
        [
            rows(width),
            full((width,)),
            full(query_down.shape),
            full(latent_down.shape),
            full((QR,)),
            full((KVR,)),
            full(query_up.shape),
            full(latent_up.shape),
            full(out_weight.shape),
            rows(128),
            rows(128),
            rows(128),
        ],
        [
            rows(width),
            full((length // 8, LAT)),
            rows(QR),
            rows(KVR),
            rows(wide),
            rows(wide),
            rows(128),
            rows(wide),
            pl.BlockSpec((8, TILE), lambda i, *_: (0, i)),
            rows(width),
        ],
        [
            shaped(length, width),
            shaped(length // 8, LAT, dtype=F32),
            shaped(length, QR),
            shaped(length, KVR),
            shaped(length, wide),
            shaped(length, wide),
            shaped(length, 128),
            shaped(length, wide),
            shaped(8, length, dtype=F32),
            shaped(length, width),
        ],
        "attend",
        grid=(length // TILE,),
        me=me,
        scratch=[
            pltpu.VMEM((TILE, LAT), F32),
            pltpu.VMEM((wide, width), BF16),
            pltpu.VMEM((wide, QR), BF16),
            pltpu.VMEM((128, width), BF16),
            pltpu.VMEM((length, wide), BF16),
            pltpu.VMEM((length, 128), BF16),
        ],
    )


def attend_back_kernel(
    heads,
    attention_back,
    out_weight,
    queries,
    keyvals,
    rope_keys,
    log_total,
    query_up,
    latent_up,
    keep,
    low,
    high,
    both_back,
    partial,
    spread,
    spread_up,
    kv_grad,
    rope_grad,
    code_grad,
):
    step = pl.program_id(0)

    @pl.when(step == 0)
    def _():
        spread_out_weight(out_weight, spread, heads)
        spread_query_up(query_up, spread_up, heads)
        kv_grad[...] = jnp.zeros_like(kv_grad)
        rope_grad[...] = jnp.zeros_like(rope_grad)

    heads_back = dot(attention_back[...], spread[...], NT).astype(BF16)
    tables = keep[...], low[...], high[...]

    def tile(index):
        keys = TILE * (index + 1)
        low_part = low_lanes((keys, 128))
        for h in range(heads):
            lanes = slice(128 * h, 128 * h + 128)
            kv_h = keyvals[:keys, lanes]
            key = jnp.where(low_part, kv_h, rope_keys[:keys, :])
            query = queries[:, lanes]
            back = heads_back[:, lanes]
            scores = dot(key, query, NT) * SCALE
            probs = jnp.exp(scores - log_total[h : h + 1, :])
            probs = jnp.where(causal(keys, TILE, TILE * index), probs, 0.0)
            prob_back = dot(kv_h, back, NT)
            mean = jnp.sum(probs * prob_back, axis=0, keepdims=True)
            score_back = (probs * (prob_back - mean)).astype(BF16)
            of_values = dot(probs.astype(BF16), back)
            of_keys = dot(score_back, query) * SCALE
            kv_grad[:keys, lanes] += of_values + jnp.where(low_part, of_keys, 0.0)
            rope_grad[:keys, :] += jnp.where(low_part, 0.0, of_keys)
            of_query = dot(score_back, key, TN) * SCALE
            both_back[here, lanes] = turn(of_query, *tables, back=True).astype(BF16)

    wide = 128 * heads
    here = pl.ds(pl.multiple_of(step * TILE, TILE), TILE)
    for index in range(2):
        pl.when(step == index)(functools.partial(tile, index))
    code_grad[here, :] = dot(both_back[here, :wide], spread_up[...]).astype(BF16)

    @pl.when(step == 1)
    def _():
        kv = kv_grad[...].astype(BF16)
        both_back[:, wide:] = kv
        partial[:, :QR] = code_grad[...]
        partial[:, QR:LAT] = dot(kv, latent_up[...], NT).astype(BF16)
        partial[:, LAT:] = rope_grad[...].astype(BF16)


def attend_back(attention_back, out_weight, queries, keyvals, rope_keys, log_total, query_up, latent_up, tables, needs):
    query_up = query_up.T
    length, width = attention_back.shape
    heads = out_weight.shape[0] // DV
    wide = 128 * heads

    def rows(columns):
        return pl.BlockSpec((TILE, columns), lambda i, *_: (i, 0))

    return call(
        functools.partial(attend_back_kernel, heads),
        (attention_back, out_weight, queries, keyvals, rope_keys, log_total, query_up, latent_up, *tables),
        [
            rows(width),
            full(out_weight.shape),
            rows(wide),
            full((length, wide)),
            full((length, 128)),
            pl.BlockSpec((8, TILE), lambda i, *_: (0, i)),
            full(query_up.shape),
            full(latent_up.shape),
            rows(128),
            rows(128),
            rows(128),
        ],
        [full((length, 2 * wide)), full((length, WIDE))],
        [shaped(length, 2 * wide), shaped(length, WIDE)],
        "attend_back",
        grid=(length // TILE,),
        scratch=[
            pltpu.VMEM((wide, width), BF16),
            pltpu.VMEM((wide, QR), BF16),
            pltpu.VMEM((length, wide), F32),
            pltpu.VMEM((length, 128), F32),
            pltpu.VMEM((length, QR), BF16),
        ],
        needs=needs,
    )


def add_up(got):
    total = got[0].astype(F32)
    for k in range(1, 8):
        total = total + got[k].astype(F32)
    return total


STEPS = 2


def residual_kernel(me, got, tokens, gain, residual, many):
    del me
    total = tokens[...].astype(F32) + add_up(got)
    residual[...] = total
    second_in = (total * root(total) * row(gain)).astype(BF16)
    for k in range(8):
        many[k] = second_in


def own_specs(rows, width):
    step = rows // STEPS
    return (
        pl.BlockSpec((8, step, width), lambda i, me: (0, i, 0)),
        pl.BlockSpec((step, width), lambda i, me: (i, 0)),
        pl.BlockSpec((step, width), lambda i, me: (me[0] * STEPS + i, 0)),
    )


def residual_of(me, got, tokens, gain, needs):
    width = tokens.shape[1]
    rows = tokens.shape[0] // 8
    eight, one, own = own_specs(rows, width)
    return call(
        residual_kernel,
        (got.reshape(8, rows, width), tokens, gain),
        [eight, own, full((width,))],
        [one, eight],
        [shaped(rows, width, dtype=F32), shaped(8, rows, width)],
        "residual",
        grid=(STEPS,),
        needs=needs,
        me=me,
        limit=58,
    )


def residual_back_kernel(me, got, residual, cotangent, gain, many, gain_part):
    del me
    second_back = add_up(got)
    values = residual[...]
    factor = root(values)
    normed = values * factor
    part = jnp.sum(second_back * normed, axis=0, keepdims=True)

    @pl.when(pl.program_id(0) == 0)
    def _():
        gain_part[...] = part

    @pl.when(pl.program_id(0) > 0)
    def _():
        gain_part[...] += part

    back = cotangent[...].astype(F32) + norm_back(second_back, normed, factor, row(gain))
    back = back.astype(BF16)
    for k in range(8):
        many[k] = back


def residual_back_of(me, got, residual, cotangent, gain, needs):
    rows, width = residual.shape
    eight, one, own = own_specs(rows, width)
    return call(
        residual_back_kernel,
        (got.reshape(8, rows, width), residual, cotangent, gain),
        [eight, one, own, full((width,))],
        [eight, full((1, width))],
        [shaped(8, rows, width), shaped(1, width, dtype=F32)],
        "residual_back",
        grid=(STEPS,),
        needs=needs,
        me=me,
        limit=58,
    )


def ffn_kernel(
    second_in, gate_weight, up_weight, inner_back, gate_back, up_back, inner, partial
):
    taken = second_in[...]
    gate = dot(taken, gate_weight[...], NT)
    up = dot(taken, up_weight[...], NT)
    sigma = 1.0 / (1.0 + jnp.exp(-gate))
    act = gate * sigma
    units = gate.shape[1]
    back = inner_back[...]
    of_gate = (back * up * sigma * (1.0 + gate * (1.0 - sigma))).astype(BF16)
    of_up = (back * act).astype(BF16)
    for out, values in ((gate_back, of_gate), (up_back, of_up), (inner, (act * up).astype(BF16))):
        out[:, :units] = values
        out[:, units:] = jnp.zeros((values.shape[0], out.shape[1] - units), BF16)
    partial[...] = (dot(of_gate, gate_weight[...]) + dot(of_up, up_weight[...])).astype(BF16)


def ffn(second_in, gate_weight, up_weight, inner_back, needs):
    length, width = second_in.shape
    units = gate_weight.shape[0]
    wide = -(-units // 128) * 128

    def rows(columns):
        return pl.BlockSpec((TILE, columns), lambda i, *_: (i, 0))

    return call(
        ffn_kernel,
        (second_in, gate_weight, up_weight, inner_back),
        [rows(width), full((units, width)), full((units, width)), rows(units)],
        [rows(wide), rows(wide), rows(wide), rows(width)],
        [shaped(length, wide)] * 3 + [shaped(length, width)],
        "ffn",
        grid=(length // TILE,),
        needs=needs,
    )


def ffn_down_kernel(places, inner, down_weight, residual, *refs):
    outs, total = refs[:4], refs[4]
    for i in range(2):
        rows = slice(i * TILE, i * TILE + TILE)
        total[rows, :] = dot(inner[rows, : down_weight.shape[0]], down_weight[...]).astype(BF16)
    count = residual.shape[0]
    own = pl.ds(pl.multiple_of(places[4] * count, count), count)
    total[own, :] = (total[own, :].astype(F32) + residual[...]).astype(BF16)
    for k, out in enumerate(outs):
        rows = out.shape[0]
        out[...] = total[pl.ds(pl.multiple_of(places[k] * rows, rows), rows), :]


def ffn_down(places, inner, down_weight, residual, needs):
    length, width = inner.shape[0], down_weight.shape[1]
    block = (length // 4, width)
    return call(
        ffn_down_kernel,
        (inner, down_weight, residual),
        [full(inner.shape), full(down_weight.shape), full(residual.shape)],
        [full(block)] * 4,
        [shaped(*block)] * 4,
        "ffn_down",
        scratch=[pltpu.VMEM((length, width), BF16)],
        needs=needs,
        me=places,
    )


def halves_kernel(blocks, width, starts, *refs):
    sources, outs, turned = refs[:blocks], refs[blocks : 3 * blocks], refs[3 * blocks]
    for n in range(blocks):
        source, keep, give = sources[n], outs[2 * n], outs[2 * n + 1]
        columns, each = source.shape[1], width[n]
        for c in range(0, columns, 256):
            turned[c : c + 256, :] = source[:, c : c + 256].T
        for which, out in enumerate((keep, give)):
            for k in range(8):
                first = pl.multiple_of(starts[8 * which + k] * each, 16)
                out[each * k : each * k + each, :] = turned[pl.ds(first, each), :]


def halves(starts, values, needs):
    length = values[0].shape[0]
    widths = [item.shape[1] // 16 for item in values]
    shapes = [(8 * w, length) for w in widths for _ in range(2)]
    return call(
        functools.partial(halves_kernel, len(values), widths),
        tuple(values),
        [full(item.shape) for item in values],
        [full(s) for s in shapes],
        [shaped(*s) for s in shapes],
        "halves",
        scratch=[pltpu.VMEM((max(item.shape[1] for item in values), length), BF16)],
        needs=needs,
        me=starts,
    )


ORDER = (2, 1, 3, 0)


def ffn_grads_kernel(in_keep, in_got, cot_keep, cot_got, *refs):
    ours, theirs, outs = refs[:3], refs[3:6], refs[6:]
    units = outs[0].shape[1] // 3

    def block(*parts):
        for n, (keep, got) in enumerate(((in_keep, in_got), (in_keep, in_got), (cot_keep, cot_got))):
            total = dot(keep[...], ours[n][...]) + dot(got[...], theirs[n][...])
            total = total[:, :units].astype(BF16)
            first = 0
            for out in parts:
                count = out.shape[0]
                out[:, units * n : units * n + units] = total[first : first + count]
                first += count

    for s, parts in enumerate((outs[:2], outs[2:3], outs[3:4], outs[4:])):
        pl.when(pl.program_id(0) == s)(functools.partial(block, *parts))


def ffn_grads(in_keep, in_got, cot_keep, cot_got, ours, theirs, units, needs):
    length, wide = ours[0].shape
    rows = in_keep.shape[0] // 4

    def index(i):
        return (jnp.where(i == 0, 2, jnp.where(i == 1, 1, jnp.where(i == 2, 3, 0))), 0)

    left = pl.BlockSpec((rows, length), index)
    out = (rows, 3 * units)
    outs = [(rows // 2, 3 * units)] * 2 + [out] * 3
    return call(
        ffn_grads_kernel,
        (in_keep, in_got, cot_keep, cot_got, *ours, *theirs),
        [left] * 4 + [full((length, wide))] * 6,
        [full(s) for s in outs],
        [shaped(*s) for s in outs],
        "ffn_grads",
        grid=(4,),
        needs=needs,
    )


def attn_grads_kernel(widths, *refs):
    keeps, gots, outs = refs[:3], refs[3:6], refs[10:]
    wide = outs[0].shape[1]
    ours, theirs = (
        (heads, both.at[:, :wide], both.at[:, wide:]) for heads, both in (refs[6:8], refs[8:10])
    )
    rows = sum(widths)
    for out, k in zip(outs, ORDER):
        first = 0
        for n, each in enumerate(widths):
            part = slice(2 * each * k, 2 * each * k + 2 * each)
            total = dot(keeps[n][part, :], ours[n][...]) + dot(gots[n][part, :], theirs[n][...])
            total = total.astype(BF16)
            out[first : first + each, :] = total[:each]
            out[rows + first : rows + first + each, :] = total[each:]
            first += each


def attn_grads(keeps, gots, ours, theirs, needs):
    widths = [item.shape[0] // 8 for item in keeps]
    rows, wide = sum(widths), ours[0].shape[1]
    args = (*keeps, *gots, *ours, *theirs)
    outs = [(2 * rows, wide)] * 4
    return call(
        functools.partial(attn_grads_kernel, widths),
        args,
        [full(item.shape) for item in args],
        [full(s) for s in outs],
        [shaped(*s) for s in outs],
        "attn_grads",
        needs=needs,
    )


UP = [(i, (i + 1) % 4) for i in range(4)]
DOWN = [(i, (i + 3) % 4) for i in range(4)]
ACROSS = [(i, (i + 2) % 4) for i in range(4)]


def relay_kernel(up, from_below, down, from_above, up_out, down_out):
    @pl.when(pl.program_id(0) == 0)
    def _():
        up_out[...] = (up[...].astype(F32) + from_below[...].astype(F32)).astype(BF16)
        down_out[...] = down[...]

    @pl.when(pl.program_id(0) == 1)
    def _():
        up_out[...] = up[...]
        down_out[...] = (down[...].astype(F32) + from_above[...].astype(F32)).astype(BF16)


def relay(up, from_below, down, from_above, needs):
    rows, width = from_below.shape
    half = pl.BlockSpec((rows, width), lambda i, *_: (i, 0))
    return call(
        relay_kernel,
        (up, from_below, down, from_above),
        [half, full((rows, width)), half, full((rows, width))],
        [half, half],
        [shaped(2 * rows, width)] * 2,
        "relay",
        grid=(2,),
        needs=needs,
    )


def add_chips_kernel(*refs):
    ins, keep, give = refs[:-2], refs[-2], refs[-1]
    count = len(ins) // 2
    keep[...] = sum(item[...].astype(F32) for item in ins[:count])
    give[...] = sum(item[...].astype(F32) for item in ins[count:]).astype(BF16)


def add_chips(items, needs):
    rows, width = items[0].shape[0] // 2, items[0].shape[1]
    step = rows // 2 if rows % 32 == 0 and (rows // 2) % 16 == 0 else rows
    count = rows // step
    mine = pl.BlockSpec((step, width), lambda i, *_: (i, 0))
    other = pl.BlockSpec((step, width), lambda i, *_: (i + count, 0))
    return call(
        add_chips_kernel,
        (*items, *items),
        [mine] * len(items) + [other] * len(items),
        [mine, mine],
        [shaped(rows, width, dtype=F32), shaped(rows, width)],
        "add_chips",
        grid=(count,),
        needs=needs,
    )


def add_all_kernel(*refs):
    refs[-1][...] = sum(item[...].astype(F32) for item in refs[:-1]).astype(BF16)


def add_all(items, needs):
    rows, width = items[0].shape
    half = pl.BlockSpec((rows // 2, width), lambda i, *_: (i, 0))
    return call(
        add_all_kernel,
        tuple(items),
        [half] * len(items),
        [half],
        [shaped(rows, width)],
        "add_all",
        grid=(2,),
        needs=needs,
        limit=58,
    )


def over_z(blocks):
    return [lax.ppermute(blocks[k], "z", [(i, i ^ k) for i in range(4)]) for k in (1, 2, 3)]


def assemble_kernel(places, *refs):
    del places
    for k in range(4):

        @pl.when(pl.program_id(0) == k)
        def _(k=k):
            refs[4][...] = refs[k][...]


def assemble(places, blocks, needs):
    rows, width = blocks[0].shape
    return call(
        assemble_kernel,
        tuple(blocks),
        [full(item.shape) for item in blocks],
        [pl.BlockSpec((rows, width), lambda i, places: (places[i], 0))],
        [shaped(4 * rows, width)],
        "assemble",
        grid=(4,),
        needs=needs,
        me=places,
    )[0][0]


def over_cores(values):
    return lax.ppermute(values, "core", SWAP)


def latents_back_kernel(
    me, got, latents, query_gain, latent_gain, keep, low, high, many, own, gain_part, turns, sems
):
    rows = own.shape[0]
    here = pl.ds(pl.multiple_of(me[0] * rows, rows), rows)
    copies = [
        pltpu.make_async_copy(table.at[here, :], turns.at[n], sems.at[n])
        for n, table in enumerate((keep, low, high))
    ]
    for copy in copies:
        copy.start()
    total = add_up(got)
    for copy in copies:
        copy.wait()

    def back(lanes, gain):
        upstream, values = total[:, lanes], latents[:, lanes]
        factor = root(values)
        normed = values * factor
        gain_part[:, lanes] = jnp.sum(upstream * normed, axis=0, keepdims=True)
        return norm_back(upstream, normed, factor, row(gain)).astype(BF16)

    own[:, :QR] = back(slice(0, QR), query_gain)
    own[:, QR:LAT] = back(slice(QR, LAT), latent_gain)
    own[:, LAT:] = turn(total[:, LAT:], turns[0], turns[1], turns[2], back=True).astype(BF16)
    for k in range(8):
        many[k] = own[...]


def latents_back_of(me, got, latents, query_gain, latent_gain, tables, needs):
    rows = latents.shape[0]
    return call(
        latents_back_kernel,
        (got.reshape(8, rows, WIDE), latents, query_gain, latent_gain, *tables),
        [full((8, rows, WIDE)), full(latents.shape), full((QR,)), full((KVR,)), HBM, HBM, HBM],
        [full((8, rows, WIDE)), full((rows, WIDE)), full((1, LAT))],
        [shaped(8, rows, WIDE), shaped(rows, WIDE), shaped(1, LAT, dtype=F32)],
        "latents_back",
        scratch=[
            pltpu.VMEM((3, rows, 128), F32),
            pltpu.SemaphoreType.DMA((3,)),
        ],
        needs=needs,
        me=me,
        limit=24,
    )


def first_back_of(raw_back, query_down, latent_down, rope_down):
    rope_down[...] = jnp.zeros_like(rope_down)
    rope_down[64:96, :] = latent_down[KVR:, :]
    return (
        dot(raw_back[:, :QR], query_down[...], NT)
        + dot(raw_back[:, QR:LAT], latent_down[:KVR, :])
        + dot(raw_back[:, LAT:], rope_down[...])
    )


def first_gain_kernel(
    me, raw_back, tokens, query_down, latent_down, gain_part, rope_down, own, sem
):
    rows = own.shape[0]
    here = pl.ds(pl.multiple_of(me[0] * rows, rows), rows)
    copy = pltpu.make_async_copy(tokens.at[here, :], own, sem)
    copy.start()
    first_back = first_back_of(raw_back, query_down, latent_down, rope_down)
    copy.wait()
    values = own[...].astype(F32)
    gain_part[...] = jnp.sum(first_back * (values * root(values)), axis=0, keepdims=True)


def first_gain_of(me, own_raw_back, tokens, query_down, latent_down, needs):
    width = tokens.shape[1]
    return call(
        first_gain_kernel,
        (own_raw_back, tokens, query_down, latent_down.T),
        [full(own_raw_back.shape), HBM, full(query_down.shape), full(latent_down.shape[::-1])],
        [full((1, width))],
        [shaped(1, width, dtype=F32)],
        "first_gain",
        scratch=[
            pltpu.VMEM((128, width), BF16),
            pltpu.VMEM((own_raw_back.shape[0], width), BF16),
            pltpu.SemaphoreType.DMA,
        ],
        needs=needs,
        me=me,
    )


def tokens_back_kernel(
    raw_back, tokens, attention_back, query_down, latent_down, gain, tokens_grad, rope_down
):
    first_back = first_back_of(raw_back, query_down, latent_down, rope_down)
    values = tokens[...].astype(F32)
    factor = root(values)
    tokens_grad[...] = attention_back[...].astype(F32) + norm_back(
        first_back, values * factor, factor, row(gain)
    )


def tokens_back_of(raw_back, tokens, attention_back, query_down, latent_down, gain, needs):
    length, width = tokens.shape

    def rows(columns):
        return pl.BlockSpec((TILE, columns), lambda i, *_: (i, 0))

    return call(
        tokens_back_kernel,
        (raw_back, tokens, attention_back, query_down, latent_down.T, gain),
        [
            rows(WIDE),
            rows(width),
            rows(width),
            full(query_down.shape),
            full(latent_down.shape[::-1]),
            full((width,)),
        ],
        [rows(width)],
        [shaped(length, width, dtype=F32)],
        "tokens_back",
        grid=(length // TILE,),
        scratch=[pltpu.VMEM((128, width), BF16)],
        needs=needs,
    )


def finish_ffn_kernel(keep, got, gate, up, down):
    units = gate.shape[1]
    for n, out in enumerate((gate, up, down)):
        lanes = slice(units * n, units * n + units)
        out[...] = keep[:, lanes] + got[:, lanes].astype(F32)


def finish_ffn(keep, got, needs):
    rows, width = keep.shape
    out = (rows, width // 3)
    return call(
        finish_ffn_kernel,
        (keep, got),
        [full(keep.shape), full(got.shape)],
        [full(out)] * 3,
        [shaped(*out, dtype=F32)] * 3,
        "finish_ffn",
        needs=needs,
    )


def finish_attn_kernel(heads, keep, got, out_grad, query_grad, latent_grad):
    total = keep[...] + got[...].astype(F32)
    for h in range(heads):
        lanes = slice(128 * h, 128 * h + 128)
        out_grad[:, 64 * h : 64 * h + 64] = total[:160, 128 * h + 64 : 128 * h + 128]
        query_grad[:, 96 * h : 96 * h + 96] = total[160:208, 128 * h : 128 * h + 96]
    latent_grad[...] = total[208:224]


def finish_attn(keep, got, needs):
    heads = keep.shape[1] // 128
    outs = [(160, 64 * heads), (48, 96 * heads), (16, 128 * heads)]
    return call(
        functools.partial(finish_attn_kernel, heads),
        (keep, got),
        [full(keep.shape), full(got.shape)],
        [full(s) for s in outs],
        [shaped(*s, dtype=F32) for s in outs],
        "finish_attn",
        needs=needs,
    )


GAINS = ((0, 160), (160, 160), (320, 48), (368, 16))


def down_parts_kernel(own_in, raw_back, gains, out):
    total = dot(own_in[...], raw_back[...]).astype(BF16)
    for d in range(16):
        out[d, :20, :] = total[20 * d : 20 * d + 20]
        out[d, 20:, :] = jnp.zeros((4, WIDE), BF16)
        out[d, 20:21, :] = gains[d : d + 1, :]


def down_parts(own_in, raw_back, gains, needs):
    args = (own_in, raw_back, gains)
    return call(
        down_parts_kernel,
        args,
        [full(item.shape) for item in args],
        [full((16, 24, WIDE))],
        [shaped(16, 24, WIDE)],
        "down_parts",
        needs=needs,
        limit=24,
    )


def sum_copies_kernel(got, many):
    total = got[0].astype(F32)
    for d in range(1, 16):
        total = total + got[d].astype(F32)
    for k in range(8):
        many[k] = total.astype(BF16)


def sum_copies(got, needs):
    return call(
        sum_copies_kernel,
        (got,),
        [full(got.shape)],
        [full((8, 24, WIDE))],
        [shaped(8, 24, WIDE)],
        "sum_copies",
        needs=needs,
        limit=24,
    )


def finish_down_kernel(everyone, query_grad, latent_grad, *gains):
    for t in range(8):
        values = everyone[t].astype(F32)
        query_grad[20 * t : 20 * t + 20, :] = values[:20, :QR]
        latent_grad[20 * t : 20 * t + 20, :KVR] = values[:20, QR:LAT]
        latent_grad[20 * t : 20 * t + 20, KVR:] = values[:20, LAT + 64 : LAT + 96]
    total = sum(everyone[t, 16:24, :].astype(F32) for t in range(8))[4:5, :]
    for out, (first, count) in zip(gains, GAINS):
        out[...] = total[:, first : first + count]


def finish_down(everyone):
    everyone = everyone.reshape(8, 24, WIDE)
    outs = [(160, QR), (160, KVR + ROPE)] + [(1, count) for _, count in GAINS]
    return call(
        finish_down_kernel,
        (everyone,),
        [full(everyone.shape)],
        [full(s) for s in outs],
        [shaped(*s, dtype=F32) for s in outs],
        "finish_down",
        limit=24,
    )[0]


def exchange(blocks):
    return lax.all_to_all(blocks.reshape(-1, blocks.shape[-1]), TP, 0, 0, tiled=True)


def on_device(
    tokens,
    first_gain,
    query_down,
    query_gain,
    query_up,
    latent_down,
    latent_gain,
    latent_up,
    out_weight,
    second_gain,
    gate_weight,
    up_weight,
    down_weight,
    cotangent,
):
    length = tokens.shape[0]
    me = lax.axis_index(TP).astype(jnp.int32).reshape(1)
    y, xl, core = lax.axis_index("y"), lax.axis_index("xl"), lax.axis_index("core")
    starts = jnp.stack(
        [
            ((y + k) % 4 * 2 + (xl ^ j)) * 2 + c
            for c in (core, 1 - core)
            for k in range(4)
            for j in range(2)
        ]
    ).astype(jnp.int32)
    places = jnp.stack([lax.axis_index("z") ^ k for k in range(4)] + [me[0]]).astype(jnp.int32)
    z_order = jnp.stack([(lax.axis_index("z") + k) % 4 for k in range(4)]).astype(jnp.int32)
    tables = rope_tables(length)

    gate_turned, up_turned = gate_weight.T, up_weight.T

    (
        first_in,
        latents,
        query_code,
        latent_code,
        queries,
        keyvals,
        rope_keys,
        heads_out,
        log_total,
        attn_partial,
    ), started = attend(
        me,
        tokens,
        first_gain,
        query_down,
        latent_down,
        query_gain,
        latent_gain,
        query_up,
        latent_up,
        out_weight,
        tables,
    )
    attn_got = exchange(attn_partial)

    (cot_keep, cot_give), picked = halves(starts, [cotangent], [started])
    inner_back = dot(cotangent, down_weight, NT)
    cot_got = over_cores(cot_give)

    (residual, second_many), _ = residual_of(
        me, attn_got, tokens, second_gain, [picked, cot_got]
    )
    second_in = exchange(second_many)

    turned_in = first_in.T.reshape(16, 8, 20, length)
    own_in = lax.dynamic_slice_in_dim(turned_in, me[0], 1, 1).reshape(320, length)
    (code_keep, code_give, lat_keep, lat_give), picked = halves(
        starts, [query_code, latent_code], [residual]
    )
    code_got, lat_got = over_cores(code_give), over_cores(lat_give)
    heads_got = over_cores(heads_out)

    (gate_back, up_back, inner, back_partial), done = ffn(
        second_in, gate_turned, up_turned, inner_back, [picked, own_in, code_got, lat_got, heads_got]
    )
    back_got = exchange(back_partial)

    ours = (gate_back, up_back, inner)
    theirs = [over_cores(item) for item in ours]
    (in_keep, in_give), _ = halves(starts, [second_in], [done])
    in_got = over_cores(in_give)
    (far_up, far_down, ffn_up, ffn_down_way, ffn_own), done = ffn_grads(in_keep, in_got, cot_keep, cot_got, ours, theirs, gate_weight.shape[1], [])
    below, above = lax.ppermute(far_up, "y", UP), lax.ppermute(far_down, "y", DOWN)

    (back_many, second_gain_part), done = residual_back_of(
        me, back_got, residual, cotangent, second_gain, [done]
    )
    attention_back = exchange(back_many)
    mixed_blocks, done = ffn_down(places, inner, down_weight, residual, [done])
    mixed_got = over_z(mixed_blocks)
    (ffn_up, ffn_down_way), done = relay(ffn_up, below, ffn_down_way, above, [done])
    below, above = lax.ppermute(ffn_up, "y", UP), lax.ppermute(ffn_down_way, "y", DOWN)

    (both_back, latents_partial), back_done = attend_back(
        attention_back,
        out_weight,
        queries,
        keyvals,
        rope_keys,
        log_total,
        query_up,
        latent_up,
        tables,
        [done],
    )
    latents_got = exchange(latents_partial)

    (out_keep, out_give), picked = halves(starts, [attention_back], [back_done])
    (out_keep, out_give), done = halves(
        starts, [attention_back], [back_done, below, above, *mixed_got]
    )
    (mixed_part,), done = add_all([mixed_blocks[0], *mixed_got], [done])
    mixed_other = lax.ppermute(mixed_part, "xh", SWAP)

    (raw_many, own_raw, latent_gain_parts), done = latents_back_of(
        me, latents_got, latents, query_gain, latent_gain, tables, [done]
    )
    raw_back = exchange(raw_many)

    out_got, both_got = over_cores(out_give), over_cores(both_back)
    (attn_across, attn_up, attn_down, attn_own), done = attn_grads(
        (out_keep, code_keep, lat_keep),
        (out_got, code_got, lat_got),
        (heads_out, both_back),
        (heads_got, both_got),
        [done],
    )
    (first_gain_part,), done = first_gain_of(
        me, own_raw, tokens, query_down, latent_down, [done]
    )
    attn_got = [
        lax.ppermute(attn_across, "y", ACROSS),
        lax.ppermute(attn_up, "y", UP),
        lax.ppermute(attn_down, "y", DOWN),
    ]
    gains = jnp.concatenate(
        [
            first_gain_part.reshape(16, -1),
            second_gain_part.reshape(16, -1),
            latent_gain_parts[0, :QR].reshape(16, -1),
            latent_gain_parts[0, QR:].reshape(16, -1),
        ],
        axis=1,
    ).astype(BF16)
    gains = jnp.pad(gains, ((0, 0), (0, WIDE - gains.shape[1])))
    (ffn_keep, ffn_give), done = add_chips([ffn_own, below, above], [done])
    ffn_got = lax.ppermute(ffn_give, "xl", SWAP)
    (parts,), done = down_parts(own_in, raw_back, gains, [done, attn_got[1], attn_got[2]])
    parts_got = lax.all_to_all(parts, DP, 0, 0, tiled=True)

    (mixed_part,), done = add_all([mixed_part, mixed_other], [done])
    from_above, across, from_below = (
        lax.ppermute(mixed_part, "z", way) for way in (DOWN, ACROSS, UP)
    )
    (tokens_grad,), done = tokens_back_of(
        raw_back, tokens, attention_back, query_down, latent_down, first_gain, [done]
    )
    (many,), summed = sum_copies(parts_got, [done])
    everyone = exchange(many)

    (attn_keep, attn_give), done = add_chips([attn_own, *attn_got], [summed])
    attn_other = lax.ppermute(attn_give, "xl", SWAP)
    (gate_weight_grad, up_weight_grad, down_weight_grad), done = finish_ffn(
        ffn_keep, ffn_got, [done]
    )
    (out_weight_grad, query_up_grad, latent_up_grad), done = finish_attn(
        attn_keep, attn_other, [done]
    )
    (
        query_down_grad,
        latent_down_grad,
        first_gain_grad,
        second_gain_grad,
        query_gain_grad,
        latent_gain_grad,
    ) = finish_down(everyone)

    mixed = assemble(
        z_order, [mixed_part, from_above, across, from_below], [done]
    )

    return (
        mixed,
        tokens_grad,
        first_gain_grad[0],
        query_down_grad,
        query_gain_grad[0],
        query_up_grad,
        latent_down_grad,
        latent_gain_grad[0],
        latent_up_grad,
        out_weight_grad.T,
        second_gain_grad[0],
        gate_weight_grad,
        up_weight_grad,
        down_weight_grad.T,
    )


def solution(mesh):
    grid = Mesh(mesh.devices.reshape(4, 2, 2, 2, 4), ("y", "xl", "core", "xh", "z"))
    in_specs = (
        P(DP, None),
        P(),
        P(),
        P(),
        P(None, TP),
        P(),
        P(),
        P(None, TP),
        P(TP, None),
        P(),
        P(None, TP),
        P(None, TP),
        P(TP, None),
        P(DP, None),
    )
    out_specs = (
        P(DP, None),
        P(DP, None),
        P(DP),
        P(DP, None),
        P(DP),
        P(DP, TP),
        P(DP, None),
        P(DP),
        P(DP, TP),
        P(TP, DP),
        P(DP),
        P(DP, TP),
        P(DP, TP),
        P(TP, DP),
    )
    return jax.shard_map(
        on_device, mesh=grid, in_specs=in_specs, out_specs=out_specs, check_vma=False
    )
```

```python
import functools

import jax
import jax.numpy as jnp
import numpy as np
from jax import lax
from jax.experimental import pallas as pl
from jax.experimental.pallas import tpu as pltpu
from jax.sharding import Mesh, PartitionSpec as P

NOPE = 64
ROPE = 32
DV = 64
KVR = 256
QR = 768
LAT = QR + KVR
WIDE = LAT + 128

EPS = 1e-05
BASE = 10000.0
SCALE = (NOPE + ROPE) ** (-0.5)

DP = ("y", "xl", "core")
TP = ("xh", "z")
SWAP = [(0, 1), (1, 0)]
F32 = jnp.float32
BF16 = jnp.bfloat16
NT = (((1,), (1,)), ((), ()))
TN = (((0,), (0,)), ((), ()))
NN = (((1,), (0,)), ((), ()))
TILE = 256


def dot(left, right, dims=NN):
    return lax.dot_general(left, right, dims, preferred_element_type=F32)


def params(limit=56):
    return pltpu.CompilerParams(vmem_limit_bytes=limit * 2**20)


HBM = pl.BlockSpec(memory_space=pltpu.HBM)


def call(kernel, args, in_specs, out_specs, out_shape, name, grid=(1,), scratch=(), needs=(), me=None, limit=60):
    first = 0 if me is None else 1
    n_in, n_out = len(args), len(out_shape)

    def body(*refs):
        ins = refs[: first + n_in]
        rest = refs[first + n_in + len(needs) :]
        mark = rest[n_out]

        @pl.when(pl.program_id(0) == 0)
        def _():
            mark[...] = jnp.zeros_like(mark)

        kernel(*ins, *rest[:n_out], *rest[n_out + 1 :])

    *outs, mark = pl.pallas_call(
        body,
        grid_spec=pltpu.PrefetchScalarGridSpec(
            num_scalar_prefetch=first,
            grid=grid,
            in_specs=list(in_specs) + [HBM] * len(needs),
            out_specs=list(out_specs) + [full((8, 128))],
            scratch_shapes=list(scratch),
        ),
        out_shape=list(out_shape) + [jax.ShapeDtypeStruct((8, 128), F32)],
        compiler_params=params(limit),
        cost_estimate=pl.CostEstimate(flops=1, bytes_accessed=1, transcendentals=0),
        name=name,
    )(*(() if me is None else (me,)), *args, *needs)
    return outs, mark


def shaped(*shape, dtype=BF16):
    return jax.ShapeDtypeStruct(shape, dtype)


def full(shape):
    return pl.BlockSpec(shape, lambda *_: (0,) * len(shape))


def rope_tables(length):
    half = ROPE // 2
    rates = np.exp(np.arange(half, dtype=np.float32) * np.float32(-2.0 * np.log(BASE) / ROPE))
    angles = np.arange(length, dtype=np.float32)[:, None] * rates.astype(np.float32)[None, :]
    cosine, sine = np.cos(angles), np.sin(angles)
    keep = np.zeros((length, 128), np.float32)
    keep[:, :NOPE] = 1.0
    keep[:, 64:80] = cosine
    keep[:, 80:96] = cosine
    low = np.zeros((length, 128), np.float32)
    low[:, 64:80] = -sine
    high = np.zeros((length, 128), np.float32)
    high[:, 80:96] = sine
    return jnp.asarray(keep), jnp.asarray(low), jnp.asarray(high)


def turn(values, keep, low, high, back=False):
    moved = pltpu.roll(values, 112, 1) * low + pltpu.roll(values, 16, 1) * high
    return values * keep - moved if back else values * keep + moved


def root(values):
    return lax.rsqrt(jnp.mean(values * values, axis=-1, keepdims=True) + EPS)


def norm_back(upstream, normed, factor, gain):
    scaled = upstream * gain
    return factor * (scaled - normed * jnp.mean(scaled * normed, axis=-1, keepdims=True))


def spread_out_weight(weight_ref, spread_ref, heads):
    spread_ref[...] = jnp.zeros_like(spread_ref)
    for h in range(heads):
        spread_ref[128 * h + 64 : 128 * h + 128, :] = weight_ref[64 * h : 64 * h + 64, :]


def spread_query_up(weight_ref, spread_ref, heads):
    spread_ref[...] = jnp.zeros_like(spread_ref)
    for h in range(heads):
        spread_ref[128 * h : 128 * h + 96, :] = weight_ref[96 * h : 96 * h + 96, :]


def row(ref):
    return ref[...].reshape(1, -1)


def low_lanes(shape):
    return lax.broadcasted_iota(jnp.int32, shape, 1) < NOPE


def causal(keys, queries, first_query):
    key_ids = lax.broadcasted_iota(jnp.int32, (keys, queries), 0)
    query_ids = lax.broadcasted_iota(jnp.int32, (keys, queries), 1) + first_query
    return key_ids <= query_ids


def attend_kernel(
    heads,
    me,
    tokens,
    first_gain,
    query_down,
    latent_down,
    query_gain,
    latent_gain,
    query_up,
    latent_up,
    out_weight,
    keep,
    low,
    high,
    first_in,
    latents,
    query_code,
    latent_code,
    queries,
    keyvals,
    rope_keys,
    heads_out,
    log_total,
    partial,
    raw_latents,
    spread,
    spread_up,
    rope_down,
    kv_all,
    rope_all,
):
    step = pl.program_id(0)

    @pl.when(step == 0)
    def _():
        spread_out_weight(out_weight, spread, heads)
        spread_query_up(query_up, spread_up, heads)
        rope_down[...] = jnp.zeros_like(rope_down)
        rope_down[64:96, :] = latent_down[KVR:, :]

    def rows_of(index, carry):
        rows = pl.ds(pl.multiple_of(index * 32, 32), 32)
        values = tokens[rows, :].astype(F32)
        first_in[rows, :] = (values * root(values) * row(first_gain)).astype(BF16)
        return carry

    lax.fori_loop(0, TILE // 32, rows_of, 0)
    taken = first_in[...]
    query_latent = dot(taken, query_down[...])
    raw_latents[:, :QR] = query_latent
    code = (query_latent * root(query_latent) * row(query_gain)).astype(BF16)
    query_code[...] = code
    latent = dot(taken, latent_down[:KVR, :], NT)
    raw_latents[:, QR:] = latent
    count = latents.shape[0]
    own = me[0] * count

    @pl.when(own // TILE == step)
    def _():
        latents[...] = raw_latents[pl.ds(pl.multiple_of(own % TILE, count), count), :]

    lcode = (latent * root(latent) * row(latent_gain)).astype(BF16)
    latent_code[...] = lcode
    tables = keep[...], low[...], high[...]
    rope = turn(dot(taken, rope_down[...], NT), *tables).astype(BF16)
    rope_keys[...] = rope
    here = pl.ds(pl.multiple_of(step * TILE, TILE), TILE)
    rope_all[here, :] = rope
    kv = dot(lcode, latent_up[...]).astype(BF16)
    keyvals[...] = kv
    kv_all[here, :] = kv
    raw = dot(code, spread_up[...], NT)
    for h in range(heads):
        lanes = slice(128 * h, 128 * h + 128)
        queries[:, lanes] = turn(raw[:, lanes], *tables).astype(BF16)

    def tile(index):
        keys = TILE * (index + 1)
        for h in range(heads):
            lanes = slice(128 * h, 128 * h + 128)
            kv_h = kv_all[:keys, lanes]
            key = jnp.where(low_lanes((keys, 128)), kv_h, rope_all[:keys, :])
            scores = dot(key, queries[:, lanes], NT) * SCALE
            scores = jnp.where(causal(keys, TILE, TILE * index), scores, -1e30)
            top = jnp.max(scores, axis=0, keepdims=True)
            weights = jnp.exp(scores - top)
            total = jnp.sum(weights, axis=0, keepdims=True)
            log_total[h : h + 1, :] = top + jnp.log(total)
            probs = (weights * (1.0 / total)).astype(BF16)
            heads_out[:, lanes] = dot(probs, kv_h, TN).astype(BF16)

    for index in range(2):
        pl.when(step == index)(functools.partial(tile, index))
    partial[...] = dot(heads_out[...], spread[...]).astype(BF16)


def attend(me, tokens, first_gain, query_down, latent_down, query_gain, latent_gain, query_up, latent_up, out_weight, tables):
    latent_down, query_up = latent_down.T, query_up.T
    length, width = tokens.shape
    heads = out_weight.shape[0] // DV
    wide = 128 * heads

    def rows(columns):
        return pl.BlockSpec((TILE, columns), lambda i, *_: (i, 0))

    return call(
        functools.partial(attend_kernel, heads),
        (tokens, first_gain, query_down, latent_down, query_gain, latent_gain, query_up, latent_up, out_weight, *tables),
        [
            rows(width),
            full((width,)),
            full(query_down.shape),
            full(latent_down.shape),
            full((QR,)),
            full((KVR,)),
            full(query_up.shape),
            full(latent_up.shape),
            full(out_weight.shape),
            rows(128),
            rows(128),
            rows(128),
        ],
        [
            rows(width),
            full((length // 8, LAT)),
            rows(QR),
            rows(KVR),
            rows(wide),
            rows(wide),
            rows(128),
            rows(wide),
            pl.BlockSpec((8, TILE), lambda i, *_: (0, i)),
            rows(width),
        ],
        [
            shaped(length, width),
            shaped(length // 8, LAT, dtype=F32),
            shaped(length, QR),
            shaped(length, KVR),
            shaped(length, wide),
            shaped(length, wide),
            shaped(length, 128),
            shaped(length, wide),
            shaped(8, length, dtype=F32),
            shaped(length, width),
        ],
        "attend",
        grid=(length // TILE,),
        me=me,
        scratch=[
            pltpu.VMEM((TILE, LAT), F32),
            pltpu.VMEM((wide, width), BF16),
            pltpu.VMEM((wide, QR), BF16),
            pltpu.VMEM((128, width), BF16),
            pltpu.VMEM((length, wide), BF16),
            pltpu.VMEM((length, 128), BF16),
        ],
    )


def attend_back_kernel(
    heads,
    attention_back,
    out_weight,
    queries,
    keyvals,
    rope_keys,
    log_total,
    query_up,
    latent_up,
    keep,
    low,
    high,
    both_back,
    partial,
    spread,
    spread_up,
    kv_grad,
    rope_grad,
    code_grad,
):
    step = pl.program_id(0)

    @pl.when(step == 0)
    def _():
        spread_out_weight(out_weight, spread, heads)
        spread_query_up(query_up, spread_up, heads)
        kv_grad[...] = jnp.zeros_like(kv_grad)
        rope_grad[...] = jnp.zeros_like(rope_grad)

    heads_back = dot(attention_back[...], spread[...], NT).astype(BF16)
    tables = keep[...], low[...], high[...]

    def tile(index):
        keys = TILE * (index + 1)
        low_part = low_lanes((keys, 128))
        for h in range(heads):
            lanes = slice(128 * h, 128 * h + 128)
            kv_h = keyvals[:keys, lanes]
            key = jnp.where(low_part, kv_h, rope_keys[:keys, :])
            query = queries[:, lanes]
            back = heads_back[:, lanes]
            scores = dot(key, query, NT) * SCALE
            probs = jnp.exp(scores - log_total[h : h + 1, :])
            probs = jnp.where(causal(keys, TILE, TILE * index), probs, 0.0)
            prob_back = dot(kv_h, back, NT)
            mean = jnp.sum(probs * prob_back, axis=0, keepdims=True)
            score_back = (probs * (prob_back - mean)).astype(BF16)
            of_values = dot(probs.astype(BF16), back)
            of_keys = dot(score_back, query) * SCALE
            kv_grad[:keys, lanes] += of_values + jnp.where(low_part, of_keys, 0.0)
            rope_grad[:keys, :] += jnp.where(low_part, 0.0, of_keys)
            of_query = dot(score_back, key, TN) * SCALE
            both_back[here, lanes] = turn(of_query, *tables, back=True).astype(BF16)

    wide = 128 * heads
    here = pl.ds(pl.multiple_of(step * TILE, TILE), TILE)
    for index in range(2):
        pl.when(step == index)(functools.partial(tile, index))
    code_grad[here, :] = dot(both_back[here, :wide], spread_up[...]).astype(BF16)

    @pl.when(step == 1)
    def _():
        kv = kv_grad[...].astype(BF16)
        both_back[:, wide:] = kv
        partial[:, :QR] = code_grad[...]
        partial[:, QR:LAT] = dot(kv, latent_up[...], NT).astype(BF16)
        partial[:, LAT:] = rope_grad[...].astype(BF16)


def attend_back(attention_back, out_weight, queries, keyvals, rope_keys, log_total, query_up, latent_up, tables, needs):
    query_up = query_up.T
    length, width = attention_back.shape
    heads = out_weight.shape[0] // DV
    wide = 128 * heads

    def rows(columns):
        return pl.BlockSpec((TILE, columns), lambda i, *_: (i, 0))

    return call(
        functools.partial(attend_back_kernel, heads),
        (attention_back, out_weight, queries, keyvals, rope_keys, log_total, query_up, latent_up, *tables),
        [
            rows(width),
            full(out_weight.shape),
            rows(wide),
            full((length, wide)),
            full((length, 128)),
            pl.BlockSpec((8, TILE), lambda i, *_: (0, i)),
            full(query_up.shape),
            full(latent_up.shape),
            rows(128),
            rows(128),
            rows(128),
        ],
        [full((length, 2 * wide)), full((length, WIDE))],
        [shaped(length, 2 * wide), shaped(length, WIDE)],
        "attend_back",
        grid=(length // TILE,),
        scratch=[
            pltpu.VMEM((wide, width), BF16),
            pltpu.VMEM((wide, QR), BF16),
            pltpu.VMEM((length, wide), F32),
            pltpu.VMEM((length, 128), F32),
            pltpu.VMEM((length, QR), BF16),
        ],
        needs=needs,
    )


def add_up(got):
    total = got[0].astype(F32)
    for k in range(1, 8):
        total = total + got[k].astype(F32)
    return total


STEPS = 2


def residual_kernel(me, got, tokens, gain, residual, many):
    del me
    total = tokens[...].astype(F32) + add_up(got)
    residual[...] = total
    second_in = (total * root(total) * row(gain)).astype(BF16)
    for k in range(8):
        many[k] = second_in


def own_specs(rows, width):
    step = rows // STEPS
    return (
        pl.BlockSpec((8, step, width), lambda i, me: (0, i, 0)),
        pl.BlockSpec((step, width), lambda i, me: (i, 0)),
        pl.BlockSpec((step, width), lambda i, me: (me[0] * STEPS + i, 0)),
    )


def residual_of(me, got, tokens, gain, needs):
    width = tokens.shape[1]
    rows = tokens.shape[0] // 8
    eight, one, own = own_specs(rows, width)
    return call(
        residual_kernel,
        (got.reshape(8, rows, width), tokens, gain),
        [eight, own, full((width,))],
        [one, eight],
        [shaped(rows, width, dtype=F32), shaped(8, rows, width)],
        "residual",
        grid=(STEPS,),
        needs=needs,
        me=me,
        limit=58,
    )


def residual_back_kernel(me, got, residual, cotangent, gain, many, gain_part):
    del me
    second_back = add_up(got)
    values = residual[...]
    factor = root(values)
    normed = values * factor
    part = jnp.sum(second_back * normed, axis=0, keepdims=True)

    @pl.when(pl.program_id(0) == 0)
    def _():
        gain_part[...] = part

    @pl.when(pl.program_id(0) > 0)
    def _():
        gain_part[...] += part

    back = cotangent[...].astype(F32) + norm_back(second_back, normed, factor, row(gain))
    back = back.astype(BF16)
    for k in range(8):
        many[k] = back


def residual_back_of(me, got, residual, cotangent, gain, needs):
    rows, width = residual.shape
    eight, one, own = own_specs(rows, width)
    return call(
        residual_back_kernel,
        (got.reshape(8, rows, width), residual, cotangent, gain),
        [eight, one, own, full((width,))],
        [eight, full((1, width))],
        [shaped(8, rows, width), shaped(1, width, dtype=F32)],
        "residual_back",
        grid=(STEPS,),
        needs=needs,
        me=me,
        limit=58,
    )


def ffn_kernel(
    second_in, gate_weight, up_weight, inner_back, gate_back, up_back, inner, partial
):
    taken = second_in[...]
    gate = dot(taken, gate_weight[...], NT)
    up = dot(taken, up_weight[...], NT)
    sigma = 1.0 / (1.0 + jnp.exp(-gate))
    act = gate * sigma
    units = gate.shape[1]
    back = inner_back[...]
    of_gate = (back * up * sigma * (1.0 + gate * (1.0 - sigma))).astype(BF16)
    of_up = (back * act).astype(BF16)
    for out, values in ((gate_back, of_gate), (up_back, of_up), (inner, (act * up).astype(BF16))):
        out[:, :units] = values
        out[:, units:] = jnp.zeros((values.shape[0], out.shape[1] - units), BF16)
    partial[...] = (dot(of_gate, gate_weight[...]) + dot(of_up, up_weight[...])).astype(BF16)


def ffn(second_in, gate_weight, up_weight, inner_back, needs):
    length, width = second_in.shape
    units = gate_weight.shape[0]
    wide = -(-units // 128) * 128

    def rows(columns):
        return pl.BlockSpec((TILE, columns), lambda i, *_: (i, 0))

    return call(
        ffn_kernel,
        (second_in, gate_weight, up_weight, inner_back),
        [rows(width), full((units, width)), full((units, width)), rows(units)],
        [rows(wide), rows(wide), rows(wide), rows(width)],
        [shaped(length, wide)] * 3 + [shaped(length, width)],
        "ffn",
        grid=(length // TILE,),
        needs=needs,
    )


def ffn_down_kernel(places, inner, down_weight, residual, *refs):
    outs, total = refs[:4], refs[4]
    for i in range(2):
        rows = slice(i * TILE, i * TILE + TILE)
        total[rows, :] = dot(inner[rows, : down_weight.shape[0]], down_weight[...]).astype(BF16)
    count = residual.shape[0]
    own = pl.ds(pl.multiple_of(places[4] * count, count), count)
    total[own, :] = (total[own, :].astype(F32) + residual[...]).astype(BF16)
    for k, out in enumerate(outs):
        rows = out.shape[0]
        out[...] = total[pl.ds(pl.multiple_of(places[k] * rows, rows), rows), :]


def ffn_down(places, inner, down_weight, residual, needs):
    length, width = inner.shape[0], down_weight.shape[1]
    block = (length // 4, width)
    return call(
        ffn_down_kernel,
        (inner, down_weight, residual),
        [full(inner.shape), full(down_weight.shape), full(residual.shape)],
        [full(block)] * 4,
        [shaped(*block)] * 4,
        "ffn_down",
        scratch=[pltpu.VMEM((length, width), BF16)],
        needs=needs,
        me=places,
    )


def halves_kernel(blocks, width, starts, *refs):
    sources, outs, turned = refs[:blocks], refs[blocks : 3 * blocks], refs[3 * blocks]
    for n in range(blocks):
        source, keep, give = sources[n], outs[2 * n], outs[2 * n + 1]
        columns, each = source.shape[1], width[n]
        for c in range(0, columns, 256):
            turned[c : c + 256, :] = source[:, c : c + 256].T
        for which, out in enumerate((keep, give)):
            for k in range(8):
                first = pl.multiple_of(starts[8 * which + k] * each, 16)
                out[each * k : each * k + each, :] = turned[pl.ds(first, each), :]


def halves(starts, values, needs):
    length = values[0].shape[0]
    widths = [item.shape[1] // 16 for item in values]
    shapes = [(8 * w, length) for w in widths for _ in range(2)]
    return call(
        functools.partial(halves_kernel, len(values), widths),
        tuple(values),
        [full(item.shape) for item in values],
        [full(s) for s in shapes],
        [shaped(*s) for s in shapes],
        "halves",
        scratch=[pltpu.VMEM((max(item.shape[1] for item in values), length), BF16)],
        needs=needs,
        me=starts,
    )


ORDER = (2, 1, 3, 0)


def ffn_grads_kernel(in_keep, in_got, cot_keep, cot_got, *refs):
    ours, theirs, outs = refs[:3], refs[3:6], refs[6:]
    units = outs[0].shape[1] // 3

    def block(*parts):
        for n, (keep, got) in enumerate(((in_keep, in_got), (in_keep, in_got), (cot_keep, cot_got))):
            total = dot(keep[...], ours[n][...]) + dot(got[...], theirs[n][...])
            total = total[:, :units].astype(BF16)
            first = 0
            for out in parts:
                count = out.shape[0]
                out[:, units * n : units * n + units] = total[first : first + count]
                first += count

    for s, parts in enumerate((outs[:2], outs[2:3], outs[3:4], outs[4:])):
        pl.when(pl.program_id(0) == s)(functools.partial(block, *parts))


def ffn_grads(in_keep, in_got, cot_keep, cot_got, ours, theirs, units, needs):
    length, wide = ours[0].shape
    rows = in_keep.shape[0] // 4

    def index(i):
        return (jnp.where(i == 0, 2, jnp.where(i == 1, 1, jnp.where(i == 2, 3, 0))), 0)

    left = pl.BlockSpec((rows, length), index)
    out = (rows, 3 * units)
    outs = [(rows // 2, 3 * units)] * 2 + [out] * 3
    return call(
        ffn_grads_kernel,
        (in_keep, in_got, cot_keep, cot_got, *ours, *theirs),
        [left] * 4 + [full((length, wide))] * 6,
        [full(s) for s in outs],
        [shaped(*s) for s in outs],
        "ffn_grads",
        grid=(4,),
        needs=needs,
    )


def attn_grads_kernel(widths, *refs):
    keeps, gots, outs = refs[:3], refs[3:6], refs[10:]
    wide = outs[0].shape[1]
    ours, theirs = (
        (heads, both.at[:, :wide], both.at[:, wide:]) for heads, both in (refs[6:8], refs[8:10])
    )
    rows = sum(widths)
    for out, k in zip(outs, ORDER):
        first = 0
        for n, each in enumerate(widths):
            part = slice(2 * each * k, 2 * each * k + 2 * each)
            total = dot(keeps[n][part, :], ours[n][...]) + dot(gots[n][part, :], theirs[n][...])
            total = total.astype(BF16)
            out[first : first + each, :] = total[:each]
            out[rows + first : rows + first + each, :] = total[each:]
            first += each


def attn_grads(keeps, gots, ours, theirs, needs):
    widths = [item.shape[0] // 8 for item in keeps]
    rows, wide = sum(widths), ours[0].shape[1]
    args = (*keeps, *gots, *ours, *theirs)
    outs = [(2 * rows, wide)] * 4
    return call(
        functools.partial(attn_grads_kernel, widths),
        args,
        [full(item.shape) for item in args],
        [full(s) for s in outs],
        [shaped(*s) for s in outs],
        "attn_grads",
        needs=needs,
    )


UP = [(i, (i + 1) % 4) for i in range(4)]
DOWN = [(i, (i + 3) % 4) for i in range(4)]
ACROSS = [(i, (i + 2) % 4) for i in range(4)]


def relay_kernel(up, from_below, down, from_above, up_out, down_out):
    @pl.when(pl.program_id(0) == 0)
    def _():
        up_out[...] = (up[...].astype(F32) + from_below[...].astype(F32)).astype(BF16)
        down_out[...] = down[...]

    @pl.when(pl.program_id(0) == 1)
    def _():
        up_out[...] = up[...]
        down_out[...] = (down[...].astype(F32) + from_above[...].astype(F32)).astype(BF16)


def relay(up, from_below, down, from_above, needs):
    rows, width = from_below.shape
    half = pl.BlockSpec((rows, width), lambda i, *_: (i, 0))
    return call(
        relay_kernel,
        (up, from_below, down, from_above),
        [half, full((rows, width)), half, full((rows, width))],
        [half, half],
        [shaped(2 * rows, width)] * 2,
        "relay",
        grid=(2,),
        needs=needs,
    )


def add_chips_kernel(*refs):
    ins, keep, give = refs[:-2], refs[-2], refs[-1]
    count = len(ins) // 2
    keep[...] = sum(item[...].astype(F32) for item in ins[:count])
    give[...] = sum(item[...].astype(F32) for item in ins[count:]).astype(BF16)


def add_chips(items, needs):
    rows, width = items[0].shape[0] // 2, items[0].shape[1]
    step = rows // 2 if rows % 32 == 0 and (rows // 2) % 16 == 0 else rows
    count = rows // step
    mine = pl.BlockSpec((step, width), lambda i, *_: (i, 0))
    other = pl.BlockSpec((step, width), lambda i, *_: (i + count, 0))
    return call(
        add_chips_kernel,
        (*items, *items),
        [mine] * len(items) + [other] * len(items),
        [mine, mine],
        [shaped(rows, width, dtype=F32), shaped(rows, width)],
        "add_chips",
        grid=(count,),
        needs=needs,
    )


def add_all_kernel(*refs):
    refs[-1][...] = sum(item[...].astype(F32) for item in refs[:-1]).astype(BF16)


def add_all(items, needs):
    rows, width = items[0].shape
    half = pl.BlockSpec((rows // 2, width), lambda i, *_: (i, 0))
    return call(
        add_all_kernel,
        tuple(items),
        [half] * len(items),
        [half],
        [shaped(rows, width)],
        "add_all",
        grid=(2,),
        needs=needs,
        limit=58,
    )


def over_z(blocks):
    return [lax.ppermute(blocks[k], "z", [(i, i ^ k) for i in range(4)]) for k in (1, 2, 3)]


def assemble_kernel(places, own, above, across, below, out, sems):
    rows = own.shape[0]
    copies = [
        pltpu.make_async_copy(
            item, out.at[pl.ds(pl.multiple_of(places[k] * rows, rows), rows), :], sems.at[k]
        )
        for k, item in enumerate((own, above, across, below))
    ]
    for copy in copies:
        copy.start()
    for copy in copies:
        copy.wait()


def assemble(places, blocks, needs):
    rows, width = blocks[0].shape
    return call(
        assemble_kernel,
        tuple(blocks),
        [HBM] * 4,
        [HBM],
        [shaped(4 * rows, width)],
        "assemble",
        scratch=[pltpu.SemaphoreType.DMA((4,))],
        needs=needs,
        me=places,
    )[0][0]


def over_cores(values):
    return lax.ppermute(values, "core", SWAP)


def latents_back_kernel(
    me, got, latents, query_gain, latent_gain, keep, low, high, many, own, gain_part, turns, sems
):
    rows = own.shape[0]
    here = pl.ds(pl.multiple_of(me[0] * rows, rows), rows)
    copies = [
        pltpu.make_async_copy(table.at[here, :], turns.at[n], sems.at[n])
        for n, table in enumerate((keep, low, high))
    ]
    for copy in copies:
        copy.start()
    total = add_up(got)
    for copy in copies:
        copy.wait()

    def back(lanes, gain):
        upstream, values = total[:, lanes], latents[:, lanes]
        factor = root(values)
        normed = values * factor
        gain_part[:, lanes] = jnp.sum(upstream * normed, axis=0, keepdims=True)
        return norm_back(upstream, normed, factor, row(gain)).astype(BF16)

    own[:, :QR] = back(slice(0, QR), query_gain)
    own[:, QR:LAT] = back(slice(QR, LAT), latent_gain)
    own[:, LAT:] = turn(total[:, LAT:], turns[0], turns[1], turns[2], back=True).astype(BF16)
    for k in range(8):
        many[k] = own[...]


def latents_back_of(me, got, latents, query_gain, latent_gain, tables, needs):
    rows = latents.shape[0]
    return call(
        latents_back_kernel,
        (got.reshape(8, rows, WIDE), latents, query_gain, latent_gain, *tables),
        [full((8, rows, WIDE)), full(latents.shape), full((QR,)), full((KVR,)), HBM, HBM, HBM],
        [full((8, rows, WIDE)), full((rows, WIDE)), full((1, LAT))],
        [shaped(8, rows, WIDE), shaped(rows, WIDE), shaped(1, LAT, dtype=F32)],
        "latents_back",
        scratch=[
            pltpu.VMEM((3, rows, 128), F32),
            pltpu.SemaphoreType.DMA((3,)),
        ],
        needs=needs,
        me=me,
        limit=24,
    )


def first_back_of(raw_back, query_down, latent_down, rope_down):
    rope_down[...] = jnp.zeros_like(rope_down)
    rope_down[64:96, :] = latent_down[KVR:, :]
    return (
        dot(raw_back[:, :QR], query_down[...], NT)
        + dot(raw_back[:, QR:LAT], latent_down[:KVR, :])
        + dot(raw_back[:, LAT:], rope_down[...])
    )


def tokens_back_kernel(
    raw_back, tokens, attention_back, query_down, latent_down, gain, tokens_grad, rope_down
):
    first_back = first_back_of(raw_back, query_down, latent_down, rope_down)
    values = tokens[...].astype(F32)
    factor = root(values)
    tokens_grad[...] = attention_back[...].astype(F32) + norm_back(
        first_back, values * factor, factor, row(gain)
    )


def tokens_back_of(raw_back, tokens, attention_back, query_down, latent_down, gain, needs):
    length, width = tokens.shape

    def rows(columns):
        return pl.BlockSpec((TILE, columns), lambda i, *_: (i, 0))

    return call(
        tokens_back_kernel,
        (raw_back, tokens, attention_back, query_down, latent_down.T, gain),
        [
            rows(WIDE),
            rows(width),
            rows(width),
            full(query_down.shape),
            full(latent_down.shape[::-1]),
            full((width,)),
        ],
        [rows(width)],
        [shaped(length, width, dtype=F32)],
        "tokens_back",
        grid=(length // TILE,),
        scratch=[pltpu.VMEM((128, width), BF16)],
        needs=needs,
    )


def finish_ffn_kernel(keep, got, gate, up, down):
    units = gate.shape[1]
    for n, out in enumerate((gate, up, down)):
        lanes = slice(units * n, units * n + units)
        out[...] = keep[:, lanes] + got[:, lanes].astype(F32)


def finish_ffn(keep, got, needs):
    rows, width = keep.shape
    out = (rows, width // 3)
    return call(
        finish_ffn_kernel,
        (keep, got),
        [full(keep.shape), full(got.shape)],
        [full(out)] * 3,
        [shaped(*out, dtype=F32)] * 3,
        "finish_ffn",
        needs=needs,
    )


def finish_attn_kernel(heads, keep, got, out_grad, query_grad, latent_grad):
    total = keep[...] + got[...].astype(F32)
    for h in range(heads):
        lanes = slice(128 * h, 128 * h + 128)
        out_grad[:, 64 * h : 64 * h + 64] = total[:160, 128 * h + 64 : 128 * h + 128]
        query_grad[:, 96 * h : 96 * h + 96] = total[160:208, 128 * h : 128 * h + 96]
    latent_grad[...] = total[208:224]


def finish_attn(keep, got, needs):
    heads = keep.shape[1] // 128
    outs = [(160, 64 * heads), (48, 96 * heads), (16, 128 * heads)]
    return call(
        functools.partial(finish_attn_kernel, heads),
        (keep, got),
        [full(keep.shape), full(got.shape)],
        [full(s) for s in outs],
        [shaped(*s, dtype=F32) for s in outs],
        "finish_attn",
        needs=needs,
    )


GAINS = ((0, 160), (160, 48), (208, 16))


def down_parts_kernel(own_in, raw_back, gains, out):
    total = dot(own_in[...], raw_back[...]).astype(BF16)
    for d in range(16):
        out[d, :20, :] = total[20 * d : 20 * d + 20]
        out[d, 20:, :] = jnp.zeros((4, WIDE), BF16)
        out[d, 20:21, :] = gains[d : d + 1, :]


def down_parts(own_in, raw_back, gains, needs):
    args = (own_in, raw_back, gains)
    return call(
        down_parts_kernel,
        args,
        [full(item.shape) for item in args],
        [full((16, 24, WIDE))],
        [shaped(16, 24, WIDE)],
        "down_parts",
        needs=needs,
        limit=24,
    )


def sum_copies_kernel(got, many):
    total = got[0].astype(F32)
    for d in range(1, 16):
        total = total + got[d].astype(F32)
    for k in range(8):
        many[k] = total.astype(BF16)


def sum_copies(got, needs):
    return call(
        sum_copies_kernel,
        (got,),
        [full(got.shape)],
        [full((8, 24, WIDE))],
        [shaped(8, 24, WIDE)],
        "sum_copies",
        needs=needs,
        limit=24,
    )


def finish_down_kernel(
    block, everyone, query_down, latent_down, gain, query_grad, latent_grad, first, *rest
):
    *gains, query_rows, sems = rest
    rows = query_grad.shape[0]
    here = pl.ds(pl.multiple_of(block[0] * rows, 32), rows)
    copy = pltpu.make_async_copy(query_down.at[here, :], query_rows, sems)
    copy.start()
    for t in range(8):
        values = everyone[t].astype(F32)
        query_grad[20 * t : 20 * t + 20, :] = values[:20, :QR]
        latent_grad[20 * t : 20 * t + 20, :KVR] = values[:20, QR:LAT]
        latent_grad[20 * t : 20 * t + 20, KVR:] = values[:20, LAT + 64 : LAT + 96]
    total = sum(everyone[t, 16:24, :].astype(F32) for t in range(8))[4:5, :]
    for out, (start, count) in zip(gains, GAINS):
        out[...] = total[:, start : start + count]
    copy.wait()


    def row_sums(values):
        ones = jnp.ones((8, values.shape[1]), F32)
        return lax.dot_general(
            ones, values, NT, precision=lax.Precision.HIGHEST, preferred_element_type=F32
        )[:1]

    of_query = row_sums(query_rows[...].astype(F32) * query_grad[...])
    of_latent = row_sums(latent_down[...].astype(F32) * latent_grad[...])
    first[...] = (of_query + of_latent) / gain[...]


def finish_down(block, everyone, query_down, latent_down, gain, needs):
    everyone = everyone.reshape(8, 24, WIDE)
    rows = query_down.shape[0] // 16
    start = block[0] * rows
    latent_rows = lax.dynamic_slice_in_dim(latent_down, start, rows, 0)
    gain_rows = lax.dynamic_slice_in_dim(gain, start, rows, 0)[None]
    outs = [(rows, QR), (rows, KVR + ROPE), (1, rows)] + [(1, count) for _, count in GAINS]
    return call(
        finish_down_kernel,
        (everyone, query_down, latent_rows, gain_rows),
        [full(everyone.shape), HBM, full(latent_rows.shape), full(gain_rows.shape)],
        [full(s) for s in outs],
        [shaped(*s, dtype=F32) for s in outs],
        "finish_down",
        scratch=[
            pltpu.VMEM((rows, QR), BF16),
            pltpu.SemaphoreType.DMA,
        ],
        needs=needs,
        me=block,
        limit=58,
    )[0]


def exchange(blocks):
    return lax.all_to_all(blocks.reshape(-1, blocks.shape[-1]), TP, 0, 0, tiled=True)


def on_device(
    tokens,
    first_gain,
    query_down,
    query_gain,
    query_up,
    latent_down,
    latent_gain,
    latent_up,
    out_weight,
    second_gain,
    gate_weight,
    up_weight,
    down_weight,
    cotangent,
):
    length = tokens.shape[0]
    me = lax.axis_index(TP).astype(jnp.int32).reshape(1)
    y, xl, core = lax.axis_index("y"), lax.axis_index("xl"), lax.axis_index("core")
    starts = jnp.stack(
        [
            ((y + k) % 4 * 2 + (xl ^ j)) * 2 + c
            for c in (core, 1 - core)
            for k in range(4)
            for j in range(2)
        ]
    ).astype(jnp.int32)
    places = jnp.stack([lax.axis_index("z") ^ k for k in range(4)] + [me[0]]).astype(jnp.int32)
    z_order = jnp.stack([(lax.axis_index("z") + k) % 4 for k in range(4)]).astype(jnp.int32)
    block = ((y * 2 + xl) * 2 + core).astype(jnp.int32).reshape(1)
    tables = rope_tables(length)

    gate_turned, up_turned = gate_weight.T, up_weight.T

    (
        first_in,
        latents,
        query_code,
        latent_code,
        queries,
        keyvals,
        rope_keys,
        heads_out,
        log_total,
        attn_partial,
    ), started = attend(
        me,
        tokens,
        first_gain,
        query_down,
        latent_down,
        query_gain,
        latent_gain,
        query_up,
        latent_up,
        out_weight,
        tables,
    )
    attn_got = exchange(attn_partial)

    (cot_keep, cot_give), picked = halves(starts, [cotangent], [started])
    inner_back = dot(cotangent, down_weight, NT)
    cot_got = over_cores(cot_give)

    (residual, second_many), _ = residual_of(
        me, attn_got, tokens, second_gain, [picked, cot_got]
    )
    second_in = exchange(second_many)

    turned_in = first_in.T.reshape(16, 8, 20, length)
    own_in = lax.dynamic_slice_in_dim(turned_in, me[0], 1, 1).reshape(320, length)
    (code_keep, code_give, lat_keep, lat_give), picked = halves(
        starts, [query_code, latent_code], [residual]
    )
    code_got, lat_got = over_cores(code_give), over_cores(lat_give)
    heads_got = over_cores(heads_out)

    (gate_back, up_back, inner, back_partial), done = ffn(
        second_in, gate_turned, up_turned, inner_back, [picked, own_in, code_got, lat_got, heads_got]
    )
    back_got = exchange(back_partial)

    ours = (gate_back, up_back, inner)
    theirs = [over_cores(item) for item in ours]
    (in_keep, in_give), _ = halves(starts, [second_in], [done])
    in_got = over_cores(in_give)
    (far_up, far_down, ffn_up, ffn_down_way, ffn_own), done = ffn_grads(in_keep, in_got, cot_keep, cot_got, ours, theirs, gate_weight.shape[1], [])
    below, above = lax.ppermute(far_up, "y", UP), lax.ppermute(far_down, "y", DOWN)

    (back_many, second_gain_part), done = residual_back_of(
        me, back_got, residual, cotangent, second_gain, [done]
    )
    attention_back = exchange(back_many)
    mixed_blocks, done = ffn_down(places, inner, down_weight, residual, [done])
    mixed_got = over_z(mixed_blocks)
    (ffn_up, ffn_down_way), done = relay(ffn_up, below, ffn_down_way, above, [done])
    below, above = lax.ppermute(ffn_up, "y", UP), lax.ppermute(ffn_down_way, "y", DOWN)

    (both_back, latents_partial), back_done = attend_back(
        attention_back,
        out_weight,
        queries,
        keyvals,
        rope_keys,
        log_total,
        query_up,
        latent_up,
        tables,
        [done],
    )
    latents_got = exchange(latents_partial)

    (out_keep, out_give), picked = halves(starts, [attention_back], [back_done])
    (out_keep, out_give), done = halves(
        starts, [attention_back], [back_done, below, above, *mixed_got]
    )
    (mixed_part,), done = add_all([mixed_blocks[0], *mixed_got], [done])
    mixed_other = lax.ppermute(mixed_part, "xh", SWAP)

    (raw_many, own_raw, latent_gain_parts), done = latents_back_of(
        me, latents_got, latents, query_gain, latent_gain, tables, [done]
    )
    raw_back = exchange(raw_many)

    out_got, both_got = over_cores(out_give), over_cores(both_back)
    (attn_across, attn_up, attn_down, attn_own), done = attn_grads(
        (out_keep, code_keep, lat_keep),
        (out_got, code_got, lat_got),
        (heads_out, both_back),
        (heads_got, both_got),
        [done],
    )
    attn_got = [
        lax.ppermute(attn_across, "y", ACROSS),
        lax.ppermute(attn_up, "y", UP),
        lax.ppermute(attn_down, "y", DOWN),
    ]
    gains = jnp.concatenate(
        [
            second_gain_part.reshape(16, -1),
            latent_gain_parts[0, :QR].reshape(16, -1),
            latent_gain_parts[0, QR:].reshape(16, -1),
        ],
        axis=1,
    ).astype(BF16)
    gains = jnp.pad(gains, ((0, 0), (0, WIDE - gains.shape[1])))
    (ffn_keep, ffn_give), done = add_chips([ffn_own, below, above], [done])
    ffn_got = lax.ppermute(ffn_give, "xl", SWAP)
    (parts,), done = down_parts(own_in, raw_back, gains, [done, attn_got[1], attn_got[2]])
    parts_got = lax.all_to_all(parts, DP, 0, 0, tiled=True)

    (mixed_part,), done = add_all([mixed_part, mixed_other], [done])
    from_above, across, from_below = (
        lax.ppermute(mixed_part, "z", way) for way in (DOWN, ACROSS, UP)
    )
    (tokens_grad,), done = tokens_back_of(
        raw_back, tokens, attention_back, query_down, latent_down, first_gain, [done]
    )
    (many,), summed = sum_copies(parts_got, [done])
    everyone = exchange(many)

    (attn_keep, attn_give), done = add_chips([attn_own, *attn_got], [summed])
    attn_other = lax.ppermute(attn_give, "xl", SWAP)
    (gate_weight_grad, up_weight_grad, down_weight_grad), done = finish_ffn(
        ffn_keep, ffn_got, [done]
    )
    (out_weight_grad, query_up_grad, latent_up_grad), done = finish_attn(
        attn_keep, attn_other, [done]
    )
    (
        query_down_grad,
        latent_down_grad,
        first_gain_grad,
        second_gain_grad,
        query_gain_grad,
        latent_gain_grad,
    ) = finish_down(block, everyone, query_down, latent_down, first_gain, [])

    mixed = assemble(
        z_order, [mixed_part, from_above, across, from_below], [done]
    )

    return (
        mixed,
        tokens_grad,
        first_gain_grad[0],
        query_down_grad,
        query_gain_grad[0],
        query_up_grad,
        latent_down_grad,
        latent_gain_grad[0],
        latent_up_grad,
        out_weight_grad.T,
        second_gain_grad[0],
        gate_weight_grad,
        up_weight_grad,
        down_weight_grad.T,
    )


def solution(mesh):
    grid = Mesh(mesh.devices.reshape(4, 2, 2, 2, 4), ("y", "xl", "core", "xh", "z"))
    in_specs = (
        P(DP, None),
        P(),
        P(),
        P(),
        P(None, TP),
        P(),
        P(),
        P(None, TP),
        P(TP, None),
        P(),
        P(None, TP),
        P(None, TP),
        P(TP, None),
        P(DP, None),
    )
    out_specs = (
        P(DP, None),
        P(DP, None),
        P(DP),
        P(DP, None),
        P(DP),
        P(DP, TP),
        P(DP, None),
        P(DP),
        P(DP, TP),
        P(TP, DP),
        P(DP),
        P(DP, TP),
        P(DP, TP),
        P(TP, DP),
    )
    return jax.shard_map(
        on_device, mesh=grid, in_specs=in_specs, out_specs=out_specs, check_vma=False
    )
```

```python
import functools

import jax
import jax.numpy as jnp
import numpy as np
from jax import lax
from jax.experimental import pallas as pl
from jax.experimental.pallas import tpu as pltpu
from jax.sharding import Mesh, PartitionSpec as P

NOPE = 64
ROPE = 32
DV = 64
KVR = 256
QR = 768
LAT = QR + KVR
WIDE = LAT + 128

EPS = 1e-05
BASE = 10000.0
SCALE = (NOPE + ROPE) ** (-0.5)

DP = ("y", "xl", "core")
TP = ("xh", "z")
SWAP = [(0, 1), (1, 0)]
F32 = jnp.float32
BF16 = jnp.bfloat16
NT = (((1,), (1,)), ((), ()))
TN = (((0,), (0,)), ((), ()))
NN = (((1,), (0,)), ((), ()))
TILE = 256


def dot(left, right, dims=NN):
    return lax.dot_general(left, right, dims, preferred_element_type=F32)


def params(limit=56):
    return pltpu.CompilerParams(vmem_limit_bytes=limit * 2**20)


HBM = pl.BlockSpec(memory_space=pltpu.HBM)


def call(kernel, args, in_specs, out_specs, out_shape, name, grid=(1,), scratch=(), needs=(), me=None, limit=60, near=()):
    args = [
        item if n in near else pltpu.with_memory_space_constraint(item, pltpu.HBM)
        for n, item in enumerate(args)
    ]
    needs = [pltpu.with_memory_space_constraint(item, pltpu.HBM) for item in needs]
    first = 0 if me is None else 1
    n_in, n_out = len(args), len(out_shape)

    def body(*refs):
        ins = refs[: first + n_in]
        rest = refs[first + n_in + len(needs) :]
        mark = rest[n_out]

        @pl.when(pl.program_id(0) == 0)
        def _():
            mark[...] = jnp.zeros_like(mark)

        kernel(*ins, *rest[:n_out], *rest[n_out + 1 :])

    *outs, mark = pl.pallas_call(
        body,
        grid_spec=pltpu.PrefetchScalarGridSpec(
            num_scalar_prefetch=first,
            grid=grid,
            in_specs=list(in_specs) + [HBM] * len(needs),
            out_specs=list(out_specs) + [full((8, 128))],
            scratch_shapes=list(scratch),
        ),
        out_shape=list(out_shape) + [shaped(8, 128, dtype=F32)],
        compiler_params=params(limit),
        cost_estimate=pl.CostEstimate(flops=1, bytes_accessed=1, transcendentals=0),
        name=name,
    )(*(() if me is None else (me,)), *args, *needs)
    return outs, mark


def shaped(*shape, dtype=BF16):
    return pltpu.HBM(shape, dtype)


def full(shape):
    return pl.BlockSpec(shape, lambda *_: (0,) * len(shape))


def rope_tables(length):
    half = ROPE // 2
    rates = np.exp(np.arange(half, dtype=np.float32) * np.float32(-2.0 * np.log(BASE) / ROPE))
    angles = np.arange(length, dtype=np.float32)[:, None] * rates.astype(np.float32)[None, :]
    cosine, sine = np.cos(angles), np.sin(angles)
    keep = np.zeros((length, 128), np.float32)
    keep[:, :NOPE] = 1.0
    keep[:, 64:80] = cosine
    keep[:, 80:96] = cosine
    low = np.zeros((length, 128), np.float32)
    low[:, 64:80] = -sine
    high = np.zeros((length, 128), np.float32)
    high[:, 80:96] = sine
    return jnp.asarray(keep), jnp.asarray(low), jnp.asarray(high)


def turn(values, keep, low, high, back=False):
    moved = pltpu.roll(values, 112, 1) * low + pltpu.roll(values, 16, 1) * high
    return values * keep - moved if back else values * keep + moved


def root(values):
    return lax.rsqrt(jnp.mean(values * values, axis=-1, keepdims=True) + EPS)


def norm_back(upstream, normed, factor, gain):
    scaled = upstream * gain
    return factor * (scaled - normed * jnp.mean(scaled * normed, axis=-1, keepdims=True))


def spread_out_weight(weight_ref, spread_ref, heads):
    spread_ref[...] = jnp.zeros_like(spread_ref)
    for h in range(heads):
        spread_ref[128 * h + 64 : 128 * h + 128, :] = weight_ref[64 * h : 64 * h + 64, :]


def spread_query_up(weight_ref, spread_ref, heads):
    spread_ref[...] = jnp.zeros_like(spread_ref)
    for h in range(heads):
        spread_ref[128 * h : 128 * h + 96, :] = weight_ref[96 * h : 96 * h + 96, :]


def row(ref):
    return ref[...].reshape(1, -1)


def low_lanes(shape):
    return lax.broadcasted_iota(jnp.int32, shape, 1) < NOPE


def causal(keys, queries, first_query):
    key_ids = lax.broadcasted_iota(jnp.int32, (keys, queries), 0)
    query_ids = lax.broadcasted_iota(jnp.int32, (keys, queries), 1) + first_query
    return key_ids <= query_ids


def attend_kernel(
    heads,
    me,
    tokens,
    first_gain,
    query_down,
    latent_down,
    query_gain,
    latent_gain,
    query_up,
    latent_up,
    out_weight,
    keep,
    low,
    high,
    first_in,
    latents,
    query_code,
    latent_code,
    queries,
    keyvals,
    rope_keys,
    heads_out,
    log_total,
    partial,
    raw_latents,
    spread,
    spread_up,
    rope_down,
    kv_all,
    rope_all,
):
    step = pl.program_id(0)

    @pl.when(step == 0)
    def _():
        spread_out_weight(out_weight, spread, heads)
        spread_query_up(query_up, spread_up, heads)
        rope_down[...] = jnp.zeros_like(rope_down)
        rope_down[64:96, :] = latent_down[KVR:, :]

    def rows_of(index, carry):
        rows = pl.ds(pl.multiple_of(index * 32, 32), 32)
        values = tokens[rows, :].astype(F32)
        first_in[rows, :] = (values * root(values) * row(first_gain)).astype(BF16)
        return carry

    lax.fori_loop(0, TILE // 32, rows_of, 0)
    taken = first_in[...]
    query_latent = dot(taken, query_down[...])
    raw_latents[:, :QR] = query_latent
    code = (query_latent * root(query_latent) * row(query_gain)).astype(BF16)
    query_code[...] = code
    latent = dot(taken, latent_down[:KVR, :], NT)
    raw_latents[:, QR:] = latent
    count = latents.shape[0]
    own = me[0] * count

    @pl.when(own // TILE == step)
    def _():
        latents[...] = raw_latents[pl.ds(pl.multiple_of(own % TILE, count), count), :]

    lcode = (latent * root(latent) * row(latent_gain)).astype(BF16)
    latent_code[...] = lcode
    tables = keep[...], low[...], high[...]
    rope = turn(dot(taken, rope_down[...], NT), *tables).astype(BF16)
    rope_keys[...] = rope
    here = pl.ds(pl.multiple_of(step * TILE, TILE), TILE)
    rope_all[here, :] = rope
    kv = dot(lcode, latent_up[...]).astype(BF16)
    keyvals[...] = kv
    kv_all[here, :] = kv
    raw = dot(code, spread_up[...], NT)
    for h in range(heads):
        lanes = slice(128 * h, 128 * h + 128)
        queries[:, lanes] = turn(raw[:, lanes], *tables).astype(BF16)

    def tile(index):
        keys = TILE * (index + 1)
        for h in range(heads):
            lanes = slice(128 * h, 128 * h + 128)
            kv_h = kv_all[:keys, lanes]
            key = jnp.where(low_lanes((keys, 128)), kv_h, rope_all[:keys, :])
            scores = dot(key, queries[:, lanes], NT) * SCALE
            scores = jnp.where(causal(keys, TILE, TILE * index), scores, -1e30)
            top = jnp.max(scores, axis=0, keepdims=True)
            weights = jnp.exp(scores - top)
            total = jnp.sum(weights, axis=0, keepdims=True)
            log_total[h : h + 1, :] = top + jnp.log(total)
            probs = (weights * (1.0 / total)).astype(BF16)
            heads_out[:, lanes] = dot(probs, kv_h, TN).astype(BF16)

    for index in range(2):
        pl.when(step == index)(functools.partial(tile, index))
    partial[...] = dot(heads_out[...], spread[...]).astype(BF16)


def attend(me, tokens, first_gain, query_down, latent_down, query_gain, latent_gain, query_up, latent_up, out_weight, tables):
    latent_down, query_up = latent_down.T, query_up.T
    length, width = tokens.shape
    heads = out_weight.shape[0] // DV
    wide = 128 * heads

    def rows(columns):
        return pl.BlockSpec((TILE, columns), lambda i, *_: (i, 0))

    return call(
        functools.partial(attend_kernel, heads),
        (tokens, first_gain, query_down, latent_down, query_gain, latent_gain, query_up, latent_up, out_weight, *tables),
        [
            rows(width),
            full((width,)),
            full(query_down.shape),
            full(latent_down.shape),
            full((QR,)),
            full((KVR,)),
            full(query_up.shape),
            full(latent_up.shape),
            full(out_weight.shape),
            rows(128),
            rows(128),
            rows(128),
        ],
        [
            rows(width),
            full((length // 8, LAT)),
            rows(QR),
            rows(KVR),
            rows(wide),
            rows(wide),
            rows(128),
            rows(wide),
            pl.BlockSpec((8, TILE), lambda i, *_: (0, i)),
            rows(width),
        ],
        [
            shaped(length, width),
            shaped(length // 8, LAT, dtype=F32),
            shaped(length, QR),
            shaped(length, KVR),
            shaped(length, wide),
            shaped(length, wide),
            shaped(length, 128),
            shaped(length, wide),
            shaped(8, length, dtype=F32),
            shaped(length, width),
        ],
        "attend",
        grid=(length // TILE,),
        me=me,
        scratch=[
            pltpu.VMEM((TILE, LAT), F32),
            pltpu.VMEM((wide, width), BF16),
            pltpu.VMEM((wide, QR), BF16),
            pltpu.VMEM((128, width), BF16),
            pltpu.VMEM((length, wide), BF16),
            pltpu.VMEM((length, 128), BF16),
        ],
    )


def attend_back_kernel(
    heads,
    attention_back,
    out_weight,
    queries,
    keyvals,
    rope_keys,
    log_total,
    query_up,
    latent_up,
    keep,
    low,
    high,
    both_back,
    partial,
    spread,
    spread_up,
    kv_grad,
    rope_grad,
    code_grad,
):
    step = pl.program_id(0)

    @pl.when(step == 0)
    def _():
        spread_out_weight(out_weight, spread, heads)
        spread_query_up(query_up, spread_up, heads)
        kv_grad[...] = jnp.zeros_like(kv_grad)
        rope_grad[...] = jnp.zeros_like(rope_grad)

    heads_back = dot(attention_back[...], spread[...], NT).astype(BF16)
    tables = keep[...], low[...], high[...]

    def tile(index):
        keys = TILE * (index + 1)
        low_part = low_lanes((keys, 128))
        for h in range(heads):
            lanes = slice(128 * h, 128 * h + 128)
            kv_h = keyvals[:keys, lanes]
            key = jnp.where(low_part, kv_h, rope_keys[:keys, :])
            query = queries[:, lanes]
            back = heads_back[:, lanes]
            scores = dot(key, query, NT) * SCALE
            probs = jnp.exp(scores - log_total[h : h + 1, :])
            probs = jnp.where(causal(keys, TILE, TILE * index), probs, 0.0)
            prob_back = dot(kv_h, back, NT)
            mean = jnp.sum(probs * prob_back, axis=0, keepdims=True)
            score_back = (probs * (prob_back - mean)).astype(BF16)
            of_values = dot(probs.astype(BF16), back)
            of_keys = dot(score_back, query) * SCALE
            kv_grad[:keys, lanes] += of_values + jnp.where(low_part, of_keys, 0.0)
            rope_grad[:keys, :] += jnp.where(low_part, 0.0, of_keys)
            of_query = dot(score_back, key, TN) * SCALE
            both_back[here, lanes] = turn(of_query, *tables, back=True).astype(BF16)

    wide = 128 * heads
    here = pl.ds(pl.multiple_of(step * TILE, TILE), TILE)
    for index in range(2):
        pl.when(step == index)(functools.partial(tile, index))
    code_grad[here, :] = dot(both_back[here, :wide], spread_up[...]).astype(BF16)

    @pl.when(step == 1)
    def _():
        kv = kv_grad[...].astype(BF16)
        both_back[:, wide:] = kv
        partial[:, :QR] = code_grad[...]
        partial[:, QR:LAT] = dot(kv, latent_up[...], NT).astype(BF16)
        partial[:, LAT:] = rope_grad[...].astype(BF16)


def attend_back(attention_back, out_weight, queries, keyvals, rope_keys, log_total, query_up, latent_up, tables, needs):
    query_up = query_up.T
    length, width = attention_back.shape
    heads = out_weight.shape[0] // DV
    wide = 128 * heads

    def rows(columns):
        return pl.BlockSpec((TILE, columns), lambda i, *_: (i, 0))

    return call(
        functools.partial(attend_back_kernel, heads),
        (attention_back, out_weight, queries, keyvals, rope_keys, log_total, query_up, latent_up, *tables),
        [
            rows(width),
            full(out_weight.shape),
            rows(wide),
            full((length, wide)),
            full((length, 128)),
            pl.BlockSpec((8, TILE), lambda i, *_: (0, i)),
            full(query_up.shape),
            full(latent_up.shape),
            rows(128),
            rows(128),
            rows(128),
        ],
        [full((length, 2 * wide)), full((length, WIDE))],
        [shaped(length, 2 * wide), shaped(length, WIDE)],
        "attend_back",
        grid=(length // TILE,),
        scratch=[
            pltpu.VMEM((wide, width), BF16),
            pltpu.VMEM((wide, QR), BF16),
            pltpu.VMEM((length, wide), F32),
            pltpu.VMEM((length, 128), F32),
            pltpu.VMEM((length, QR), BF16),
        ],
        needs=needs,
        limit=44,
        near=(0,),
    )


def add_up(got):
    total = got[0].astype(F32)
    for k in range(1, 8):
        total = total + got[k].astype(F32)
    return total


STEPS = 2


def residual_kernel(me, got, tokens, gain, residual, many):
    del me
    total = tokens[...].astype(F32) + add_up(got)
    residual[...] = total
    second_in = (total * root(total) * row(gain)).astype(BF16)
    for k in range(8):
        many[k] = second_in


def own_specs(rows, width):
    step = rows // STEPS
    return (
        pl.BlockSpec((8, step, width), lambda i, me: (0, i, 0)),
        pl.BlockSpec((step, width), lambda i, me: (i, 0)),
        pl.BlockSpec((step, width), lambda i, me: (me[0] * STEPS + i, 0)),
    )


def residual_of(me, got, tokens, gain, needs):
    width = tokens.shape[1]
    rows = tokens.shape[0] // 8
    eight, one, own = own_specs(rows, width)
    return call(
        residual_kernel,
        (got.reshape(8, rows, width), tokens, gain),
        [eight, own, full((width,))],
        [one, eight],
        [shaped(rows, width, dtype=F32), shaped(8, rows, width)],
        "residual",
        grid=(STEPS,),
        needs=needs,
        me=me,
        limit=24,
        near=(0,),
    )


def residual_back_kernel(me, got, residual, cotangent, gain, many, gain_part):
    del me
    second_back = add_up(got)
    values = residual[...]
    factor = root(values)
    normed = values * factor
    part = jnp.sum(second_back * normed, axis=0, keepdims=True)

    @pl.when(pl.program_id(0) == 0)
    def _():
        gain_part[...] = part

    @pl.when(pl.program_id(0) > 0)
    def _():
        gain_part[...] += part

    back = cotangent[...].astype(F32) + norm_back(second_back, normed, factor, row(gain))
    back = back.astype(BF16)
    for k in range(8):
        many[k] = back


def residual_back_of(me, got, residual, cotangent, gain, needs):
    rows, width = residual.shape
    eight, one, own = own_specs(rows, width)
    return call(
        residual_back_kernel,
        (got.reshape(8, rows, width), residual, cotangent, gain),
        [eight, one, own, full((width,))],
        [eight, full((1, width))],
        [shaped(8, rows, width), shaped(1, width, dtype=F32)],
        "residual_back",
        grid=(STEPS,),
        needs=needs,
        me=me,
        limit=24,
        near=(0,),
    )


def ffn_kernel(
    second_in, gate_weight, up_weight, inner_back, gate_back, up_back, inner, partial
):
    taken = second_in[...]
    gate = dot(taken, gate_weight[...], NT)
    up = dot(taken, up_weight[...], NT)
    sigma = 1.0 / (1.0 + jnp.exp(-gate))
    act = gate * sigma
    units = gate.shape[1]
    back = inner_back[...]
    of_gate = (back * up * sigma * (1.0 + gate * (1.0 - sigma))).astype(BF16)
    of_up = (back * act).astype(BF16)
    for out, values in ((gate_back, of_gate), (up_back, of_up), (inner, (act * up).astype(BF16))):
        out[:, :units] = values
        out[:, units:] = jnp.zeros((values.shape[0], out.shape[1] - units), BF16)
    partial[...] = (dot(of_gate, gate_weight[...]) + dot(of_up, up_weight[...])).astype(BF16)


def ffn(second_in, gate_weight, up_weight, inner_back, needs):
    length, width = second_in.shape
    units = gate_weight.shape[0]
    wide = -(-units // 128) * 128

    def rows(columns):
        return pl.BlockSpec((TILE, columns), lambda i, *_: (i, 0))

    return call(
        ffn_kernel,
        (second_in, gate_weight, up_weight, inner_back),
        [rows(width), full((units, width)), full((units, width)), rows(units)],
        [rows(wide), rows(wide), rows(wide), rows(width)],
        [shaped(length, wide)] * 3 + [shaped(length, width)],
        "ffn",
        grid=(length // TILE,),
        needs=needs,
        limit=44,
        near=(0,),
    )


def ffn_down_kernel(places, inner, down_weight, residual, *refs):
    outs, total = refs[:4], refs[4]
    for i in range(2):
        rows = slice(i * TILE, i * TILE + TILE)
        total[rows, :] = dot(inner[rows, : down_weight.shape[0]], down_weight[...]).astype(BF16)
    count = residual.shape[0]
    own = pl.ds(pl.multiple_of(places[4] * count, count), count)
    total[own, :] = (total[own, :].astype(F32) + residual[...]).astype(BF16)
    for k, out in enumerate(outs):
        rows = out.shape[0]
        out[...] = total[pl.ds(pl.multiple_of(places[k] * rows, rows), rows), :]


def ffn_down(places, inner, down_weight, residual, needs):
    length, width = inner.shape[0], down_weight.shape[1]
    block = (length // 4, width)
    return call(
        ffn_down_kernel,
        (inner, down_weight, residual),
        [full(inner.shape), full(down_weight.shape), full(residual.shape)],
        [full(block)] * 4,
        [shaped(*block)] * 4,
        "ffn_down",
        scratch=[pltpu.VMEM((length, width), BF16)],
        needs=needs,
        me=places,
    )


def halves_kernel(blocks, width, starts, *refs):
    sources, outs, turned = refs[:blocks], refs[blocks : 3 * blocks], refs[3 * blocks]
    for n in range(blocks):
        source, keep, give = sources[n], outs[2 * n], outs[2 * n + 1]
        columns, each = source.shape[1], width[n]
        for c in range(0, columns, 256):
            turned[c : c + 256, :] = source[:, c : c + 256].T
        for which, out in enumerate((keep, give)):
            for k in range(8):
                first = pl.multiple_of(starts[8 * which + k] * each, 16)
                out[each * k : each * k + each, :] = turned[pl.ds(first, each), :]


def halves(starts, values, needs):
    length = values[0].shape[0]
    widths = [item.shape[1] // 16 for item in values]
    shapes = [(8 * w, length) for w in widths for _ in range(2)]
    return call(
        functools.partial(halves_kernel, len(values), widths),
        tuple(values),
        [full(item.shape) for item in values],
        [full(s) for s in shapes],
        [shaped(*s) for s in shapes],
        "halves",
        scratch=[pltpu.VMEM((max(item.shape[1] for item in values), length), BF16)],
        needs=needs,
        me=starts,
        limit=24,
        near=(0,),
    )


ORDER = (2, 1, 3, 0)


def ffn_grads_kernel(in_keep, in_got, cot_keep, cot_got, *refs):
    ours, theirs, outs = refs[:3], refs[3:6], refs[6:]
    units = outs[0].shape[1] // 3

    def block(*parts):
        for n, (keep, got) in enumerate(((in_keep, in_got), (in_keep, in_got), (cot_keep, cot_got))):
            total = dot(keep[...], ours[n][...]) + dot(got[...], theirs[n][...])
            total = total[:, :units].astype(BF16)
            first = 0
            for out in parts:
                count = out.shape[0]
                out[:, units * n : units * n + units] = total[first : first + count]
                first += count

    for s, parts in enumerate((outs[:2], outs[2:3], outs[3:4], outs[4:])):
        pl.when(pl.program_id(0) == s)(functools.partial(block, *parts))


def ffn_grads(in_keep, in_got, cot_keep, cot_got, ours, theirs, units, needs):
    length, wide = ours[0].shape
    rows = in_keep.shape[0] // 4

    def index(i):
        return (jnp.where(i == 0, 2, jnp.where(i == 1, 1, jnp.where(i == 2, 3, 0))), 0)

    left = pl.BlockSpec((rows, length), index)
    out = (rows, 3 * units)
    outs = [(rows // 2, 3 * units)] * 2 + [out] * 3
    return call(
        ffn_grads_kernel,
        (in_keep, in_got, cot_keep, cot_got, *ours, *theirs),
        [left] * 4 + [full((length, wide))] * 6,
        [full(s) for s in outs],
        [shaped(*s) for s in outs],
        "ffn_grads",
        grid=(4,),
        needs=needs,
    )


def attn_grads_kernel(widths, *refs):
    keeps, gots, outs = refs[:3], refs[3:6], refs[10:]
    wide = outs[0].shape[1]
    ours, theirs = (
        (heads, both.at[:, :wide], both.at[:, wide:]) for heads, both in (refs[6:8], refs[8:10])
    )
    rows = sum(widths)
    for out, k in zip(outs, ORDER):
        first = 0
        for n, each in enumerate(widths):
            part = slice(2 * each * k, 2 * each * k + 2 * each)
            total = dot(keeps[n][part, :], ours[n][...]) + dot(gots[n][part, :], theirs[n][...])
            total = total.astype(BF16)
            out[first : first + each, :] = total[:each]
            out[rows + first : rows + first + each, :] = total[each:]
            first += each


def attn_grads(keeps, gots, ours, theirs, needs):
    widths = [item.shape[0] // 8 for item in keeps]
    rows, wide = sum(widths), ours[0].shape[1]
    args = (*keeps, *gots, *ours, *theirs)
    outs = [(2 * rows, wide)] * 4
    return call(
        functools.partial(attn_grads_kernel, widths),
        args,
        [full(item.shape) for item in args],
        [full(s) for s in outs],
        [shaped(*s) for s in outs],
        "attn_grads",
        needs=needs,
    )


UP = [(i, (i + 1) % 4) for i in range(4)]
DOWN = [(i, (i + 3) % 4) for i in range(4)]
ACROSS = [(i, (i + 2) % 4) for i in range(4)]


def relay_kernel(up, from_below, down, from_above, up_out, down_out):
    @pl.when(pl.program_id(0) == 0)
    def _():
        up_out[...] = (up[...].astype(F32) + from_below[...].astype(F32)).astype(BF16)
        down_out[...] = down[...]

    @pl.when(pl.program_id(0) == 1)
    def _():
        up_out[...] = up[...]
        down_out[...] = (down[...].astype(F32) + from_above[...].astype(F32)).astype(BF16)


def relay(up, from_below, down, from_above, needs):
    rows, width = from_below.shape
    half = pl.BlockSpec((rows, width), lambda i, *_: (i, 0))
    return call(
        relay_kernel,
        (up, from_below, down, from_above),
        [half, full((rows, width)), half, full((rows, width))],
        [half, half],
        [shaped(2 * rows, width)] * 2,
        "relay",
        grid=(2,),
        needs=needs,
    )


def add_chips_kernel(*refs):
    ins, keep, give = refs[:-2], refs[-2], refs[-1]
    count = len(ins) // 2
    keep[...] = sum(item[...].astype(F32) for item in ins[:count])
    give[...] = sum(item[...].astype(F32) for item in ins[count:]).astype(BF16)


def add_chips(items, needs):
    rows, width = items[0].shape[0] // 2, items[0].shape[1]
    step = rows // 2 if rows % 32 == 0 and (rows // 2) % 16 == 0 else rows
    count = rows // step
    mine = pl.BlockSpec((step, width), lambda i, *_: (i, 0))
    other = pl.BlockSpec((step, width), lambda i, *_: (i + count, 0))
    return call(
        add_chips_kernel,
        (*items, *items),
        [mine] * len(items) + [other] * len(items),
        [mine, mine],
        [shaped(rows, width, dtype=F32), shaped(rows, width)],
        "add_chips",
        grid=(count,),
        needs=needs,
    )


def add_all_kernel(*refs):
    refs[-1][...] = sum(item[...].astype(F32) for item in refs[:-1]).astype(BF16)


def add_all(items, needs):
    rows, width = items[0].shape
    half = pl.BlockSpec((rows // 2, width), lambda i, *_: (i, 0))
    return call(
        add_all_kernel,
        tuple(items),
        [half] * len(items),
        [half],
        [shaped(rows, width)],
        "add_all",
        grid=(2,),
        needs=needs,
        limit=58,
    )


def over_z(blocks):
    return [lax.ppermute(blocks[k], "z", [(i, i ^ k) for i in range(4)]) for k in (1, 2, 3)]


def assemble_kernel(places, *refs):
    del places
    for k in range(4):

        @pl.when(pl.program_id(0) == k)
        def _(k=k):
            refs[4][...] = refs[k][...]


def assemble(places, blocks, needs):
    rows, width = blocks[0].shape
    return call(
        assemble_kernel,
        tuple(blocks),
        [full(item.shape) for item in blocks],
        [pl.BlockSpec((rows, width), lambda i, places: (places[i], 0))],
        [shaped(4 * rows, width)],
        "assemble",
        grid=(4,),
        needs=needs,
        me=places,
    )[0][0]


def over_cores(values):
    return lax.ppermute(values, "core", SWAP)


def latents_back_kernel(
    me, got, latents, query_gain, latent_gain, keep, low, high, many, own, gain_part, turns, sems
):
    rows = own.shape[0]
    here = pl.ds(pl.multiple_of(me[0] * rows, rows), rows)
    copies = [
        pltpu.make_async_copy(table.at[here, :], turns.at[n], sems.at[n])
        for n, table in enumerate((keep, low, high))
    ]
    for copy in copies:
        copy.start()
    total = add_up(got)
    for copy in copies:
        copy.wait()

    def back(lanes, gain):
        upstream, values = total[:, lanes], latents[:, lanes]
        factor = root(values)
        normed = values * factor
        gain_part[:, lanes] = jnp.sum(upstream * normed, axis=0, keepdims=True)
        return norm_back(upstream, normed, factor, row(gain)).astype(BF16)

    own[:, :QR] = back(slice(0, QR), query_gain)
    own[:, QR:LAT] = back(slice(QR, LAT), latent_gain)
    own[:, LAT:] = turn(total[:, LAT:], turns[0], turns[1], turns[2], back=True).astype(BF16)
    for k in range(8):
        many[k] = own[...]


def latents_back_of(me, got, latents, query_gain, latent_gain, tables, needs):
    rows = latents.shape[0]
    return call(
        latents_back_kernel,
        (got.reshape(8, rows, WIDE), latents, query_gain, latent_gain, *tables),
        [full((8, rows, WIDE)), full(latents.shape), full((QR,)), full((KVR,)), HBM, HBM, HBM],
        [full((8, rows, WIDE)), full((rows, WIDE)), full((1, LAT))],
        [shaped(8, rows, WIDE), shaped(rows, WIDE), shaped(1, LAT, dtype=F32)],
        "latents_back",
        scratch=[
            pltpu.VMEM((3, rows, 128), F32),
            pltpu.SemaphoreType.DMA((3,)),
        ],
        needs=needs,
        me=me,
        limit=24,
        near=(0,),
    )


def first_back_of(raw_back, query_down, latent_down, rope_down):
    rope_down[...] = jnp.zeros_like(rope_down)
    rope_down[64:96, :] = latent_down[KVR:, :]
    return (
        dot(raw_back[:, :QR], query_down[...], NT)
        + dot(raw_back[:, QR:LAT], latent_down[:KVR, :])
        + dot(raw_back[:, LAT:], rope_down[...])
    )


def tokens_back_kernel(
    raw_back, tokens, attention_back, query_down, latent_down, gain, tokens_grad, rope_down
):
    first_back = first_back_of(raw_back, query_down, latent_down, rope_down)
    values = tokens[...].astype(F32)
    factor = root(values)
    tokens_grad[...] = attention_back[...].astype(F32) + norm_back(
        first_back, values * factor, factor, row(gain)
    )


def tokens_back_of(raw_back, tokens, attention_back, query_down, latent_down, gain, needs):
    length, width = tokens.shape

    def rows(columns):
        return pl.BlockSpec((TILE, columns), lambda i, *_: (i, 0))

    return call(
        tokens_back_kernel,
        (raw_back, tokens, attention_back, query_down, latent_down.T, gain),
        [
            rows(WIDE),
            rows(width),
            rows(width),
            full(query_down.shape),
            full(latent_down.shape[::-1]),
            full((width,)),
        ],
        [rows(width)],
        [shaped(length, width, dtype=F32)],
        "tokens_back",
        grid=(length // TILE,),
        scratch=[pltpu.VMEM((128, width), BF16)],
        needs=needs,
    )


def finish_ffn_kernel(keep, got, gate, up, down):
    units = gate.shape[1]
    for n, out in enumerate((gate, up, down)):
        lanes = slice(units * n, units * n + units)
        out[...] = keep[:, lanes] + got[:, lanes].astype(F32)


def finish_ffn(keep, got, needs):
    rows, width = keep.shape
    out = (rows, width // 3)
    return call(
        finish_ffn_kernel,
        (keep, got),
        [full(keep.shape), full(got.shape)],
        [full(out)] * 3,
        [shaped(*out, dtype=F32)] * 3,
        "finish_ffn",
        needs=needs,
    )


def finish_attn_kernel(heads, keep, got, out_grad, query_grad, latent_grad):
    total = keep[...] + got[...].astype(F32)
    for h in range(heads):
        lanes = slice(128 * h, 128 * h + 128)
        out_grad[:, 64 * h : 64 * h + 64] = total[:160, 128 * h + 64 : 128 * h + 128]
        query_grad[:, 96 * h : 96 * h + 96] = total[160:208, 128 * h : 128 * h + 96]
    latent_grad[...] = total[208:224]


def finish_attn(keep, got, needs):
    heads = keep.shape[1] // 128
    outs = [(160, 64 * heads), (48, 96 * heads), (16, 128 * heads)]
    return call(
        functools.partial(finish_attn_kernel, heads),
        (keep, got),
        [full(keep.shape), full(got.shape)],
        [full(s) for s in outs],
        [shaped(*s, dtype=F32) for s in outs],
        "finish_attn",
        needs=needs,
    )


GAINS = ((0, 160), (160, 48), (208, 16))


def down_parts_kernel(own_in, raw_back, gains, out):
    total = dot(own_in[...], raw_back[...]).astype(BF16)
    for d in range(16):
        out[d, :20, :] = total[20 * d : 20 * d + 20]
        out[d, 20:, :] = jnp.zeros((4, WIDE), BF16)
        out[d, 20:21, :] = gains[d : d + 1, :]


def down_parts(own_in, raw_back, gains, needs):
    args = (own_in, raw_back, gains)
    return call(
        down_parts_kernel,
        args,
        [full(item.shape) for item in args],
        [full((16, 24, WIDE))],
        [shaped(16, 24, WIDE)],
        "down_parts",
        needs=needs,
        limit=24,
    )


def sum_copies_kernel(got, many):
    total = got[0].astype(F32)
    for d in range(1, 16):
        total = total + got[d].astype(F32)
    for k in range(8):
        many[k] = total.astype(BF16)


def sum_copies(got, needs):
    return call(
        sum_copies_kernel,
        (got,),
        [full(got.shape)],
        [full((8, 24, WIDE))],
        [shaped(8, 24, WIDE)],
        "sum_copies",
        needs=needs,
        limit=24,
    )


def finish_down_kernel(
    block, everyone, query_down, latent_down, gain, query_grad, latent_grad, first, *rest
):
    *gains, query_rows, sems = rest
    rows = query_grad.shape[0]
    here = pl.ds(pl.multiple_of(block[0] * rows, 32), rows)
    copy = pltpu.make_async_copy(query_down.at[here, :], query_rows, sems)
    copy.start()
    for t in range(8):
        values = everyone[t].astype(F32)
        query_grad[20 * t : 20 * t + 20, :] = values[:20, :QR]
        latent_grad[20 * t : 20 * t + 20, :KVR] = values[:20, QR:LAT]
        latent_grad[20 * t : 20 * t + 20, KVR:] = values[:20, LAT + 64 : LAT + 96]
    total = sum(everyone[t, 16:24, :].astype(F32) for t in range(8))[4:5, :]
    for out, (start, count) in zip(gains, GAINS):
        out[...] = total[:, start : start + count]
    copy.wait()


    def row_sums(values):
        ones = jnp.ones((8, values.shape[1]), F32)
        return lax.dot_general(
            ones, values, NT, precision=lax.Precision.HIGHEST, preferred_element_type=F32
        )[:1]

    of_query = row_sums(query_rows[...].astype(F32) * query_grad[...])
    of_latent = row_sums(latent_down[...].astype(F32) * latent_grad[...])
    first[...] = (of_query + of_latent) / gain[...]


def finish_down(block, everyone, query_down, latent_down, gain, needs):
    everyone = everyone.reshape(8, 24, WIDE)
    rows = query_down.shape[0] // 16
    start = block[0] * rows
    latent_rows = lax.dynamic_slice_in_dim(latent_down, start, rows, 0)
    gain_rows = lax.dynamic_slice_in_dim(gain, start, rows, 0)[None]
    outs = [(rows, QR), (rows, KVR + ROPE), (1, rows)] + [(1, count) for _, count in GAINS]
    return call(
        finish_down_kernel,
        (everyone, query_down, latent_rows, gain_rows),
        [full(everyone.shape), HBM, full(latent_rows.shape), full(gain_rows.shape)],
        [full(s) for s in outs],
        [shaped(*s, dtype=F32) for s in outs],
        "finish_down",
        scratch=[
            pltpu.VMEM((rows, QR), BF16),
            pltpu.SemaphoreType.DMA,
        ],
        needs=needs,
        me=block,
        limit=58,
    )[0]


def exchange(blocks):
    return lax.all_to_all(blocks.reshape(-1, blocks.shape[-1]), TP, 0, 0, tiled=True)


def on_device(
    tokens,
    first_gain,
    query_down,
    query_gain,
    query_up,
    latent_down,
    latent_gain,
    latent_up,
    out_weight,
    second_gain,
    gate_weight,
    up_weight,
    down_weight,
    cotangent,
):
    length = tokens.shape[0]
    me = lax.axis_index(TP).astype(jnp.int32).reshape(1)
    y, xl, core = lax.axis_index("y"), lax.axis_index("xl"), lax.axis_index("core")
    starts = jnp.stack(
        [
            ((y + k) % 4 * 2 + (xl ^ j)) * 2 + c
            for c in (core, 1 - core)
            for k in range(4)
            for j in range(2)
        ]
    ).astype(jnp.int32)
    places = jnp.stack([lax.axis_index("z") ^ k for k in range(4)] + [me[0]]).astype(jnp.int32)
    z_order = jnp.stack([(lax.axis_index("z") + k) % 4 for k in range(4)]).astype(jnp.int32)
    block = ((y * 2 + xl) * 2 + core).astype(jnp.int32).reshape(1)
    tables = rope_tables(length)

    gate_turned, up_turned = gate_weight.T, up_weight.T

    (
        first_in,
        latents,
        query_code,
        latent_code,
        queries,
        keyvals,
        rope_keys,
        heads_out,
        log_total,
        attn_partial,
    ), started = attend(
        me,
        tokens,
        first_gain,
        query_down,
        latent_down,
        query_gain,
        latent_gain,
        query_up,
        latent_up,
        out_weight,
        tables,
    )
    attn_got = exchange(attn_partial)

    (cot_keep, cot_give), picked = halves(starts, [cotangent], [started])
    inner_back = dot(cotangent, down_weight, NT)
    cot_got = over_cores(cot_give)

    (residual, second_many), _ = residual_of(
        me, attn_got, tokens, second_gain, [picked, cot_got]
    )
    second_in = exchange(second_many)

    turned_in = first_in.T.reshape(16, 8, 20, length)
    own_in = lax.dynamic_slice_in_dim(turned_in, me[0], 1, 1).reshape(320, length)
    (code_keep, code_give, lat_keep, lat_give), picked = halves(
        starts, [query_code, latent_code], [residual]
    )
    code_got, lat_got = over_cores(code_give), over_cores(lat_give)
    heads_got = over_cores(heads_out)

    (gate_back, up_back, inner, back_partial), done = ffn(
        second_in, gate_turned, up_turned, inner_back, [picked, own_in, code_got, lat_got, heads_got]
    )
    back_got = exchange(back_partial)

    ours = (gate_back, up_back, inner)
    theirs = [over_cores(item) for item in ours]
    (in_keep, in_give), _ = halves(starts, [second_in], [done])
    in_got = over_cores(in_give)
    (far_up, far_down, ffn_up, ffn_down_way, ffn_own), done = ffn_grads(in_keep, in_got, cot_keep, cot_got, ours, theirs, gate_weight.shape[1], [])
    below, above = lax.ppermute(far_up, "y", UP), lax.ppermute(far_down, "y", DOWN)

    (back_many, second_gain_part), done = residual_back_of(
        me, back_got, residual, cotangent, second_gain, [done]
    )
    attention_back = exchange(back_many)
    mixed_blocks, done = ffn_down(places, inner, down_weight, residual, [done])
    mixed_got = over_z(mixed_blocks)
    (ffn_up, ffn_down_way), done = relay(ffn_up, below, ffn_down_way, above, [done])
    below, above = lax.ppermute(ffn_up, "y", UP), lax.ppermute(ffn_down_way, "y", DOWN)

    (both_back, latents_partial), back_done = attend_back(
        attention_back,
        out_weight,
        queries,
        keyvals,
        rope_keys,
        log_total,
        query_up,
        latent_up,
        tables,
        [done],
    )
    latents_got = exchange(latents_partial)

    (out_keep, out_give), picked = halves(starts, [attention_back], [back_done])
    (out_keep, out_give), done = halves(
        starts, [attention_back], [back_done, below, above, *mixed_got]
    )
    (mixed_part,), done = add_all([mixed_blocks[0], *mixed_got], [done])
    mixed_other = lax.ppermute(mixed_part, "xh", SWAP)

    (raw_many, own_raw, latent_gain_parts), done = latents_back_of(
        me, latents_got, latents, query_gain, latent_gain, tables, [done]
    )
    raw_back = exchange(raw_many)

    out_got, both_got = over_cores(out_give), over_cores(both_back)
    (attn_across, attn_up, attn_down, attn_own), done = attn_grads(
        (out_keep, code_keep, lat_keep),
        (out_got, code_got, lat_got),
        (heads_out, both_back),
        (heads_got, both_got),
        [done],
    )
    attn_got = [
        lax.ppermute(attn_across, "y", ACROSS),
        lax.ppermute(attn_up, "y", UP),
        lax.ppermute(attn_down, "y", DOWN),
    ]
    gains = jnp.concatenate(
        [
            second_gain_part.reshape(16, -1),
            latent_gain_parts[0, :QR].reshape(16, -1),
            latent_gain_parts[0, QR:].reshape(16, -1),
        ],
        axis=1,
    ).astype(BF16)
    gains = jnp.pad(gains, ((0, 0), (0, WIDE - gains.shape[1])))
    (ffn_keep, ffn_give), done = add_chips([ffn_own, below, above], [done])
    ffn_got = lax.ppermute(ffn_give, "xl", SWAP)
    (parts,), done = down_parts(own_in, raw_back, gains, [done, attn_got[1], attn_got[2]])
    parts_got = lax.all_to_all(parts, DP, 0, 0, tiled=True)

    (mixed_part,), done = add_all([mixed_part, mixed_other], [done])
    from_above, across, from_below = (
        lax.ppermute(mixed_part, "z", way) for way in (DOWN, ACROSS, UP)
    )
    (tokens_grad,), done = tokens_back_of(
        raw_back, tokens, attention_back, query_down, latent_down, first_gain, [done]
    )
    (many,), summed = sum_copies(parts_got, [done])
    everyone = exchange(many)

    (attn_keep, attn_give), done = add_chips([attn_own, *attn_got], [summed])
    attn_other = lax.ppermute(attn_give, "xl", SWAP)
    (gate_weight_grad, up_weight_grad, down_weight_grad), done = finish_ffn(
        ffn_keep, ffn_got, [done]
    )
    (out_weight_grad, query_up_grad, latent_up_grad), done = finish_attn(
        attn_keep, attn_other, [done]
    )
    (
        query_down_grad,
        latent_down_grad,
        first_gain_grad,
        second_gain_grad,
        query_gain_grad,
        latent_gain_grad,
    ) = finish_down(block, everyone, query_down, latent_down, first_gain, [])

    mixed = assemble(
        z_order, [mixed_part, from_above, across, from_below], [done]
    )

    return (
        mixed,
        tokens_grad,
        first_gain_grad[0],
        query_down_grad,
        query_gain_grad[0],
        query_up_grad,
        latent_down_grad,
        latent_gain_grad[0],
        latent_up_grad,
        out_weight_grad.T,
        second_gain_grad[0],
        gate_weight_grad,
        up_weight_grad,
        down_weight_grad.T,
    )


def solution(mesh):
    grid = Mesh(mesh.devices.reshape(4, 2, 2, 2, 4), ("y", "xl", "core", "xh", "z"))
    in_specs = (
        P(DP, None),
        P(),
        P(),
        P(),
        P(None, TP),
        P(),
        P(),
        P(None, TP),
        P(TP, None),
        P(),
        P(None, TP),
        P(None, TP),
        P(TP, None),
        P(DP, None),
    )
    out_specs = (
        P(DP, None),
        P(DP, None),
        P(DP),
        P(DP, None),
        P(DP),
        P(DP, TP),
        P(DP, None),
        P(DP),
        P(DP, TP),
        P(TP, DP),
        P(DP),
        P(DP, TP),
        P(DP, TP),
        P(TP, DP),
    )
    return jax.shard_map(
        on_device, mesh=grid, in_specs=in_specs, out_specs=out_specs, check_vma=False
    )
```

```python
import functools

import jax
import jax.numpy as jnp
import numpy as np
from jax import lax
from jax.experimental import pallas as pl
from jax.experimental.pallas import tpu as pltpu
from jax.sharding import Mesh, PartitionSpec as P

NOPE = 64
ROPE = 32
DV = 64
KVR = 256
QR = 768
LAT = QR + KVR
WIDE = LAT + 128

EPS = 1e-05
BASE = 10000.0
SCALE = (NOPE + ROPE) ** (-0.5)

DP = ("y", "xl", "core")
TP = ("xh", "z")
SWAP = [(0, 1), (1, 0)]
F32 = jnp.float32
BF16 = jnp.bfloat16
NT = (((1,), (1,)), ((), ()))
TN = (((0,), (0,)), ((), ()))
NN = (((1,), (0,)), ((), ()))
TILE = 256


def dot(left, right, dims=NN):
    return lax.dot_general(left, right, dims, preferred_element_type=F32)


def params(limit=56):
    return pltpu.CompilerParams(vmem_limit_bytes=limit * 2**20)


HBM = pl.BlockSpec(memory_space=pltpu.HBM)


def call(kernel, args, in_specs, out_specs, out_shape, name, grid=(1,), scratch=(), needs=(), me=None, limit=60, near=()):
    args = [
        item if n in near else pltpu.with_memory_space_constraint(item, pltpu.HBM)
        for n, item in enumerate(args)
    ]
    needs = [pltpu.with_memory_space_constraint(item, pltpu.HBM) for item in needs]
    first = 0 if me is None else 1
    n_in, n_out = len(args), len(out_shape)

    def body(*refs):
        ins = refs[: first + n_in]
        rest = refs[first + n_in + len(needs) :]
        mark = rest[n_out]

        @pl.when(pl.program_id(0) == 0)
        def _():
            mark[...] = jnp.zeros_like(mark)

        kernel(*ins, *rest[:n_out], *rest[n_out + 1 :])

    *outs, mark = pl.pallas_call(
        body,
        grid_spec=pltpu.PrefetchScalarGridSpec(
            num_scalar_prefetch=first,
            grid=grid,
            in_specs=list(in_specs) + [HBM] * len(needs),
            out_specs=list(out_specs) + [full((8, 128))],
            scratch_shapes=list(scratch),
        ),
        out_shape=list(out_shape) + [shaped(8, 128, dtype=F32)],
        compiler_params=params(limit),
        cost_estimate=pl.CostEstimate(flops=1, bytes_accessed=1, transcendentals=0),
        name=name,
    )(*(() if me is None else (me,)), *args, *needs)
    return outs, mark


def shaped(*shape, dtype=BF16):
    return pltpu.HBM(shape, dtype)


def full(shape):
    return pl.BlockSpec(shape, lambda *_: (0,) * len(shape))


def rope_tables(length):
    half = ROPE // 2
    rates = np.exp(np.arange(half, dtype=np.float32) * np.float32(-2.0 * np.log(BASE) / ROPE))
    angles = np.arange(length, dtype=np.float32)[:, None] * rates.astype(np.float32)[None, :]
    cosine, sine = np.cos(angles), np.sin(angles)
    keep = np.zeros((length, 128), np.float32)
    keep[:, :NOPE] = 1.0
    keep[:, 64:80] = cosine
    keep[:, 80:96] = cosine
    low = np.zeros((length, 128), np.float32)
    low[:, 64:80] = -sine
    high = np.zeros((length, 128), np.float32)
    high[:, 80:96] = sine
    return jnp.asarray(keep), jnp.asarray(low), jnp.asarray(high)


def turn(values, keep, low, high, back=False):
    moved = pltpu.roll(values, 112, 1) * low + pltpu.roll(values, 16, 1) * high
    return values * keep - moved if back else values * keep + moved


def root(values):
    return lax.rsqrt(jnp.mean(values * values, axis=-1, keepdims=True) + EPS)


def norm_back(upstream, normed, factor, gain):
    scaled = upstream * gain
    return factor * (scaled - normed * jnp.mean(scaled * normed, axis=-1, keepdims=True))


def spread_out_weight(weight_ref, spread_ref, heads):
    spread_ref[...] = jnp.zeros_like(spread_ref)
    for h in range(heads):
        spread_ref[128 * h + 64 : 128 * h + 128, :] = weight_ref[64 * h : 64 * h + 64, :]


def spread_query_up(weight_ref, spread_ref, heads):
    spread_ref[...] = jnp.zeros_like(spread_ref)
    for h in range(heads):
        spread_ref[128 * h : 128 * h + 96, :] = weight_ref[96 * h : 96 * h + 96, :]


def row(ref):
    return ref[...].reshape(1, -1)


def low_lanes(shape):
    return lax.broadcasted_iota(jnp.int32, shape, 1) < NOPE


def causal(keys, queries, first_query):
    key_ids = lax.broadcasted_iota(jnp.int32, (keys, queries), 0)
    query_ids = lax.broadcasted_iota(jnp.int32, (keys, queries), 1) + first_query
    return key_ids <= query_ids


def attend_kernel(
    heads,
    me,
    tokens,
    first_gain,
    query_down,
    latent_down,
    query_gain,
    latent_gain,
    query_up,
    latent_up,
    out_weight,
    keep,
    low,
    high,
    first_in,
    latents,
    query_code,
    latent_code,
    queries,
    keyvals,
    rope_keys,
    heads_out,
    log_total,
    partial,
    raw_latents,
    spread,
    spread_up,
    rope_down,
    kv_all,
    rope_all,
):
    step = pl.program_id(0)

    @pl.when(step == 0)
    def _():
        spread_out_weight(out_weight, spread, heads)
        spread_query_up(query_up, spread_up, heads)
        rope_down[...] = jnp.zeros_like(rope_down)
        rope_down[64:96, :] = latent_down[KVR:, :]

    def rows_of(index, carry):
        rows = pl.ds(pl.multiple_of(index * 32, 32), 32)
        values = tokens[rows, :].astype(F32)
        first_in[rows, :] = (values * root(values) * row(first_gain)).astype(BF16)
        return carry

    lax.fori_loop(0, TILE // 32, rows_of, 0)
    taken = first_in[...]
    query_latent = dot(taken, query_down[...])
    raw_latents[:, :QR] = query_latent
    code = (query_latent * root(query_latent) * row(query_gain)).astype(BF16)
    query_code[...] = code
    latent = dot(taken, latent_down[:KVR, :], NT)
    raw_latents[:, QR:] = latent
    count = latents.shape[0]
    own = me[0] * count

    @pl.when(own // TILE == step)
    def _():
        latents[...] = raw_latents[pl.ds(pl.multiple_of(own % TILE, count), count), :]

    lcode = (latent * root(latent) * row(latent_gain)).astype(BF16)
    latent_code[...] = lcode
    tables = keep[...], low[...], high[...]
    rope = turn(dot(taken, rope_down[...], NT), *tables).astype(BF16)
    rope_keys[...] = rope
    here = pl.ds(pl.multiple_of(step * TILE, TILE), TILE)
    rope_all[here, :] = rope
    kv = dot(lcode, latent_up[...]).astype(BF16)
    keyvals[...] = kv
    kv_all[here, :] = kv
    raw = dot(code, spread_up[...], NT)
    for h in range(heads):
        lanes = slice(128 * h, 128 * h + 128)
        queries[:, lanes] = turn(raw[:, lanes], *tables).astype(BF16)

    def tile(index):
        keys = TILE * (index + 1)
        for h in range(heads):
            lanes = slice(128 * h, 128 * h + 128)
            kv_h = kv_all[:keys, lanes]
            key = jnp.where(low_lanes((keys, 128)), kv_h, rope_all[:keys, :])
            scores = dot(key, queries[:, lanes], NT) * SCALE
            scores = jnp.where(causal(keys, TILE, TILE * index), scores, -1e30)
            top = jnp.max(scores, axis=0, keepdims=True)
            weights = jnp.exp(scores - top)
            total = jnp.sum(weights, axis=0, keepdims=True)
            log_total[h : h + 1, :] = top + jnp.log(total)
            probs = (weights * (1.0 / total)).astype(BF16)
            heads_out[:, lanes] = dot(probs, kv_h, TN).astype(BF16)

    for index in range(2):
        pl.when(step == index)(functools.partial(tile, index))
    partial[...] = dot(heads_out[...], spread[...]).astype(BF16)


def attend(me, tokens, first_gain, query_down, latent_down, query_gain, latent_gain, query_up, latent_up, out_weight, tables):
    latent_down, query_up = latent_down.T, query_up.T
    length, width = tokens.shape
    heads = out_weight.shape[0] // DV
    wide = 128 * heads

    def rows(columns):
        return pl.BlockSpec((TILE, columns), lambda i, *_: (i, 0))

    return call(
        functools.partial(attend_kernel, heads),
        (tokens, first_gain, query_down, latent_down, query_gain, latent_gain, query_up, latent_up, out_weight, *tables),
        [
            rows(width),
            full((width,)),
            full(query_down.shape),
            full(latent_down.shape),
            full((QR,)),
            full((KVR,)),
            full(query_up.shape),
            full(latent_up.shape),
            full(out_weight.shape),
            rows(128),
            rows(128),
            rows(128),
        ],
        [
            rows(width),
            full((length // 8, LAT)),
            rows(QR),
            rows(KVR),
            rows(wide),
            rows(wide),
            rows(128),
            rows(wide),
            pl.BlockSpec((8, TILE), lambda i, *_: (0, i)),
            rows(width),
        ],
        [
            shaped(length, width),
            shaped(length // 8, LAT, dtype=F32),
            shaped(length, QR),
            shaped(length, KVR),
            shaped(length, wide),
            shaped(length, wide),
            shaped(length, 128),
            shaped(length, wide),
            shaped(8, length, dtype=F32),
            shaped(length, width),
        ],
        "attend",
        grid=(length // TILE,),
        me=me,
        scratch=[
            pltpu.VMEM((TILE, LAT), F32),
            pltpu.VMEM((wide, width), BF16),
            pltpu.VMEM((wide, QR), BF16),
            pltpu.VMEM((128, width), BF16),
            pltpu.VMEM((length, wide), BF16),
            pltpu.VMEM((length, 128), BF16),
        ],
    )


def attend_back_kernel(
    heads,
    attention_back,
    out_weight,
    queries,
    keyvals,
    rope_keys,
    log_total,
    query_up,
    latent_up,
    keep,
    low,
    high,
    both_back,
    partial,
    spread,
    spread_up,
    kv_grad,
    rope_grad,
    code_grad,
):
    step = pl.program_id(0)

    @pl.when(step == 0)
    def _():
        spread_out_weight(out_weight, spread, heads)
        spread_query_up(query_up, spread_up, heads)
        kv_grad[...] = jnp.zeros_like(kv_grad)
        rope_grad[...] = jnp.zeros_like(rope_grad)

    heads_back = dot(attention_back[...], spread[...], NT).astype(BF16)
    tables = keep[...], low[...], high[...]

    def tile(index):
        keys = TILE * (index + 1)
        low_part = low_lanes((keys, 128))
        for h in range(heads):
            lanes = slice(128 * h, 128 * h + 128)
            kv_h = keyvals[:keys, lanes]
            key = jnp.where(low_part, kv_h, rope_keys[:keys, :])
            query = queries[:, lanes]
            back = heads_back[:, lanes]
            scores = dot(key, query, NT) * SCALE
            probs = jnp.exp(scores - log_total[h : h + 1, :])
            probs = jnp.where(causal(keys, TILE, TILE * index), probs, 0.0)
            prob_back = dot(kv_h, back, NT)
            mean = jnp.sum(probs * prob_back, axis=0, keepdims=True)
            score_back = (probs * (prob_back - mean)).astype(BF16)
            of_values = dot(probs.astype(BF16), back)
            of_keys = dot(score_back, query) * SCALE
            kv_grad[:keys, lanes] += of_values + jnp.where(low_part, of_keys, 0.0)
            rope_grad[:keys, :] += jnp.where(low_part, 0.0, of_keys)
            of_query = dot(score_back, key, TN) * SCALE
            both_back[here, lanes] = turn(of_query, *tables, back=True).astype(BF16)

    wide = 128 * heads
    here = pl.ds(pl.multiple_of(step * TILE, TILE), TILE)
    for index in range(2):
        pl.when(step == index)(functools.partial(tile, index))
    code_grad[here, :] = dot(both_back[here, :wide], spread_up[...]).astype(BF16)

    @pl.when(step == 1)
    def _():
        kv = kv_grad[...].astype(BF16)
        both_back[:, wide:] = kv
        partial[:, :QR] = code_grad[...]
        partial[:, QR:LAT] = dot(kv, latent_up[...], NT).astype(BF16)
        partial[:, LAT:] = rope_grad[...].astype(BF16)


def attend_back(attention_back, out_weight, queries, keyvals, rope_keys, log_total, query_up, latent_up, tables, needs):
    query_up = query_up.T
    length, width = attention_back.shape
    heads = out_weight.shape[0] // DV
    wide = 128 * heads

    def rows(columns):
        return pl.BlockSpec((TILE, columns), lambda i, *_: (i, 0))

    return call(
        functools.partial(attend_back_kernel, heads),
        (attention_back, out_weight, queries, keyvals, rope_keys, log_total, query_up, latent_up, *tables),
        [
            rows(width),
            full(out_weight.shape),
            rows(wide),
            full((length, wide)),
            full((length, 128)),
            pl.BlockSpec((8, TILE), lambda i, *_: (0, i)),
            full(query_up.shape),
            full(latent_up.shape),
            rows(128),
            rows(128),
            rows(128),
        ],
        [full((length, 2 * wide)), full((length, WIDE))],
        [shaped(length, 2 * wide), shaped(length, WIDE)],
        "attend_back",
        grid=(length // TILE,),
        scratch=[
            pltpu.VMEM((wide, width), BF16),
            pltpu.VMEM((wide, QR), BF16),
            pltpu.VMEM((length, wide), F32),
            pltpu.VMEM((length, 128), F32),
            pltpu.VMEM((length, QR), BF16),
        ],
        needs=needs,
        limit=44,
        near=(0,),
    )


def add_up(got):
    total = got[0].astype(F32)
    for k in range(1, 8):
        total = total + got[k].astype(F32)
    return total


STEPS = 2


def residual_kernel(me, got, tokens, gain, residual, many):
    del me
    total = tokens[...].astype(F32) + add_up(got)
    residual[...] = total
    second_in = (total * root(total) * row(gain)).astype(BF16)
    for k in range(8):
        many[k] = second_in


def own_specs(rows, width):
    step = rows // STEPS
    return (
        pl.BlockSpec((8, step, width), lambda i, me: (0, i, 0)),
        pl.BlockSpec((step, width), lambda i, me: (i, 0)),
        pl.BlockSpec((step, width), lambda i, me: (me[0] * STEPS + i, 0)),
    )


def residual_of(me, got, tokens, gain, needs):
    width = tokens.shape[1]
    rows = tokens.shape[0] // 8
    eight, one, own = own_specs(rows, width)
    return call(
        residual_kernel,
        (got.reshape(8, rows, width), tokens, gain),
        [eight, own, full((width,))],
        [one, eight],
        [shaped(rows, width, dtype=F32), shaped(8, rows, width)],
        "residual",
        grid=(STEPS,),
        needs=needs,
        me=me,
        limit=24,
        near=(0,),
    )


def residual_back_kernel(me, got, residual, cotangent, gain, many, gain_part):
    del me
    second_back = add_up(got)
    values = residual[...]
    factor = root(values)
    normed = values * factor
    part = jnp.sum(second_back * normed, axis=0, keepdims=True)

    @pl.when(pl.program_id(0) == 0)
    def _():
        gain_part[...] = part

    @pl.when(pl.program_id(0) > 0)
    def _():
        gain_part[...] += part

    back = cotangent[...].astype(F32) + norm_back(second_back, normed, factor, row(gain))
    back = back.astype(BF16)
    for k in range(8):
        many[k] = back


def residual_back_of(me, got, residual, cotangent, gain, needs):
    rows, width = residual.shape
    eight, one, own = own_specs(rows, width)
    return call(
        residual_back_kernel,
        (got.reshape(8, rows, width), residual, cotangent, gain),
        [eight, one, own, full((width,))],
        [eight, full((1, width))],
        [shaped(8, rows, width), shaped(1, width, dtype=F32)],
        "residual_back",
        grid=(STEPS,),
        needs=needs,
        me=me,
        limit=24,
        near=(0,),
    )


def ffn_kernel(
    second_in, gate_weight, up_weight, inner_back, gate_back, up_back, inner, partial
):
    taken = second_in[...]
    gate = dot(taken, gate_weight[...], NT)
    up = dot(taken, up_weight[...], NT)
    sigma = 1.0 / (1.0 + jnp.exp(-gate))
    act = gate * sigma
    units = gate.shape[1]
    back = inner_back[...].astype(F32)
    of_gate = (back * up * sigma * (1.0 + gate * (1.0 - sigma))).astype(BF16)
    of_up = (back * act).astype(BF16)
    for out, values in ((gate_back, of_gate), (up_back, of_up), (inner, (act * up).astype(BF16))):
        out[:, :units] = values
        out[:, units:] = jnp.zeros((values.shape[0], out.shape[1] - units), BF16)
    partial[...] = (dot(of_gate, gate_weight[...]) + dot(of_up, up_weight[...])).astype(BF16)


def ffn(second_in, gate_weight, up_weight, inner_back, needs):
    length, width = second_in.shape
    units = gate_weight.shape[0]
    wide = -(-units // 128) * 128

    def rows(columns):
        return pl.BlockSpec((TILE, columns), lambda i, *_: (i, 0))

    return call(
        ffn_kernel,
        (second_in, gate_weight, up_weight, inner_back),
        [rows(width), full((units, width)), full((units, width)), rows(units)],
        [rows(wide), rows(wide), rows(wide), rows(width)],
        [shaped(length, wide)] * 3 + [shaped(length, width)],
        "ffn",
        grid=(length // TILE,),
        needs=needs,
        limit=44,
        near=(0,),
    )


def ffn_down_kernel(places, inner, down_weight, residual, *refs):
    outs, total = refs[:4], refs[4]
    for i in range(2):
        rows = slice(i * TILE, i * TILE + TILE)
        total[rows, :] = dot(inner[rows, : down_weight.shape[0]], down_weight[...]).astype(BF16)
    count = residual.shape[0]
    own = pl.ds(pl.multiple_of(places[4] * count, count), count)
    total[own, :] = (total[own, :].astype(F32) + residual[...]).astype(BF16)
    for k, out in enumerate(outs):
        rows = out.shape[0]
        out[...] = total[pl.ds(pl.multiple_of(places[k] * rows, rows), rows), :]


def ffn_down(places, inner, down_weight, residual, needs):
    length, width = inner.shape[0], down_weight.shape[1]
    block = (length // 4, width)
    return call(
        ffn_down_kernel,
        (inner, down_weight, residual),
        [full(inner.shape), full(down_weight.shape), full(residual.shape)],
        [full(block)] * 4,
        [shaped(*block)] * 4,
        "ffn_down",
        scratch=[pltpu.VMEM((length, width), BF16)],
        needs=needs,
        me=places,
    )


def halves_kernel(blocks, width, starts, *refs):
    sources, outs, turned = refs[:blocks], refs[blocks : 3 * blocks], refs[3 * blocks]
    for n in range(blocks):
        source, keep, give = sources[n], outs[2 * n], outs[2 * n + 1]
        columns, each = source.shape[1], width[n]
        for c in range(0, columns, 256):
            turned[c : c + 256, :] = source[:, c : c + 256].T
        for which, out in enumerate((keep, give)):
            for k in range(8):
                first = pl.multiple_of(starts[8 * which + k] * each, 16)
                out[each * k : each * k + each, :] = turned[pl.ds(first, each), :]


def halves(starts, values, needs):
    length = values[0].shape[0]
    widths = [item.shape[1] // 16 for item in values]
    shapes = [(8 * w, length) for w in widths for _ in range(2)]
    return call(
        functools.partial(halves_kernel, len(values), widths),
        tuple(values),
        [full(item.shape) for item in values],
        [full(s) for s in shapes],
        [shaped(*s) for s in shapes],
        "halves",
        scratch=[pltpu.VMEM((max(item.shape[1] for item in values), length), BF16)],
        needs=needs,
        me=starts,
        limit=24,
        near=(0,),
    )


ORDER = (2, 1, 3, 0)


def ffn_grads_kernel(in_keep, in_got, cot_keep, cot_got, *refs):
    ours, theirs, outs = refs[:3], refs[3:6], refs[6:]
    units = outs[0].shape[1] // 3

    def block(*parts):
        for n, (keep, got) in enumerate(((in_keep, in_got), (in_keep, in_got), (cot_keep, cot_got))):
            total = dot(keep[...], ours[n][...]) + dot(got[...], theirs[n][...])
            total = total[:, :units].astype(BF16)
            first = 0
            for out in parts:
                count = out.shape[0]
                out[:, units * n : units * n + units] = total[first : first + count]
                first += count

    for s, parts in enumerate((outs[:2], outs[2:3], outs[3:4], outs[4:])):
        pl.when(pl.program_id(0) == s)(functools.partial(block, *parts))


def ffn_grads(in_keep, in_got, cot_keep, cot_got, ours, theirs, units, needs):
    length, wide = ours[0].shape
    rows = in_keep.shape[0] // 4

    def index(i):
        return (jnp.where(i == 0, 2, jnp.where(i == 1, 1, jnp.where(i == 2, 3, 0))), 0)

    left = pl.BlockSpec((rows, length), index)
    out = (rows, 3 * units)
    outs = [(rows // 2, 3 * units)] * 2 + [out] * 3
    return call(
        ffn_grads_kernel,
        (in_keep, in_got, cot_keep, cot_got, *ours, *theirs),
        [left] * 4 + [full((length, wide))] * 6,
        [full(s) for s in outs],
        [shaped(*s) for s in outs],
        "ffn_grads",
        grid=(4,),
        needs=needs,
    )


def attn_grads_kernel(widths, *refs):
    keeps, gots, outs = refs[:3], refs[3:6], refs[10:]
    wide = outs[0].shape[1]
    ours, theirs = (
        (heads, both.at[:, :wide], both.at[:, wide:]) for heads, both in (refs[6:8], refs[8:10])
    )
    rows = outs[0].shape[0] // 2
    heads = wide // 128
    for out, k in zip(outs, ORDER):
        first = 0
        for n, each in enumerate(widths):
            part = slice(2 * each * k, 2 * each * k + 2 * each)
            total = dot(keeps[n][part, :], ours[n][...]) + dot(gots[n][part, :], theirs[n][...])
            if n == 0:
                for j in range(4):
                    half = total[j * each // 2 : (j + 1) * each // 2]
                    top, left = j // 2 * rows, j % 2 * (wide // 2)
                    for h in range(heads):
                        out[top : top + each // 2, left + 64 * h : left + 64 * h + 64] = half[
                            :, 128 * h + 64 : 128 * h + 128
                        ].astype(BF16)
                first += each // 2
                continue
            total = total.astype(BF16)
            out[first : first + each, :] = total[:each]
            out[rows + first : rows + first + each, :] = total[each:]
            first += each


def attn_grads(keeps, gots, ours, theirs, needs):
    widths = [item.shape[0] // 8 for item in keeps]
    rows, wide = sum(widths) - widths[0] // 2, ours[0].shape[1]
    args = (*keeps, *gots, *ours, *theirs)
    outs = [(2 * rows, wide)] * 4
    return call(
        functools.partial(attn_grads_kernel, widths),
        args,
        [full(item.shape) for item in args],
        [full(s) for s in outs],
        [shaped(*s) for s in outs],
        "attn_grads",
        needs=needs,
    )


UP = [(i, (i + 1) % 4) for i in range(4)]
DOWN = [(i, (i + 3) % 4) for i in range(4)]
ACROSS = [(i, (i + 2) % 4) for i in range(4)]


def relay_kernel(up, from_below, down, from_above, up_out, down_out):
    @pl.when(pl.program_id(0) == 0)
    def _():
        up_out[...] = (up[...].astype(F32) + from_below[...].astype(F32)).astype(BF16)
        down_out[...] = down[...]

    @pl.when(pl.program_id(0) == 1)
    def _():
        up_out[...] = up[...]
        down_out[...] = (down[...].astype(F32) + from_above[...].astype(F32)).astype(BF16)


def relay(up, from_below, down, from_above, needs):
    rows, width = from_below.shape
    half = pl.BlockSpec((rows, width), lambda i, *_: (i, 0))
    return call(
        relay_kernel,
        (up, from_below, down, from_above),
        [half, full((rows, width)), half, full((rows, width))],
        [half, half],
        [shaped(2 * rows, width)] * 2,
        "relay",
        grid=(2,),
        needs=needs,
    )


def add_chips_kernel(*refs):
    ins, keep, give = refs[:-2], refs[-2], refs[-1]
    count = len(ins) // 2
    keep[...] = sum(item[...].astype(F32) for item in ins[:count])
    give[...] = sum(item[...].astype(F32) for item in ins[count:]).astype(BF16)


def add_chips(items, needs):
    rows, width = items[0].shape[0] // 2, items[0].shape[1]
    step = rows // 2 if rows % 32 == 0 and (rows // 2) % 16 == 0 else rows
    count = rows // step
    mine = pl.BlockSpec((step, width), lambda i, *_: (i, 0))
    other = pl.BlockSpec((step, width), lambda i, *_: (i + count, 0))
    return call(
        add_chips_kernel,
        (*items, *items),
        [mine] * len(items) + [other] * len(items),
        [mine, mine],
        [shaped(rows, width, dtype=F32), shaped(rows, width)],
        "add_chips",
        grid=(count,),
        needs=needs,
    )


def add_all_kernel(*refs):
    refs[-1][...] = sum(item[...].astype(F32) for item in refs[:-1]).astype(BF16)


def add_all(items, needs):
    rows, width = items[0].shape
    half = pl.BlockSpec((rows // 2, width), lambda i, *_: (i, 0))
    return call(
        add_all_kernel,
        tuple(items),
        [half] * len(items),
        [half],
        [shaped(rows, width)],
        "add_all",
        grid=(2,),
        needs=needs,
        limit=58,
    )


def over_z(blocks):
    return [lax.ppermute(blocks[k], "z", [(i, i ^ k) for i in range(4)]) for k in (1, 2, 3)]


def over_cores(values):
    return lax.ppermute(values, "core", SWAP)


def latents_back_kernel(
    me, got, latents, query_gain, latent_gain, keep, low, high, many, own, gain_part, turns, sems
):
    rows = own.shape[0]
    here = pl.ds(pl.multiple_of(me[0] * rows, rows), rows)
    copies = [
        pltpu.make_async_copy(table.at[here, :], turns.at[n], sems.at[n])
        for n, table in enumerate((keep, low, high))
    ]
    for copy in copies:
        copy.start()
    total = add_up(got)
    for copy in copies:
        copy.wait()

    def back(lanes, gain):
        upstream, values = total[:, lanes], latents[:, lanes]
        factor = root(values)
        normed = values * factor
        gain_part[:, lanes] = jnp.sum(upstream * normed, axis=0, keepdims=True)
        return norm_back(upstream, normed, factor, row(gain)).astype(BF16)

    own[:, :QR] = back(slice(0, QR), query_gain)
    own[:, QR:LAT] = back(slice(QR, LAT), latent_gain)
    own[:, LAT:] = turn(total[:, LAT:], turns[0], turns[1], turns[2], back=True).astype(BF16)
    for k in range(8):
        many[k] = own[...]


def latents_back_of(me, got, latents, query_gain, latent_gain, tables, needs):
    rows = latents.shape[0]
    return call(
        latents_back_kernel,
        (got.reshape(8, rows, WIDE), latents, query_gain, latent_gain, *tables),
        [full((8, rows, WIDE)), full(latents.shape), full((QR,)), full((KVR,)), HBM, HBM, HBM],
        [full((8, rows, WIDE)), full((rows, WIDE)), full((1, LAT))],
        [shaped(8, rows, WIDE), shaped(rows, WIDE), shaped(1, LAT, dtype=F32)],
        "latents_back",
        scratch=[
            pltpu.VMEM((3, rows, 128), F32),
            pltpu.SemaphoreType.DMA((3,)),
        ],
        needs=needs,
        me=me,
        limit=24,
        near=(0,),
    )


def first_back_of(raw_back, query_down, latent_down, rope_down):
    rope_down[...] = jnp.zeros_like(rope_down)
    rope_down[64:96, :] = latent_down[KVR:, :]
    return (
        dot(raw_back[:, :QR], query_down[...], NT)
        + dot(raw_back[:, QR:LAT], latent_down[:KVR, :])
        + dot(raw_back[:, LAT:], rope_down[...])
    )


def tokens_back_kernel(
    raw_back, tokens, attention_back, query_down, latent_down, gain, tokens_grad, rope_down
):
    first_back = first_back_of(raw_back, query_down, latent_down, rope_down)
    values = tokens[...].astype(F32)
    factor = root(values)
    tokens_grad[...] = attention_back[...].astype(F32) + norm_back(
        first_back, values * factor, factor, row(gain)
    )


def tokens_back_of(raw_back, tokens, attention_back, query_down, latent_down, gain, needs):
    length, width = tokens.shape

    def rows(columns):
        return pl.BlockSpec((TILE, columns), lambda i, *_: (i, 0))

    return call(
        tokens_back_kernel,
        (raw_back, tokens, attention_back, query_down, latent_down.T, gain),
        [
            rows(WIDE),
            rows(width),
            rows(width),
            full(query_down.shape),
            full(latent_down.shape[::-1]),
            full((width,)),
        ],
        [rows(width)],
        [shaped(length, width, dtype=F32)],
        "tokens_back",
        grid=(length // TILE,),
        scratch=[pltpu.VMEM((128, width), BF16)],
        needs=needs,
    )


GAINS = ((0, 160), (160, 48), (208, 16))


def down_parts_kernel(own_in, raw_back, gains, out):
    total = dot(own_in[...], raw_back[...]).astype(BF16)
    for d in range(16):
        out[d, :20, :] = total[20 * d : 20 * d + 20]
        out[d, 20:, :] = jnp.zeros((4, WIDE), BF16)
        out[d, 20:21, :] = gains[d : d + 1, :]


def down_parts(own_in, raw_back, gains, needs):
    args = (own_in, raw_back, gains)
    return call(
        down_parts_kernel,
        args,
        [full(item.shape) for item in args],
        [full((16, 24, WIDE))],
        [shaped(16, 24, WIDE)],
        "down_parts",
        needs=needs,
        limit=24,
    )


def sum_copies_kernel(got, many):
    total = got[0].astype(F32)
    for d in range(1, 16):
        total = total + got[d].astype(F32)
    for k in range(8):
        many[k] = total.astype(BF16)


def sum_copies(got, needs):
    return call(
        sum_copies_kernel,
        (got,),
        [full(got.shape)],
        [full((8, 24, WIDE))],
        [shaped(8, 24, WIDE)],
        "sum_copies",
        needs=needs,
        limit=24,
    )


def finish_kernel(heads, places, *refs):
    ins, outs, sems = refs[:12], refs[12:-1], refs[-1]
    ffn_keep, ffn_got, attn_keep, attn_got, everyone, query_rows, latent_rows, gain = ins[4:]
    mixed, gate, up, down, out_grad, query_up, latent_up, query_grad, latent_grad = outs[:9]
    first, *gains = outs[9:]
    count = ins[0].shape[0]
    copies = [
        pltpu.make_async_copy(
            item, mixed.at[pl.ds(pl.multiple_of(places[k] * count, count), count), :], sems.at[k]
        )
        for k, item in enumerate(ins[:4])
    ]
    for copy in copies:
        copy.start()

    units = gate.shape[1]
    for n, out in enumerate((gate, up, down)):
        lanes = slice(units * n, units * n + units)
        out[...] = ffn_keep[:, lanes] + ffn_got[:, lanes].astype(F32)

    total = attn_keep[...] + attn_got[...].astype(F32)
    out_grad[:80, :] = total[:80, : 64 * heads]
    out_grad[80:, :] = total[:80, 64 * heads :]
    for h in range(heads):
        query_up[:, 96 * h : 96 * h + 96] = total[80:128, 128 * h : 128 * h + 96]
    latent_up[...] = total[128:144]

    for t in range(8):
        values = everyone[t].astype(F32)
        query_grad[20 * t : 20 * t + 20, :] = values[:20, :QR]
        latent_grad[20 * t : 20 * t + 20, :KVR] = values[:20, QR:LAT]
        latent_grad[20 * t : 20 * t + 20, KVR:] = values[:20, LAT + 64 : LAT + 96]
    total = sum(everyone[t, 16:24, :].astype(F32) for t in range(8))[4:5, :]
    for out, (start, width) in zip(gains, GAINS):
        out[...] = total[:, start : start + width]

    def row_sums(values):
        return dot(jnp.ones((8, values.shape[1]), BF16), values.astype(BF16), NT)[:1]

    of_query = row_sums(query_rows[...].astype(F32) * query_grad[...])
    of_latent = row_sums(latent_rows[...].astype(F32) * latent_grad[...])
    first[...] = (of_query + of_latent) / gain[...]
    for copy in copies:
        copy.wait()


def finish(places, mixed, ffn, attn, everyone, query_rows, latent_rows, gain_rows):
    everyone = everyone.reshape(8, 24, WIDE)
    rows, units = ffn[0].shape[0], ffn[0].shape[1] // 3
    heads = attn[0].shape[1] // 128
    count, width = mixed[0].shape
    args = (*mixed, *ffn, *attn, everyone, query_rows, latent_rows, gain_rows)
    outs = [(rows, units)] * 3 + [(rows, 64 * heads), (48, 96 * heads), (16, 128 * heads)]
    outs += [(rows, QR), (rows, KVR + ROPE), (1, rows)] + [(1, each) for _, each in GAINS]
    return call(
        functools.partial(finish_kernel, heads),
        args,
        [full(item.shape) for item in args],
        [HBM] + [full(s) for s in outs],
        [shaped(4 * count, width)] + [shaped(*s, dtype=F32) for s in outs],
        "finish",
        scratch=[pltpu.SemaphoreType.DMA((4,))],
        me=places,
    )[0]


def exchange(blocks):
    return lax.all_to_all(blocks.reshape(-1, blocks.shape[-1]), TP, 0, 0, tiled=True)


def on_device(
    tokens,
    first_gain,
    query_down,
    query_gain,
    query_up,
    latent_down,
    latent_gain,
    latent_up,
    out_weight,
    second_gain,
    gate_weight,
    up_weight,
    down_weight,
    cotangent,
):
    length = tokens.shape[0]
    me = lax.axis_index(TP).astype(jnp.int32).reshape(1)
    y, xl, core = lax.axis_index("y"), lax.axis_index("xl"), lax.axis_index("core")
    starts = jnp.stack(
        [
            ((y + k) % 4 * 2 + (xl ^ j)) * 2 + c
            for c in (core, 1 - core)
            for k in range(4)
            for j in range(2)
        ]
    ).astype(jnp.int32)
    places = jnp.stack([lax.axis_index("z") ^ k for k in range(4)] + [me[0]]).astype(jnp.int32)
    z_order = jnp.stack([(lax.axis_index("z") + k) % 4 for k in range(4)]).astype(jnp.int32)
    first_row = ((y * 2 + xl) * 2 + core) * 160
    query_rows, latent_rows = (
        lax.dynamic_slice_in_dim(item, first_row, 160, 0) for item in (query_down, latent_down)
    )
    gain_rows = lax.dynamic_slice_in_dim(first_gain, first_row, 160, 0)[None]
    tables = rope_tables(length)

    gate_turned, up_turned = gate_weight.T, up_weight.T

    (
        first_in,
        latents,
        query_code,
        latent_code,
        queries,
        keyvals,
        rope_keys,
        heads_out,
        log_total,
        attn_partial,
    ), started = attend(
        me,
        tokens,
        first_gain,
        query_down,
        latent_down,
        query_gain,
        latent_gain,
        query_up,
        latent_up,
        out_weight,
        tables,
    )
    attn_got = exchange(attn_partial)

    (cot_keep, cot_give), picked = halves(starts, [cotangent], [started])
    inner_back = dot(cotangent, down_weight, NT).astype(BF16)
    cot_got = over_cores(cot_give)

    (residual, second_many), _ = residual_of(
        me, attn_got, tokens, second_gain, [picked, cot_got, query_rows, latent_rows, gain_rows, z_order]
    )
    second_in = exchange(second_many)

    turned_in = first_in.T.reshape(16, 8, 20, length)
    own_in = lax.dynamic_slice_in_dim(turned_in, me[0], 1, 1).reshape(320, length)
    (code_keep, code_give, lat_keep, lat_give), picked = halves(
        starts, [query_code, latent_code], [residual]
    )
    code_got, lat_got = over_cores(code_give), over_cores(lat_give)
    heads_got = over_cores(heads_out)

    (gate_back, up_back, inner, back_partial), done = ffn(
        second_in, gate_turned, up_turned, inner_back, [picked, own_in, code_got, lat_got, heads_got]
    )
    back_got = exchange(back_partial)

    ours = (gate_back, up_back, inner)
    theirs = [over_cores(item) for item in ours]
    (in_keep, in_give), _ = halves(starts, [second_in], [done])
    in_got = over_cores(in_give)
    (far_up, far_down, ffn_up, ffn_down_way, ffn_own), done = ffn_grads(in_keep, in_got, cot_keep, cot_got, ours, theirs, gate_weight.shape[1], [])
    below, above = lax.ppermute(far_up, "y", UP), lax.ppermute(far_down, "y", DOWN)

    (back_many, second_gain_part), done = residual_back_of(
        me, back_got, residual, cotangent, second_gain, [done]
    )
    attention_back = exchange(back_many)
    mixed_blocks, done = ffn_down(places, inner, down_weight, residual, [done])
    mixed_got = over_z(mixed_blocks)
    (ffn_up, ffn_down_way), done = relay(ffn_up, below, ffn_down_way, above, [done])
    below, above = lax.ppermute(ffn_up, "y", UP), lax.ppermute(ffn_down_way, "y", DOWN)

    (both_back, latents_partial), back_done = attend_back(
        attention_back,
        out_weight,
        queries,
        keyvals,
        rope_keys,
        log_total,
        query_up,
        latent_up,
        tables,
        [done],
    )
    latents_got = exchange(latents_partial)

    (out_keep, out_give), picked = halves(starts, [attention_back], [back_done])
    (out_keep, out_give), done = halves(
        starts, [attention_back], [back_done, below, above, *mixed_got]
    )
    (mixed_part,), done = add_all([mixed_blocks[0], *mixed_got], [done])
    mixed_other = lax.ppermute(mixed_part, "xh", SWAP)

    (raw_many, own_raw, latent_gain_parts), done = latents_back_of(
        me, latents_got, latents, query_gain, latent_gain, tables, [done]
    )
    raw_back = exchange(raw_many)

    out_got, both_got = over_cores(out_give), over_cores(both_back)
    (attn_across, attn_up, attn_down, attn_own), done = attn_grads(
        (out_keep, code_keep, lat_keep),
        (out_got, code_got, lat_got),
        (heads_out, both_back),
        (heads_got, both_got),
        [done],
    )
    attn_got = [
        lax.ppermute(attn_across, "y", ACROSS),
        lax.ppermute(attn_up, "y", UP),
        lax.ppermute(attn_down, "y", DOWN),
    ]
    gains = jnp.concatenate(
        [
            second_gain_part.reshape(16, -1),
            latent_gain_parts[0, :QR].reshape(16, -1),
            latent_gain_parts[0, QR:].reshape(16, -1),
        ],
        axis=1,
    ).astype(BF16)
    gains = jnp.pad(gains, ((0, 0), (0, WIDE - gains.shape[1])))
    (ffn_keep, ffn_give), done = add_chips([ffn_own, below, above], [done])
    ffn_got = lax.ppermute(ffn_give, "xl", SWAP)
    (parts,), done = down_parts(own_in, raw_back, gains, [done, attn_got[1], attn_got[2]])
    parts_got = lax.all_to_all(parts, DP, 0, 0, tiled=True)

    (mixed_part,), done = add_all([mixed_part, mixed_other], [done])
    from_above, across, from_below = (
        lax.ppermute(mixed_part, "z", way) for way in (DOWN, ACROSS, UP)
    )
    (many,), done = sum_copies(parts_got, [done])
    everyone = exchange(many)

    (attn_keep, attn_give), done = add_chips([attn_own, *attn_got], [done])
    attn_other = lax.ppermute(attn_give, "xl", SWAP)
    (tokens_grad,), done = tokens_back_of(
        raw_back, tokens, attention_back, query_down, latent_down, first_gain, [done]
    )
    (
        mixed,
        gate_weight_grad,
        up_weight_grad,
        down_weight_grad,
        out_weight_grad,
        query_up_grad,
        latent_up_grad,
        query_down_grad,
        latent_down_grad,
        first_gain_grad,
        second_gain_grad,
        query_gain_grad,
        latent_gain_grad,
    ) = finish(
        z_order,
        (mixed_part, from_above, across, from_below),
        (ffn_keep, ffn_got),
        (attn_keep, attn_other),
        everyone,
        query_rows,
        latent_rows,
        gain_rows,
    )

    return (
        mixed,
        tokens_grad,
        first_gain_grad[0],
        query_down_grad,
        query_gain_grad[0],
        query_up_grad,
        latent_down_grad,
        latent_gain_grad[0],
        latent_up_grad,
        out_weight_grad.T,
        second_gain_grad[0],
        gate_weight_grad,
        up_weight_grad,
        down_weight_grad.T,
    )


def solution(mesh):
    grid = Mesh(mesh.devices.reshape(4, 2, 2, 2, 4), ("y", "xl", "core", "xh", "z"))
    in_specs = (
        P(DP, None),
        P(),
        P(),
        P(),
        P(None, TP),
        P(),
        P(),
        P(None, TP),
        P(TP, None),
        P(),
        P(None, TP),
        P(None, TP),
        P(TP, None),
        P(DP, None),
    )
    out_specs = (
        P(DP, None),
        P(DP, None),
        P(DP),
        P(DP, None),
        P(DP),
        P(DP, TP),
        P(DP, None),
        P(DP),
        P(DP, TP),
        P(TP, DP),
        P(DP),
        P(DP, TP),
        P(DP, TP),
        P(TP, DP),
    )
    return jax.shard_map(
        on_device, mesh=grid, in_specs=in_specs, out_specs=out_specs, check_vma=False
    )
```

```python
import functools

import jax
import jax.numpy as jnp
import numpy as np
from jax import lax
from jax.experimental import pallas as pl
from jax.experimental.pallas import tpu as pltpu
from jax.sharding import Mesh, PartitionSpec as P

NOPE = 64
ROPE = 32
DV = 64
KVR = 256
QR = 768
LAT = QR + KVR
WIDE = LAT + 128

EPS = 1e-05
BASE = 10000.0
SCALE = (NOPE + ROPE) ** (-0.5)

DP = ("y", "xl", "core")
TP = ("xh", "z")
SWAP = [(0, 1), (1, 0)]
F32 = jnp.float32
BF16 = jnp.bfloat16
NT = (((1,), (1,)), ((), ()))
TN = (((0,), (0,)), ((), ()))
NN = (((1,), (0,)), ((), ()))
TILE = 256


def dot(left, right, dims=NN):
    return lax.dot_general(left, right, dims, preferred_element_type=F32)


def params(limit=56):
    return pltpu.CompilerParams(vmem_limit_bytes=limit * 2**20)


HBM = pl.BlockSpec(memory_space=pltpu.HBM)


def call(kernel, args, in_specs, out_specs, out_shape, name, grid=(1,), scratch=(), needs=(), me=None, limit=60, near=()):
    args = [
        item if n in near else pltpu.with_memory_space_constraint(item, pltpu.HBM)
        for n, item in enumerate(args)
    ]
    needs = [pltpu.with_memory_space_constraint(item, pltpu.HBM) for item in needs]
    first = 0 if me is None else 1
    n_in, n_out = len(args), len(out_shape)

    def body(*refs):
        ins = refs[: first + n_in]
        rest = refs[first + n_in + len(needs) :]
        mark = rest[n_out]

        @pl.when(pl.program_id(0) == 0)
        def _():
            mark[...] = jnp.zeros_like(mark)

        kernel(*ins, *rest[:n_out], *rest[n_out + 1 :])

    *outs, mark = pl.pallas_call(
        body,
        grid_spec=pltpu.PrefetchScalarGridSpec(
            num_scalar_prefetch=first,
            grid=grid,
            in_specs=list(in_specs) + [HBM] * len(needs),
            out_specs=list(out_specs) + [full((8, 128))],
            scratch_shapes=list(scratch),
        ),
        out_shape=list(out_shape) + [shaped(8, 128, dtype=F32)],
        compiler_params=params(limit),
        cost_estimate=pl.CostEstimate(flops=1, bytes_accessed=1, transcendentals=0),
        name=name,
    )(*(() if me is None else (me,)), *args, *needs)
    return outs, mark


def shaped(*shape, dtype=BF16):
    return pltpu.HBM(shape, dtype)


def full(shape):
    return pl.BlockSpec(shape, lambda *_: (0,) * len(shape))


def rope_tables(length):
    half = ROPE // 2
    rates = np.exp(np.arange(half, dtype=np.float32) * np.float32(-2.0 * np.log(BASE) / ROPE))
    angles = np.arange(length, dtype=np.float32)[:, None] * rates.astype(np.float32)[None, :]
    cosine, sine = np.cos(angles), np.sin(angles)
    keep = np.zeros((length, 128), np.float32)
    keep[:, :NOPE] = 1.0
    keep[:, 64:80] = cosine
    keep[:, 80:96] = cosine
    low = np.zeros((length, 128), np.float32)
    low[:, 64:80] = -sine
    high = np.zeros((length, 128), np.float32)
    high[:, 80:96] = sine
    return jnp.asarray(keep), jnp.asarray(low), jnp.asarray(high)


def turn(values, keep, low, high, back=False):
    moved = pltpu.roll(values, 112, 1) * low + pltpu.roll(values, 16, 1) * high
    return values * keep - moved if back else values * keep + moved


def root(values):
    return lax.rsqrt(jnp.mean(values * values, axis=-1, keepdims=True) + EPS)


def norm_back(upstream, normed, factor, gain):
    scaled = upstream * gain
    return factor * (scaled - normed * jnp.mean(scaled * normed, axis=-1, keepdims=True))


def spread_out_weight(weight_ref, spread_ref, heads):
    spread_ref[...] = jnp.zeros_like(spread_ref)
    for h in range(heads):
        spread_ref[128 * h + 64 : 128 * h + 128, :] = weight_ref[64 * h : 64 * h + 64, :]


def spread_query_up(weight_ref, spread_ref, heads):
    spread_ref[...] = jnp.zeros_like(spread_ref)
    for h in range(heads):
        spread_ref[128 * h : 128 * h + 96, :] = weight_ref[96 * h : 96 * h + 96, :]


def row(ref):
    return ref[...].reshape(1, -1)


def low_lanes(shape):
    return lax.broadcasted_iota(jnp.int32, shape, 1) < NOPE


def causal(keys, queries, first_query):
    key_ids = lax.broadcasted_iota(jnp.int32, (keys, queries), 0)
    query_ids = lax.broadcasted_iota(jnp.int32, (keys, queries), 1) + first_query
    return key_ids <= query_ids


def attend_kernel(
    heads,
    me,
    tokens,
    first_gain,
    query_down,
    latent_down,
    query_gain,
    latent_gain,
    query_up,
    latent_up,
    out_weight,
    keep,
    low,
    high,
    first_in,
    latents,
    query_code,
    latent_code,
    queries,
    keyvals,
    rope_keys,
    heads_out,
    log_total,
    partial,
    raw_latents,
    spread,
    spread_up,
    rope_down,
    kv_all,
    rope_all,
):
    step = pl.program_id(0)

    @pl.when(step == 0)
    def _():
        spread_out_weight(out_weight, spread, heads)
        spread_query_up(query_up, spread_up, heads)
        rope_down[...] = jnp.zeros_like(rope_down)
        rope_down[64:96, :] = latent_down[KVR:, :]

    def rows_of(index, carry):
        rows = pl.ds(pl.multiple_of(index * 16, 16), 16)
        values = tokens[rows, :].astype(F32)
        first_in[rows, :] = (values * root(values) * row(first_gain)).astype(BF16)
        return carry

    lax.fori_loop(0, TILE // 16, rows_of, 0, unroll=True)
    taken = first_in[...]
    query_latent = dot(taken, query_down[...])
    raw_latents[:, :QR] = query_latent
    code = (query_latent * root(query_latent) * row(query_gain)).astype(BF16)
    query_code[...] = code
    latent = dot(taken, latent_down[:KVR, :], NT)
    raw_latents[:, QR:] = latent
    count = latents.shape[0]
    own = me[0] * count

    @pl.when(own // TILE == step)
    def _():
        latents[...] = raw_latents[pl.ds(pl.multiple_of(own % TILE, count), count), :]

    lcode = (latent * root(latent) * row(latent_gain)).astype(BF16)
    latent_code[...] = lcode
    tables = keep[...], low[...], high[...]
    rope = turn(dot(taken, rope_down[...], NT), *tables).astype(BF16)
    rope_keys[...] = rope
    here = pl.ds(pl.multiple_of(step * TILE, TILE), TILE)
    rope_all[here, :] = rope
    kv = dot(lcode, latent_up[...]).astype(BF16)
    keyvals[...] = kv
    kv_all[here, :] = kv
    raw = dot(code, spread_up[...], NT)
    for h in range(heads):
        lanes = slice(128 * h, 128 * h + 128)
        queries[:, lanes] = turn(raw[:, lanes], *tables).astype(BF16)

    def tile(index):
        keys = TILE * (index + 1)
        for h in range(heads):
            lanes = slice(128 * h, 128 * h + 128)
            kv_h = kv_all[:keys, lanes]
            key = jnp.where(low_lanes((keys, 128)), kv_h, rope_all[:keys, :])
            scores = dot(key, queries[:, lanes], NT) * SCALE
            scores = jnp.where(causal(keys, TILE, TILE * index), scores, -1e30)
            top = jnp.max(scores, axis=0, keepdims=True)
            weights = jnp.exp(scores - top)
            total = jnp.sum(weights, axis=0, keepdims=True)
            log_total[h : h + 1, :] = top + jnp.log(total)
            probs = (weights * (1.0 / total)).astype(BF16)
            heads_out[:, lanes] = dot(probs, kv_h, TN).astype(BF16)

    for index in range(2):
        pl.when(step == index)(functools.partial(tile, index))
    partial[...] = dot(heads_out[...], spread[...]).astype(BF16)


def attend(me, tokens, first_gain, query_down, latent_down, query_gain, latent_gain, query_up, latent_up, out_weight, tables):
    latent_down, query_up = latent_down.T, query_up.T
    length, width = tokens.shape
    heads = out_weight.shape[0] // DV
    wide = 128 * heads

    def rows(columns):
        return pl.BlockSpec((TILE, columns), lambda i, *_: (i, 0))

    return call(
        functools.partial(attend_kernel, heads),
        (tokens, first_gain, query_down, latent_down, query_gain, latent_gain, query_up, latent_up, out_weight, *tables),
        [
            rows(width),
            full((width,)),
            full(query_down.shape),
            full(latent_down.shape),
            full((QR,)),
            full((KVR,)),
            full(query_up.shape),
            full(latent_up.shape),
            full(out_weight.shape),
            rows(128),
            rows(128),
            rows(128),
        ],
        [
            rows(width),
            full((length // 8, LAT)),
            rows(QR),
            rows(KVR),
            rows(wide),
            rows(wide),
            rows(128),
            rows(wide),
            pl.BlockSpec((8, TILE), lambda i, *_: (0, i)),
            rows(width),
        ],
        [
            shaped(length, width),
            shaped(length // 8, LAT, dtype=F32),
            shaped(length, QR),
            shaped(length, KVR),
            shaped(length, wide),
            shaped(length, wide),
            shaped(length, 128),
            shaped(length, wide),
            shaped(8, length, dtype=F32),
            shaped(length, width),
        ],
        "attend",
        grid=(length // TILE,),
        me=me,
        scratch=[
            pltpu.VMEM((TILE, LAT), F32),
            pltpu.VMEM((wide, width), BF16),
            pltpu.VMEM((wide, QR), BF16),
            pltpu.VMEM((128, width), BF16),
            pltpu.VMEM((length, wide), BF16),
            pltpu.VMEM((length, 128), BF16),
        ],
    )


def attend_back_kernel(
    heads,
    attention_back,
    out_weight,
    queries,
    keyvals,
    rope_keys,
    log_total,
    query_up,
    latent_up,
    keep,
    low,
    high,
    both_back,
    partial,
    spread,
    spread_up,
    kv_grad,
    rope_grad,
    code_grad,
):
    step = pl.program_id(0)

    @pl.when(step == 0)
    def _():
        spread_out_weight(out_weight, spread, heads)
        spread_query_up(query_up, spread_up, heads)
        kv_grad[...] = jnp.zeros_like(kv_grad)
        rope_grad[...] = jnp.zeros_like(rope_grad)

    heads_back = dot(attention_back[...], spread[...], NT).astype(BF16)
    tables = keep[...], low[...], high[...]

    def tile(index):
        keys = TILE * (index + 1)
        low_part = low_lanes((keys, 128))
        for h in range(heads):
            lanes = slice(128 * h, 128 * h + 128)
            kv_h = keyvals[:keys, lanes]
            key = jnp.where(low_part, kv_h, rope_keys[:keys, :])
            query = queries[:, lanes]
            back = heads_back[:, lanes]
            scores = dot(key, query, NT) * SCALE
            probs = jnp.exp(scores - log_total[h : h + 1, :])
            probs = jnp.where(causal(keys, TILE, TILE * index), probs, 0.0)
            prob_back = dot(kv_h, back, NT)
            mean = jnp.sum(probs * prob_back, axis=0, keepdims=True)
            score_back = (probs * (prob_back - mean)).astype(BF16)
            of_values = dot(probs.astype(BF16), back)
            of_keys = dot(score_back, query) * SCALE
            kv_grad[:keys, lanes] += of_values + jnp.where(low_part, of_keys, 0.0)
            rope_grad[:keys, :] += jnp.where(low_part, 0.0, of_keys)
            of_query = dot(score_back, key, TN) * SCALE
            both_back[here, lanes] = turn(of_query, *tables, back=True).astype(BF16)

    wide = 128 * heads
    here = pl.ds(pl.multiple_of(step * TILE, TILE), TILE)
    for index in range(2):
        pl.when(step == index)(functools.partial(tile, index))
    code_grad[here, :] = dot(both_back[here, :wide], spread_up[...]).astype(BF16)

    @pl.when(step == 1)
    def _():
        kv = kv_grad[...].astype(BF16)
        both_back[:, wide:] = kv
        partial[:, :QR] = code_grad[...]
        partial[:, QR:LAT] = dot(kv, latent_up[...], NT).astype(BF16)
        partial[:, LAT:] = rope_grad[...].astype(BF16)


def attend_back(attention_back, out_weight, queries, keyvals, rope_keys, log_total, query_up, latent_up, tables, needs):
    query_up = query_up.T
    length, width = attention_back.shape
    heads = out_weight.shape[0] // DV
    wide = 128 * heads

    def rows(columns):
        return pl.BlockSpec((TILE, columns), lambda i, *_: (i, 0))

    return call(
        functools.partial(attend_back_kernel, heads),
        (attention_back, out_weight, queries, keyvals, rope_keys, log_total, query_up, latent_up, *tables),
        [
            rows(width),
            full(out_weight.shape),
            rows(wide),
            full((length, wide)),
            full((length, 128)),
            pl.BlockSpec((8, TILE), lambda i, *_: (0, i)),
            full(query_up.shape),
            full(latent_up.shape),
            rows(128),
            rows(128),
            rows(128),
        ],
        [full((length, 2 * wide)), full((length, WIDE))],
        [shaped(length, 2 * wide), shaped(length, WIDE)],
        "attend_back",
        grid=(length // TILE,),
        scratch=[
            pltpu.VMEM((wide, width), BF16),
            pltpu.VMEM((wide, QR), BF16),
            pltpu.VMEM((length, wide), F32),
            pltpu.VMEM((length, 128), F32),
            pltpu.VMEM((length, QR), BF16),
        ],
        needs=needs,
        limit=44,
        near=(0,),
    )


def add_up(got):
    total = got[0].astype(F32)
    for k in range(1, 8):
        total = total + got[k].astype(F32)
    return total


STEPS = 2


def residual_kernel(me, got, tokens, gain, residual, many):
    del me
    total = tokens[...].astype(F32) + add_up(got)
    residual[...] = total
    second_in = (total * root(total) * row(gain)).astype(BF16)
    for k in range(8):
        many[k] = second_in


def own_specs(rows, width):
    step = rows // STEPS
    return (
        pl.BlockSpec((8, step, width), lambda i, me: (0, i, 0)),
        pl.BlockSpec((step, width), lambda i, me: (i, 0)),
        pl.BlockSpec((step, width), lambda i, me: (me[0] * STEPS + i, 0)),
    )


def residual_of(me, got, tokens, gain, needs):
    width = tokens.shape[1]
    rows = tokens.shape[0] // 8
    eight, one, own = own_specs(rows, width)
    return call(
        residual_kernel,
        (got.reshape(8, rows, width), tokens, gain),
        [eight, own, full((width,))],
        [one, eight],
        [shaped(rows, width, dtype=F32), shaped(8, rows, width)],
        "residual",
        grid=(STEPS,),
        needs=needs,
        me=me,
        limit=24,
        near=(0,),
    )


def residual_back_kernel(me, got, residual, cotangent, gain, many, gain_part):
    del me
    second_back = add_up(got)
    values = residual[...]
    factor = root(values)
    normed = values * factor
    part = jnp.sum(second_back * normed, axis=0, keepdims=True)

    @pl.when(pl.program_id(0) == 0)
    def _():
        gain_part[...] = part

    @pl.when(pl.program_id(0) > 0)
    def _():
        gain_part[...] += part

    back = cotangent[...].astype(F32) + norm_back(second_back, normed, factor, row(gain))
    back = back.astype(BF16)
    for k in range(8):
        many[k] = back


def residual_back_of(me, got, residual, cotangent, gain, needs):
    rows, width = residual.shape
    eight, one, own = own_specs(rows, width)
    return call(
        residual_back_kernel,
        (got.reshape(8, rows, width), residual, cotangent, gain),
        [eight, one, own, full((width,))],
        [eight, full((1, width))],
        [shaped(8, rows, width), shaped(1, width, dtype=F32)],
        "residual_back",
        grid=(STEPS,),
        needs=needs,
        me=me,
        limit=24,
        near=(0,),
    )


def ffn_kernel(
    second_in, gate_weight, up_weight, inner_back, gate_back, up_back, inner, partial
):
    taken = second_in[...]
    gate = dot(taken, gate_weight[...], NT)
    up = dot(taken, up_weight[...], NT)
    sigma = 1.0 / (1.0 + jnp.exp(-gate))
    act = gate * sigma
    units = gate.shape[1]
    back = inner_back[...].astype(F32)
    of_gate = (back * up * sigma * (1.0 + gate * (1.0 - sigma))).astype(BF16)
    of_up = (back * act).astype(BF16)
    for out, values in ((gate_back, of_gate), (up_back, of_up), (inner, (act * up).astype(BF16))):
        out[:, :units] = values
        out[:, units:] = jnp.zeros((values.shape[0], out.shape[1] - units), BF16)
    partial[...] = (dot(of_gate, gate_weight[...]) + dot(of_up, up_weight[...])).astype(BF16)


def ffn(second_in, gate_weight, up_weight, inner_back, needs):
    length, width = second_in.shape
    units = gate_weight.shape[0]
    wide = -(-units // 128) * 128

    def rows(columns):
        return pl.BlockSpec((TILE, columns), lambda i, *_: (i, 0))

    return call(
        ffn_kernel,
        (second_in, gate_weight, up_weight, inner_back),
        [rows(width), full((units, width)), full((units, width)), rows(units)],
        [rows(wide), rows(wide), rows(wide), rows(width)],
        [shaped(length, wide)] * 3 + [shaped(length, width)],
        "ffn",
        grid=(length // TILE,),
        needs=needs,
        limit=44,
        near=(0,),
    )


def ffn_down_kernel(places, inner, down_weight, residual, *refs):
    outs, total = refs[:4], refs[4]
    for i in range(2):
        rows = slice(i * TILE, i * TILE + TILE)
        total[rows, :] = dot(inner[rows, : down_weight.shape[0]], down_weight[...]).astype(BF16)
    count = residual.shape[0]
    own = pl.ds(pl.multiple_of(places[4] * count, count), count)
    total[own, :] = (total[own, :].astype(F32) + residual[...]).astype(BF16)
    for k, out in enumerate(outs):
        rows = out.shape[0]
        out[...] = total[pl.ds(pl.multiple_of(places[k] * rows, rows), rows), :]


def ffn_down(places, inner, down_weight, residual, needs):
    length, width = inner.shape[0], down_weight.shape[1]
    block = (length // 4, width)
    return call(
        ffn_down_kernel,
        (inner, down_weight, residual),
        [full(inner.shape), full(down_weight.shape), full(residual.shape)],
        [full(block)] * 4,
        [shaped(*block)] * 4,
        "ffn_down",
        scratch=[pltpu.VMEM((length, width), BF16)],
        needs=needs,
        me=places,
    )


def halves_kernel(blocks, width, starts, *refs):
    sources, outs, turned = refs[:blocks], refs[blocks : 3 * blocks], refs[3 * blocks]
    for n in range(blocks):
        source, keep, give = sources[n], outs[2 * n], outs[2 * n + 1]
        columns, each = source.shape[1], width[n]
        for c in range(0, columns, 256):
            turned[c : c + 256, :] = source[:, c : c + 256].T
        for which, out in enumerate((keep, give)):
            for k in range(8):
                first = pl.multiple_of(starts[8 * which + k] * each, 16)
                out[each * k : each * k + each, :] = turned[pl.ds(first, each), :]


def halves(starts, values, needs):
    length = values[0].shape[0]
    widths = [item.shape[1] // 16 for item in values]
    shapes = [(8 * w, length) for w in widths for _ in range(2)]
    return call(
        functools.partial(halves_kernel, len(values), widths),
        tuple(values),
        [full(item.shape) for item in values],
        [full(s) for s in shapes],
        [shaped(*s) for s in shapes],
        "halves",
        scratch=[pltpu.VMEM((max(item.shape[1] for item in values), length), BF16)],
        needs=needs,
        me=starts,
        limit=24,
        near=(0,),
    )


ORDER = (2, 1, 3, 0)


def ffn_grads_kernel(in_keep, in_got, cot_keep, cot_got, *refs):
    ours, theirs, outs = refs[:3], refs[3:6], refs[6:]
    units = outs[0].shape[1] // 3

    def block(*parts):
        for n, (keep, got) in enumerate(((in_keep, in_got), (in_keep, in_got), (cot_keep, cot_got))):
            total = dot(keep[...], ours[n][...]) + dot(got[...], theirs[n][...])
            total = total[:, :units].astype(BF16)
            first = 0
            for out in parts:
                count = out.shape[0]
                out[:, units * n : units * n + units] = total[first : first + count]
                first += count

    for s, parts in enumerate((outs[:2], outs[2:3], outs[3:4], outs[4:])):
        pl.when(pl.program_id(0) == s)(functools.partial(block, *parts))


def ffn_grads(in_keep, in_got, cot_keep, cot_got, ours, theirs, units, needs):
    length, wide = ours[0].shape
    rows = in_keep.shape[0] // 4

    def index(i):
        return (jnp.where(i == 0, 2, jnp.where(i == 1, 1, jnp.where(i == 2, 3, 0))), 0)

    left = pl.BlockSpec((rows, length), index)
    out = (rows, 3 * units)
    outs = [(rows // 2, 3 * units)] * 2 + [out] * 3
    return call(
        ffn_grads_kernel,
        (in_keep, in_got, cot_keep, cot_got, *ours, *theirs),
        [left] * 4 + [full((length, wide))] * 6,
        [full(s) for s in outs],
        [shaped(*s) for s in outs],
        "ffn_grads",
        grid=(4,),
        needs=needs,
    )


def attn_grads_kernel(widths, *refs):
    keeps, gots, outs = refs[:3], refs[3:6], refs[10:]
    wide = outs[0].shape[1]
    ours, theirs = (
        (heads, both.at[:, :wide], both.at[:, wide:]) for heads, both in (refs[6:8], refs[8:10])
    )
    rows = outs[0].shape[0] // 2
    heads = wide // 128
    for out, k in zip(outs, ORDER):
        first = 0
        for n, each in enumerate(widths):
            part = slice(2 * each * k, 2 * each * k + 2 * each)
            total = dot(keeps[n][part, :], ours[n][...]) + dot(gots[n][part, :], theirs[n][...])
            if n == 0:
                for j in range(4):
                    half = total[j * each // 2 : (j + 1) * each // 2]
                    top, left = j // 2 * rows, j % 2 * (wide // 2)
                    for h in range(heads):
                        out[top : top + each // 2, left + 64 * h : left + 64 * h + 64] = half[
                            :, 128 * h + 64 : 128 * h + 128
                        ].astype(BF16)
                first += each // 2
                continue
            total = total.astype(BF16)
            out[first : first + each, :] = total[:each]
            out[rows + first : rows + first + each, :] = total[each:]
            first += each


def attn_grads(keeps, gots, ours, theirs, needs):
    widths = [item.shape[0] // 8 for item in keeps]
    rows, wide = sum(widths) - widths[0] // 2, ours[0].shape[1]
    args = (*keeps, *gots, *ours, *theirs)
    outs = [(2 * rows, wide)] * 4
    return call(
        functools.partial(attn_grads_kernel, widths),
        args,
        [full(item.shape) for item in args],
        [full(s) for s in outs],
        [shaped(*s) for s in outs],
        "attn_grads",
        needs=needs,
    )


UP = [(i, (i + 1) % 4) for i in range(4)]
DOWN = [(i, (i + 3) % 4) for i in range(4)]
ACROSS = [(i, (i + 2) % 4) for i in range(4)]


def relay_kernel(up, from_below, down, from_above, up_out, down_out):
    @pl.when(pl.program_id(0) == 0)
    def _():
        up_out[...] = (up[...].astype(F32) + from_below[...].astype(F32)).astype(BF16)
        down_out[...] = down[...]

    @pl.when(pl.program_id(0) == 1)
    def _():
        up_out[...] = up[...]
        down_out[...] = (down[...].astype(F32) + from_above[...].astype(F32)).astype(BF16)


def relay(up, from_below, down, from_above, needs):
    rows, width = from_below.shape
    half = pl.BlockSpec((rows, width), lambda i, *_: (i, 0))
    return call(
        relay_kernel,
        (up, from_below, down, from_above),
        [half, full((rows, width)), half, full((rows, width))],
        [half, half],
        [shaped(2 * rows, width)] * 2,
        "relay",
        grid=(2,),
        needs=needs,
    )


def add_chips_kernel(*refs):
    ins, keep, give = refs[:-2], refs[-2], refs[-1]
    count = len(ins) // 2
    keep[...] = sum(item[...].astype(F32) for item in ins[:count])
    give[...] = sum(item[...].astype(F32) for item in ins[count:]).astype(BF16)


def add_chips(items, needs):
    rows, width = items[0].shape[0] // 2, items[0].shape[1]
    step = rows // 2 if rows % 32 == 0 and (rows // 2) % 16 == 0 else rows
    count = rows // step
    mine = pl.BlockSpec((step, width), lambda i, *_: (i, 0))
    other = pl.BlockSpec((step, width), lambda i, *_: (i + count, 0))
    return call(
        add_chips_kernel,
        (*items, *items),
        [mine] * len(items) + [other] * len(items),
        [mine, mine],
        [shaped(rows, width, dtype=F32), shaped(rows, width)],
        "add_chips",
        grid=(count,),
        needs=needs,
    )


def add_all_kernel(*refs):
    refs[-1][...] = sum(item[...].astype(F32) for item in refs[:-1]).astype(BF16)


def add_all(items, needs):
    rows, width = items[0].shape
    half = pl.BlockSpec((rows // 2, width), lambda i, *_: (i, 0))
    return call(
        add_all_kernel,
        tuple(items),
        [half] * len(items),
        [half],
        [shaped(rows, width)],
        "add_all",
        grid=(2,),
        needs=needs,
        limit=58,
    )


def over_z(blocks):
    return [lax.ppermute(blocks[k], "z", [(i, i ^ k) for i in range(4)]) for k in (1, 2, 3)]


def over_cores(values):
    return lax.ppermute(values, "core", SWAP)


def latents_back_kernel(
    me, got, latents, query_gain, latent_gain, keep, low, high, many, own, gain_part, turns, sems
):
    rows = own.shape[0]
    here = pl.ds(pl.multiple_of(me[0] * rows, rows), rows)
    copies = [
        pltpu.make_async_copy(table.at[here, :], turns.at[n], sems.at[n])
        for n, table in enumerate((keep, low, high))
    ]
    for copy in copies:
        copy.start()
    total = add_up(got)
    for copy in copies:
        copy.wait()

    def back(lanes, gain):
        upstream, values = total[:, lanes], latents[:, lanes]
        factor = root(values)
        normed = values * factor
        gain_part[:, lanes] = jnp.sum(upstream * normed, axis=0, keepdims=True)
        return norm_back(upstream, normed, factor, row(gain)).astype(BF16)

    own[:, :QR] = back(slice(0, QR), query_gain)
    own[:, QR:LAT] = back(slice(QR, LAT), latent_gain)
    own[:, LAT:] = turn(total[:, LAT:], turns[0], turns[1], turns[2], back=True).astype(BF16)
    for k in range(8):
        many[k] = own[...]


def latents_back_of(me, got, latents, query_gain, latent_gain, tables, needs):
    rows = latents.shape[0]
    return call(
        latents_back_kernel,
        (got.reshape(8, rows, WIDE), latents, query_gain, latent_gain, *tables),
        [full((8, rows, WIDE)), full(latents.shape), full((QR,)), full((KVR,)), HBM, HBM, HBM],
        [full((8, rows, WIDE)), full((rows, WIDE)), full((1, LAT))],
        [shaped(8, rows, WIDE), shaped(rows, WIDE), shaped(1, LAT, dtype=F32)],
        "latents_back",
        scratch=[
            pltpu.VMEM((3, rows, 128), F32),
            pltpu.SemaphoreType.DMA((3,)),
        ],
        needs=needs,
        me=me,
        limit=24,
        near=(0,),
    )


def first_back_of(raw_back, query_down, latent_down, rope_down):
    rope_down[...] = jnp.zeros_like(rope_down)
    rope_down[64:96, :] = latent_down[KVR:, :]
    return (
        dot(raw_back[:, :QR], query_down[...], NT)
        + dot(raw_back[:, QR:LAT], latent_down[:KVR, :])
        + dot(raw_back[:, LAT:], rope_down[...])
    )


def tokens_back_kernel(
    raw_back, tokens, attention_back, query_down, latent_down, gain, tokens_grad, rope_down
):
    first_back = first_back_of(raw_back, query_down, latent_down, rope_down)
    values = tokens[...].astype(F32)
    factor = root(values)
    tokens_grad[...] = attention_back[...].astype(F32) + norm_back(
        first_back, values * factor, factor, row(gain)
    )


def tokens_back_of(raw_back, tokens, attention_back, query_down, latent_down, gain, needs):
    length, width = tokens.shape

    def rows(columns):
        return pl.BlockSpec((TILE, columns), lambda i, *_: (i, 0))

    return call(
        tokens_back_kernel,
        (raw_back, tokens, attention_back, query_down, latent_down.T, gain),
        [
            rows(WIDE),
            rows(width),
            rows(width),
            full(query_down.shape),
            full(latent_down.shape[::-1]),
            full((width,)),
        ],
        [rows(width)],
        [shaped(length, width, dtype=F32)],
        "tokens_back",
        grid=(length // TILE,),
        scratch=[pltpu.VMEM((128, width), BF16)],
        needs=needs,
    )


GAINS = ((0, 160), (160, 48), (208, 16))


def down_parts_kernel(own_in, raw_back, gains, out):
    total = dot(own_in[...], raw_back[...]).astype(BF16)
    for d in range(16):
        out[d, :20, :] = total[20 * d : 20 * d + 20]
        out[d, 20:, :] = jnp.zeros((4, WIDE), BF16)
        out[d, 20:21, :] = gains[d : d + 1, :]


def down_parts(own_in, raw_back, gains, needs):
    args = (own_in, raw_back, gains)
    return call(
        down_parts_kernel,
        args,
        [full(item.shape) for item in args],
        [full((16, 24, WIDE))],
        [shaped(16, 24, WIDE)],
        "down_parts",
        needs=needs,
        limit=24,
    )


def sum_copies_kernel(got, many):
    total = got[0].astype(F32)
    for d in range(1, 16):
        total = total + got[d].astype(F32)
    for k in range(8):
        many[k] = total.astype(BF16)


def sum_copies(got, needs):
    return call(
        sum_copies_kernel,
        (got,),
        [full(got.shape)],
        [full((8, 24, WIDE))],
        [shaped(8, 24, WIDE)],
        "sum_copies",
        needs=needs,
        limit=24,
    )


def finish_kernel(heads, places, *refs):
    ins, outs, sems = refs[:13], refs[13:-1], refs[-1]
    ffn_keep, ffn_got, attn_keep, attn_got, everyone, query_rows, latent_rows, gain = ins[5:]
    mixed, gate, up, down, out_grad, query_up, latent_up, query_grad, latent_grad = outs[:9]
    first, *gains = outs[9:]
    count = ins[0].shape[0]
    half = count // 2
    copies = [
        pltpu.make_async_copy(
            item,
            mixed.at[pl.ds(pl.multiple_of(places[k] * count + skip, half), item.shape[0]), :],
            sems.at[n],
        )
        for n, (item, k, skip) in enumerate(
            zip(ins[:5], (0, 1, 2, 2, 3), (0, 0, 0, half, 0), strict=True)
        )
    ]
    for copy in copies:
        copy.start()

    units = gate.shape[1]
    for n, out in enumerate((gate, up, down)):
        lanes = slice(units * n, units * n + units)
        out[...] = ffn_keep[:, lanes] + ffn_got[:, lanes].astype(F32)

    total = attn_keep[...] + attn_got[...].astype(F32)
    out_grad[:80, :] = total[:80, : 64 * heads]
    out_grad[80:, :] = total[:80, 64 * heads :]
    for h in range(heads):
        query_up[:, 96 * h : 96 * h + 96] = total[80:128, 128 * h : 128 * h + 96]
    latent_up[...] = total[128:144]

    for t in range(8):
        values = everyone[t].astype(F32)
        query_grad[20 * t : 20 * t + 20, :] = values[:20, :QR]
        latent_grad[20 * t : 20 * t + 20, :KVR] = values[:20, QR:LAT]
        latent_grad[20 * t : 20 * t + 20, KVR:] = values[:20, LAT + 64 : LAT + 96]
    total = sum(everyone[t, 16:24, :].astype(F32) for t in range(8))[4:5, :]
    for out, (start, width) in zip(gains, GAINS):
        out[...] = total[:, start : start + width]

    def row_sums(values):
        return dot(jnp.ones((8, values.shape[1]), BF16), values.astype(BF16), NT)[:1]

    of_query = row_sums(query_rows[...].astype(F32) * query_grad[...])
    of_latent = row_sums(latent_rows[...].astype(F32) * latent_grad[...])
    first[...] = (of_query + of_latent) / gain[...]
    for copy in copies:
        copy.wait()


def finish(places, mixed, ffn, attn, everyone, query_rows, latent_rows, gain_rows):
    everyone = everyone.reshape(8, 24, WIDE)
    rows, units = ffn[0].shape[0], ffn[0].shape[1] // 3
    heads = attn[0].shape[1] // 128
    count, width = mixed[0].shape
    args = (*mixed, *ffn, *attn, everyone, query_rows, latent_rows, gain_rows)
    outs = [(rows, units)] * 3 + [(rows, 64 * heads), (48, 96 * heads), (16, 128 * heads)]
    outs += [(rows, QR), (rows, KVR + ROPE), (1, rows)] + [(1, each) for _, each in GAINS]
    return call(
        functools.partial(finish_kernel, heads),
        args,
        [full(item.shape) for item in args],
        [HBM] + [full(s) for s in outs],
        [shaped(4 * count, width)] + [shaped(*s, dtype=F32) for s in outs],
        "finish",
        scratch=[pltpu.SemaphoreType.DMA((5,))],
        me=places,
    )[0]


def exchange(blocks):
    return lax.all_to_all(blocks.reshape(-1, blocks.shape[-1]), TP, 0, 0, tiled=True)


def on_device(
    tokens,
    first_gain,
    query_down,
    query_gain,
    query_up,
    latent_down,
    latent_gain,
    latent_up,
    out_weight,
    second_gain,
    gate_weight,
    up_weight,
    down_weight,
    cotangent,
):
    length = tokens.shape[0]
    me = lax.axis_index(TP).astype(jnp.int32).reshape(1)
    y, xl, core = lax.axis_index("y"), lax.axis_index("xl"), lax.axis_index("core")
    starts = jnp.stack(
        [
            ((y + k) % 4 * 2 + (xl ^ j)) * 2 + c
            for c in (core, 1 - core)
            for k in range(4)
            for j in range(2)
        ]
    ).astype(jnp.int32)
    places = jnp.stack([lax.axis_index("z") ^ k for k in range(4)] + [me[0]]).astype(jnp.int32)
    z_order = jnp.stack([(lax.axis_index("z") + k) % 4 for k in range(4)]).astype(jnp.int32)
    first_row = ((y * 2 + xl) * 2 + core) * 160
    query_rows, latent_rows = (
        lax.dynamic_slice_in_dim(item, first_row, 160, 0) for item in (query_down, latent_down)
    )
    gain_rows = lax.dynamic_slice_in_dim(first_gain, first_row, 160, 0)[None]
    tables = rope_tables(length)

    gate_turned, up_turned = gate_weight.T, up_weight.T

    (
        first_in,
        latents,
        query_code,
        latent_code,
        queries,
        keyvals,
        rope_keys,
        heads_out,
        log_total,
        attn_partial,
    ), started = attend(
        me,
        tokens,
        first_gain,
        query_down,
        latent_down,
        query_gain,
        latent_gain,
        query_up,
        latent_up,
        out_weight,
        tables,
    )
    attn_got = exchange(attn_partial)

    (cot_keep, cot_give), picked = halves(starts, [cotangent], [started])
    inner_back = dot(cotangent, down_weight, NT).astype(BF16)
    cot_got = over_cores(cot_give)

    (residual, second_many), _ = residual_of(
        me, attn_got, tokens, second_gain, [picked, cot_got, query_rows, latent_rows, gain_rows, z_order]
    )
    second_in = exchange(second_many)

    turned_in = first_in.T.reshape(16, 8, 20, length)
    own_in = lax.dynamic_slice_in_dim(turned_in, me[0], 1, 1).reshape(320, length)
    (code_keep, code_give, lat_keep, lat_give), picked = halves(
        starts, [query_code, latent_code], [residual]
    )
    code_got, lat_got = over_cores(code_give), over_cores(lat_give)
    heads_got = over_cores(heads_out)

    (gate_back, up_back, inner, back_partial), done = ffn(
        second_in, gate_turned, up_turned, inner_back, [picked, own_in, code_got, lat_got, heads_got]
    )
    back_got = exchange(back_partial)

    ours = (gate_back, up_back, inner)
    theirs = [over_cores(item) for item in ours]
    (in_keep, in_give), _ = halves(starts, [second_in], [done])
    in_got = over_cores(in_give)
    (far_up, far_down, ffn_up, ffn_down_way, ffn_own), done = ffn_grads(in_keep, in_got, cot_keep, cot_got, ours, theirs, gate_weight.shape[1], [])
    below, above = lax.ppermute(far_up, "y", UP), lax.ppermute(far_down, "y", DOWN)

    (back_many, second_gain_part), done = residual_back_of(
        me, back_got, residual, cotangent, second_gain, [done]
    )
    attention_back = exchange(back_many)
    mixed_blocks, done = ffn_down(places, inner, down_weight, residual, [done])
    mixed_got = over_z(mixed_blocks)
    (ffn_up, ffn_down_way), done = relay(ffn_up, below, ffn_down_way, above, [done])
    below, above = lax.ppermute(ffn_up, "y", UP), lax.ppermute(ffn_down_way, "y", DOWN)

    (both_back, latents_partial), back_done = attend_back(
        attention_back,
        out_weight,
        queries,
        keyvals,
        rope_keys,
        log_total,
        query_up,
        latent_up,
        tables,
        [done],
    )
    latents_got = exchange(latents_partial)

    (out_keep, out_give), picked = halves(starts, [attention_back], [back_done])
    (out_keep, out_give), done = halves(
        starts, [attention_back], [back_done, below, above, *mixed_got]
    )
    (mixed_part,), done = add_all([mixed_blocks[0], *mixed_got], [done])
    mixed_other = lax.ppermute(mixed_part, "xh", SWAP)

    (raw_many, own_raw, latent_gain_parts), done = latents_back_of(
        me, latents_got, latents, query_gain, latent_gain, tables, [done]
    )
    raw_back = exchange(raw_many)

    out_got, both_got = over_cores(out_give), over_cores(both_back)
    (attn_across, attn_up, attn_down, attn_own), done = attn_grads(
        (out_keep, code_keep, lat_keep),
        (out_got, code_got, lat_got),
        (heads_out, both_back),
        (heads_got, both_got),
        [done],
    )
    attn_got = [
        lax.ppermute(attn_across, "y", ACROSS),
        lax.ppermute(attn_up, "y", UP),
        lax.ppermute(attn_down, "y", DOWN),
    ]
    gains = jnp.concatenate(
        [
            second_gain_part.reshape(16, -1),
            latent_gain_parts[0, :QR].reshape(16, -1),
            latent_gain_parts[0, QR:].reshape(16, -1),
        ],
        axis=1,
    ).astype(BF16)
    gains = jnp.pad(gains, ((0, 0), (0, WIDE - gains.shape[1])))
    (ffn_keep, ffn_give), done = add_chips([ffn_own, below, above], [done])
    ffn_got = lax.ppermute(ffn_give, "xl", SWAP)
    (parts,), done = down_parts(own_in, raw_back, gains, [done, attn_got[1], attn_got[2]])
    parts_got = lax.all_to_all(parts, DP, 0, 0, tiled=True)

    (mixed_part,), done = add_all([mixed_part, mixed_other], [done])
    from_above, from_below = (lax.ppermute(mixed_part, "z", way) for way in (DOWN, UP))
    half = mixed_part.shape[0] // 2
    far_low = lax.ppermute(from_below[:half], "z", UP)
    far_high = lax.ppermute(from_above[half:], "z", DOWN)
    (many,), done = sum_copies(parts_got, [done])
    everyone = exchange(many)

    (attn_keep, attn_give), done = add_chips([attn_own, *attn_got], [done])
    attn_other = lax.ppermute(attn_give, "xl", SWAP)
    (tokens_grad,), done = tokens_back_of(
        raw_back, tokens, attention_back, query_down, latent_down, first_gain, [done]
    )
    (
        mixed,
        gate_weight_grad,
        up_weight_grad,
        down_weight_grad,
        out_weight_grad,
        query_up_grad,
        latent_up_grad,
        query_down_grad,
        latent_down_grad,
        first_gain_grad,
        second_gain_grad,
        query_gain_grad,
        latent_gain_grad,
    ) = finish(
        z_order,
        (mixed_part, from_above, far_low, far_high, from_below),
        (ffn_keep, ffn_got),
        (attn_keep, attn_other),
        everyone,
        query_rows,
        latent_rows,
        gain_rows,
    )

    return (
        mixed,
        tokens_grad,
        first_gain_grad[0],
        query_down_grad,
        query_gain_grad[0],
        query_up_grad,
        latent_down_grad,
        latent_gain_grad[0],
        latent_up_grad,
        out_weight_grad.T,
        second_gain_grad[0],
        gate_weight_grad,
        up_weight_grad,
        down_weight_grad.T,
    )


def solution(mesh):
    grid = Mesh(mesh.devices.reshape(4, 2, 2, 2, 4), ("y", "xl", "core", "xh", "z"))
    in_specs = (
        P(DP, None),
        P(),
        P(),
        P(),
        P(None, TP),
        P(),
        P(),
        P(None, TP),
        P(TP, None),
        P(),
        P(None, TP),
        P(None, TP),
        P(TP, None),
        P(DP, None),
    )
    out_specs = (
        P(DP, None),
        P(DP, None),
        P(DP),
        P(DP, None),
        P(DP),
        P(DP, TP),
        P(DP, None),
        P(DP),
        P(DP, TP),
        P(TP, DP),
        P(DP),
        P(DP, TP),
        P(DP, TP),
        P(TP, DP),
    )
    return jax.shard_map(
        on_device, mesh=grid, in_specs=in_specs, out_specs=out_specs, check_vma=False
    )
```

```python
import functools

import jax
import jax.numpy as jnp
import numpy as np
from jax import lax
from jax.experimental import pallas as pl
from jax.experimental.pallas import tpu as pltpu
from jax.sharding import Mesh, PartitionSpec as P

NOPE = 64
ROPE = 32
DV = 64
KVR = 256
QR = 768
LAT = QR + KVR
WIDE = LAT + 128

EPS = 1e-05
BASE = 10000.0
SCALE = (NOPE + ROPE) ** (-0.5)

DP = ("y", "xl", "core")
TP = ("xh", "z")
SWAP = [(0, 1), (1, 0)]
F32 = jnp.float32
BF16 = jnp.bfloat16
NT = (((1,), (1,)), ((), ()))
TN = (((0,), (0,)), ((), ()))
NN = (((1,), (0,)), ((), ()))
TILE = 256


def dot(left, right, dims=NN):
    return lax.dot_general(left, right, dims, preferred_element_type=F32)


def params(limit=56):
    return pltpu.CompilerParams(vmem_limit_bytes=limit * 2**20)


HBM = pl.BlockSpec(memory_space=pltpu.HBM)


def call(kernel, args, in_specs, out_specs, out_shape, name, grid=(1,), scratch=(), needs=(), me=None, limit=60, near=()):
    args = [
        item if n in near else pltpu.with_memory_space_constraint(item, pltpu.HBM)
        for n, item in enumerate(args)
    ]
    needs = [pltpu.with_memory_space_constraint(item, pltpu.HBM) for item in needs]
    first = 0 if me is None else 1
    n_in, n_out = len(args), len(out_shape)

    def body(*refs):
        ins = refs[: first + n_in]
        rest = refs[first + n_in + len(needs) :]
        mark = rest[n_out]

        @pl.when(pl.program_id(0) == 0)
        def _():
            mark[...] = jnp.zeros_like(mark)

        kernel(*ins, *rest[:n_out], *rest[n_out + 1 :])

    *outs, mark = pl.pallas_call(
        body,
        grid_spec=pltpu.PrefetchScalarGridSpec(
            num_scalar_prefetch=first,
            grid=grid,
            in_specs=list(in_specs) + [HBM] * len(needs),
            out_specs=list(out_specs) + [full((8, 128))],
            scratch_shapes=list(scratch),
        ),
        out_shape=list(out_shape) + [shaped(8, 128, dtype=F32)],
        compiler_params=params(limit),
        cost_estimate=pl.CostEstimate(flops=1, bytes_accessed=1, transcendentals=0),
        name=name,
    )(*(() if me is None else (me,)), *args, *needs)
    return outs, mark


def shaped(*shape, dtype=BF16):
    return pltpu.HBM(shape, dtype)


def full(shape):
    return pl.BlockSpec(shape, lambda *_: (0,) * len(shape))


def rope_tables(length):
    half = ROPE // 2
    rates = np.exp(np.arange(half, dtype=np.float32) * np.float32(-2.0 * np.log(BASE) / ROPE))
    angles = np.arange(length, dtype=np.float32)[:, None] * rates.astype(np.float32)[None, :]
    cosine, sine = np.cos(angles), np.sin(angles)
    keep = np.zeros((length, 128), np.float32)
    keep[:, :NOPE] = 1.0
    keep[:, 64:80] = cosine
    keep[:, 80:96] = cosine
    low = np.zeros((length, 128), np.float32)
    low[:, 64:80] = -sine
    high = np.zeros((length, 128), np.float32)
    high[:, 80:96] = sine
    return jnp.asarray(keep), jnp.asarray(low), jnp.asarray(high)


def turn(values, keep, low, high, back=False):
    moved = pltpu.roll(values, 112, 1) * low + pltpu.roll(values, 16, 1) * high
    return values * keep - moved if back else values * keep + moved


def root(values):
    return lax.rsqrt(jnp.mean(values * values, axis=-1, keepdims=True) + EPS)


def norm_back(upstream, normed, factor, gain):
    scaled = upstream * gain
    return factor * (scaled - normed * jnp.mean(scaled * normed, axis=-1, keepdims=True))


def spread_out_weight(weight_ref, spread_ref, heads):
    spread_ref[...] = jnp.zeros_like(spread_ref)
    for h in range(heads):
        spread_ref[128 * h + 64 : 128 * h + 128, :] = weight_ref[64 * h : 64 * h + 64, :]


def spread_query_up(weight_ref, spread_ref, heads):
    spread_ref[...] = jnp.zeros_like(spread_ref)
    for h in range(heads):
        spread_ref[128 * h : 128 * h + 96, :] = weight_ref[96 * h : 96 * h + 96, :]


def row(ref):
    return ref[...].reshape(1, -1)


def low_lanes(shape):
    return lax.broadcasted_iota(jnp.int32, shape, 1) < NOPE


def causal(keys, queries, first_query):
    key_ids = lax.broadcasted_iota(jnp.int32, (keys, queries), 0)
    query_ids = lax.broadcasted_iota(jnp.int32, (keys, queries), 1) + first_query
    return key_ids <= query_ids


def attend_kernel(
    heads,
    me,
    tokens,
    first_gain,
    query_down,
    latent_down,
    query_gain,
    latent_gain,
    query_up,
    latent_up,
    out_weight,
    keep,
    low,
    high,
    first_in,
    latents,
    query_code,
    latent_code,
    queries,
    keyvals,
    rope_keys,
    heads_out,
    log_total,
    partial,
    raw_latents,
    spread,
    spread_up,
    rope_down,
    kv_all,
    rope_all,
):
    step = pl.program_id(0)

    @pl.when(step == 0)
    def _():
        spread_out_weight(out_weight, spread, heads)
        spread_query_up(query_up, spread_up, heads)
        rope_down[...] = jnp.zeros_like(rope_down)
        rope_down[64:96, :] = latent_down[KVR:, :]

    def rows_of(index, carry):
        rows = pl.ds(pl.multiple_of(index * 16, 16), 16)
        values = tokens[rows, :].astype(F32)
        first_in[rows, :] = (values * root(values) * row(first_gain)).astype(BF16)
        return carry

    lax.fori_loop(0, TILE // 16, rows_of, 0, unroll=True)
    taken = first_in[...]
    query_latent = dot(taken, query_down[...])
    raw_latents[:, :QR] = query_latent
    code = (query_latent * root(query_latent) * row(query_gain)).astype(BF16)
    query_code[...] = code
    latent = dot(taken, latent_down[:KVR, :], NT)
    raw_latents[:, QR:] = latent
    count = latents.shape[0]
    own = me[0] * count

    @pl.when(own // TILE == step)
    def _():
        latents[...] = raw_latents[pl.ds(pl.multiple_of(own % TILE, count), count), :]

    lcode = (latent * root(latent) * row(latent_gain)).astype(BF16)
    latent_code[...] = lcode
    tables = keep[...], low[...], high[...]
    rope = turn(dot(taken, rope_down[...], NT), *tables).astype(BF16)
    rope_keys[...] = rope
    here = pl.ds(pl.multiple_of(step * TILE, TILE), TILE)
    rope_all[here, :] = rope
    kv = dot(lcode, latent_up[...]).astype(BF16)
    keyvals[...] = kv
    kv_all[here, :] = kv
    raw = dot(code, spread_up[...], NT)
    for h in range(heads):
        lanes = slice(128 * h, 128 * h + 128)
        queries[:, lanes] = turn(raw[:, lanes], *tables).astype(BF16)

    def tile(index):
        keys = TILE * (index + 1)
        for h in range(heads):
            lanes = slice(128 * h, 128 * h + 128)
            kv_h = kv_all[:keys, lanes]
            key = jnp.where(low_lanes((keys, 128)), kv_h, rope_all[:keys, :])
            scores = dot(key, queries[:, lanes], NT) * SCALE
            scores = jnp.where(causal(keys, TILE, TILE * index), scores, -1e30)
            top = jnp.max(scores, axis=0, keepdims=True)
            weights = jnp.exp(scores - top)
            total = jnp.sum(weights, axis=0, keepdims=True)
            log_total[h : h + 1, :] = top + jnp.log(total)
            probs = (weights * (1.0 / total)).astype(BF16)
            heads_out[:, lanes] = dot(probs, kv_h, TN).astype(BF16)

    for index in range(2):
        pl.when(step == index)(functools.partial(tile, index))
    partial[...] = dot(heads_out[...], spread[...]).astype(BF16)


def attend(me, tokens, first_gain, query_down, latent_down, query_gain, latent_gain, query_up, latent_up, out_weight, tables):
    latent_down, query_up = latent_down.T, query_up.T
    length, width = tokens.shape
    heads = out_weight.shape[0] // DV
    wide = 128 * heads

    def rows(columns):
        return pl.BlockSpec((TILE, columns), lambda i, *_: (i, 0))

    return call(
        functools.partial(attend_kernel, heads),
        (tokens, first_gain, query_down, latent_down, query_gain, latent_gain, query_up, latent_up, out_weight, *tables),
        [
            rows(width),
            full((width,)),
            full(query_down.shape),
            full(latent_down.shape),
            full((QR,)),
            full((KVR,)),
            full(query_up.shape),
            full(latent_up.shape),
            full(out_weight.shape),
            rows(128),
            rows(128),
            rows(128),
        ],
        [
            rows(width),
            full((length // 8, LAT)),
            rows(QR),
            rows(KVR),
            rows(wide),
            rows(wide),
            rows(128),
            rows(wide),
            pl.BlockSpec((8, TILE), lambda i, *_: (0, i)),
            rows(width),
        ],
        [
            shaped(length, width),
            shaped(length // 8, LAT, dtype=F32),
            shaped(length, QR),
            shaped(length, KVR),
            shaped(length, wide),
            shaped(length, wide),
            shaped(length, 128),
            shaped(length, wide),
            shaped(8, length, dtype=F32),
            shaped(length, width),
        ],
        "attend",
        grid=(length // TILE,),
        me=me,
        scratch=[
            pltpu.VMEM((TILE, LAT), F32),
            pltpu.VMEM((wide, width), BF16),
            pltpu.VMEM((wide, QR), BF16),
            pltpu.VMEM((128, width), BF16),
            pltpu.VMEM((length, wide), BF16),
            pltpu.VMEM((length, 128), BF16),
        ],
    )


def attend_back_kernel(
    heads,
    attention_back,
    out_weight,
    queries,
    keyvals,
    rope_keys,
    log_total,
    query_up,
    latent_up,
    keep,
    low,
    high,
    both_back,
    partial,
    spread,
    spread_up,
    kv_grad,
    rope_grad,
    code_grad,
):
    step = pl.program_id(0)

    @pl.when(step == 0)
    def _():
        spread_out_weight(out_weight, spread, heads)
        spread_query_up(query_up, spread_up, heads)
        kv_grad[...] = jnp.zeros_like(kv_grad)
        rope_grad[...] = jnp.zeros_like(rope_grad)

    heads_back = dot(attention_back[...], spread[...], NT).astype(BF16)
    tables = keep[...], low[...], high[...]

    def tile(index):
        keys = TILE * (index + 1)
        low_part = low_lanes((keys, 128))
        for h in range(heads):
            lanes = slice(128 * h, 128 * h + 128)
            kv_h = keyvals[:keys, lanes]
            key = jnp.where(low_part, kv_h, rope_keys[:keys, :])
            query = queries[:, lanes]
            back = heads_back[:, lanes]
            scores = dot(key, query, NT) * SCALE
            probs = jnp.exp(scores - log_total[h : h + 1, :])
            probs = jnp.where(causal(keys, TILE, TILE * index), probs, 0.0)
            prob_back = dot(kv_h, back, NT)
            mean = jnp.sum(probs * prob_back, axis=0, keepdims=True)
            score_back = (probs * (prob_back - mean)).astype(BF16)
            of_values = dot(probs.astype(BF16), back)
            of_keys = dot(score_back, query) * SCALE
            kv_grad[:keys, lanes] += of_values + jnp.where(low_part, of_keys, 0.0)
            rope_grad[:keys, :] += jnp.where(low_part, 0.0, of_keys)
            of_query = dot(score_back, key, TN) * SCALE
            both_back[here, lanes] = turn(of_query, *tables, back=True).astype(BF16)

    wide = 128 * heads
    here = pl.ds(pl.multiple_of(step * TILE, TILE), TILE)
    for index in range(2):
        pl.when(step == index)(functools.partial(tile, index))
    code_grad[here, :] = dot(both_back[here, :wide], spread_up[...]).astype(BF16)

    @pl.when(step == 1)
    def _():
        kv = kv_grad[...].astype(BF16)
        both_back[:, wide:] = kv
        partial[:, :QR] = code_grad[...]
        partial[:, QR:LAT] = dot(kv, latent_up[...], NT).astype(BF16)
        partial[:, LAT:] = rope_grad[...].astype(BF16)


def attend_back(attention_back, out_weight, queries, keyvals, rope_keys, log_total, query_up, latent_up, tables, needs):
    query_up = query_up.T
    length, width = attention_back.shape
    heads = out_weight.shape[0] // DV
    wide = 128 * heads

    def rows(columns):
        return pl.BlockSpec((TILE, columns), lambda i, *_: (i, 0))

    return call(
        functools.partial(attend_back_kernel, heads),
        (attention_back, out_weight, queries, keyvals, rope_keys, log_total, query_up, latent_up, *tables),
        [
            rows(width),
            full(out_weight.shape),
            rows(wide),
            full((length, wide)),
            full((length, 128)),
            pl.BlockSpec((8, TILE), lambda i, *_: (0, i)),
            full(query_up.shape),
            full(latent_up.shape),
            rows(128),
            rows(128),
            rows(128),
        ],
        [full((length, 2 * wide)), full((length, WIDE))],
        [shaped(length, 2 * wide), shaped(length, WIDE)],
        "attend_back",
        grid=(length // TILE,),
        scratch=[
            pltpu.VMEM((wide, width), BF16),
            pltpu.VMEM((wide, QR), BF16),
            pltpu.VMEM((length, wide), F32),
            pltpu.VMEM((length, 128), F32),
            pltpu.VMEM((length, QR), BF16),
        ],
        needs=needs,
        limit=44,
        near=(0,),
    )


def after(values, *others):
    def nothing(*refs):
        del refs

    return pl.pallas_call(
        nothing,
        in_specs=[HBM] * (1 + len(others)),
        out_specs=HBM,
        out_shape=shaped(*values.shape, dtype=values.dtype),
        input_output_aliases={0: 0},
        compiler_params=params(60),
        cost_estimate=pl.CostEstimate(flops=1, bytes_accessed=1, transcendentals=0),
        name="after",
    )(values, *others)


def add_up(got):
    total = got[0].astype(F32)
    for k in range(1, 8):
        total = total + got[k].astype(F32)
    return total


STEPS = 2


def residual_kernel(me, got, tokens, gain, residual, many):
    del me
    total = tokens[...].astype(F32) + add_up(got)
    residual[...] = total
    second_in = (total * root(total) * row(gain)).astype(BF16)
    for k in range(8):
        many[k] = second_in


def own_specs(rows, width):
    step = rows // STEPS
    return (
        pl.BlockSpec((8, step, width), lambda i, me: (0, i, 0)),
        pl.BlockSpec((step, width), lambda i, me: (i, 0)),
        pl.BlockSpec((step, width), lambda i, me: (me[0] * STEPS + i, 0)),
    )


def residual_of(me, got, tokens, gain, needs):
    width = tokens.shape[1]
    rows = tokens.shape[0] // 8
    eight, one, own = own_specs(rows, width)
    return call(
        residual_kernel,
        (got.reshape(8, rows, width), tokens, gain),
        [eight, own, full((width,))],
        [one, eight],
        [shaped(rows, width, dtype=F32), shaped(8, rows, width)],
        "residual",
        grid=(STEPS,),
        needs=needs,
        me=me,
        limit=24,
        near=(0,),
    )


def residual_back_kernel(me, got, residual, cotangent, gain, many, gain_part):
    del me
    second_back = add_up(got)
    values = residual[...]
    factor = root(values)
    normed = values * factor
    part = jnp.sum(second_back * normed, axis=0, keepdims=True)

    @pl.when(pl.program_id(0) == 0)
    def _():
        gain_part[...] = part

    @pl.when(pl.program_id(0) > 0)
    def _():
        gain_part[...] += part

    back = cotangent[...].astype(F32) + norm_back(second_back, normed, factor, row(gain))
    back = back.astype(BF16)
    for k in range(8):
        many[k] = back


def residual_back_of(me, got, residual, cotangent, gain, needs):
    rows, width = residual.shape
    eight, one, own = own_specs(rows, width)
    return call(
        residual_back_kernel,
        (got.reshape(8, rows, width), residual, cotangent, gain),
        [eight, one, own, full((width,))],
        [eight, full((1, width))],
        [shaped(8, rows, width), shaped(1, width, dtype=F32)],
        "residual_back",
        grid=(STEPS,),
        needs=needs,
        me=me,
        limit=24,
        near=(0,),
    )


def ffn_kernel(
    second_in, gate_weight, up_weight, inner_back, gate_back, up_back, inner, partial
):
    taken = second_in[...]
    gate = dot(taken, gate_weight[...], NT)
    up = dot(taken, up_weight[...], NT)
    sigma = 1.0 / (1.0 + jnp.exp(-gate))
    act = gate * sigma
    units = gate.shape[1]
    back = inner_back[...].astype(F32)
    of_gate = (back * up * sigma * (1.0 + gate * (1.0 - sigma))).astype(BF16)
    of_up = (back * act).astype(BF16)
    for out, values in ((gate_back, of_gate), (up_back, of_up), (inner, (act * up).astype(BF16))):
        out[:, :units] = values
        out[:, units:] = jnp.zeros((values.shape[0], out.shape[1] - units), BF16)
    partial[...] = (dot(of_gate, gate_weight[...]) + dot(of_up, up_weight[...])).astype(BF16)


def ffn(second_in, gate_weight, up_weight, inner_back, needs):
    length, width = second_in.shape
    units = gate_weight.shape[0]
    wide = -(-units // 128) * 128

    def rows(columns):
        return pl.BlockSpec((TILE, columns), lambda i, *_: (i, 0))

    return call(
        ffn_kernel,
        (second_in, gate_weight, up_weight, inner_back),
        [rows(width), full((units, width)), full((units, width)), rows(units)],
        [rows(wide), rows(wide), rows(wide), rows(width)],
        [shaped(length, wide)] * 3 + [shaped(length, width)],
        "ffn",
        grid=(length // TILE,),
        needs=needs,
        limit=44,
        near=(0,),
    )


def ffn_down_kernel(places, inner, down_weight, residual, *refs):
    outs, total = refs[:4], refs[4]
    for i in range(2):
        rows = slice(i * TILE, i * TILE + TILE)
        total[rows, :] = dot(inner[rows, : down_weight.shape[0]], down_weight[...]).astype(BF16)
    count = residual.shape[0]
    own = pl.ds(pl.multiple_of(places[4] * count, count), count)
    total[own, :] = (total[own, :].astype(F32) + residual[...]).astype(BF16)
    for k, out in enumerate(outs):
        rows = out.shape[0]
        out[...] = total[pl.ds(pl.multiple_of(places[k] * rows, rows), rows), :]


def ffn_down(places, inner, down_weight, residual, needs):
    length, width = inner.shape[0], down_weight.shape[1]
    block = (length // 4, width)
    return call(
        ffn_down_kernel,
        (inner, down_weight, residual),
        [full(inner.shape), full(down_weight.shape), full(residual.shape)],
        [full(block)] * 4,
        [shaped(*block)] * 4,
        "ffn_down",
        scratch=[pltpu.VMEM((length, width), BF16)],
        needs=needs,
        me=places,
    )


def halves_kernel(blocks, width, starts, *refs):
    sources, outs, turned = refs[:blocks], refs[blocks : 3 * blocks], refs[3 * blocks]
    for n in range(blocks):
        source, keep, give = sources[n], outs[2 * n], outs[2 * n + 1]
        columns, each = source.shape[1], width[n]
        for c in range(0, columns, 256):
            turned[c : c + 256, :] = source[:, c : c + 256].T
        for which, out in enumerate((keep, give)):
            for k in range(8):
                first = pl.multiple_of(starts[8 * which + k] * each, 16)
                out[each * k : each * k + each, :] = turned[pl.ds(first, each), :]


def halves(starts, values, needs):
    length = values[0].shape[0]
    widths = [item.shape[1] // 16 for item in values]
    shapes = [(8 * w, length) for w in widths for _ in range(2)]
    return call(
        functools.partial(halves_kernel, len(values), widths),
        tuple(values),
        [full(item.shape) for item in values],
        [full(s) for s in shapes],
        [shaped(*s) for s in shapes],
        "halves",
        scratch=[pltpu.VMEM((max(item.shape[1] for item in values), length), BF16)],
        needs=needs,
        me=starts,
        limit=24,
        near=(0,),
    )


ORDER = (2, 1, 3, 0)


def ffn_grads_kernel(in_keep, in_got, cot_keep, cot_got, *refs):
    ours, theirs, outs = refs[:3], refs[3:6], refs[6:]
    units = outs[0].shape[1] // 3

    def block(*parts):
        for n, (keep, got) in enumerate(((in_keep, in_got), (in_keep, in_got), (cot_keep, cot_got))):
            total = dot(keep[...], ours[n][...]) + dot(got[...], theirs[n][...])
            total = total[:, :units].astype(BF16)
            first = 0
            for out in parts:
                count = out.shape[0]
                out[:, units * n : units * n + units] = total[first : first + count]
                first += count

    for s, parts in enumerate((outs[:2], outs[2:3], outs[3:4], outs[4:])):
        pl.when(pl.program_id(0) == s)(functools.partial(block, *parts))


def ffn_grads(in_keep, in_got, cot_keep, cot_got, ours, theirs, units, needs):
    length, wide = ours[0].shape
    rows = in_keep.shape[0] // 4

    def index(i):
        return (jnp.where(i == 0, 2, jnp.where(i == 1, 1, jnp.where(i == 2, 3, 0))), 0)

    left = pl.BlockSpec((rows, length), index)
    out = (rows, 3 * units)
    outs = [(rows // 2, 3 * units)] * 2 + [out] * 3
    return call(
        ffn_grads_kernel,
        (in_keep, in_got, cot_keep, cot_got, *ours, *theirs),
        [left] * 4 + [full((length, wide))] * 6,
        [full(s) for s in outs],
        [shaped(*s) for s in outs],
        "ffn_grads",
        grid=(4,),
        needs=needs,
    )


def attn_grads_kernel(widths, *refs):
    keeps, gots, outs = refs[:3], refs[3:6], refs[10:]
    wide = outs[0].shape[1]
    ours, theirs = (
        (heads, both.at[:, :wide], both.at[:, wide:]) for heads, both in (refs[6:8], refs[8:10])
    )
    rows = outs[0].shape[0] // 2
    heads = wide // 128
    for out, k in zip(outs, ORDER):
        first = 0
        for n, each in enumerate(widths):
            part = slice(2 * each * k, 2 * each * k + 2 * each)
            total = dot(keeps[n][part, :], ours[n][...]) + dot(gots[n][part, :], theirs[n][...])
            if n == 0:
                for j in range(4):
                    half = total[j * each // 2 : (j + 1) * each // 2]
                    top, left = j // 2 * rows, j % 2 * (wide // 2)
                    for h in range(heads):
                        out[top : top + each // 2, left + 64 * h : left + 64 * h + 64] = half[
                            :, 128 * h + 64 : 128 * h + 128
                        ].astype(BF16)
                first += each // 2
                continue
            total = total.astype(BF16)
            out[first : first + each, :] = total[:each]
            out[rows + first : rows + first + each, :] = total[each:]
            first += each


def attn_grads(keeps, gots, ours, theirs, needs):
    widths = [item.shape[0] // 8 for item in keeps]
    rows, wide = sum(widths) - widths[0] // 2, ours[0].shape[1]
    args = (*keeps, *gots, *ours, *theirs)
    outs = [(2 * rows, wide)] * 4
    return call(
        functools.partial(attn_grads_kernel, widths),
        args,
        [full(item.shape) for item in args],
        [full(s) for s in outs],
        [shaped(*s) for s in outs],
        "attn_grads",
        needs=needs,
        limit=40,
        near=(3, 9),
    )


UP = [(i, (i + 1) % 4) for i in range(4)]
DOWN = [(i, (i + 3) % 4) for i in range(4)]
ACROSS = [(i, (i + 2) % 4) for i in range(4)]


def relay_kernel(up, from_below, down, from_above, up_out, down_out):
    @pl.when(pl.program_id(0) == 0)
    def _():
        up_out[...] = (up[...].astype(F32) + from_below[...].astype(F32)).astype(BF16)
        down_out[...] = down[...]

    @pl.when(pl.program_id(0) == 1)
    def _():
        up_out[...] = up[...]
        down_out[...] = (down[...].astype(F32) + from_above[...].astype(F32)).astype(BF16)


def relay(up, from_below, down, from_above, needs):
    rows, width = from_below.shape
    half = pl.BlockSpec((rows, width), lambda i, *_: (i, 0))
    return call(
        relay_kernel,
        (up, from_below, down, from_above),
        [half, full((rows, width)), half, full((rows, width))],
        [half, half],
        [shaped(2 * rows, width)] * 2,
        "relay",
        grid=(2,),
        needs=needs,
    )


def add_chips_kernel(*refs):
    ins, keep, give = refs[:-2], refs[-2], refs[-1]
    count = len(ins) // 2
    keep[...] = sum(item[...].astype(F32) for item in ins[:count])
    give[...] = sum(item[...].astype(F32) for item in ins[count:]).astype(BF16)


def add_chips(items, needs):
    rows, width = items[0].shape[0] // 2, items[0].shape[1]
    step = rows // 2 if rows % 32 == 0 and (rows // 2) % 16 == 0 else rows
    count = rows // step
    mine = pl.BlockSpec((step, width), lambda i, *_: (i, 0))
    other = pl.BlockSpec((step, width), lambda i, *_: (i + count, 0))
    return call(
        add_chips_kernel,
        (*items, *items),
        [mine] * len(items) + [other] * len(items),
        [mine, mine],
        [shaped(rows, width, dtype=F32), shaped(rows, width)],
        "add_chips",
        grid=(count,),
        needs=needs,
    )


def add_all_kernel(*refs):
    refs[-1][...] = sum(item[...].astype(F32) for item in refs[:-1]).astype(BF16)


def add_all(items, needs):
    rows, width = items[0].shape
    half = pl.BlockSpec((rows // 2, width), lambda i, *_: (i, 0))
    return call(
        add_all_kernel,
        tuple(items),
        [half] * len(items),
        [half],
        [shaped(rows, width)],
        "add_all",
        grid=(2,),
        needs=needs,
        limit=58,
    )


def over_z(blocks):
    return [lax.ppermute(blocks[k], "z", [(i, i ^ k) for i in range(4)]) for k in (1, 2, 3)]


def over_cores(values):
    return lax.ppermute(values, "core", SWAP)


def latents_back_kernel(
    me, got, latents, query_gain, latent_gain, keep, low, high, many, own, gain_part, turns, sems
):
    rows = own.shape[0]
    here = pl.ds(pl.multiple_of(me[0] * rows, rows), rows)
    copies = [
        pltpu.make_async_copy(table.at[here, :], turns.at[n], sems.at[n])
        for n, table in enumerate((keep, low, high))
    ]
    for copy in copies:
        copy.start()
    total = add_up(got)
    for copy in copies:
        copy.wait()

    def back(lanes, gain):
        upstream, values = total[:, lanes], latents[:, lanes]
        factor = root(values)
        normed = values * factor
        gain_part[:, lanes] = jnp.sum(upstream * normed, axis=0, keepdims=True)
        return norm_back(upstream, normed, factor, row(gain)).astype(BF16)

    own[:, :QR] = back(slice(0, QR), query_gain)
    own[:, QR:LAT] = back(slice(QR, LAT), latent_gain)
    own[:, LAT:] = turn(total[:, LAT:], turns[0], turns[1], turns[2], back=True).astype(BF16)
    for k in range(8):
        many[k] = own[...]


def latents_back_of(me, got, latents, query_gain, latent_gain, tables, needs):
    rows = latents.shape[0]
    return call(
        latents_back_kernel,
        (got.reshape(8, rows, WIDE), latents, query_gain, latent_gain, *tables),
        [full((8, rows, WIDE)), full(latents.shape), full((QR,)), full((KVR,)), HBM, HBM, HBM],
        [full((8, rows, WIDE)), full((rows, WIDE)), full((1, LAT))],
        [shaped(8, rows, WIDE), shaped(rows, WIDE), shaped(1, LAT, dtype=F32)],
        "latents_back",
        scratch=[
            pltpu.VMEM((3, rows, 128), F32),
            pltpu.SemaphoreType.DMA((3,)),
        ],
        needs=needs,
        me=me,
        limit=24,
        near=(0,),
    )


def first_back_of(raw_back, query_down, latent_down, rope_down):
    rope_down[...] = jnp.zeros_like(rope_down)
    rope_down[64:96, :] = latent_down[KVR:, :]
    return (
        dot(raw_back[:, :QR], query_down[...], NT)
        + dot(raw_back[:, QR:LAT], latent_down[:KVR, :])
        + dot(raw_back[:, LAT:], rope_down[...])
    )


def tokens_back_kernel(
    raw_back, tokens, attention_back, query_down, latent_down, gain, tokens_grad, rope_down
):
    first_back = first_back_of(raw_back, query_down, latent_down, rope_down)
    values = tokens[...].astype(F32)
    factor = root(values)
    tokens_grad[...] = attention_back[...].astype(F32) + norm_back(
        first_back, values * factor, factor, row(gain)
    )


def tokens_back_of(raw_back, tokens, attention_back, query_down, latent_down, gain, needs):
    length, width = tokens.shape

    def rows(columns):
        return pl.BlockSpec((TILE, columns), lambda i, *_: (i, 0))

    return call(
        tokens_back_kernel,
        (raw_back, tokens, attention_back, query_down, latent_down.T, gain),
        [
            rows(WIDE),
            rows(width),
            rows(width),
            full(query_down.shape),
            full(latent_down.shape[::-1]),
            full((width,)),
        ],
        [rows(width)],
        [shaped(length, width, dtype=F32)],
        "tokens_back",
        grid=(length // TILE,),
        scratch=[pltpu.VMEM((128, width), BF16)],
        needs=needs,
    )


GAINS = ((0, 160), (160, 48), (208, 16))


def down_parts_kernel(own_in, raw_back, gains, out):
    total = dot(own_in[...], raw_back[...]).astype(BF16)
    for d in range(16):
        out[d, :20, :] = total[20 * d : 20 * d + 20]
        out[d, 20:, :] = jnp.zeros((4, WIDE), BF16)
        out[d, 20:21, :] = gains[d : d + 1, :]


def down_parts(own_in, raw_back, gains, needs):
    args = (own_in, raw_back, gains)
    return call(
        down_parts_kernel,
        args,
        [full(item.shape) for item in args],
        [full((16, 24, WIDE))],
        [shaped(16, 24, WIDE)],
        "down_parts",
        needs=needs,
        limit=24,
        near=(1,),
    )


def sum_copies_kernel(got, many):
    total = got[0].astype(F32)
    for d in range(1, 16):
        total = total + got[d].astype(F32)
    for k in range(8):
        many[k] = total.astype(BF16)


def sum_copies(got, needs):
    return call(
        sum_copies_kernel,
        (got,),
        [full(got.shape)],
        [full((8, 24, WIDE))],
        [shaped(8, 24, WIDE)],
        "sum_copies",
        needs=needs,
        limit=24,
        near=(0,),
    )


def finish_kernel(heads, places, *refs):
    ins, outs, sems = refs[:13], refs[13:-1], refs[-1]
    ffn_keep, ffn_got, attn_keep, attn_got, everyone, query_rows, latent_rows, gain = ins[5:]
    mixed, gate, up, down, out_grad, query_up, latent_up, query_grad, latent_grad = outs[:9]
    first, *gains = outs[9:]
    count = ins[0].shape[0]
    half = count // 2
    copies = [
        pltpu.make_async_copy(
            item,
            mixed.at[pl.ds(pl.multiple_of(places[k] * count + skip, half), item.shape[0]), :],
            sems.at[n],
        )
        for n, (item, k, skip) in enumerate(
            zip(ins[:5], (0, 1, 2, 2, 3), (0, 0, 0, half, 0), strict=True)
        )
    ]
    for copy in copies:
        copy.start()

    units = gate.shape[1]
    for n, out in enumerate((gate, up, down)):
        lanes = slice(units * n, units * n + units)
        out[...] = ffn_keep[:, lanes] + ffn_got[:, lanes].astype(F32)

    total = attn_keep[...] + attn_got[...].astype(F32)
    out_grad[:80, :] = total[:80, : 64 * heads]
    out_grad[80:, :] = total[:80, 64 * heads :]
    for h in range(heads):
        query_up[:, 96 * h : 96 * h + 96] = total[80:128, 128 * h : 128 * h + 96]
    latent_up[...] = total[128:144]

    for t in range(8):
        values = everyone[t].astype(F32)
        query_grad[20 * t : 20 * t + 20, :] = values[:20, :QR]
        latent_grad[20 * t : 20 * t + 20, :KVR] = values[:20, QR:LAT]
        latent_grad[20 * t : 20 * t + 20, KVR:] = values[:20, LAT + 64 : LAT + 96]
    total = sum(everyone[t, 16:24, :].astype(F32) for t in range(8))[4:5, :]
    for out, (start, width) in zip(gains, GAINS):
        out[...] = total[:, start : start + width]

    def row_sums(values):
        return dot(jnp.ones((8, values.shape[1]), BF16), values.astype(BF16), NT)[:1]

    of_query = row_sums(query_rows[...].astype(F32) * query_grad[...])
    of_latent = row_sums(latent_rows[...].astype(F32) * latent_grad[...])
    first[...] = (of_query + of_latent) / gain[...]
    for copy in copies:
        copy.wait()


def finish(places, mixed, ffn, attn, everyone, query_rows, latent_rows, gain_rows):
    everyone = everyone.reshape(8, 24, WIDE)
    rows, units = ffn[0].shape[0], ffn[0].shape[1] // 3
    heads = attn[0].shape[1] // 128
    count, width = mixed[0].shape
    args = (*mixed, *ffn, *attn, everyone, query_rows, latent_rows, gain_rows)
    outs = [(rows, units)] * 3 + [(rows, 64 * heads), (48, 96 * heads), (16, 128 * heads)]
    outs += [(rows, QR), (rows, KVR + ROPE), (1, rows)] + [(1, each) for _, each in GAINS]
    return call(
        functools.partial(finish_kernel, heads),
        args,
        [full(item.shape) for item in args],
        [HBM] + [full(s) for s in outs],
        [shaped(4 * count, width)] + [shaped(*s, dtype=F32) for s in outs],
        "finish",
        scratch=[pltpu.SemaphoreType.DMA((5,))],
        me=places,
    )[0]


def exchange(blocks):
    return lax.all_to_all(blocks.reshape(-1, blocks.shape[-1]), TP, 0, 0, tiled=True)


def on_device(
    tokens,
    first_gain,
    query_down,
    query_gain,
    query_up,
    latent_down,
    latent_gain,
    latent_up,
    out_weight,
    second_gain,
    gate_weight,
    up_weight,
    down_weight,
    cotangent,
):
    length = tokens.shape[0]
    me = lax.axis_index(TP).astype(jnp.int32).reshape(1)
    y, xl, core = lax.axis_index("y"), lax.axis_index("xl"), lax.axis_index("core")
    starts = jnp.stack(
        [
            ((y + k) % 4 * 2 + (xl ^ j)) * 2 + c
            for c in (core, 1 - core)
            for k in range(4)
            for j in range(2)
        ]
    ).astype(jnp.int32)
    places = jnp.stack([lax.axis_index("z") ^ k for k in range(4)] + [me[0]]).astype(jnp.int32)
    z_order = jnp.stack([(lax.axis_index("z") + k) % 4 for k in range(4)]).astype(jnp.int32)
    first_row = ((y * 2 + xl) * 2 + core) * 160
    query_rows, latent_rows = (
        lax.dynamic_slice_in_dim(item, first_row, 160, 0) for item in (query_down, latent_down)
    )
    gain_rows = lax.dynamic_slice_in_dim(first_gain, first_row, 160, 0)[None]
    tables = rope_tables(length)

    gate_turned, up_turned = gate_weight.T, up_weight.T

    (
        first_in,
        latents,
        query_code,
        latent_code,
        queries,
        keyvals,
        rope_keys,
        heads_out,
        log_total,
        attn_partial,
    ), started = attend(
        me,
        tokens,
        first_gain,
        query_down,
        latent_down,
        query_gain,
        latent_gain,
        query_up,
        latent_up,
        out_weight,
        tables,
    )
    attn_got = exchange(attn_partial)

    (cot_keep, cot_give), picked = halves(starts, [cotangent], [started])
    inner_back = dot(cotangent, down_weight, NT).astype(BF16)
    cot_got = over_cores(cot_give)

    (residual, second_many), _ = residual_of(
        me, attn_got, tokens, second_gain, [picked, cot_got, query_rows, latent_rows, gain_rows, z_order]
    )
    second_in = exchange(second_many)

    turned_in = first_in.T.reshape(16, 8, 20, length)
    own_in = lax.dynamic_slice_in_dim(turned_in, me[0], 1, 1).reshape(320, length)
    (code_keep, code_give, lat_keep, lat_give), picked = halves(
        starts, [query_code, latent_code], [residual]
    )
    code_got, lat_got = over_cores(code_give), over_cores(lat_give)
    heads_got = over_cores(heads_out)

    (gate_back, up_back, inner, back_partial), done = ffn(
        second_in, gate_turned, up_turned, inner_back, [picked, own_in, code_got, lat_got, heads_got]
    )
    back_got = exchange(back_partial)

    ours = (gate_back, up_back, inner)
    theirs = [over_cores(item) for item in ours]
    (in_keep, in_give), _ = halves(starts, [second_in], [done])
    in_got = over_cores(in_give)
    (far_up, far_down, ffn_up, ffn_down_way, ffn_own), done = ffn_grads(in_keep, in_got, cot_keep, cot_got, ours, theirs, gate_weight.shape[1], [])
    below, above = lax.ppermute(far_up, "y", UP), lax.ppermute(far_down, "y", DOWN)

    (back_many, second_gain_part), done = residual_back_of(
        me, back_got, residual, cotangent, second_gain, [done]
    )
    attention_back = exchange(back_many)
    mixed_blocks, done = ffn_down(places, inner, down_weight, residual, [done])
    mixed_got = over_z(mixed_blocks)
    (ffn_up, ffn_down_way), done = relay(ffn_up, below, ffn_down_way, above, [done])
    below, above = lax.ppermute(ffn_up, "y", UP), lax.ppermute(ffn_down_way, "y", DOWN)

    (both_back, latents_partial), back_done = attend_back(
        attention_back,
        out_weight,
        queries,
        keyvals,
        rope_keys,
        log_total,
        query_up,
        latent_up,
        tables,
        [done],
    )
    latents_got = exchange(latents_partial)

    (out_keep, out_give), picked = halves(starts, [attention_back], [back_done])
    (out_keep, out_give), done = halves(
        starts, [attention_back], [back_done, below, above, *mixed_got]
    )
    (mixed_part,), done = add_all([mixed_blocks[0], *mixed_got], [done])

    (raw_many, own_raw, latent_gain_parts), done = latents_back_of(
        me, latents_got, latents, query_gain, latent_gain, tables, [done]
    )
    raw_back = exchange(raw_many)

    out_got, both_got = over_cores(out_give), over_cores(both_back)
    (attn_across, attn_up, attn_down, attn_own), done = attn_grads(
        (out_keep, code_keep, lat_keep),
        (out_got, code_got, lat_got),
        (heads_out, both_back),
        (heads_got, both_got),
        [done],
    )
    mixed_part = after(mixed_part, done)
    mixed_other = lax.ppermute(mixed_part, "xh", SWAP)
    attn_got = [
        lax.ppermute(attn_across, "y", ACROSS),
        lax.ppermute(attn_up, "y", UP),
        lax.ppermute(attn_down, "y", DOWN),
    ]
    gains = jnp.concatenate(
        [
            second_gain_part.reshape(16, -1),
            latent_gain_parts[0, :QR].reshape(16, -1),
            latent_gain_parts[0, QR:].reshape(16, -1),
        ],
        axis=1,
    ).astype(BF16)
    gains = jnp.pad(gains, ((0, 0), (0, WIDE - gains.shape[1])))
    (ffn_keep, ffn_give), done = add_chips([ffn_own, below, above], [done])
    ffn_got = lax.ppermute(ffn_give, "xl", SWAP)
    (parts,), done = down_parts(own_in, raw_back, gains, [done, attn_got[1], attn_got[2]])
    parts_got = lax.all_to_all(parts, DP, 0, 0, tiled=True)

    (tokens_grad,), done = tokens_back_of(
        raw_back, tokens, attention_back, query_down, latent_down, first_gain, [done]
    )
    (mixed_part,), done = add_all([mixed_part, mixed_other], [done])
    from_above, from_below = (lax.ppermute(mixed_part, "z", way) for way in (DOWN, UP))
    half = mixed_part.shape[0] // 2
    far_low = lax.ppermute(from_below[:half], "z", UP)
    far_high = lax.ppermute(from_above[half:], "z", DOWN)
    (many,), done = sum_copies(parts_got, [done])
    everyone = exchange(many)

    (attn_keep, attn_give), done = add_chips([attn_own, *attn_got], [done])
    attn_other = lax.ppermute(attn_give, "xl", SWAP)
    (
        mixed,
        gate_weight_grad,
        up_weight_grad,
        down_weight_grad,
        out_weight_grad,
        query_up_grad,
        latent_up_grad,
        query_down_grad,
        latent_down_grad,
        first_gain_grad,
        second_gain_grad,
        query_gain_grad,
        latent_gain_grad,
    ) = finish(
        z_order,
        (mixed_part, from_above, far_low, far_high, from_below),
        (ffn_keep, ffn_got),
        (attn_keep, attn_other),
        everyone,
        query_rows,
        latent_rows,
        gain_rows,
    )

    return (
        mixed,
        tokens_grad,
        first_gain_grad[0],
        query_down_grad,
        query_gain_grad[0],
        query_up_grad,
        latent_down_grad,
        latent_gain_grad[0],
        latent_up_grad,
        out_weight_grad.T,
        second_gain_grad[0],
        gate_weight_grad,
        up_weight_grad,
        down_weight_grad.T,
    )


def solution(mesh):
    grid = Mesh(mesh.devices.reshape(4, 2, 2, 2, 4), ("y", "xl", "core", "xh", "z"))
    in_specs = (
        P(DP, None),
        P(),
        P(),
        P(),
        P(None, TP),
        P(),
        P(),
        P(None, TP),
        P(TP, None),
        P(),
        P(None, TP),
        P(None, TP),
        P(TP, None),
        P(DP, None),
    )
    out_specs = (
        P(DP, None),
        P(DP, None),
        P(DP),
        P(DP, None),
        P(DP),
        P(DP, TP),
        P(DP, None),
        P(DP),
        P(DP, TP),
        P(TP, DP),
        P(DP),
        P(DP, TP),
        P(DP, TP),
        P(TP, DP),
    )
    return jax.shard_map(
        on_device, mesh=grid, in_specs=in_specs, out_specs=out_specs, check_vma=False
    )
```

```python
import functools

import jax
import jax.numpy as jnp
import numpy as np
from jax import lax
from jax.experimental import pallas as pl
from jax.experimental.pallas import tpu as pltpu
from jax.sharding import Mesh, PartitionSpec as P

NOPE = 64
ROPE = 32
DV = 64
KVR = 256
QR = 768
LAT = QR + KVR
WIDE = LAT + 128

EPS = 1e-05
BASE = 10000.0
SCALE = (NOPE + ROPE) ** (-0.5)

DP = ("y", "xl", "core")
TP = ("xh", "z")
SWAP = [(0, 1), (1, 0)]
F32 = jnp.float32
BF16 = jnp.bfloat16
NT = (((1,), (1,)), ((), ()))
TN = (((0,), (0,)), ((), ()))
NN = (((1,), (0,)), ((), ()))
TILE = 256


def dot(left, right, dims=NN):
    return lax.dot_general(left, right, dims, preferred_element_type=F32)


def params(limit=56):
    return pltpu.CompilerParams(vmem_limit_bytes=limit * 2**20)


HBM = pl.BlockSpec(memory_space=pltpu.HBM)


def call(kernel, args, in_specs, out_specs, out_shape, name, grid=(1,), scratch=(), needs=(), me=None, limit=60, near=()):
    args = [
        item if n in near else pltpu.with_memory_space_constraint(item, pltpu.HBM)
        for n, item in enumerate(args)
    ]
    needs = [pltpu.with_memory_space_constraint(item, pltpu.HBM) for item in needs]
    first = 0 if me is None else 1
    n_in, n_out = len(args), len(out_shape)

    def body(*refs):
        ins = refs[: first + n_in]
        rest = refs[first + n_in + len(needs) :]
        mark = rest[n_out]

        @pl.when(pl.program_id(0) == 0)
        def _():
            mark[...] = jnp.zeros_like(mark)

        kernel(*ins, *rest[:n_out], *rest[n_out + 1 :])

    *outs, mark = pl.pallas_call(
        body,
        grid_spec=pltpu.PrefetchScalarGridSpec(
            num_scalar_prefetch=first,
            grid=grid,
            in_specs=list(in_specs) + [HBM] * len(needs),
            out_specs=list(out_specs) + [full((8, 128))],
            scratch_shapes=list(scratch),
        ),
        out_shape=list(out_shape) + [shaped(8, 128, dtype=F32)],
        compiler_params=params(limit),
        cost_estimate=pl.CostEstimate(flops=1, bytes_accessed=1, transcendentals=0),
        name=name,
    )(*(() if me is None else (me,)), *args, *needs)
    return outs, mark


def shaped(*shape, dtype=BF16):
    return pltpu.HBM(shape, dtype)


def full(shape):
    return pl.BlockSpec(shape, lambda *_: (0,) * len(shape))


def rope_tables(length):
    half = ROPE // 2
    rates = np.exp(np.arange(half, dtype=np.float32) * np.float32(-2.0 * np.log(BASE) / ROPE))
    angles = np.arange(length, dtype=np.float32)[:, None] * rates.astype(np.float32)[None, :]
    cosine, sine = np.cos(angles), np.sin(angles)
    keep = np.zeros((length, 128), np.float32)
    keep[:, :NOPE] = 1.0
    keep[:, 64:80] = cosine
    keep[:, 80:96] = cosine
    low = np.zeros((length, 128), np.float32)
    low[:, 64:80] = -sine
    high = np.zeros((length, 128), np.float32)
    high[:, 80:96] = sine
    return jnp.asarray(keep), jnp.asarray(low), jnp.asarray(high)


def turn(values, keep, low, high, back=False):
    moved = pltpu.roll(values, 112, 1) * low + pltpu.roll(values, 16, 1) * high
    return values * keep - moved if back else values * keep + moved


def root(values):
    return lax.rsqrt(jnp.mean(values * values, axis=-1, keepdims=True) + EPS)


def norm_back(upstream, normed, factor, gain):
    scaled = upstream * gain
    return factor * (scaled - normed * jnp.mean(scaled * normed, axis=-1, keepdims=True))


def spread_out_weight(weight_ref, spread_ref, heads):
    spread_ref[...] = jnp.zeros_like(spread_ref)
    for h in range(heads):
        spread_ref[128 * h + 64 : 128 * h + 128, :] = weight_ref[64 * h : 64 * h + 64, :]


def spread_query_up(weight_ref, spread_ref, heads):
    spread_ref[...] = jnp.zeros_like(spread_ref)
    for h in range(heads):
        spread_ref[128 * h : 128 * h + 96, :] = weight_ref[96 * h : 96 * h + 96, :]


def row(ref):
    return ref[...].reshape(1, -1)


def low_lanes(shape):
    return lax.broadcasted_iota(jnp.int32, shape, 1) < NOPE


def causal(keys, queries, first_query):
    key_ids = lax.broadcasted_iota(jnp.int32, (keys, queries), 0)
    query_ids = lax.broadcasted_iota(jnp.int32, (keys, queries), 1) + first_query
    return key_ids <= query_ids


def attend_kernel(
    heads,
    me,
    tokens,
    first_gain,
    query_down,
    latent_down,
    query_gain,
    latent_gain,
    query_up,
    latent_up,
    out_weight,
    keep,
    low,
    high,
    first_in,
    latents,
    query_code,
    latent_code,
    queries,
    keyvals,
    rope_keys,
    heads_out,
    log_total,
    partial,
    raw_latents,
    spread,
    spread_up,
    rope_down,
    kv_all,
    rope_all,
):
    step = pl.program_id(0)

    @pl.when(step == 0)
    def _():
        spread_out_weight(out_weight, spread, heads)
        spread_query_up(query_up, spread_up, heads)
        rope_down[...] = jnp.zeros_like(rope_down)
        rope_down[64:96, :] = latent_down[KVR:, :]

    def rows_of(index, carry):
        rows = pl.ds(pl.multiple_of(index * 16, 16), 16)
        values = tokens[rows, :].astype(F32)
        first_in[rows, :] = (values * root(values) * row(first_gain)).astype(BF16)
        return carry

    lax.fori_loop(0, TILE // 16, rows_of, 0, unroll=True)
    taken = first_in[...]
    query_latent = dot(taken, query_down[...])
    raw_latents[:, :QR] = query_latent
    code = (query_latent * root(query_latent) * row(query_gain)).astype(BF16)
    query_code[...] = code
    latent = dot(taken, latent_down[:KVR, :], NT)
    raw_latents[:, QR:] = latent
    count = latents.shape[0]
    own = me[0] * count

    @pl.when(own // TILE == step)
    def _():
        latents[...] = raw_latents[pl.ds(pl.multiple_of(own % TILE, count), count), :]

    lcode = (latent * root(latent) * row(latent_gain)).astype(BF16)
    latent_code[...] = lcode
    tables = keep[...], low[...], high[...]
    rope = turn(dot(taken, rope_down[...], NT), *tables).astype(BF16)
    rope_keys[...] = rope
    here = pl.ds(pl.multiple_of(step * TILE, TILE), TILE)
    rope_all[here, :] = rope
    kv = dot(lcode, latent_up[...]).astype(BF16)
    keyvals[...] = kv
    kv_all[here, :] = kv
    raw = dot(code, spread_up[...], NT)
    for h in range(heads):
        lanes = slice(128 * h, 128 * h + 128)
        queries[:, lanes] = turn(raw[:, lanes], *tables).astype(BF16)

    def tile(index):
        keys = TILE * (index + 1)
        for h in range(heads):
            lanes = slice(128 * h, 128 * h + 128)
            kv_h = kv_all[:keys, lanes]
            key = jnp.where(low_lanes((keys, 128)), kv_h, rope_all[:keys, :])
            scores = dot(key, queries[:, lanes], NT) * SCALE
            scores = jnp.where(causal(keys, TILE, TILE * index), scores, -1e30)
            top = jnp.max(scores, axis=0, keepdims=True)
            weights = jnp.exp(scores - top)
            total = jnp.sum(weights, axis=0, keepdims=True)
            log_total[h : h + 1, :] = top + jnp.log(total)
            probs = (weights * (1.0 / total)).astype(BF16)
            heads_out[:, lanes] = dot(probs, kv_h, TN).astype(BF16)

    for index in range(2):
        pl.when(step == index)(functools.partial(tile, index))
    partial[...] = dot(heads_out[...], spread[...]).astype(BF16)


def attend(me, tokens, first_gain, query_down, latent_down, query_gain, latent_gain, query_up, latent_up, out_weight, tables):
    latent_down, query_up = latent_down.T, query_up.T
    length, width = tokens.shape
    heads = out_weight.shape[0] // DV
    wide = 128 * heads

    def rows(columns):
        return pl.BlockSpec((TILE, columns), lambda i, *_: (i, 0))

    return call(
        functools.partial(attend_kernel, heads),
        (tokens, first_gain, query_down, latent_down, query_gain, latent_gain, query_up, latent_up, out_weight, *tables),
        [
            rows(width),
            full((width,)),
            full(query_down.shape),
            full(latent_down.shape),
            full((QR,)),
            full((KVR,)),
            full(query_up.shape),
            full(latent_up.shape),
            full(out_weight.shape),
            rows(128),
            rows(128),
            rows(128),
        ],
        [
            rows(width),
            full((length // 8, LAT)),
            rows(QR),
            rows(KVR),
            rows(wide),
            rows(wide),
            rows(128),
            rows(wide),
            pl.BlockSpec((8, TILE), lambda i, *_: (0, i)),
            rows(width),
        ],
        [
            shaped(length, width),
            shaped(length // 8, LAT, dtype=F32),
            shaped(length, QR),
            shaped(length, KVR),
            shaped(length, wide),
            shaped(length, wide),
            shaped(length, 128),
            shaped(length, wide),
            shaped(8, length, dtype=F32),
            shaped(length, width),
        ],
        "attend",
        grid=(length // TILE,),
        me=me,
        scratch=[
            pltpu.VMEM((TILE, LAT), F32),
            pltpu.VMEM((wide, width), BF16),
            pltpu.VMEM((wide, QR), BF16),
            pltpu.VMEM((128, width), BF16),
            pltpu.VMEM((length, wide), BF16),
            pltpu.VMEM((length, 128), BF16),
        ],
    )


def attend_back_kernel(
    heads,
    attention_back,
    out_weight,
    queries,
    keyvals,
    rope_keys,
    log_total,
    query_up,
    latent_up,
    keep,
    low,
    high,
    both_back,
    partial,
    spread,
    spread_up,
    kv_grad,
    rope_grad,
    code_grad,
):
    step = pl.program_id(0)

    @pl.when(step == 0)
    def _():
        spread_out_weight(out_weight, spread, heads)
        spread_query_up(query_up, spread_up, heads)
        kv_grad[...] = jnp.zeros_like(kv_grad)
        rope_grad[...] = jnp.zeros_like(rope_grad)

    heads_back = dot(attention_back[...], spread[...], NT).astype(BF16)
    tables = keep[...], low[...], high[...]

    def tile(index):
        keys = TILE * (index + 1)
        low_part = low_lanes((keys, 128))
        for h in range(heads):
            lanes = slice(128 * h, 128 * h + 128)
            kv_h = keyvals[:keys, lanes]
            key = jnp.where(low_part, kv_h, rope_keys[:keys, :])
            query = queries[:, lanes]
            back = heads_back[:, lanes]
            scores = dot(key, query, NT) * SCALE
            probs = jnp.exp(scores - log_total[h : h + 1, :])
            probs = jnp.where(causal(keys, TILE, TILE * index), probs, 0.0)
            prob_back = dot(kv_h, back, NT)
            mean = jnp.sum(probs * prob_back, axis=0, keepdims=True)
            score_back = (probs * (prob_back - mean)).astype(BF16)
            of_values = dot(probs.astype(BF16), back)
            of_keys = dot(score_back, query) * SCALE
            kv_grad[:keys, lanes] += of_values + jnp.where(low_part, of_keys, 0.0)
            rope_grad[:keys, :] += jnp.where(low_part, 0.0, of_keys)
            of_query = dot(score_back, key, TN) * SCALE
            both_back[here, lanes] = turn(of_query, *tables, back=True).astype(BF16)

    wide = 128 * heads
    here = pl.ds(pl.multiple_of(step * TILE, TILE), TILE)
    for index in range(2):
        pl.when(step == index)(functools.partial(tile, index))
    code_grad[here, :] = dot(both_back[here, :wide], spread_up[...]).astype(BF16)

    @pl.when(step == 1)
    def _():
        kv = kv_grad[...].astype(BF16)
        both_back[:, wide:] = kv
        partial[:, :QR] = code_grad[...]
        partial[:, QR:LAT] = dot(kv, latent_up[...], NT).astype(BF16)
        partial[:, LAT:] = rope_grad[...].astype(BF16)


def attend_back(attention_back, out_weight, queries, keyvals, rope_keys, log_total, query_up, latent_up, tables, needs):
    query_up = query_up.T
    length, width = attention_back.shape
    heads = out_weight.shape[0] // DV
    wide = 128 * heads

    def rows(columns):
        return pl.BlockSpec((TILE, columns), lambda i, *_: (i, 0))

    return call(
        functools.partial(attend_back_kernel, heads),
        (attention_back, out_weight, queries, keyvals, rope_keys, log_total, query_up, latent_up, *tables),
        [
            rows(width),
            full(out_weight.shape),
            rows(wide),
            full((length, wide)),
            full((length, 128)),
            pl.BlockSpec((8, TILE), lambda i, *_: (0, i)),
            full(query_up.shape),
            full(latent_up.shape),
            rows(128),
            rows(128),
            rows(128),
        ],
        [full((length, 2 * wide)), full((length, WIDE))],
        [shaped(length, 2 * wide), shaped(length, WIDE)],
        "attend_back",
        grid=(length // TILE,),
        scratch=[
            pltpu.VMEM((wide, width), BF16),
            pltpu.VMEM((wide, QR), BF16),
            pltpu.VMEM((length, wide), F32),
            pltpu.VMEM((length, 128), F32),
            pltpu.VMEM((length, QR), BF16),
        ],
        needs=needs,
        limit=44,
        near=(0,),
    )


def add_up(got):
    total = got[0].astype(F32)
    for k in range(1, 8):
        total = total + got[k].astype(F32)
    return total


STEPS = 2


def residual_kernel(me, got, tokens, gain, residual, many):
    del me
    total = tokens[...].astype(F32) + add_up(got)
    residual[...] = total
    second_in = (total * root(total) * row(gain)).astype(BF16)
    for k in range(8):
        many[k] = second_in


def own_specs(rows, width):
    step = rows // STEPS
    return (
        pl.BlockSpec((8, step, width), lambda i, me: (0, i, 0)),
        pl.BlockSpec((step, width), lambda i, me: (i, 0)),
        pl.BlockSpec((step, width), lambda i, me: (me[0] * STEPS + i, 0)),
    )


def residual_of(me, got, tokens, gain, needs):
    width = tokens.shape[1]
    rows = tokens.shape[0] // 8
    eight, one, own = own_specs(rows, width)
    return call(
        residual_kernel,
        (got.reshape(8, rows, width), tokens, gain),
        [eight, own, full((width,))],
        [one, eight],
        [shaped(rows, width, dtype=F32), shaped(8, rows, width)],
        "residual",
        grid=(STEPS,),
        needs=needs,
        me=me,
        limit=24,
        near=(0,),
    )


def residual_back_kernel(me, got, residual, cotangent, gain, many, gain_part):
    del me
    second_back = add_up(got)
    values = residual[...]
    factor = root(values)
    normed = values * factor
    part = jnp.sum(second_back * normed, axis=0, keepdims=True)

    @pl.when(pl.program_id(0) == 0)
    def _():
        gain_part[...] = part

    @pl.when(pl.program_id(0) > 0)
    def _():
        gain_part[...] += part

    back = cotangent[...].astype(F32) + norm_back(second_back, normed, factor, row(gain))
    back = back.astype(BF16)
    for k in range(8):
        many[k] = back


def residual_back_of(me, got, residual, cotangent, gain, needs):
    rows, width = residual.shape
    eight, one, own = own_specs(rows, width)
    return call(
        residual_back_kernel,
        (got.reshape(8, rows, width), residual, cotangent, gain),
        [eight, one, own, full((width,))],
        [eight, full((1, width))],
        [shaped(8, rows, width), shaped(1, width, dtype=F32)],
        "residual_back",
        grid=(STEPS,),
        needs=needs,
        me=me,
        limit=24,
        near=(0,),
    )


def ffn_kernel(
    second_in, gate_weight, up_weight, inner_back, gate_back, up_back, inner, partial
):
    taken = second_in[...]
    gate = dot(taken, gate_weight[...], NT)
    up = dot(taken, up_weight[...], NT)
    sigma = 1.0 / (1.0 + jnp.exp(-gate))
    act = gate * sigma
    units = gate.shape[1]
    back = inner_back[...].astype(F32)
    of_gate = (back * up * sigma * (1.0 + gate * (1.0 - sigma))).astype(BF16)
    of_up = (back * act).astype(BF16)
    for out, values in ((gate_back, of_gate), (up_back, of_up), (inner, (act * up).astype(BF16))):
        out[:, :units] = values
        out[:, units:] = jnp.zeros((values.shape[0], out.shape[1] - units), BF16)
    partial[...] = (dot(of_gate, gate_weight[...]) + dot(of_up, up_weight[...])).astype(BF16)


def ffn(second_in, gate_weight, up_weight, inner_back, needs):
    length, width = second_in.shape
    units = gate_weight.shape[0]
    wide = -(-units // 128) * 128

    def rows(columns):
        return pl.BlockSpec((TILE, columns), lambda i, *_: (i, 0))

    return call(
        ffn_kernel,
        (second_in, gate_weight, up_weight, inner_back),
        [rows(width), full((units, width)), full((units, width)), rows(units)],
        [rows(wide), rows(wide), rows(wide), rows(width)],
        [shaped(length, wide)] * 3 + [shaped(length, width)],
        "ffn",
        grid=(length // TILE,),
        needs=needs,
        limit=44,
        near=(0,),
    )


def ffn_down_kernel(places, inner, down_weight, residual, *refs):
    outs, total = refs[:4], refs[4]
    for i in range(2):
        rows = slice(i * TILE, i * TILE + TILE)
        total[rows, :] = dot(inner[rows, : down_weight.shape[0]], down_weight[...]).astype(BF16)
    count = residual.shape[0]
    own = pl.ds(pl.multiple_of(places[4] * count, count), count)
    total[own, :] = (total[own, :].astype(F32) + residual[...]).astype(BF16)
    for k, out in enumerate(outs):
        rows = out.shape[0]
        out[...] = total[pl.ds(pl.multiple_of(places[k] * rows, rows), rows), :]


def ffn_down(places, inner, down_weight, residual, needs):
    length, width = inner.shape[0], down_weight.shape[1]
    block = (length // 4, width)
    return call(
        ffn_down_kernel,
        (inner, down_weight, residual),
        [full(inner.shape), full(down_weight.shape), full(residual.shape)],
        [full(block)] * 4,
        [shaped(*block)] * 4,
        "ffn_down",
        scratch=[pltpu.VMEM((length, width), BF16)],
        needs=needs,
        me=places,
    )


def halves_kernel(blocks, width, starts, *refs):
    sources, outs, turned = refs[:blocks], refs[blocks : 3 * blocks], refs[3 * blocks]
    for n in range(blocks):
        source, keep, give = sources[n], outs[2 * n], outs[2 * n + 1]
        columns, each = source.shape[1], width[n]
        for c in range(0, columns, 256):
            turned[c : c + 256, :] = source[:, c : c + 256].T
        for which, out in enumerate((keep, give)):
            for k in range(8):
                first = pl.multiple_of(starts[8 * which + k] * each, 16)
                out[each * k : each * k + each, :] = turned[pl.ds(first, each), :]


def halves(starts, values, needs):
    length = values[0].shape[0]
    widths = [item.shape[1] // 16 for item in values]
    shapes = [(8 * w, length) for w in widths for _ in range(2)]
    return call(
        functools.partial(halves_kernel, len(values), widths),
        tuple(values),
        [full(item.shape) for item in values],
        [full(s) for s in shapes],
        [shaped(*s) for s in shapes],
        "halves",
        scratch=[pltpu.VMEM((max(item.shape[1] for item in values), length), BF16)],
        needs=needs,
        me=starts,
        limit=24,
        near=(0,),
    )


ORDER = (2, 1, 3, 0)


def ffn_grads_kernel(in_keep, in_got, cot_keep, cot_got, *refs):
    ours, theirs, outs = refs[:3], refs[3:6], refs[6:]
    units = outs[0].shape[1] // 3

    def block(*parts):
        for n, (keep, got) in enumerate(((in_keep, in_got), (in_keep, in_got), (cot_keep, cot_got))):
            total = dot(keep[...], ours[n][...]) + dot(got[...], theirs[n][...])
            total = total[:, :units].astype(BF16)
            first = 0
            for out in parts:
                count = out.shape[0]
                out[:, units * n : units * n + units] = total[first : first + count]
                first += count

    for s, parts in enumerate((outs[:2], outs[2:3], outs[3:4], outs[4:])):
        pl.when(pl.program_id(0) == s)(functools.partial(block, *parts))


def ffn_grads(in_keep, in_got, cot_keep, cot_got, ours, theirs, units, needs):
    length, wide = ours[0].shape
    rows = in_keep.shape[0] // 4

    def index(i):
        return (jnp.where(i == 0, 2, jnp.where(i == 1, 1, jnp.where(i == 2, 3, 0))), 0)

    left = pl.BlockSpec((rows, length), index)
    out = (rows, 3 * units)
    outs = [(rows // 2, 3 * units)] * 2 + [out] * 3
    return call(
        ffn_grads_kernel,
        (in_keep, in_got, cot_keep, cot_got, *ours, *theirs),
        [left] * 4 + [full((length, wide))] * 6,
        [full(s) for s in outs],
        [shaped(*s) for s in outs],
        "ffn_grads",
        grid=(4,),
        needs=needs,
    )


def attn_grads_kernel(widths, *refs):
    keeps, gots, outs = refs[:3], refs[3:6], refs[10:]
    wide = outs[0].shape[1]
    ours, theirs = (
        (heads, both.at[:, :wide], both.at[:, wide:]) for heads, both in (refs[6:8], refs[8:10])
    )
    rows = outs[0].shape[0] // 2
    heads = wide // 128
    for out, k in zip(outs, ORDER):
        first = 0
        for n, each in enumerate(widths):
            part = slice(2 * each * k, 2 * each * k + 2 * each)
            total = dot(keeps[n][part, :], ours[n][...]) + dot(gots[n][part, :], theirs[n][...])
            if n == 0:
                for j in range(4):
                    half = total[j * each // 2 : (j + 1) * each // 2]
                    top, left = j // 2 * rows, j % 2 * (wide // 2)
                    for h in range(heads):
                        out[top : top + each // 2, left + 64 * h : left + 64 * h + 64] = half[
                            :, 128 * h + 64 : 128 * h + 128
                        ].astype(BF16)
                first += each // 2
                continue
            total = total.astype(BF16)
            out[first : first + each, :] = total[:each]
            out[rows + first : rows + first + each, :] = total[each:]
            first += each


def attn_grads(keeps, gots, ours, theirs, needs):
    widths = [item.shape[0] // 8 for item in keeps]
    rows, wide = sum(widths) - widths[0] // 2, ours[0].shape[1]
    args = (*keeps, *gots, *ours, *theirs)
    outs = [(2 * rows, wide)] * 4
    return call(
        functools.partial(attn_grads_kernel, widths),
        args,
        [full(item.shape) for item in args],
        [full(s) for s in outs],
        [shaped(*s) for s in outs],
        "attn_grads",
        needs=needs,
        limit=40,
        near=(3, 9),
    )


UP = [(i, (i + 1) % 4) for i in range(4)]
DOWN = [(i, (i + 3) % 4) for i in range(4)]
ACROSS = [(i, (i + 2) % 4) for i in range(4)]


def relay_kernel(up, from_below, down, from_above, up_out, down_out):
    @pl.when(pl.program_id(0) == 0)
    def _():
        up_out[...] = (up[...].astype(F32) + from_below[...].astype(F32)).astype(BF16)
        down_out[...] = down[...]

    @pl.when(pl.program_id(0) == 1)
    def _():
        up_out[...] = up[...]
        down_out[...] = (down[...].astype(F32) + from_above[...].astype(F32)).astype(BF16)


def relay(up, from_below, down, from_above, needs):
    rows, width = from_below.shape
    half = pl.BlockSpec((rows, width), lambda i, *_: (i, 0))
    return call(
        relay_kernel,
        (up, from_below, down, from_above),
        [half, full((rows, width)), half, full((rows, width))],
        [half, half],
        [shaped(2 * rows, width)] * 2,
        "relay",
        grid=(2,),
        needs=needs,
    )


def add_chips_kernel(*refs):
    ins, keep, give = refs[:-2], refs[-2], refs[-1]
    count = len(ins) // 2
    keep[...] = sum(item[...].astype(F32) for item in ins[:count])
    give[...] = sum(item[...].astype(F32) for item in ins[count:]).astype(BF16)


def add_chips(items, needs):
    rows, width = items[0].shape[0] // 2, items[0].shape[1]
    step = rows // 2 if rows % 32 == 0 and (rows // 2) % 16 == 0 else rows
    count = rows // step
    mine = pl.BlockSpec((step, width), lambda i, *_: (i, 0))
    other = pl.BlockSpec((step, width), lambda i, *_: (i + count, 0))
    return call(
        add_chips_kernel,
        (*items, *items),
        [mine] * len(items) + [other] * len(items),
        [mine, mine],
        [shaped(rows, width, dtype=F32), shaped(rows, width)],
        "add_chips",
        grid=(count,),
        needs=needs,
    )


def add_all_kernel(*refs):
    refs[-1][...] = sum(item[...].astype(F32) for item in refs[:-1]).astype(BF16)


def add_all(items, needs):
    rows, width = items[0].shape
    half = pl.BlockSpec((rows // 2, width), lambda i, *_: (i, 0))
    return call(
        add_all_kernel,
        tuple(items),
        [half] * len(items),
        [half],
        [shaped(rows, width)],
        "add_all",
        grid=(2,),
        needs=needs,
        limit=58,
    )


def over_z(blocks):
    return [lax.ppermute(blocks[k], "z", [(i, i ^ k) for i in range(4)]) for k in (1, 2, 3)]


def over_cores(values):
    return lax.ppermute(values, "core", SWAP)


def latents_back_kernel(
    me, got, latents, query_gain, latent_gain, keep, low, high, many, own, gain_part, turns, sems
):
    rows = own.shape[0]
    here = pl.ds(pl.multiple_of(me[0] * rows, rows), rows)
    copies = [
        pltpu.make_async_copy(table.at[here, :], turns.at[n], sems.at[n])
        for n, table in enumerate((keep, low, high))
    ]
    for copy in copies:
        copy.start()
    total = add_up(got)
    for copy in copies:
        copy.wait()

    def back(lanes, gain):
        upstream, values = total[:, lanes], latents[:, lanes]
        factor = root(values)
        normed = values * factor
        gain_part[:, lanes] = jnp.sum(upstream * normed, axis=0, keepdims=True)
        return norm_back(upstream, normed, factor, row(gain)).astype(BF16)

    own[:, :QR] = back(slice(0, QR), query_gain)
    own[:, QR:LAT] = back(slice(QR, LAT), latent_gain)
    own[:, LAT:] = turn(total[:, LAT:], turns[0], turns[1], turns[2], back=True).astype(BF16)
    for k in range(8):
        many[k] = own[...]


def latents_back_of(me, got, latents, query_gain, latent_gain, tables, needs):
    rows = latents.shape[0]
    return call(
        latents_back_kernel,
        (got.reshape(8, rows, WIDE), latents, query_gain, latent_gain, *tables),
        [full((8, rows, WIDE)), full(latents.shape), full((QR,)), full((KVR,)), HBM, HBM, HBM],
        [full((8, rows, WIDE)), full((rows, WIDE)), full((1, LAT))],
        [shaped(8, rows, WIDE), shaped(rows, WIDE), shaped(1, LAT, dtype=F32)],
        "latents_back",
        scratch=[
            pltpu.VMEM((3, rows, 128), F32),
            pltpu.SemaphoreType.DMA((3,)),
        ],
        needs=needs,
        me=me,
        limit=24,
        near=(0,),
    )


def first_back_of(raw_back, query_down, latent_down, rope_down):
    rope_down[...] = jnp.zeros_like(rope_down)
    rope_down[64:96, :] = latent_down[KVR:, :]
    return (
        dot(raw_back[:, :QR], query_down[...], NT)
        + dot(raw_back[:, QR:LAT], latent_down[:KVR, :])
        + dot(raw_back[:, LAT:], rope_down[...])
    )


def tokens_back_kernel(
    raw_back, tokens, attention_back, query_down, latent_down, gain, tokens_grad, rope_down
):
    first_back = first_back_of(raw_back, query_down, latent_down, rope_down)
    values = tokens[...].astype(F32)
    factor = root(values)
    tokens_grad[...] = attention_back[...].astype(F32) + norm_back(
        first_back, values * factor, factor, row(gain)
    )


def tokens_back_of(raw_back, tokens, attention_back, query_down, latent_down, gain, needs):
    length, width = tokens.shape

    def rows(columns):
        return pl.BlockSpec((TILE, columns), lambda i, *_: (i, 0))

    return call(
        tokens_back_kernel,
        (raw_back, tokens, attention_back, query_down, latent_down.T, gain),
        [
            rows(WIDE),
            rows(width),
            rows(width),
            full(query_down.shape),
            full(latent_down.shape[::-1]),
            full((width,)),
        ],
        [rows(width)],
        [shaped(length, width, dtype=F32)],
        "tokens_back",
        grid=(length // TILE,),
        scratch=[pltpu.VMEM((128, width), BF16)],
        needs=needs,
    )


GAINS = ((0, 160), (160, 48), (208, 16))


def down_parts_kernel(own_in, raw_back, gains, out):
    total = dot(own_in[...], raw_back[...]).astype(BF16)
    for d in range(16):
        out[d, :20, :] = total[20 * d : 20 * d + 20]
        out[d, 20:, :] = jnp.zeros((4, WIDE), BF16)
        out[d, 20:21, :] = gains[d : d + 1, :]


def down_parts(own_in, raw_back, gains, needs):
    args = (own_in, raw_back, gains)
    return call(
        down_parts_kernel,
        args,
        [full(item.shape) for item in args],
        [full((16, 24, WIDE))],
        [shaped(16, 24, WIDE)],
        "down_parts",
        needs=needs,
        limit=24,
        near=(1,),
    )


def sum_copies_kernel(got, many):
    total = got[0].astype(F32)
    for d in range(1, 16):
        total = total + got[d].astype(F32)
    for k in range(8):
        many[k] = total.astype(BF16)


def sum_copies(got, needs):
    return call(
        sum_copies_kernel,
        (got,),
        [full(got.shape)],
        [full((8, 24, WIDE))],
        [shaped(8, 24, WIDE)],
        "sum_copies",
        needs=needs,
        limit=24,
        near=(0,),
    )


def finish_kernel(heads, places, *refs):
    ins, outs, sems = refs[:13], refs[13:-1], refs[-1]
    ffn_keep, ffn_got, attn_keep, attn_got, everyone, query_rows, latent_rows, gain = ins[5:]
    mixed, gate, up, down, out_grad, query_up, latent_up, query_grad, latent_grad = outs[:9]
    first, *gains = outs[9:]
    count = ins[0].shape[0]
    half = count // 2
    copies = [
        pltpu.make_async_copy(
            item,
            mixed.at[pl.ds(pl.multiple_of(places[k] * count + skip, half), item.shape[0]), :],
            sems.at[n],
        )
        for n, (item, k, skip) in enumerate(
            zip(ins[:5], (0, 1, 2, 2, 3), (0, 0, 0, half, 0), strict=True)
        )
    ]
    for copy in copies:
        copy.start()

    units = gate.shape[1]
    for n, out in enumerate((gate, up, down)):
        lanes = slice(units * n, units * n + units)
        out[...] = ffn_keep[:, lanes] + ffn_got[:, lanes].astype(F32)

    total = attn_keep[...] + attn_got[...].astype(F32)
    out_grad[:80, :] = total[:80, : 64 * heads]
    out_grad[80:, :] = total[:80, 64 * heads :]
    for h in range(heads):
        query_up[:, 96 * h : 96 * h + 96] = total[80:128, 128 * h : 128 * h + 96]
    latent_up[...] = total[128:144]

    for t in range(8):
        values = everyone[t].astype(F32)
        query_grad[20 * t : 20 * t + 20, :] = values[:20, :QR]
        latent_grad[20 * t : 20 * t + 20, :KVR] = values[:20, QR:LAT]
        latent_grad[20 * t : 20 * t + 20, KVR:] = values[:20, LAT + 64 : LAT + 96]
    total = sum(everyone[t, 16:24, :].astype(F32) for t in range(8))[4:5, :]
    for out, (start, width) in zip(gains, GAINS):
        out[...] = total[:, start : start + width]

    def row_sums(values):
        return dot(jnp.ones((8, values.shape[1]), BF16), values.astype(BF16), NT)[:1]

    of_query = row_sums(query_rows[...].astype(F32) * query_grad[...])
    of_latent = row_sums(latent_rows[...].astype(F32) * latent_grad[...])
    first[...] = (of_query + of_latent) / gain[...]
    for copy in copies:
        copy.wait()


def finish(places, mixed, ffn, attn, everyone, query_rows, latent_rows, gain_rows):
    everyone = everyone.reshape(8, 24, WIDE)
    rows, units = ffn[0].shape[0], ffn[0].shape[1] // 3
    heads = attn[0].shape[1] // 128
    count, width = mixed[0].shape
    args = (*mixed, *ffn, *attn, everyone, query_rows, latent_rows, gain_rows)
    outs = [(rows, units)] * 3 + [(rows, 64 * heads), (48, 96 * heads), (16, 128 * heads)]
    outs += [(rows, QR), (rows, KVR + ROPE), (1, rows)] + [(1, each) for _, each in GAINS]
    return call(
        functools.partial(finish_kernel, heads),
        args,
        [full(item.shape) for item in args],
        [HBM] + [full(s) for s in outs],
        [shaped(4 * count, width)] + [shaped(*s, dtype=F32) for s in outs],
        "finish",
        scratch=[pltpu.SemaphoreType.DMA((5,))],
        me=places,
    )[0]


def exchange(blocks):
    return lax.all_to_all(blocks.reshape(-1, blocks.shape[-1]), TP, 0, 0, tiled=True)


def on_device(
    tokens,
    first_gain,
    query_down,
    query_gain,
    query_up,
    latent_down,
    latent_gain,
    latent_up,
    out_weight,
    second_gain,
    gate_weight,
    up_weight,
    down_weight,
    cotangent,
):
    length = tokens.shape[0]
    me = lax.axis_index(TP).astype(jnp.int32).reshape(1)
    y, xl, core = lax.axis_index("y"), lax.axis_index("xl"), lax.axis_index("core")
    starts = jnp.stack(
        [
            ((y + k) % 4 * 2 + (xl ^ j)) * 2 + c
            for c in (core, 1 - core)
            for k in range(4)
            for j in range(2)
        ]
    ).astype(jnp.int32)
    places = jnp.stack([lax.axis_index("z") ^ k for k in range(4)] + [me[0]]).astype(jnp.int32)
    z_order = jnp.stack([(lax.axis_index("z") + k) % 4 for k in range(4)]).astype(jnp.int32)
    first_row = ((y * 2 + xl) * 2 + core) * 160
    query_rows, latent_rows = (
        lax.dynamic_slice_in_dim(item, first_row, 160, 0) for item in (query_down, latent_down)
    )
    gain_rows = lax.dynamic_slice_in_dim(first_gain, first_row, 160, 0)[None]
    tables = rope_tables(length)

    gate_turned, up_turned = gate_weight.T, up_weight.T

    (
        first_in,
        latents,
        query_code,
        latent_code,
        queries,
        keyvals,
        rope_keys,
        heads_out,
        log_total,
        attn_partial,
    ), started = attend(
        me,
        tokens,
        first_gain,
        query_down,
        latent_down,
        query_gain,
        latent_gain,
        query_up,
        latent_up,
        out_weight,
        tables,
    )
    attn_got = exchange(attn_partial)

    (cot_keep, cot_give), picked = halves(starts, [cotangent], [started])
    inner_back = dot(cotangent, down_weight, NT).astype(BF16)
    cot_got = over_cores(cot_give)

    (residual, second_many), _ = residual_of(
        me, attn_got, tokens, second_gain, [picked, cot_got, query_rows, latent_rows, gain_rows, z_order]
    )
    second_in = exchange(second_many)

    turned_in = first_in.T.reshape(16, 8, 20, length)
    own_in = lax.dynamic_slice_in_dim(turned_in, me[0], 1, 1).reshape(320, length)
    (code_keep, code_give, lat_keep, lat_give), picked = halves(
        starts, [query_code, latent_code], [residual]
    )
    code_got, lat_got = over_cores(code_give), over_cores(lat_give)
    heads_got = over_cores(heads_out)

    (gate_back, up_back, inner, back_partial), done = ffn(
        second_in, gate_turned, up_turned, inner_back, [picked, own_in, code_got, lat_got, heads_got]
    )
    back_got = exchange(back_partial)

    ours = (gate_back, up_back, inner)
    theirs = [over_cores(item) for item in ours]
    (in_keep, in_give), _ = halves(starts, [second_in], [done])
    in_got = over_cores(in_give)
    (far_up, far_down, ffn_up, ffn_down_way, ffn_own), done = ffn_grads(in_keep, in_got, cot_keep, cot_got, ours, theirs, gate_weight.shape[1], [])
    below, above = lax.ppermute(far_up, "y", UP), lax.ppermute(far_down, "y", DOWN)

    (back_many, second_gain_part), done = residual_back_of(
        me, back_got, residual, cotangent, second_gain, [done]
    )
    attention_back = exchange(back_many)
    mixed_blocks, done = ffn_down(places, inner, down_weight, residual, [done])
    mixed_got = over_z(mixed_blocks)
    (ffn_up, ffn_down_way), done = relay(ffn_up, below, ffn_down_way, above, [done])
    below, above = lax.ppermute(ffn_up, "y", UP), lax.ppermute(ffn_down_way, "y", DOWN)

    (both_back, latents_partial), back_done = attend_back(
        attention_back,
        out_weight,
        queries,
        keyvals,
        rope_keys,
        log_total,
        query_up,
        latent_up,
        tables,
        [done],
    )
    latents_got = exchange(latents_partial)

    (out_keep, out_give), picked = halves(starts, [attention_back], [back_done])
    (out_keep, out_give), done = halves(
        starts, [attention_back], [back_done, below, above, *mixed_got]
    )

    (raw_many, own_raw, latent_gain_parts), done = latents_back_of(
        me, latents_got, latents, query_gain, latent_gain, tables, [done]
    )
    raw_back = exchange(raw_many)

    out_got, both_got = over_cores(out_give), over_cores(both_back)
    (attn_across, attn_up, attn_down, attn_own), done = attn_grads(
        (out_keep, code_keep, lat_keep),
        (out_got, code_got, lat_got),
        (heads_out, both_back),
        (heads_got, both_got),
        [done],
    )
    (mixed_part,), done = add_all([mixed_blocks[0], *mixed_got], [done])
    mixed_other = lax.ppermute(mixed_part, "xh", SWAP)
    attn_got = [
        lax.ppermute(attn_across, "y", ACROSS),
        lax.ppermute(attn_up, "y", UP),
        lax.ppermute(attn_down, "y", DOWN),
    ]
    gains = jnp.concatenate(
        [
            second_gain_part.reshape(16, -1),
            latent_gain_parts[0, :QR].reshape(16, -1),
            latent_gain_parts[0, QR:].reshape(16, -1),
        ],
        axis=1,
    ).astype(BF16)
    gains = jnp.pad(gains, ((0, 0), (0, WIDE - gains.shape[1])))
    (ffn_keep, ffn_give), done = add_chips([ffn_own, below, above], [done])
    ffn_got = lax.ppermute(ffn_give, "xl", SWAP)
    (parts,), done = down_parts(own_in, raw_back, gains, [done, attn_got[1], attn_got[2]])
    parts_got = lax.all_to_all(parts, DP, 0, 0, tiled=True)

    (tokens_grad,), done = tokens_back_of(
        raw_back, tokens, attention_back, query_down, latent_down, first_gain, [done]
    )
    (mixed_part,), done = add_all([mixed_part, mixed_other], [done])
    from_above, from_below = (lax.ppermute(mixed_part, "z", way) for way in (DOWN, UP))
    half = mixed_part.shape[0] // 2
    far_low = lax.ppermute(from_below[:half], "z", UP)
    far_high = lax.ppermute(from_above[half:], "z", DOWN)
    (many,), done = sum_copies(parts_got, [done])
    everyone = exchange(many)

    (attn_keep, attn_give), done = add_chips([attn_own, *attn_got], [done])
    attn_other = lax.ppermute(attn_give, "xl", SWAP)
    (
        mixed,
        gate_weight_grad,
        up_weight_grad,
        down_weight_grad,
        out_weight_grad,
        query_up_grad,
        latent_up_grad,
        query_down_grad,
        latent_down_grad,
        first_gain_grad,
        second_gain_grad,
        query_gain_grad,
        latent_gain_grad,
    ) = finish(
        z_order,
        (mixed_part, from_above, far_low, far_high, from_below),
        (ffn_keep, ffn_got),
        (attn_keep, attn_other),
        everyone,
        query_rows,
        latent_rows,
        gain_rows,
    )

    return (
        mixed,
        tokens_grad,
        first_gain_grad[0],
        query_down_grad,
        query_gain_grad[0],
        query_up_grad,
        latent_down_grad,
        latent_gain_grad[0],
        latent_up_grad,
        out_weight_grad.T,
        second_gain_grad[0],
        gate_weight_grad,
        up_weight_grad,
        down_weight_grad.T,
    )


def solution(mesh):
    grid = Mesh(mesh.devices.reshape(4, 2, 2, 2, 4), ("y", "xl", "core", "xh", "z"))
    in_specs = (
        P(DP, None),
        P(),
        P(),
        P(),
        P(None, TP),
        P(),
        P(),
        P(None, TP),
        P(TP, None),
        P(),
        P(None, TP),
        P(None, TP),
        P(TP, None),
        P(DP, None),
    )
    out_specs = (
        P(DP, None),
        P(DP, None),
        P(DP),
        P(DP, None),
        P(DP),
        P(DP, TP),
        P(DP, None),
        P(DP),
        P(DP, TP),
        P(TP, DP),
        P(DP),
        P(DP, TP),
        P(DP, TP),
        P(TP, DP),
    )
    return jax.shard_map(
        on_device, mesh=grid, in_specs=in_specs, out_specs=out_specs, check_vma=False
    )
```
